32 devices in a mesh: branch: 4 (over y, x), rows: 2 (over core), batch: 4 (over z).
Axes of the slice: x: 2, y: 2, z: 4, core: 2. Of those that a mesh axis runs over, the one named last changes fastest.
Arguments:
- trunk_input: bfloat16 [4, 24, 128, 2048], P('batch', 'rows', None, 'branch'), may hold values from -6.4 to 6.4, as said below
- conv_reduce: bfloat16 [2048, 512], P(None, 'branch'), may hold values from -0.125 to 0.125
- conv_dilated: bfloat16 [3, 3, 512, 512], P(None, None, None, 'branch'), may hold values from -0.09375 to 0.09375
- conv_expand: bfloat16 [512, 2048], P(None, 'branch'), may hold values from -0.25 to 0.25
- reduction_norm_params: float32 [2, 512], P(None, 'branch'), may hold values from -1.6 to 1.6, as said below
- dilated_norm_params: float32 [2, 512], P(None, 'branch'), may hold values from -1.6 to 1.6, as said below
- expansion_norm_params: float32 [2, 2048], P(None, 'branch'), may hold values from -1.6 to 1.6, as said below
- aspp_point: bfloat16 [256, 2048], P('branch'), may hold values from -0.125 to 0.125
- aspp_rates: bfloat16 [3, 3, 3, 256, 2048], P(None, None, None, 'branch'), may hold values from -0.046875 to 0.046875
- aspp_pool: bfloat16 [256, 2048], P('branch'), may hold values from -0.125 to 0.125
- branch_norms: float32 [2, 4, 256], P(None, None, 'branch'), may hold values from -1.6 to 1.6, as said below
- pooling_norm_params: float32 [2, 256], P(None, 'branch'), may hold values from -1.6 to 1.6, as said below
- aspp_project: bfloat16 [256, 5, 256], P('branch'), may hold values from -0.15625 to 0.15625
- projection_norm_params: float32 [2, 256], P(None, 'branch'), may hold values from -1.6 to 1.6, as said below
- head_weight: bfloat16 [256, 22], replicated, may hold values from -0.375 to 0.375
- head_bias: float32 [22], replicated, may hold values from -1.5 to 1.5
- log_vars: float32 [3], replicated, may hold values from -0.7 to 0.7
- crop_boxes: int32 [4, 4], replicated, may hold values from 0 to 128, as said below
- seg_labels: int32 [4, 24, 128], P('batch', 'rows'), may hold values from 0 to 18
- depth_target: float32 [4, 24, 128], P('batch', 'rows'), may hold values from -4 to 4
- normal_target: float32 [4, 2, 24, 128], P('batch', None, 'rows'), may hold values from -3 to 3
Outputs:
- aspp_features: bfloat16 [4, 24, 128, 256], P('batch', 'rows', None, 'branch')
- total_loss: float32 [], replicated
- grad_input: float32 [4, 24, 128, 2048], P('batch', 'rows', None, 'branch')
- grad_reduce: float32 [2048, 512], P(('rows', 'batch'), 'branch')
- grad_dilated: float32 [3, 3, 512, 512], P(None, None, ('rows', 'batch'), 'branch')
- grad_expand: float32 [512, 2048], P(('rows', 'batch'), 'branch')
- grad_norm_reduce: float32 [2, 512], P(None, 'branch')
- gradient_dilated_norm: float32 [2, 512], P(None, 'branch')
- grad_norm_expand: float32 [2, 2048], P(None, 'branch')
- grad_point: float32 [256, 2048], P('branch', ('rows', 'batch'))
- grad_rates: float32 [3, 3, 3, 256, 2048], P(None, None, None, 'branch', ('rows', 'batch'))
- grad_pool: float32 [256, 2048], P('branch', ('rows', 'batch'))
- grad_branch_norms: float32 [2, 4, 256], P(None, None, 'branch')
- grad_pool_norm: float32 [2, 256], P(None, 'branch')
- grad_project: float32 [256, 5, 256], P('branch', None, ('rows', 'batch'))
- grad_project_norm: float32 [2, 256], P(None, 'branch')
- grad_head_weight: float32 [256, 22], replicated
- grad_head_bias: float32 [22], replicated
- grad_log_vars: float32 [3], replicated
The draws below stay inside these ranges and needn't reach their ends.
Inputs may be any that keep to these rules, and one draw needn't show every extreme that they name: `trunk_input`: the values of one image and channel scatter around a mean of their own. `reduction_norm_params`: row 0 holds gains, row 1 biases. `dilated_norm_params`: row 0 holds gains, row 1 biases. `expansion_norm_params`: row 0 holds gains, row 1 biases. `branch_norms`: row 0 holds gains, row 1 biases. `pooling_norm_params`: row 0 holds gains, row 1 biases. `projection_norm_params`: row 0 holds gains, row 1 biases. `crop_boxes`: each region lies inside the canvas and is either 24 rows by 96 columns or 16 rows by 128 columns; both kinds occur in every draw.
All inputs are finite; a program needn't handle non-finite values.
Results may differ from the reference program's by a relative error of at most 0.025.
The reference program's roundings to bfloat16 on the way count: a program that leaves them out, or rounds other values in their place, can miss the bound.
Values may be sent and summed in bfloat16 or wider, within the bound.
A program may use at most 384 MiB of HBM per device.

```python
import jax
import jax.numpy as jnp
from jax import lax

CH = 2048
MID = 512
ASPP = 256
CLASSES = 19
WIDTH = 128
HEADS = 22
IMAGES = 4
HEIGHT = 24


def affine_rows(key, row_shape):
    gain_key, bias_key = jax.random.split(key)
    gains = jax.random.uniform(gain_key, row_shape, jnp.float32, 0.5, 1.5)
    biases = 0.4 * jnp.clip(jax.random.normal(bias_key, row_shape, jnp.float32), -4.0, 4.0)
    return jnp.stack([gains, biases])


def draw_trunk_input(key, part):
    key = jax.random.fold_in(key, 1)
    noise_key, offset_key = jax.random.split(key)
    offsets = jnp.clip(jax.random.normal(offset_key, (IMAGES, 1, 1, CH), jnp.float32), -4.0, 4.0)
    noise = jnp.clip(jax.random.normal(noise_key, (IMAGES, HEIGHT, WIDTH, CH), jnp.float32), -5.0, 5.0)
    return (0.8 * noise + 0.6 * offsets).astype(jnp.bfloat16)


def draw_reduction_norm_params(key, part):
    key = jax.random.fold_in(key, 11)
    return affine_rows(key, (MID,))


def draw_dilated_norm_params(key, part):
    key = jax.random.fold_in(key, 12)
    return affine_rows(key, (MID,))


def draw_expansion_norm_params(key, part):
    key = jax.random.fold_in(key, 13)
    return affine_rows(key, (CH,))


def draw_branch_norms(key, part):
    key = jax.random.fold_in(key, 14)
    return affine_rows(key, (4, ASPP))


def draw_pooling_norm_params(key, part):
    key = jax.random.fold_in(key, 15)
    return affine_rows(key, (ASPP,))


def draw_projection_norm_params(key, part):
    key = jax.random.fold_in(key, 16)
    return affine_rows(key, (ASPP,))


def draw_crop_boxes(key, part):
    key = jax.random.fold_in(key, 7)
    kind_key, pick_key, top_key, left_key = jax.random.split(key, 4)
    crop_kinds = jax.random.randint(kind_key, (IMAGES,), 0, 2)
    forced = jax.random.randint(pick_key, (), 0, IMAGES)
    positions = jnp.arange(IMAGES)
    crop_kinds = jnp.where(positions == forced, 1, crop_kinds)
    crop_kinds = jnp.where(positions == (forced + 1) % IMAGES, 0, crop_kinds)
    heights = jnp.where(crop_kinds == 1, HEIGHT, 2 * HEIGHT // 3)
    widths = jnp.where(crop_kinds == 1, 3 * WIDTH // 4, WIDTH)
    top_rows = jax.random.randint(top_key, (IMAGES,), 0, HEIGHT - heights + 1)
    left_cols = jax.random.randint(left_key, (IMAGES,), 0, WIDTH - widths + 1)
    return jnp.stack([top_rows, left_cols, heights, widths], axis=1).astype(jnp.int32)


def plant(values, own_key, low, largest):
    shape = values.shape
    index_at = [jax.random.randint(jax.random.fold_in(own_key, axis), (), 0, shape[axis]) for axis in range(len(shape))]
    values = values.at[tuple(index_at)].set(low)
    longest = shape.index(max(shape))
    index_at[longest] = (index_at[longest] + 1) % shape[longest]
    return values.at[tuple(index_at)].set(largest)


def level_of(own_key, dims, cuts, low, high):
    loudness, own = 1.0, jax.random.fold_in(own_key, 6)
    for axis_at, parts in cuts:
        draws = jnp.exp(jax.random.uniform(jax.random.fold_in(own, axis_at), (parts,), jnp.float32, low / len(cuts), high / len(cuts)))
        loudness = loudness * jnp.repeat(draws, dims[axis_at] // parts).reshape([-1 if axis == axis_at else 1 for axis in range(len(dims))])
    return loudness


def scatter_about(stream_key, dims, scale, most, cuts=(), held_as=jnp.bfloat16):
    result = scale * jax.random.normal(stream_key, dims, jnp.float32)
    if cuts:
        result = result * level_of(stream_key, dims, cuts, -0.22, 0.18)
    return jnp.clip(result, -most, most).astype(held_as)


def setup_inputs(seed: int = 0) -> dict:
    seeds = jax.random.split(jax.random.key(seed), 22)
    trunk_input = draw_trunk_input(jax.random.fold_in(seeds[21], 71), 0)
    conv_reduce = scatter_about(seeds[1], (CH, MID), CH ** -0.5, 0.125, ((1, 4),))
    conv_dilated = scatter_about(seeds[2], (3, 3, MID, MID), (9 * MID) ** -0.5, 0.09375, ((3, 4),))
    conv_expand = scatter_about(seeds[3], (MID, CH), MID ** -0.5, 0.25, ((1, 4),))
    reduction_norm_params = draw_reduction_norm_params(jax.random.fold_in(seeds[21], 71), 0)
    dilated_norm_params = draw_dilated_norm_params(jax.random.fold_in(seeds[21], 71), 0)
    expansion_norm_params = draw_expansion_norm_params(jax.random.fold_in(seeds[21], 71), 0)
    aspp_point = scatter_about(seeds[7], (ASPP, CH), CH ** -0.5, 0.125, ((0, 4),))
    aspp_rates = scatter_about(seeds[8], (3, 3, 3, ASPP, CH), (9 * CH) ** -0.5, 0.046875, ((3, 4),))
    aspp_pool = scatter_about(seeds[9], (ASPP, CH), CH ** -0.5, 0.125, ((0, 4),))
    branch_norms = draw_branch_norms(jax.random.fold_in(seeds[21], 71), 0)
    pooling_norm_params = draw_pooling_norm_params(jax.random.fold_in(seeds[21], 71), 0)
    aspp_project = scatter_about(seeds[12], (ASPP, 5, ASPP), (5 * ASPP) ** -0.5, 0.15625, ((0, 4),))
    projection_norm_params = draw_projection_norm_params(jax.random.fold_in(seeds[21], 71), 0)
    head_weight = scatter_about(seeds[14], (ASPP, HEADS), ASPP ** -0.5, 0.375)
    head_bias = scatter_about(seeds[15], (HEADS,), 0.3, 1.5, (), jnp.float32)
    log_vars = jnp.clip(jax.random.uniform(seeds[16], (3,), jnp.float32, -0.7, 0.7), -0.7, 0.7)
    crop_boxes = draw_crop_boxes(jax.random.fold_in(seeds[21], 71), 0)
    seg_labels = plant(jax.random.randint(seeds[18], (IMAGES, HEIGHT, WIDTH), 0, CLASSES), jax.random.fold_in(seeds[18], 1), 0, CLASSES - 1).astype(jnp.int32)
    depth_target = scatter_about(seeds[19], (IMAGES, HEIGHT, WIDTH), 1.0, 4.0, ((0, 4), (1, 2)), jnp.float32)
    normal_target = scatter_about(seeds[20], (IMAGES, 2, HEIGHT, WIDTH), 0.7, 3.0, ((0, 4), (2, 2)), jnp.float32)
    return dict(trunk_input=trunk_input, conv_reduce=conv_reduce, conv_dilated=conv_dilated, conv_expand=conv_expand, reduction_norm_params=reduction_norm_params, dilated_norm_params=dilated_norm_params, expansion_norm_params=expansion_norm_params, aspp_point=aspp_point, aspp_rates=aspp_rates, aspp_pool=aspp_pool, branch_norms=branch_norms, pooling_norm_params=pooling_norm_params, aspp_project=aspp_project, projection_norm_params=projection_norm_params, head_weight=head_weight, head_bias=head_bias, log_vars=log_vars, crop_boxes=crop_boxes, seg_labels=seg_labels, depth_target=depth_target, normal_target=normal_target)


EPS = 1e-05
HIGH = lax.Precision.HIGHEST
RATES = (12, 24, 36)

@jax.custom_vjp
def low(v):
    return lax.optimization_barrier(v.astype(jnp.bfloat16)).astype(jnp.float32)

@jax.custom_vjp
def low_back(v):
    return v

def low_keep(v):
    return (low(v), None)

def low_pass(kept, grad):
    return (grad,)

def back_keep(v):
    return (v, None)

def back_low(kept, grad):
    return (low(grad),)
low.defvjp(low_keep, low_pass)
low_back.defvjp(back_keep, back_low)

def move(tensor, offset, axis_id):
    length = tensor.shape[axis_id]
    if offset == 0:
        return tensor
    if abs(offset) >= length:
        return jnp.zeros_like(tensor)
    widths = [(0, 0)] * tensor.ndim
    if offset > 0:
        widths[axis_id] = (offset, 0)
        return lax.slice_in_dim(jnp.pad(tensor, widths), 0, length, axis=axis_id)
    widths[axis_id] = (0, -offset)
    return lax.slice_in_dim(jnp.pad(tensor, widths), -offset, length - offset, axis=axis_id)

def matmul(lhs_arr, rhs_arr):
    return jnp.dot(lhs_arr, rhs_arr, precision=HIGH)

def normalize(tensor, weight, counted, affine):
    axes_list = tuple(range(weight.ndim))
    weight_full = weight.reshape(weight.shape + (1,) * (tensor.ndim - weight.ndim))
    mean_val = lax.optimization_barrier(jnp.sum(tensor * weight_full, axis=axes_list)) / counted
    centered = tensor - mean_val
    variance = lax.optimization_barrier(jnp.sum(weight_full * centered * centered, axis=axes_list)) / counted
    return affine[0] * centered * lax.rsqrt(variance + EPS) + affine[1]

def dilated_conv(source, kernel, dilation):
    summed = 0.0
    for row_tap in range(3):
        for col_tap in range(3):
            shifted = move(move(source, -(row_tap - 1) * dilation, 1), -(col_tap - 1) * dilation, 2)
            summed = summed + matmul(shifted, kernel[row_tap, col_tap])
    return summed

def rate_branch(source, kernel, dilation):
    partials = []
    for row_tap in range(3):
        summed = 0.0
        for col_tap in range(3):
            summed = summed + matmul(move(source, -(col_tap - 1) * dilation, 2), kernel[row_tap, col_tap].T)
        partials.append(summed)
    upper = move(low(partials[0]), dilation, 1)
    lower_part = move(low(partials[2]), -dilation, 1)
    return low_back(partials[1] + upper + lower_part)

def forward(params, valid, pixel_number_count, image_areas, seg_labels, depth_target, normal_target):
    trunk_input, conv_reduce, conv_dilated, conv_expand, reduction_norm_params, dilated_norm_params, expansion_norm_params, aspp_point, aspp_rates, aspp_pool, branch_norms, pooling_norm_params, aspp_project, projection_norm_params, head_weight, head_bias, log_vars = params
    reduced_output = low_back(matmul(trunk_input, conv_reduce))
    hidden_one = low(jax.nn.silu(normalize(reduced_output, valid, pixel_number_count, reduction_norm_params)))
    dilated = low_back(jax.checkpoint(dilated_conv, static_argnums=(2,))(hidden_one, conv_dilated, 4))
    hidden_two = low(jax.nn.silu(normalize(dilated, valid, pixel_number_count, dilated_norm_params)))
    expanded_output = low_back(matmul(hidden_two, conv_expand))
    trunk_out = low(jax.nn.silu(normalize(expanded_output, valid, pixel_number_count, expansion_norm_params) + trunk_input))
    branches = [low_back(matmul(trunk_out, aspp_point.T))]
    for branch_id in range(3):
        branches.append(jax.checkpoint(rate_branch, static_argnums=(2,))(trunk_out, aspp_rates[branch_id], RATES[branch_id]))
    stacked = jnp.stack(branches, axis=3)
    spatial = low(jax.nn.silu(normalize(stacked, valid, pixel_number_count, branch_norms)))
    pooled = low(jnp.einsum('bhw,bhwc->bc', valid, trunk_out, precision=HIGH) / image_areas[:, None])
    pooling_convolution = low_back(matmul(pooled, aspp_pool.T))
    image_overall_count = pooled.shape[0]
    pool_act = low(jax.nn.silu(normalize(pooling_convolution, jnp.ones((image_overall_count,), jnp.float32), float(image_overall_count), pooling_norm_params)))
    pool_wide = jnp.broadcast_to(pool_act[:, None, None, None, :], stacked.shape[:3] + (1, pool_act.shape[1]))
    concat = jnp.concatenate([spatial, pool_wide], axis=3)
    projected_output = low_back(jnp.einsum('bhwsc,dsc->bhwd', concat, aspp_project, precision=HIGH))
    features = low(jax.nn.silu(normalize(projected_output, valid, pixel_number_count, projection_norm_params)))
    logits = matmul(features, head_weight) + head_bias
    seg_logits = logits[..., :CLASSES]
    classes_hot = (seg_labels[..., None] == jnp.arange(CLASSES, dtype=jnp.int32)).astype(jnp.float32)
    cross = jax.nn.logsumexp(seg_logits, axis=-1) - lax.optimization_barrier(jnp.sum(seg_logits * classes_hot, axis=-1))
    depth_gap = logits[..., CLASSES] - depth_target
    normal_gap = logits[..., CLASSES + 1:] - jnp.moveaxis(normal_target, 1, 3)
    task_losses = jnp.stack([jnp.sum(valid * cross), jnp.sum(valid * (jnp.sqrt(depth_gap * depth_gap + 1.0) - 1.0)), jnp.sum(valid * lax.optimization_barrier(jnp.sum(normal_gap * normal_gap, axis=-1)))]) / pixel_number_count
    objective = jnp.sum(jnp.exp(-log_vars) * task_losses + log_vars)
    return (objective, features)

def reference(trunk_input, conv_reduce, conv_dilated, conv_expand, reduction_norm_params, dilated_norm_params, expansion_norm_params, aspp_point, aspp_rates, aspp_pool, branch_norms, pooling_norm_params, aspp_project, projection_norm_params, head_weight, head_bias, log_vars, crop_boxes, seg_labels, depth_target, normal_target):
    row_ids = jnp.arange(HEIGHT, dtype=jnp.int32)
    col_ids = jnp.arange(WIDTH, dtype=jnp.int32)
    inside_rows = (row_ids[None, :] >= crop_boxes[:, 0:1]) & (row_ids[None, :] < crop_boxes[:, 0:1] + crop_boxes[:, 2:3])
    inside_cols = (col_ids[None, :] >= crop_boxes[:, 1:2]) & (col_ids[None, :] < crop_boxes[:, 1:2] + crop_boxes[:, 3:4])
    valid = (inside_rows[:, :, None] & inside_cols[:, None, :]).astype(jnp.float32)
    pixel_number_count = jnp.sum(valid)
    image_areas = lax.optimization_barrier(jnp.sum(valid, axis=(1, 2)))
    params = tuple((tensor.astype(jnp.float32) for tensor in (trunk_input, conv_reduce, conv_dilated, conv_expand, reduction_norm_params, dilated_norm_params, expansion_norm_params, aspp_point, aspp_rates, aspp_pool, branch_norms, pooling_norm_params, aspp_project, projection_norm_params, head_weight, head_bias, log_vars)))

    def objective_of(*tensors):
        return forward(tensors, valid, pixel_number_count, image_areas, seg_labels, depth_target, normal_target)
    total_loss, pullback, features = jax.vjp(objective_of, *params, has_aux=True)
    gradients = pullback(jnp.ones((), jnp.float32))
    return (features.astype(jnp.bfloat16), total_loss, gradients[0], gradients[1], gradients[2], gradients[3], gradients[4], gradients[5], gradients[6], gradients[7], gradients[8], gradients[9], gradients[10], gradients[11], gradients[12], gradients[13], gradients[14], gradients[15], gradients[16])
```

```python
import jax
import jax.numpy as jnp
from jax import lax
from jax.experimental import pallas as pl
from jax.experimental.pallas import tpu as pltpu
from jax.sharding import PartitionSpec as P

EPS = 1e-05
HIGH = lax.Precision.HIGHEST
RATES = (12, 24, 36)


def padded(cells, sides, width):
    for axis, dim in sides:
        count = lax.axis_size(axis)
        ends = count - 1
        head = lax.slice_in_dim(cells, 0, width, axis=dim)
        tail = lax.slice_in_dim(cells, cells.shape[dim] - width, cells.shape[dim], axis=dim)
        cells = jnp.concatenate(
            [
                lax.ppermute(tail, axis, [(i, (i + 1) % count) for i in range(ends)]),
                cells,
                lax.ppermute(head, axis, [((i + 1) % count, i) for i in range(ends)]),
            ],
            axis=dim,
        )
    return cells


def shifted_2(block, axis, distance):
    devices = range(lax.axis_size(axis))
    route = [(i - distance, i) for i in devices if i - distance in devices]
    return lax.ppermute(block, axis, route)


def move(tensor, offset, axis_id):
    length = tensor.shape[axis_id]
    if offset == 0:
        return tensor
    widths = [(0, 0)] * tensor.ndim
    if offset > 0:
        widths[axis_id] = (offset, 0)
        return lax.slice_in_dim(jnp.pad(tensor, widths), 0, length, axis=axis_id)
    widths[axis_id] = (0, -offset)
    return lax.slice_in_dim(jnp.pad(tensor, widths), -offset, length - offset, axis=axis_id)


def forward_dot(lhs_arr, rhs_arr):
    return jnp.dot(lhs_arr, rhs_arr, preferred_element_type=jnp.float32)


def backward_dot(grad_arr, kernel):
    return lax.dot_general(
        grad_arr,
        kernel,
        (((grad_arr.ndim - 1,), (1,)), ((), ())),
        preferred_element_type=jnp.float32,
    )


def pixel_dot(source, grad_arr):
    return lax.dot_general(
        source, grad_arr, (((0, 1, 2), (0, 1, 2)), ((), ())), preferred_element_type=jnp.float32
    )


def silu_slope(pre_act):
    sigmoid_v = jax.nn.sigmoid(pre_act)
    return sigmoid_v * (1.0 + pre_act * (1.0 - sigmoid_v))


def widen(tensor):
    return lax.all_gather(tensor, "branch", axis=3, tiled=True)


def narrow(tensor):
    return lax.psum_scatter(
        tensor.astype(jnp.bfloat16), "branch", scatter_dimension=3, tiled=True
    ).astype(jnp.float32)


def pad_rows(tensor):
    return padded(tensor, (("rows", 1),), 4)


def send_down(tensor, hops):
    if hops >= lax.axis_size("rows"):
        return jnp.zeros_like(tensor)
    return shifted_2(tensor, "rows", hops)


def send_up(tensor, hops):
    if hops >= lax.axis_size("rows"):
        return jnp.zeros_like(tensor)
    return shifted_2(tensor, "rows", -hops)


def over_rows(tensor):
    return lax.psum(tensor, "rows")


def norm_ahead_pass(tensor, weight, counted, affine):
    summed = lax.psum(jnp.sum(tensor * weight, axis=0), ("rows", "batch"))
    mean_val = summed / counted
    centered = tensor - mean_val
    spread = lax.psum(jnp.sum(weight * centered * centered, axis=0), ("rows", "batch"))
    variance = spread / counted
    inverse = lax.rsqrt(variance + EPS)
    normed = centered * inverse
    return (affine[0] * normed + affine[1], normed, inverse)


def norm_reverse_pass(grad_out, normed, inverse, weight_all, weight_stat, counted, affine):
    grad_bias, grad_gain = lax.psum(
        (jnp.sum(grad_out * weight_all, axis=0), jnp.sum(grad_out * normed * weight_all, axis=0)),
        ("rows", "batch"),
    )
    gain_row = affine[0]
    grad_in = inverse * (
        gain_row * grad_out - weight_stat / counted * gain_row * (grad_bias + normed * grad_gain)
    )
    return (grad_in, jnp.stack([grad_gain, grad_bias]))


def stacked_taps(kernels, col_tap):
    return jnp.concatenate([kernels[0, col_tap], kernels[1, col_tap], kernels[2, col_tap]], axis=0)


MESH = pl.DeviceIdType.MESH
F32 = jnp.float32
BF16 = jnp.bfloat16
VMEM_LIMIT = 60 * 2**20


class Net:
    def __init__(self, send_sems, recv_sems):
        self.m = lax.axis_index("branch")
        self.r = lax.axis_index("rows")
        self.z = lax.axis_index("batch")
        self.send_sems, self.recv_sems, self.count = send_sems, recv_sems, 0
        self.side = (self.m ^ 1, self.r, self.z)
        self.over = (self.m ^ 2, self.r, self.z)
        self.diagonal = (self.m ^ 3, self.r, self.z)
        self.core = (self.m, 1 - self.r, self.z)
        self.slot = self.r * 4 + self.z
        self.group = [
            (self.m, lax.rem(self.r + i, 2), lax.rem(self.z + j, 4))
            for i in range(2)
            for j in range(4)
            if i or j
        ]

    def send(self, src, dst, device):
        i = self.count
        self.count += 1
        copy = pltpu.make_async_remote_copy(
            src_ref=src,
            dst_ref=dst,
            send_sem=self.send_sems.at[i],
            recv_sem=self.recv_sems.at[i],
            device_id=device,
            device_id_type=MESH,
        )
        copy.start()
        return copy


def greet(peers):
    barrier = pltpu.get_barrier_semaphore()
    for peer in peers:
        pl.semaphore_signal(barrier, inc=1, device_id=peer, device_id_type=MESH)
    pl.semaphore_wait(barrier, len(peers))


def each_rows(total, step, body):
    def run(i, carry):
        body(pl.ds(pl.multiple_of(i * step, step), step))
        return carry

    lax.fori_loop(0, total // step, run, 0)


def lane_block(index, width=128):
    return pl.ds(pl.multiple_of(index * width, width), width)


def wide(tile, width):
    count = width // tile.shape[1]
    return tile if count == 1 else jnp.concatenate([tile] * count, axis=1)


def column_sums(fn, total, width, number):
    step = 16384 // width

    def run(i, sums):
        terms = fn(pl.ds(pl.multiple_of(i * step, step), step))
        return tuple(
            s + jnp.sum(t.reshape(step // 8, 8, width), axis=0) for s, t in zip(sums, terms)
        )

    sums = lax.fori_loop(
        0, total // step, run, tuple(jnp.zeros((8, width), F32) for _ in range(number))
    )
    return [jnp.sum(s, axis=0, keepdims=True) for s in sums]


def fold(row):
    return row + pltpu.roll(wide(row, 128), 64, 1)


def exchange(net, outgoing, incoming):
    copies = [net.send(outgoing, incoming.at[net.slot], peer) for peer in net.group]
    incoming[net.slot] = outgoing[...]
    for copy in copies:
        copy.wait()


def statistics(net, value_ref, mask_ref, outgoing, incoming, counted, folded=False):
    total, width = value_ref.shape
    same = fold if folded else (lambda row: row)
    first, number = column_sums(
        lambda at: (value_ref[at, :] * wide(mask_ref[at, :], width), wide(mask_ref[at, :], width)),
        total,
        width,
        2,
    )
    first, number = same(first), same(number)
    centre = first / jnp.maximum(number, 1.0)

    def squares(at):
        gap = value_ref[at, :] - centre
        return (gap * gap * wide(mask_ref[at, :], width),)

    second = same(column_sums(squares, total, width, 1)[0])
    outgoing[0:1, :] = first
    outgoing[1:2, :] = second
    outgoing[2:3, :] = number
    exchange(net, outgoing, incoming)
    firsts, seconds, numbers = incoming[:, 0, :], incoming[:, 1, :], incoming[:, 2, :]
    mean = jnp.sum(firsts, axis=0, keepdims=True) / counted
    drift = firsts / jnp.maximum(numbers, 1.0) - mean
    variance = jnp.sum(seconds + numbers * drift * drift, axis=0, keepdims=True) / counted
    return mean, lax.rsqrt(variance + EPS)


def gather_blocks(net, part, rows):
    pieces, size = 4, rows // 4
    own, side, over = net.m, net.m ^ 1, net.m ^ 2

    def at(i):
        return pl.ds(i * size, size)

    to_side, to_over = [], []
    for i in range(pieces):
        j = pieces - 1 - i
        to_side.append(net.send(part(own, at(i)), part(own, at(i)), net.side))
        to_over.append(net.send(part(own, at(j)), part(own, at(j)), net.over))
    passed = []
    for i in range(pieces):
        j = pieces - 1 - i
        to_side[i].wait_recv()
        if i < pieces // 2:
            passed.append(net.send(part(side, at(i)), part(side, at(i)), net.over))
        to_over[i].wait_recv()
        if i < pieces // 2:
            passed.append(net.send(part(over, at(j)), part(over, at(j)), net.side))
    for copy in to_side + to_over:
        copy.wait_send()
    for copy in passed:
        copy.wait()


def sum_scatter(net, part, bufs, out):
    far, to_side, to_over, far_side, far_over, from_side, from_over = bufs
    rows, width = out.shape
    half, step = rows // 2, 16384 // width
    head, tail = pl.ds(0, half), pl.ds(half, half)
    across, side, over = net.m ^ 3, net.m ^ 1, net.m ^ 2

    def fill(target, index, base):
        def body(at):
            rows_at = pl.ds(pl.multiple_of(at.start + base, step), step)
            target[rows_at, :] = part[index, rows_at, :].astype(BF16)

        each_rows(half, step, body)

    def combine(target, index, base, arrived):
        def body(at):
            rows_at = pl.ds(pl.multiple_of(at.start + base, step), step)
            target[rows_at, :] = (part[index, rows_at, :] + arrived[at, :].astype(F32)).astype(BF16)

        each_rows(half, step, body)

    fill(far, across, 0)
    first = net.send(far.at[head], far_side, net.side)
    fill(far, across, half)
    second = net.send(far.at[tail], far_over, net.over)
    fill(to_side, side, 0)
    third = net.send(to_side.at[head], from_side.at[head], net.side)
    fill(to_over, over, half)
    fourth = net.send(to_over.at[tail], from_over.at[tail], net.over)
    second.wait_recv()
    combine(to_side, side, half, far_over)
    fifth = net.send(to_side.at[tail], from_side.at[tail], net.side)
    first.wait_recv()
    combine(to_over, over, 0, far_side)
    sixth = net.send(to_over.at[head], from_over.at[head], net.over)
    for copy in (third, fourth, fifth, sixth):
        copy.wait_recv()

    def body(at):
        out[at, :] = (
            part[net.m, at, :] + from_side[at, :].astype(F32) + from_over[at, :].astype(F32)
        )

    each_rows(rows, step, body)
    for copy in (first, second, third, fourth, fifth, sixth):
        copy.wait_send()


def scatter_buffers(rows, width):
    whole, half = pltpu.VMEM((rows, width), BF16), pltpu.VMEM((rows // 2, width), BF16)
    return [whole, whole, whole, half, half, whole, whole]


def sigmoid(u):
    return 0.5 * jnp.tanh(0.5 * u) + 0.5


def slope(u):
    s = sigmoid(u)
    return s * (1.0 + u * (1.0 - s))


def mm(a, b):
    return jnp.dot(a, b, preferred_element_type=F32)


def mm_t(a, b):
    return lax.dot_general(a, b, (((1,), (1,)), ((), ())), preferred_element_type=F32)


def tm_m(a, b):
    return lax.dot_general(a, b, (((0,), (0,)), ((), ())), preferred_element_type=F32)


def bottleneck_forward(
    x, w_reduce, w_dilated, w_expand, mask, affine_1, affine_2, affine_3, counted_ref,
    reduced, stats_1, hidden, dilated, stats_2, hidden_two, expanded, stats_3, trunk,
    w_taps, part, b0, b1, b2, b3, b4, b5, b6, left, right, out_1, in_1, out_2, in_2, out_3, in_3,
    local_sems, send_sems, recv_sems,
):
    net = Net(send_sems, recv_sems)
    counted = counted_ref[0, 0]
    loads = []
    for i in range(3):
        for j in range(3):
            loads.append(
                pltpu.make_async_copy(
                    w_dilated.at[i, j],
                    w_taps.at[i, :, pl.ds(j * 128, 128)],
                    local_sems.at[i * 3 + j],
                )
            )
            loads[-1].start()
    greet([net.side, net.over] + net.group)

    def reduce_rows(at):
        cells = x[at, :]
        for b in range(4):
            part[b, at, :] = mm(cells, w_reduce[b])

    each_rows(1536, 384, reduce_rows)
    sum_scatter(net, part, (b0, b1, b2, b3, b4, b5, b6), reduced)
    mean, inverse = statistics(net, reduced, mask, out_1, in_1, counted)
    stats_1[0:1, :] = mean
    stats_1[1:2, :] = inverse
    stats_1[2:8, :] = jnp.zeros((6, 128), F32)

    def activate_1(at):
        u = affine_1[0:1, :] * ((reduced[at, :] - mean) * inverse) + affine_1[1:2, :]
        rows_at = pl.ds(pl.multiple_of(at.start + 512, 128), 128)
        hidden[rows_at, lane_block(net.m)] = (u * sigmoid(u)).astype(BF16)

    each_rows(1536, 128, activate_1)
    hidden[pl.ds(pl.multiple_of(net.r * 2048, 128), 512), :] = jnp.zeros((512, 512), BF16)

    def hidden_block(b, at):
        return hidden.at[pl.ds(at.start + 512, at.size), lane_block(b)]

    gather_blocks(net, hidden_block, 1536)
    halo = net.send(
        hidden.at[pl.ds(pl.multiple_of(1536 - net.r * 1024, 128), 512)],
        hidden.at[pl.ds(pl.multiple_of(net.r * 2048, 128), 512)],
        net.core,
    )
    for side in (left, right):
        side[:, 0:8, :] = jnp.zeros((12, 8, 128), F32)
        side[:, 136:144, :] = jnp.zeros((12, 8, 128), F32)
    for load in loads:
        load.wait()
    halo.wait()

    def dilated_rows(i, carry):
        total = 0.0
        for tap in range(3):
            rows_at = pl.ds(pl.multiple_of((i * 3 + 4 * tap) * 128, 128), 384)
            total = total + mm(hidden[rows_at, :], w_taps[tap])
        dilated[pl.ds(pl.multiple_of(i * 384, 128), 384), :] = total[:, 128:256]
        left[pl.ds(i * 3, 3), 8:136, :] = total[:, 0:128].reshape(3, 128, 128)
        right[pl.ds(i * 3, 3), 8:136, :] = total[:, 256:384].reshape(3, 128, 128)
        return carry

    lax.fori_loop(0, 4, dilated_rows, 0)

    def add_columns(i, carry):
        at = pl.ds(pl.multiple_of(i * 128, 128), 128)
        dilated[at, :] = dilated[at, :] + left[i, 4:132, :] + right[i, 12:140, :]
        return carry

    lax.fori_loop(0, 12, add_columns, 0)
    mean, inverse = statistics(net, dilated, mask, out_2, in_2, counted)
    stats_2[0:1, :] = mean
    stats_2[1:2, :] = inverse
    stats_2[2:8, :] = jnp.zeros((6, 128), F32)

    def activate_2(at):
        u = affine_2[0:1, :] * ((dilated[at, :] - mean) * inverse) + affine_2[1:2, :]
        hidden_two[at, lane_block(net.m)] = (u * sigmoid(u)).astype(BF16)

    each_rows(1536, 128, activate_2)
    gather_blocks(net, lambda b, at: hidden_two.at[at, lane_block(b)], 1536)

    def expand_rows(at):
        expanded[at, :] = mm(hidden_two[at, :], w_expand[...])

    each_rows(1536, 384, expand_rows)
    mean_3, inverse_3 = statistics(net, expanded, mask, out_3, in_3, counted)
    stats_3[0:1, :] = mean_3
    stats_3[1:2, :] = inverse_3
    stats_3[2:8, :] = jnp.zeros((6, 512), F32)

    def activate_3(at):
        u = affine_3[0:1, :] * ((expanded[at, :] - mean_3) * inverse_3) + affine_3[1:2, :]
        u = u + x[at, :].astype(F32)
        trunk[at, :] = (u * sigmoid(u)).astype(BF16)

    each_rows(1536, 32, activate_3)


def call_kernel(body, name, number, args, hbm, outs, scratch, sems):
    vmem = pl.BlockSpec(memory_space=pltpu.VMEM)
    specs = [pl.BlockSpec(memory_space=pl.ANY) if i in hbm else vmem for i in range(len(args))]
    return pl.pallas_call(
        body,
        out_shape=[jax.ShapeDtypeStruct(s, d) for s, d in outs],
        in_specs=specs,
        out_specs=[vmem] * len(outs),
        scratch_shapes=list(scratch)
        + [pltpu.SemaphoreType.DMA((sems,)), pltpu.SemaphoreType.DMA((sems,))],
        name=name,
        compiler_params=pltpu.CompilerParams(
            collective_id=number, has_side_effects=True, vmem_limit_bytes=VMEM_LIMIT
        ),
    )(*args)


def padded_affine(affine):
    return jnp.concatenate([affine, jnp.zeros((6, affine.shape[1]), F32)], axis=0)


def run_bottleneck(x, w_reduce, w_dilated, w_expand, mask, affines, counted):
    return call_kernel(
        bottleneck_forward,
        "bottleneck",
        0,
        [x, w_reduce, w_dilated, w_expand, mask, *[padded_affine(a) for a in affines], counted],
        (2,),
        [
            ((1536, 128), F32),
            ((8, 128), F32),
            ((2560, 512), BF16),
            ((1536, 128), F32),
            ((8, 128), F32),
            ((1536, 512), BF16),
            ((1536, 512), F32),
            ((8, 512), F32),
            ((1536, 512), BF16),
        ],
        [
            pltpu.VMEM((3, 512, 384), BF16),
            pltpu.VMEM((4, 1536, 128), F32),
            *scatter_buffers(1536, 128),
            pltpu.VMEM((12, 144, 128), F32),
            pltpu.VMEM((12, 144, 128), F32),
            pltpu.VMEM((8, 128), F32),
            pltpu.VMEM((8, 8, 128), F32),
            pltpu.VMEM((8, 128), F32),
            pltpu.VMEM((8, 8, 128), F32),
            pltpu.VMEM((8, 512), F32),
            pltpu.VMEM((8, 8, 512), F32),
            pltpu.SemaphoreType.DMA((9,)),
        ],
        64,
    )


def local(
    trunk_input,
    conv_reduce,
    conv_dilated,
    conv_expand,
    reduction_norm_params,
    dilated_norm_params,
    expansion_norm_params,
    aspp_point,
    aspp_rates,
    aspp_pool,
    branch_norms,
    pooling_norm_params,
    aspp_project,
    projection_norm_params,
    head_weight,
    head_bias,
    log_vars,
    crop_boxes,
    seg_labels,
    depth_target,
    normal_target,
):
    image_inputs, tile_row_count, frame_columns, quarter = trunk_input.shape
    pixels = image_inputs * tile_row_count * frame_columns
    branch_part = aspp_point.shape[0]
    branch_total = lax.axis_size("branch")
    row_portion = 1.0 / lax.axis_size("rows")
    image_overall_count = float(crop_boxes.shape[0])
    first_image = lax.axis_index("batch") * image_inputs
    first_row = lax.axis_index("rows") * tile_row_count
    my_boxes = lax.dynamic_slice_in_dim(crop_boxes, first_image, image_inputs, 0)
    row_ids = first_row + jnp.arange(tile_row_count, dtype=jnp.int32)
    col_ids = jnp.arange(frame_columns, dtype=jnp.int32)
    inside_rows = (row_ids[None, :] >= my_boxes[:, 0:1]) & (
        row_ids[None, :] < my_boxes[:, 0:1] + my_boxes[:, 2:3]
    )
    inside_cols = (col_ids[None, :] >= my_boxes[:, 1:2]) & (
        col_ids[None, :] < my_boxes[:, 1:2] + my_boxes[:, 3:4]
    )
    valid_mask = (inside_rows[:, :, None] & inside_cols[:, None, :]).astype(jnp.float32)
    mask_column_vector = valid_mask.reshape(pixels, 1)
    mask_flat = valid_mask.reshape(pixels)
    pixel_number_count = jnp.sum((crop_boxes[:, 2] * crop_boxes[:, 3]).astype(jnp.float32))
    image_areas = (my_boxes[:, 2] * my_boxes[:, 3]).astype(jnp.float32)
    input_full = widen(trunk_input)
    reduced_output = forward_dot(input_full, conv_reduce).reshape(pixels, -1)
    normalized_first, standardized_first, inverse_deviation_first = norm_ahead_pass(
        reduced_output, mask_column_vector, pixel_number_count, reduction_norm_params
    )
    hidden_one = (
        jax.nn.silu(normalized_first)
        .astype(jnp.bfloat16)
        .reshape(image_inputs, tile_row_count, frame_columns, -1)
    )
    hidden_full = widen(pad_rows(hidden_one))
    dilated_out = 0.0
    for row_tap in range(3):
        band = hidden_full[:, 4 * row_tap : 4 * row_tap + tile_row_count]
        for col_tap in range(3):
            dilated_out = dilated_out + forward_dot(
                move(band, -(col_tap - 1) * 4, 2), conv_dilated[row_tap, col_tap]
            )
    normalized_second, standardized_second, inverse_deviation_second = norm_ahead_pass(
        dilated_out.reshape(pixels, -1), mask_column_vector, pixel_number_count, dilated_norm_params
    )
    hidden_two = (
        jax.nn.silu(normalized_second)
        .astype(jnp.bfloat16)
        .reshape(image_inputs, tile_row_count, frame_columns, -1)
    )
    hidden_two_full = widen(hidden_two)
    expanded_output = forward_dot(hidden_two_full, conv_expand).reshape(pixels, -1)
    normalized_third, standardized_third, inverse_deviation_third = norm_ahead_pass(
        expanded_output, mask_column_vector, pixel_number_count, expansion_norm_params
    )
    residual_sum = normalized_third + trunk_input.reshape(pixels, -1).astype(jnp.float32)
    trunk_out = (
        jax.nn.silu(residual_sum)
        .astype(jnp.bfloat16)
        .reshape(image_inputs, tile_row_count, frame_columns, quarter)
    )
    trunk_full = widen(trunk_out)
    branch_outs = [backward_dot(trunk_full, aspp_point)]
    for branch_id in range(3):
        dilation = RATES[branch_id]
        hops = dilation // tile_row_count
        partials = [0.0, 0.0, 0.0]
        for col_tap in range(3):
            shifted = move(trunk_full, -(col_tap - 1) * dilation, 2)
            products = backward_dot(shifted, stacked_taps(aspp_rates[branch_id], col_tap))
            for row_tap in range(3):
                partials[row_tap] = (
                    partials[row_tap]
                    + products[..., row_tap * branch_part : (row_tap + 1) * branch_part]
                )
        upper = send_down(partials[0].astype(jnp.bfloat16), hops).astype(jnp.float32)
        lower_part = send_up(partials[2].astype(jnp.bfloat16), hops).astype(jnp.float32)
        branch_outs.append(partials[1] + upper + lower_part)
    spatial_flattened = jnp.stack(branch_outs, axis=3).reshape(pixels, -1)
    branch_gain_bias = branch_norms.reshape(2, -1)
    normalized_spatial, standardized_spatial, inverse_deviation_spatial = norm_ahead_pass(
        spatial_flattened, mask_column_vector, pixel_number_count, branch_gain_bias
    )
    spatial_act = (
        jax.nn.silu(normalized_spatial)
        .astype(jnp.bfloat16)
        .reshape(image_inputs, tile_row_count, frame_columns, 4, branch_part)
    )
    pooled_local = lax.dot_general(
        valid_mask.astype(jnp.bfloat16),
        trunk_full,
        (((1, 2), (1, 2)), ((0,), (0,))),
        preferred_element_type=jnp.float32,
    )
    pooled = (over_rows(pooled_local) / image_areas[:, None]).astype(jnp.bfloat16)
    pooling_convolution = backward_dot(pooled, aspp_pool)
    normalized_poolbranch, standardized_poolbranch, inverse_deviation_poolbranch = norm_ahead_pass(
        pooling_convolution, row_portion, image_overall_count, pooling_norm_params
    )
    pool_act = jax.nn.silu(normalized_poolbranch).astype(jnp.bfloat16)
    pool_wide = jnp.broadcast_to(
        pool_act[:, None, None, None, :],
        (image_inputs, tile_row_count, frame_columns, 1, branch_part),
    )
    concat = jnp.concatenate([spatial_act, pool_wide], axis=3)
    concat_flat = widen(concat).reshape(pixels, -1)
    proj_kernel = (
        aspp_project.reshape(branch_part, 5, branch_total, branch_part)
        .transpose(0, 2, 1, 3)
        .reshape(branch_part, 5 * branch_total * branch_part)
    )
    projected_output = backward_dot(concat_flat, proj_kernel)
    normalized_projector, standardized_projector, inverse_deviation_projector = norm_ahead_pass(
        projected_output, mask_column_vector, pixel_number_count, projection_norm_params
    )
    features = (
        jax.nn.silu(normalized_projector)
        .astype(jnp.bfloat16)
        .reshape(image_inputs, tile_row_count, frame_columns, -1)
    )
    features_wide = widen(features).reshape(pixels, -1).astype(jnp.float32)
    head_wide = head_weight.astype(jnp.float32)
    logits = jnp.dot(features_wide, head_wide, precision=HIGH) + head_bias
    classes = head_bias.shape[0] - 3
    seg_logits = logits[:, :classes]
    labels_flat = seg_labels.reshape(pixels)
    classes_hot = (labels_flat[:, None] == jnp.arange(classes, dtype=jnp.int32)[None, :]).astype(
        jnp.float32
    )
    cross = jax.nn.logsumexp(seg_logits, axis=1) - jnp.sum(seg_logits * classes_hot, axis=1)
    depth_gap = logits[:, classes] - depth_target.reshape(pixels)
    smooth_abs = jnp.sqrt(depth_gap * depth_gap + 1.0)
    normal_gap = logits[:, classes + 1 :] - jnp.moveaxis(normal_target, 1, 3).reshape(pixels, 2)
    local_losses = jnp.stack(
        [
            jnp.sum(mask_flat * cross),
            jnp.sum(mask_flat * (smooth_abs - 1.0)),
            jnp.sum(mask_flat * jnp.sum(normal_gap * normal_gap, axis=1)),
        ]
    )
    task_weights = jnp.exp(-log_vars)
    grad_seg = (jax.nn.softmax(seg_logits, axis=1) - classes_hot) * (
        task_weights[0] / pixel_number_count * mask_flat
    )[:, None]
    grad_depth = depth_gap / smooth_abs * (task_weights[1] / pixel_number_count * mask_flat)
    grad_normal = 2.0 * normal_gap * (task_weights[2] / pixel_number_count * mask_flat)[:, None]
    grad_logits = jnp.concatenate([grad_seg, grad_depth[:, None], grad_normal], axis=1)
    head_local = lax.dot_general(
        features_wide, grad_logits, (((0,), (0,)), ((), ())), precision=HIGH
    )
    loss_parts, grad_head_weight, grad_head_bias = lax.psum(
        (local_losses, head_local, jnp.sum(grad_logits, axis=0)), ("rows", "batch")
    )
    task_losses = loss_parts / pixel_number_count
    total_loss = jnp.sum(task_weights * task_losses + log_vars)
    grad_log_vars = 1.0 - task_weights * task_losses
    grad_features = jnp.dot(grad_logits, head_wide.T, precision=HIGH)
    my_features_grad = lax.dynamic_slice_in_dim(
        grad_features, lax.axis_index("branch") * branch_part, branch_part, 1
    )
    gradient_before_projector = my_features_grad * silu_slope(normalized_projector)
    grad_proj_in, grad_project_norm = norm_reverse_pass(
        gradient_before_projector,
        standardized_projector,
        inverse_deviation_projector,
        1.0,
        mask_column_vector,
        pixel_number_count,
        projection_norm_params,
    )
    grad_proj_low = grad_proj_in.astype(jnp.bfloat16)
    proj_kernel_grad = lax.dot_general(
        grad_proj_low, concat_flat, (((0,), (0,)), ((), ())), preferred_element_type=jnp.float32
    )
    grad_project_local = (
        proj_kernel_grad.reshape(branch_part, branch_total, 5, branch_part)
        .transpose(0, 2, 1, 3)
        .reshape(branch_part, 5, branch_total * branch_part)
    )
    concat_grad = forward_dot(grad_proj_low, proj_kernel).reshape(
        image_inputs, tile_row_count, frame_columns, -1
    )
    concat_grad = narrow(concat_grad).reshape(pixels, 5, branch_part)
    pool_grad_img = over_rows(
        jnp.sum(concat_grad[:, 4, :].reshape(image_inputs, -1, branch_part), axis=1)
    )
    gradient_before_poolbranch = pool_grad_img * silu_slope(normalized_poolbranch)
    grad_pool_conv, grad_pool_norm = norm_reverse_pass(
        gradient_before_poolbranch,
        standardized_poolbranch,
        inverse_deviation_poolbranch,
        row_portion,
        1.0,
        image_overall_count,
        pooling_norm_params,
    )
    pool_conv_low = grad_pool_conv.astype(jnp.bfloat16)
    grad_pool_local = (
        lax.dot_general(
            pool_conv_low, pooled, (((0,), (0,)), ((), ())), preferred_element_type=jnp.float32
        )
        * row_portion
    )
    pooled_grad = forward_dot(pool_conv_low, aspp_pool)
    gradient_before_spatialbranch = concat_grad[:, :4, :].reshape(pixels, -1) * silu_slope(
        normalized_spatial
    )
    grad_spatial, branch_norm_grad = norm_reverse_pass(
        gradient_before_spatialbranch,
        standardized_spatial,
        inverse_deviation_spatial,
        1.0,
        mask_column_vector,
        pixel_number_count,
        branch_gain_bias,
    )
    grad_branch_norms = branch_norm_grad.reshape(2, 4, branch_part)
    spatial_low = grad_spatial.astype(jnp.bfloat16).reshape(
        image_inputs, tile_row_count, frame_columns, 4, branch_part
    )
    point_grad = spatial_low[:, :, :, 0]
    grad_point_local = pixel_dot(point_grad, trunk_full)
    trunk_grad = forward_dot(point_grad, aspp_point)
    trunk_grad = (
        trunk_grad + valid_mask[..., None] * (pooled_grad / image_areas[:, None])[:, None, None, :]
    )
    rate_grads = []
    for branch_id in range(3):
        dilation = RATES[branch_id]
        hops = dilation // tile_row_count
        centre = spatial_low[:, :, :, branch_id + 1]
        grad_taps = jnp.concatenate(
            [send_up(centre, hops), centre, send_down(centre, hops)], axis=3
        )
        per_col = []
        for col_tap in range(3):
            shifted = move(trunk_full, -(col_tap - 1) * dilation, 2)
            per_col.append(pixel_dot(grad_taps, shifted))
            tap_grad = forward_dot(grad_taps, stacked_taps(aspp_rates[branch_id], col_tap))
            trunk_grad = trunk_grad + move(tap_grad, (col_tap - 1) * dilation, 2)
        col_stack = jnp.stack(per_col, axis=0).reshape(3, 3, branch_part, -1)
        rate_grads.append(col_stack.transpose(1, 0, 2, 3))
    grad_rates_local = jnp.stack(rate_grads, axis=0)
    trunk_own = narrow(trunk_grad).reshape(pixels, -1)
    gradient_shortcut = trunk_own * silu_slope(residual_sum)
    grad_expanded, grad_norm_expand = norm_reverse_pass(
        gradient_shortcut,
        standardized_third,
        inverse_deviation_third,
        1.0,
        mask_column_vector,
        pixel_number_count,
        expansion_norm_params,
    )
    expanded_low = grad_expanded.astype(jnp.bfloat16).reshape(
        image_inputs, tile_row_count, frame_columns, -1
    )
    grad_expand_local = pixel_dot(hidden_two_full, expanded_low)
    hidden_two_grad = narrow(backward_dot(expanded_low, conv_expand)).reshape(pixels, -1)
    gradient_before_second = hidden_two_grad * silu_slope(normalized_second)
    gradient_dilated_input, gradient_dilated_norm = norm_reverse_pass(
        gradient_before_second,
        standardized_second,
        inverse_deviation_second,
        1.0,
        mask_column_vector,
        pixel_number_count,
        dilated_norm_params,
    )
    dilated_lowprec = gradient_dilated_input.astype(jnp.bfloat16).reshape(
        image_inputs, tile_row_count, frame_columns, -1
    )
    dilated_padded = pad_rows(dilated_lowprec)
    hidden_one_grad = 0.0
    kernel_grads = []
    for row_tap in range(3):
        band = hidden_full[:, 4 * row_tap : 4 * row_tap + tile_row_count]
        grad_band = dilated_padded[:, 8 - 4 * row_tap : 8 - 4 * row_tap + tile_row_count]
        for col_tap in range(3):
            kernel_grads.append(pixel_dot(move(band, -(col_tap - 1) * 4, 2), dilated_lowprec))
            hidden_one_grad = hidden_one_grad + backward_dot(
                move(grad_band, (col_tap - 1) * 4, 2), conv_dilated[row_tap, col_tap]
            )
    grad_dilated_local = jnp.stack(kernel_grads, axis=0).reshape(3, 3, hidden_full.shape[3], -1)
    hidden_one_own = narrow(hidden_one_grad).reshape(pixels, -1)
    gradient_before_first = hidden_one_own * silu_slope(normalized_first)
    grad_reduced, grad_norm_reduce = norm_reverse_pass(
        gradient_before_first,
        standardized_first,
        inverse_deviation_first,
        1.0,
        mask_column_vector,
        pixel_number_count,
        reduction_norm_params,
    )
    reduced_low = grad_reduced.astype(jnp.bfloat16).reshape(
        image_inputs, tile_row_count, frame_columns, -1
    )
    grad_reduce_local = pixel_dot(input_full, reduced_low)
    input_grad = narrow(backward_dot(reduced_low, conv_reduce))
    grad_input = input_grad + gradient_shortcut.reshape(
        image_inputs, tile_row_count, frame_columns, quarter
    )
    grad_reduce, grad_dilated, grad_expand, grad_point, grad_rates, grad_pool, grad_project = (
        lax.psum_scatter(grad_reduce_local, ("rows", "batch"), scatter_dimension=0, tiled=True),
        lax.psum_scatter(grad_dilated_local, ("rows", "batch"), scatter_dimension=2, tiled=True),
        lax.psum_scatter(grad_expand_local, ("rows", "batch"), scatter_dimension=0, tiled=True),
        lax.psum_scatter(grad_point_local, ("rows", "batch"), scatter_dimension=1, tiled=True),
        lax.psum_scatter(grad_rates_local, ("rows", "batch"), scatter_dimension=4, tiled=True),
        lax.psum_scatter(grad_pool_local, ("rows", "batch"), scatter_dimension=1, tiled=True),
        lax.psum_scatter(grad_project_local, ("rows", "batch"), scatter_dimension=2, tiled=True),
    )
    return (
        features,
        total_loss,
        grad_input,
        grad_reduce,
        grad_dilated,
        grad_expand,
        grad_norm_reduce,
        gradient_dilated_norm,
        grad_norm_expand,
        grad_point,
        grad_rates,
        grad_pool,
        grad_branch_norms,
        grad_pool_norm,
        grad_project,
        grad_project_norm,
        grad_head_weight,
        grad_head_bias,
        grad_log_vars,
    )


def fast_local(
    trunk_input,
    conv_reduce,
    conv_dilated,
    conv_expand,
    reduction_norm_params,
    dilated_norm_params,
    expansion_norm_params,
    aspp_point,
    aspp_rates,
    aspp_pool,
    branch_norms,
    pooling_norm_params,
    aspp_project,
    projection_norm_params,
    head_weight,
    head_bias,
    log_vars,
    crop_boxes,
    seg_labels,
    depth_target,
    normal_target,
):
    image_inputs, tile_row_count, frame_columns, quarter = trunk_input.shape
    pixels = image_inputs * tile_row_count * frame_columns
    branch_part = aspp_point.shape[0]
    branch_total = lax.axis_size("branch")
    row_portion = 1.0 / lax.axis_size("rows")
    image_overall_count = float(crop_boxes.shape[0])
    first_image = lax.axis_index("batch") * image_inputs
    first_row = lax.axis_index("rows") * tile_row_count
    my_boxes = lax.dynamic_slice_in_dim(crop_boxes, first_image, image_inputs, 0)
    row_ids = first_row + jnp.arange(tile_row_count, dtype=jnp.int32)
    col_ids = jnp.arange(frame_columns, dtype=jnp.int32)
    inside_rows = (row_ids[None, :] >= my_boxes[:, 0:1]) & (
        row_ids[None, :] < my_boxes[:, 0:1] + my_boxes[:, 2:3]
    )
    inside_cols = (col_ids[None, :] >= my_boxes[:, 1:2]) & (
        col_ids[None, :] < my_boxes[:, 1:2] + my_boxes[:, 3:4]
    )
    valid_mask = (inside_rows[:, :, None] & inside_cols[:, None, :]).astype(jnp.float32)
    mask_column_vector = valid_mask.reshape(pixels, 1)
    mask_flat = valid_mask.reshape(pixels)
    pixel_number_count = jnp.sum((crop_boxes[:, 2] * crop_boxes[:, 3]).astype(jnp.float32))
    image_areas = (my_boxes[:, 2] * my_boxes[:, 3]).astype(jnp.float32)
    x_own = trunk_input.reshape(pixels, quarter)
    w_reduce = lax.all_to_all(conv_reduce.reshape(4, 512, 128), "branch", 0, 0)
    mask_lanes = jnp.broadcast_to(mask_column_vector, (pixels, 128))
    counted_cell = pixel_number_count.reshape(1, 1)
    (
        reduced_output,
        stats_1,
        hidden_pad,
        dilated_out,
        stats_2,
        hidden_two_full,
        expanded_output,
        stats_3,
        trunk_out,
    ) = run_bottleneck(
        x_own,
        w_reduce,
        conv_dilated,
        conv_expand,
        mask_lanes,
        (reduction_norm_params, dilated_norm_params, expansion_norm_params),
        counted_cell,
    )
    input_full = widen(trunk_input)
    hidden_full = hidden_pad.reshape(1, 20, 128, 512)
    hidden_two_full = hidden_two_full.reshape(1, 12, 128, 512)

    def again(value, stats, affine):
        inverse = stats[1]
        normed = (value - stats[0]) * inverse
        return affine[0] * normed + affine[1], normed, inverse

    normalized_first, standardized_first, inverse_deviation_first = again(
        reduced_output, stats_1, reduction_norm_params
    )
    normalized_second, standardized_second, inverse_deviation_second = again(
        dilated_out, stats_2, dilated_norm_params
    )
    normalized_third, standardized_third, inverse_deviation_third = again(
        expanded_output, stats_3, expansion_norm_params
    )
    residual_sum = normalized_third + x_own.astype(jnp.float32)
    trunk_full = widen(trunk_out.reshape(image_inputs, tile_row_count, frame_columns, quarter))
    branch_outs = [backward_dot(trunk_full, aspp_point)]
    for branch_id in range(3):
        dilation = RATES[branch_id]
        hops = dilation // tile_row_count
        partials = [0.0, 0.0, 0.0]
        for col_tap in range(3):
            shifted = move(trunk_full, -(col_tap - 1) * dilation, 2)
            products = backward_dot(shifted, stacked_taps(aspp_rates[branch_id], col_tap))
            for row_tap in range(3):
                partials[row_tap] = (
                    partials[row_tap]
                    + products[..., row_tap * branch_part : (row_tap + 1) * branch_part]
                )
        upper = send_down(partials[0].astype(jnp.bfloat16), hops).astype(jnp.float32)
        lower_part = send_up(partials[2].astype(jnp.bfloat16), hops).astype(jnp.float32)
        branch_outs.append(partials[1] + upper + lower_part)
    spatial_flattened = jnp.stack(branch_outs, axis=3).reshape(pixels, -1)
    branch_gain_bias = branch_norms.reshape(2, -1)
    normalized_spatial, standardized_spatial, inverse_deviation_spatial = norm_ahead_pass(
        spatial_flattened, mask_column_vector, pixel_number_count, branch_gain_bias
    )
    spatial_act = (
        jax.nn.silu(normalized_spatial)
        .astype(jnp.bfloat16)
        .reshape(image_inputs, tile_row_count, frame_columns, 4, branch_part)
    )
    pooled_local = lax.dot_general(
        valid_mask.astype(jnp.bfloat16),
        trunk_full,
        (((1, 2), (1, 2)), ((0,), (0,))),
        preferred_element_type=jnp.float32,
    )
    pooled = (over_rows(pooled_local) / image_areas[:, None]).astype(jnp.bfloat16)
    pooling_convolution = backward_dot(pooled, aspp_pool)
    normalized_poolbranch, standardized_poolbranch, inverse_deviation_poolbranch = norm_ahead_pass(
        pooling_convolution, row_portion, image_overall_count, pooling_norm_params
    )
    pool_act = jax.nn.silu(normalized_poolbranch).astype(jnp.bfloat16)
    pool_wide = jnp.broadcast_to(
        pool_act[:, None, None, None, :],
        (image_inputs, tile_row_count, frame_columns, 1, branch_part),
    )
    concat = jnp.concatenate([spatial_act, pool_wide], axis=3)
    concat_flat = widen(concat).reshape(pixels, -1)
    proj_kernel = (
        aspp_project.reshape(branch_part, 5, branch_total, branch_part)
        .transpose(0, 2, 1, 3)
        .reshape(branch_part, 5 * branch_total * branch_part)
    )
    projected_output = backward_dot(concat_flat, proj_kernel)
    normalized_projector, standardized_projector, inverse_deviation_projector = norm_ahead_pass(
        projected_output, mask_column_vector, pixel_number_count, projection_norm_params
    )
    features = (
        jax.nn.silu(normalized_projector)
        .astype(jnp.bfloat16)
        .reshape(image_inputs, tile_row_count, frame_columns, -1)
    )
    features_wide = widen(features).reshape(pixels, -1).astype(jnp.float32)
    head_wide = head_weight.astype(jnp.float32)
    logits = jnp.dot(features_wide, head_wide, precision=HIGH) + head_bias
    classes = head_bias.shape[0] - 3
    seg_logits = logits[:, :classes]
    labels_flat = seg_labels.reshape(pixels)
    classes_hot = (labels_flat[:, None] == jnp.arange(classes, dtype=jnp.int32)[None, :]).astype(
        jnp.float32
    )
    cross = jax.nn.logsumexp(seg_logits, axis=1) - jnp.sum(seg_logits * classes_hot, axis=1)
    depth_gap = logits[:, classes] - depth_target.reshape(pixels)
    smooth_abs = jnp.sqrt(depth_gap * depth_gap + 1.0)
    normal_gap = logits[:, classes + 1 :] - jnp.moveaxis(normal_target, 1, 3).reshape(pixels, 2)
    local_losses = jnp.stack(
        [
            jnp.sum(mask_flat * cross),
            jnp.sum(mask_flat * (smooth_abs - 1.0)),
            jnp.sum(mask_flat * jnp.sum(normal_gap * normal_gap, axis=1)),
        ]
    )
    task_weights = jnp.exp(-log_vars)
    grad_seg = (jax.nn.softmax(seg_logits, axis=1) - classes_hot) * (
        task_weights[0] / pixel_number_count * mask_flat
    )[:, None]
    grad_depth = depth_gap / smooth_abs * (task_weights[1] / pixel_number_count * mask_flat)
    grad_normal = 2.0 * normal_gap * (task_weights[2] / pixel_number_count * mask_flat)[:, None]
    grad_logits = jnp.concatenate([grad_seg, grad_depth[:, None], grad_normal], axis=1)
    head_local = lax.dot_general(
        features_wide, grad_logits, (((0,), (0,)), ((), ())), precision=HIGH
    )
    loss_parts, grad_head_weight, grad_head_bias = lax.psum(
        (local_losses, head_local, jnp.sum(grad_logits, axis=0)), ("rows", "batch")
    )
    task_losses = loss_parts / pixel_number_count
    total_loss = jnp.sum(task_weights * task_losses + log_vars)
    grad_log_vars = 1.0 - task_weights * task_losses
    grad_features = jnp.dot(grad_logits, head_wide.T, precision=HIGH)
    my_features_grad = lax.dynamic_slice_in_dim(
        grad_features, lax.axis_index("branch") * branch_part, branch_part, 1
    )
    gradient_before_projector = my_features_grad * silu_slope(normalized_projector)
    grad_proj_in, grad_project_norm = norm_reverse_pass(
        gradient_before_projector,
        standardized_projector,
        inverse_deviation_projector,
        1.0,
        mask_column_vector,
        pixel_number_count,
        projection_norm_params,
    )
    grad_proj_low = grad_proj_in.astype(jnp.bfloat16)
    proj_kernel_grad = lax.dot_general(
        grad_proj_low, concat_flat, (((0,), (0,)), ((), ())), preferred_element_type=jnp.float32
    )
    grad_project_local = (
        proj_kernel_grad.reshape(branch_part, branch_total, 5, branch_part)
        .transpose(0, 2, 1, 3)
        .reshape(branch_part, 5, branch_total * branch_part)
    )
    concat_grad = forward_dot(grad_proj_low, proj_kernel).reshape(
        image_inputs, tile_row_count, frame_columns, -1
    )
    concat_grad = narrow(concat_grad).reshape(pixels, 5, branch_part)
    pool_grad_img = over_rows(
        jnp.sum(concat_grad[:, 4, :].reshape(image_inputs, -1, branch_part), axis=1)
    )
    gradient_before_poolbranch = pool_grad_img * silu_slope(normalized_poolbranch)
    grad_pool_conv, grad_pool_norm = norm_reverse_pass(
        gradient_before_poolbranch,
        standardized_poolbranch,
        inverse_deviation_poolbranch,
        row_portion,
        1.0,
        image_overall_count,
        pooling_norm_params,
    )
    pool_conv_low = grad_pool_conv.astype(jnp.bfloat16)
    grad_pool_local = (
        lax.dot_general(
            pool_conv_low, pooled, (((0,), (0,)), ((), ())), preferred_element_type=jnp.float32
        )
        * row_portion
    )
    pooled_grad = forward_dot(pool_conv_low, aspp_pool)
    gradient_before_spatialbranch = concat_grad[:, :4, :].reshape(pixels, -1) * silu_slope(
        normalized_spatial
    )
    grad_spatial, branch_norm_grad = norm_reverse_pass(
        gradient_before_spatialbranch,
        standardized_spatial,
        inverse_deviation_spatial,
        1.0,
        mask_column_vector,
        pixel_number_count,
        branch_gain_bias,
    )
    grad_branch_norms = branch_norm_grad.reshape(2, 4, branch_part)
    spatial_low = grad_spatial.astype(jnp.bfloat16).reshape(
        image_inputs, tile_row_count, frame_columns, 4, branch_part
    )
    point_grad = spatial_low[:, :, :, 0]
    grad_point_local = pixel_dot(point_grad, trunk_full)
    trunk_grad = forward_dot(point_grad, aspp_point)
    trunk_grad = (
        trunk_grad + valid_mask[..., None] * (pooled_grad / image_areas[:, None])[:, None, None, :]
    )
    rate_grads = []
    for branch_id in range(3):
        dilation = RATES[branch_id]
        hops = dilation // tile_row_count
        centre = spatial_low[:, :, :, branch_id + 1]
        grad_taps = jnp.concatenate(
            [send_up(centre, hops), centre, send_down(centre, hops)], axis=3
        )
        per_col = []
        for col_tap in range(3):
            shifted = move(trunk_full, -(col_tap - 1) * dilation, 2)
            per_col.append(pixel_dot(grad_taps, shifted))
            tap_grad = forward_dot(grad_taps, stacked_taps(aspp_rates[branch_id], col_tap))
            trunk_grad = trunk_grad + move(tap_grad, (col_tap - 1) * dilation, 2)
        col_stack = jnp.stack(per_col, axis=0).reshape(3, 3, branch_part, -1)
        rate_grads.append(col_stack.transpose(1, 0, 2, 3))
    grad_rates_local = jnp.stack(rate_grads, axis=0)
    trunk_own = narrow(trunk_grad).reshape(pixels, -1)
    gradient_shortcut = trunk_own * silu_slope(residual_sum)
    grad_expanded, grad_norm_expand = norm_reverse_pass(
        gradient_shortcut,
        standardized_third,
        inverse_deviation_third,
        1.0,
        mask_column_vector,
        pixel_number_count,
        expansion_norm_params,
    )
    expanded_low = grad_expanded.astype(jnp.bfloat16).reshape(
        image_inputs, tile_row_count, frame_columns, -1
    )
    grad_expand_local = pixel_dot(hidden_two_full, expanded_low)
    hidden_two_grad = narrow(backward_dot(expanded_low, conv_expand)).reshape(pixels, -1)
    gradient_before_second = hidden_two_grad * silu_slope(normalized_second)
    gradient_dilated_input, gradient_dilated_norm = norm_reverse_pass(
        gradient_before_second,
        standardized_second,
        inverse_deviation_second,
        1.0,
        mask_column_vector,
        pixel_number_count,
        dilated_norm_params,
    )
    dilated_lowprec = gradient_dilated_input.astype(jnp.bfloat16).reshape(
        image_inputs, tile_row_count, frame_columns, -1
    )
    dilated_padded = pad_rows(dilated_lowprec)
    hidden_one_grad = 0.0
    kernel_grads = []
    for row_tap in range(3):
        band = hidden_full[:, 4 * row_tap : 4 * row_tap + tile_row_count]
        grad_band = dilated_padded[:, 8 - 4 * row_tap : 8 - 4 * row_tap + tile_row_count]
        for col_tap in range(3):
            kernel_grads.append(pixel_dot(move(band, -(col_tap - 1) * 4, 2), dilated_lowprec))
            hidden_one_grad = hidden_one_grad + backward_dot(
                move(grad_band, (col_tap - 1) * 4, 2), conv_dilated[row_tap, col_tap]
            )
    grad_dilated_local = jnp.stack(kernel_grads, axis=0).reshape(3, 3, hidden_full.shape[3], -1)
    hidden_one_own = narrow(hidden_one_grad).reshape(pixels, -1)
    gradient_before_first = hidden_one_own * silu_slope(normalized_first)
    grad_reduced, grad_norm_reduce = norm_reverse_pass(
        gradient_before_first,
        standardized_first,
        inverse_deviation_first,
        1.0,
        mask_column_vector,
        pixel_number_count,
        reduction_norm_params,
    )
    reduced_low = grad_reduced.astype(jnp.bfloat16).reshape(
        image_inputs, tile_row_count, frame_columns, -1
    )
    grad_reduce_local = pixel_dot(input_full, reduced_low)
    input_grad = narrow(backward_dot(reduced_low, conv_reduce))
    grad_input = input_grad + gradient_shortcut.reshape(
        image_inputs, tile_row_count, frame_columns, quarter
    )
    grad_reduce, grad_dilated, grad_expand, grad_point, grad_rates, grad_pool, grad_project = (
        lax.psum_scatter(grad_reduce_local, ("rows", "batch"), scatter_dimension=0, tiled=True),
        lax.psum_scatter(grad_dilated_local, ("rows", "batch"), scatter_dimension=2, tiled=True),
        lax.psum_scatter(grad_expand_local, ("rows", "batch"), scatter_dimension=0, tiled=True),
        lax.psum_scatter(grad_point_local, ("rows", "batch"), scatter_dimension=1, tiled=True),
        lax.psum_scatter(grad_rates_local, ("rows", "batch"), scatter_dimension=4, tiled=True),
        lax.psum_scatter(grad_pool_local, ("rows", "batch"), scatter_dimension=1, tiled=True),
        lax.psum_scatter(grad_project_local, ("rows", "batch"), scatter_dimension=2, tiled=True),
    )
    return (
        features,
        total_loss,
        grad_input,
        grad_reduce,
        grad_dilated,
        grad_expand,
        grad_norm_reduce,
        gradient_dilated_norm,
        grad_norm_expand,
        grad_point,
        grad_rates,
        grad_pool,
        grad_branch_norms,
        grad_pool_norm,
        grad_project,
        grad_project_norm,
        grad_head_weight,
        grad_head_bias,
        grad_log_vars,
    )


def solution(mesh):
    in_specs = (
        P("batch", "rows", None, "branch"),
        P(None, "branch"),
        P(None, None, None, "branch"),
        P(None, "branch"),
        P(None, "branch"),
        P(None, "branch"),
        P(None, "branch"),
        P("branch", None),
        P(None, None, None, "branch", None),
        P("branch", None),
        P(None, None, "branch"),
        P(None, "branch"),
        P("branch", None, None),
        P(None, "branch"),
        P(),
        P(),
        P(),
        P(),
        P("batch", "rows", None),
        P("batch", "rows", None),
        P("batch", None, "rows", None),
    )
    out_specs = (
        P("batch", "rows", None, "branch"),
        P(),
        P("batch", "rows", None, "branch"),
        P(("rows", "batch"), "branch"),
        P(None, None, ("rows", "batch"), "branch"),
        P(("rows", "batch"), "branch"),
        P(None, "branch"),
        P(None, "branch"),
        P(None, "branch"),
        P("branch", ("rows", "batch")),
        P(None, None, None, "branch", ("rows", "batch")),
        P("branch", ("rows", "batch")),
        P(None, None, "branch"),
        P(None, "branch"),
        P("branch", None, ("rows", "batch")),
        P(None, "branch"),
        P(),
        P(),
        P(),
    )
    small = (mesh.shape["branch"], mesh.shape["rows"], mesh.shape["batch"]) == (4, 2, 4)
    body = fast_local if small else local
    return jax.shard_map(body, mesh=mesh, in_specs=in_specs, out_specs=out_specs, check_vma=False)
```

```python
import types

import jax
import jax.numpy as jnp
from jax import lax
from jax.experimental import pallas as pl
from jax.experimental.pallas import tpu as pltpu
from jax.sharding import PartitionSpec as P

EPS = 1e-05
HIGH = lax.Precision.HIGHEST
RATES = (12, 24, 36)


def padded(cells, sides, width):
    for axis, dim in sides:
        count = lax.axis_size(axis)
        ends = count - 1
        head = lax.slice_in_dim(cells, 0, width, axis=dim)
        tail = lax.slice_in_dim(cells, cells.shape[dim] - width, cells.shape[dim], axis=dim)
        cells = jnp.concatenate(
            [
                lax.ppermute(tail, axis, [(i, (i + 1) % count) for i in range(ends)]),
                cells,
                lax.ppermute(head, axis, [((i + 1) % count, i) for i in range(ends)]),
            ],
            axis=dim,
        )
    return cells


def shifted_2(block, axis, distance):
    devices = range(lax.axis_size(axis))
    route = [(i - distance, i) for i in devices if i - distance in devices]
    return lax.ppermute(block, axis, route)


def move(tensor, offset, axis_id):
    length = tensor.shape[axis_id]
    if offset == 0:
        return tensor
    widths = [(0, 0)] * tensor.ndim
    if offset > 0:
        widths[axis_id] = (offset, 0)
        return lax.slice_in_dim(jnp.pad(tensor, widths), 0, length, axis=axis_id)
    widths[axis_id] = (0, -offset)
    return lax.slice_in_dim(jnp.pad(tensor, widths), -offset, length - offset, axis=axis_id)


def forward_dot(lhs_arr, rhs_arr):
    return jnp.dot(lhs_arr, rhs_arr, preferred_element_type=jnp.float32)


def backward_dot(grad_arr, kernel):
    return lax.dot_general(
        grad_arr,
        kernel,
        (((grad_arr.ndim - 1,), (1,)), ((), ())),
        preferred_element_type=jnp.float32,
    )


def pixel_dot(source, grad_arr):
    return lax.dot_general(
        source, grad_arr, (((0, 1, 2), (0, 1, 2)), ((), ())), preferred_element_type=jnp.float32
    )


def silu_slope(pre_act):
    sigmoid_v = jax.nn.sigmoid(pre_act)
    return sigmoid_v * (1.0 + pre_act * (1.0 - sigmoid_v))


def widen(tensor):
    return lax.all_gather(tensor, "branch", axis=3, tiled=True)


def narrow(tensor):
    return lax.psum_scatter(
        tensor.astype(jnp.bfloat16), "branch", scatter_dimension=3, tiled=True
    ).astype(jnp.float32)


def pad_rows(tensor):
    return padded(tensor, (("rows", 1),), 4)


def send_down(tensor, hops):
    if hops >= lax.axis_size("rows"):
        return jnp.zeros_like(tensor)
    return shifted_2(tensor, "rows", hops)


def send_up(tensor, hops):
    if hops >= lax.axis_size("rows"):
        return jnp.zeros_like(tensor)
    return shifted_2(tensor, "rows", -hops)


def over_rows(tensor):
    return lax.psum(tensor, "rows")


def norm_ahead_pass(tensor, weight, counted, affine):
    summed = lax.psum(jnp.sum(tensor * weight, axis=0), ("rows", "batch"))
    mean_val = summed / counted
    centered = tensor - mean_val
    spread = lax.psum(jnp.sum(weight * centered * centered, axis=0), ("rows", "batch"))
    variance = spread / counted
    inverse = lax.rsqrt(variance + EPS)
    normed = centered * inverse
    return (affine[0] * normed + affine[1], normed, inverse)


def norm_reverse_pass(grad_out, normed, inverse, weight_all, weight_stat, counted, affine):
    grad_bias, grad_gain = lax.psum(
        (jnp.sum(grad_out * weight_all, axis=0), jnp.sum(grad_out * normed * weight_all, axis=0)),
        ("rows", "batch"),
    )
    gain_row = affine[0]
    grad_in = inverse * (
        gain_row * grad_out - weight_stat / counted * gain_row * (grad_bias + normed * grad_gain)
    )
    return (grad_in, jnp.stack([grad_gain, grad_bias]))


def stacked_taps(kernels, col_tap):
    return jnp.concatenate([kernels[0, col_tap], kernels[1, col_tap], kernels[2, col_tap]], axis=0)


MESH = pl.DeviceIdType.MESH
F32 = jnp.float32
BF16 = jnp.bfloat16
VMEM_LIMIT = 60 * 2**20


class Net:
    def __init__(self, send_sems, recv_sems):
        self.m = lax.axis_index("branch")
        self.r = lax.axis_index("rows")
        self.z = lax.axis_index("batch")
        self.send_sems, self.recv_sems, self.count = send_sems, recv_sems, 0
        self.side = (self.m ^ 1, self.r, self.z)
        self.over = (self.m ^ 2, self.r, self.z)
        self.diagonal = (self.m ^ 3, self.r, self.z)
        self.core = (self.m, 1 - self.r, self.z)
        self.slot = self.r * 4 + self.z
        self.group = [
            (self.m, lax.rem(self.r + i, 2), lax.rem(self.z + j, 4))
            for i in range(2)
            for j in range(4)
            if i or j
        ]

    def send(self, src, dst, device):
        i = self.count
        self.count += 1
        copy = pltpu.make_async_remote_copy(
            src_ref=src,
            dst_ref=dst,
            send_sem=self.send_sems.at[i],
            recv_sem=self.recv_sems.at[i],
            device_id=device,
            device_id_type=MESH,
        )
        copy.start()
        return copy


def greet(peers, perhaps=None):
    barrier = pltpu.get_barrier_semaphore()
    for peer in peers:
        pl.semaphore_signal(barrier, inc=1, device_id=peer, device_id_type=MESH)
    if perhaps is None:
        pl.semaphore_wait(barrier, len(peers))
        return
    peer, there = perhaps

    @pl.when(there)
    def _():
        pl.semaphore_signal(barrier, inc=1, device_id=peer, device_id_type=MESH)

    pl.semaphore_wait(barrier, len(peers) + there.astype(jnp.int32))


def each_rows(total, step, body):
    def run(i, carry):
        body(pl.ds(pl.multiple_of(i * step, step), step))
        return carry

    lax.fori_loop(0, total // step, run, 0)


def lane_block(index, width=128):
    return pl.ds(pl.multiple_of(index * width, width), width)


def wide(tile, width):
    count = width // tile.shape[1]
    return tile if count == 1 else jnp.concatenate([tile] * count, axis=1)


def column_sums(fn, total, width, number):
    step = 16384 // width

    def run(i, sums):
        terms = fn(pl.ds(pl.multiple_of(i * step, step), step))
        return tuple(
            s + jnp.sum(t.reshape(step // 8, 8, width), axis=0) for s, t in zip(sums, terms)
        )

    sums = lax.fori_loop(
        0, total // step, run, tuple(jnp.zeros((8, width), F32) for _ in range(number))
    )
    return [jnp.sum(s, axis=0, keepdims=True) for s in sums]


def fold(row):
    return row + pltpu.roll(wide(row, 128), 64, 1)


def exchange(net, outgoing, incoming, meanwhile=None):
    copies = [net.send(outgoing, incoming.at[net.slot], peer) for peer in net.group]
    incoming[net.slot] = outgoing[...]
    if meanwhile is not None:
        meanwhile()
    for copy in copies:
        copy.wait()


def statistics(net, value_ref, mask_ref, outgoing, incoming, counted, folded=False, extra=None):
    total, width = value_ref.shape
    same = fold if folded else (lambda row: row)
    first, number = column_sums(
        lambda at: (value_ref[at, :] * wide(mask_ref[at, :], width), wide(mask_ref[at, :], width)),
        total,
        width,
        2,
    )
    first, number = same(first), same(number)
    centre = first / jnp.maximum(number, 1.0)

    def squares(at):
        gap = value_ref[at, :] - centre
        return (gap * gap * wide(mask_ref[at, :], width),)

    second = same(column_sums(squares, total, width, 1)[0])
    outgoing[0:1, :] = first
    outgoing[1:2, :] = second
    outgoing[2:3, :] = number
    if extra is not None:
        outgoing[3:4, :] = extra
    exchange(net, outgoing, incoming)
    firsts, seconds, numbers = incoming[:, 0, :], incoming[:, 1, :], incoming[:, 2, :]
    mean = jnp.sum(firsts, axis=0, keepdims=True) / counted
    drift = firsts / jnp.maximum(numbers, 1.0) - mean
    variance = jnp.sum(seconds + numbers * drift * drift, axis=0, keepdims=True) / counted
    return mean, lax.rsqrt(variance + EPS)


def gather_blocks(net, part, rows):
    pieces, size = 4, rows // 4
    own, side, over = net.m, net.m ^ 1, net.m ^ 2

    def at(i):
        return pl.ds(i * size, size)

    to_side, to_over = [], []
    for i in range(pieces):
        j = pieces - 1 - i
        to_side.append(net.send(part(own, at(i)), part(own, at(i)), net.side))
        to_over.append(net.send(part(own, at(j)), part(own, at(j)), net.over))
    passed = []
    for i in range(pieces):
        j = pieces - 1 - i
        to_side[i].wait_recv()
        if i < pieces // 2:
            passed.append(net.send(part(side, at(i)), part(side, at(i)), net.over))
        to_over[i].wait_recv()
        if i < pieces // 2:
            passed.append(net.send(part(over, at(j)), part(over, at(j)), net.side))
    for copy in to_side + to_over:
        copy.wait_send()
    for copy in passed:
        copy.wait()


def sum_scatter(net, part, bufs, out, meanwhile=None):
    far, to_side, to_over, far_side, far_over, from_side, from_over = bufs
    rows, width = out.shape
    half, step = rows // 2, 16384 // width
    head, tail = pl.ds(0, half), pl.ds(half, half)
    across, side, over = net.m ^ 3, net.m ^ 1, net.m ^ 2

    def fill(target, index, base):
        def body(at):
            rows_at = pl.ds(pl.multiple_of(at.start + base, step), step)
            target[rows_at, :] = part[index, rows_at, :].astype(BF16)

        each_rows(half, step, body)

    def combine(target, index, base, arrived):
        def body(at):
            rows_at = pl.ds(pl.multiple_of(at.start + base, step), step)
            target[rows_at, :] = (part[index, rows_at, :] + arrived[at, :].astype(F32)).astype(BF16)

        each_rows(half, step, body)

    fill(far, across, 0)
    first = net.send(far.at[head], far_side, net.side)
    fill(far, across, half)
    second = net.send(far.at[tail], far_over, net.over)
    fill(to_side, side, 0)
    third = net.send(to_side.at[head], from_side.at[head], net.side)
    fill(to_over, over, half)
    fourth = net.send(to_over.at[tail], from_over.at[tail], net.over)
    second.wait_recv()
    combine(to_side, side, half, far_over)
    fifth = net.send(to_side.at[tail], from_side.at[tail], net.side)
    first.wait_recv()
    combine(to_over, over, 0, far_side)
    sixth = net.send(to_over.at[head], from_over.at[head], net.over)
    if meanwhile is not None:
        meanwhile()
    for copy in (third, fourth, fifth, sixth):
        copy.wait_recv()

    def body(at):
        out[at, :] = (
            part[net.m, at, :] + from_side[at, :].astype(F32) + from_over[at, :].astype(F32)
        )

    each_rows(rows, step, body)
    for copy in (first, second, third, fourth, fifth, sixth):
        copy.wait_send()


def gradient_sums(
    net, grad_ref, normed, outgoing, incoming, folded=False, extra=None, meanwhile=None
):
    total, width = grad_ref.shape
    same = fold if folded else (lambda row: row)
    bias, gain = column_sums(
        lambda at: (grad_ref[at, :], grad_ref[at, :] * normed(at)), total, width, 2
    )
    outgoing[0:1, :] = same(bias)
    outgoing[1:2, :] = same(gain)
    if extra is not None:
        outgoing[2:3, :] = extra
    exchange(net, outgoing, incoming, meanwhile)
    bias = jnp.sum(incoming[:, 0, :], axis=0, keepdims=True)
    gain = jnp.sum(incoming[:, 1, :], axis=0, keepdims=True)
    return bias, gain


def keep_rows(ref, first, second):
    width = ref.shape[1]
    ref[0:1, :] = first
    ref[1:2, :] = second
    ref[2:8, :] = jnp.zeros((6, width), F32)


def pair(a, b):
    low = lax.broadcasted_iota(jnp.int32, (a.shape[0], 128), 1) < 64
    results = []
    for g in range(2):
        left, right = a[:, g * 128 : g * 128 + 128], b[:, g * 128 : g * 128 + 128]
        results.append(jnp.where(low, left, pltpu.roll(right, 64, 1)))
        results.append(jnp.where(low, pltpu.roll(left, 64, 1), right))
    return results


def unpair(blocks):
    low = lax.broadcasted_iota(jnp.int32, blocks[0].shape, 1) < 64
    firsts, seconds = [], []
    for g in range(2):
        left, right = blocks[2 * g], blocks[2 * g + 1]
        firsts.append(jnp.where(low, left, pltpu.roll(right, 64, 1)))
        seconds.append(jnp.where(low, pltpu.roll(left, 64, 1), right))
    return jnp.concatenate(firsts, axis=1), jnp.concatenate(seconds, axis=1)


def split_three(row):
    high = row.astype(BF16)
    rest = row - high.astype(F32)
    middle = rest.astype(BF16)
    low = (rest - middle.astype(F32)).astype(BF16)
    return high, middle, low


def zero_margins(ref, side, width):
    rows, _, lanes = ref.shape
    ref[:, 0:side, :] = jnp.zeros((rows, side, lanes), F32)
    ref[:, side + width : 2 * side + width, :] = jnp.zeros((rows, side, lanes), F32)


def scatter_buffers(rows, width):
    whole, half = pltpu.VMEM((rows, width), BF16), pltpu.VMEM((rows // 2, width), BF16)
    return [whole, whole, whole, half, half, whole, whole]


def sigmoid(u):
    return 0.5 * jnp.tanh(0.5 * u) + 0.5


def slope(u):
    s = sigmoid(u)
    return s * (1.0 + u * (1.0 - s))


def mm(a, b):
    return jnp.dot(a, b, preferred_element_type=F32)


def mm_t(a, b):
    return lax.dot_general(a, b, (((1,), (1,)), ((), ())), preferred_element_type=F32)


def tm_m(a, b):
    return lax.dot_general(a, b, (((0,), (0,)), ((), ())), preferred_element_type=F32)


def call_kernel(body, name, number, args, outs, scratch, sems, hbm=(), smem=("boxes",)):
    vmem, anywhere = pl.BlockSpec(memory_space=pltpu.VMEM), pl.BlockSpec(memory_space=pl.ANY)
    names = [*args, *outs, *scratch]
    places = {name: anywhere for name in hbm}
    places.update({name: pl.BlockSpec(memory_space=pltpu.SMEM) for name in smem})

    def kernel(*refs):
        k = types.SimpleNamespace(**dict(zip(names, refs)))
        body(Net(refs[-2], refs[-1]), k)

    results = pl.pallas_call(
        kernel,
        out_shape=[jax.ShapeDtypeStruct(s, d) for s, d in outs.values()],
        in_specs=[places.get(name, vmem) for name in args],
        out_specs=[places.get(name, vmem) for name in outs],
        scratch_shapes=list(scratch.values())
        + [pltpu.SemaphoreType.DMA((sems,)), pltpu.SemaphoreType.DMA((sems,))],
        name=name,
        compiler_params=pltpu.CompilerParams(
            collective_id=number, has_side_effects=True, vmem_limit_bytes=VMEM_LIMIT
        ),
    )(*args.values())
    return types.SimpleNamespace(**dict(zip(outs, results)))


def pixel_count(boxes):
    total = boxes[0, 2] * boxes[0, 3]
    for b in range(1, 4):
        total = total + boxes[b, 2] * boxes[b, 3]
    return total.astype(F32)


def exchange_scratch(label, width):
    return {
        f"out_{label}": pltpu.VMEM((8, width), F32),
        f"in_{label}": pltpu.VMEM((8, 8, width), F32),
    }


def scatter_scratch(label, rows, width):
    return {f"{label}_{i}": b for i, b in enumerate(scatter_buffers(rows, width))}


def scatter_refs(k, label):
    return [getattr(k, f"{label}_{i}") for i in range(7)]


def load_taps(k):
    loads = []
    for i in range(3):
        for j in range(3):
            loads.append(
                pltpu.make_async_copy(
                    k.w_dilated.at[i, j],
                    k.w_taps.at[i, :, pl.ds(j * 128, 128)],
                    k.local_sems.at[i * 3 + j],
                )
            )
            loads[-1].start()
    return loads


def send_halo(net, padded):
    lanes = padded.shape[1]
    padded[pl.ds(pl.multiple_of(net.r * 2048, 128), 512), :] = jnp.zeros((512, lanes), BF16)
    return net.send(
        padded.at[pl.ds(pl.multiple_of(1536 - net.r * 1024, 128), 512)],
        padded.at[pl.ds(pl.multiple_of(net.r * 2048, 128), 512)],
        net.core,
    )


def bottleneck_forward(net, k):
    counted = pixel_count(k.boxes)
    loads = load_taps(k)
    own_reduce = pltpu.make_async_copy(
        k.conv_reduce.at[lane_block(net.m, 512)], k.w_reduce.at[net.m], k.local_sems.at[9]
    )
    own_reduce.start()
    greet([net.side, net.over, net.diagonal] + net.group)
    branches = [(net.m ^ 3, net.diagonal), (net.m ^ 1, net.side), (net.m ^ 2, net.over)]
    arrivals = [
        net.send(k.conv_reduce.at[lane_block(b, 512)], k.w_reduce.at[net.m], peer)
        for b, peer in branches
    ]

    top, left_edge = k.boxes[net.z, 0], k.boxes[net.z, 1]
    bottom, right_edge = top + k.boxes[net.z, 2], left_edge + k.boxes[net.z, 3]
    column = lax.broadcasted_iota(jnp.int32, (128, 128), 0)
    column_inside = jnp.where((column >= left_edge) & (column < right_edge), 1.0, 0.0)

    def mask_rows(i, carry):
        row = jnp.full((128, 128), net.r * 12 + i, jnp.int32)
        inside = jnp.where((row >= top) & (row < bottom), column_inside, 0.0)
        k.mask[pl.ds(pl.multiple_of(i * 128, 128), 128), :] = inside
        return carry

    lax.fori_loop(0, 12, mask_rows, 0)

    def reduce_for(b):
        def reduce_rows(at):
            k.part[b, at, :] = mm(k.x[at, :], k.w_reduce[b])

        each_rows(1536, 384, reduce_rows)

    own_reduce.wait()
    reduce_for(net.m)
    arrivals[1].wait()
    reduce_for(net.m ^ 1)
    arrivals[2].wait()
    reduce_for(net.m ^ 2)
    arrivals[0].wait()
    reduce_for(net.m ^ 3)
    sum_scatter(net, k.part, scatter_refs(k, "sum"), k.reduced)

    half = pl.ds(pl.multiple_of(net.r * 32, 32), 32)
    late = []

    def weight_block(kind, b):
        lanes = lane_block(b, 512)
        if kind == "edge":
            return k.aspp_rates.at[0, 2 * net.r, :, :, lanes], k.w_pyramid.at[pl.ds(10, 3), net.m]
        if kind == "point":
            return k.aspp_point.at[half, lanes], k.w_pyramid.at[0, net.m, half]
        if kind == "project":
            return k.project.at[half], k.w_project.at[net.m, half]
        return (
            k.aspp_rates.at[kind, 1, :, half, lanes],
            k.w_pyramid.at[pl.ds(1 + 3 * kind, 3), net.m, half],
        )

    def spread_weights(*kinds):
        for kind in kinds:
            src, dst = weight_block(kind, net.m)
            late.append(pltpu.make_async_copy(src, dst, k.local_sems.at[10 + len(late) // 4]))
            late[-1].start()
            for b, peer in branches:
                src, dst = weight_block(kind, b)
                late.append(net.send(src, dst, peer))

    spread_weights("edge")
    mean, inverse = statistics(net, k.reduced, k.mask, k.out_1, k.in_1, counted)
    keep_rows(k.stats_1, mean, inverse)

    def activate_1(at):
        u = k.affine_1[0:1, :] * ((k.reduced[at, :] - mean) * inverse) + k.affine_1[1:2, :]
        rows_at = pl.ds(pl.multiple_of(at.start + 512, 128), 128)
        k.hidden[rows_at, lane_block(net.m)] = (u * sigmoid(u)).astype(BF16)

    each_rows(1536, 128, activate_1)
    gather_blocks(
        net, lambda b, at: k.hidden.at[pl.ds(at.start + 512, at.size), lane_block(b)], 1536
    )
    halo = send_halo(net, k.hidden)
    spread_weights("project", "point", 0)
    zero_margins(k.left, 8, 128)
    zero_margins(k.right, 8, 128)
    for load in loads:
        load.wait()
    halo.wait()

    def dilated_rows(i, carry):
        total = 0.0
        for tap in range(3):
            rows_at = pl.ds(pl.multiple_of((i * 3 + 4 * tap) * 128, 128), 384)
            total = total + mm(k.hidden[rows_at, :], k.w_taps[tap])
        k.dilated[pl.ds(pl.multiple_of(i * 384, 128), 384), :] = total[:, 128:256]
        k.left[pl.ds(i * 3, 3), 8:136, :] = total[:, 0:128].reshape(3, 128, 128)
        k.right[pl.ds(i * 3, 3), 8:136, :] = total[:, 256:384].reshape(3, 128, 128)
        return carry

    lax.fori_loop(0, 4, dilated_rows, 0)

    def add_columns(i, carry):
        at = pl.ds(pl.multiple_of(i * 128, 128), 128)
        k.dilated[at, :] = k.dilated[at, :] + k.left[i, 4:132, :] + k.right[i, 12:140, :]
        return carry

    lax.fori_loop(0, 12, add_columns, 0)
    mean_2, inverse_2 = statistics(net, k.dilated, k.mask, k.out_2, k.in_2, counted)
    keep_rows(k.stats_2, mean_2, inverse_2)

    def activate_2(at):
        u = k.affine_2[0:1, :] * ((k.dilated[at, :] - mean_2) * inverse_2) + k.affine_2[1:2, :]
        k.hidden_two[at, lane_block(net.m)] = (u * sigmoid(u)).astype(BF16)

    each_rows(1536, 128, activate_2)
    gather_blocks(net, lambda b, at: k.hidden_two.at[at, lane_block(b)], 1536)
    spread_weights(1, 2)

    def expand_rows(at):
        k.expanded[at, :] = mm(k.hidden_two[at, :], k.w_expand[...])

    each_rows(1536, 384, expand_rows)
    mean_3, inverse_3 = statistics(net, k.expanded, k.mask, k.out_3, k.in_3, counted)
    keep_rows(k.stats_3, mean_3, inverse_3)
    for copy in late:
        copy.wait()
    swaps = [
        net.send(ref.at[..., half, :], ref.at[..., half, :], net.core)
        for ref in (k.w_pyramid.at[pl.ds(0, 10)], k.w_project)
    ]

    def activate_3(at):
        u = k.affine_3[0:1, :] * ((k.expanded[at, :] - mean_3) * inverse_3) + k.affine_3[1:2, :]
        u = u + k.x[at, :].astype(F32)
        k.trunk[at, :] = (u * sigmoid(u)).astype(BF16)

    each_rows(1536, 32, activate_3)
    for copy in swaps:
        copy.wait()


def run_bottleneck(args):
    return call_kernel(
        bottleneck_forward,
        "bottleneck",
        0,
        args,
        dict(
            mask=((1536, 128), F32),
            w_reduce=((4, 512, 128), BF16),
            w_pyramid=((13, 4, 64, 512), BF16),
            w_project=((4, 64, 1280), BF16),
            reduced=((1536, 128), F32),
            stats_1=((8, 128), F32),
            hidden=((2560, 512), BF16),
            dilated=((1536, 128), F32),
            stats_2=((8, 128), F32),
            hidden_two=((1536, 512), BF16),
            expanded=((1536, 512), F32),
            stats_3=((8, 512), F32),
            trunk=((1536, 512), BF16),
        ),
        dict(
            w_taps=pltpu.VMEM((3, 512, 384), BF16),
            part=pltpu.VMEM((4, 1536, 128), F32),
            **scatter_scratch("sum", 1536, 128),
            left=pltpu.VMEM((12, 144, 128), F32),
            right=pltpu.VMEM((12, 144, 128), F32),
            **exchange_scratch(1, 128),
            **exchange_scratch(2, 128),
            **exchange_scratch(3, 512),
            local_sems=pltpu.SemaphoreType.DMA((16,)),
        ),
        96,
        hbm=(
            "conv_reduce",
            "w_dilated",
            "aspp_point",
            "aspp_rates",
            "project",
            "w_pyramid",
            "w_project",
        ),
    )


def pyramid_forward(net, k):
    counted = pixel_count(k.boxes)
    area = (k.boxes[net.z, 2] * k.boxes[net.z, 3]).astype(F32)
    near = [
        (lax.rem(net.m + a, 4), lax.rem(net.r + b, 2), net.z)
        for a in range(4)
        for b in range(2)
        if a or b
    ]
    greet(net.group + [peer for i, peer in enumerate(near) if i])

    (own_sum,) = column_sums(
        lambda at: (k.trunk[at, :].astype(F32) * wide(k.mask[at, :], 512),), 1536, 512, 1
    )
    k.out_pool[...] = jnp.broadcast_to(own_sum, (8, 512))
    place = net.m * 2 + net.r
    pool_copies = [net.send(k.out_pool, k.in_pool.at[place], peer) for peer in near]
    k.in_pool[place] = k.out_pool[...]

    zero_margins(k.cells, 40, 128)

    def fill(i, carry):
        at = pl.ds(pl.multiple_of(i * 128, 128), 128)
        k.cells[i, 40:168, :] = k.trunk[at, :].astype(F32)
        return carry

    lax.fori_loop(0, 12, fill, 0)

    def shifted(i, offset):
        cells = k.cells[pl.ds(i * 3, 3), 40 + offset : 168 + offset, :]
        return cells.reshape(384, 512).astype(BF16)

    def rows_of(i):
        return pl.ds(pl.multiple_of(i * 384, 128), 384)

    def edge_rows(i, carry):
        total = 0.0
        for j in range(3):
            total = total + mm_t(shifted(i, 12 * (j - 1)), k.w_pyramid[10 + j])
        k.edge_out[rows_of(i), :] = total.astype(BF16)
        return carry

    lax.fori_loop(0, 4, edge_rows, 0)
    edge = net.send(k.edge_out, k.edge_in, net.core)

    def outer_rows(i, carry):
        second, third = 0.0, 0.0
        for j in range(3):
            second = second + mm_t(shifted(i, 24 * (j - 1)), k.w_pyramid[4 + j])
        for j in range(3):
            third = third + mm_t(shifted(i, 36 * (j - 1)), k.w_pyramid[7 + j])
        for b, block in enumerate(pair(second, third)):
            k.part[b, rows_of(i), 128:256] = block
        return carry

    lax.fori_loop(0, 4, outer_rows, 0)
    edge.wait()

    def inner_rows(i, carry):
        point = mm_t(k.trunk[rows_of(i), :], k.w_pyramid[0])
        first = k.edge_in[rows_of(i), :].astype(F32)
        for j in range(3):
            first = first + mm_t(shifted(i, 12 * (j - 1)), k.w_pyramid[1 + j])
        for b, block in enumerate(pair(point, first)):
            k.part[b, rows_of(i), 0:128] = block
        return carry

    lax.fori_loop(0, 4, inner_rows, 0)
    sum_scatter(net, k.part, scatter_refs(k, "sum"), k.branches)

    low_256 = lax.broadcasted_iota(jnp.int32, (256, 128), 1) < 64
    odd = lax.rem(net.m, 2) == 1

    def slot(s):
        lanes = pl.ds(pl.multiple_of(s * 256 + (net.m // 2) * 128, 128), 128)
        block = k.w_slots[:, lanes].astype(F32)
        return jnp.where(odd, pltpu.roll(block, 64, 1), block)

    for s in range(0, 4, 2):
        both = jnp.where(low_256, slot(s), pltpu.roll(slot(s + 1), 64, 1))
        k.w_project[:, s * 64 : s * 64 + 128] = both.astype(BF16)
    k.w_slot[...] = jnp.where(low_256, slot(4), 0.0).astype(BF16)
    k.w_pool[0:64, :] = k.aspp_pool[...]
    k.w_pool[64:128, :] = k.aspp_pool[...]

    for copy in pool_copies:
        copy.wait()
    for b in range(4):
        pooled = (k.in_pool[2 * b, 0:1, :] + k.in_pool[2 * b + 1, 0:1, :]) / area
        k.pooled[:, b * 512 : b * 512 + 512] = jnp.broadcast_to(pooled, (16, 512)).astype(BF16)
    pool_conv = mm_t(k.pooled[...], k.w_pool[...])[0:1, :]
    mean, inverse = statistics(
        net, k.branches, k.mask, k.out_1, k.in_1, counted, extra=wide(pool_conv, 256)
    )
    every = k.in_1[0:4, 3, 0:128]
    pool_mean = jnp.sum(every, axis=0, keepdims=True) / 4.0
    pool_gap = every - pool_mean
    pool_inverse = lax.rsqrt(jnp.sum(pool_gap * pool_gap, axis=0, keepdims=True) / 4.0 + EPS)
    pool_normed = pool_gap * pool_inverse
    pool_gain, pool_bias = k.affine_p[2:3, :], k.affine_p[3:4, :]
    pool_u = pool_gain * pool_normed + pool_bias
    k.rows_scratch[0:4, :] = pool_u * sigmoid(pool_u)
    pool_act = jnp.broadcast_to(k.rows_scratch[pl.ds(net.z, 1), :], (16, 128)).astype(BF16)

    def normed_branch(at):
        return (k.branches[at, :] - mean) * inverse

    gain_b, bias_b = k.affine_b[0:1, :], k.affine_b[1:2, :]

    def activate_branches(at):
        u = gain_b * normed_branch(at) + bias_b
        k.spatial[at, :] = (u * sigmoid(u)).astype(BF16)

    each_rows(1536, 64, activate_branches)

    pool_row = mm_t(pool_act, k.w_slot[...])[0:1, :]

    def project_rows(i, carry):
        at = pl.ds(pl.multiple_of(i * 384, 128), 384)
        below = pl.ds(pl.multiple_of(i * 384 + 768, 128), 384)
        first = mm_t(k.spatial[at, :], k.w_project[...]) + pool_row
        second = mm_t(k.spatial[below, :], k.w_project[...]) + pool_row
        for b, block in enumerate(pair(first, second)):
            k.part_2[b, at, :] = block
        return carry

    lax.fori_loop(0, 2, project_rows, 0)
    low_128 = lax.broadcasted_iota(jnp.int32, (128, 128), 1) < 64

    def pair_mask(at):
        below = pl.ds(pl.multiple_of(at.start + 768, 128), 128)
        k.mask_pairs[at, :] = jnp.where(low_128, k.mask[at, :], k.mask[below, :])

    each_rows(768, 128, pair_mask)
    sum_scatter(net, k.part_2, scatter_refs(k, "sum2"), k.projected)
    mean_p, inverse_p = statistics(
        net, k.projected, k.mask_pairs, k.out_2, k.in_2, counted, folded=True
    )
    gain_p, bias_p = k.affine_p[0:1, :], k.affine_p[1:2, :]

    def normed_projected(at):
        return (k.projected[at, :] - mean_p) * inverse_p

    def activate_projected(at):
        u = gain_p * normed_projected(at) + bias_p
        k.gathered[net.m, at, :] = (u * sigmoid(u)).astype(BF16)

    each_rows(768, 128, activate_projected)
    gather_blocks(net, lambda b, at: k.gathered.at[b, at], 768)

    def spread(source, target):
        def body(at):
            first, second = unpair([source[b, at, :].astype(F32) for b in range(4)])
            target[at, :] = first.astype(BF16)
            target[pl.ds(pl.multiple_of(at.start + 768, 128), 128), :] = second.astype(BF16)

        each_rows(768, 128, body)

    k.features[...] = k.gathered[net.m]
    spread(k.gathered, k.wide_features)

    class_row = lax.broadcasted_iota(jnp.int32, (32, 512), 0)
    is_class, is_depth = class_row < 19, class_row == 19
    is_normal = (class_row == 20) | (class_row == 21)
    bias_column = wide(k.head_columns[0], 512)
    weight_column = wide(k.head_columns[1], 512)
    top_row, left_edge = k.boxes[net.z, 0], k.boxes[net.z, 1]
    bottom_row, right_edge = top_row + k.boxes[net.z, 2], left_edge + k.boxes[net.z, 3]
    lane = lax.broadcasted_iota(jnp.int32, (1, 512), 1)

    def four_rows(rows):
        return jnp.concatenate(rows, axis=1)
    loss_sums, bias_sums = 0.0, 0.0
    for chunk in range(3):
        at = pl.ds(chunk * 512, 512)
        logits = mm_t(k.head[...], k.wide_features[at, :]) + bias_column
        row_id, column_id = net.r * 12 + chunk * 4 + lane // 128, lane % 128
        inside = (row_id >= top_row) & (row_id < bottom_row)
        inside = inside & (column_id >= left_edge) & (column_id < right_edge)
        inside = jnp.where(inside, 1.0, 0.0)
        span = range(chunk * 4, chunk * 4 + 4)
        label = four_rows([k.labels[0, y : y + 1, :] for y in span])
        target = jnp.where(is_depth, four_rows([k.depth[0, y : y + 1, :] for y in span]), 0.0)
        for n in range(2):
            normal = four_rows([k.normal[0, n, y : y + 1, :] for y in span])
            target = jnp.where(class_row == 20 + n, normal, target)
        top = jnp.max(jnp.where(is_class, logits, -jnp.inf), axis=0, keepdims=True)
        powers = jnp.where(is_class, jnp.exp(jnp.where(is_class, logits - top, 0.0)), 0.0)
        power_sum = jnp.sum(powers, axis=0, keepdims=True)
        onehot = jnp.where(class_row == label, 1.0, 0.0)
        cross = jnp.log(power_sum) + top - jnp.sum(logits * onehot, axis=0, keepdims=True)
        gap = logits - target
        smooth = jnp.sqrt(gap * gap + 1.0)
        loss = jnp.where(class_row == 0, cross, 0.0)
        loss = jnp.where(is_depth, smooth - 1.0, loss)
        loss = jnp.where(is_normal, gap * gap, loss) * inside
        grad = jnp.where(is_class, powers / power_sum - onehot, 0.0)
        grad = jnp.where(is_depth, gap / smooth, grad)
        grad = jnp.where(is_normal, 2.0 * gap, grad) * (weight_column * inside)
        loss_sums = loss_sums + jnp.sum(loss, axis=1, keepdims=True)
        bias_sums = bias_sums + jnp.sum(grad, axis=1, keepdims=True)
        high = grad.astype(BF16)
        k.grad_logits[0:32, at] = high
        k.grad_logits[32:64, at] = (grad - high.astype(F32)).astype(BF16)
    head_terms = mm(k.grad_logits[...], k.wide_features[...])
    k.out_head[0:32, :] = head_terms[0:32, :] + head_terms[32:64, :]
    k.out_head[32:64, :] = jnp.broadcast_to(bias_sums, (32, 256))
    k.out_head[64:96, :] = jnp.broadcast_to(loss_sums, (32, 256))
    head_copies = [net.send(k.out_head, k.in_head.at[net.slot], peer) for peer in net.group]
    k.in_head[net.slot] = k.out_head[...]

    own_head = k.head[:, lane_block(net.m // 2)].astype(F32)
    own_head = jnp.where(odd, pltpu.roll(own_head, 64, 1), own_head)
    own_head = jnp.where(low_128[0:32, :], own_head, 0.0)
    head_low = jnp.concatenate([own_head, own_head], axis=0).astype(BF16)
    own_head = pltpu.roll(own_head, 64, 1)
    head_high = jnp.concatenate([own_head, own_head], axis=0).astype(BF16)
    k.grad_p[...] = tm_m(k.grad_logits[:, 0:768], head_low) + tm_m(
        k.grad_logits[:, 768:1536], head_high
    )

    def back_features(at):
        k.grad_p[at, :] = k.grad_p[at, :] * slope(gain_p * normed_projected(at) + bias_p)

    each_rows(768, 128, back_features)
    bias_grad, gain_grad = gradient_sums(
        net, k.grad_p, normed_projected, k.out_3, k.in_3, folded=True
    )
    keep_rows(k.norm_p, gain_grad, bias_grad)

    def back_projected(at):
        shared = k.mask_pairs[at, :] / counted * gain_p
        grad = gain_p * k.grad_p[at, :] - shared * (bias_grad + normed_projected(at) * gain_grad)
        k.gathered_grad[net.m, at, :] = (inverse_p * grad).astype(BF16)

    each_rows(768, 128, back_projected)
    gather_blocks(net, lambda b, at: k.gathered_grad.at[b, at], 768)
    spread(k.gathered_grad, k.grad_projected)
    (pixel_sum,) = column_sums(lambda at: (k.grad_projected[at, :].astype(F32),), 1536, 256, 1)
    row_16 = lax.broadcasted_iota(jnp.int32, (16, 256), 0)
    terms = jnp.zeros((16, 256), F32)
    for i, term in enumerate(split_three(pixel_sum)):
        terms = jnp.where(row_16 == i, term.astype(F32), terms)
    terms = terms.astype(BF16)
    pool_grad = jnp.sum(mm(terms, k.w_slot[...]), axis=0, keepdims=True)

    def project_gradient():
        for b in range(2):
            lanes = slice(b * 128, b * 128 + 128)
            grad = tm_m(k.grad_projected[:, lanes], k.spatial[...])
            k.grad_project[b * 4 : b * 4 + 4, :, 0:256] = grad.reshape(4, 32, 256).astype(BF16)
        grad = tm_m(terms, pool_act)
        k.grad_project[:, :, 256:384] = grad.reshape(8, 32, 128).astype(BF16)

    def back_spatial(at):
        grad = mm(k.grad_projected[at, :], k.w_project[...])
        k.grad_b[at, :] = grad * slope(gain_b * normed_branch(at) + bias_b)

    each_rows(1536, 128, back_spatial)
    bias_grad_b, gain_grad_b = gradient_sums(
        net,
        k.grad_b,
        normed_branch,
        k.out_4,
        k.in_4,
        extra=wide(pool_grad, 256),
        meanwhile=project_gradient,
    )
    keep_rows(k.norm_b, gain_grad_b, bias_grad_b)

    pool_terms = k.in_4[0:4, 2, 0:128] + k.in_4[4:8, 2, 0:128]
    pool_terms = pool_terms * slope(pool_u)
    pool_bias_grad = jnp.sum(pool_terms, axis=0, keepdims=True)
    pool_gain_grad = jnp.sum(pool_terms * pool_normed, axis=0, keepdims=True)
    keep_rows(k.norm_pool, pool_gain_grad, pool_bias_grad)
    pool_back = pool_inverse * (
        pool_gain * pool_terms
        - pool_gain / 4.0 * (pool_bias_grad + pool_normed * pool_gain_grad)
    )
    low = lax.broadcasted_iota(jnp.int32, (4, 128), 1) < 64
    k.rows_scratch[4:8, :] = jnp.where(low, pool_back, 0.0)
    grad_conv = jnp.broadcast_to(k.rows_scratch[pl.ds(net.z + 4, 1), :], (16, 128)).astype(BF16)
    spread_back = mm(grad_conv, k.w_pool[...])[0:8, :]
    for b in range(4):
        k.out_back[b] = spread_back[:, b * 512 : b * 512 + 512]
    back_copies = [
        net.send(k.out_back.at[lax.rem(net.m + a, 4)], k.in_back.at[a], (lax.rem(net.m + a, 4), net.r, net.z))
        for a in range(1, 4)
    ]

    only_first = lax.broadcasted_iota(jnp.int32, (16, 128), 0) == 0
    one_row = jnp.where(only_first, grad_conv.astype(F32) * 0.5, 0.0).astype(BF16)
    for e in range(8):
        grad = tm_m(one_row, k.pooled[:, e * 256 : e * 256 + 256])
        k.grad_pool[e] = grad[0:64, :].astype(BF16)

    def back_branches(at):
        shared = wide(k.mask[at, :], 256) / counted * gain_b
        grad = gain_b * k.grad_b[at, :] - shared * (bias_grad_b + normed_branch(at) * gain_grad_b)
        k.grad_branches[at, :] = (inverse * grad).astype(BF16)

    each_rows(1536, 64, back_branches)
    for copy in back_copies:
        copy.wait()
    k.grad_pooled[...] = (k.out_back[net.m] + k.in_back[1] + k.in_back[2] + k.in_back[3]) / area
    for copy in head_copies:
        copy.wait()
    k.head_sums[...] = jnp.sum(k.in_head[...], axis=0)


def run_pyramid(args):
    return call_kernel(
        pyramid_forward,
        "pyramid",
        1,
        args,
        dict(
            features=((768, 128), BF16),
            norm_p=((8, 128), F32),
            grad_project=((8, 32, 384), BF16),
            grad_pool=((8, 64, 256), BF16),
            norm_b=((8, 256), F32),
            norm_pool=((8, 128), F32),
            grad_branches=((1536, 256), BF16),
            grad_pooled=((8, 512), F32),
            head_sums=((96, 256), F32),
        ),
        dict(
            pooled=pltpu.VMEM((16, 2048), BF16),
            spatial=pltpu.VMEM((1536, 256), BF16),
            grad_projected=pltpu.VMEM((1536, 256), BF16),
            w_project=pltpu.VMEM((256, 256), BF16),
            w_slot=pltpu.VMEM((256, 128), BF16),
            w_pool=pltpu.VMEM((128, 2048), BF16),
            mask_pairs=pltpu.VMEM((768, 128), F32),
            out_pool=pltpu.VMEM((8, 512), F32),
            in_pool=pltpu.VMEM((8, 8, 512), F32),
            cells=pltpu.VMEM((12, 208, 512), F32),
            edge_out=pltpu.VMEM((1536, 256), BF16),
            edge_in=pltpu.VMEM((1536, 256), BF16),
            part=pltpu.VMEM((4, 1536, 256), F32),
            **scatter_scratch("sum", 1536, 256),
            branches=pltpu.VMEM((1536, 256), F32),
            rows_scratch=pltpu.VMEM((8, 128), F32),
            part_2=pltpu.VMEM((4, 768, 128), F32),
            **scatter_scratch("sum2", 768, 128),
            projected=pltpu.VMEM((768, 128), F32),
            gathered=pltpu.VMEM((4, 768, 128), BF16),
            wide_features=pltpu.VMEM((1536, 256), BF16),
            grad_logits=pltpu.VMEM((64, 1536), BF16),
            out_head=pltpu.VMEM((96, 256), F32),
            in_head=pltpu.VMEM((8, 96, 256), F32),
            grad_p=pltpu.VMEM((768, 128), F32),
            gathered_grad=pltpu.VMEM((4, 768, 128), BF16),
            grad_b=pltpu.VMEM((1536, 256), F32),
            out_back=pltpu.VMEM((4, 8, 512), F32),
            in_back=pltpu.VMEM((4, 8, 512), F32),
            **exchange_scratch(1, 256),
            **exchange_scratch(2, 128),
            **exchange_scratch(3, 128),
            **exchange_scratch(4, 256),
        ),
        96,
    )


def core_halves(net, whole, arrived):
    away = pl.ds(pl.multiple_of(4 - 4 * net.r, 4), 4)
    return net.send(whole.at[away], arrived, net.core)


def add_halves(net, whole, arrived, target):
    for z in range(4):
        total = whole[4 * net.r + z].astype(F32) + arrived[z].astype(F32)
        target[z] = total.astype(target.dtype)


def pyramid_backward(net, k):
    counted = pixel_count(k.boxes)
    greet([net.side, net.over] + net.group)
    k.blocks[net.m] = k.grad_branches[...]
    gather_blocks(net, lambda b, at: k.blocks.at[b, at], 1536)
    beside = net.send(k.blocks.at[:, :, pl.ds(0, 128)], k.other, net.core)
    zero_margins(k.cells, 40, 128)

    def rows_of(i, size=384):
        return pl.ds(pl.multiple_of(i * size, 128), size)

    def taps(source, lane, second, rate, base):
        def fill(i, carry):
            blocks = [
                source[b, rows_of(i, 128), lane * 128 : lane * 128 + 128].astype(F32)
                for b in range(4)
            ]
            k.cells[i, 40:168, :] = unpair(blocks)[second]
            return carry

        lax.fori_loop(0, 12, fill, 0)

        def cut(i, carry):
            for j in range(3):
                start = 40 - rate * (j - 1)
                k.shifts[base + j, rows_of(i, 128), :] = k.cells[i, start : start + 128, :].astype(
                    BF16
                )
            return carry

        lax.fori_loop(0, 12, cut, 0)

    def point(i, carry):
        blocks = [k.blocks[b, rows_of(i, 128), 0:128].astype(F32) for b in range(4)]
        k.shifts[0, rows_of(i, 128), :] = unpair(blocks)[0].astype(BF16)
        return carry

    lax.fori_loop(0, 12, point, 0)
    taps(k.blocks, 0, 1, 12, 1)
    taps(k.blocks, 1, 0, 24, 4)
    taps(k.blocks, 1, 1, 36, 7)
    beside.wait()
    taps(k.other, 0, 1, 12, 10)

    def trunk_rows(i, carry):
        total = 0.0
        for t in range(13):
            total = total + mm(k.shifts[t, rows_of(i), :], k.w_pyramid[t])
        k.shortcut[rows_of(i), :] = total
        return carry

    lax.fori_loop(0, 4, trunk_rows, 0)
    mean, inverse = k.stats_3[0:1, :], k.stats_3[1:2, :]
    gain, bias = k.affine_3[0:1, :], k.affine_3[1:2, :]
    pooled = k.grad_pooled[0:1, :]

    def normed(at):
        return (k.expanded[at, :] - mean) * inverse

    def back_trunk(at):
        u = gain * normed(at) + bias + k.x[at, :].astype(F32)
        grad = k.shortcut[at, :] + wide(k.mask[at, :], 512) * pooled
        k.shortcut[at, :] = grad * slope(u)

    each_rows(1536, 32, back_trunk)

    def weight_gradient(t, slot):
        grad = tm_m(k.shifts[t], k.trunk[...])
        k.grad_pyramid[:, slot] = grad.reshape(8, 32, 512).astype(BF16)

    def run(low, high, shift):
        def body(t, carry):
            weight_gradient(t, t + shift)
            return carry

        lax.fori_loop(low, high, body, 0)

    swaps = []

    def weight_gradients():
        weight_gradient(0, 0)
        run(1, 4, 3)
        run(4, 10, 6)
        run(10, 13, net.r * 6 - 9)
        for j in range(3):
            k.grad_pyramid[:, 7 - net.r * 6 + j] = jnp.zeros((8, 32, 512), BF16)
        swaps.append(core_halves(net, k.grad_pyramid, k.core_pyramid))
        swaps.append(core_halves(net, k.grad_project, k.core_project))
        swaps.append(core_halves(net, k.grad_pool, k.core_pool))

    bias_grad, gain_grad = gradient_sums(
        net, k.shortcut, normed, k.out_1, k.in_1, meanwhile=weight_gradients
    )
    keep_rows(k.norm_3, gain_grad, bias_grad)

    def back_expanded(at):
        shared = wide(k.mask[at, :], 512) / counted * gain
        grad = gain * k.shortcut[at, :] - shared * (bias_grad + normed(at) * gain_grad)
        k.grad_expanded[at, :] = (inverse * grad).astype(BF16)

    each_rows(1536, 32, back_expanded)
    for swap in swaps:
        swap.wait()

    def add_pyramid(i, carry):
        for z in range(4):
            total = k.grad_pyramid[4 * net.r + z, i].astype(F32) + k.core_pyramid[z, i].astype(F32)
            k.half_pyramid[z, i] = total.astype(BF16)
        return carry

    lax.fori_loop(0, 16, add_pyramid, 0)
    add_halves(net, k.grad_project, k.core_project, k.half_project)
    add_halves(net, k.grad_pool, k.core_pool, k.half_pool)


def run_pyramid_backward(args):
    return call_kernel(
        pyramid_backward,
        "pyramid_back",
        2,
        args,
        dict(
            shortcut=((1536, 512), F32),
            grad_expanded=((1536, 512), BF16),
            norm_3=((8, 512), F32),
            half_pyramid=((4, 16, 32, 512), BF16),
            half_project=((4, 32, 384), BF16),
            half_pool=((4, 64, 256), BF16),
        ),
        dict(
            grad_pyramid=pltpu.VMEM((8, 16, 32, 512), BF16),
            core_pyramid=pltpu.VMEM((4, 16, 32, 512), BF16),
            core_project=pltpu.VMEM((4, 32, 384), BF16),
            core_pool=pltpu.VMEM((4, 64, 256), BF16),
            blocks=pltpu.VMEM((4, 1536, 256), BF16),
            other=pltpu.VMEM((4, 1536, 128), BF16),
            cells=pltpu.VMEM((12, 208, 256), F32),
            shifts=pltpu.VMEM((13, 1536, 256), BF16),
            **exchange_scratch(1, 512),
        ),
        32,
    )


def bottleneck_backward(net, k):
    counted = pixel_count(k.boxes)
    loads = load_taps(k)
    odd = lax.rem(net.slot, 2)
    owners = []
    for which in (odd, 1 - odd):
        part = 2 * net.m + which
        owners.append((net.slot // 2, part // 4, lax.rem(part, 4)))
    stays = net.slot // 2 == net.m
    moves = jnp.logical_not(stays)
    greet([net.side, net.over] + net.group + [owners[1]], (owners[0], moves))

    def along_z(source, target):
        return [
            net.send(
                source.at[lax.rem(net.z + d, 4)],
                target.at[d - 1],
                (net.m, net.r, lax.rem(net.z + d, 4)),
            )
            for d in (1, 2, 3)
        ]

    def to_owners(views, arrived, sem):
        first = pltpu.make_async_remote_copy(
            src_ref=views(0),
            dst_ref=arrived.at[0],
            send_sem=net.send_sems.at[net.count],
            recv_sem=net.recv_sems.at[net.count],
            device_id=owners[0],
            device_id_type=MESH,
        )
        net.count += 1
        kept = pltpu.make_async_copy(views(0), arrived.at[0], sem)
        pl.when(moves)(first.start)
        pl.when(stays)(kept.start)
        second = net.send(views(1), arrived.at[1], owners[1])

        def wait():
            pl.when(moves)(first.wait)
            pl.when(stays)(kept.wait)
            second.wait()

        return wait

    pyramid_moves = along_z(k.half_pyramid, k.z_pyramid)
    small_moves = along_z(k.half_project, k.z_project) + along_z(k.half_pool, k.z_pool)

    def rows_of(i, size=384):
        return pl.ds(pl.multiple_of(i * size, 128), size)

    def expand_rows(at):
        total = mm_t(k.grad_expanded[at, :], k.w_expand[...])
        for b in range(4):
            k.part[b, at, :] = total[:, b * 128 : b * 128 + 128]

    each_rows(1536, 384, expand_rows)

    def expand_gradient():
        def body(b, carry):
            grad = tm_m(k.hidden_two[:, lane_block(b)], k.grad_expanded[...])
            k.grad_expand[pl.ds(2 * b, 2)] = grad.reshape(2, 64, 512).astype(BF16)
            return carry

        lax.fori_loop(0, 4, body, 0)

    sum_scatter(net, k.part, scatter_refs(k, "sum"), k.grad_2, meanwhile=expand_gradient)

    def norm_back(grad, value, stats, affine, outgoing, incoming, store, kept, meanwhile=None):
        mean, inverse = stats[0:1, :], stats[1:2, :]
        gain, bias = affine[0:1, :], affine[1:2, :]

        def normed(at):
            return (value[at, :] - mean) * inverse

        def through(at):
            grad[at, :] = grad[at, :] * slope(gain * normed(at) + bias)

        each_rows(1536, 128, through)
        bias_grad, gain_grad = gradient_sums(
            net, grad, normed, outgoing, incoming, meanwhile=meanwhile
        )
        keep_rows(kept, gain_grad, bias_grad)

        def back(at):
            shared = k.mask[at, :] / counted * gain
            result = gain * grad[at, :] - shared * (bias_grad + normed(at) * gain_grad)
            store(at, (inverse * result).astype(BF16))

        each_rows(1536, 128, back)

    def store_2(at, value):
        k.grad_pad[pl.ds(pl.multiple_of(at.start + 512, 128), 128), :] = value

    norm_back(k.grad_2, k.dilated, k.stats_2, k.affine_2, k.out_2, k.in_2, store_2, k.norm_2)
    halo = send_halo(net, k.grad_pad)
    zero_margins(k.cells, 8, 128)
    halo.wait()

    def spread(i, carry):
        k.cells[i, 8:136, :] = k.grad_pad[rows_of(i, 128), :].astype(F32)
        for j in range(3):
            start = 8 - 4 * (j - 1)
            k.grad_taps[rows_of(i, 128), j * 128 : j * 128 + 128] = k.cells[
                i, start : start + 128, :
            ].astype(BF16)
        return carry

    lax.fori_loop(0, 20, spread, 0)
    for load in loads:
        load.wait()

    def dilated_rows(i, carry):
        total = 0.0
        for tap in range(3):
            at = pl.ds(pl.multiple_of((i * 3 + 8 - 4 * tap) * 128, 128), 384)
            total = total + mm_t(k.grad_taps[at, :], k.w_taps[tap])
        for b in range(4):
            k.part[b, rows_of(i), :] = total[:, b * 128 : b * 128 + 128]
        return carry

    lax.fori_loop(0, 4, dilated_rows, 0)
    swaps = []

    def dilated_gradient():
        for i in range(3):

            def body(b, carry):
                band = k.hidden[pl.ds(i * 512, 1536), lane_block(b)]
                grad = tm_m(band, k.grad_taps[pl.ds(512, 1536), :])
                for j in range(3):
                    block = grad[:, j * 128 : j * 128 + 128].reshape(2, 64, 128)
                    rows = slice((i * 3 + j) * 64, (i * 3 + j) * 64 + 64)
                    k.grad_dilated[pl.ds(2 * b, 2), rows, :] = block.astype(BF16)
                return carry

            lax.fori_loop(0, 4, body, 0)
        swaps.append(core_halves(net, k.grad_dilated, k.core_dilated))
        swaps.append(core_halves(net, k.grad_expand, k.core_expand))

    sum_scatter(net, k.part, scatter_refs(k, "sum2"), k.grad_1, meanwhile=dilated_gradient)

    def store_1(at, value):
        k.grad_reduced[at, lane_block(net.m)] = value

    late_moves = []

    def pass_halves():
        for swap in swaps:
            swap.wait()
        add_halves(net, k.grad_dilated, k.core_dilated, k.half_dilated)
        add_halves(net, k.grad_expand, k.core_expand, k.half_expand)
        late_moves.extend(along_z(k.half_dilated, k.z_dilated))
        late_moves.extend(along_z(k.half_expand, k.z_expand))

    norm_back(
        k.grad_1,
        k.reduced,
        k.stats_1,
        k.affine_1,
        k.out_1,
        k.in_1,
        store_1,
        k.norm_1,
        meanwhile=pass_halves,
    )
    gather_blocks(net, lambda b, at: k.grad_reduced.at[at, lane_block(b)], 1536)

    def reduce_gradient(b, carry):
        grad = tm_m(k.grad_reduced[:, lane_block(b)], k.x[...])
        k.grad_reduce[pl.ds(2 * b, 2)] = grad.reshape(2, 64, 512).astype(BF16)
        return carry

    lax.fori_loop(0, 4, reduce_gradient, 0)
    swap = core_halves(net, k.grad_reduce, k.core_reduce)

    def finish(half, arrived):
        return half[net.z].astype(F32) + sum(arrived[d].astype(F32) for d in range(3))

    for move_ in pyramid_moves + small_moves:
        move_.wait()

    def sum_pyramid(i, carry):
        total = k.half_pyramid[net.z, i].astype(F32)
        for d in range(3):
            total = total + k.z_pyramid[d, i].astype(F32)
        k.sum_pyramid[i] = total.astype(BF16)
        return carry

    lax.fori_loop(0, 16, sum_pyramid, 0)
    k.sum_project[...] = finish(k.half_project, k.z_project)
    k.sum_pool[...] = finish(k.half_pool, k.z_pool)

    def lanes_for(i):
        return lane_block(odd if i == 0 else 1 - odd, 256)

    wait_pyramid = to_owners(
        lambda i: k.sum_pyramid.at[:, :, lanes_for(i)], k.own_pyramid, k.local_sems.at[9]
    )
    wait_project = to_owners(lambda i: k.sum_project, k.own_project, k.local_sems.at[10])
    swap.wait()
    add_halves(net, k.grad_reduce, k.core_reduce, k.half_reduce)
    reduce_moves = along_z(k.half_reduce, k.z_reduce)

    def input_rows(at):
        total = k.shortcut[at, :]
        for b in range(4):
            total = total + mm_t(k.grad_reduced[at, b * 128 : b * 128 + 128], k.w_reduce[b])
        k.grad_input[at, :] = total

    each_rows(1536, 384, input_rows)
    for move_ in reduce_moves:
        move_.wait()
    k.sum_reduce[...] = finish(k.half_reduce, k.z_reduce)
    wait_reduce = to_owners(
        lambda i: k.sum_reduce.at[:, lanes_for(i)], k.own_reduce, k.local_sems.at[11]
    )
    for move_ in late_moves:
        move_.wait()
    k.sum_dilated[...] = finish(k.half_dilated, k.z_dilated)
    k.sum_expand[...] = finish(k.half_expand, k.z_expand)
    wait_pyramid()

    def rows_for(i):
        return pl.ds(pl.multiple_of((odd if i == 0 else 1 - odd) * 32, 32), 32)

    nothing = jnp.zeros((64, 256), F32)
    for tap in (9, 10, 11, 15, 16, 17, 18, 19, 20, 24, 25, 26):
        k.grad_rates[tap] = nothing
    for slot in range(16):
        for i in range(2):
            block = k.own_pyramid[i, slot].astype(F32)
            if slot == 0:
                k.grad_point[rows_for(i), :] = block
            else:
                tap = slot - 1 if slot < 10 else slot + 2 if slot < 13 else slot + 8
                k.grad_rates[tap, rows_for(i), :] = block
    wait_project()
    wait_reduce()


def run_bottleneck_backward(args):
    return call_kernel(
        bottleneck_backward,
        "bottleneck_back",
        3,
        args,
        dict(
            grad_input=((1536, 512), F32),
            norm_2=((8, 128), F32),
            norm_1=((8, 128), F32),
            grad_rates=((27, 64, 256), F32),
            grad_point=((64, 256), F32),
            own_project=((2, 32, 384), F32),
            sum_pool=((64, 256), F32),
            sum_dilated=((576, 128), F32),
            sum_expand=((64, 512), F32),
            own_reduce=((2, 64, 256), F32),
        ),
        dict(
            grad_taps=pltpu.VMEM((2560, 384), BF16),
            grad_reduced=pltpu.VMEM((1536, 512), BF16),
            z_pyramid=pltpu.VMEM((3, 16, 32, 512), BF16),
            z_project=pltpu.VMEM((3, 32, 384), BF16),
            z_pool=pltpu.VMEM((3, 64, 256), BF16),
            sum_pyramid=pltpu.VMEM((16, 32, 512), BF16),
            own_pyramid=pltpu.VMEM((2, 16, 32, 256), BF16),
            sum_project=pltpu.VMEM((32, 384), F32),
            sum_reduce=pltpu.VMEM((64, 512), F32),
            grad_expand=pltpu.VMEM((8, 64, 512), BF16),
            core_expand=pltpu.VMEM((4, 64, 512), BF16),
            half_expand=pltpu.VMEM((4, 64, 512), BF16),
            z_expand=pltpu.VMEM((3, 64, 512), BF16),
            grad_reduce=pltpu.VMEM((8, 64, 512), BF16),
            core_reduce=pltpu.VMEM((4, 64, 512), BF16),
            half_reduce=pltpu.VMEM((4, 64, 512), BF16),
            z_reduce=pltpu.VMEM((3, 64, 512), BF16),
            grad_dilated=pltpu.VMEM((8, 576, 128), BF16),
            core_dilated=pltpu.VMEM((4, 576, 128), BF16),
            half_dilated=pltpu.VMEM((4, 576, 128), BF16),
            z_dilated=pltpu.VMEM((3, 576, 128), BF16),
            w_taps=pltpu.VMEM((3, 512, 384), BF16),
            part=pltpu.VMEM((4, 1536, 128), F32),
            **scatter_scratch("sum", 1536, 128),
            **scatter_scratch("sum2", 1536, 128),
            grad_2=pltpu.VMEM((1536, 128), F32),
            grad_1=pltpu.VMEM((1536, 128), F32),
            grad_pad=pltpu.VMEM((2560, 128), BF16),
            cells=pltpu.VMEM((20, 144, 128), F32),
            **exchange_scratch(2, 128),
            **exchange_scratch(1, 128),
            local_sems=pltpu.SemaphoreType.DMA((12,)),
        ),
        96,
        hbm=("w_dilated",),
    )


def fast_local(
    trunk_input,
    conv_reduce,
    conv_dilated,
    conv_expand,
    reduction_norm_params,
    dilated_norm_params,
    expansion_norm_params,
    aspp_point,
    aspp_rates,
    aspp_pool,
    branch_norms,
    pooling_norm_params,
    aspp_project,
    projection_norm_params,
    head_weight,
    head_bias,
    log_vars,
    crop_boxes,
    seg_labels,
    depth_target,
    normal_target,
):
    x = trunk_input.reshape(1536, 512)
    forward = run_bottleneck(
        dict(
            x=x,
            conv_reduce=conv_reduce,
            w_dilated=conv_dilated,
            w_expand=conv_expand,
            aspp_point=aspp_point,
            aspp_rates=aspp_rates,
            project=aspp_project.reshape(64, 1280),
            affine_1=reduction_norm_params,
            affine_2=dilated_norm_params,
            affine_3=expansion_norm_params,
            boxes=crop_boxes,
        )
    )
    w_pyramid = forward.w_pyramid.reshape(13, 256, 512)

    count = jnp.sum((crop_boxes[:, 2] * crop_boxes[:, 3]).astype(F32))
    task_weights = jnp.exp(-log_vars)
    by_row = jnp.concatenate(
        [jnp.full((19,), task_weights[0]), task_weights[1:2], jnp.full((2,), task_weights[2])]
    )
    columns = jnp.pad(jnp.stack([head_bias, by_row / count]), ((0, 0), (0, 10)))
    both = jnp.concatenate([projection_norm_params, pooling_norm_params], axis=0)
    middle = run_pyramid(
        dict(
            trunk=forward.trunk,
            mask=forward.mask,
            w_pyramid=w_pyramid,
            affine_b=branch_norms.reshape(2, 256),
            affine_p=jnp.concatenate([both, both], axis=1),
            aspp_pool=aspp_pool,
            w_slots=forward.w_project.reshape(256, 1280),
            head=jnp.pad(head_weight.T, ((0, 10), (0, 0))),
            head_columns=jnp.broadcast_to(columns[:, :, None], (2, 32, 128)),
            labels=seg_labels,
            depth=depth_target,
            normal=normal_target,
            boxes=crop_boxes,
        )
    )
    features = jnp.concatenate([middle.features[:, :64], middle.features[:, 64:]], axis=0)
    sums = middle.head_sums
    losses = jnp.stack([sums[64, 0], sums[83, 0], sums[84, 0] + sums[85, 0]]) / count

    back = run_pyramid_backward(
        dict(
            grad_branches=middle.grad_branches,
            w_pyramid=w_pyramid,
            x=x,
            trunk=forward.trunk,
            expanded=forward.expanded,
            stats_3=forward.stats_3,
            affine_3=expansion_norm_params,
            mask=forward.mask,
            grad_pooled=middle.grad_pooled,
            grad_project=middle.grad_project,
            grad_pool=middle.grad_pool,
            boxes=crop_boxes,
        )
    )
    last = run_bottleneck_backward(
        dict(
            grad_expanded=back.grad_expanded,
            shortcut=back.shortcut,
            half_pyramid=back.half_pyramid,
            half_project=back.half_project,
            half_pool=back.half_pool,
            x=x,
            hidden=forward.hidden,
            hidden_two=forward.hidden_two,
            w_expand=conv_expand,
            w_dilated=conv_dilated,
            w_reduce=forward.w_reduce,
            dilated=forward.dilated,
            stats_2=forward.stats_2,
            affine_2=dilated_norm_params,
            reduced=forward.reduced,
            stats_1=forward.stats_1,
            affine_1=reduction_norm_params,
            mask=forward.mask,
            boxes=crop_boxes,
        )
    )
    odd = lax.rem(lax.axis_index("batch"), 2)

    def in_order(blocks):
        return jnp.where(odd == 0, blocks, blocks[::-1])

    project_rows = in_order(last.own_project).reshape(64, 6, 64)[:, :5]
    grad_project = jnp.where(odd == 0, project_rows[:, :, :32], project_rows[:, :, 32:])
    grad_reduce = in_order(last.own_reduce).reshape(128, 256).T
    return (
        features.reshape(1, 12, 128, 64),
        jnp.sum(task_weights * losses + log_vars),
        last.grad_input.reshape(1, 12, 128, 512),
        grad_reduce,
        last.sum_dilated.reshape(3, 3, 64, 128),
        last.sum_expand,
        last.norm_1[:2],
        last.norm_2[:2],
        back.norm_3[:2],
        last.grad_point,
        last.grad_rates.reshape(3, 3, 3, 64, 256),
        last.sum_pool,
        middle.norm_b[:2].reshape(2, 4, 64),
        middle.norm_pool[:2, :64],
        grad_project,
        middle.norm_p[:2, :64],
        sums[:22, :].T,
        sums[32:54, 0],
        1.0 - task_weights * losses,
    )


def local(
    trunk_input,
    conv_reduce,
    conv_dilated,
    conv_expand,
    reduction_norm_params,
    dilated_norm_params,
    expansion_norm_params,
    aspp_point,
    aspp_rates,
    aspp_pool,
    branch_norms,
    pooling_norm_params,
    aspp_project,
    projection_norm_params,
    head_weight,
    head_bias,
    log_vars,
    crop_boxes,
    seg_labels,
    depth_target,
    normal_target,
):
    image_inputs, tile_row_count, frame_columns, quarter = trunk_input.shape
    pixels = image_inputs * tile_row_count * frame_columns
    branch_part = aspp_point.shape[0]
    branch_total = lax.axis_size("branch")
    row_portion = 1.0 / lax.axis_size("rows")
    image_overall_count = float(crop_boxes.shape[0])
    first_image = lax.axis_index("batch") * image_inputs
    first_row = lax.axis_index("rows") * tile_row_count
    my_boxes = lax.dynamic_slice_in_dim(crop_boxes, first_image, image_inputs, 0)
    row_ids = first_row + jnp.arange(tile_row_count, dtype=jnp.int32)
    col_ids = jnp.arange(frame_columns, dtype=jnp.int32)
    inside_rows = (row_ids[None, :] >= my_boxes[:, 0:1]) & (
        row_ids[None, :] < my_boxes[:, 0:1] + my_boxes[:, 2:3]
    )
    inside_cols = (col_ids[None, :] >= my_boxes[:, 1:2]) & (
        col_ids[None, :] < my_boxes[:, 1:2] + my_boxes[:, 3:4]
    )
    valid_mask = (inside_rows[:, :, None] & inside_cols[:, None, :]).astype(jnp.float32)
    mask_column_vector = valid_mask.reshape(pixels, 1)
    mask_flat = valid_mask.reshape(pixels)
    pixel_number_count = jnp.sum((crop_boxes[:, 2] * crop_boxes[:, 3]).astype(jnp.float32))
    image_areas = (my_boxes[:, 2] * my_boxes[:, 3]).astype(jnp.float32)
    input_full = widen(trunk_input)
    reduced_output = forward_dot(input_full, conv_reduce).reshape(pixels, -1)
    normalized_first, standardized_first, inverse_deviation_first = norm_ahead_pass(
        reduced_output, mask_column_vector, pixel_number_count, reduction_norm_params
    )
    hidden_one = (
        jax.nn.silu(normalized_first)
        .astype(jnp.bfloat16)
        .reshape(image_inputs, tile_row_count, frame_columns, -1)
    )
    hidden_full = widen(pad_rows(hidden_one))
    dilated_out = 0.0
    for row_tap in range(3):
        band = hidden_full[:, 4 * row_tap : 4 * row_tap + tile_row_count]
        for col_tap in range(3):
            dilated_out = dilated_out + forward_dot(
                move(band, -(col_tap - 1) * 4, 2), conv_dilated[row_tap, col_tap]
            )
    normalized_second, standardized_second, inverse_deviation_second = norm_ahead_pass(
        dilated_out.reshape(pixels, -1), mask_column_vector, pixel_number_count, dilated_norm_params
    )
    hidden_two = (
        jax.nn.silu(normalized_second)
        .astype(jnp.bfloat16)
        .reshape(image_inputs, tile_row_count, frame_columns, -1)
    )
    hidden_two_full = widen(hidden_two)
    expanded_output = forward_dot(hidden_two_full, conv_expand).reshape(pixels, -1)
    normalized_third, standardized_third, inverse_deviation_third = norm_ahead_pass(
        expanded_output, mask_column_vector, pixel_number_count, expansion_norm_params
    )
    residual_sum = normalized_third + trunk_input.reshape(pixels, -1).astype(jnp.float32)
    trunk_out = (
        jax.nn.silu(residual_sum)
        .astype(jnp.bfloat16)
        .reshape(image_inputs, tile_row_count, frame_columns, quarter)
    )
    trunk_full = widen(trunk_out)
    branch_outs = [backward_dot(trunk_full, aspp_point)]
    for branch_id in range(3):
        dilation = RATES[branch_id]
        hops = dilation // tile_row_count
        partials = [0.0, 0.0, 0.0]
        for col_tap in range(3):
            shifted = move(trunk_full, -(col_tap - 1) * dilation, 2)
            products = backward_dot(shifted, stacked_taps(aspp_rates[branch_id], col_tap))
            for row_tap in range(3):
                partials[row_tap] = (
                    partials[row_tap]
                    + products[..., row_tap * branch_part : (row_tap + 1) * branch_part]
                )
        upper = send_down(partials[0].astype(jnp.bfloat16), hops).astype(jnp.float32)
        lower_part = send_up(partials[2].astype(jnp.bfloat16), hops).astype(jnp.float32)
        branch_outs.append(partials[1] + upper + lower_part)
    spatial_flattened = jnp.stack(branch_outs, axis=3).reshape(pixels, -1)
    branch_gain_bias = branch_norms.reshape(2, -1)
    normalized_spatial, standardized_spatial, inverse_deviation_spatial = norm_ahead_pass(
        spatial_flattened, mask_column_vector, pixel_number_count, branch_gain_bias
    )
    spatial_act = (
        jax.nn.silu(normalized_spatial)
        .astype(jnp.bfloat16)
        .reshape(image_inputs, tile_row_count, frame_columns, 4, branch_part)
    )
    pooled_local = lax.dot_general(
        valid_mask.astype(jnp.bfloat16),
        trunk_full,
        (((1, 2), (1, 2)), ((0,), (0,))),
        preferred_element_type=jnp.float32,
    )
    pooled = (over_rows(pooled_local) / image_areas[:, None]).astype(jnp.bfloat16)
    pooling_convolution = backward_dot(pooled, aspp_pool)
    normalized_poolbranch, standardized_poolbranch, inverse_deviation_poolbranch = norm_ahead_pass(
        pooling_convolution, row_portion, image_overall_count, pooling_norm_params
    )
    pool_act = jax.nn.silu(normalized_poolbranch).astype(jnp.bfloat16)
    pool_wide = jnp.broadcast_to(
        pool_act[:, None, None, None, :],
        (image_inputs, tile_row_count, frame_columns, 1, branch_part),
    )
    concat = jnp.concatenate([spatial_act, pool_wide], axis=3)
    concat_flat = widen(concat).reshape(pixels, -1)
    proj_kernel = (
        aspp_project.reshape(branch_part, 5, branch_total, branch_part)
        .transpose(0, 2, 1, 3)
        .reshape(branch_part, 5 * branch_total * branch_part)
    )
    projected_output = backward_dot(concat_flat, proj_kernel)
    normalized_projector, standardized_projector, inverse_deviation_projector = norm_ahead_pass(
        projected_output, mask_column_vector, pixel_number_count, projection_norm_params
    )
    features = (
        jax.nn.silu(normalized_projector)
        .astype(jnp.bfloat16)
        .reshape(image_inputs, tile_row_count, frame_columns, -1)
    )
    features_wide = widen(features).reshape(pixels, -1).astype(jnp.float32)
    head_wide = head_weight.astype(jnp.float32)
    logits = jnp.dot(features_wide, head_wide, precision=HIGH) + head_bias
    classes = head_bias.shape[0] - 3
    seg_logits = logits[:, :classes]
    labels_flat = seg_labels.reshape(pixels)
    classes_hot = (labels_flat[:, None] == jnp.arange(classes, dtype=jnp.int32)[None, :]).astype(
        jnp.float32
    )
    cross = jax.nn.logsumexp(seg_logits, axis=1) - jnp.sum(seg_logits * classes_hot, axis=1)
    depth_gap = logits[:, classes] - depth_target.reshape(pixels)
    smooth_abs = jnp.sqrt(depth_gap * depth_gap + 1.0)
    normal_gap = logits[:, classes + 1 :] - jnp.moveaxis(normal_target, 1, 3).reshape(pixels, 2)
    local_losses = jnp.stack(
        [
            jnp.sum(mask_flat * cross),
            jnp.sum(mask_flat * (smooth_abs - 1.0)),
            jnp.sum(mask_flat * jnp.sum(normal_gap * normal_gap, axis=1)),
        ]
    )
    task_weights = jnp.exp(-log_vars)
    grad_seg = (jax.nn.softmax(seg_logits, axis=1) - classes_hot) * (
        task_weights[0] / pixel_number_count * mask_flat
    )[:, None]
    grad_depth = depth_gap / smooth_abs * (task_weights[1] / pixel_number_count * mask_flat)
    grad_normal = 2.0 * normal_gap * (task_weights[2] / pixel_number_count * mask_flat)[:, None]
    grad_logits = jnp.concatenate([grad_seg, grad_depth[:, None], grad_normal], axis=1)
    head_local = lax.dot_general(
        features_wide, grad_logits, (((0,), (0,)), ((), ())), precision=HIGH
    )
    loss_parts, grad_head_weight, grad_head_bias = lax.psum(
        (local_losses, head_local, jnp.sum(grad_logits, axis=0)), ("rows", "batch")
    )
    task_losses = loss_parts / pixel_number_count
    total_loss = jnp.sum(task_weights * task_losses + log_vars)
    grad_log_vars = 1.0 - task_weights * task_losses
    grad_features = jnp.dot(grad_logits, head_wide.T, precision=HIGH)
    my_features_grad = lax.dynamic_slice_in_dim(
        grad_features, lax.axis_index("branch") * branch_part, branch_part, 1
    )
    gradient_before_projector = my_features_grad * silu_slope(normalized_projector)
    grad_proj_in, grad_project_norm = norm_reverse_pass(
        gradient_before_projector,
        standardized_projector,
        inverse_deviation_projector,
        1.0,
        mask_column_vector,
        pixel_number_count,
        projection_norm_params,
    )
    grad_proj_low = grad_proj_in.astype(jnp.bfloat16)
    proj_kernel_grad = lax.dot_general(
        grad_proj_low, concat_flat, (((0,), (0,)), ((), ())), preferred_element_type=jnp.float32
    )
    grad_project_local = (
        proj_kernel_grad.reshape(branch_part, branch_total, 5, branch_part)
        .transpose(0, 2, 1, 3)
        .reshape(branch_part, 5, branch_total * branch_part)
    )
    concat_grad = forward_dot(grad_proj_low, proj_kernel).reshape(
        image_inputs, tile_row_count, frame_columns, -1
    )
    concat_grad = narrow(concat_grad).reshape(pixels, 5, branch_part)
    pool_grad_img = over_rows(
        jnp.sum(concat_grad[:, 4, :].reshape(image_inputs, -1, branch_part), axis=1)
    )
    gradient_before_poolbranch = pool_grad_img * silu_slope(normalized_poolbranch)
    grad_pool_conv, grad_pool_norm = norm_reverse_pass(
        gradient_before_poolbranch,
        standardized_poolbranch,
        inverse_deviation_poolbranch,
        row_portion,
        1.0,
        image_overall_count,
        pooling_norm_params,
    )
    pool_conv_low = grad_pool_conv.astype(jnp.bfloat16)
    grad_pool_local = (
        lax.dot_general(
            pool_conv_low, pooled, (((0,), (0,)), ((), ())), preferred_element_type=jnp.float32
        )
        * row_portion
    )
    pooled_grad = forward_dot(pool_conv_low, aspp_pool)
    gradient_before_spatialbranch = concat_grad[:, :4, :].reshape(pixels, -1) * silu_slope(
        normalized_spatial
    )
    grad_spatial, branch_norm_grad = norm_reverse_pass(
        gradient_before_spatialbranch,
        standardized_spatial,
        inverse_deviation_spatial,
        1.0,
        mask_column_vector,
        pixel_number_count,
        branch_gain_bias,
    )
    grad_branch_norms = branch_norm_grad.reshape(2, 4, branch_part)
    spatial_low = grad_spatial.astype(jnp.bfloat16).reshape(
        image_inputs, tile_row_count, frame_columns, 4, branch_part
    )
    point_grad = spatial_low[:, :, :, 0]
    grad_point_local = pixel_dot(point_grad, trunk_full)
    trunk_grad = forward_dot(point_grad, aspp_point)
    trunk_grad = (
        trunk_grad + valid_mask[..., None] * (pooled_grad / image_areas[:, None])[:, None, None, :]
    )
    rate_grads = []
    for branch_id in range(3):
        dilation = RATES[branch_id]
        hops = dilation // tile_row_count
        centre = spatial_low[:, :, :, branch_id + 1]
        grad_taps = jnp.concatenate(
            [send_up(centre, hops), centre, send_down(centre, hops)], axis=3
        )
        per_col = []
        for col_tap in range(3):
            shifted = move(trunk_full, -(col_tap - 1) * dilation, 2)
            per_col.append(pixel_dot(grad_taps, shifted))
            tap_grad = forward_dot(grad_taps, stacked_taps(aspp_rates[branch_id], col_tap))
            trunk_grad = trunk_grad + move(tap_grad, (col_tap - 1) * dilation, 2)
        col_stack = jnp.stack(per_col, axis=0).reshape(3, 3, branch_part, -1)
        rate_grads.append(col_stack.transpose(1, 0, 2, 3))
    grad_rates_local = jnp.stack(rate_grads, axis=0)
    trunk_own = narrow(trunk_grad).reshape(pixels, -1)
    gradient_shortcut = trunk_own * silu_slope(residual_sum)
    grad_expanded, grad_norm_expand = norm_reverse_pass(
        gradient_shortcut,
        standardized_third,
        inverse_deviation_third,
        1.0,
        mask_column_vector,
        pixel_number_count,
        expansion_norm_params,
    )
    expanded_low = grad_expanded.astype(jnp.bfloat16).reshape(
        image_inputs, tile_row_count, frame_columns, -1
    )
    grad_expand_local = pixel_dot(hidden_two_full, expanded_low)
    hidden_two_grad = narrow(backward_dot(expanded_low, conv_expand)).reshape(pixels, -1)
    gradient_before_second = hidden_two_grad * silu_slope(normalized_second)
    gradient_dilated_input, gradient_dilated_norm = norm_reverse_pass(
        gradient_before_second,
        standardized_second,
        inverse_deviation_second,
        1.0,
        mask_column_vector,
        pixel_number_count,
        dilated_norm_params,
    )
    dilated_lowprec = gradient_dilated_input.astype(jnp.bfloat16).reshape(
        image_inputs, tile_row_count, frame_columns, -1
    )
    dilated_padded = pad_rows(dilated_lowprec)
    hidden_one_grad = 0.0
    kernel_grads = []
    for row_tap in range(3):
        band = hidden_full[:, 4 * row_tap : 4 * row_tap + tile_row_count]
        grad_band = dilated_padded[:, 8 - 4 * row_tap : 8 - 4 * row_tap + tile_row_count]
        for col_tap in range(3):
            kernel_grads.append(pixel_dot(move(band, -(col_tap - 1) * 4, 2), dilated_lowprec))
            hidden_one_grad = hidden_one_grad + backward_dot(
                move(grad_band, (col_tap - 1) * 4, 2), conv_dilated[row_tap, col_tap]
            )
    grad_dilated_local = jnp.stack(kernel_grads, axis=0).reshape(3, 3, hidden_full.shape[3], -1)
    hidden_one_own = narrow(hidden_one_grad).reshape(pixels, -1)
    gradient_before_first = hidden_one_own * silu_slope(normalized_first)
    grad_reduced, grad_norm_reduce = norm_reverse_pass(
        gradient_before_first,
        standardized_first,
        inverse_deviation_first,
        1.0,
        mask_column_vector,
        pixel_number_count,
        reduction_norm_params,
    )
    reduced_low = grad_reduced.astype(jnp.bfloat16).reshape(
        image_inputs, tile_row_count, frame_columns, -1
    )
    grad_reduce_local = pixel_dot(input_full, reduced_low)
    input_grad = narrow(backward_dot(reduced_low, conv_reduce))
    grad_input = input_grad + gradient_shortcut.reshape(
        image_inputs, tile_row_count, frame_columns, quarter
    )
    grad_reduce, grad_dilated, grad_expand, grad_point, grad_rates, grad_pool, grad_project = (
        lax.psum_scatter(grad_reduce_local, ("rows", "batch"), scatter_dimension=0, tiled=True),
        lax.psum_scatter(grad_dilated_local, ("rows", "batch"), scatter_dimension=2, tiled=True),
        lax.psum_scatter(grad_expand_local, ("rows", "batch"), scatter_dimension=0, tiled=True),
        lax.psum_scatter(grad_point_local, ("rows", "batch"), scatter_dimension=1, tiled=True),
        lax.psum_scatter(grad_rates_local, ("rows", "batch"), scatter_dimension=4, tiled=True),
        lax.psum_scatter(grad_pool_local, ("rows", "batch"), scatter_dimension=1, tiled=True),
        lax.psum_scatter(grad_project_local, ("rows", "batch"), scatter_dimension=2, tiled=True),
    )
    return (
        features,
        total_loss,
        grad_input,
        grad_reduce,
        grad_dilated,
        grad_expand,
        grad_norm_reduce,
        gradient_dilated_norm,
        grad_norm_expand,
        grad_point,
        grad_rates,
        grad_pool,
        grad_branch_norms,
        grad_pool_norm,
        grad_project,
        grad_project_norm,
        grad_head_weight,
        grad_head_bias,
        grad_log_vars,
    )


def solution(mesh):
    in_specs = (
        P("batch", "rows", None, "branch"),
        P(None, "branch"),
        P(None, None, None, "branch"),
        P(None, "branch"),
        P(None, "branch"),
        P(None, "branch"),
        P(None, "branch"),
        P("branch", None),
        P(None, None, None, "branch", None),
        P("branch", None),
        P(None, None, "branch"),
        P(None, "branch"),
        P("branch", None, None),
        P(None, "branch"),
        P(),
        P(),
        P(),
        P(),
        P("batch", "rows", None),
        P("batch", "rows", None),
        P("batch", None, "rows", None),
    )
    out_specs = (
        P("batch", "rows", None, "branch"),
        P(),
        P("batch", "rows", None, "branch"),
        P(("rows", "batch"), "branch"),
        P(None, None, ("rows", "batch"), "branch"),
        P(("rows", "batch"), "branch"),
        P(None, "branch"),
        P(None, "branch"),
        P(None, "branch"),
        P("branch", ("rows", "batch")),
        P(None, None, None, "branch", ("rows", "batch")),
        P("branch", ("rows", "batch")),
        P(None, None, "branch"),
        P(None, "branch"),
        P("branch", None, ("rows", "batch")),
        P(None, "branch"),
        P(),
        P(),
        P(),
    )
    small = (mesh.shape["branch"], mesh.shape["rows"], mesh.shape["batch"]) == (4, 2, 4)
    body = fast_local if small else local
    return jax.shard_map(body, mesh=mesh, in_specs=in_specs, out_specs=out_specs, check_vma=False)
```

```python
import types

import jax
import jax.numpy as jnp
from jax import lax
from jax.experimental import pallas as pl
from jax.experimental.pallas import tpu as pltpu
from jax.sharding import PartitionSpec as P

EPS = 1e-05
HIGH = lax.Precision.HIGHEST
RATES = (12, 24, 36)


def padded(cells, sides, width):
    for axis, dim in sides:
        count = lax.axis_size(axis)
        ends = count - 1
        head = lax.slice_in_dim(cells, 0, width, axis=dim)
        tail = lax.slice_in_dim(cells, cells.shape[dim] - width, cells.shape[dim], axis=dim)
        cells = jnp.concatenate(
            [
                lax.ppermute(tail, axis, [(i, (i + 1) % count) for i in range(ends)]),
                cells,
                lax.ppermute(head, axis, [((i + 1) % count, i) for i in range(ends)]),
            ],
            axis=dim,
        )
    return cells


def shifted_2(block, axis, distance):
    devices = range(lax.axis_size(axis))
    route = [(i - distance, i) for i in devices if i - distance in devices]
    return lax.ppermute(block, axis, route)


def move(tensor, offset, axis_id):
    length = tensor.shape[axis_id]
    if offset == 0:
        return tensor
    widths = [(0, 0)] * tensor.ndim
    if offset > 0:
        widths[axis_id] = (offset, 0)
        return lax.slice_in_dim(jnp.pad(tensor, widths), 0, length, axis=axis_id)
    widths[axis_id] = (0, -offset)
    return lax.slice_in_dim(jnp.pad(tensor, widths), -offset, length - offset, axis=axis_id)


def forward_dot(lhs_arr, rhs_arr):
    return jnp.dot(lhs_arr, rhs_arr, preferred_element_type=jnp.float32)


def backward_dot(grad_arr, kernel):
    return lax.dot_general(
        grad_arr,
        kernel,
        (((grad_arr.ndim - 1,), (1,)), ((), ())),
        preferred_element_type=jnp.float32,
    )


def pixel_dot(source, grad_arr):
    return lax.dot_general(
        source, grad_arr, (((0, 1, 2), (0, 1, 2)), ((), ())), preferred_element_type=jnp.float32
    )


def silu_slope(pre_act):
    sigmoid_v = jax.nn.sigmoid(pre_act)
    return sigmoid_v * (1.0 + pre_act * (1.0 - sigmoid_v))


def widen(tensor):
    return lax.all_gather(tensor, "branch", axis=3, tiled=True)


def narrow(tensor):
    return lax.psum_scatter(
        tensor.astype(jnp.bfloat16), "branch", scatter_dimension=3, tiled=True
    ).astype(jnp.float32)


def pad_rows(tensor):
    return padded(tensor, (("rows", 1),), 4)


def send_down(tensor, hops):
    if hops >= lax.axis_size("rows"):
        return jnp.zeros_like(tensor)
    return shifted_2(tensor, "rows", hops)


def send_up(tensor, hops):
    if hops >= lax.axis_size("rows"):
        return jnp.zeros_like(tensor)
    return shifted_2(tensor, "rows", -hops)


def over_rows(tensor):
    return lax.psum(tensor, "rows")


def norm_ahead_pass(tensor, weight, counted, affine):
    summed = lax.psum(jnp.sum(tensor * weight, axis=0), ("rows", "batch"))
    mean_val = summed / counted
    centered = tensor - mean_val
    spread = lax.psum(jnp.sum(weight * centered * centered, axis=0), ("rows", "batch"))
    variance = spread / counted
    inverse = lax.rsqrt(variance + EPS)
    normed = centered * inverse
    return (affine[0] * normed + affine[1], normed, inverse)


def norm_reverse_pass(grad_out, normed, inverse, weight_all, weight_stat, counted, affine):
    grad_bias, grad_gain = lax.psum(
        (jnp.sum(grad_out * weight_all, axis=0), jnp.sum(grad_out * normed * weight_all, axis=0)),
        ("rows", "batch"),
    )
    gain_row = affine[0]
    grad_in = inverse * (
        gain_row * grad_out - weight_stat / counted * gain_row * (grad_bias + normed * grad_gain)
    )
    return (grad_in, jnp.stack([grad_gain, grad_bias]))


def stacked_taps(kernels, col_tap):
    return jnp.concatenate([kernels[0, col_tap], kernels[1, col_tap], kernels[2, col_tap]], axis=0)


MESH = pl.DeviceIdType.MESH
F32 = jnp.float32
BF16 = jnp.bfloat16
VMEM_LIMIT = 60 * 2**20


class Net:
    def __init__(self, send_sems, recv_sems):
        self.m = lax.axis_index("branch")
        self.r = lax.axis_index("rows")
        self.z = lax.axis_index("batch")
        self.send_sems, self.recv_sems, self.count = send_sems, recv_sems, 0
        self.side = (self.m ^ 1, self.r, self.z)
        self.over = (self.m ^ 2, self.r, self.z)
        self.diagonal = (self.m ^ 3, self.r, self.z)
        self.core = (self.m, 1 - self.r, self.z)
        self.slot = self.r * 4 + self.z
        self.group = [
            (self.m, lax.rem(self.r + i, 2), lax.rem(self.z + j, 4))
            for i in range(2)
            for j in range(4)
            if i or j
        ]

    def send(self, src, dst, device):
        i = self.count
        self.count += 1
        copy = pltpu.make_async_remote_copy(
            src_ref=src,
            dst_ref=dst,
            send_sem=self.send_sems.at[i],
            recv_sem=self.recv_sems.at[i],
            device_id=device,
            device_id_type=MESH,
        )
        copy.start()
        return copy


def greet(peers, perhaps=None):
    barrier = pltpu.get_barrier_semaphore()
    for peer in peers:
        pl.semaphore_signal(barrier, inc=1, device_id=peer, device_id_type=MESH)
    if perhaps is None:
        pl.semaphore_wait(barrier, len(peers))
        return
    peer, there = perhaps

    @pl.when(there)
    def _():
        pl.semaphore_signal(barrier, inc=1, device_id=peer, device_id_type=MESH)

    pl.semaphore_wait(barrier, len(peers) + there.astype(jnp.int32))


def each_rows(total, step, body):
    def run(i, carry):
        body(pl.ds(pl.multiple_of(i * step, step), step))
        return carry

    lax.fori_loop(0, total // step, run, 0)


def lane_block(index, width=128):
    return pl.ds(pl.multiple_of(index * width, width), width)


def wide(tile, width):
    count = width // tile.shape[1]
    return tile if count == 1 else jnp.concatenate([tile] * count, axis=1)


def column_sums(fn, total, width, number):
    step = 16384 // width

    def run(i, sums):
        terms = fn(pl.ds(pl.multiple_of(i * step, step), step))
        return tuple(
            s + jnp.sum(t.reshape(step // 8, 8, width), axis=0) for s, t in zip(sums, terms)
        )

    sums = lax.fori_loop(
        0, total // step, run, tuple(jnp.zeros((8, width), F32) for _ in range(number))
    )
    return [jnp.sum(s, axis=0, keepdims=True) for s in sums]


def fold(row):
    return row + pltpu.roll(wide(row, 128), 64, 1)


def exchange(net, outgoing, incoming, meanwhile=None):
    copies = [net.send(outgoing, incoming.at[net.slot], peer) for peer in net.group]
    incoming[net.slot] = outgoing[...]
    if meanwhile is not None:
        meanwhile()
    for copy in copies:
        copy.wait()


def pack(outgoing, first, second, extra=None):
    for i in range(first.shape[1] // 128):
        outgoing[2 * i : 2 * i + 1, :] = first[:, i * 128 : i * 128 + 128]
        outgoing[2 * i + 1 : 2 * i + 2, :] = second[:, i * 128 : i * 128 + 128]
    if extra is not None:
        outgoing[4:5, :] = extra


def unpack(incoming, width):
    count = width // 128
    firsts = [incoming[:, 2 * i, :] for i in range(count)]
    seconds = [incoming[:, 2 * i + 1, :] for i in range(count)]
    return jnp.concatenate(firsts, axis=1), jnp.concatenate(seconds, axis=1)


def statistics(
    net, value_ref, mask_ref, counts, outgoing, incoming, counted, folded=False, extra=None
):
    total, width = value_ref.shape
    same = fold if folded else (lambda row: row)
    (first,) = column_sums(
        lambda at: (value_ref[at, :] * wide(mask_ref[at, :], width),), total, width, 1
    )
    first = same(first)
    own = jnp.sum(jnp.where(lax.broadcasted_iota(jnp.int32, (8, 128), 0) == net.slot, counts, 0.0), axis=0, keepdims=True)
    centre = first / jnp.maximum(wide(own, width), 1.0)

    def squares(at):
        gap = value_ref[at, :] - centre
        return (gap * gap * wide(mask_ref[at, :], width),)

    second = same(column_sums(squares, total, width, 1)[0])
    pack(outgoing, first, second, extra)
    exchange(net, outgoing, incoming)
    firsts, seconds = unpack(incoming, width)
    numbers = wide(counts, width)
    mean = jnp.sum(firsts, axis=0, keepdims=True) / counted
    drift = firsts / jnp.maximum(numbers, 1.0) - mean
    variance = jnp.sum(seconds + numbers * drift * drift, axis=0, keepdims=True) / counted
    return mean, lax.rsqrt(variance + EPS)


def gather_blocks(net, part, rows, meanwhile=None):
    pieces, size = 4, rows // 4
    own, side, over = net.m, net.m ^ 1, net.m ^ 2

    def at(i):
        return pl.ds(i * size, size)

    to_side, to_over = [], []
    for i in range(pieces):
        j = pieces - 1 - i
        to_side.append(net.send(part(own, at(i)), part(own, at(i)), net.side))
        to_over.append(net.send(part(own, at(j)), part(own, at(j)), net.over))
    passed = []
    for i in range(pieces):
        j = pieces - 1 - i
        to_side[i].wait_recv()
        if i < pieces // 2:
            passed.append(net.send(part(side, at(i)), part(side, at(i)), net.over))
        to_over[i].wait_recv()
        if i < pieces // 2:
            passed.append(net.send(part(over, at(j)), part(over, at(j)), net.side))
    if meanwhile is not None:
        meanwhile()
    for copy in to_side + to_over:
        copy.wait_send()
    for copy in passed:
        copy.wait()


def sum_scatter(net, part, bufs, out, meanwhile=None):
    far, to_side, to_over, far_side, far_over, from_side, from_over = bufs
    rows, width = out.shape
    half, step = rows // 2, 16384 // width
    head, tail = pl.ds(0, half), pl.ds(half, half)
    across, side, over = net.m ^ 3, net.m ^ 1, net.m ^ 2

    def fill(target, index, base):
        def body(at):
            rows_at = pl.ds(pl.multiple_of(at.start + base, step), step)
            target[rows_at, :] = part[index, rows_at, :].astype(BF16)

        each_rows(half, step, body)

    def combine(target, index, base, arrived):
        def body(at):
            rows_at = pl.ds(pl.multiple_of(at.start + base, step), step)
            target[rows_at, :] = (part[index, rows_at, :] + arrived[at, :].astype(F32)).astype(BF16)

        each_rows(half, step, body)

    fill(far, across, 0)
    first = net.send(far.at[head], far_side, net.side)
    fill(far, across, half)
    second = net.send(far.at[tail], far_over, net.over)
    fill(to_side, side, 0)
    third = net.send(to_side.at[head], from_side.at[head], net.side)
    fill(to_over, over, half)
    fourth = net.send(to_over.at[tail], from_over.at[tail], net.over)
    second.wait_recv()
    combine(to_side, side, half, far_over)
    fifth = net.send(to_side.at[tail], from_side.at[tail], net.side)
    first.wait_recv()
    combine(to_over, over, 0, far_side)
    sixth = net.send(to_over.at[head], from_over.at[head], net.over)
    if meanwhile is not None:
        meanwhile()
    for copy in (third, fourth, fifth, sixth):
        copy.wait_recv()

    def body(at):
        out[at, :] = (
            part[net.m, at, :] + from_side[at, :].astype(F32) + from_over[at, :].astype(F32)
        )

    each_rows(rows, step, body)
    for copy in (first, second, third, fourth, fifth, sixth):
        copy.wait_send()


def gradient_sums(
    net, grad_ref, normed, outgoing, incoming, folded=False, extra=None, meanwhile=None
):
    total, width = grad_ref.shape
    same = fold if folded else (lambda row: row)
    bias, gain = column_sums(
        lambda at: (grad_ref[at, :], grad_ref[at, :] * normed(at)), total, width, 2
    )
    pack(outgoing, same(bias), same(gain), extra)
    exchange(net, outgoing, incoming, meanwhile)
    biases, gains = unpack(incoming, width)
    return jnp.sum(biases, axis=0, keepdims=True), jnp.sum(gains, axis=0, keepdims=True)


def keep_rows(ref, first, second):
    width = ref.shape[1]
    ref[0:1, :] = first
    ref[1:2, :] = second
    ref[2:8, :] = jnp.zeros((6, width), F32)


def pair(a, b):
    low = lax.broadcasted_iota(jnp.int32, (a.shape[0], 128), 1) < 64
    results = []
    for g in range(2):
        left, right = a[:, g * 128 : g * 128 + 128], b[:, g * 128 : g * 128 + 128]
        results.append(jnp.where(low, left, pltpu.roll(right, 64, 1)))
        results.append(jnp.where(low, pltpu.roll(left, 64, 1), right))
    return results


def unpair(blocks):
    low = lax.broadcasted_iota(jnp.int32, blocks[0].shape, 1) < 64
    firsts, seconds = [], []
    for g in range(2):
        left, right = blocks[2 * g], blocks[2 * g + 1]
        firsts.append(jnp.where(low, left, pltpu.roll(right, 64, 1)))
        seconds.append(jnp.where(low, pltpu.roll(left, 64, 1), right))
    return jnp.concatenate(firsts, axis=1), jnp.concatenate(seconds, axis=1)


def split_three(row):
    high = row.astype(BF16)
    rest = row - high.astype(F32)
    middle = rest.astype(BF16)
    low = (rest - middle.astype(F32)).astype(BF16)
    return high, middle, low


def zero_margins(ref, side, width):
    rows, _, lanes = ref.shape
    ref[:, 0:side, :] = jnp.zeros((rows, side, lanes), F32)
    ref[:, side + width : 2 * side + width, :] = jnp.zeros((rows, side, lanes), F32)


def scatter_buffers(rows, width):
    whole, half = pltpu.VMEM((rows, width), BF16), pltpu.VMEM((rows // 2, width), BF16)
    return [whole, whole, whole, half, half, whole, whole]


def sigmoid(u):
    return 0.5 * jnp.tanh(0.5 * u) + 0.5


def slope(u):
    s = sigmoid(u)
    return s * (1.0 + u * (1.0 - s))


def mm(a, b):
    return jnp.dot(a, b, preferred_element_type=F32)


def mm_t(a, b):
    return lax.dot_general(a, b, (((1,), (1,)), ((), ())), preferred_element_type=F32)


def tm_m(a, b):
    return lax.dot_general(a, b, (((0,), (0,)), ((), ())), preferred_element_type=F32)


def call_kernel(body, name, number, args, outs, scratch, sems, hbm=(), smem=("boxes",)):
    vmem, anywhere = pl.BlockSpec(memory_space=pltpu.VMEM), pl.BlockSpec(memory_space=pl.ANY)
    names = [*args, *outs, *scratch]
    places = {name: anywhere for name in hbm}
    places.update({name: pl.BlockSpec(memory_space=pltpu.SMEM) for name in smem})

    def kernel(*refs):
        k = types.SimpleNamespace(**dict(zip(names, refs)))
        body(Net(refs[-2], refs[-1]) if sems else None, k)

    results = pl.pallas_call(
        kernel,
        out_shape=[jax.ShapeDtypeStruct(s, d) for s, d in outs.values()],
        in_specs=[places.get(name, vmem) for name in args],
        out_specs=[places.get(name, vmem) for name in outs],
        scratch_shapes=list(scratch.values()) + [pltpu.SemaphoreType.DMA((sems,))] * (2 if sems else 0),
        name=name,
        compiler_params=pltpu.CompilerParams(
            collective_id=number, has_side_effects=bool(sems), vmem_limit_bytes=VMEM_LIMIT
        ),
    )(*args.values())
    return types.SimpleNamespace(**dict(zip(outs, results)))


def pixel_count(boxes):
    total = boxes[0, 2] * boxes[0, 3]
    for b in range(1, 4):
        total = total + boxes[b, 2] * boxes[b, 3]
    return total.astype(F32)


def tile_counts(net, boxes):
    slot = lax.broadcasted_iota(jnp.int32, (8, 128), 0)
    result = jnp.zeros((8, 128), F32)
    for s in range(8):
        top, height, width = boxes[s % 4, 0], boxes[s % 4, 2], boxes[s % 4, 3]
        first, last = (s // 4) * 12, (s // 4) * 12 + 12
        rows = jnp.minimum(top + height, last) - jnp.maximum(top, first)
        result = jnp.where(slot == s, (jnp.maximum(rows, 0) * width).astype(F32), result)
    return result


def exchange_scratch(label):
    return {
        f"out_{label}": pltpu.VMEM((8, 128), F32),
        f"in_{label}": pltpu.VMEM((8, 8, 128), F32),
    }


def scatter_scratch(label, rows, width):
    return {f"{label}_{i}": b for i, b in enumerate(scatter_buffers(rows, width))}


def scatter_refs(k, label):
    return [getattr(k, f"{label}_{i}") for i in range(7)]


def load_taps(k):
    loads = []
    for i in range(3):
        for j in range(3):
            loads.append(
                pltpu.make_async_copy(
                    k.w_dilated.at[i, j],
                    k.w_taps.at[i, :, pl.ds(j * 128, 128)],
                    k.local_sems.at[i * 3 + j],
                )
            )
            loads[-1].start()
    return loads


def send_halo(net, padded):
    lanes = padded.shape[1]
    padded[pl.ds(pl.multiple_of(net.r * 2048, 128), 512), :] = jnp.zeros((512, lanes), BF16)
    return net.send(
        padded.at[pl.ds(pl.multiple_of(1536 - net.r * 1024, 128), 512)],
        padded.at[pl.ds(pl.multiple_of(net.r * 2048, 128), 512)],
        net.core,
    )


def bottleneck_forward(net, k):
    counted, counts = pixel_count(k.boxes), tile_counts(net, k.boxes)
    loads = load_taps(k)
    own_reduce = pltpu.make_async_copy(
        k.conv_reduce.at[lane_block(net.m, 512)], k.w_reduce.at[net.m], k.local_sems.at[9]
    )
    own_reduce.start()
    greet([net.side, net.over, net.diagonal] + net.group)
    branches = [(net.m ^ 3, net.diagonal), (net.m ^ 1, net.side), (net.m ^ 2, net.over)]
    arrivals = [
        net.send(k.conv_reduce.at[lane_block(b, 512)], k.w_reduce.at[net.m], peer)
        for b, peer in branches
    ]

    top, left_edge = k.boxes[net.z, 0], k.boxes[net.z, 1]
    bottom, right_edge = top + k.boxes[net.z, 2], left_edge + k.boxes[net.z, 3]
    column = lax.broadcasted_iota(jnp.int32, (128, 128), 0)
    column_inside = jnp.where((column >= left_edge) & (column < right_edge), 1.0, 0.0)

    def mask_rows(i, carry):
        row = jnp.full((128, 128), net.r * 12 + i, jnp.int32)
        inside = jnp.where((row >= top) & (row < bottom), column_inside, 0.0)
        k.mask[pl.ds(pl.multiple_of(i * 128, 128), 128), :] = inside
        return carry

    lax.fori_loop(0, 12, mask_rows, 0)

    def reduce_for(b):
        def reduce_rows(at):
            k.part[b, at, :] = mm(k.x[at, :], k.w_reduce[b])

        each_rows(1536, 384, reduce_rows)

    own_reduce.wait()
    reduce_for(net.m)
    arrivals[1].wait()
    reduce_for(net.m ^ 1)
    arrivals[2].wait()
    reduce_for(net.m ^ 2)
    arrivals[0].wait()
    reduce_for(net.m ^ 3)
    sum_scatter(net, k.part, scatter_refs(k, "sum"), k.reduced)

    half = pl.ds(pl.multiple_of(net.r * 32, 32), 32)
    late = []

    def weight_block(kind, b):
        lanes = lane_block(b, 512)
        if kind == "edge":
            return k.aspp_rates.at[0, 2 * net.r, :, :, lanes], k.w_pyramid.at[pl.ds(10, 3), net.m]
        if kind == "point":
            return k.aspp_point.at[half, lanes], k.w_pyramid.at[0, net.m, half]
        if kind == "project":
            return k.project.at[half], k.w_project.at[net.m, half]
        return (
            k.aspp_rates.at[kind, 1, :, half, lanes],
            k.w_pyramid.at[pl.ds(1 + 3 * kind, 3), net.m, half],
        )

    def spread_weights(*kinds):
        for kind in kinds:
            src, dst = weight_block(kind, net.m)
            late.append(pltpu.make_async_copy(src, dst, k.local_sems.at[10 + len(late) // 4]))
            late[-1].start()
            for b, peer in branches:
                src, dst = weight_block(kind, b)
                late.append(net.send(src, dst, peer))

    spread_weights("edge")
    mean, inverse = statistics(net, k.reduced, k.mask, counts, k.out_1, k.in_1, counted)
    keep_rows(k.stats_1, mean, inverse)

    def activate_1(at):
        u = k.affine_1[0:1, :] * ((k.reduced[at, :] - mean) * inverse) + k.affine_1[1:2, :]
        rows_at = pl.ds(pl.multiple_of(at.start + 512, 128), 128)
        k.hidden[rows_at, lane_block(net.m)] = (u * sigmoid(u)).astype(BF16)

    each_rows(1536, 128, activate_1)
    gather_blocks(
        net, lambda b, at: k.hidden.at[pl.ds(at.start + 512, at.size), lane_block(b)], 1536
    )
    halo = send_halo(net, k.hidden)
    spread_weights("project", "point", 0)
    zero_margins(k.left, 8, 128)
    zero_margins(k.right, 8, 128)
    for load in loads:
        load.wait()
    halo.wait()

    def dilated_rows(i, carry):
        total = 0.0
        for tap in range(3):
            rows_at = pl.ds(pl.multiple_of((i * 3 + 4 * tap) * 128, 128), 384)
            total = total + mm(k.hidden[rows_at, :], k.w_taps[tap])
        k.dilated[pl.ds(pl.multiple_of(i * 384, 128), 384), :] = total[:, 128:256]
        k.left[pl.ds(i * 3, 3), 8:136, :] = total[:, 0:128].reshape(3, 128, 128)
        k.right[pl.ds(i * 3, 3), 8:136, :] = total[:, 256:384].reshape(3, 128, 128)
        return carry

    lax.fori_loop(0, 4, dilated_rows, 0)

    def add_columns(i, carry):
        at = pl.ds(pl.multiple_of(i * 128, 128), 128)
        k.dilated[at, :] = k.dilated[at, :] + k.left[i, 4:132, :] + k.right[i, 12:140, :]
        return carry

    lax.fori_loop(0, 12, add_columns, 0)
    mean_2, inverse_2 = statistics(net, k.dilated, k.mask, counts, k.out_2, k.in_2, counted)
    keep_rows(k.stats_2, mean_2, inverse_2)

    def activate_2(at):
        u = k.affine_2[0:1, :] * ((k.dilated[at, :] - mean_2) * inverse_2) + k.affine_2[1:2, :]
        k.hidden_two[at, lane_block(net.m)] = (u * sigmoid(u)).astype(BF16)

    each_rows(1536, 128, activate_2)
    gather_blocks(net, lambda b, at: k.hidden_two.at[at, lane_block(b)], 1536)
    spread_weights(1, 2)

    def expand_rows(at):
        k.expanded[at, :] = mm(k.hidden_two[at, :], k.w_expand[...])

    each_rows(1536, 384, expand_rows)
    mean_3, inverse_3 = statistics(net, k.expanded, k.mask, counts, k.out_3, k.in_3, counted)
    keep_rows(k.stats_3, mean_3, inverse_3)
    for copy in late:
        copy.wait()
    swaps = [
        net.send(ref.at[..., half, :], ref.at[..., half, :], net.core)
        for ref in (k.w_pyramid.at[pl.ds(0, 10)], k.w_project)
    ]

    def activate_3(at):
        u = k.affine_3[0:1, :] * ((k.expanded[at, :] - mean_3) * inverse_3) + k.affine_3[1:2, :]
        u = u + k.x[at, :].astype(F32)
        k.trunk[at, :] = (u * sigmoid(u)).astype(BF16)

    each_rows(1536, 32, activate_3)
    for copy in swaps:
        copy.wait()


def run_bottleneck(args):
    return call_kernel(
        bottleneck_forward,
        "bottleneck",
        0,
        args,
        dict(
            mask=((1536, 128), F32),
            w_reduce=((4, 512, 128), BF16),
            w_pyramid=((13, 4, 64, 512), BF16),
            w_project=((4, 64, 1280), BF16),
            reduced=((1536, 128), F32),
            stats_1=((8, 128), F32),
            hidden=((2560, 512), BF16),
            dilated=((1536, 128), F32),
            stats_2=((8, 128), F32),
            hidden_two=((1536, 512), BF16),
            expanded=((1536, 512), F32),
            stats_3=((8, 512), F32),
            trunk=((1536, 512), BF16),
        ),
        dict(
            w_taps=pltpu.VMEM((3, 512, 384), BF16),
            part=pltpu.VMEM((4, 1536, 128), F32),
            **scatter_scratch("sum", 1536, 128),
            left=pltpu.VMEM((12, 144, 128), F32),
            right=pltpu.VMEM((12, 144, 128), F32),
            **exchange_scratch(1),
            **exchange_scratch(2),
            **exchange_scratch(3),
            local_sems=pltpu.SemaphoreType.DMA((16,)),
        ),
        96,
        hbm=(
            "conv_reduce",
            "w_dilated",
            "aspp_point",
            "aspp_rates",
            "project",
            "w_pyramid",
            "w_project",
        ),
    )


def pyramid_forward(net, k):
    counted, counts = pixel_count(k.boxes), tile_counts(net, k.boxes)
    area = (k.boxes[net.z, 2] * k.boxes[net.z, 3]).astype(F32)
    near = [
        (lax.rem(net.m + a, 4), lax.rem(net.r + b, 2), net.z)
        for a in range(4)
        for b in range(2)
        if a or b
    ]
    greet(net.group + [peer for i, peer in enumerate(near) if i])

    for b in range(4):
        k.affine_b[0:2, b * 64 : b * 64 + 64] = k.branch_norms[:, b, :]
    for i in range(2):
        k.affine_p[0:2, i * 64 : i * 64 + 64] = k.norm_project[...]
        k.affine_p[2:4, i * 64 : i * 64 + 64] = k.norm_pooling[...]
    k.head_rows[...] = jnp.zeros((32, 256), F32)
    k.head_rows[0:22, :] = k.head_weight[...].astype(F32).T

    (own_sum,) = column_sums(
        lambda at: (k.trunk[at, :].astype(F32) * wide(k.mask[at, :], 512),), 1536, 512, 1
    )
    k.out_pool[...] = jnp.broadcast_to(own_sum, (8, 512))
    place = net.m * 2 + net.r
    pool_copies = [net.send(k.out_pool, k.in_pool.at[place], peer) for peer in near]
    k.in_pool[place] = k.out_pool[...]

    zero_margins(k.cells, 40, 128)

    def fill(i, carry):
        at = pl.ds(pl.multiple_of(i * 128, 128), 128)
        k.cells[i, 40:168, :] = k.trunk[at, :].astype(F32)
        return carry

    lax.fori_loop(0, 12, fill, 0)

    def shifted(i, offset):
        cells = k.cells[pl.ds(i * 3, 3), 40 + offset : 168 + offset, :]
        return cells.reshape(384, 512).astype(BF16)

    def rows_of(i):
        return pl.ds(pl.multiple_of(i * 384, 128), 384)

    def edge_rows(i, carry):
        total = 0.0
        for j in range(3):
            total = total + mm_t(shifted(i, 12 * (j - 1)), k.w_pyramid[10 + j])
        k.edge_out[rows_of(i), :] = total.astype(BF16)
        return carry

    lax.fori_loop(0, 4, edge_rows, 0)
    edge = net.send(k.edge_out, k.edge_in, net.core)

    def outer_rows(i, carry):
        second, third = 0.0, 0.0
        for j in range(3):
            second = second + mm_t(shifted(i, 24 * (j - 1)), k.w_pyramid[4 + j])
        for j in range(3):
            third = third + mm_t(shifted(i, 36 * (j - 1)), k.w_pyramid[7 + j])
        for b, block in enumerate(pair(second, third)):
            k.part[b, rows_of(i), 128:256] = block
        return carry

    lax.fori_loop(0, 4, outer_rows, 0)
    edge.wait()

    def inner_rows(i, carry):
        point = mm_t(k.trunk[rows_of(i), :], k.w_pyramid[0])
        first = k.edge_in[rows_of(i), :].astype(F32)
        for j in range(3):
            first = first + mm_t(shifted(i, 12 * (j - 1)), k.w_pyramid[1 + j])
        for b, block in enumerate(pair(point, first)):
            k.part[b, rows_of(i), 0:128] = block
        return carry

    lax.fori_loop(0, 4, inner_rows, 0)
    sum_scatter(net, k.part, scatter_refs(k, "sum"), k.branches)

    low_256 = lax.broadcasted_iota(jnp.int32, (256, 128), 1) < 64
    odd = lax.rem(net.m, 2) == 1

    def slot(s):
        lanes = pl.ds(pl.multiple_of(s * 256 + (net.m // 2) * 128, 128), 128)
        block = k.w_slots[:, lanes].astype(F32)
        return jnp.where(odd, pltpu.roll(block, 64, 1), block)

    for s in range(0, 4, 2):
        both = jnp.where(low_256, slot(s), pltpu.roll(slot(s + 1), 64, 1))
        k.w_project[:, s * 64 : s * 64 + 128] = both.astype(BF16)
    k.w_slot[...] = jnp.where(low_256, slot(4), 0.0).astype(BF16)
    k.w_pool[0:64, :] = k.aspp_pool[...]
    k.w_pool[64:128, :] = k.aspp_pool[...]

    for copy in pool_copies:
        copy.wait()
    for b in range(4):
        pooled = (k.in_pool[2 * b, 0:1, :] + k.in_pool[2 * b + 1, 0:1, :]) / area
        k.pooled[:, b * 512 : b * 512 + 512] = jnp.broadcast_to(pooled, (16, 512)).astype(BF16)
    pool_conv = mm_t(k.pooled[...], k.w_pool[...])[0:1, :]
    mean, inverse = statistics(
        net, k.branches, k.mask, counts, k.out_1, k.in_1, counted, extra=pool_conv
    )
    every = k.in_1[0:4, 4, :]
    pool_mean = jnp.sum(every, axis=0, keepdims=True) / 4.0
    pool_gap = every - pool_mean
    pool_inverse = lax.rsqrt(jnp.sum(pool_gap * pool_gap, axis=0, keepdims=True) / 4.0 + EPS)
    pool_normed = pool_gap * pool_inverse
    pool_gain, pool_bias = k.affine_p[2:3, :], k.affine_p[3:4, :]
    pool_u = pool_gain * pool_normed + pool_bias
    k.rows_scratch[0:4, :] = pool_u * sigmoid(pool_u)
    pool_act = jnp.broadcast_to(k.rows_scratch[pl.ds(net.z, 1), :], (16, 128)).astype(BF16)

    def normed_branch(at):
        return (k.branches[at, :] - mean) * inverse

    gain_b, bias_b = k.affine_b[0:1, :], k.affine_b[1:2, :]

    def activate_branches(at):
        u = gain_b * normed_branch(at) + bias_b
        k.spatial[at, :] = (u * sigmoid(u)).astype(BF16)

    each_rows(1536, 64, activate_branches)

    pool_row = mm_t(pool_act, k.w_slot[...])[0:1, :]

    def project_rows(i, carry):
        at = pl.ds(pl.multiple_of(i * 384, 128), 384)
        below = pl.ds(pl.multiple_of(i * 384 + 768, 128), 384)
        first = mm_t(k.spatial[at, :], k.w_project[...]) + pool_row
        second = mm_t(k.spatial[below, :], k.w_project[...]) + pool_row
        for b, block in enumerate(pair(first, second)):
            k.part_2[b, at, :] = block
        return carry

    lax.fori_loop(0, 2, project_rows, 0)
    low_128 = lax.broadcasted_iota(jnp.int32, (128, 128), 1) < 64

    def pair_mask(at):
        below = pl.ds(pl.multiple_of(at.start + 768, 128), 128)
        k.mask_pairs[at, :] = jnp.where(low_128, k.mask[at, :], k.mask[below, :])

    each_rows(768, 128, pair_mask)
    sum_scatter(net, k.part_2, scatter_refs(k, "sum2"), k.projected)
    mean_p, inverse_p = statistics(
        net, k.projected, k.mask_pairs, counts, k.out_2, k.in_2, counted, folded=True
    )
    gain_p, bias_p = k.affine_p[0:1, :], k.affine_p[1:2, :]

    def normed_projected(at):
        return (k.projected[at, :] - mean_p) * inverse_p

    def activate_projected(at):
        u = gain_p * normed_projected(at) + bias_p
        k.gathered[net.m, at, :] = (u * sigmoid(u)).astype(BF16)

    each_rows(768, 128, activate_projected)
    gather_blocks(net, lambda b, at: k.gathered.at[b, at], 768)

    def spread(source, target):
        def body(at):
            first, second = unpair([source[b, at, :].astype(F32) for b in range(4)])
            target[at, :] = first.astype(BF16)
            target[pl.ds(pl.multiple_of(at.start + 768, 128), 128), :] = second.astype(BF16)

        each_rows(768, 128, body)

    k.features[...] = k.gathered[net.m]
    spread(k.gathered, k.wide_features)

    class_row = lax.broadcasted_iota(jnp.int32, (32, 512), 0)
    is_class, is_depth = class_row < 19, class_row == 19
    is_normal = (class_row == 20) | (class_row == 21)
    tile_row = lax.broadcasted_iota(jnp.int32, (32, 128), 0)
    bias_column = jnp.zeros((32, 128), F32)
    for c in range(22):
        bias_column = jnp.where(tile_row == c, k.head_bias[c], bias_column)
    task = [jnp.exp(jnp.full((32, 128), -k.log_vars[t], F32)) / counted for t in range(3)]
    weight_column = jnp.where(tile_row < 19, task[0], jnp.where(tile_row == 19, task[1], task[2]))
    bias_column, weight_column = wide(bias_column, 512), wide(weight_column, 512)
    k.head[...] = k.head_rows[...].astype(BF16)
    top_row, left_edge = k.boxes[net.z, 0], k.boxes[net.z, 1]
    bottom_row, right_edge = top_row + k.boxes[net.z, 2], left_edge + k.boxes[net.z, 3]
    lane = lax.broadcasted_iota(jnp.int32, (1, 512), 1)

    def four_rows(rows):
        return jnp.concatenate(rows, axis=1)
    loss_sums, bias_sums = 0.0, 0.0
    for chunk in range(3):
        at = pl.ds(chunk * 512, 512)
        logits = mm_t(k.head[...], k.wide_features[at, :]) + bias_column
        row_id, column_id = net.r * 12 + chunk * 4 + lane // 128, lane % 128
        inside = (row_id >= top_row) & (row_id < bottom_row)
        inside = inside & (column_id >= left_edge) & (column_id < right_edge)
        inside = jnp.where(inside, 1.0, 0.0)
        span = range(chunk * 4, chunk * 4 + 4)
        label = four_rows([k.labels[0, y : y + 1, :] for y in span])
        target = jnp.where(is_depth, four_rows([k.depth[0, y : y + 1, :] for y in span]), 0.0)
        for n in range(2):
            normal = four_rows([k.normal[0, n, y : y + 1, :] for y in span])
            target = jnp.where(class_row == 20 + n, normal, target)
        top = jnp.max(jnp.where(is_class, logits, -jnp.inf), axis=0, keepdims=True)
        powers = jnp.where(is_class, jnp.exp(jnp.where(is_class, logits - top, 0.0)), 0.0)
        power_sum = jnp.sum(powers, axis=0, keepdims=True)
        onehot = jnp.where(class_row == label, 1.0, 0.0)
        cross = jnp.log(power_sum) + top - jnp.sum(logits * onehot, axis=0, keepdims=True)
        gap = logits - target
        smooth = jnp.sqrt(gap * gap + 1.0)
        loss = jnp.where(class_row == 0, cross, 0.0)
        loss = jnp.where(is_depth, smooth - 1.0, loss)
        loss = jnp.where(is_normal, gap * gap, loss) * inside
        grad = jnp.where(is_class, powers / power_sum - onehot, 0.0)
        grad = jnp.where(is_depth, gap / smooth, grad)
        grad = jnp.where(is_normal, 2.0 * gap, grad) * (weight_column * inside)
        loss_sums = loss_sums + jnp.sum(loss, axis=1, keepdims=True)
        bias_sums = bias_sums + jnp.sum(grad, axis=1, keepdims=True)
        high = grad.astype(BF16)
        k.grad_logits[0:32, at] = high
        k.grad_logits[32:64, at] = (grad - high.astype(F32)).astype(BF16)
    head_terms = mm(k.grad_logits[...], k.wide_features[...])
    k.out_head[:, 0:256] = head_terms[0:32, :] + head_terms[32:64, :]
    first_lane = lax.broadcasted_iota(jnp.int32, (32, 128), 1) == 0
    k.out_head[:, 256:384] = jnp.where(first_lane, bias_sums, loss_sums)
    quarter = pl.ds(pl.multiple_of(net.m * 8, 8), 8)
    head_copies = [
        net.send(k.out_head.at[quarter], k.in_head.at[net.slot], peer) for peer in net.group
    ]
    k.in_head[net.slot] = k.out_head[quarter, :]

    own_head = k.head_rows[:, lane_block(net.m // 2)]
    own_head = jnp.where(odd, pltpu.roll(own_head, 64, 1), own_head)
    own_head = jnp.where(low_128[0:32, :], own_head, 0.0)
    head_low = jnp.concatenate([own_head, own_head], axis=0).astype(BF16)
    own_head = pltpu.roll(own_head, 64, 1)
    head_high = jnp.concatenate([own_head, own_head], axis=0).astype(BF16)
    k.grad_p[...] = tm_m(k.grad_logits[:, 0:768], head_low) + tm_m(
        k.grad_logits[:, 768:1536], head_high
    )

    def back_features(at):
        k.grad_p[at, :] = k.grad_p[at, :] * slope(gain_p * normed_projected(at) + bias_p)

    each_rows(768, 128, back_features)
    bias_grad, gain_grad = gradient_sums(
        net, k.grad_p, normed_projected, k.out_3, k.in_3, folded=True
    )
    keep_rows(k.norm_p, gain_grad, bias_grad)

    def back_projected(at):
        shared = k.mask_pairs[at, :] / counted * gain_p
        grad = gain_p * k.grad_p[at, :] - shared * (bias_grad + normed_projected(at) * gain_grad)
        k.gathered_grad[net.m, at, :] = (inverse_p * grad).astype(BF16)

    each_rows(768, 128, back_projected)
    gather_blocks(net, lambda b, at: k.gathered_grad.at[b, at], 768)
    spread(k.gathered_grad, k.grad_projected)
    (pixel_sum,) = column_sums(lambda at: (k.grad_projected[at, :].astype(F32),), 1536, 256, 1)
    row_16 = lax.broadcasted_iota(jnp.int32, (16, 256), 0)
    terms = jnp.zeros((16, 256), F32)
    for i, term in enumerate(split_three(pixel_sum)):
        terms = jnp.where(row_16 == i, term.astype(F32), terms)
    terms = terms.astype(BF16)
    tall = jnp.concatenate([terms] * 8, axis=0)
    pool_grad = jnp.sum(mm(tall, k.w_slot[...]), axis=0, keepdims=True) * 0.125

    def project_gradient():
        for b in range(2):
            lanes = slice(b * 128, b * 128 + 128)
            grad = tm_m(k.grad_projected[:, lanes], k.spatial[...])
            k.grad_project[b * 4 : b * 4 + 4, :, 0:256] = grad.reshape(4, 32, 256).astype(BF16)
        grad = tm_m(terms, pool_act)
        k.grad_project[:, :, 256:384] = grad.reshape(8, 32, 128).astype(BF16)

    def back_spatial(at):
        grad = mm(k.grad_projected[at, :], k.w_project[...])
        k.grad_b[at, :] = grad * slope(gain_b * normed_branch(at) + bias_b)

    each_rows(1536, 128, back_spatial)
    bias_grad_b, gain_grad_b = gradient_sums(
        net,
        k.grad_b,
        normed_branch,
        k.out_4,
        k.in_4,
        extra=pool_grad,
        meanwhile=project_gradient,
    )
    keep_rows(k.norm_b, gain_grad_b, bias_grad_b)

    pool_terms = k.in_4[0:4, 4, :] + k.in_4[4:8, 4, :]
    pool_terms = pool_terms * slope(pool_u)
    pool_bias_grad = jnp.sum(pool_terms, axis=0, keepdims=True)
    pool_gain_grad = jnp.sum(pool_terms * pool_normed, axis=0, keepdims=True)
    keep_rows(k.norm_pool, pool_gain_grad, pool_bias_grad)
    pool_back = pool_inverse * (
        pool_gain * pool_terms
        - pool_gain / 4.0 * (pool_bias_grad + pool_normed * pool_gain_grad)
    )
    low = lax.broadcasted_iota(jnp.int32, (4, 128), 1) < 64
    k.rows_scratch[4:8, :] = jnp.where(low, pool_back, 0.0)
    grad_conv = jnp.broadcast_to(k.rows_scratch[pl.ds(net.z + 4, 1), :], (16, 128)).astype(BF16)
    spread_back = mm(grad_conv, k.w_pool[...])[0:8, :]
    for b in range(4):
        k.out_back[b] = spread_back[:, b * 512 : b * 512 + 512]
    back_copies = [
        net.send(k.out_back.at[lax.rem(net.m + a, 4)], k.in_back.at[a], (lax.rem(net.m + a, 4), net.r, net.z))
        for a in range(1, 4)
    ]

    only_first = lax.broadcasted_iota(jnp.int32, (16, 128), 0) == 0
    one_row = jnp.where(only_first, grad_conv.astype(F32) * 0.5, 0.0).astype(BF16)
    for e in range(8):
        grad = tm_m(one_row, k.pooled[:, e * 256 : e * 256 + 256])
        k.grad_pool[e] = grad[0:64, :].astype(BF16)

    def back_branches(at):
        shared = wide(k.mask[at, :], 256) / counted * gain_b
        grad = gain_b * k.grad_b[at, :] - shared * (bias_grad_b + normed_branch(at) * gain_grad_b)
        k.grad_branches[at, :] = (inverse * grad).astype(BF16)

    for copy in back_copies:
        copy.wait()
    k.grad_pooled[...] = (k.out_back[net.m] + k.in_back[1] + k.in_back[2] + k.in_back[3]) / area
    for copy in head_copies:
        copy.wait()
    k.head_sums[quarter, :] = jnp.sum(k.in_head[...], axis=0)
    head_copies = [
        net.send(k.head_sums.at[quarter], k.head_sums.at[quarter], (lax.rem(net.m + a, 4), net.r, net.z))
        for a in range(1, 4)
    ]
    each_rows(1536, 64, back_branches)
    for copy in head_copies:
        copy.wait()


def run_pyramid(args):
    return call_kernel(
        pyramid_forward,
        "pyramid",
        1,
        args,
        dict(
            features=((768, 128), BF16),
            norm_p=((8, 128), F32),
            grad_project=((8, 32, 384), BF16),
            grad_pool=((8, 64, 256), BF16),
            norm_b=((8, 256), F32),
            norm_pool=((8, 128), F32),
            grad_branches=((1536, 256), BF16),
            grad_pooled=((8, 512), F32),
            head_sums=((32, 384), F32),
        ),
        dict(
            affine_b=pltpu.VMEM((8, 256), F32),
            affine_p=pltpu.VMEM((8, 128), F32),
            head_rows=pltpu.VMEM((32, 256), F32),
            head=pltpu.VMEM((32, 256), BF16),
            pooled=pltpu.VMEM((16, 2048), BF16),
            spatial=pltpu.VMEM((1536, 256), BF16),
            grad_projected=pltpu.VMEM((1536, 256), BF16),
            w_project=pltpu.VMEM((256, 256), BF16),
            w_slot=pltpu.VMEM((256, 128), BF16),
            w_pool=pltpu.VMEM((128, 2048), BF16),
            mask_pairs=pltpu.VMEM((768, 128), F32),
            out_pool=pltpu.VMEM((8, 512), F32),
            in_pool=pltpu.VMEM((8, 8, 512), F32),
            cells=pltpu.VMEM((12, 208, 512), F32),
            edge_out=pltpu.VMEM((1536, 256), BF16),
            edge_in=pltpu.VMEM((1536, 256), BF16),
            part=pltpu.VMEM((4, 1536, 256), F32),
            **scatter_scratch("sum", 1536, 256),
            branches=pltpu.VMEM((1536, 256), F32),
            rows_scratch=pltpu.VMEM((8, 128), F32),
            part_2=pltpu.VMEM((4, 768, 128), F32),
            **scatter_scratch("sum2", 768, 128),
            projected=pltpu.VMEM((768, 128), F32),
            gathered=pltpu.VMEM((4, 768, 128), BF16),
            wide_features=pltpu.VMEM((1536, 256), BF16),
            grad_logits=pltpu.VMEM((64, 1536), BF16),
            out_head=pltpu.VMEM((32, 384), F32),
            in_head=pltpu.VMEM((8, 8, 384), F32),
            grad_p=pltpu.VMEM((768, 128), F32),
            gathered_grad=pltpu.VMEM((4, 768, 128), BF16),
            grad_b=pltpu.VMEM((1536, 256), F32),
            out_back=pltpu.VMEM((4, 8, 512), F32),
            in_back=pltpu.VMEM((4, 8, 512), F32),
            **exchange_scratch(1),
            **exchange_scratch(2),
            **exchange_scratch(3),
            **exchange_scratch(4),
        ),
        96,
        smem=("boxes", "head_bias", "log_vars"),
    )


def core_halves(net, whole, arrived):
    away = pl.ds(pl.multiple_of(4 - 4 * net.r, 4), 4)
    return net.send(whole.at[away], arrived, net.core)


def add_halves(net, whole, arrived, target):
    for z in range(4):
        total = whole[4 * net.r + z].astype(F32) + arrived[z].astype(F32)
        target[z] = total.astype(target.dtype)


def z_copies(net, source, target):
    copies = []
    for d in (1, 2, 3):
        i = net.count
        net.count += 1
        there = lax.rem(net.z + d, 4)
        copies.append(
            pltpu.make_async_remote_copy(
                src_ref=source.at[there],
                dst_ref=target.at[d - 1],
                send_sem=net.send_sems.at[i],
                recv_sem=net.recv_sems.at[i],
                device_id=(net.m, net.r, there),
                device_id_type=MESH,
            )
        )
    return copies


def along_z(net, source, target):
    copies = z_copies(net, source, target)
    for copy in copies:
        copy.start()
    return copies


def finish_z(net, half, arrived):
    return half[net.z].astype(F32) + sum(arrived[d].astype(F32) for d in range(3))


def add_z(net, half, arrived, target):
    def body(i, carry):
        total = half[net.z, i].astype(F32)
        for d in range(3):
            total = total + arrived[d, i].astype(F32)
        target[i] = total.astype(BF16)
        return carry

    lax.fori_loop(0, 16, body, 0)


def pyramid_backward(net, k):
    counted = pixel_count(k.boxes)
    greet([net.side, net.over] + net.group)
    k.blocks[net.m] = k.grad_branches[...]
    small = [
        core_halves(net, k.grad_project, k.core_project),
        core_halves(net, k.grad_pool, k.core_pool),
    ]
    for c in range(4):
        zero_margins(k.cells.at[c], 40, 128)

    def rows_of(i, size=384):
        return pl.ds(pl.multiple_of(i * size, 128), size)

    low = lax.broadcasted_iota(jnp.int32, (128, 128), 1) < 64
    near = net.m // 2
    far = 1 - near
    mine_first = net.r == near
    mine_second = net.r == far

    def both(source, pair_of, i, lane):
        at = slice(lane * 128, lane * 128 + 128)
        left = source[2 * pair_of, rows_of(i, 128), at].astype(F32)
        right = source[2 * pair_of + 1, rows_of(i, 128), at].astype(F32)
        first = jnp.where(low, left, pltpu.roll(right, 64, 1))
        return first, jnp.where(low, pltpu.roll(left, 64, 1), right)

    def shift_rows(pair_of, i, cell, rate, base):
        for j in range(3):
            start = 40 - rate * (j - 1)
            block = k.cells[cell, i, start : start + 128, :].astype(BF16)
            k.shifts[base + j, rows_of(i, 128), lane_block(pair_of)] = block

    def build(pair_of):
        def fill(i, carry):
            point, first = both(k.blocks, pair_of, i, 0)
            k.shifts[0, rows_of(i, 128), lane_block(pair_of)] = point.astype(BF16)
            second, third = both(k.blocks, pair_of, i, 1)
            k.cells[0, i, 40:168, :] = first
            k.cells[1, i, 40:168, :] = second
            k.cells[2, i, 40:168, :] = third
            return carry

        lax.fori_loop(0, 12, fill, 0)

        def spread(i, carry):
            for cell, rate, base in ((0, 12, 1), (1, 24, 4), (2, 36, 7)):
                shift_rows(pair_of, i, cell, rate, base)
            return carry

        lax.fori_loop(0, 12, spread, 0)

    def build_edge(pair_of):
        def fill(i, carry):
            k.cells[3, i, 40:168, :] = both(k.other, pair_of, i, 0)[1]
            return carry

        lax.fori_loop(0, 12, fill, 0)

        def spread(i, carry):
            shift_rows(pair_of, i, 3, 12, 10)
            return carry

        lax.fori_loop(0, 12, spread, 0)

    def weight_gradients(pair_of):
        owners = pl.ds(4 * pair_of, 4)

        def run(start, stop, shift):
            def body(t, carry):
                grad = tm_m(k.shifts[t, :, lane_block(pair_of)], k.trunk[...])
                k.grad_pyramid[owners, t + shift] = grad.reshape(4, 32, 512).astype(BF16)
                return carry

            lax.fori_loop(start, stop, body, 0)

        run(0, 1, 0)
        run(1, 4, 3)
        run(4, 10, 6)
        run(10, 13, net.r * 6 - 9)
        for j in range(3):
            k.grad_pyramid[owners, 7 - net.r * 6 + j] = jnp.zeros((4, 32, 512), BF16)

    def beside(pair_of):
        view = (pl.ds(2 * pair_of, 2), slice(None), pl.ds(0, 128))
        return net.send(k.blocks.at[view], k.other.at[pl.ds(2 * pair_of, 2)], net.core)

    def to_core(pair_of):
        i = net.count
        net.count += 1
        return pltpu.make_async_remote_copy(
            src_ref=k.grad_pyramid.at[pl.ds(4 * pair_of, 4)],
            dst_ref=k.core_pyramid,
            send_sem=net.send_sems.at[i],
            recv_sem=net.recv_sems.at[i],
            device_id=net.core,
            device_id_type=MESH,
        )

    def add_core(pair_of):
        def body(i, carry):
            for z in range(4):
                total = k.grad_pyramid[4 * pair_of + z, i].astype(F32)
                total = total + k.core_pyramid[z, i].astype(F32)
                k.half_pyramid[z, i] = total.astype(BF16)
            return carry

        lax.fori_loop(0, 16, body, 0)

    first_swap = []

    def near_pair():
        copy = beside(near)
        build(near)
        copy.wait()
        build_edge(near)
        weight_gradients(near)
        first_swap.append(to_core(near))
        pl.when(mine_second)(first_swap[0].start)

    gather_blocks(net, lambda b, at: k.blocks.at[b, at], 1536, meanwhile=near_pair)
    copy = beside(far)
    build(far)
    for swap in small:
        swap.wait()
    add_halves(net, k.grad_project, k.core_project, k.half_project)
    add_halves(net, k.grad_pool, k.core_pool, k.half_pool)
    small_moves = along_z(net, k.half_project, k.z_project) + along_z(net, k.half_pool, k.z_pool)
    copy.wait()
    build_edge(far)
    z_moves = z_copies(net, k.half_pyramid, k.z_pyramid)

    @pl.when(mine_first)
    def _():
        first_swap[0].wait_recv()
        add_core(near)
        for move_ in z_moves:
            move_.start()

    def trunk_rows(i, carry):
        total = 0.0
        for t in range(13):
            total = total + mm(k.shifts[t, rows_of(i), :], k.w_pyramid[t])
        k.shortcut[rows_of(i), :] = total
        return carry

    lax.fori_loop(0, 4, trunk_rows, 0)
    mean, inverse = k.stats_3[0:1, :], k.stats_3[1:2, :]
    gain, bias = k.affine_3[0:1, :], k.affine_3[1:2, :]
    pooled = k.grad_pooled[0:1, :]

    def normed(at):
        return (k.expanded[at, :] - mean) * inverse

    def back_trunk(at):
        u = gain * normed(at) + bias + k.x[at, :].astype(F32)
        grad = k.shortcut[at, :] + wide(k.mask[at, :], 512) * pooled
        k.shortcut[at, :] = grad * slope(u)

    each_rows(1536, 32, back_trunk)

    second_swap = to_core(far)

    def far_gradients():
        weight_gradients(far)
        pl.when(mine_first)(second_swap.start)

    bias_grad, gain_grad = gradient_sums(
        net, k.shortcut, normed, k.out_1, k.in_1, meanwhile=far_gradients
    )
    keep_rows(k.norm_3, gain_grad, bias_grad)

    def back_expanded(at):
        shared = wide(k.mask[at, :], 512) / counted * gain
        grad = gain * k.shortcut[at, :] - shared * (bias_grad + normed(at) * gain_grad)
        k.grad_expanded[at, :] = (inverse * grad).astype(BF16)

    each_rows(1536, 32, back_expanded)
    for move_ in small_moves:
        move_.wait()
    k.sum_project[...] = finish_z(net, k.half_project, k.z_project)
    k.sum_pool[...] = finish_z(net, k.half_pool, k.z_pool)

    @pl.when(mine_second)
    def _():
        first_swap[0].wait_send()
        second_swap.wait_recv()
        add_core(far)

    @pl.when(mine_first)
    def _():
        second_swap.wait_send()
        for move_ in z_moves:
            move_.wait()
        add_z(net, k.half_pyramid, k.z_pyramid, k.sum_pyramid)


def run_pyramid_backward(args):
    return call_kernel(
        pyramid_backward,
        "pyramid_back",
        2,
        args,
        dict(
            shortcut=((1536, 512), F32),
            grad_expanded=((1536, 512), BF16),
            norm_3=((8, 512), F32),
            half_pyramid=((4, 16, 32, 512), BF16),
            sum_pyramid=((16, 32, 512), BF16),
            sum_project=((32, 384), F32),
            sum_pool=((64, 256), F32),
        ),
        dict(
            half_project=pltpu.VMEM((4, 32, 384), BF16),
            half_pool=pltpu.VMEM((4, 64, 256), BF16),
            z_pyramid=pltpu.VMEM((3, 16, 32, 512), BF16),
            z_project=pltpu.VMEM((3, 32, 384), BF16),
            z_pool=pltpu.VMEM((3, 64, 256), BF16),
            grad_pyramid=pltpu.VMEM((8, 16, 32, 512), BF16),
            core_pyramid=pltpu.VMEM((4, 16, 32, 512), BF16),
            core_project=pltpu.VMEM((4, 32, 384), BF16),
            core_pool=pltpu.VMEM((4, 64, 256), BF16),
            blocks=pltpu.VMEM((4, 1536, 256), BF16),
            other=pltpu.VMEM((4, 1536, 128), BF16),
            cells=pltpu.VMEM((4, 12, 208, 128), F32),
            shifts=pltpu.VMEM((13, 1536, 256), BF16),
            **exchange_scratch(1),
        ),
        48,
    )


def bottleneck_backward(net, k):
    counted = pixel_count(k.boxes)
    loads = load_taps(k)
    odd = lax.rem(net.slot, 2)
    owners = []
    for which in (odd, 1 - odd):
        part = 2 * net.m + which
        owners.append((net.slot // 2, part // 4, lax.rem(part, 4)))
    stays = net.slot // 2 == net.m
    moves = jnp.logical_not(stays)
    greet([net.side, net.over] + net.group + [owners[1]], (owners[0], moves))

    def to_owners(views, arrived, sem, start=True):
        first = pltpu.make_async_remote_copy(
            src_ref=views(0),
            dst_ref=arrived.at[0],
            send_sem=net.send_sems.at[net.count],
            recv_sem=net.recv_sems.at[net.count],
            device_id=owners[0],
            device_id_type=MESH,
        )
        net.count += 1
        kept = pltpu.make_async_copy(views(0), arrived.at[0], sem)
        i = net.count
        net.count += 1
        second = pltpu.make_async_remote_copy(
            src_ref=views(1),
            dst_ref=arrived.at[1],
            send_sem=net.send_sems.at[i],
            recv_sem=net.recv_sems.at[i],
            device_id=owners[1],
            device_id_type=MESH,
        )

        def begin():
            pl.when(moves)(first.start)
            pl.when(stays)(kept.start)
            second.start()

        def wait():
            pl.when(moves)(first.wait)
            pl.when(stays)(kept.wait)
            second.wait()

        if start:
            begin()
            return wait
        return begin, wait

    def lanes_for(i):
        return lane_block(odd if i == 0 else 1 - odd, 256)

    early = net.r == net.m // 2
    is_late = net.r == 1 - net.m // 2
    pyramid_moves = z_copies(net, k.half_pyramid, k.z_pyramid)

    begin_pyramid, wait_pyramid = to_owners(
        lambda i: k.pyramid_sum.at[:, :, lanes_for(i)], k.own_pyramid, k.local_sems.at[9], False
    )

    @pl.when(is_late)
    def _():
        for move_ in pyramid_moves:
            move_.start()

    @pl.when(early)
    def _():
        k.pyramid_sum[...] = k.sum_pyramid[...]
        begin_pyramid()

    wait_project = to_owners(lambda i: k.sum_project, k.own_project, k.local_sems.at[10])

    def rows_of(i, size=384):
        return pl.ds(pl.multiple_of(i * size, 128), size)

    def expand_rows(at):
        total = mm_t(k.grad_expanded[at, :], k.w_expand[...])
        for b in range(4):
            k.part[b, at, :] = total[:, b * 128 : b * 128 + 128]

    each_rows(1536, 384, expand_rows)
    swaps, late_moves = [], []

    def expand_gradient():
        def body(b, carry):
            grad = tm_m(k.hidden_two[:, lane_block(b)], k.grad_expanded[...])
            k.grad_expand[pl.ds(2 * b, 2)] = grad.reshape(2, 64, 512).astype(BF16)
            return carry

        lax.fori_loop(0, 4, body, 0)
        swaps.append(core_halves(net, k.grad_expand, k.core_expand))

    sum_scatter(net, k.part, scatter_refs(k, "sum"), k.grad_2, meanwhile=expand_gradient)

    def norm_back(grad, value, stats, affine, outgoing, incoming, store, kept, meanwhile=None):
        mean, inverse = stats[0:1, :], stats[1:2, :]
        gain, bias = affine[0:1, :], affine[1:2, :]

        def normed(at):
            return (value[at, :] - mean) * inverse

        def through(at):
            grad[at, :] = grad[at, :] * slope(gain * normed(at) + bias)

        each_rows(1536, 128, through)
        bias_grad, gain_grad = gradient_sums(
            net, grad, normed, outgoing, incoming, meanwhile=meanwhile
        )
        keep_rows(kept, gain_grad, bias_grad)

        def back(at):
            shared = k.mask[at, :] / counted * gain
            result = gain * grad[at, :] - shared * (bias_grad + normed(at) * gain_grad)
            store(at, (inverse * result).astype(BF16))

        each_rows(1536, 128, back)

    def store_2(at, value):
        k.grad_pad[pl.ds(pl.multiple_of(at.start + 512, 128), 128), :] = value

    def pass_expand():
        swaps.pop().wait()
        add_halves(net, k.grad_expand, k.core_expand, k.half_expand)
        late_moves.extend(along_z(net, k.half_expand, k.z_expand))

    norm_back(
        k.grad_2,
        k.dilated,
        k.stats_2,
        k.affine_2,
        k.out_2,
        k.in_2,
        store_2,
        k.norm_2,
        meanwhile=pass_expand,
    )
    halo = send_halo(net, k.grad_pad)
    zero_margins(k.cells, 8, 128)
    halo.wait()

    def spread(i, carry):
        k.cells[i, 8:136, :] = k.grad_pad[rows_of(i, 128), :].astype(F32)
        for j in range(3):
            start = 8 - 4 * (j - 1)
            k.grad_taps[rows_of(i, 128), j * 128 : j * 128 + 128] = k.cells[
                i, start : start + 128, :
            ].astype(BF16)
        return carry

    lax.fori_loop(0, 20, spread, 0)
    for load in loads:
        load.wait()

    def dilated_rows(i, carry):
        total = 0.0
        for tap in range(3):
            at = pl.ds(pl.multiple_of((i * 3 + 8 - 4 * tap) * 128, 128), 384)
            total = total + mm_t(k.grad_taps[at, :], k.w_taps[tap])
        for b in range(4):
            k.part[b, rows_of(i), :] = total[:, b * 128 : b * 128 + 128]
        return carry

    lax.fori_loop(0, 4, dilated_rows, 0)
    def dilated_gradient():
        for i in range(3):

            def body(b, carry):
                band = k.hidden[pl.ds(i * 512, 1536), lane_block(b)]
                grad = tm_m(band, k.grad_taps[pl.ds(512, 1536), :])
                for j in range(3):
                    block = grad[:, j * 128 : j * 128 + 128].reshape(2, 64, 128)
                    rows = slice((i * 3 + j) * 64, (i * 3 + j) * 64 + 64)
                    k.grad_dilated[pl.ds(2 * b, 2), rows, :] = block.astype(BF16)
                return carry

            lax.fori_loop(0, 4, body, 0)
        swaps.append(core_halves(net, k.grad_dilated, k.core_dilated))

    sum_scatter(net, k.part, scatter_refs(k, "sum2"), k.grad_1, meanwhile=dilated_gradient)

    def store_1(at, value):
        k.grad_reduced[at, lane_block(net.m)] = value

    def pass_halves():
        swaps.pop().wait()
        add_halves(net, k.grad_dilated, k.core_dilated, k.half_dilated)
        late_moves.extend(along_z(net, k.half_dilated, k.z_dilated))

        @pl.when(is_late)
        def _():
            for move_ in pyramid_moves:
                move_.wait()
            add_z(net, k.half_pyramid, k.z_pyramid, k.pyramid_sum)
            begin_pyramid()

    norm_back(
        k.grad_1,
        k.reduced,
        k.stats_1,
        k.affine_1,
        k.out_1,
        k.in_1,
        store_1,
        k.norm_1,
        meanwhile=pass_halves,
    )
    gather_blocks(net, lambda b, at: k.grad_reduced.at[at, lane_block(b)], 1536)

    def reduce_gradient(b, carry):
        grad = tm_m(k.grad_reduced[:, lane_block(b)], k.x[...])
        k.grad_reduce[pl.ds(2 * b, 2)] = grad.reshape(2, 64, 512).astype(BF16)
        return carry

    lax.fori_loop(0, 4, reduce_gradient, 0)
    swap = core_halves(net, k.grad_reduce, k.core_reduce)

    swap.wait()
    add_halves(net, k.grad_reduce, k.core_reduce, k.half_reduce)
    reduce_moves = along_z(net, k.half_reduce, k.z_reduce)

    for move_ in reduce_moves:
        move_.wait()
    k.sum_reduce[...] = finish_z(net, k.half_reduce, k.z_reduce)
    wait_reduce = to_owners(
        lambda i: k.sum_reduce.at[:, lanes_for(i)], k.own_reduce, k.local_sems.at[11]
    )
    for move_ in late_moves:
        move_.wait()
    k.sum_dilated[...] = finish_z(net, k.half_dilated, k.z_dilated)
    k.sum_expand[...] = finish_z(net, k.half_expand, k.z_expand)
    wait_pyramid()
    wait_project()
    wait_reduce()


def run_bottleneck_backward(args):
    return call_kernel(
        bottleneck_backward,
        "bottleneck_back",
        3,
        args,
        dict(
            grad_reduced=((1536, 512), BF16),
            norm_2=((8, 128), F32),
            norm_1=((8, 128), F32),
            own_pyramid=((2, 16, 32, 256), BF16),
            own_project=((2, 32, 384), F32),
            sum_dilated=((576, 128), F32),
            sum_expand=((64, 512), F32),
            own_reduce=((2, 64, 256), F32),
        ),
        dict(
            grad_taps=pltpu.VMEM((2560, 384), BF16),
            z_pyramid=pltpu.VMEM((3, 16, 32, 512), BF16),
            pyramid_sum=pltpu.VMEM((16, 32, 512), BF16),
            sum_reduce=pltpu.VMEM((64, 512), F32),
            grad_expand=pltpu.VMEM((8, 64, 512), BF16),
            core_expand=pltpu.VMEM((4, 64, 512), BF16),
            half_expand=pltpu.VMEM((4, 64, 512), BF16),
            z_expand=pltpu.VMEM((3, 64, 512), BF16),
            grad_reduce=pltpu.VMEM((8, 64, 512), BF16),
            core_reduce=pltpu.VMEM((4, 64, 512), BF16),
            half_reduce=pltpu.VMEM((4, 64, 512), BF16),
            z_reduce=pltpu.VMEM((3, 64, 512), BF16),
            grad_dilated=pltpu.VMEM((8, 576, 128), BF16),
            core_dilated=pltpu.VMEM((4, 576, 128), BF16),
            half_dilated=pltpu.VMEM((4, 576, 128), BF16),
            z_dilated=pltpu.VMEM((3, 576, 128), BF16),
            w_taps=pltpu.VMEM((3, 512, 384), BF16),
            part=pltpu.VMEM((4, 1536, 128), F32),
            **scatter_scratch("sum", 1536, 128),
            **scatter_scratch("sum2", 1536, 128),
            grad_2=pltpu.VMEM((1536, 128), F32),
            grad_1=pltpu.VMEM((1536, 128), F32),
            grad_pad=pltpu.VMEM((2560, 128), BF16),
            cells=pltpu.VMEM((20, 144, 128), F32),
            **exchange_scratch(2),
            **exchange_scratch(1),
            local_sems=pltpu.SemaphoreType.DMA((12,)),
        ),
        96,
        hbm=("w_dilated",),
    )


def finish(net, k):
    counted = pixel_count(k.boxes)
    odd = lax.rem(lax.axis_index("batch"), 2)

    def rows_for(i):
        return pl.ds(pl.multiple_of((odd if i == 0 else 1 - odd) * 32, 32), 32)

    nothing = jnp.zeros((64, 256), F32)
    for tap in (9, 10, 11, 15, 16, 17, 18, 19, 20, 24, 25, 26):
        k.grad_rates[tap] = nothing
    for slot in range(16):
        for i in range(2):
            block = k.own_pyramid[i, slot].astype(F32)
            if slot == 0:
                k.grad_point[rows_for(i), :] = block
            else:
                tap = slot - 1 if slot < 10 else slot + 2 if slot < 13 else slot + 8
                k.grad_rates[tap, rows_for(i), :] = block
    low = lax.broadcasted_iota(jnp.int32, (768, 128), 1) < 64
    packed = k.packed[...].astype(F32)
    k.features[0:768, :] = packed[:, 0:64].astype(BF16)
    k.features[768:1536, :] = pltpu.roll(packed, 64, 1)[:, 0:64].astype(BF16)
    for i in range(2):
        block = k.own_project[i]
        for slot in range(5):
            part = block[:, (slot // 2) * 128 : (slot // 2) * 128 + 128]
            if slot % 2:
                part = pltpu.roll(part, 64, 1)
            part = jnp.where(odd == 1, pltpu.roll(part, 96, 1), part)
            k.grad_project[rows_for(i), slot, :] = part[:, 0:32]
    rows = jnp.concatenate([k.own_reduce[0], k.own_reduce[1]], axis=0)
    swapped = jnp.concatenate([k.own_reduce[1], k.own_reduce[0]], axis=0)
    k.grad_reduce[...] = jnp.where(odd == 0, rows, swapped).T
    k.grad_dilated[...] = k.from_dilated[...].reshape(9, 64, 128)
    k.grad_expand[...] = k.from_expand[...]
    k.grad_pool[...] = k.from_pool[...]
    k.grad_norm_1[...] = k.norm_1[0:2, :]
    k.grad_norm_2[...] = k.norm_2[0:2, :]
    k.grad_norm_3[...] = k.norm_3[0:2, :]
    for b in range(4):
        k.grad_norm_b[:, b, :] = k.norm_b[0:2, b * 64 : b * 64 + 64]
    k.grad_norm_pool[...] = k.norm_pool[0:2, 0:64]
    k.grad_norm_p[...] = k.norm_p[0:2, 0:64]
    k.grad_head_weight[...] = k.head_sums[:, 0:256].T[:, 0:22]
    columns = k.head_sums[:, 256:384].T
    k.grad_head_bias[...] = columns[0:1, 0:22]
    loss = columns[1:2, :]
    task = lax.broadcasted_iota(jnp.int32, (1, 32), 1)

    def total(inside):
        return jnp.sum(jnp.where(inside, loss, 0.0), axis=1, keepdims=True) / counted

    terms = [total(task == 0), total(task == 19), total((task == 20) | (task == 21))]
    lane = lax.broadcasted_iota(jnp.int32, (1, 128), 1)
    losses = jnp.where(lane == 0, terms[0], jnp.where(lane == 1, terms[1], terms[2]))
    log_vars = jnp.where(
        lane == 0, k.log_vars[0], jnp.where(lane == 1, k.log_vars[1], k.log_vars[2])
    )
    weighted = jnp.exp(-log_vars) * losses
    k.total_loss[...] = jnp.sum(
        jnp.where(lane < 3, weighted + log_vars, 0.0), axis=1, keepdims=True
    )
    k.grad_log_vars[...] = (1.0 - weighted)[:, 0:3]

    def input_rows(at):
        total = k.shortcut[at, :]
        for b in range(4):
            total = total + mm_t(k.grad_reduced[at, b * 128 : b * 128 + 128], k.w_reduce[b])
        k.grad_input[at, :] = total

    each_rows(1536, 384, input_rows)


def run_finish(args):
    return call_kernel(
        finish,
        "finish",
        None,
        args,
        dict(
            features=((1536, 64), BF16),
            total_loss=((1, 1), F32),
            grad_input=((1536, 512), F32),
            grad_reduce=((256, 128), F32),
            grad_dilated=((9, 64, 128), F32),
            grad_expand=((64, 512), F32),
            grad_norm_1=((2, 128), F32),
            grad_norm_2=((2, 128), F32),
            grad_norm_3=((2, 512), F32),
            grad_point=((64, 256), F32),
            grad_rates=((27, 64, 256), F32),
            grad_pool=((64, 256), F32),
            grad_norm_b=((2, 4, 64), F32),
            grad_norm_pool=((2, 64), F32),
            grad_project=((64, 5, 32), F32),
            grad_norm_p=((2, 64), F32),
            grad_head_weight=((256, 22), F32),
            grad_head_bias=((1, 22), F32),
            grad_log_vars=((1, 3), F32),
        ),
        {},
        0,
        smem=("boxes", "log_vars"),
    )


def fast_local(
    trunk_input,
    conv_reduce,
    conv_dilated,
    conv_expand,
    reduction_norm_params,
    dilated_norm_params,
    expansion_norm_params,
    aspp_point,
    aspp_rates,
    aspp_pool,
    branch_norms,
    pooling_norm_params,
    aspp_project,
    projection_norm_params,
    head_weight,
    head_bias,
    log_vars,
    crop_boxes,
    seg_labels,
    depth_target,
    normal_target,
):
    x = trunk_input.reshape(1536, 512)
    forward = run_bottleneck(
        dict(
            x=x,
            conv_reduce=conv_reduce,
            w_dilated=conv_dilated,
            w_expand=conv_expand,
            aspp_point=aspp_point,
            aspp_rates=aspp_rates,
            project=aspp_project.reshape(64, 1280),
            affine_1=reduction_norm_params,
            affine_2=dilated_norm_params,
            affine_3=expansion_norm_params,
            boxes=crop_boxes,
        )
    )
    w_pyramid = forward.w_pyramid.reshape(13, 256, 512)

    middle = run_pyramid(
        dict(
            trunk=forward.trunk,
            mask=forward.mask,
            w_pyramid=w_pyramid,
            branch_norms=branch_norms,
            norm_project=projection_norm_params,
            norm_pooling=pooling_norm_params,
            aspp_pool=aspp_pool,
            w_slots=forward.w_project.reshape(256, 1280),
            head_weight=head_weight,
            head_bias=head_bias,
            log_vars=log_vars,
            labels=seg_labels,
            depth=depth_target,
            normal=normal_target,
            boxes=crop_boxes,
        )
    )
    back = run_pyramid_backward(
        dict(
            grad_branches=middle.grad_branches,
            w_pyramid=w_pyramid,
            x=x,
            trunk=forward.trunk,
            expanded=forward.expanded,
            stats_3=forward.stats_3,
            affine_3=expansion_norm_params,
            mask=forward.mask,
            grad_pooled=middle.grad_pooled,
            grad_project=middle.grad_project,
            grad_pool=middle.grad_pool,
            boxes=crop_boxes,
        )
    )
    last = run_bottleneck_backward(
        dict(
            grad_expanded=back.grad_expanded,
            half_pyramid=back.half_pyramid,
            sum_pyramid=back.sum_pyramid,
            sum_project=back.sum_project,
            x=x,
            hidden=forward.hidden,
            hidden_two=forward.hidden_two,
            w_expand=conv_expand,
            w_dilated=conv_dilated,
            dilated=forward.dilated,
            stats_2=forward.stats_2,
            affine_2=dilated_norm_params,
            reduced=forward.reduced,
            stats_1=forward.stats_1,
            affine_1=reduction_norm_params,
            mask=forward.mask,
            boxes=crop_boxes,
        )
    )
    done = run_finish(
        dict(
            shortcut=back.shortcut,
            grad_reduced=last.grad_reduced,
            w_reduce=forward.w_reduce,
            own_pyramid=last.own_pyramid,
            packed=middle.features,
            own_project=last.own_project,
            own_reduce=last.own_reduce,
            from_dilated=last.sum_dilated,
            from_expand=last.sum_expand,
            from_pool=back.sum_pool,
            norm_1=last.norm_1,
            norm_2=last.norm_2,
            norm_3=back.norm_3,
            norm_b=middle.norm_b,
            norm_pool=middle.norm_pool,
            norm_p=middle.norm_p,
            head_sums=middle.head_sums,
            log_vars=log_vars,
            boxes=crop_boxes,
        )
    )
    return (
        done.features.reshape(1, 12, 128, 64),
        done.total_loss.reshape(()),
        done.grad_input.reshape(1, 12, 128, 512),
        done.grad_reduce,
        done.grad_dilated.reshape(3, 3, 64, 128),
        done.grad_expand,
        done.grad_norm_1,
        done.grad_norm_2,
        done.grad_norm_3,
        done.grad_point,
        done.grad_rates.reshape(3, 3, 3, 64, 256),
        done.grad_pool,
        done.grad_norm_b,
        done.grad_norm_pool,
        done.grad_project,
        done.grad_norm_p,
        done.grad_head_weight,
        done.grad_head_bias.reshape(22),
        done.grad_log_vars.reshape(3),
    )


def local(
    trunk_input,
    conv_reduce,
    conv_dilated,
    conv_expand,
    reduction_norm_params,
    dilated_norm_params,
    expansion_norm_params,
    aspp_point,
    aspp_rates,
    aspp_pool,
    branch_norms,
    pooling_norm_params,
    aspp_project,
    projection_norm_params,
    head_weight,
    head_bias,
    log_vars,
    crop_boxes,
    seg_labels,
    depth_target,
    normal_target,
):
    image_inputs, tile_row_count, frame_columns, quarter = trunk_input.shape
    pixels = image_inputs * tile_row_count * frame_columns
    branch_part = aspp_point.shape[0]
    branch_total = lax.axis_size("branch")
    row_portion = 1.0 / lax.axis_size("rows")
    image_overall_count = float(crop_boxes.shape[0])
    first_image = lax.axis_index("batch") * image_inputs
    first_row = lax.axis_index("rows") * tile_row_count
    my_boxes = lax.dynamic_slice_in_dim(crop_boxes, first_image, image_inputs, 0)
    row_ids = first_row + jnp.arange(tile_row_count, dtype=jnp.int32)
    col_ids = jnp.arange(frame_columns, dtype=jnp.int32)
    inside_rows = (row_ids[None, :] >= my_boxes[:, 0:1]) & (
        row_ids[None, :] < my_boxes[:, 0:1] + my_boxes[:, 2:3]
    )
    inside_cols = (col_ids[None, :] >= my_boxes[:, 1:2]) & (
        col_ids[None, :] < my_boxes[:, 1:2] + my_boxes[:, 3:4]
    )
    valid_mask = (inside_rows[:, :, None] & inside_cols[:, None, :]).astype(jnp.float32)
    mask_column_vector = valid_mask.reshape(pixels, 1)
    mask_flat = valid_mask.reshape(pixels)
    pixel_number_count = jnp.sum((crop_boxes[:, 2] * crop_boxes[:, 3]).astype(jnp.float32))
    image_areas = (my_boxes[:, 2] * my_boxes[:, 3]).astype(jnp.float32)
    input_full = widen(trunk_input)
    reduced_output = forward_dot(input_full, conv_reduce).reshape(pixels, -1)
    normalized_first, standardized_first, inverse_deviation_first = norm_ahead_pass(
        reduced_output, mask_column_vector, pixel_number_count, reduction_norm_params
    )
    hidden_one = (
        jax.nn.silu(normalized_first)
        .astype(jnp.bfloat16)
        .reshape(image_inputs, tile_row_count, frame_columns, -1)
    )
    hidden_full = widen(pad_rows(hidden_one))
    dilated_out = 0.0
    for row_tap in range(3):
        band = hidden_full[:, 4 * row_tap : 4 * row_tap + tile_row_count]
        for col_tap in range(3):
            dilated_out = dilated_out + forward_dot(
                move(band, -(col_tap - 1) * 4, 2), conv_dilated[row_tap, col_tap]
            )
    normalized_second, standardized_second, inverse_deviation_second = norm_ahead_pass(
        dilated_out.reshape(pixels, -1), mask_column_vector, pixel_number_count, dilated_norm_params
    )
    hidden_two = (
        jax.nn.silu(normalized_second)
        .astype(jnp.bfloat16)
        .reshape(image_inputs, tile_row_count, frame_columns, -1)
    )
    hidden_two_full = widen(hidden_two)
    expanded_output = forward_dot(hidden_two_full, conv_expand).reshape(pixels, -1)
    normalized_third, standardized_third, inverse_deviation_third = norm_ahead_pass(
        expanded_output, mask_column_vector, pixel_number_count, expansion_norm_params
    )
    residual_sum = normalized_third + trunk_input.reshape(pixels, -1).astype(jnp.float32)
    trunk_out = (
        jax.nn.silu(residual_sum)
        .astype(jnp.bfloat16)
        .reshape(image_inputs, tile_row_count, frame_columns, quarter)
    )
    trunk_full = widen(trunk_out)
    branch_outs = [backward_dot(trunk_full, aspp_point)]
    for branch_id in range(3):
        dilation = RATES[branch_id]
        hops = dilation // tile_row_count
        partials = [0.0, 0.0, 0.0]
        for col_tap in range(3):
            shifted = move(trunk_full, -(col_tap - 1) * dilation, 2)
            products = backward_dot(shifted, stacked_taps(aspp_rates[branch_id], col_tap))
            for row_tap in range(3):
                partials[row_tap] = (
                    partials[row_tap]
                    + products[..., row_tap * branch_part : (row_tap + 1) * branch_part]
                )
        upper = send_down(partials[0].astype(jnp.bfloat16), hops).astype(jnp.float32)
        lower_part = send_up(partials[2].astype(jnp.bfloat16), hops).astype(jnp.float32)
        branch_outs.append(partials[1] + upper + lower_part)
    spatial_flattened = jnp.stack(branch_outs, axis=3).reshape(pixels, -1)
    branch_gain_bias = branch_norms.reshape(2, -1)
    normalized_spatial, standardized_spatial, inverse_deviation_spatial = norm_ahead_pass(
        spatial_flattened, mask_column_vector, pixel_number_count, branch_gain_bias
    )
    spatial_act = (
        jax.nn.silu(normalized_spatial)
        .astype(jnp.bfloat16)
        .reshape(image_inputs, tile_row_count, frame_columns, 4, branch_part)
    )
    pooled_local = lax.dot_general(
        valid_mask.astype(jnp.bfloat16),
        trunk_full,
        (((1, 2), (1, 2)), ((0,), (0,))),
        preferred_element_type=jnp.float32,
    )
    pooled = (over_rows(pooled_local) / image_areas[:, None]).astype(jnp.bfloat16)
    pooling_convolution = backward_dot(pooled, aspp_pool)
    normalized_poolbranch, standardized_poolbranch, inverse_deviation_poolbranch = norm_ahead_pass(
        pooling_convolution, row_portion, image_overall_count, pooling_norm_params
    )
    pool_act = jax.nn.silu(normalized_poolbranch).astype(jnp.bfloat16)
    pool_wide = jnp.broadcast_to(
        pool_act[:, None, None, None, :],
        (image_inputs, tile_row_count, frame_columns, 1, branch_part),
    )
    concat = jnp.concatenate([spatial_act, pool_wide], axis=3)
    concat_flat = widen(concat).reshape(pixels, -1)
    proj_kernel = (
        aspp_project.reshape(branch_part, 5, branch_total, branch_part)
        .transpose(0, 2, 1, 3)
        .reshape(branch_part, 5 * branch_total * branch_part)
    )
    projected_output = backward_dot(concat_flat, proj_kernel)
    normalized_projector, standardized_projector, inverse_deviation_projector = norm_ahead_pass(
        projected_output, mask_column_vector, pixel_number_count, projection_norm_params
    )
    features = (
        jax.nn.silu(normalized_projector)
        .astype(jnp.bfloat16)
        .reshape(image_inputs, tile_row_count, frame_columns, -1)
    )
    features_wide = widen(features).reshape(pixels, -1).astype(jnp.float32)
    head_wide = head_weight.astype(jnp.float32)
    logits = jnp.dot(features_wide, head_wide, precision=HIGH) + head_bias
    classes = head_bias.shape[0] - 3
    seg_logits = logits[:, :classes]
    labels_flat = seg_labels.reshape(pixels)
    classes_hot = (labels_flat[:, None] == jnp.arange(classes, dtype=jnp.int32)[None, :]).astype(
        jnp.float32
    )
    cross = jax.nn.logsumexp(seg_logits, axis=1) - jnp.sum(seg_logits * classes_hot, axis=1)
    depth_gap = logits[:, classes] - depth_target.reshape(pixels)
    smooth_abs = jnp.sqrt(depth_gap * depth_gap + 1.0)
    normal_gap = logits[:, classes + 1 :] - jnp.moveaxis(normal_target, 1, 3).reshape(pixels, 2)
    local_losses = jnp.stack(
        [
            jnp.sum(mask_flat * cross),
            jnp.sum(mask_flat * (smooth_abs - 1.0)),
            jnp.sum(mask_flat * jnp.sum(normal_gap * normal_gap, axis=1)),
        ]
    )
    task_weights = jnp.exp(-log_vars)
    grad_seg = (jax.nn.softmax(seg_logits, axis=1) - classes_hot) * (
        task_weights[0] / pixel_number_count * mask_flat
    )[:, None]
    grad_depth = depth_gap / smooth_abs * (task_weights[1] / pixel_number_count * mask_flat)
    grad_normal = 2.0 * normal_gap * (task_weights[2] / pixel_number_count * mask_flat)[:, None]
    grad_logits = jnp.concatenate([grad_seg, grad_depth[:, None], grad_normal], axis=1)
    head_local = lax.dot_general(
        features_wide, grad_logits, (((0,), (0,)), ((), ())), precision=HIGH
    )
    loss_parts, grad_head_weight, grad_head_bias = lax.psum(
        (local_losses, head_local, jnp.sum(grad_logits, axis=0)), ("rows", "batch")
    )
    task_losses = loss_parts / pixel_number_count
    total_loss = jnp.sum(task_weights * task_losses + log_vars)
    grad_log_vars = 1.0 - task_weights * task_losses
    grad_features = jnp.dot(grad_logits, head_wide.T, precision=HIGH)
    my_features_grad = lax.dynamic_slice_in_dim(
        grad_features, lax.axis_index("branch") * branch_part, branch_part, 1
    )
    gradient_before_projector = my_features_grad * silu_slope(normalized_projector)
    grad_proj_in, grad_project_norm = norm_reverse_pass(
        gradient_before_projector,
        standardized_projector,
        inverse_deviation_projector,
        1.0,
        mask_column_vector,
        pixel_number_count,
        projection_norm_params,
    )
    grad_proj_low = grad_proj_in.astype(jnp.bfloat16)
    proj_kernel_grad = lax.dot_general(
        grad_proj_low, concat_flat, (((0,), (0,)), ((), ())), preferred_element_type=jnp.float32
    )
    grad_project_local = (
        proj_kernel_grad.reshape(branch_part, branch_total, 5, branch_part)
        .transpose(0, 2, 1, 3)
        .reshape(branch_part, 5, branch_total * branch_part)
    )
    concat_grad = forward_dot(grad_proj_low, proj_kernel).reshape(
        image_inputs, tile_row_count, frame_columns, -1
    )
    concat_grad = narrow(concat_grad).reshape(pixels, 5, branch_part)
    pool_grad_img = over_rows(
        jnp.sum(concat_grad[:, 4, :].reshape(image_inputs, -1, branch_part), axis=1)
    )
    gradient_before_poolbranch = pool_grad_img * silu_slope(normalized_poolbranch)
    grad_pool_conv, grad_pool_norm = norm_reverse_pass(
        gradient_before_poolbranch,
        standardized_poolbranch,
        inverse_deviation_poolbranch,
        row_portion,
        1.0,
        image_overall_count,
        pooling_norm_params,
    )
    pool_conv_low = grad_pool_conv.astype(jnp.bfloat16)
    grad_pool_local = (
        lax.dot_general(
            pool_conv_low, pooled, (((0,), (0,)), ((), ())), preferred_element_type=jnp.float32
        )
        * row_portion
    )
    pooled_grad = forward_dot(pool_conv_low, aspp_pool)
    gradient_before_spatialbranch = concat_grad[:, :4, :].reshape(pixels, -1) * silu_slope(
        normalized_spatial
    )
    grad_spatial, branch_norm_grad = norm_reverse_pass(
        gradient_before_spatialbranch,
        standardized_spatial,
        inverse_deviation_spatial,
        1.0,
        mask_column_vector,
        pixel_number_count,
        branch_gain_bias,
    )
    grad_branch_norms = branch_norm_grad.reshape(2, 4, branch_part)
    spatial_low = grad_spatial.astype(jnp.bfloat16).reshape(
        image_inputs, tile_row_count, frame_columns, 4, branch_part
    )
    point_grad = spatial_low[:, :, :, 0]
    grad_point_local = pixel_dot(point_grad, trunk_full)
    trunk_grad = forward_dot(point_grad, aspp_point)
    trunk_grad = (
        trunk_grad + valid_mask[..., None] * (pooled_grad / image_areas[:, None])[:, None, None, :]
    )
    rate_grads = []
    for branch_id in range(3):
        dilation = RATES[branch_id]
        hops = dilation // tile_row_count
        centre = spatial_low[:, :, :, branch_id + 1]
        grad_taps = jnp.concatenate(
            [send_up(centre, hops), centre, send_down(centre, hops)], axis=3
        )
        per_col = []
        for col_tap in range(3):
            shifted = move(trunk_full, -(col_tap - 1) * dilation, 2)
            per_col.append(pixel_dot(grad_taps, shifted))
            tap_grad = forward_dot(grad_taps, stacked_taps(aspp_rates[branch_id], col_tap))
            trunk_grad = trunk_grad + move(tap_grad, (col_tap - 1) * dilation, 2)
        col_stack = jnp.stack(per_col, axis=0).reshape(3, 3, branch_part, -1)
        rate_grads.append(col_stack.transpose(1, 0, 2, 3))
    grad_rates_local = jnp.stack(rate_grads, axis=0)
    trunk_own = narrow(trunk_grad).reshape(pixels, -1)
    gradient_shortcut = trunk_own * silu_slope(residual_sum)
    grad_expanded, grad_norm_expand = norm_reverse_pass(
        gradient_shortcut,
        standardized_third,
        inverse_deviation_third,
        1.0,
        mask_column_vector,
        pixel_number_count,
        expansion_norm_params,
    )
    expanded_low = grad_expanded.astype(jnp.bfloat16).reshape(
        image_inputs, tile_row_count, frame_columns, -1
    )
    grad_expand_local = pixel_dot(hidden_two_full, expanded_low)
    hidden_two_grad = narrow(backward_dot(expanded_low, conv_expand)).reshape(pixels, -1)
    gradient_before_second = hidden_two_grad * silu_slope(normalized_second)
    gradient_dilated_input, gradient_dilated_norm = norm_reverse_pass(
        gradient_before_second,
        standardized_second,
        inverse_deviation_second,
        1.0,
        mask_column_vector,
        pixel_number_count,
        dilated_norm_params,
    )
    dilated_lowprec = gradient_dilated_input.astype(jnp.bfloat16).reshape(
        image_inputs, tile_row_count, frame_columns, -1
    )
    dilated_padded = pad_rows(dilated_lowprec)
    hidden_one_grad = 0.0
    kernel_grads = []
    for row_tap in range(3):
        band = hidden_full[:, 4 * row_tap : 4 * row_tap + tile_row_count]
        grad_band = dilated_padded[:, 8 - 4 * row_tap : 8 - 4 * row_tap + tile_row_count]
        for col_tap in range(3):
            kernel_grads.append(pixel_dot(move(band, -(col_tap - 1) * 4, 2), dilated_lowprec))
            hidden_one_grad = hidden_one_grad + backward_dot(
                move(grad_band, (col_tap - 1) * 4, 2), conv_dilated[row_tap, col_tap]
            )
    grad_dilated_local = jnp.stack(kernel_grads, axis=0).reshape(3, 3, hidden_full.shape[3], -1)
    hidden_one_own = narrow(hidden_one_grad).reshape(pixels, -1)
    gradient_before_first = hidden_one_own * silu_slope(normalized_first)
    grad_reduced, grad_norm_reduce = norm_reverse_pass(
        gradient_before_first,
        standardized_first,
        inverse_deviation_first,
        1.0,
        mask_column_vector,
        pixel_number_count,
        reduction_norm_params,
    )
    reduced_low = grad_reduced.astype(jnp.bfloat16).reshape(
        image_inputs, tile_row_count, frame_columns, -1
    )
    grad_reduce_local = pixel_dot(input_full, reduced_low)
    input_grad = narrow(backward_dot(reduced_low, conv_reduce))
    grad_input = input_grad + gradient_shortcut.reshape(
        image_inputs, tile_row_count, frame_columns, quarter
    )
    grad_reduce, grad_dilated, grad_expand, grad_point, grad_rates, grad_pool, grad_project = (
        lax.psum_scatter(grad_reduce_local, ("rows", "batch"), scatter_dimension=0, tiled=True),
        lax.psum_scatter(grad_dilated_local, ("rows", "batch"), scatter_dimension=2, tiled=True),
        lax.psum_scatter(grad_expand_local, ("rows", "batch"), scatter_dimension=0, tiled=True),
        lax.psum_scatter(grad_point_local, ("rows", "batch"), scatter_dimension=1, tiled=True),
        lax.psum_scatter(grad_rates_local, ("rows", "batch"), scatter_dimension=4, tiled=True),
        lax.psum_scatter(grad_pool_local, ("rows", "batch"), scatter_dimension=1, tiled=True),
        lax.psum_scatter(grad_project_local, ("rows", "batch"), scatter_dimension=2, tiled=True),
    )
    return (
        features,
        total_loss,
        grad_input,
        grad_reduce,
        grad_dilated,
        grad_expand,
        grad_norm_reduce,
        gradient_dilated_norm,
        grad_norm_expand,
        grad_point,
        grad_rates,
        grad_pool,
        grad_branch_norms,
        grad_pool_norm,
        grad_project,
        grad_project_norm,
        grad_head_weight,
        grad_head_bias,
        grad_log_vars,
    )


def solution(mesh):
    in_specs = (
        P("batch", "rows", None, "branch"),
        P(None, "branch"),
        P(None, None, None, "branch"),
        P(None, "branch"),
        P(None, "branch"),
        P(None, "branch"),
        P(None, "branch"),
        P("branch", None),
        P(None, None, None, "branch", None),
        P("branch", None),
        P(None, None, "branch"),
        P(None, "branch"),
        P("branch", None, None),
        P(None, "branch"),
        P(),
        P(),
        P(),
        P(),
        P("batch", "rows", None),
        P("batch", "rows", None),
        P("batch", None, "rows", None),
    )
    out_specs = (
        P("batch", "rows", None, "branch"),
        P(),
        P("batch", "rows", None, "branch"),
        P(("rows", "batch"), "branch"),
        P(None, None, ("rows", "batch"), "branch"),
        P(("rows", "batch"), "branch"),
        P(None, "branch"),
        P(None, "branch"),
        P(None, "branch"),
        P("branch", ("rows", "batch")),
        P(None, None, None, "branch", ("rows", "batch")),
        P("branch", ("rows", "batch")),
        P(None, None, "branch"),
        P(None, "branch"),
        P("branch", None, ("rows", "batch")),
        P(None, "branch"),
        P(),
        P(),
        P(),
    )
    small = (mesh.shape["branch"], mesh.shape["rows"], mesh.shape["batch"]) == (4, 2, 4)
    body = fast_local if small else local
    return jax.shard_map(body, mesh=mesh, in_specs=in_specs, out_specs=out_specs, check_vma=False)
```

```python
import types

import jax
import jax.numpy as jnp
from jax import lax
from jax.experimental import pallas as pl
from jax.experimental.pallas import tpu as pltpu
from jax.sharding import PartitionSpec as P

EPS = 1e-05
HIGH = lax.Precision.HIGHEST
RATES = (12, 24, 36)


def padded(cells, sides, width):
    for axis, dim in sides:
        count = lax.axis_size(axis)
        ends = count - 1
        head = lax.slice_in_dim(cells, 0, width, axis=dim)
        tail = lax.slice_in_dim(cells, cells.shape[dim] - width, cells.shape[dim], axis=dim)
        cells = jnp.concatenate(
            [
                lax.ppermute(tail, axis, [(i, (i + 1) % count) for i in range(ends)]),
                cells,
                lax.ppermute(head, axis, [((i + 1) % count, i) for i in range(ends)]),
            ],
            axis=dim,
        )
    return cells


def shifted_2(block, axis, distance):
    devices = range(lax.axis_size(axis))
    route = [(i - distance, i) for i in devices if i - distance in devices]
    return lax.ppermute(block, axis, route)


def move(tensor, offset, axis_id):
    length = tensor.shape[axis_id]
    if offset == 0:
        return tensor
    widths = [(0, 0)] * tensor.ndim
    if offset > 0:
        widths[axis_id] = (offset, 0)
        return lax.slice_in_dim(jnp.pad(tensor, widths), 0, length, axis=axis_id)
    widths[axis_id] = (0, -offset)
    return lax.slice_in_dim(jnp.pad(tensor, widths), -offset, length - offset, axis=axis_id)


def forward_dot(lhs_arr, rhs_arr):
    return jnp.dot(lhs_arr, rhs_arr, preferred_element_type=jnp.float32)


def backward_dot(grad_arr, kernel):
    return lax.dot_general(
        grad_arr,
        kernel,
        (((grad_arr.ndim - 1,), (1,)), ((), ())),
        preferred_element_type=jnp.float32,
    )


def pixel_dot(source, grad_arr):
    return lax.dot_general(
        source, grad_arr, (((0, 1, 2), (0, 1, 2)), ((), ())), preferred_element_type=jnp.float32
    )


def silu_slope(pre_act):
    sigmoid_v = jax.nn.sigmoid(pre_act)
    return sigmoid_v * (1.0 + pre_act * (1.0 - sigmoid_v))


def widen(tensor):
    return lax.all_gather(tensor, "branch", axis=3, tiled=True)


def narrow(tensor):
    return lax.psum_scatter(
        tensor.astype(jnp.bfloat16), "branch", scatter_dimension=3, tiled=True
    ).astype(jnp.float32)


def pad_rows(tensor):
    return padded(tensor, (("rows", 1),), 4)


def send_down(tensor, hops):
    if hops >= lax.axis_size("rows"):
        return jnp.zeros_like(tensor)
    return shifted_2(tensor, "rows", hops)


def send_up(tensor, hops):
    if hops >= lax.axis_size("rows"):
        return jnp.zeros_like(tensor)
    return shifted_2(tensor, "rows", -hops)


def over_rows(tensor):
    return lax.psum(tensor, "rows")


def norm_ahead_pass(tensor, weight, counted, affine):
    summed = lax.psum(jnp.sum(tensor * weight, axis=0), ("rows", "batch"))
    mean_val = summed / counted
    centered = tensor - mean_val
    spread = lax.psum(jnp.sum(weight * centered * centered, axis=0), ("rows", "batch"))
    variance = spread / counted
    inverse = lax.rsqrt(variance + EPS)
    normed = centered * inverse
    return (affine[0] * normed + affine[1], normed, inverse)


def norm_reverse_pass(grad_out, normed, inverse, weight_all, weight_stat, counted, affine):
    grad_bias, grad_gain = lax.psum(
        (jnp.sum(grad_out * weight_all, axis=0), jnp.sum(grad_out * normed * weight_all, axis=0)),
        ("rows", "batch"),
    )
    gain_row = affine[0]
    grad_in = inverse * (
        gain_row * grad_out - weight_stat / counted * gain_row * (grad_bias + normed * grad_gain)
    )
    return (grad_in, jnp.stack([grad_gain, grad_bias]))


def stacked_taps(kernels, col_tap):
    return jnp.concatenate([kernels[0, col_tap], kernels[1, col_tap], kernels[2, col_tap]], axis=0)


MESH = pl.DeviceIdType.MESH
F32 = jnp.float32
BF16 = jnp.bfloat16
VMEM_LIMIT = 60 * 2**20


class Net:
    def __init__(self, send_sems, recv_sems):
        self.m = lax.axis_index("branch")
        self.r = lax.axis_index("rows")
        self.z = lax.axis_index("batch")
        self.send_sems, self.recv_sems, self.count = send_sems, recv_sems, 0
        self.side = (self.m ^ 1, self.r, self.z)
        self.over = (self.m ^ 2, self.r, self.z)
        self.diagonal = (self.m ^ 3, self.r, self.z)
        self.core = (self.m, 1 - self.r, self.z)
        self.slot = self.r * 4 + self.z
        self.group = [
            (self.m, lax.rem(self.r + i, 2), lax.rem(self.z + j, 4))
            for i in range(2)
            for j in range(4)
            if i or j
        ]

    def send(self, src, dst, device):
        i = self.count
        self.count += 1
        copy = pltpu.make_async_remote_copy(
            src_ref=src,
            dst_ref=dst,
            send_sem=self.send_sems.at[i],
            recv_sem=self.recv_sems.at[i],
            device_id=device,
            device_id_type=MESH,
        )
        copy.start()
        return copy


def greet(peers, perhaps=()):
    barrier = pltpu.get_barrier_semaphore()
    for peer in peers:
        pl.semaphore_signal(barrier, inc=1, device_id=peer, device_id_type=MESH)
    awaited = len(peers)
    for peer, there in perhaps:

        @pl.when(there)
        def _(peer=peer):
            pl.semaphore_signal(barrier, inc=1, device_id=peer, device_id_type=MESH)

        awaited = awaited + there.astype(jnp.int32)
    pl.semaphore_wait(barrier, awaited)


def each_rows(total, step, body):
    def run(i, carry):
        body(pl.ds(pl.multiple_of(i * step, step), step))
        return carry

    lax.fori_loop(0, total // step, run, 0)


def lane_block(index, width=128):
    return pl.ds(pl.multiple_of(index * width, width), width)


def wide(tile, width):
    count = width // tile.shape[1]
    return tile if count == 1 else jnp.concatenate([tile] * count, axis=1)


def column_sums(fn, total, width, number):
    step = 16384 // width

    def run(i, sums):
        terms = fn(pl.ds(pl.multiple_of(i * step, step), step))
        return tuple(
            s + jnp.sum(t.reshape(step // 8, 8, width), axis=0) for s, t in zip(sums, terms)
        )

    sums = lax.fori_loop(
        0, total // step, run, tuple(jnp.zeros((8, width), F32) for _ in range(number))
    )
    return [jnp.sum(s, axis=0, keepdims=True) for s in sums]


def fold(row):
    return row + pltpu.roll(wide(row, 128), 64, 1)


def exchange(net, outgoing, incoming, meanwhile=None):
    copies = [net.send(outgoing, incoming.at[net.slot], peer) for peer in net.group]
    incoming[net.slot] = outgoing[...]
    if meanwhile is not None:
        meanwhile()
    for copy in copies:
        copy.wait()


def pack(outgoing, first, second, extra=None):
    for i in range(first.shape[1] // 128):
        outgoing[2 * i : 2 * i + 1, :] = first[:, i * 128 : i * 128 + 128]
        outgoing[2 * i + 1 : 2 * i + 2, :] = second[:, i * 128 : i * 128 + 128]
    if extra is not None:
        outgoing[4:5, :] = extra


def unpack(incoming, width):
    count = width // 128
    firsts = [incoming[:, 2 * i, :] for i in range(count)]
    seconds = [incoming[:, 2 * i + 1, :] for i in range(count)]
    return jnp.concatenate(firsts, axis=1), jnp.concatenate(seconds, axis=1)


def statistics(
    net, value_ref, mask_ref, counts, outgoing, incoming, counted, folded=False, extra=None
):
    total, width = value_ref.shape
    same = fold if folded else (lambda row: row)
    (first,) = column_sums(
        lambda at: (value_ref[at, :] * wide(mask_ref[at, :], width),), total, width, 1
    )
    first = same(first)
    own = jnp.sum(jnp.where(lax.broadcasted_iota(jnp.int32, (8, 128), 0) == net.slot, counts, 0.0), axis=0, keepdims=True)
    centre = first / jnp.maximum(wide(own, width), 1.0)

    def squares(at):
        gap = value_ref[at, :] - centre
        return (gap * gap * wide(mask_ref[at, :], width),)

    second = same(column_sums(squares, total, width, 1)[0])
    pack(outgoing, first, second, extra)
    exchange(net, outgoing, incoming)
    firsts, seconds = unpack(incoming, width)
    numbers = wide(counts, width)
    mean = jnp.sum(firsts, axis=0, keepdims=True) / counted
    drift = firsts / jnp.maximum(numbers, 1.0) - mean
    variance = jnp.sum(seconds + numbers * drift * drift, axis=0, keepdims=True) / counted
    return mean, lax.rsqrt(variance + EPS)


def gather_blocks(net, part, rows, meanwhile=None):
    pieces, size = 4, rows // 4
    own, side, over = net.m, net.m ^ 1, net.m ^ 2

    def at(i):
        return pl.ds(i * size, size)

    to_side, to_over = [], []
    for i in range(pieces):
        j = pieces - 1 - i
        to_side.append(net.send(part(own, at(i)), part(own, at(i)), net.side))
        to_over.append(net.send(part(own, at(j)), part(own, at(j)), net.over))
    passed = []
    for i in range(pieces):
        j = pieces - 1 - i
        to_side[i].wait_recv()
        if i < pieces // 2:
            passed.append(net.send(part(side, at(i)), part(side, at(i)), net.over))
        to_over[i].wait_recv()
        if i < pieces // 2:
            passed.append(net.send(part(over, at(j)), part(over, at(j)), net.side))
    if meanwhile is not None:
        meanwhile()
    for copy in to_side + to_over:
        copy.wait_send()
    for copy in passed:
        copy.wait()


def sum_scatter(net, part, bufs, out, meanwhile=None, produce=None):
    far, to_side, to_over, far_side, far_over, from_side, from_over = bufs
    rows, width = out.shape
    half, step = rows // 2, 16384 // width
    head, tail = pl.ds(0, half), pl.ds(half, half)
    across, side, over = net.m ^ 3, net.m ^ 1, net.m ^ 2

    def fill(target, index, base):
        def body(at):
            rows_at = pl.ds(pl.multiple_of(at.start + base, step), step)
            target[rows_at, :] = part[index, rows_at, :].astype(BF16)

        each_rows(half, step, body)

    def combine(target, index, base, arrived):
        def body(at):
            rows_at = pl.ds(pl.multiple_of(at.start + base, step), step)
            target[rows_at, :] = (part[index, rows_at, :] + arrived[at, :].astype(F32)).astype(BF16)

        each_rows(half, step, body)

    if produce is not None:
        produce(0)
    fill(far, across, 0)
    first = net.send(far.at[head], far_side, net.side)
    if produce is not None:
        produce(1)
    fill(far, across, half)
    second = net.send(far.at[tail], far_over, net.over)
    fill(to_side, side, 0)
    third = net.send(to_side.at[head], from_side.at[head], net.side)
    fill(to_over, over, half)
    fourth = net.send(to_over.at[tail], from_over.at[tail], net.over)
    second.wait_recv()
    combine(to_side, side, half, far_over)
    fifth = net.send(to_side.at[tail], from_side.at[tail], net.side)
    first.wait_recv()
    combine(to_over, over, 0, far_side)
    sixth = net.send(to_over.at[head], from_over.at[head], net.over)
    if meanwhile is not None:
        meanwhile()
    for copy in (third, fourth, fifth, sixth):
        copy.wait_recv()

    def body(at):
        out[at, :] = (
            part[net.m, at, :] + from_side[at, :].astype(F32) + from_over[at, :].astype(F32)
        )

    each_rows(rows, step, body)
    for copy in (first, second, third, fourth, fifth, sixth):
        copy.wait_send()


def gradient_sums(
    net, grad_ref, normed, outgoing, incoming, folded=False, extra=None, meanwhile=None
):
    total, width = grad_ref.shape
    same = fold if folded else (lambda row: row)
    bias, gain = column_sums(
        lambda at: (grad_ref[at, :], grad_ref[at, :] * normed(at)), total, width, 2
    )
    pack(outgoing, same(bias), same(gain), extra)
    exchange(net, outgoing, incoming, meanwhile)
    biases, gains = unpack(incoming, width)
    return jnp.sum(biases, axis=0, keepdims=True), jnp.sum(gains, axis=0, keepdims=True)


def keep_rows(ref, first, second):
    width = ref.shape[1]
    ref[0:1, :] = first
    ref[1:2, :] = second
    ref[2:8, :] = jnp.zeros((6, width), F32)


def pair(a, b):
    low = lax.broadcasted_iota(jnp.int32, (a.shape[0], 128), 1) < 64
    results = []
    for g in range(2):
        left, right = a[:, g * 128 : g * 128 + 128], b[:, g * 128 : g * 128 + 128]
        results.append(jnp.where(low, left, pltpu.roll(right, 64, 1)))
        results.append(jnp.where(low, pltpu.roll(left, 64, 1), right))
    return results


def unpair(blocks):
    low = lax.broadcasted_iota(jnp.int32, blocks[0].shape, 1) < 64
    firsts, seconds = [], []
    for g in range(2):
        left, right = blocks[2 * g], blocks[2 * g + 1]
        firsts.append(jnp.where(low, left, pltpu.roll(right, 64, 1)))
        seconds.append(jnp.where(low, pltpu.roll(left, 64, 1), right))
    return jnp.concatenate(firsts, axis=1), jnp.concatenate(seconds, axis=1)


def split_three(row):
    high = row.astype(BF16)
    rest = row - high.astype(F32)
    middle = rest.astype(BF16)
    low = (rest - middle.astype(F32)).astype(BF16)
    return high, middle, low


def zero_margins(ref, side, width):
    rows, _, lanes = ref.shape
    ref[:, 0:side, :] = jnp.zeros((rows, side, lanes), F32)
    ref[:, side + width : 2 * side + width, :] = jnp.zeros((rows, side, lanes), F32)


def scatter_buffers(rows, width):
    whole, half = pltpu.VMEM((rows, width), BF16), pltpu.VMEM((rows // 2, width), BF16)
    return [whole, whole, whole, half, half, whole, whole]


def sigmoid(u):
    return 0.5 * jnp.tanh(0.5 * u) + 0.5


def slope(u):
    s = sigmoid(u)
    return s * (1.0 + u * (1.0 - s))


def mm(a, b):
    return jnp.dot(a, b, preferred_element_type=F32)


def mm_t(a, b):
    return lax.dot_general(a, b, (((1,), (1,)), ((), ())), preferred_element_type=F32)


def tm_m(a, b):
    return lax.dot_general(a, b, (((0,), (0,)), ((), ())), preferred_element_type=F32)


class Streams:
    def __init__(self, ins, outs, sems):
        self.ins = {n: pltpu.make_async_copy(*pair, sems.at[i]) for i, (n, pair) in enumerate(ins)}
        self.outs = {
            n: pltpu.make_async_copy(*pair, sems.at[len(ins) + i])
            for i, (n, pair) in enumerate(outs)
        }
        self.left = []
        for copy in self.ins.values():
            copy.start()

    def need(self, *names):
        for name in names:
            self.ins.pop(name).wait()

    def done(self, *names):
        for name in names:
            copy = self.outs.pop(name)
            copy.start()
            self.left.append(copy)

    def finish(self):
        self.need(*list(self.ins))
        self.done(*list(self.outs))
        for copy in self.left:
            copy.wait()


def call_kernel(
    body, name, number, args, outs, scratch, sems, hbm=(), smem=("boxes",), stream=()
):
    vmem, anywhere = pl.BlockSpec(memory_space=pltpu.VMEM), pl.BlockSpec(memory_space=pl.ANY)
    stream_in = [n for n in args if n in stream]
    stream_out = [n for n in outs if n in stream]
    buffers = {n: pltpu.VMEM(args[n].shape, args[n].dtype) for n in stream_in}
    buffers.update({n: pltpu.VMEM(*outs[n]) for n in stream_out})
    names = [f"far_{n}" if n in stream else n for n in [*args, *outs]]
    names = [*names, *scratch, *buffers, "stream_sems"]
    places = {name: anywhere for name in [*hbm, *stream]}
    places.update({name: pl.BlockSpec(memory_space=pltpu.SMEM) for name in smem})

    def kernel(*refs):
        k = types.SimpleNamespace(**dict(zip(names, refs)))
        held = vars(k)
        k.stream = Streams(
            [(n, (held[f"far_{n}"], held[n])) for n in stream_in],
            [(n, (held[n], held[f"far_{n}"])) for n in stream_out],
            k.stream_sems,
        )
        body(Net(refs[-2], refs[-1]) if sems else None, k)
        k.stream.finish()

    results = pl.pallas_call(
        kernel,
        out_shape=[jax.ShapeDtypeStruct(s, d) for s, d in outs.values()],
        in_specs=[places.get(name, vmem) for name in args],
        out_specs=[places.get(name, vmem) for name in outs],
        scratch_shapes=[
            *scratch.values(),
            *buffers.values(),
            pltpu.SemaphoreType.DMA((max(len(buffers), 1),)),
            *([pltpu.SemaphoreType.DMA((sems,))] * (2 if sems else 0)),
        ],
        name=name,
        compiler_params=pltpu.CompilerParams(
            collective_id=number, has_side_effects=bool(sems), vmem_limit_bytes=VMEM_LIMIT
        ),
    )(*args.values())
    return types.SimpleNamespace(**dict(zip(outs, results)))


def pixel_count(boxes):
    total = boxes[0, 2] * boxes[0, 3]
    for b in range(1, 4):
        total = total + boxes[b, 2] * boxes[b, 3]
    return total.astype(F32)


def tile_counts(net, boxes):
    slot = lax.broadcasted_iota(jnp.int32, (8, 128), 0)
    result = jnp.zeros((8, 128), F32)
    for s in range(8):
        top, height, width = boxes[s % 4, 0], boxes[s % 4, 2], boxes[s % 4, 3]
        first, last = (s // 4) * 12, (s // 4) * 12 + 12
        rows = jnp.minimum(top + height, last) - jnp.maximum(top, first)
        result = jnp.where(slot == s, (jnp.maximum(rows, 0) * width).astype(F32), result)
    return result


def exchange_scratch(label):
    return {
        f"out_{label}": pltpu.VMEM((8, 128), F32),
        f"in_{label}": pltpu.VMEM((8, 8, 128), F32),
    }


def scatter_scratch(label, rows, width):
    return {f"{label}_{i}": b for i, b in enumerate(scatter_buffers(rows, width))}


def scatter_refs(k, label):
    return [getattr(k, f"{label}_{i}") for i in range(7)]


def load_taps(k):
    loads = []
    for i in range(3):
        for j in range(3):
            loads.append(
                pltpu.make_async_copy(
                    k.w_dilated.at[i, j],
                    k.w_taps.at[i, :, pl.ds(j * 128, 128)],
                    k.local_sems.at[i * 3 + j],
                )
            )
            loads[-1].start()
    return loads


def send_halo(net, padded):
    lanes = padded.shape[1]
    padded[pl.ds(pl.multiple_of(net.r * 2048, 128), 512), :] = jnp.zeros((512, lanes), BF16)
    return net.send(
        padded.at[pl.ds(pl.multiple_of(1536 - net.r * 1024, 128), 512)],
        padded.at[pl.ds(pl.multiple_of(net.r * 2048, 128), 512)],
        net.core,
    )


def bottleneck_forward(net, k):
    counted, counts = pixel_count(k.boxes), tile_counts(net, k.boxes)
    loads = load_taps(k)
    own_reduce = pltpu.make_async_copy(
        k.conv_reduce.at[lane_block(net.m, 512)], k.w_reduce.at[net.m], k.local_sems.at[9]
    )
    own_reduce.start()
    greet([net.side, net.over, net.diagonal] + net.group)
    branches = [(net.m ^ 3, net.diagonal), (net.m ^ 1, net.side), (net.m ^ 2, net.over)]
    arrivals = [
        net.send(k.conv_reduce.at[lane_block(b, 512)], k.w_reduce.at[net.m], peer)
        for b, peer in branches
    ]

    top, left_edge = k.boxes[net.z, 0], k.boxes[net.z, 1]
    bottom, right_edge = top + k.boxes[net.z, 2], left_edge + k.boxes[net.z, 3]
    column = lax.broadcasted_iota(jnp.int32, (128, 128), 0)
    column_inside = jnp.where((column >= left_edge) & (column < right_edge), 1.0, 0.0)

    def mask_rows(i, carry):
        row = jnp.full((128, 128), net.r * 12 + i, jnp.int32)
        inside = jnp.where((row >= top) & (row < bottom), column_inside, 0.0)
        k.mask[pl.ds(pl.multiple_of(i * 128, 128), 128), :] = inside
        return carry

    lax.fori_loop(0, 12, mask_rows, 0)
    k.stream.done("mask")
    k.stream.need("x")

    def reduce_for(b):
        def reduce_rows(at):
            k.part[b, at, :] = mm(k.x[at, :], k.w_reduce[b])

        each_rows(1536, 384, reduce_rows)

    own_reduce.wait()
    reduce_for(net.m)
    arrivals[1].wait()
    reduce_for(net.m ^ 1)
    arrivals[2].wait()
    reduce_for(net.m ^ 2)
    arrivals[0].wait()
    k.stream.done("w_reduce")

    def far_half(half):
        def reduce_rows(at):
            at = pl.ds(pl.multiple_of(at.start + half * 768, 128), 384)
            k.part[net.m ^ 3, at, :] = mm(k.x[at, :], k.w_reduce[net.m ^ 3])

        each_rows(768, 384, reduce_rows)

    sum_scatter(net, k.part, scatter_refs(k, "sum"), k.reduced, produce=far_half)
    k.stream.done("reduced")

    half = pl.ds(pl.multiple_of(net.r * 32, 32), 32)
    late = []

    def weight_block(kind, b):
        lanes = lane_block(b, 512)
        if kind == "edge":
            return k.aspp_rates.at[0, 2 * net.r, :, :, lanes], k.w_pyramid.at[pl.ds(10, 3), net.m]
        if kind == "point":
            return k.aspp_point.at[half, lanes], k.w_pyramid.at[0, net.m, half]
        if kind == "project":
            return k.project.at[:, half], k.w_project.at[net.m, :, half]
        return (
            k.aspp_rates.at[kind, 1, :, half, lanes],
            k.w_pyramid.at[pl.ds(1 + 3 * kind, 3), net.m, half],
        )

    def spread_weights(*kinds):
        for kind in kinds:
            src, dst = weight_block(kind, net.m)
            late.append(pltpu.make_async_copy(src, dst, k.local_sems.at[10 + len(late) // 4]))
            late[-1].start()
            for b, peer in branches:
                src, dst = weight_block(kind, b)
                late.append(net.send(src, dst, peer))

    spread_weights("edge")
    mean, inverse = statistics(net, k.reduced, k.mask, counts, k.out_1, k.in_1, counted)
    keep_rows(k.stats_1, mean, inverse)

    def activate_1(at):
        u = k.affine_1[0:1, :] * ((k.reduced[at, :] - mean) * inverse) + k.affine_1[1:2, :]
        rows_at = pl.ds(pl.multiple_of(at.start + 512, 128), 128)
        k.hidden[rows_at, lane_block(net.m)] = (u * sigmoid(u)).astype(BF16)

    each_rows(1536, 128, activate_1)
    gather_blocks(
        net, lambda b, at: k.hidden.at[pl.ds(at.start + 512, at.size), lane_block(b)], 1536
    )
    halo = send_halo(net, k.hidden)
    spread_weights("project", "point", 0)
    zero_margins(k.left, 8, 128)
    zero_margins(k.right, 8, 128)
    for load in loads:
        load.wait()
    halo.wait()
    k.stream.done("hidden")

    def dilated_rows(i, carry):
        total = 0.0
        for tap in range(3):
            rows_at = pl.ds(pl.multiple_of((i * 3 + 4 * tap) * 128, 128), 384)
            total = total + mm(k.hidden[rows_at, :], k.w_taps[tap])
        k.dilated[pl.ds(pl.multiple_of(i * 384, 128), 384), :] = total[:, 128:256]
        k.left[pl.ds(i * 3, 3), 8:136, :] = total[:, 0:128].reshape(3, 128, 128)
        k.right[pl.ds(i * 3, 3), 8:136, :] = total[:, 256:384].reshape(3, 128, 128)
        return carry

    lax.fori_loop(0, 4, dilated_rows, 0)

    def add_columns(i, carry):
        at = pl.ds(pl.multiple_of(i * 128, 128), 128)
        k.dilated[at, :] = k.dilated[at, :] + k.left[i, 4:132, :] + k.right[i, 12:140, :]
        return carry

    lax.fori_loop(0, 12, add_columns, 0)
    k.stream.done("dilated")
    mean_2, inverse_2 = statistics(net, k.dilated, k.mask, counts, k.out_2, k.in_2, counted)
    keep_rows(k.stats_2, mean_2, inverse_2)

    def activate_2(at):
        u = k.affine_2[0:1, :] * ((k.dilated[at, :] - mean_2) * inverse_2) + k.affine_2[1:2, :]
        k.hidden_two[at, lane_block(net.m)] = (u * sigmoid(u)).astype(BF16)

    each_rows(1536, 128, activate_2)
    gather_blocks(net, lambda b, at: k.hidden_two.at[at, lane_block(b)], 1536)
    spread_weights(1, 2)
    k.stream.done("hidden_two")
    k.stream.need("w_expand")

    def expand_rows(at):
        k.expanded[at, :] = mm(k.hidden_two[at, :], k.w_expand[...])

    each_rows(1536, 384, expand_rows)
    k.stream.done("expanded")
    mean_3, inverse_3 = statistics(net, k.expanded, k.mask, counts, k.out_3, k.in_3, counted)
    keep_rows(k.stats_3, mean_3, inverse_3)
    for copy in late:
        copy.wait()
    swaps = [
        net.send(ref.at[..., half, :], ref.at[..., half, :], net.core)
        for ref in (k.w_pyramid.at[pl.ds(0, 10)], k.w_project)
    ]

    def activate_3(at):
        u = k.affine_3[0:1, :] * ((k.expanded[at, :] - mean_3) * inverse_3) + k.affine_3[1:2, :]
        u = u + k.x[at, :].astype(F32)
        k.trunk[at, :] = (u * sigmoid(u)).astype(BF16)

    each_rows(1536, 32, activate_3)
    for copy in swaps:
        copy.wait()


def run_bottleneck(args):
    return call_kernel(
        bottleneck_forward,
        "bottleneck",
        0,
        args,
        dict(
            mask=((1536, 128), F32),
            w_reduce=((4, 512, 128), BF16),
            w_pyramid=((13, 4, 64, 512), BF16),
            w_project=((4, 5, 64, 256), BF16),
            reduced=((1536, 128), F32),
            stats_1=((8, 128), F32),
            hidden=((2560, 512), BF16),
            dilated=((1536, 128), F32),
            stats_2=((8, 128), F32),
            hidden_two=((1536, 512), BF16),
            expanded=((1536, 512), F32),
            stats_3=((8, 512), F32),
            trunk=((1536, 512), BF16),
        ),
        dict(
            w_taps=pltpu.VMEM((3, 512, 384), BF16),
            part=pltpu.VMEM((4, 1536, 128), F32),
            **scatter_scratch("sum", 1536, 128),
            left=pltpu.VMEM((12, 144, 128), F32),
            right=pltpu.VMEM((12, 144, 128), F32),
            **exchange_scratch(1),
            **exchange_scratch(2),
            **exchange_scratch(3),
            local_sems=pltpu.SemaphoreType.DMA((16,)),
        ),
        96,
        hbm=(
            "conv_reduce",
            "w_dilated",
            "aspp_point",
            "aspp_rates",
            "project",
            "w_pyramid",
            "w_project",
        ),
        stream=(
            "x",
            "w_expand",
            "mask",
            "w_reduce",
            "reduced",
            "hidden",
            "dilated",
            "hidden_two",
            "expanded",
        ),
    )


def pyramid_forward(net, k):
    counted, counts = pixel_count(k.boxes), tile_counts(net, k.boxes)
    area = (k.boxes[net.z, 2] * k.boxes[net.z, 3]).astype(F32)
    near = [
        (lax.rem(net.m + a, 4), lax.rem(net.r + b, 2), net.z)
        for a in range(4)
        for b in range(2)
        if a or b
    ]
    greet(net.group + [peer for i, peer in enumerate(near) if i])

    for b in range(4):
        k.affine_b[0:2, b * 64 : b * 64 + 64] = k.branch_norms[:, b, :]
    for i in range(2):
        k.affine_p[0:2, i * 64 : i * 64 + 64] = k.norm_project[...]
        k.affine_p[2:4, i * 64 : i * 64 + 64] = k.norm_pooling[...]
    k.head_rows[...] = jnp.zeros((32, 256), F32)
    k.head_rows[0:22, :] = k.head_weight[...].astype(F32)

    k.stream.need("mask")

    (own_sum,) = column_sums(
        lambda at: (k.trunk[at, :].astype(F32) * wide(k.mask[at, :], 512),), 1536, 512, 1
    )
    k.out_pool[...] = jnp.broadcast_to(own_sum, (8, 512))
    place = net.m * 2 + net.r
    pool_copies = [net.send(k.out_pool, k.in_pool.at[place], peer) for peer in near]
    k.in_pool[place] = k.out_pool[...]

    zero_margins(k.cells, 40, 128)

    def fill(i, carry):
        at = pl.ds(pl.multiple_of(i * 128, 128), 128)
        k.cells[i, 40:168, :] = k.trunk[at, :].astype(F32)
        return carry

    lax.fori_loop(0, 12, fill, 0)

    def shifted(i, offset):
        cells = k.cells[pl.ds(i * 3, 3), 40 + offset : 168 + offset, :]
        return cells.reshape(384, 512).astype(BF16)

    def rows_of(i):
        return pl.ds(pl.multiple_of(i * 384, 128), 384)

    def edge_rows(i, carry):
        total = 0.0
        for j in range(3):
            total = total + mm_t(shifted(i, 12 * (j - 1)), k.w_pyramid[10 + j])
        k.edge_out[rows_of(i), :] = total.astype(BF16)
        return carry

    k.stream.need("w_pyramid")
    lax.fori_loop(0, 4, edge_rows, 0)
    edge = net.send(k.edge_out, k.edge_in, net.core)

    def outer_rows(i, carry):
        second, third = 0.0, 0.0
        for j in range(3):
            second = second + mm_t(shifted(i, 24 * (j - 1)), k.w_pyramid[4 + j])
        for j in range(3):
            third = third + mm_t(shifted(i, 36 * (j - 1)), k.w_pyramid[7 + j])
        for b, block in enumerate(pair(second, third)):
            k.part[b, rows_of(i), 128:256] = block
        return carry

    def inner_rows(i, carry):
        point = mm_t(k.trunk[rows_of(i), :], k.w_pyramid[0])
        first = k.edge_in[rows_of(i), :].astype(F32)
        for j in range(3):
            first = first + mm_t(shifted(i, 12 * (j - 1)), k.w_pyramid[1 + j])
        for b, block in enumerate(pair(point, first)):
            k.part[b, rows_of(i), 0:128] = block
        return carry

    def half_tile(half):
        lax.fori_loop(2 * half, 2 * half + 2, outer_rows, 0)
        if half == 0:
            edge.wait()
        lax.fori_loop(2 * half, 2 * half + 2, inner_rows, 0)

    sum_scatter(net, k.part, scatter_refs(k, "sum"), k.branches, produce=half_tile)

    low_256 = lax.broadcasted_iota(jnp.int32, (256, 128), 1) < 64
    odd = lax.rem(net.m, 2) == 1

    def slot(s):
        lanes = lane_block(net.m // 2)
        block = jnp.concatenate([k.w_slots[b, s, :, lanes] for b in range(4)], axis=0).astype(F32)
        return jnp.where(odd, pltpu.roll(block, 64, 1), block)

    for s in range(0, 4, 2):
        both = jnp.where(low_256, slot(s), pltpu.roll(slot(s + 1), 64, 1))
        k.w_project[:, s * 64 : s * 64 + 128] = both.astype(BF16)
    k.w_slot[...] = jnp.where(low_256, slot(4), 0.0).astype(BF16)
    k.w_pool[0:64, :] = k.aspp_pool[...]
    k.w_pool[64:128, :] = k.aspp_pool[...]

    for copy in pool_copies:
        copy.wait()
    for b in range(4):
        pooled = (k.in_pool[2 * b, 0:1, :] + k.in_pool[2 * b + 1, 0:1, :]) / area
        k.pooled[:, b * 512 : b * 512 + 512] = jnp.broadcast_to(pooled, (16, 512)).astype(BF16)
    pool_conv = mm_t(k.pooled[...], k.w_pool[...])[0:1, :]
    mean, inverse = statistics(
        net, k.branches, k.mask, counts, k.out_1, k.in_1, counted, extra=pool_conv
    )
    every = k.in_1[0:4, 4, :]
    pool_mean = jnp.sum(every, axis=0, keepdims=True) / 4.0
    pool_gap = every - pool_mean
    pool_inverse = lax.rsqrt(jnp.sum(pool_gap * pool_gap, axis=0, keepdims=True) / 4.0 + EPS)
    pool_normed = pool_gap * pool_inverse
    pool_gain, pool_bias = k.affine_p[2:3, :], k.affine_p[3:4, :]
    pool_u = pool_gain * pool_normed + pool_bias
    k.rows_scratch[0:4, :] = pool_u * sigmoid(pool_u)
    pool_act = jnp.broadcast_to(k.rows_scratch[pl.ds(net.z, 1), :], (16, 128)).astype(BF16)

    def normed_branch(at):
        return (k.branches[at, :] - mean) * inverse

    gain_b, bias_b = k.affine_b[0:1, :], k.affine_b[1:2, :]

    def activate_branches(at):
        u = gain_b * normed_branch(at) + bias_b
        k.spatial[at, :] = (u * sigmoid(u)).astype(BF16)

    each_rows(1536, 64, activate_branches)

    pool_row = mm_t(pool_act, k.w_slot[...])[0:1, :]

    def project_rows(i, carry):
        at = pl.ds(pl.multiple_of(i * 384, 128), 384)
        below = pl.ds(pl.multiple_of(i * 384 + 768, 128), 384)
        first = mm_t(k.spatial[at, :], k.w_project[...]) + pool_row
        second = mm_t(k.spatial[below, :], k.w_project[...]) + pool_row
        for b, block in enumerate(pair(first, second)):
            k.part_2[b, at, :] = block
        return carry

    def project_half(half):
        project_rows(half, 0)

    low_128 = lax.broadcasted_iota(jnp.int32, (128, 128), 1) < 64

    def pair_mask(at):
        below = pl.ds(pl.multiple_of(at.start + 768, 128), 128)
        k.mask_pairs[at, :] = jnp.where(low_128, k.mask[at, :], k.mask[below, :])

    each_rows(768, 128, pair_mask)
    sum_scatter(net, k.part_2, scatter_refs(k, "sum2"), k.projected, produce=project_half)
    mean_p, inverse_p = statistics(
        net, k.projected, k.mask_pairs, counts, k.out_2, k.in_2, counted, folded=True
    )
    gain_p, bias_p = k.affine_p[0:1, :], k.affine_p[1:2, :]

    def normed_projected(at):
        return (k.projected[at, :] - mean_p) * inverse_p

    def activate_projected(at):
        u = gain_p * normed_projected(at) + bias_p
        k.gathered[net.m, at, :] = (u * sigmoid(u)).astype(BF16)

    each_rows(768, 128, activate_projected)
    gather_blocks(net, lambda b, at: k.gathered.at[b, at], 768)

    def spread(source, target):
        def body(at):
            first, second = unpair([source[b, at, :].astype(F32) for b in range(4)])
            target[at, :] = first.astype(BF16)
            target[pl.ds(pl.multiple_of(at.start + 768, 128), 128), :] = second.astype(BF16)

        each_rows(768, 128, body)

    k.features[...] = k.gathered[net.m]
    spread(k.gathered, k.wide_features)

    class_row = lax.broadcasted_iota(jnp.int32, (32, 512), 0)
    is_class, is_depth = class_row < 19, class_row == 19
    is_normal = (class_row == 20) | (class_row == 21)
    tile_row = lax.broadcasted_iota(jnp.int32, (32, 128), 0)
    bias_column = jnp.zeros((32, 128), F32)
    for c in range(22):
        bias_column = jnp.where(tile_row == c, k.head_bias[c], bias_column)
    task = [jnp.exp(jnp.full((32, 128), -k.log_vars[t], F32)) / counted for t in range(3)]
    weight_column = jnp.where(tile_row < 19, task[0], jnp.where(tile_row == 19, task[1], task[2]))
    bias_column, weight_column = wide(bias_column, 512), wide(weight_column, 512)
    k.head[...] = k.head_rows[...].astype(BF16)
    top_row, left_edge = k.boxes[net.z, 0], k.boxes[net.z, 1]
    bottom_row, right_edge = top_row + k.boxes[net.z, 2], left_edge + k.boxes[net.z, 3]
    lane = lax.broadcasted_iota(jnp.int32, (1, 512), 1)

    def four_rows(rows):
        return jnp.concatenate(rows, axis=1)
    loss_sums, bias_sums = 0.0, 0.0
    for chunk in range(3):
        at = pl.ds(chunk * 512, 512)
        logits = mm_t(k.head[...], k.wide_features[at, :]) + bias_column
        row_id, column_id = net.r * 12 + chunk * 4 + lane // 128, lane % 128
        inside = (row_id >= top_row) & (row_id < bottom_row)
        inside = inside & (column_id >= left_edge) & (column_id < right_edge)
        inside = jnp.where(inside, 1.0, 0.0)
        span = range(chunk * 4, chunk * 4 + 4)
        label = four_rows([k.labels[y] for y in span])
        target = jnp.where(is_depth, four_rows([k.depth[y] for y in span]), 0.0)
        for n in range(2):
            normal = four_rows([k.normal[y, n : n + 1, :] for y in span])
            target = jnp.where(class_row == 20 + n, normal, target)
        top = jnp.max(jnp.where(is_class, logits, -jnp.inf), axis=0, keepdims=True)
        powers = jnp.where(is_class, jnp.exp(jnp.where(is_class, logits - top, 0.0)), 0.0)
        power_sum = jnp.sum(powers, axis=0, keepdims=True)
        onehot = jnp.where(class_row == label, 1.0, 0.0)
        cross = jnp.log(power_sum) + top - jnp.sum(logits * onehot, axis=0, keepdims=True)
        gap = logits - target
        smooth = jnp.sqrt(gap * gap + 1.0)
        loss = jnp.where(class_row == 0, cross, 0.0)
        loss = jnp.where(is_depth, smooth - 1.0, loss)
        loss = jnp.where(is_normal, gap * gap, loss) * inside
        grad = jnp.where(is_class, powers / power_sum - onehot, 0.0)
        grad = jnp.where(is_depth, gap / smooth, grad)
        grad = jnp.where(is_normal, 2.0 * gap, grad) * (weight_column * inside)
        loss_sums = loss_sums + jnp.sum(loss, axis=1, keepdims=True)
        bias_sums = bias_sums + jnp.sum(grad, axis=1, keepdims=True)
        high = grad.astype(BF16)
        k.grad_logits[0:32, at] = high
        k.grad_logits[32:64, at] = (grad - high.astype(F32)).astype(BF16)
    head_terms = mm(k.grad_logits[...], k.wide_features[...])
    k.out_head[:, 0:256] = head_terms[0:32, :] + head_terms[32:64, :]
    first_lane = lax.broadcasted_iota(jnp.int32, (32, 128), 1) == 0
    k.out_head[:, 256:384] = jnp.where(first_lane, bias_sums, loss_sums)
    quarter = pl.ds(pl.multiple_of(net.m * 8, 8), 8)
    head_copies = [
        net.send(k.out_head.at[quarter], k.in_head.at[net.slot], peer) for peer in net.group
    ]
    k.in_head[net.slot] = k.out_head[quarter, :]

    own_head = k.head_rows[:, lane_block(net.m // 2)]
    own_head = jnp.where(odd, pltpu.roll(own_head, 64, 1), own_head)
    own_head = jnp.where(low_128[0:32, :], own_head, 0.0)
    head_low = jnp.concatenate([own_head, own_head], axis=0).astype(BF16)
    own_head = pltpu.roll(own_head, 64, 1)
    head_high = jnp.concatenate([own_head, own_head], axis=0).astype(BF16)
    k.grad_p[...] = tm_m(k.grad_logits[:, 0:768], head_low) + tm_m(
        k.grad_logits[:, 768:1536], head_high
    )

    def back_features(at):
        k.grad_p[at, :] = k.grad_p[at, :] * slope(gain_p * normed_projected(at) + bias_p)

    each_rows(768, 128, back_features)
    bias_grad, gain_grad = gradient_sums(
        net, k.grad_p, normed_projected, k.out_3, k.in_3, folded=True
    )
    keep_rows(k.norm_p, gain_grad, bias_grad)

    def back_projected(at):
        shared = k.mask_pairs[at, :] / counted * gain_p
        grad = gain_p * k.grad_p[at, :] - shared * (bias_grad + normed_projected(at) * gain_grad)
        k.gathered_grad[net.m, at, :] = (inverse_p * grad).astype(BF16)

    each_rows(768, 128, back_projected)
    gather_blocks(net, lambda b, at: k.gathered_grad.at[b, at], 768)
    spread(k.gathered_grad, k.grad_projected)
    (pixel_sum,) = column_sums(lambda at: (k.grad_projected[at, :].astype(F32),), 1536, 256, 1)
    row_16 = lax.broadcasted_iota(jnp.int32, (16, 256), 0)
    terms = jnp.zeros((16, 256), F32)
    for i, term in enumerate(split_three(pixel_sum)):
        terms = jnp.where(row_16 == i, term.astype(F32), terms)
    terms = terms.astype(BF16)
    tall = jnp.concatenate([terms] * 8, axis=0)
    pool_grad = jnp.sum(mm(tall, k.w_slot[...]), axis=0, keepdims=True) * 0.125

    def project_gradient():
        for b in range(2):
            lanes = slice(b * 128, b * 128 + 128)
            grad = tm_m(k.grad_projected[:, lanes], k.spatial[...])
            k.grad_project[b * 4 : b * 4 + 4, :, 0:256] = grad.reshape(4, 32, 256).astype(BF16)
        grad = tm_m(terms, pool_act)
        k.grad_project[:, :, 256:384] = grad.reshape(8, 32, 128).astype(BF16)

    def back_spatial(at):
        grad = mm(k.grad_projected[at, :], k.w_project[...])
        k.grad_b[at, :] = grad * slope(gain_b * normed_branch(at) + bias_b)

    each_rows(1536, 128, back_spatial)
    bias_grad_b, gain_grad_b = gradient_sums(
        net,
        k.grad_b,
        normed_branch,
        k.out_4,
        k.in_4,
        extra=pool_grad,
        meanwhile=project_gradient,
    )
    keep_rows(k.norm_b, gain_grad_b, bias_grad_b)

    pool_terms = k.in_4[0:4, 4, :] + k.in_4[4:8, 4, :]
    pool_terms = pool_terms * slope(pool_u)
    pool_bias_grad = jnp.sum(pool_terms, axis=0, keepdims=True)
    pool_gain_grad = jnp.sum(pool_terms * pool_normed, axis=0, keepdims=True)
    keep_rows(k.norm_pool, pool_gain_grad, pool_bias_grad)
    pool_back = pool_inverse * (
        pool_gain * pool_terms
        - pool_gain / 4.0 * (pool_bias_grad + pool_normed * pool_gain_grad)
    )
    low = lax.broadcasted_iota(jnp.int32, (4, 128), 1) < 64
    k.rows_scratch[4:8, :] = jnp.where(low, pool_back, 0.0)
    grad_conv = jnp.broadcast_to(k.rows_scratch[pl.ds(net.z + 4, 1), :], (16, 128)).astype(BF16)
    spread_back = mm(grad_conv, k.w_pool[...])[0:8, :]
    for b in range(4):
        k.out_back[b] = spread_back[:, b * 512 : b * 512 + 512]
    back_copies = [
        net.send(k.out_back.at[lax.rem(net.m + a, 4)], k.in_back.at[a], (lax.rem(net.m + a, 4), net.r, net.z))
        for a in range(1, 4)
    ]

    only_first = lax.broadcasted_iota(jnp.int32, (16, 128), 0) == 0
    one_row = jnp.where(only_first, grad_conv.astype(F32) * 0.5, 0.0).astype(BF16)
    for e in range(8):
        grad = tm_m(one_row, k.pooled[:, e * 256 : e * 256 + 256])
        k.grad_pool[e] = grad[0:64, :].astype(BF16)

    def back_branches(at):
        shared = wide(k.mask[at, :], 256) / counted * gain_b
        grad = gain_b * k.grad_b[at, :] - shared * (bias_grad_b + normed_branch(at) * gain_grad_b)
        k.grad_branches[at, :] = (inverse * grad).astype(BF16)

    for copy in back_copies:
        copy.wait()
    k.grad_pooled[...] = (k.out_back[net.m] + k.in_back[1] + k.in_back[2] + k.in_back[3]) / area
    for copy in head_copies:
        copy.wait()
    k.head_sums[quarter, :] = jnp.sum(k.in_head[...], axis=0)
    head_copies = [
        net.send(k.head_sums.at[quarter], k.head_sums.at[quarter], (lax.rem(net.m + a, 4), net.r, net.z))
        for a in range(1, 4)
    ]
    each_rows(1536, 64, back_branches)
    for copy in head_copies:
        copy.wait()


def run_pyramid(args):
    return call_kernel(
        pyramid_forward,
        "pyramid",
        1,
        args,
        dict(
            features=((768, 128), BF16),
            norm_p=((8, 128), F32),
            grad_project=((8, 32, 384), BF16),
            grad_pool=((8, 64, 256), BF16),
            norm_b=((8, 256), F32),
            norm_pool=((8, 128), F32),
            grad_branches=((1536, 256), BF16),
            grad_pooled=((8, 512), F32),
            head_sums=((32, 384), F32),
        ),
        dict(
            affine_b=pltpu.VMEM((8, 256), F32),
            affine_p=pltpu.VMEM((8, 128), F32),
            head_rows=pltpu.VMEM((32, 256), F32),
            head=pltpu.VMEM((32, 256), BF16),
            pooled=pltpu.VMEM((16, 2048), BF16),
            spatial=pltpu.VMEM((1536, 256), BF16),
            grad_projected=pltpu.VMEM((1536, 256), BF16),
            w_project=pltpu.VMEM((256, 256), BF16),
            w_slot=pltpu.VMEM((256, 128), BF16),
            w_pool=pltpu.VMEM((128, 2048), BF16),
            mask_pairs=pltpu.VMEM((768, 128), F32),
            out_pool=pltpu.VMEM((8, 512), F32),
            in_pool=pltpu.VMEM((8, 8, 512), F32),
            cells=pltpu.VMEM((12, 208, 512), F32),
            edge_out=pltpu.VMEM((1536, 256), BF16),
            edge_in=pltpu.VMEM((1536, 256), BF16),
            part=pltpu.VMEM((4, 1536, 256), F32),
            **scatter_scratch("sum", 1536, 256),
            branches=pltpu.VMEM((1536, 256), F32),
            rows_scratch=pltpu.VMEM((8, 128), F32),
            part_2=pltpu.VMEM((4, 768, 128), F32),
            **scatter_scratch("sum2", 768, 128),
            projected=pltpu.VMEM((768, 128), F32),
            gathered=pltpu.VMEM((4, 768, 128), BF16),
            wide_features=pltpu.VMEM((1536, 256), BF16),
            grad_logits=pltpu.VMEM((64, 1536), BF16),
            out_head=pltpu.VMEM((32, 384), F32),
            in_head=pltpu.VMEM((8, 8, 384), F32),
            grad_p=pltpu.VMEM((768, 128), F32),
            gathered_grad=pltpu.VMEM((4, 768, 128), BF16),
            grad_b=pltpu.VMEM((1536, 256), F32),
            out_back=pltpu.VMEM((4, 8, 512), F32),
            in_back=pltpu.VMEM((4, 8, 512), F32),
            **exchange_scratch(1),
            **exchange_scratch(2),
            **exchange_scratch(3),
            **exchange_scratch(4),
        ),
        96,
        smem=("boxes", "head_bias", "log_vars"),
        stream=("mask", "w_pyramid"),
    )


def core_halves(net, whole, arrived):
    away = pl.ds(pl.multiple_of(4 - 4 * net.r, 4), 4)
    return net.send(whole.at[away], arrived, net.core)


def add_halves(net, whole, arrived, target):
    for z in range(4):
        total = whole[4 * net.r + z].astype(F32) + arrived[z].astype(F32)
        target[z] = total.astype(target.dtype)


def chunk_of(z):
    return 2 * lax.rem(z, 2) + z // 2


def along_z(net, source, target, chunk=lambda z: z):
    copies = []
    for d in (1, 2, 3):
        there = lax.rem(net.z + d, 4)
        copies.append(
            net.send(source.at[chunk(there)], target.at[d - 1], (net.m, net.r, there))
        )
    return copies


def finish_z(net, half, arrived, chunk=lambda z: z):
    return half[chunk(net.z)].astype(F32) + sum(arrived[d].astype(F32) for d in range(3))


class PairSums:
    def __init__(self, net, half, other, pair, last):
        self.net, self.half, self.other, self.pair, self.last = net, half, other, pair, last
        kept, away = lax.rem(net.z, 2), lax.rem(net.z + 1, 2)
        self.kept = 2 * kept
        self.first = self.copy(half.at[pl.ds(2 * away, 2)], other, net.z + 1 - 2 * kept)
        self.high = net.z // 2
        self.second = self.copy(pair.at[1 - self.high], last, net.z + 2 - 4 * self.high)

    def copy(self, src, dst, z):
        net, i = self.net, self.net.count
        net.count += 1
        return pltpu.make_async_remote_copy(
            src_ref=src,
            dst_ref=dst,
            send_sem=net.send_sems.at[i],
            recv_sem=net.recv_sems.at[i],
            device_id=(net.m, net.r, z),
            device_id_type=MESH,
        )

    def begin(self):
        self.first.start()

    def go_on(self, half):
        self.first.wait()

        def body(i, carry):
            for h in range(2):
                total = half[self.kept + h, i].astype(F32) + self.other[h, i].astype(F32)
                self.pair[h, i] = total.astype(BF16)
            return carry

        lax.fori_loop(0, half.shape[1], body, 0)
        self.second.start()

    def finish(self, target):
        self.second.wait()

        def body(i, carry):
            total = self.pair[self.high, i].astype(F32) + self.last[i].astype(F32)
            target[i] = total.astype(BF16)
            return carry

        lax.fori_loop(0, target.shape[0], body, 0)


def pyramid_backward(net, k):
    counted = pixel_count(k.boxes)
    greet([net.side, net.over] + net.group)
    k.blocks[net.m] = k.grad_branches[...]
    small = [
        core_halves(net, k.grad_project, k.core_project),
        core_halves(net, k.grad_pool, k.core_pool),
    ]
    for c in range(4):
        zero_margins(k.cells.at[c], 40, 128)

    def rows_of(i, size=384):
        return pl.ds(pl.multiple_of(i * size, 128), size)

    low = lax.broadcasted_iota(jnp.int32, (128, 128), 1) < 64
    near = net.m // 2
    far = 1 - near
    mine_first = net.r == near
    mine_second = net.r == far

    def both(source, pair_of, i, lane):
        at = slice(lane * 128, lane * 128 + 128)
        left = source[2 * pair_of, rows_of(i, 128), at].astype(F32)
        right = source[2 * pair_of + 1, rows_of(i, 128), at].astype(F32)
        first = jnp.where(low, left, pltpu.roll(right, 64, 1))
        return first, jnp.where(low, pltpu.roll(left, 64, 1), right)

    def shift_rows(pair_of, i, cell, rate, base):
        for j in range(3):
            start = 40 - rate * (j - 1)
            block = k.cells[cell, i, start : start + 128, :].astype(BF16)
            k.shifts[base + j, rows_of(i, 128), lane_block(pair_of)] = block

    def build(pair_of):
        def fill(i, carry):
            point, first = both(k.blocks, pair_of, i, 0)
            k.shifts[0, rows_of(i, 128), lane_block(pair_of)] = point.astype(BF16)
            second, third = both(k.blocks, pair_of, i, 1)
            k.cells[0, i, 40:168, :] = first
            k.cells[1, i, 40:168, :] = second
            k.cells[2, i, 40:168, :] = third
            return carry

        lax.fori_loop(0, 12, fill, 0)

        def spread(i, carry):
            for cell, rate, base in ((0, 12, 1), (1, 24, 4), (2, 36, 7)):
                shift_rows(pair_of, i, cell, rate, base)
            return carry

        lax.fori_loop(0, 12, spread, 0)

    def build_edge(pair_of):
        def fill(i, carry):
            k.cells[3, i, 40:168, :] = both(k.other, pair_of, i, 0)[1]
            return carry

        lax.fori_loop(0, 12, fill, 0)

        def spread(i, carry):
            shift_rows(pair_of, i, 3, 12, 10)
            return carry

        lax.fori_loop(0, 12, spread, 0)

    def weight_gradients(pair_of):
        owners = pl.ds(4 * pair_of, 4)

        def run(start, stop, shift):
            def body(t, carry):
                grad = tm_m(k.shifts[t, :, lane_block(pair_of)], k.trunk[...])
                k.grad_pyramid[owners, t + shift] = grad.reshape(4, 32, 512).astype(BF16)
                return carry

            lax.fori_loop(start, stop, body, 0)

        run(0, 1, 0)
        run(1, 4, 3)
        run(4, 10, 6)
        run(10, 13, net.r * 6 - 9)
        for j in range(3):
            k.grad_pyramid[owners, 7 - net.r * 6 + j] = jnp.zeros((4, 32, 512), BF16)

    def beside(pair_of):
        view = (pl.ds(2 * pair_of, 2), slice(None), pl.ds(0, 128))
        return net.send(k.blocks.at[view], k.other.at[pl.ds(2 * pair_of, 2)], net.core)

    def to_core(pair_of):
        i = net.count
        net.count += 1
        return pltpu.make_async_remote_copy(
            src_ref=k.grad_pyramid.at[pl.ds(4 * pair_of, 4)],
            dst_ref=k.core_pyramid,
            send_sem=net.send_sems.at[i],
            recv_sem=net.recv_sems.at[i],
            device_id=net.core,
            device_id_type=MESH,
        )

    def add_core(pair_of):
        def body(i, carry):
            for z in range(4):
                total = k.grad_pyramid[4 * pair_of + z, i].astype(F32)
                total = total + k.core_pyramid[z, i].astype(F32)
                k.half_pyramid[z, i] = total.astype(BF16)
            return carry

        lax.fori_loop(0, 16, body, 0)

    first_swap = []

    def near_pair():
        copy = beside(near)
        build(near)
        copy.wait()
        build_edge(near)
        k.stream.need("trunk")
        weight_gradients(near)
        first_swap.append(to_core(near))
        pl.when(mine_second)(first_swap[0].start)

    gather_blocks(net, lambda b, at: k.blocks.at[b, at], 1536, meanwhile=near_pair)
    copy = beside(far)
    build(far)
    for swap in small:
        swap.wait()
    add_halves(net, k.grad_project, k.core_project, k.half_project)
    add_halves(net, k.grad_pool, k.core_pool, k.half_pool)
    small_moves = along_z(net, k.half_project, k.z_project, chunk_of)
    small_moves = small_moves + along_z(net, k.half_pool, k.z_pool)
    copy.wait()
    build_edge(far)
    pair_sums = PairSums(net, k.half_pyramid, k.z_other, k.z_pair, k.z_last)

    @pl.when(mine_first)
    def _():
        first_swap[0].wait_recv()
        add_core(near)
        pair_sums.begin()

    def trunk_rows(i, carry):
        total = 0.0
        for t in range(13):
            total = total + mm(k.shifts[t, rows_of(i), :], k.w_pyramid[t])
        k.shortcut[rows_of(i), :] = total
        return carry

    k.stream.need("w_pyramid", "expanded", "x", "mask")
    lax.fori_loop(0, 4, trunk_rows, 0)
    mean, inverse = k.stats_3[0:1, :], k.stats_3[1:2, :]
    gain, bias = k.affine_3[0:1, :], k.affine_3[1:2, :]
    pooled = k.grad_pooled[0:1, :]

    def normed(at):
        return (k.expanded[at, :] - mean) * inverse

    def back_trunk(at):
        u = gain * normed(at) + bias + k.x[at, :].astype(F32)
        grad = k.shortcut[at, :] + wide(k.mask[at, :], 512) * pooled
        k.shortcut[at, :] = grad * slope(u)

    each_rows(1536, 32, back_trunk)
    k.stream.done("shortcut")

    second_swap = to_core(far)

    def far_gradients():
        weight_gradients(far)

        @pl.when(mine_first)
        def _():
            second_swap.start()
            pair_sums.go_on(k.half_pyramid)

    bias_grad, gain_grad = gradient_sums(
        net, k.shortcut, normed, k.out_1, k.in_1, meanwhile=far_gradients
    )
    keep_rows(k.norm_3, gain_grad, bias_grad)

    def back_expanded(at):
        shared = wide(k.mask[at, :], 512) / counted * gain
        grad = gain * k.shortcut[at, :] - shared * (bias_grad + normed(at) * gain_grad)
        k.grad_expanded[at, :] = (inverse * grad).astype(BF16)

    each_rows(1536, 32, back_expanded)
    k.stream.done("grad_expanded")
    for move_ in small_moves:
        move_.wait()
    k.sum_project[...] = finish_z(net, k.half_project, k.z_project, chunk_of)
    k.sum_pool[...] = finish_z(net, k.half_pool, k.z_pool)

    @pl.when(mine_second)
    def _():
        first_swap[0].wait_send()
        second_swap.wait_recv()
        add_core(far)

    @pl.when(mine_first)
    def _():
        second_swap.wait_send()
        pair_sums.finish(k.sum_pyramid)


def pair_scratch():
    return dict(
        z_other=pltpu.VMEM((2, 16, 32, 512), BF16),
        z_pair=pltpu.VMEM((2, 16, 32, 512), BF16),
        z_last=pltpu.VMEM((16, 32, 512), BF16),
    )


def run_pyramid_backward(args):
    return call_kernel(
        pyramid_backward,
        "pyramid_back",
        2,
        args,
        dict(
            shortcut=((1536, 512), F32),
            grad_expanded=((1536, 512), BF16),
            norm_3=((8, 512), F32),
            half_pyramid=((4, 16, 32, 512), BF16),
            sum_pyramid=((16, 32, 512), BF16),
            sum_project=((32, 384), F32),
            sum_pool=((64, 256), F32),
        ),
        dict(
            half_project=pltpu.VMEM((4, 32, 384), BF16),
            half_pool=pltpu.VMEM((4, 64, 256), BF16),
            **pair_scratch(),
            z_project=pltpu.VMEM((3, 32, 384), BF16),
            z_pool=pltpu.VMEM((3, 64, 256), BF16),
            grad_pyramid=pltpu.VMEM((8, 16, 32, 512), BF16),
            core_pyramid=pltpu.VMEM((4, 16, 32, 512), BF16),
            core_project=pltpu.VMEM((4, 32, 384), BF16),
            core_pool=pltpu.VMEM((4, 64, 256), BF16),
            blocks=pltpu.VMEM((4, 1536, 256), BF16),
            other=pltpu.VMEM((4, 1536, 128), BF16),
            cells=pltpu.VMEM((4, 12, 208, 128), F32),
            shifts=pltpu.VMEM((13, 1536, 256), BF16),
            **exchange_scratch(1),
        ),
        48,
        stream=("w_pyramid", "expanded", "x", "mask", "trunk", "shortcut", "grad_expanded"),
    )


def bottleneck_backward(net, k):
    counted = pixel_count(k.boxes)
    loads = load_taps(k)
    high = net.z // 2
    owners, givers = [], []
    for which in (high, 1 - high):
        part = 2 * net.m + which
        owners.append((2 * net.r + lax.rem(net.z, 2), part // 4, lax.rem(part, 4)))
    odd = lax.rem(net.z, 2)
    for which in (odd, 1 - odd):
        givers.append((net.slot // 2, net.m // 2, lax.rem(net.m, 2) + 2 * which))
    here = net.m * 8 + net.slot
    moves = owners[0][0] * 8 + owners[0][1] * 4 + owners[0][2] != here
    stays = jnp.logical_not(moves)
    greet(
        [net.side, net.over] + net.group + [owners[1], givers[1]],
        [(owners[0], moves), (givers[0], moves)],
    )

    def to_owners(views, arrived, sem, start=True):
        first = pltpu.make_async_remote_copy(
            src_ref=views(0),
            dst_ref=arrived.at[0],
            send_sem=net.send_sems.at[net.count],
            recv_sem=net.recv_sems.at[net.count],
            device_id=owners[0],
            device_id_type=MESH,
        )
        net.count += 1
        kept = pltpu.make_async_copy(views(0), arrived.at[0], sem)
        i = net.count
        net.count += 1
        second = pltpu.make_async_remote_copy(
            src_ref=views(1),
            dst_ref=arrived.at[1],
            send_sem=net.send_sems.at[i],
            recv_sem=net.recv_sems.at[i],
            device_id=owners[1],
            device_id_type=MESH,
        )

        def begin():
            pl.when(moves)(first.start)
            pl.when(stays)(kept.start)
            second.start()

        def wait():
            pl.when(moves)(first.wait)
            pl.when(stays)(kept.wait)
            second.wait()

        if start:
            begin()
            return wait
        return begin, wait

    def lanes_for(i):
        return lane_block(high if i == 0 else 1 - high, 256)

    early = net.r == net.m // 2
    is_late = net.r == 1 - net.m // 2
    pair_sums = PairSums(net, k.far_half_pyramid, k.z_other, k.z_pair, k.z_last)

    begin_pyramid, wait_pyramid = to_owners(
        lambda i: k.pyramid_sum.at[:, :, lanes_for(i)], k.own_pyramid, k.local_sems.at[9], False
    )

    @pl.when(is_late)
    def _():
        pair_sums.begin()

    @pl.when(early)
    def _():
        k.pyramid_sum[...] = k.sum_pyramid[...]
        begin_pyramid()

    wait_project = to_owners(lambda i: k.sum_project, k.own_project, k.local_sems.at[10])

    def rows_of(i, size=384):
        return pl.ds(pl.multiple_of(i * size, 128), size)

    def expand_half(half):
        def expand_rows(at):
            at = pl.ds(pl.multiple_of(at.start + half * 768, 128), 384)
            total = mm_t(k.grad_expanded[at, :], k.w_expand[...])
            for b in range(4):
                k.part[b, at, :] = total[:, b * 128 : b * 128 + 128]

        each_rows(768, 384, expand_rows)

    swaps, late_moves = [], []

    def expand_gradient():
        k.stream.need("hidden_two")

        def body(b, carry):
            grad = tm_m(k.hidden_two[:, lane_block(b)], k.grad_expanded[...])
            k.grad_expand[pl.ds(2 * b, 2)] = grad.reshape(2, 64, 512).astype(BF16)
            return carry

        lax.fori_loop(0, 4, body, 0)
        swaps.append(core_halves(net, k.grad_expand, k.core_expand))

    sum_scatter(net, k.part, scatter_refs(k, "sum"), k.grad_2, meanwhile=expand_gradient, produce=expand_half)
    k.stream.need("dilated", "mask")

    def norm_back(grad, value, stats, affine, outgoing, incoming, store, kept, meanwhile=None):
        mean, inverse = stats[0:1, :], stats[1:2, :]
        gain, bias = affine[0:1, :], affine[1:2, :]

        def normed(at):
            return (value[at, :] - mean) * inverse

        def through(at):
            grad[at, :] = grad[at, :] * slope(gain * normed(at) + bias)

        each_rows(1536, 128, through)
        bias_grad, gain_grad = gradient_sums(
            net, grad, normed, outgoing, incoming, meanwhile=meanwhile
        )
        keep_rows(kept, gain_grad, bias_grad)

        def back(at):
            shared = k.mask[at, :] / counted * gain
            result = gain * grad[at, :] - shared * (bias_grad + normed(at) * gain_grad)
            store(at, (inverse * result).astype(BF16))

        each_rows(1536, 128, back)

    def store_2(at, value):
        k.grad_pad[pl.ds(pl.multiple_of(at.start + 512, 128), 128), :] = value

    def pass_expand():
        k.stream.need("half_pyramid")

        @pl.when(is_late)
        def _():
            pair_sums.go_on(k.half_pyramid)

        swaps.pop().wait()
        add_halves(net, k.grad_expand, k.core_expand, k.half_expand)
        late_moves.extend(along_z(net, k.half_expand, k.z_expand))

    norm_back(
        k.grad_2,
        k.dilated,
        k.stats_2,
        k.affine_2,
        k.out_2,
        k.in_2,
        store_2,
        k.norm_2,
        meanwhile=pass_expand,
    )
    halo = send_halo(net, k.grad_pad)
    zero_margins(k.cells, 8, 128)
    halo.wait()

    def spread(i, carry):
        k.cells[i, 8:136, :] = k.grad_pad[rows_of(i, 128), :].astype(F32)
        for j in range(3):
            start = 8 - 4 * (j - 1)
            k.grad_taps[rows_of(i, 128), j * 128 : j * 128 + 128] = k.cells[
                i, start : start + 128, :
            ].astype(BF16)
        return carry

    lax.fori_loop(0, 20, spread, 0)
    for load in loads:
        load.wait()

    def dilated_rows(i, carry):
        total = 0.0
        for tap in range(3):
            at = pl.ds(pl.multiple_of((i * 3 + 8 - 4 * tap) * 128, 128), 384)
            total = total + mm_t(k.grad_taps[at, :], k.w_taps[tap])
        for b in range(4):
            k.part[b, rows_of(i), :] = total[:, b * 128 : b * 128 + 128]
        return carry

    def dilated_half(half):
        lax.fori_loop(2 * half, 2 * half + 2, dilated_rows, 0)

    def dilated_gradient():
        k.stream.need("hidden")

        for i in range(3):

            def body(b, carry):
                band = k.hidden[pl.ds(i * 512, 1536), lane_block(b)]
                grad = tm_m(band, k.grad_taps[pl.ds(512, 1536), :])
                for j in range(3):
                    block = grad[:, j * 128 : j * 128 + 128].reshape(2, 64, 128)
                    rows = slice((i * 3 + j) * 64, (i * 3 + j) * 64 + 64)
                    k.grad_dilated[pl.ds(2 * b, 2), rows, :] = block.astype(BF16)
                return carry

            lax.fori_loop(0, 4, body, 0)
        swaps.append(core_halves(net, k.grad_dilated, k.core_dilated))

    sum_scatter(net, k.part, scatter_refs(k, "sum2"), k.grad_1, meanwhile=dilated_gradient, produce=dilated_half)
    k.stream.need("reduced")

    def store_1(at, value):
        k.grad_reduced[at, lane_block(net.m)] = value

    def pass_halves():
        @pl.when(is_late)
        def _():
            pair_sums.finish(k.pyramid_sum)
            begin_pyramid()

        swaps.pop().wait()
        add_halves(net, k.grad_dilated, k.core_dilated, k.half_dilated)
        late_moves.extend(along_z(net, k.half_dilated, k.z_dilated))

    norm_back(
        k.grad_1,
        k.reduced,
        k.stats_1,
        k.affine_1,
        k.out_1,
        k.in_1,
        store_1,
        k.norm_1,
        meanwhile=pass_halves,
    )
    gather_blocks(net, lambda b, at: k.grad_reduced.at[at, lane_block(b)], 1536)

    k.stream.need("x")

    def reduce_gradient(b, carry):
        grad = tm_m(k.grad_reduced[:, lane_block(b)], k.x[...])
        k.grad_reduce[pl.ds(2 * b, 2)] = grad.reshape(2, 64, 512).astype(BF16)
        return carry

    lax.fori_loop(0, 4, reduce_gradient, 0)
    swap = core_halves(net, k.grad_reduce, k.core_reduce)

    swap.wait()
    add_halves(net, k.grad_reduce, k.core_reduce, k.half_reduce)
    reduce_moves = along_z(net, k.half_reduce, k.z_reduce, chunk_of)

    k.stream.need("shortcut", "w_reduce")

    def input_rows(at):
        total = k.shortcut[at, :]
        for b in range(4):
            total = total + mm_t(k.grad_reduced[at, b * 128 : b * 128 + 128], k.w_reduce[b])
        k.grad_input[at, :] = total

    each_rows(1536, 384, input_rows)
    k.stream.done("grad_input")
    for move_ in reduce_moves:
        move_.wait()
    k.sum_reduce[...] = finish_z(net, k.half_reduce, k.z_reduce, chunk_of)
    wait_reduce = to_owners(
        lambda i: k.sum_reduce.at[:, lanes_for(i)], k.own_reduce, k.local_sems.at[11]
    )
    for move_ in late_moves:
        move_.wait()
    k.sum_dilated[...] = finish_z(net, k.half_dilated, k.z_dilated)
    k.sum_expand[...] = finish_z(net, k.half_expand, k.z_expand)
    wait_pyramid()
    wait_project()
    wait_reduce()


def run_bottleneck_backward(args):
    return call_kernel(
        bottleneck_backward,
        "bottleneck_back",
        3,
        args,
        dict(
            grad_input=((1536, 512), F32),
            norm_2=((8, 128), F32),
            norm_1=((8, 128), F32),
            own_pyramid=((2, 16, 32, 256), BF16),
            own_project=((2, 32, 384), F32),
            sum_dilated=((576, 128), F32),
            sum_expand=((64, 512), F32),
            own_reduce=((2, 64, 256), F32),
        ),
        dict(
            grad_taps=pltpu.VMEM((2560, 384), BF16),
            grad_reduced=pltpu.VMEM((1536, 512), BF16),
            **pair_scratch(),
            pyramid_sum=pltpu.VMEM((16, 32, 512), BF16),
            sum_reduce=pltpu.VMEM((64, 512), F32),
            grad_expand=pltpu.VMEM((8, 64, 512), BF16),
            core_expand=pltpu.VMEM((4, 64, 512), BF16),
            half_expand=pltpu.VMEM((4, 64, 512), BF16),
            z_expand=pltpu.VMEM((3, 64, 512), BF16),
            grad_reduce=pltpu.VMEM((8, 64, 512), BF16),
            core_reduce=pltpu.VMEM((4, 64, 512), BF16),
            half_reduce=pltpu.VMEM((4, 64, 512), BF16),
            z_reduce=pltpu.VMEM((3, 64, 512), BF16),
            grad_dilated=pltpu.VMEM((8, 576, 128), BF16),
            core_dilated=pltpu.VMEM((4, 576, 128), BF16),
            half_dilated=pltpu.VMEM((4, 576, 128), BF16),
            z_dilated=pltpu.VMEM((3, 576, 128), BF16),
            w_taps=pltpu.VMEM((3, 512, 384), BF16),
            part=pltpu.VMEM((4, 1536, 128), F32),
            **scatter_scratch("sum", 1536, 128),
            **scatter_scratch("sum2", 1536, 128),
            grad_2=pltpu.VMEM((1536, 128), F32),
            grad_1=pltpu.VMEM((1536, 128), F32),
            grad_pad=pltpu.VMEM((2560, 128), BF16),
            cells=pltpu.VMEM((20, 144, 128), F32),
            **exchange_scratch(2),
            **exchange_scratch(1),
            local_sems=pltpu.SemaphoreType.DMA((12,)),
        ),
        96,
        hbm=("w_dilated",),
        stream=(
            "half_pyramid",
            "hidden_two",
            "dilated",
            "mask",
            "hidden",
            "reduced",
            "x",
            "shortcut",
            "w_reduce",
            "grad_input",
        ),
    )


def finish(net, k):
    counted = pixel_count(k.boxes)
    odd = lax.rem(lax.axis_index("batch"), 2)

    def rows_for(i):
        return pl.ds(pl.multiple_of((odd if i == 0 else 1 - odd) * 32, 32), 32)

    nothing = jnp.zeros((64, 256), F32)
    for tap in (9, 10, 11, 15, 16, 17, 18, 19, 20, 24, 25, 26):
        k.grad_rates[tap] = nothing
    for slot in range(16):
        for i in range(2):
            block = k.own_pyramid[i, slot].astype(F32)
            if slot == 0:
                k.grad_point[rows_for(i), :] = block
            else:
                tap = slot - 1 if slot < 10 else slot + 2 if slot < 13 else slot + 8
                k.grad_rates[tap, rows_for(i), :] = block
    k.stream.done("grad_rates")
    k.stream.need("from_input")
    leave = pltpu.make_async_copy(k.from_input, k.grad_input, k.sem.at[0])
    leave.start()
    for y in range(6):
        turned = k.packed[y * 128 : y * 128 + 128, :].astype(F32).T.astype(BF16)
        k.features[y] = turned[0:64, :]
        k.features[y + 6] = turned[64:128, :]
    rows = jnp.concatenate([k.own_project[0], k.own_project[1]], axis=0)
    swapped = jnp.concatenate([k.own_project[1], k.own_project[0]], axis=0)
    k.turned[...] = jnp.where(odd == 0, rows, swapped).T
    for slot in range(5):
        start = pl.multiple_of(slot * 64 + odd * 32, 32)
        k.grad_project[slot] = k.turned[pl.ds(start, 32), :]
    rows = jnp.concatenate([k.own_reduce[0], k.own_reduce[1]], axis=0)
    swapped = jnp.concatenate([k.own_reduce[1], k.own_reduce[0]], axis=0)
    k.grad_reduce[...] = jnp.where(odd == 0, rows, swapped).T
    k.grad_dilated[...] = k.from_dilated[...].reshape(9, 64, 128)
    k.grad_expand[...] = k.from_expand[...]
    k.grad_pool[...] = k.from_pool[...]
    k.grad_norm_1[...] = k.norm_1[0:2, :]
    k.grad_norm_2[...] = k.norm_2[0:2, :]
    k.grad_norm_3[...] = k.norm_3[0:2, :]
    for b in range(4):
        k.grad_norm_b[:, b, :] = k.norm_b[0:2, b * 64 : b * 64 + 64]
    k.grad_norm_pool[...] = k.norm_pool[0:2, 0:64]
    k.grad_norm_p[...] = k.norm_p[0:2, 0:64]
    k.grad_head_weight[...] = k.head_sums[0:22, 0:256]
    columns = k.head_sums[:, 256:384].T
    k.grad_head_bias[...] = columns[0:1, 0:22]
    loss = columns[1:2, :]
    task = lax.broadcasted_iota(jnp.int32, (1, 32), 1)

    def total(inside):
        return jnp.sum(jnp.where(inside, loss, 0.0), axis=1, keepdims=True) / counted

    terms = [total(task == 0), total(task == 19), total((task == 20) | (task == 21))]
    lane = lax.broadcasted_iota(jnp.int32, (1, 128), 1)
    losses = jnp.where(lane == 0, terms[0], jnp.where(lane == 1, terms[1], terms[2]))
    log_vars = jnp.where(
        lane == 0, k.log_vars[0], jnp.where(lane == 1, k.log_vars[1], k.log_vars[2])
    )
    weighted = jnp.exp(-log_vars) * losses
    k.total_loss[...] = jnp.sum(
        jnp.where(lane < 3, weighted + log_vars, 0.0), axis=1, keepdims=True
    )
    k.grad_log_vars[...] = (1.0 - weighted)[:, 0:3]

    leave.wait()


def run_finish(args):
    return call_kernel(
        finish,
        "finish",
        None,
        args,
        dict(
            features=((12, 64, 128), BF16),
            total_loss=((1, 1), F32),
            grad_input=((1536, 512), F32),
            grad_reduce=((256, 128), F32),
            grad_dilated=((9, 64, 128), F32),
            grad_expand=((64, 512), F32),
            grad_norm_1=((2, 128), F32),
            grad_norm_2=((2, 128), F32),
            grad_norm_3=((2, 512), F32),
            grad_point=((64, 256), F32),
            grad_rates=((27, 64, 256), F32),
            grad_pool=((64, 256), F32),
            grad_norm_b=((2, 4, 64), F32),
            grad_norm_pool=((2, 64), F32),
            grad_project=((5, 32, 64), F32),
            grad_norm_p=((2, 64), F32),
            grad_head_weight=((22, 256), F32),
            grad_head_bias=((1, 22), F32),
            grad_log_vars=((1, 3), F32),
        ),
        dict(turned=pltpu.VMEM((384, 64), F32), sem=pltpu.SemaphoreType.DMA((1,))),
        0,
        hbm=("grad_input",),
        stream=("from_input", "grad_rates"),
        smem=("boxes", "log_vars"),
    )


def fast_local(
    trunk_input,
    conv_reduce,
    conv_dilated,
    conv_expand,
    reduction_norm_params,
    dilated_norm_params,
    expansion_norm_params,
    aspp_point,
    aspp_rates,
    aspp_pool,
    branch_norms,
    pooling_norm_params,
    aspp_project,
    projection_norm_params,
    head_weight,
    head_bias,
    log_vars,
    crop_boxes,
    seg_labels,
    depth_target,
    normal_target,
):
    x = trunk_input.reshape(1536, 512)
    forward = run_bottleneck(
        dict(
            x=x,
            conv_reduce=conv_reduce,
            w_dilated=conv_dilated,
            w_expand=conv_expand,
            aspp_point=aspp_point,
            aspp_rates=aspp_rates,
            project=aspp_project.transpose(1, 0, 2),
            affine_1=reduction_norm_params,
            affine_2=dilated_norm_params,
            affine_3=expansion_norm_params,
            boxes=crop_boxes,
        )
    )
    w_pyramid = forward.w_pyramid.reshape(13, 256, 512)

    middle = run_pyramid(
        dict(
            trunk=forward.trunk,
            mask=forward.mask,
            w_pyramid=w_pyramid,
            branch_norms=branch_norms,
            norm_project=projection_norm_params,
            norm_pooling=pooling_norm_params,
            aspp_pool=aspp_pool,
            w_slots=forward.w_project,
            head_weight=head_weight.T,
            head_bias=head_bias,
            log_vars=log_vars,
            labels=seg_labels.transpose(1, 0, 2),
            depth=depth_target.transpose(1, 0, 2),
            normal=normal_target.transpose(0, 2, 1, 3).reshape(12, 2, 128),
            boxes=crop_boxes,
        )
    )
    back = run_pyramid_backward(
        dict(
            grad_branches=middle.grad_branches,
            w_pyramid=w_pyramid,
            x=x,
            trunk=forward.trunk,
            expanded=forward.expanded,
            stats_3=forward.stats_3,
            affine_3=expansion_norm_params,
            mask=forward.mask,
            grad_pooled=middle.grad_pooled,
            grad_project=middle.grad_project,
            grad_pool=middle.grad_pool,
            boxes=crop_boxes,
        )
    )
    last = run_bottleneck_backward(
        dict(
            grad_expanded=back.grad_expanded,
            shortcut=back.shortcut,
            w_reduce=forward.w_reduce,
            half_pyramid=back.half_pyramid,
            sum_pyramid=back.sum_pyramid,
            sum_project=back.sum_project,
            x=x,
            hidden=forward.hidden,
            hidden_two=forward.hidden_two,
            w_expand=conv_expand,
            w_dilated=conv_dilated,
            dilated=forward.dilated,
            stats_2=forward.stats_2,
            affine_2=dilated_norm_params,
            reduced=forward.reduced,
            stats_1=forward.stats_1,
            affine_1=reduction_norm_params,
            mask=forward.mask,
            boxes=crop_boxes,
        )
    )
    done = run_finish(
        dict(
            from_input=last.grad_input,
            own_pyramid=last.own_pyramid,
            packed=middle.features,
            own_project=last.own_project,
            own_reduce=last.own_reduce,
            from_dilated=last.sum_dilated,
            from_expand=last.sum_expand,
            from_pool=back.sum_pool,
            norm_1=last.norm_1,
            norm_2=last.norm_2,
            norm_3=back.norm_3,
            norm_b=middle.norm_b,
            norm_pool=middle.norm_pool,
            norm_p=middle.norm_p,
            head_sums=middle.head_sums,
            log_vars=log_vars,
            boxes=crop_boxes,
        )
    )
    return (
        done.features.transpose(0, 2, 1).reshape(1, 12, 128, 64),
        done.total_loss.reshape(()),
        done.grad_input.reshape(1, 12, 128, 512),
        done.grad_reduce,
        done.grad_dilated.reshape(3, 3, 64, 128),
        done.grad_expand,
        done.grad_norm_1,
        done.grad_norm_2,
        done.grad_norm_3,
        done.grad_point,
        done.grad_rates.reshape(3, 3, 3, 64, 256),
        done.grad_pool,
        done.grad_norm_b,
        done.grad_norm_pool,
        done.grad_project.transpose(2, 0, 1),
        done.grad_norm_p,
        done.grad_head_weight.T,
        done.grad_head_bias.reshape(22),
        done.grad_log_vars.reshape(3),
    )


def local(
    trunk_input,
    conv_reduce,
    conv_dilated,
    conv_expand,
    reduction_norm_params,
    dilated_norm_params,
    expansion_norm_params,
    aspp_point,
    aspp_rates,
    aspp_pool,
    branch_norms,
    pooling_norm_params,
    aspp_project,
    projection_norm_params,
    head_weight,
    head_bias,
    log_vars,
    crop_boxes,
    seg_labels,
    depth_target,
    normal_target,
):
    image_inputs, tile_row_count, frame_columns, quarter = trunk_input.shape
    pixels = image_inputs * tile_row_count * frame_columns
    branch_part = aspp_point.shape[0]
    branch_total = lax.axis_size("branch")
    row_portion = 1.0 / lax.axis_size("rows")
    image_overall_count = float(crop_boxes.shape[0])
    first_image = lax.axis_index("batch") * image_inputs
    first_row = lax.axis_index("rows") * tile_row_count
    my_boxes = lax.dynamic_slice_in_dim(crop_boxes, first_image, image_inputs, 0)
    row_ids = first_row + jnp.arange(tile_row_count, dtype=jnp.int32)
    col_ids = jnp.arange(frame_columns, dtype=jnp.int32)
    inside_rows = (row_ids[None, :] >= my_boxes[:, 0:1]) & (
        row_ids[None, :] < my_boxes[:, 0:1] + my_boxes[:, 2:3]
    )
    inside_cols = (col_ids[None, :] >= my_boxes[:, 1:2]) & (
        col_ids[None, :] < my_boxes[:, 1:2] + my_boxes[:, 3:4]
    )
    valid_mask = (inside_rows[:, :, None] & inside_cols[:, None, :]).astype(jnp.float32)
    mask_column_vector = valid_mask.reshape(pixels, 1)
    mask_flat = valid_mask.reshape(pixels)
    pixel_number_count = jnp.sum((crop_boxes[:, 2] * crop_boxes[:, 3]).astype(jnp.float32))
    image_areas = (my_boxes[:, 2] * my_boxes[:, 3]).astype(jnp.float32)
    input_full = widen(trunk_input)
    reduced_output = forward_dot(input_full, conv_reduce).reshape(pixels, -1)
    normalized_first, standardized_first, inverse_deviation_first = norm_ahead_pass(
        reduced_output, mask_column_vector, pixel_number_count, reduction_norm_params
    )
    hidden_one = (
        jax.nn.silu(normalized_first)
        .astype(jnp.bfloat16)
        .reshape(image_inputs, tile_row_count, frame_columns, -1)
    )
    hidden_full = widen(pad_rows(hidden_one))
    dilated_out = 0.0
    for row_tap in range(3):
        band = hidden_full[:, 4 * row_tap : 4 * row_tap + tile_row_count]
        for col_tap in range(3):
            dilated_out = dilated_out + forward_dot(
                move(band, -(col_tap - 1) * 4, 2), conv_dilated[row_tap, col_tap]
            )
    normalized_second, standardized_second, inverse_deviation_second = norm_ahead_pass(
        dilated_out.reshape(pixels, -1), mask_column_vector, pixel_number_count, dilated_norm_params
    )
    hidden_two = (
        jax.nn.silu(normalized_second)
        .astype(jnp.bfloat16)
        .reshape(image_inputs, tile_row_count, frame_columns, -1)
    )
    hidden_two_full = widen(hidden_two)
    expanded_output = forward_dot(hidden_two_full, conv_expand).reshape(pixels, -1)
    normalized_third, standardized_third, inverse_deviation_third = norm_ahead_pass(
        expanded_output, mask_column_vector, pixel_number_count, expansion_norm_params
    )
    residual_sum = normalized_third + trunk_input.reshape(pixels, -1).astype(jnp.float32)
    trunk_out = (
        jax.nn.silu(residual_sum)
        .astype(jnp.bfloat16)
        .reshape(image_inputs, tile_row_count, frame_columns, quarter)
    )
    trunk_full = widen(trunk_out)
    branch_outs = [backward_dot(trunk_full, aspp_point)]
    for branch_id in range(3):
        dilation = RATES[branch_id]
        hops = dilation // tile_row_count
        partials = [0.0, 0.0, 0.0]
        for col_tap in range(3):
            shifted = move(trunk_full, -(col_tap - 1) * dilation, 2)
            products = backward_dot(shifted, stacked_taps(aspp_rates[branch_id], col_tap))
            for row_tap in range(3):
                partials[row_tap] = (
                    partials[row_tap]
                    + products[..., row_tap * branch_part : (row_tap + 1) * branch_part]
                )
        upper = send_down(partials[0].astype(jnp.bfloat16), hops).astype(jnp.float32)
        lower_part = send_up(partials[2].astype(jnp.bfloat16), hops).astype(jnp.float32)
        branch_outs.append(partials[1] + upper + lower_part)
    spatial_flattened = jnp.stack(branch_outs, axis=3).reshape(pixels, -1)
    branch_gain_bias = branch_norms.reshape(2, -1)
    normalized_spatial, standardized_spatial, inverse_deviation_spatial = norm_ahead_pass(
        spatial_flattened, mask_column_vector, pixel_number_count, branch_gain_bias
    )
    spatial_act = (
        jax.nn.silu(normalized_spatial)
        .astype(jnp.bfloat16)
        .reshape(image_inputs, tile_row_count, frame_columns, 4, branch_part)
    )
    pooled_local = lax.dot_general(
        valid_mask.astype(jnp.bfloat16),
        trunk_full,
        (((1, 2), (1, 2)), ((0,), (0,))),
        preferred_element_type=jnp.float32,
    )
    pooled = (over_rows(pooled_local) / image_areas[:, None]).astype(jnp.bfloat16)
    pooling_convolution = backward_dot(pooled, aspp_pool)
    normalized_poolbranch, standardized_poolbranch, inverse_deviation_poolbranch = norm_ahead_pass(
        pooling_convolution, row_portion, image_overall_count, pooling_norm_params
    )
    pool_act = jax.nn.silu(normalized_poolbranch).astype(jnp.bfloat16)
    pool_wide = jnp.broadcast_to(
        pool_act[:, None, None, None, :],
        (image_inputs, tile_row_count, frame_columns, 1, branch_part),
    )
    concat = jnp.concatenate([spatial_act, pool_wide], axis=3)
    concat_flat = widen(concat).reshape(pixels, -1)
    proj_kernel = (
        aspp_project.reshape(branch_part, 5, branch_total, branch_part)
        .transpose(0, 2, 1, 3)
        .reshape(branch_part, 5 * branch_total * branch_part)
    )
    projected_output = backward_dot(concat_flat, proj_kernel)
    normalized_projector, standardized_projector, inverse_deviation_projector = norm_ahead_pass(
        projected_output, mask_column_vector, pixel_number_count, projection_norm_params
    )
    features = (
        jax.nn.silu(normalized_projector)
        .astype(jnp.bfloat16)
        .reshape(image_inputs, tile_row_count, frame_columns, -1)
    )
    features_wide = widen(features).reshape(pixels, -1).astype(jnp.float32)
    head_wide = head_weight.astype(jnp.float32)
    logits = jnp.dot(features_wide, head_wide, precision=HIGH) + head_bias
    classes = head_bias.shape[0] - 3
    seg_logits = logits[:, :classes]
    labels_flat = seg_labels.reshape(pixels)
    classes_hot = (labels_flat[:, None] == jnp.arange(classes, dtype=jnp.int32)[None, :]).astype(
        jnp.float32
    )
    cross = jax.nn.logsumexp(seg_logits, axis=1) - jnp.sum(seg_logits * classes_hot, axis=1)
    depth_gap = logits[:, classes] - depth_target.reshape(pixels)
    smooth_abs = jnp.sqrt(depth_gap * depth_gap + 1.0)
    normal_gap = logits[:, classes + 1 :] - jnp.moveaxis(normal_target, 1, 3).reshape(pixels, 2)
    local_losses = jnp.stack(
        [
            jnp.sum(mask_flat * cross),
            jnp.sum(mask_flat * (smooth_abs - 1.0)),
            jnp.sum(mask_flat * jnp.sum(normal_gap * normal_gap, axis=1)),
        ]
    )
    task_weights = jnp.exp(-log_vars)
    grad_seg = (jax.nn.softmax(seg_logits, axis=1) - classes_hot) * (
        task_weights[0] / pixel_number_count * mask_flat
    )[:, None]
    grad_depth = depth_gap / smooth_abs * (task_weights[1] / pixel_number_count * mask_flat)
    grad_normal = 2.0 * normal_gap * (task_weights[2] / pixel_number_count * mask_flat)[:, None]
    grad_logits = jnp.concatenate([grad_seg, grad_depth[:, None], grad_normal], axis=1)
    head_local = lax.dot_general(
        features_wide, grad_logits, (((0,), (0,)), ((), ())), precision=HIGH
    )
    loss_parts, grad_head_weight, grad_head_bias = lax.psum(
        (local_losses, head_local, jnp.sum(grad_logits, axis=0)), ("rows", "batch")
    )
    task_losses = loss_parts / pixel_number_count
    total_loss = jnp.sum(task_weights * task_losses + log_vars)
    grad_log_vars = 1.0 - task_weights * task_losses
    grad_features = jnp.dot(grad_logits, head_wide.T, precision=HIGH)
    my_features_grad = lax.dynamic_slice_in_dim(
        grad_features, lax.axis_index("branch") * branch_part, branch_part, 1
    )
    gradient_before_projector = my_features_grad * silu_slope(normalized_projector)
    grad_proj_in, grad_project_norm = norm_reverse_pass(
        gradient_before_projector,
        standardized_projector,
        inverse_deviation_projector,
        1.0,
        mask_column_vector,
        pixel_number_count,
        projection_norm_params,
    )
    grad_proj_low = grad_proj_in.astype(jnp.bfloat16)
    proj_kernel_grad = lax.dot_general(
        grad_proj_low, concat_flat, (((0,), (0,)), ((), ())), preferred_element_type=jnp.float32
    )
    grad_project_local = (
        proj_kernel_grad.reshape(branch_part, branch_total, 5, branch_part)
        .transpose(0, 2, 1, 3)
        .reshape(branch_part, 5, branch_total * branch_part)
    )
    concat_grad = forward_dot(grad_proj_low, proj_kernel).reshape(
        image_inputs, tile_row_count, frame_columns, -1
    )
    concat_grad = narrow(concat_grad).reshape(pixels, 5, branch_part)
    pool_grad_img = over_rows(
        jnp.sum(concat_grad[:, 4, :].reshape(image_inputs, -1, branch_part), axis=1)
    )
    gradient_before_poolbranch = pool_grad_img * silu_slope(normalized_poolbranch)
    grad_pool_conv, grad_pool_norm = norm_reverse_pass(
        gradient_before_poolbranch,
        standardized_poolbranch,
        inverse_deviation_poolbranch,
        row_portion,
        1.0,
        image_overall_count,
        pooling_norm_params,
    )
    pool_conv_low = grad_pool_conv.astype(jnp.bfloat16)
    grad_pool_local = (
        lax.dot_general(
            pool_conv_low, pooled, (((0,), (0,)), ((), ())), preferred_element_type=jnp.float32
        )
        * row_portion
    )
    pooled_grad = forward_dot(pool_conv_low, aspp_pool)
    gradient_before_spatialbranch = concat_grad[:, :4, :].reshape(pixels, -1) * silu_slope(
        normalized_spatial
    )
    grad_spatial, branch_norm_grad = norm_reverse_pass(
        gradient_before_spatialbranch,
        standardized_spatial,
        inverse_deviation_spatial,
        1.0,
        mask_column_vector,
        pixel_number_count,
        branch_gain_bias,
    )
    grad_branch_norms = branch_norm_grad.reshape(2, 4, branch_part)
    spatial_low = grad_spatial.astype(jnp.bfloat16).reshape(
        image_inputs, tile_row_count, frame_columns, 4, branch_part
    )
    point_grad = spatial_low[:, :, :, 0]
    grad_point_local = pixel_dot(point_grad, trunk_full)
    trunk_grad = forward_dot(point_grad, aspp_point)
    trunk_grad = (
        trunk_grad + valid_mask[..., None] * (pooled_grad / image_areas[:, None])[:, None, None, :]
    )
    rate_grads = []
    for branch_id in range(3):
        dilation = RATES[branch_id]
        hops = dilation // tile_row_count
        centre = spatial_low[:, :, :, branch_id + 1]
        grad_taps = jnp.concatenate(
            [send_up(centre, hops), centre, send_down(centre, hops)], axis=3
        )
        per_col = []
        for col_tap in range(3):
            shifted = move(trunk_full, -(col_tap - 1) * dilation, 2)
            per_col.append(pixel_dot(grad_taps, shifted))
            tap_grad = forward_dot(grad_taps, stacked_taps(aspp_rates[branch_id], col_tap))
            trunk_grad = trunk_grad + move(tap_grad, (col_tap - 1) * dilation, 2)
        col_stack = jnp.stack(per_col, axis=0).reshape(3, 3, branch_part, -1)
        rate_grads.append(col_stack.transpose(1, 0, 2, 3))
    grad_rates_local = jnp.stack(rate_grads, axis=0)
    trunk_own = narrow(trunk_grad).reshape(pixels, -1)
    gradient_shortcut = trunk_own * silu_slope(residual_sum)
    grad_expanded, grad_norm_expand = norm_reverse_pass(
        gradient_shortcut,
        standardized_third,
        inverse_deviation_third,
        1.0,
        mask_column_vector,
        pixel_number_count,
        expansion_norm_params,
    )
    expanded_low = grad_expanded.astype(jnp.bfloat16).reshape(
        image_inputs, tile_row_count, frame_columns, -1
    )
    grad_expand_local = pixel_dot(hidden_two_full, expanded_low)
    hidden_two_grad = narrow(backward_dot(expanded_low, conv_expand)).reshape(pixels, -1)
    gradient_before_second = hidden_two_grad * silu_slope(normalized_second)
    gradient_dilated_input, gradient_dilated_norm = norm_reverse_pass(
        gradient_before_second,
        standardized_second,
        inverse_deviation_second,
        1.0,
        mask_column_vector,
        pixel_number_count,
        dilated_norm_params,
    )
    dilated_lowprec = gradient_dilated_input.astype(jnp.bfloat16).reshape(
        image_inputs, tile_row_count, frame_columns, -1
    )
    dilated_padded = pad_rows(dilated_lowprec)
    hidden_one_grad = 0.0
    kernel_grads = []
    for row_tap in range(3):
        band = hidden_full[:, 4 * row_tap : 4 * row_tap + tile_row_count]
        grad_band = dilated_padded[:, 8 - 4 * row_tap : 8 - 4 * row_tap + tile_row_count]
        for col_tap in range(3):
            kernel_grads.append(pixel_dot(move(band, -(col_tap - 1) * 4, 2), dilated_lowprec))
            hidden_one_grad = hidden_one_grad + backward_dot(
                move(grad_band, (col_tap - 1) * 4, 2), conv_dilated[row_tap, col_tap]
            )
    grad_dilated_local = jnp.stack(kernel_grads, axis=0).reshape(3, 3, hidden_full.shape[3], -1)
    hidden_one_own = narrow(hidden_one_grad).reshape(pixels, -1)
    gradient_before_first = hidden_one_own * silu_slope(normalized_first)
    grad_reduced, grad_norm_reduce = norm_reverse_pass(
        gradient_before_first,
        standardized_first,
        inverse_deviation_first,
        1.0,
        mask_column_vector,
        pixel_number_count,
        reduction_norm_params,
    )
    reduced_low = grad_reduced.astype(jnp.bfloat16).reshape(
        image_inputs, tile_row_count, frame_columns, -1
    )
    grad_reduce_local = pixel_dot(input_full, reduced_low)
    input_grad = narrow(backward_dot(reduced_low, conv_reduce))
    grad_input = input_grad + gradient_shortcut.reshape(
        image_inputs, tile_row_count, frame_columns, quarter
    )
    grad_reduce, grad_dilated, grad_expand, grad_point, grad_rates, grad_pool, grad_project = (
        lax.psum_scatter(grad_reduce_local, ("rows", "batch"), scatter_dimension=0, tiled=True),
        lax.psum_scatter(grad_dilated_local, ("rows", "batch"), scatter_dimension=2, tiled=True),
        lax.psum_scatter(grad_expand_local, ("rows", "batch"), scatter_dimension=0, tiled=True),
        lax.psum_scatter(grad_point_local, ("rows", "batch"), scatter_dimension=1, tiled=True),
        lax.psum_scatter(grad_rates_local, ("rows", "batch"), scatter_dimension=4, tiled=True),
        lax.psum_scatter(grad_pool_local, ("rows", "batch"), scatter_dimension=1, tiled=True),
        lax.psum_scatter(grad_project_local, ("rows", "batch"), scatter_dimension=2, tiled=True),
    )
    return (
        features,
        total_loss,
        grad_input,
        grad_reduce,
        grad_dilated,
        grad_expand,
        grad_norm_reduce,
        gradient_dilated_norm,
        grad_norm_expand,
        grad_point,
        grad_rates,
        grad_pool,
        grad_branch_norms,
        grad_pool_norm,
        grad_project,
        grad_project_norm,
        grad_head_weight,
        grad_head_bias,
        grad_log_vars,
    )


def solution(mesh):
    in_specs = (
        P("batch", "rows", None, "branch"),
        P(None, "branch"),
        P(None, None, None, "branch"),
        P(None, "branch"),
        P(None, "branch"),
        P(None, "branch"),
        P(None, "branch"),
        P("branch", None),
        P(None, None, None, "branch", None),
        P("branch", None),
        P(None, None, "branch"),
        P(None, "branch"),
        P("branch", None, None),
        P(None, "branch"),
        P(),
        P(),
        P(),
        P(),
        P("batch", "rows", None),
        P("batch", "rows", None),
        P("batch", None, "rows", None),
    )
    out_specs = (
        P("batch", "rows", None, "branch"),
        P(),
        P("batch", "rows", None, "branch"),
        P(("rows", "batch"), "branch"),
        P(None, None, ("rows", "batch"), "branch"),
        P(("rows", "batch"), "branch"),
        P(None, "branch"),
        P(None, "branch"),
        P(None, "branch"),
        P("branch", ("rows", "batch")),
        P(None, None, None, "branch", ("rows", "batch")),
        P("branch", ("rows", "batch")),
        P(None, None, "branch"),
        P(None, "branch"),
        P("branch", None, ("rows", "batch")),
        P(None, "branch"),
        P(),
        P(),
        P(),
    )
    small = (mesh.shape["branch"], mesh.shape["rows"], mesh.shape["batch"]) == (4, 2, 4)
    body = fast_local if small else local
    return jax.shard_map(body, mesh=mesh, in_specs=in_specs, out_specs=out_specs, check_vma=False)
```

```python
import types

import jax
import jax.numpy as jnp
from jax import lax
from jax.experimental import pallas as pl
from jax.experimental.pallas import tpu as pltpu
from jax.sharding import PartitionSpec as P

EPS = 1e-05
HIGH = lax.Precision.HIGHEST
RATES = (12, 24, 36)


def padded(cells, sides, width):
    for axis, dim in sides:
        count = lax.axis_size(axis)
        ends = count - 1
        head = lax.slice_in_dim(cells, 0, width, axis=dim)
        tail = lax.slice_in_dim(cells, cells.shape[dim] - width, cells.shape[dim], axis=dim)
        cells = jnp.concatenate(
            [
                lax.ppermute(tail, axis, [(i, (i + 1) % count) for i in range(ends)]),
                cells,
                lax.ppermute(head, axis, [((i + 1) % count, i) for i in range(ends)]),
            ],
            axis=dim,
        )
    return cells


def shifted_2(block, axis, distance):
    devices = range(lax.axis_size(axis))
    route = [(i - distance, i) for i in devices if i - distance in devices]
    return lax.ppermute(block, axis, route)


def move(tensor, offset, axis_id):
    length = tensor.shape[axis_id]
    if offset == 0:
        return tensor
    widths = [(0, 0)] * tensor.ndim
    if offset > 0:
        widths[axis_id] = (offset, 0)
        return lax.slice_in_dim(jnp.pad(tensor, widths), 0, length, axis=axis_id)
    widths[axis_id] = (0, -offset)
    return lax.slice_in_dim(jnp.pad(tensor, widths), -offset, length - offset, axis=axis_id)


def forward_dot(lhs_arr, rhs_arr):
    return jnp.dot(lhs_arr, rhs_arr, preferred_element_type=jnp.float32)


def backward_dot(grad_arr, kernel):
    return lax.dot_general(
        grad_arr,
        kernel,
        (((grad_arr.ndim - 1,), (1,)), ((), ())),
        preferred_element_type=jnp.float32,
    )


def pixel_dot(source, grad_arr):
    return lax.dot_general(
        source, grad_arr, (((0, 1, 2), (0, 1, 2)), ((), ())), preferred_element_type=jnp.float32
    )


def silu_slope(pre_act):
    sigmoid_v = jax.nn.sigmoid(pre_act)
    return sigmoid_v * (1.0 + pre_act * (1.0 - sigmoid_v))


def widen(tensor):
    return lax.all_gather(tensor, "branch", axis=3, tiled=True)


def narrow(tensor):
    return lax.psum_scatter(
        tensor.astype(jnp.bfloat16), "branch", scatter_dimension=3, tiled=True
    ).astype(jnp.float32)


def pad_rows(tensor):
    return padded(tensor, (("rows", 1),), 4)


def send_down(tensor, hops):
    if hops >= lax.axis_size("rows"):
        return jnp.zeros_like(tensor)
    return shifted_2(tensor, "rows", hops)


def send_up(tensor, hops):
    if hops >= lax.axis_size("rows"):
        return jnp.zeros_like(tensor)
    return shifted_2(tensor, "rows", -hops)


def over_rows(tensor):
    return lax.psum(tensor, "rows")


def norm_ahead_pass(tensor, weight, counted, affine):
    summed = lax.psum(jnp.sum(tensor * weight, axis=0), ("rows", "batch"))
    mean_val = summed / counted
    centered = tensor - mean_val
    spread = lax.psum(jnp.sum(weight * centered * centered, axis=0), ("rows", "batch"))
    variance = spread / counted
    inverse = lax.rsqrt(variance + EPS)
    normed = centered * inverse
    return (affine[0] * normed + affine[1], normed, inverse)


def norm_reverse_pass(grad_out, normed, inverse, weight_all, weight_stat, counted, affine):
    grad_bias, grad_gain = lax.psum(
        (jnp.sum(grad_out * weight_all, axis=0), jnp.sum(grad_out * normed * weight_all, axis=0)),
        ("rows", "batch"),
    )
    gain_row = affine[0]
    grad_in = inverse * (
        gain_row * grad_out - weight_stat / counted * gain_row * (grad_bias + normed * grad_gain)
    )
    return (grad_in, jnp.stack([grad_gain, grad_bias]))


def stacked_taps(kernels, col_tap):
    return jnp.concatenate([kernels[0, col_tap], kernels[1, col_tap], kernels[2, col_tap]], axis=0)


MESH = pl.DeviceIdType.MESH
F32 = jnp.float32
BF16 = jnp.bfloat16
VMEM_LIMIT = 60 * 2**20


class Net:
    def __init__(self, send_sems, recv_sems):
        self.m = lax.axis_index("branch")
        self.r = lax.axis_index("rows")
        self.z = lax.axis_index("batch")
        self.send_sems, self.recv_sems, self.count = send_sems, recv_sems, 0
        self.side = (self.m ^ 1, self.r, self.z)
        self.over = (self.m ^ 2, self.r, self.z)
        self.diagonal = (self.m ^ 3, self.r, self.z)
        self.core = (self.m, 1 - self.r, self.z)
        self.slot = self.r * 4 + self.z
        self.group = [
            (self.m, lax.rem(self.r + i, 2), lax.rem(self.z + j, 4))
            for i in range(2)
            for j in range(4)
            if i or j
        ]

    def send(self, src, dst, device):
        i = self.count
        self.count += 1
        copy = pltpu.make_async_remote_copy(
            src_ref=src,
            dst_ref=dst,
            send_sem=self.send_sems.at[i],
            recv_sem=self.recv_sems.at[i],
            device_id=device,
            device_id_type=MESH,
        )
        copy.start()
        return copy


def greet(peers, perhaps=()):
    barrier = pltpu.get_barrier_semaphore()
    for peer in peers:
        pl.semaphore_signal(barrier, inc=1, device_id=peer, device_id_type=MESH)
    awaited = len(peers)
    for peer, there in perhaps:

        @pl.when(there)
        def _(peer=peer):
            pl.semaphore_signal(barrier, inc=1, device_id=peer, device_id_type=MESH)

        awaited = awaited + there.astype(jnp.int32)
    pl.semaphore_wait(barrier, awaited)


def each_rows(total, step, body):
    def run(i, carry):
        body(pl.ds(pl.multiple_of(i * step, step), step))
        return carry

    lax.fori_loop(0, total // step, run, 0)


def lane_block(index, width=128):
    return pl.ds(pl.multiple_of(index * width, width), width)


def wide(tile, width):
    count = width // tile.shape[1]
    return tile if count == 1 else jnp.concatenate([tile] * count, axis=1)


def column_sums(fn, total, width, number):
    step = 16384 // width

    def run(i, sums):
        terms = fn(pl.ds(pl.multiple_of(i * step, step), step))
        return tuple(
            s + jnp.sum(t.reshape(step // 8, 8, width), axis=0) for s, t in zip(sums, terms)
        )

    sums = lax.fori_loop(
        0, total // step, run, tuple(jnp.zeros((8, width), F32) for _ in range(number))
    )
    return [jnp.sum(s, axis=0, keepdims=True) for s in sums]


def fold(row):
    return row + pltpu.roll(wide(row, 128), 64, 1)


def exchange(net, outgoing, incoming, meanwhile=None):
    copies = [net.send(outgoing, incoming.at[net.slot], peer) for peer in net.group]
    incoming[net.slot] = outgoing[...]
    if meanwhile is not None:
        meanwhile()
    for copy in copies:
        copy.wait()


def pack(outgoing, first, second, extra=None):
    for i in range(first.shape[1] // 128):
        outgoing[2 * i : 2 * i + 1, :] = first[:, i * 128 : i * 128 + 128]
        outgoing[2 * i + 1 : 2 * i + 2, :] = second[:, i * 128 : i * 128 + 128]
    if extra is not None:
        outgoing[4:5, :] = extra


def unpack(incoming, width):
    count = width // 128
    firsts = [incoming[:, 2 * i, :] for i in range(count)]
    seconds = [incoming[:, 2 * i + 1, :] for i in range(count)]
    return jnp.concatenate(firsts, axis=1), jnp.concatenate(seconds, axis=1)


def statistics(
    net, value_ref, mask_ref, counts, outgoing, incoming, counted, folded=False, extra=None
):
    total, width = value_ref.shape
    same = fold if folded else (lambda row: row)
    (first,) = column_sums(
        lambda at: (value_ref[at, :] * wide(mask_ref[at, :], width),), total, width, 1
    )
    first = same(first)
    own = jnp.sum(jnp.where(lax.broadcasted_iota(jnp.int32, (8, 128), 0) == net.slot, counts, 0.0), axis=0, keepdims=True)
    centre = first / jnp.maximum(wide(own, width), 1.0)

    def squares(at):
        gap = value_ref[at, :] - centre
        return (gap * gap * wide(mask_ref[at, :], width),)

    second = same(column_sums(squares, total, width, 1)[0])
    pack(outgoing, first, second, extra)
    exchange(net, outgoing, incoming)
    firsts, seconds = unpack(incoming, width)
    numbers = wide(counts, width)
    mean = jnp.sum(firsts, axis=0, keepdims=True) / counted
    drift = firsts / jnp.maximum(numbers, 1.0) - mean
    variance = jnp.sum(seconds + numbers * drift * drift, axis=0, keepdims=True) / counted
    return mean, lax.rsqrt(variance + EPS)


def gather_blocks(net, part, rows, meanwhile=None):
    pieces, size = 4, rows // 4
    own, side, over = net.m, net.m ^ 1, net.m ^ 2

    def at(i):
        return pl.ds(i * size, size)

    to_side, to_over = [], []
    for i in range(pieces):
        j = pieces - 1 - i
        to_side.append(net.send(part(own, at(i)), part(own, at(i)), net.side))
        to_over.append(net.send(part(own, at(j)), part(own, at(j)), net.over))
    passed = []
    for i in range(pieces):
        j = pieces - 1 - i
        to_side[i].wait_recv()
        if i < pieces // 2:
            passed.append(net.send(part(side, at(i)), part(side, at(i)), net.over))
        to_over[i].wait_recv()
        if i < pieces // 2:
            passed.append(net.send(part(over, at(j)), part(over, at(j)), net.side))
    if meanwhile is not None:
        meanwhile()
    for copy in to_side + to_over:
        copy.wait_send()
    for copy in passed:
        copy.wait()


def sum_scatter(net, part, bufs, out, meanwhile=None, produce=None):
    far, to_side, to_over, far_side, far_over, from_side, from_over = bufs
    rows, width = out.shape
    half, step = rows // 2, 16384 // width
    head, tail = pl.ds(0, half), pl.ds(half, half)
    across, side, over = net.m ^ 3, net.m ^ 1, net.m ^ 2

    def fill(target, index, base):
        def body(at):
            rows_at = pl.ds(pl.multiple_of(at.start + base, step), step)
            target[rows_at, :] = part[index, rows_at, :].astype(BF16)

        each_rows(half, step, body)

    def combine(target, index, base, arrived):
        def body(at):
            rows_at = pl.ds(pl.multiple_of(at.start + base, step), step)
            target[rows_at, :] = (part[index, rows_at, :] + arrived[at, :].astype(F32)).astype(BF16)

        each_rows(half, step, body)

    if produce is not None:
        produce(0)
    fill(far, across, 0)
    first = net.send(far.at[head], far_side, net.side)
    if produce is not None:
        produce(1)
    fill(far, across, half)
    second = net.send(far.at[tail], far_over, net.over)
    fill(to_side, side, 0)
    third = net.send(to_side.at[head], from_side.at[head], net.side)
    fill(to_over, over, half)
    fourth = net.send(to_over.at[tail], from_over.at[tail], net.over)
    second.wait_recv()
    combine(to_side, side, half, far_over)
    fifth = net.send(to_side.at[tail], from_side.at[tail], net.side)
    first.wait_recv()
    combine(to_over, over, 0, far_side)
    sixth = net.send(to_over.at[head], from_over.at[head], net.over)
    if meanwhile is not None:
        meanwhile()
    for copy in (third, fourth, fifth, sixth):
        copy.wait_recv()

    def body(at):
        out[at, :] = (
            part[net.m, at, :] + from_side[at, :].astype(F32) + from_over[at, :].astype(F32)
        )

    each_rows(rows, step, body)
    for copy in (first, second, third, fourth, fifth, sixth):
        copy.wait_send()


def gradient_sums(
    net, grad_ref, normed, outgoing, incoming, folded=False, extra=None, meanwhile=None
):
    total, width = grad_ref.shape
    same = fold if folded else (lambda row: row)
    bias, gain = column_sums(
        lambda at: (grad_ref[at, :], grad_ref[at, :] * normed(at)), total, width, 2
    )
    pack(outgoing, same(bias), same(gain), extra)
    exchange(net, outgoing, incoming, meanwhile)
    biases, gains = unpack(incoming, width)
    return jnp.sum(biases, axis=0, keepdims=True), jnp.sum(gains, axis=0, keepdims=True)


def keep_rows(ref, first, second):
    width = ref.shape[1]
    ref[0:1, :] = first
    ref[1:2, :] = second
    ref[2:8, :] = jnp.zeros((6, width), F32)


def pair(a, b):
    low = lax.broadcasted_iota(jnp.int32, (a.shape[0], 128), 1) < 64
    results = []
    for g in range(2):
        left, right = a[:, g * 128 : g * 128 + 128], b[:, g * 128 : g * 128 + 128]
        results.append(jnp.where(low, left, pltpu.roll(right, 64, 1)))
        results.append(jnp.where(low, pltpu.roll(left, 64, 1), right))
    return results


def unpair(blocks):
    low = lax.broadcasted_iota(jnp.int32, blocks[0].shape, 1) < 64
    firsts, seconds = [], []
    for g in range(2):
        left, right = blocks[2 * g], blocks[2 * g + 1]
        firsts.append(jnp.where(low, left, pltpu.roll(right, 64, 1)))
        seconds.append(jnp.where(low, pltpu.roll(left, 64, 1), right))
    return jnp.concatenate(firsts, axis=1), jnp.concatenate(seconds, axis=1)


def split_three(row):
    high = row.astype(BF16)
    rest = row - high.astype(F32)
    middle = rest.astype(BF16)
    low = (rest - middle.astype(F32)).astype(BF16)
    return high, middle, low


def zero_margins(ref, side, width):
    rows, _, lanes = ref.shape
    ref[:, 0:side, :] = jnp.zeros((rows, side, lanes), F32)
    ref[:, side + width : 2 * side + width, :] = jnp.zeros((rows, side, lanes), F32)


def scatter_buffers(rows, width):
    whole, half = pltpu.VMEM((rows, width), BF16), pltpu.VMEM((rows // 2, width), BF16)
    return [whole, whole, whole, half, half, whole, whole]


def sigmoid(u):
    return 0.5 * jnp.tanh(0.5 * u) + 0.5


def slope(u):
    s = sigmoid(u)
    return s * (1.0 + u * (1.0 - s))


def mm(a, b):
    return jnp.dot(a, b, preferred_element_type=F32)


def mm_t(a, b):
    return lax.dot_general(a, b, (((1,), (1,)), ((), ())), preferred_element_type=F32)


def tm_m(a, b):
    return lax.dot_general(a, b, (((0,), (0,)), ((), ())), preferred_element_type=F32)


class Streams:
    def __init__(self, ins, outs, sems):
        self.ins = {n: pltpu.make_async_copy(*pair, sems.at[i]) for i, (n, pair) in enumerate(ins)}
        self.outs = {
            n: pltpu.make_async_copy(*pair, sems.at[len(ins) + i])
            for i, (n, pair) in enumerate(outs)
        }
        self.left = []
        for copy in self.ins.values():
            copy.start()

    def need(self, **names):
        for name in names:
            self.ins.pop(name).wait()

    def done(self, **names):
        for name in names:
            copy = self.outs.pop(name)
            copy.start()
            self.left.append(copy)

    def finish(self):
        self.need(**dict.fromkeys(self.ins))
        self.done(**dict.fromkeys(self.outs))
        for copy in self.left:
            copy.wait()


def call_kernel(
    body, name, number, args, outs, scratch, sems, hbm={}, smem=dict(boxes=1), stream={}
):
    vmem, anywhere = pl.BlockSpec(memory_space=pltpu.VMEM), pl.BlockSpec(memory_space=pl.ANY)
    stream_in = [n for n in args if n in stream]
    stream_out = [n for n in outs if n in stream]
    buffers = {n: pltpu.VMEM(args[n].shape, args[n].dtype) for n in stream_in}
    buffers.update({n: pltpu.VMEM(*outs[n]) for n in stream_out})
    names = [f"far_{n}" if n in stream else n for n in [*args, *outs]]
    names = [*names, *scratch, *buffers, "stream_sems"]
    places = {name: anywhere for name in [*hbm, *stream]}
    places.update({name: pl.BlockSpec(memory_space=pltpu.SMEM) for name in smem})

    def kernel(*refs):
        k = types.SimpleNamespace(**dict(zip(names, refs)))
        held = vars(k)
        k.stream = Streams(
            [(n, (held[f"far_{n}"], held[n])) for n in stream_in],
            [(n, (held[n], held[f"far_{n}"])) for n in stream_out],
            k.stream_sems,
        )
        body(Net(refs[-2], refs[-1]) if sems else None, k)
        k.stream.finish()

    results = pl.pallas_call(
        kernel,
        out_shape=[jax.ShapeDtypeStruct(s, d) for s, d in outs.values()],
        in_specs=[places.get(name, vmem) for name in args],
        out_specs=[places.get(name, vmem) for name in outs],
        scratch_shapes=[
            *scratch.values(),
            *buffers.values(),
            pltpu.SemaphoreType.DMA((max(len(buffers), 1),)),
            *([pltpu.SemaphoreType.DMA((sems,))] * (2 if sems else 0)),
        ],
        name=name,
        compiler_params=pltpu.CompilerParams(
            collective_id=number, has_side_effects=bool(sems), vmem_limit_bytes=VMEM_LIMIT
        ),
    )(*args.values())
    return types.SimpleNamespace(**dict(zip(outs, results)))


def pixel_count(boxes):
    total = boxes[0, 2] * boxes[0, 3]
    for b in range(1, 4):
        total = total + boxes[b, 2] * boxes[b, 3]
    return total.astype(F32)


def tile_counts(net, boxes):
    slot = lax.broadcasted_iota(jnp.int32, (8, 128), 0)
    result = jnp.zeros((8, 128), F32)
    for s in range(8):
        top, height, width = boxes[s % 4, 0], boxes[s % 4, 2], boxes[s % 4, 3]
        first, last = (s // 4) * 12, (s // 4) * 12 + 12
        rows = jnp.minimum(top + height, last) - jnp.maximum(top, first)
        result = jnp.where(slot == s, (jnp.maximum(rows, 0) * width).astype(F32), result)
    return result


def exchange_scratch(label):
    return {
        f"out_{label}": pltpu.VMEM((8, 128), F32),
        f"in_{label}": pltpu.VMEM((8, 8, 128), F32),
    }


def scatter_scratch(label, rows, width):
    return {f"{label}_{i}": b for i, b in enumerate(scatter_buffers(rows, width))}


def scatter_refs(k, label):
    return [getattr(k, f"{label}_{i}") for i in range(7)]


def load_taps(k):
    loads = []
    for i in range(3):
        for j in range(3):
            loads.append(
                pltpu.make_async_copy(
                    k.w_dilated.at[i, j],
                    k.w_taps.at[i, :, pl.ds(j * 128, 128)],
                    k.local_sems.at[i * 3 + j],
                )
            )
            loads[-1].start()
    return loads


def send_halo(net, padded):
    lanes = padded.shape[1]
    padded[pl.ds(pl.multiple_of(net.r * 2048, 128), 512), :] = jnp.zeros((512, lanes), BF16)
    return net.send(
        padded.at[pl.ds(pl.multiple_of(1536 - net.r * 1024, 128), 512)],
        padded.at[pl.ds(pl.multiple_of(net.r * 2048, 128), 512)],
        net.core,
    )


def bottleneck_forward(net, k):
    counted, counts = pixel_count(k.boxes), tile_counts(net, k.boxes)
    loads = load_taps(k)
    own_reduce = pltpu.make_async_copy(
        k.conv_reduce.at[lane_block(net.m, 512)], k.w_reduce.at[net.m], k.local_sems.at[9]
    )
    own_reduce.start()
    greet([net.side, net.over, net.diagonal] + net.group)
    branches = [(net.m ^ 3, net.diagonal), (net.m ^ 1, net.side), (net.m ^ 2, net.over)]
    arrivals = [
        net.send(k.conv_reduce.at[lane_block(b, 512)], k.w_reduce.at[net.m], peer)
        for b, peer in branches
    ]

    top, left_edge = k.boxes[net.z, 0], k.boxes[net.z, 1]
    bottom, right_edge = top + k.boxes[net.z, 2], left_edge + k.boxes[net.z, 3]
    column = lax.broadcasted_iota(jnp.int32, (128, 128), 0)
    column_inside = jnp.where((column >= left_edge) & (column < right_edge), 1.0, 0.0)

    def mask_rows(i, carry):
        row = jnp.full((128, 128), net.r * 12 + i, jnp.int32)
        inside = jnp.where((row >= top) & (row < bottom), column_inside, 0.0)
        k.mask[pl.ds(pl.multiple_of(i * 128, 128), 128), :] = inside
        return carry

    lax.fori_loop(0, 12, mask_rows, 0)
    k.stream.done(mask=1)
    k.stream.need(x=1)

    def reduce_for(b):
        def reduce_rows(at):
            k.part[b, at, :] = mm(k.x[at, :], k.w_reduce[b])

        each_rows(1536, 384, reduce_rows)

    own_reduce.wait()
    reduce_for(net.m)
    arrivals[1].wait()
    reduce_for(net.m ^ 1)
    arrivals[2].wait()
    reduce_for(net.m ^ 2)
    arrivals[0].wait()
    k.stream.done(w_reduce=1)

    def far_half(half):
        def reduce_rows(at):
            at = pl.ds(pl.multiple_of(at.start + half * 768, 128), 384)
            k.part[net.m ^ 3, at, :] = mm(k.x[at, :], k.w_reduce[net.m ^ 3])

        each_rows(768, 384, reduce_rows)

    sum_scatter(net, k.part, scatter_refs(k, "sum"), k.reduced, produce=far_half)
    k.stream.done(reduced=1)

    half = pl.ds(pl.multiple_of(net.r * 32, 32), 32)
    late = []

    def weight_block(kind, b):
        lanes = lane_block(b, 512)
        if kind == "edge":
            return k.aspp_rates.at[0, 2 * net.r, :, :, lanes], k.w_pyramid.at[pl.ds(10, 3), net.m]
        if kind == "point":
            return k.aspp_point.at[half, lanes], k.w_pyramid.at[0, net.m, half]
        if kind == "project":
            return k.project.at[:, half], k.w_project.at[net.m, :, half]
        return (
            k.aspp_rates.at[kind, 1, :, half, lanes],
            k.w_pyramid.at[pl.ds(1 + 3 * kind, 3), net.m, half],
        )

    def spread_weights(*kinds):
        for kind in kinds:
            src, dst = weight_block(kind, net.m)
            late.append(pltpu.make_async_copy(src, dst, k.local_sems.at[10 + len(late) // 4]))
            late[-1].start()
            for b, peer in branches:
                src, dst = weight_block(kind, b)
                late.append(net.send(src, dst, peer))

    spread_weights("edge")
    mean, inverse = statistics(net, k.reduced, k.mask, counts, k.out_1, k.in_1, counted)
    keep_rows(k.stats_1, mean, inverse)

    def activate_1(at):
        u = k.affine_1[0:1, :] * ((k.reduced[at, :] - mean) * inverse) + k.affine_1[1:2, :]
        rows_at = pl.ds(pl.multiple_of(at.start + 512, 128), 128)
        k.hidden[rows_at, lane_block(net.m)] = (u * sigmoid(u)).astype(BF16)

    each_rows(1536, 128, activate_1)
    gather_blocks(
        net, lambda b, at: k.hidden.at[pl.ds(at.start + 512, at.size), lane_block(b)], 1536
    )
    halo = send_halo(net, k.hidden)
    spread_weights("project", "point", 0)
    zero_margins(k.left, 8, 128)
    zero_margins(k.right, 8, 128)
    for load in loads:
        load.wait()
    halo.wait()
    k.stream.done(hidden=1)

    def dilated_rows(i, carry):
        total = 0.0
        for tap in range(3):
            rows_at = pl.ds(pl.multiple_of((i * 3 + 4 * tap) * 128, 128), 384)
            total = total + mm(k.hidden[rows_at, :], k.w_taps[tap])
        k.dilated[pl.ds(pl.multiple_of(i * 384, 128), 384), :] = total[:, 128:256]
        k.left[pl.ds(i * 3, 3), 8:136, :] = total[:, 0:128].reshape(3, 128, 128)
        k.right[pl.ds(i * 3, 3), 8:136, :] = total[:, 256:384].reshape(3, 128, 128)
        return carry

    lax.fori_loop(0, 4, dilated_rows, 0)

    def add_columns(i, carry):
        at = pl.ds(pl.multiple_of(i * 128, 128), 128)
        k.dilated[at, :] = k.dilated[at, :] + k.left[i, 4:132, :] + k.right[i, 12:140, :]
        return carry

    lax.fori_loop(0, 12, add_columns, 0)
    k.stream.done(dilated=1)
    mean_2, inverse_2 = statistics(net, k.dilated, k.mask, counts, k.out_2, k.in_2, counted)
    keep_rows(k.stats_2, mean_2, inverse_2)

    def activate_2(at):
        u = k.affine_2[0:1, :] * ((k.dilated[at, :] - mean_2) * inverse_2) + k.affine_2[1:2, :]
        k.hidden_two[at, lane_block(net.m)] = (u * sigmoid(u)).astype(BF16)

    each_rows(1536, 128, activate_2)
    gather_blocks(net, lambda b, at: k.hidden_two.at[at, lane_block(b)], 1536)
    spread_weights(1, 2)
    k.stream.done(hidden_two=1)
    k.stream.need(w_expand=1)

    def expand_rows(at):
        k.expanded[at, :] = mm(k.hidden_two[at, :], k.w_expand[...])

    each_rows(1536, 384, expand_rows)
    k.stream.done(expanded=1)
    mean_3, inverse_3 = statistics(net, k.expanded, k.mask, counts, k.out_3, k.in_3, counted)
    keep_rows(k.stats_3, mean_3, inverse_3)
    for copy in late:
        copy.wait()
    swaps = [
        net.send(ref.at[..., half, :], ref.at[..., half, :], net.core)
        for ref in (k.w_pyramid.at[pl.ds(0, 10)], k.w_project)
    ]

    def activate_3(at):
        u = k.affine_3[0:1, :] * ((k.expanded[at, :] - mean_3) * inverse_3) + k.affine_3[1:2, :]
        u = u + k.x[at, :].astype(F32)
        k.trunk[at, :] = (u * sigmoid(u)).astype(BF16)

    each_rows(1536, 32, activate_3)
    for copy in swaps:
        copy.wait()


def run_bottleneck(args):
    return call_kernel(
        bottleneck_forward,
        "bottleneck",
        0,
        args,
        dict(
            mask=((1536, 128), F32),
            w_reduce=((4, 512, 128), BF16),
            w_pyramid=((13, 4, 64, 512), BF16),
            w_project=((4, 5, 64, 256), BF16),
            reduced=((1536, 128), F32),
            stats_1=((8, 128), F32),
            hidden=((2560, 512), BF16),
            dilated=((1536, 128), F32),
            stats_2=((8, 128), F32),
            hidden_two=((1536, 512), BF16),
            expanded=((1536, 512), F32),
            stats_3=((8, 512), F32),
            trunk=((1536, 512), BF16),
        ),
        dict(
            w_taps=pltpu.VMEM((3, 512, 384), BF16),
            part=pltpu.VMEM((4, 1536, 128), F32),
            **scatter_scratch("sum", 1536, 128),
            left=pltpu.VMEM((12, 144, 128), F32),
            right=pltpu.VMEM((12, 144, 128), F32),
            **exchange_scratch(1),
            **exchange_scratch(2),
            **exchange_scratch(3),
            local_sems=pltpu.SemaphoreType.DMA((16,)),
        ),
        96,
        hbm=dict(conv_reduce=1, w_dilated=1, aspp_point=1, aspp_rates=1, project=1, w_pyramid=1, w_project=1),
        stream=dict(x=1, w_expand=1, mask=1, w_reduce=1, reduced=1, hidden=1, dilated=1, hidden_two=1, expanded=1),
    )


def pyramid_forward(net, k):
    counted, counts = pixel_count(k.boxes), tile_counts(net, k.boxes)
    area = (k.boxes[net.z, 2] * k.boxes[net.z, 3]).astype(F32)
    near = [
        (lax.rem(net.m + a, 4), lax.rem(net.r + b, 2), net.z)
        for a in range(4)
        for b in range(2)
        if a or b
    ]
    greet(net.group + [peer for i, peer in enumerate(near) if i])

    for b in range(4):
        k.affine_b[0:2, b * 64 : b * 64 + 64] = k.branch_norms[:, b, :]
    for i in range(2):
        k.affine_p[0:2, i * 64 : i * 64 + 64] = k.norm_project[...]
        k.affine_p[2:4, i * 64 : i * 64 + 64] = k.norm_pooling[...]
    k.head_rows[...] = jnp.zeros((32, 256), F32)
    k.head_rows[0:22, :] = k.head_weight[...].astype(F32)

    k.stream.need(mask=1)

    (own_sum,) = column_sums(
        lambda at: (k.trunk[at, :].astype(F32) * wide(k.mask[at, :], 512),), 1536, 512, 1
    )
    k.out_pool[...] = jnp.broadcast_to(own_sum, (8, 512))
    place = net.m * 2 + net.r
    pool_copies = [net.send(k.out_pool, k.in_pool.at[place], peer) for peer in near]
    k.in_pool[place] = k.out_pool[...]

    zero_margins(k.cells, 40, 128)

    def fill(i, carry):
        at = pl.ds(pl.multiple_of(i * 128, 128), 128)
        k.cells[i, 40:168, :] = k.trunk[at, :].astype(F32)
        return carry

    lax.fori_loop(0, 12, fill, 0)

    def shifted(i, offset):
        cells = k.cells[pl.ds(i * 3, 3), 40 + offset : 168 + offset, :]
        return cells.reshape(384, 512).astype(BF16)

    def rows_of(i):
        return pl.ds(pl.multiple_of(i * 384, 128), 384)

    def edge_rows(i, carry):
        total = 0.0
        for j in range(3):
            total = total + mm_t(shifted(i, 12 * (j - 1)), k.w_pyramid[10 + j])
        k.edge_out[rows_of(i), :] = total.astype(BF16)
        return carry

    k.stream.need(w_pyramid=1)
    lax.fori_loop(0, 4, edge_rows, 0)
    edge = net.send(k.edge_out, k.edge_in, net.core)

    def outer_rows(i, carry):
        second, third = 0.0, 0.0
        for j in range(3):
            second = second + mm_t(shifted(i, 24 * (j - 1)), k.w_pyramid[4 + j])
        for j in range(3):
            third = third + mm_t(shifted(i, 36 * (j - 1)), k.w_pyramid[7 + j])
        for b, block in enumerate(pair(second, third)):
            k.part[b, rows_of(i), 128:256] = block
        return carry

    def inner_rows(i, carry):
        point = mm_t(k.trunk[rows_of(i), :], k.w_pyramid[0])
        first = k.edge_in[rows_of(i), :].astype(F32)
        for j in range(3):
            first = first + mm_t(shifted(i, 12 * (j - 1)), k.w_pyramid[1 + j])
        for b, block in enumerate(pair(point, first)):
            k.part[b, rows_of(i), 0:128] = block
        return carry

    def half_tile(half):
        lax.fori_loop(2 * half, 2 * half + 2, outer_rows, 0)
        if half == 0:
            edge.wait()
        lax.fori_loop(2 * half, 2 * half + 2, inner_rows, 0)

    sum_scatter(net, k.part, scatter_refs(k, "sum"), k.branches, produce=half_tile)

    low_256 = lax.broadcasted_iota(jnp.int32, (256, 128), 1) < 64
    odd = lax.rem(net.m, 2) == 1

    def slot(s):
        lanes = lane_block(net.m // 2)
        block = jnp.concatenate([k.w_slots[b, s, :, lanes] for b in range(4)], axis=0).astype(F32)
        return jnp.where(odd, pltpu.roll(block, 64, 1), block)

    for s in range(0, 4, 2):
        both = jnp.where(low_256, slot(s), pltpu.roll(slot(s + 1), 64, 1))
        k.w_project[:, s * 64 : s * 64 + 128] = both.astype(BF16)
    k.w_slot[...] = jnp.where(low_256, slot(4), 0.0).astype(BF16)
    k.w_pool[0:64, :] = k.aspp_pool[...]
    k.w_pool[64:128, :] = k.aspp_pool[...]

    for copy in pool_copies:
        copy.wait()
    for b in range(4):
        pooled = (k.in_pool[2 * b, 0:1, :] + k.in_pool[2 * b + 1, 0:1, :]) / area
        k.pooled[:, b * 512 : b * 512 + 512] = jnp.broadcast_to(pooled, (16, 512)).astype(BF16)
    pool_conv = mm_t(k.pooled[...], k.w_pool[...])[0:1, :]
    mean, inverse = statistics(
        net, k.branches, k.mask, counts, k.out_1, k.in_1, counted, extra=pool_conv
    )
    every = k.in_1[0:4, 4, :]
    pool_mean = jnp.sum(every, axis=0, keepdims=True) / 4.0
    pool_gap = every - pool_mean
    pool_inverse = lax.rsqrt(jnp.sum(pool_gap * pool_gap, axis=0, keepdims=True) / 4.0 + EPS)
    pool_normed = pool_gap * pool_inverse
    pool_gain, pool_bias = k.affine_p[2:3, :], k.affine_p[3:4, :]
    pool_u = pool_gain * pool_normed + pool_bias
    k.rows_scratch[0:4, :] = pool_u * sigmoid(pool_u)
    pool_act = jnp.broadcast_to(k.rows_scratch[pl.ds(net.z, 1), :], (16, 128)).astype(BF16)

    def normed_branch(at):
        return (k.branches[at, :] - mean) * inverse

    gain_b, bias_b = k.affine_b[0:1, :], k.affine_b[1:2, :]

    def activate_branches(at):
        u = gain_b * normed_branch(at) + bias_b
        k.spatial[at, :] = (u * sigmoid(u)).astype(BF16)

    each_rows(1536, 64, activate_branches)

    pool_row = mm_t(pool_act, k.w_slot[...])[0:1, :]

    def project_rows(i, carry):
        at = pl.ds(pl.multiple_of(i * 384, 128), 384)
        below = pl.ds(pl.multiple_of(i * 384 + 768, 128), 384)
        first = mm_t(k.spatial[at, :], k.w_project[...]) + pool_row
        second = mm_t(k.spatial[below, :], k.w_project[...]) + pool_row
        for b, block in enumerate(pair(first, second)):
            k.part_2[b, at, :] = block
        return carry

    def project_half(half):
        project_rows(half, 0)

    low_128 = lax.broadcasted_iota(jnp.int32, (128, 128), 1) < 64

    def pair_mask(at):
        below = pl.ds(pl.multiple_of(at.start + 768, 128), 128)
        k.mask_pairs[at, :] = jnp.where(low_128, k.mask[at, :], k.mask[below, :])

    each_rows(768, 128, pair_mask)
    sum_scatter(net, k.part_2, scatter_refs(k, "sum2"), k.projected, produce=project_half)
    mean_p, inverse_p = statistics(
        net, k.projected, k.mask_pairs, counts, k.out_2, k.in_2, counted, folded=True
    )
    gain_p, bias_p = k.affine_p[0:1, :], k.affine_p[1:2, :]

    def normed_projected(at):
        return (k.projected[at, :] - mean_p) * inverse_p

    def activate_projected(at):
        u = gain_p * normed_projected(at) + bias_p
        k.gathered[net.m, at, :] = (u * sigmoid(u)).astype(BF16)

    each_rows(768, 128, activate_projected)
    gather_blocks(net, lambda b, at: k.gathered.at[b, at], 768)

    def spread(source, target):
        def body(at):
            first, second = unpair([source[b, at, :].astype(F32) for b in range(4)])
            target[at, :] = first.astype(BF16)
            target[pl.ds(pl.multiple_of(at.start + 768, 128), 128), :] = second.astype(BF16)

        each_rows(768, 128, body)

    k.features[...] = k.gathered[net.m]
    spread(k.gathered, k.wide_features)

    class_row = lax.broadcasted_iota(jnp.int32, (32, 512), 0)
    is_class, is_depth = class_row < 19, class_row == 19
    is_normal = (class_row == 20) | (class_row == 21)
    tile_row = lax.broadcasted_iota(jnp.int32, (32, 128), 0)
    bias_column = jnp.zeros((32, 128), F32)
    for c in range(22):
        bias_column = jnp.where(tile_row == c, k.head_bias[c], bias_column)
    task = [jnp.exp(jnp.full((32, 128), -k.log_vars[t], F32)) / counted for t in range(3)]
    weight_column = jnp.where(tile_row < 19, task[0], jnp.where(tile_row == 19, task[1], task[2]))
    bias_column, weight_column = wide(bias_column, 512), wide(weight_column, 512)
    k.head[...] = k.head_rows[...].astype(BF16)
    top_row, left_edge = k.boxes[net.z, 0], k.boxes[net.z, 1]
    bottom_row, right_edge = top_row + k.boxes[net.z, 2], left_edge + k.boxes[net.z, 3]
    lane = lax.broadcasted_iota(jnp.int32, (1, 512), 1)

    def four_rows(rows):
        return jnp.concatenate(rows, axis=1)
    loss_sums, bias_sums = 0.0, 0.0
    for chunk in range(3):
        at = pl.ds(chunk * 512, 512)
        logits = mm_t(k.head[...], k.wide_features[at, :]) + bias_column
        row_id, column_id = net.r * 12 + chunk * 4 + lane // 128, lane % 128
        inside = (row_id >= top_row) & (row_id < bottom_row)
        inside = inside & (column_id >= left_edge) & (column_id < right_edge)
        inside = jnp.where(inside, 1.0, 0.0)
        span = range(chunk * 4, chunk * 4 + 4)
        label = four_rows([k.labels[y] for y in span])
        target = jnp.where(is_depth, four_rows([k.depth[y] for y in span]), 0.0)
        for n in range(2):
            normal = four_rows([k.normal[y, n : n + 1, :] for y in span])
            target = jnp.where(class_row == 20 + n, normal, target)
        top = jnp.max(jnp.where(is_class, logits, -jnp.inf), axis=0, keepdims=True)
        powers = jnp.where(is_class, jnp.exp(jnp.where(is_class, logits - top, 0.0)), 0.0)
        power_sum = jnp.sum(powers, axis=0, keepdims=True)
        onehot = jnp.where(class_row == label, 1.0, 0.0)
        cross = jnp.log(power_sum) + top - jnp.sum(logits * onehot, axis=0, keepdims=True)
        gap = logits - target
        smooth = jnp.sqrt(gap * gap + 1.0)
        loss = jnp.where(class_row == 0, cross, 0.0)
        loss = jnp.where(is_depth, smooth - 1.0, loss)
        loss = jnp.where(is_normal, gap * gap, loss) * inside
        grad = jnp.where(is_class, powers / power_sum - onehot, 0.0)
        grad = jnp.where(is_depth, gap / smooth, grad)
        grad = jnp.where(is_normal, 2.0 * gap, grad) * (weight_column * inside)
        loss_sums = loss_sums + jnp.sum(loss, axis=1, keepdims=True)
        bias_sums = bias_sums + jnp.sum(grad, axis=1, keepdims=True)
        high = grad.astype(BF16)
        k.grad_logits[0:32, at] = high
        k.grad_logits[32:64, at] = (grad - high.astype(F32)).astype(BF16)
    head_terms = mm(k.grad_logits[...], k.wide_features[...])
    k.out_head[:, 0:256] = head_terms[0:32, :] + head_terms[32:64, :]
    first_lane = lax.broadcasted_iota(jnp.int32, (32, 128), 1) == 0
    k.out_head[:, 256:384] = jnp.where(first_lane, bias_sums, loss_sums)
    quarter = pl.ds(pl.multiple_of(net.m * 8, 8), 8)
    head_copies = [
        net.send(k.out_head.at[quarter], k.in_head.at[net.slot], peer) for peer in net.group
    ]
    k.in_head[net.slot] = k.out_head[quarter, :]

    own_head = k.head_rows[:, lane_block(net.m // 2)]
    own_head = jnp.where(odd, pltpu.roll(own_head, 64, 1), own_head)
    own_head = jnp.where(low_128[0:32, :], own_head, 0.0)
    head_low = jnp.concatenate([own_head, own_head], axis=0).astype(BF16)
    own_head = pltpu.roll(own_head, 64, 1)
    head_high = jnp.concatenate([own_head, own_head], axis=0).astype(BF16)
    k.grad_p[...] = tm_m(k.grad_logits[:, 0:768], head_low) + tm_m(
        k.grad_logits[:, 768:1536], head_high
    )

    def back_features(at):
        k.grad_p[at, :] = k.grad_p[at, :] * slope(gain_p * normed_projected(at) + bias_p)

    each_rows(768, 128, back_features)
    bias_grad, gain_grad = gradient_sums(
        net, k.grad_p, normed_projected, k.out_3, k.in_3, folded=True
    )
    keep_rows(k.norm_p, gain_grad, bias_grad)

    def back_projected(at):
        shared = k.mask_pairs[at, :] / counted * gain_p
        grad = gain_p * k.grad_p[at, :] - shared * (bias_grad + normed_projected(at) * gain_grad)
        k.gathered_grad[net.m, at, :] = (inverse_p * grad).astype(BF16)

    each_rows(768, 128, back_projected)
    gather_blocks(net, lambda b, at: k.gathered_grad.at[b, at], 768)
    spread(k.gathered_grad, k.grad_projected)
    (pixel_sum,) = column_sums(lambda at: (k.grad_projected[at, :].astype(F32),), 1536, 256, 1)
    row_16 = lax.broadcasted_iota(jnp.int32, (16, 256), 0)
    terms = jnp.zeros((16, 256), F32)
    for i, term in enumerate(split_three(pixel_sum)):
        terms = jnp.where(row_16 == i, term.astype(F32), terms)
    terms = terms.astype(BF16)
    tall = jnp.concatenate([terms] * 8, axis=0)
    pool_grad = jnp.sum(mm(tall, k.w_slot[...]), axis=0, keepdims=True) * 0.125

    def project_gradient():
        for b in range(2):
            lanes = slice(b * 128, b * 128 + 128)
            grad = tm_m(k.grad_projected[:, lanes], k.spatial[...])
            k.grad_project[b * 4 : b * 4 + 4, :, 0:256] = grad.reshape(4, 32, 256).astype(BF16)
        grad = tm_m(terms, pool_act)
        k.grad_project[:, :, 256:384] = grad.reshape(8, 32, 128).astype(BF16)

    def back_spatial(at):
        grad = mm(k.grad_projected[at, :], k.w_project[...])
        k.grad_b[at, :] = grad * slope(gain_b * normed_branch(at) + bias_b)

    each_rows(1536, 128, back_spatial)
    bias_grad_b, gain_grad_b = gradient_sums(
        net,
        k.grad_b,
        normed_branch,
        k.out_4,
        k.in_4,
        extra=pool_grad,
        meanwhile=project_gradient,
    )
    keep_rows(k.norm_b, gain_grad_b, bias_grad_b)

    pool_terms = k.in_4[0:4, 4, :] + k.in_4[4:8, 4, :]
    pool_terms = pool_terms * slope(pool_u)
    pool_bias_grad = jnp.sum(pool_terms, axis=0, keepdims=True)
    pool_gain_grad = jnp.sum(pool_terms * pool_normed, axis=0, keepdims=True)
    keep_rows(k.norm_pool, pool_gain_grad, pool_bias_grad)
    pool_back = pool_inverse * (
        pool_gain * pool_terms
        - pool_gain / 4.0 * (pool_bias_grad + pool_normed * pool_gain_grad)
    )
    low = lax.broadcasted_iota(jnp.int32, (4, 128), 1) < 64
    k.rows_scratch[4:8, :] = jnp.where(low, pool_back, 0.0)
    grad_conv = jnp.broadcast_to(k.rows_scratch[pl.ds(net.z + 4, 1), :], (16, 128)).astype(BF16)
    spread_back = mm(grad_conv, k.w_pool[...])[0:8, :]
    for b in range(4):
        k.out_back[b] = spread_back[:, b * 512 : b * 512 + 512]
    back_copies = [
        net.send(k.out_back.at[lax.rem(net.m + a, 4)], k.in_back.at[a], (lax.rem(net.m + a, 4), net.r, net.z))
        for a in range(1, 4)
    ]

    only_first = lax.broadcasted_iota(jnp.int32, (16, 128), 0) == 0
    one_row = jnp.where(only_first, grad_conv.astype(F32) * 0.5, 0.0).astype(BF16)
    for e in range(8):
        grad = tm_m(one_row, k.pooled[:, e * 256 : e * 256 + 256])
        k.grad_pool[e] = grad[0:64, :].astype(BF16)

    def back_branches(at):
        shared = wide(k.mask[at, :], 256) / counted * gain_b
        grad = gain_b * k.grad_b[at, :] - shared * (bias_grad_b + normed_branch(at) * gain_grad_b)
        k.grad_branches[at, :] = (inverse * grad).astype(BF16)

    for copy in back_copies:
        copy.wait()
    k.grad_pooled[...] = (k.out_back[net.m] + k.in_back[1] + k.in_back[2] + k.in_back[3]) / area
    for copy in head_copies:
        copy.wait()
    k.head_sums[quarter, :] = jnp.sum(k.in_head[...], axis=0)
    head_copies = [
        net.send(k.head_sums.at[quarter], k.head_sums.at[quarter], (lax.rem(net.m + a, 4), net.r, net.z))
        for a in range(1, 4)
    ]
    each_rows(1536, 64, back_branches)
    for copy in head_copies:
        copy.wait()


def run_pyramid(args):
    return call_kernel(
        pyramid_forward,
        "pyramid",
        1,
        args,
        dict(
            features=((768, 128), BF16),
            norm_p=((8, 128), F32),
            grad_project=((8, 32, 384), BF16),
            grad_pool=((8, 64, 256), BF16),
            norm_b=((8, 256), F32),
            norm_pool=((8, 128), F32),
            grad_branches=((1536, 256), BF16),
            grad_pooled=((8, 512), F32),
            head_sums=((32, 384), F32),
        ),
        dict(
            affine_b=pltpu.VMEM((8, 256), F32),
            affine_p=pltpu.VMEM((8, 128), F32),
            head_rows=pltpu.VMEM((32, 256), F32),
            head=pltpu.VMEM((32, 256), BF16),
            pooled=pltpu.VMEM((16, 2048), BF16),
            spatial=pltpu.VMEM((1536, 256), BF16),
            grad_projected=pltpu.VMEM((1536, 256), BF16),
            w_project=pltpu.VMEM((256, 256), BF16),
            w_slot=pltpu.VMEM((256, 128), BF16),
            w_pool=pltpu.VMEM((128, 2048), BF16),
            mask_pairs=pltpu.VMEM((768, 128), F32),
            out_pool=pltpu.VMEM((8, 512), F32),
            in_pool=pltpu.VMEM((8, 8, 512), F32),
            cells=pltpu.VMEM((12, 208, 512), F32),
            edge_out=pltpu.VMEM((1536, 256), BF16),
            edge_in=pltpu.VMEM((1536, 256), BF16),
            part=pltpu.VMEM((4, 1536, 256), F32),
            **scatter_scratch("sum", 1536, 256),
            branches=pltpu.VMEM((1536, 256), F32),
            rows_scratch=pltpu.VMEM((8, 128), F32),
            part_2=pltpu.VMEM((4, 768, 128), F32),
            **scatter_scratch("sum2", 768, 128),
            projected=pltpu.VMEM((768, 128), F32),
            gathered=pltpu.VMEM((4, 768, 128), BF16),
            wide_features=pltpu.VMEM((1536, 256), BF16),
            grad_logits=pltpu.VMEM((64, 1536), BF16),
            out_head=pltpu.VMEM((32, 384), F32),
            in_head=pltpu.VMEM((8, 8, 384), F32),
            grad_p=pltpu.VMEM((768, 128), F32),
            gathered_grad=pltpu.VMEM((4, 768, 128), BF16),
            grad_b=pltpu.VMEM((1536, 256), F32),
            out_back=pltpu.VMEM((4, 8, 512), F32),
            in_back=pltpu.VMEM((4, 8, 512), F32),
            **exchange_scratch(1),
            **exchange_scratch(2),
            **exchange_scratch(3),
            **exchange_scratch(4),
        ),
        96,
        smem=dict(boxes=1, head_bias=1, log_vars=1),
        stream=dict(mask=1, w_pyramid=1),
    )


def core_halves(net, whole, arrived):
    away = pl.ds(pl.multiple_of(4 - 4 * net.r, 4), 4)
    return net.send(whole.at[away], arrived, net.core)


def add_halves(net, whole, arrived, target):
    for z in range(4):
        total = whole[4 * net.r + z].astype(F32) + arrived[z].astype(F32)
        target[z] = total.astype(target.dtype)


def chunk_of(net):
    return lambda z: 2 * lax.rem(z + net.m, 2) + z // 2


def along_z(net, source, target, chunk=lambda z: z):
    copies = []
    for d in (1, 2, 3):
        there = lax.rem(net.z + d, 4)
        copies.append(
            net.send(source.at[chunk(there)], target.at[d - 1], (net.m, net.r, there))
        )
    return copies


def finish_z(net, half, arrived, chunk=lambda z: z):
    return half[chunk(net.z)].astype(F32) + sum(arrived[d].astype(F32) for d in range(3))


class PairSums:
    def __init__(self, net, half, other, pair, last):
        self.net, self.half, self.other, self.pair, self.last = net, half, other, pair, last
        kept, away = lax.rem(net.z + net.m, 2), lax.rem(net.z + net.m + 1, 2)
        self.kept = 2 * kept
        beside = net.z + 1 - 2 * lax.rem(net.z, 2)
        self.first = self.copy(half.at[pl.ds(2 * away, 2)], other, beside)
        self.high = net.z // 2
        self.second = self.copy(pair.at[1 - self.high], last, net.z + 2 - 4 * self.high)

    def copy(self, src, dst, z):
        net, i = self.net, self.net.count
        net.count += 1
        return pltpu.make_async_remote_copy(
            src_ref=src,
            dst_ref=dst,
            send_sem=net.send_sems.at[i],
            recv_sem=net.recv_sems.at[i],
            device_id=(net.m, net.r, z),
            device_id_type=MESH,
        )

    def begin(self):
        self.first.start()

    def go_on(self, half):
        self.first.wait()

        def body(i, carry):
            for h in range(2):
                total = half[self.kept + h, i].astype(F32) + self.other[h, i].astype(F32)
                self.pair[h, i] = total.astype(BF16)
            return carry

        lax.fori_loop(0, half.shape[1], body, 0)
        self.second.start()

    def finish(self, target):
        self.second.wait()

        def body(i, carry):
            total = self.pair[self.high, i].astype(F32) + self.last[i].astype(F32)
            target[0, i] = total[:, 0:256].astype(BF16)
            target[1, i] = total[:, 256:512].astype(BF16)
            return carry

        lax.fori_loop(0, target.shape[1], body, 0)


def pyramid_backward(net, k):
    counted = pixel_count(k.boxes)
    greet([net.side, net.over] + net.group)
    k.blocks[net.m] = k.grad_branches[...]
    small = [
        core_halves(net, k.grad_project, k.core_project),
        core_halves(net, k.grad_pool, k.core_pool),
    ]
    for c in range(4):
        zero_margins(k.cells.at[c], 40, 128)

    def rows_of(i, size=384):
        return pl.ds(pl.multiple_of(i * size, 128), size)

    low = lax.broadcasted_iota(jnp.int32, (128, 128), 1) < 64
    near = net.m // 2
    far = 1 - near
    mine_first = net.r == near
    mine_second = net.r == far

    def both(source, pair_of, i, lane):
        at = slice(lane * 128, lane * 128 + 128)
        left = source[2 * pair_of, rows_of(i, 128), at].astype(F32)
        right = source[2 * pair_of + 1, rows_of(i, 128), at].astype(F32)
        first = jnp.where(low, left, pltpu.roll(right, 64, 1))
        return first, jnp.where(low, pltpu.roll(left, 64, 1), right)

    def shift_rows(pair_of, i, cell, rate, base):
        for j in range(3):
            start = 40 - rate * (j - 1)
            block = k.cells[cell, i, start : start + 128, :].astype(BF16)
            k.shifts[base + j, rows_of(i, 128), lane_block(pair_of)] = block

    def build(pair_of):
        def fill(i, carry):
            point, first = both(k.blocks, pair_of, i, 0)
            k.shifts[0, rows_of(i, 128), lane_block(pair_of)] = point.astype(BF16)
            second, third = both(k.blocks, pair_of, i, 1)
            k.cells[0, i, 40:168, :] = first
            k.cells[1, i, 40:168, :] = second
            k.cells[2, i, 40:168, :] = third
            return carry

        lax.fori_loop(0, 12, fill, 0)

        def spread(i, carry):
            for cell, rate, base in ((0, 12, 1), (1, 24, 4), (2, 36, 7)):
                shift_rows(pair_of, i, cell, rate, base)
            return carry

        lax.fori_loop(0, 12, spread, 0)

    def build_edge(pair_of):
        def fill(i, carry):
            k.cells[3, i, 40:168, :] = both(k.other, pair_of, i, 0)[1]
            return carry

        lax.fori_loop(0, 12, fill, 0)

        def spread(i, carry):
            shift_rows(pair_of, i, 3, 12, 10)
            return carry

        lax.fori_loop(0, 12, spread, 0)

    def weight_gradients(pair_of):
        owners = pl.ds(4 * pair_of, 4)

        def run(start, stop, shift):
            def body(t, carry):
                grad = tm_m(k.shifts[t, :, lane_block(pair_of)], k.trunk[...])
                k.grad_pyramid[owners, t + shift] = grad.reshape(4, 32, 512).astype(BF16)
                return carry

            lax.fori_loop(start, stop, body, 0)

        run(0, 1, 0)
        run(1, 4, 3)
        run(4, 10, 6)
        run(10, 13, net.r * 6 - 9)
        for j in range(3):
            k.grad_pyramid[owners, 7 - net.r * 6 + j] = jnp.zeros((4, 32, 512), BF16)

    def beside(pair_of):
        view = (pl.ds(2 * pair_of, 2), slice(None), pl.ds(0, 128))
        return net.send(k.blocks.at[view], k.other.at[pl.ds(2 * pair_of, 2)], net.core)

    def to_core(pair_of):
        i = net.count
        net.count += 1
        return pltpu.make_async_remote_copy(
            src_ref=k.grad_pyramid.at[pl.ds(4 * pair_of, 4)],
            dst_ref=k.core_pyramid,
            send_sem=net.send_sems.at[i],
            recv_sem=net.recv_sems.at[i],
            device_id=net.core,
            device_id_type=MESH,
        )

    def add_core(pair_of):
        def body(i, carry):
            for z in range(4):
                total = k.grad_pyramid[4 * pair_of + z, i].astype(F32)
                total = total + k.core_pyramid[z, i].astype(F32)
                k.half_pyramid[z, i] = total.astype(BF16)
            return carry

        lax.fori_loop(0, 16, body, 0)

    first_swap = []

    def near_pair():
        copy = beside(near)
        build(near)
        copy.wait()
        build_edge(near)
        k.stream.need(trunk=1)
        weight_gradients(near)
        first_swap.append(to_core(near))
        pl.when(mine_second)(first_swap[0].start)

    gather_blocks(net, lambda b, at: k.blocks.at[b, at], 1536, meanwhile=near_pair)
    copy = beside(far)
    build(far)
    for swap in small:
        swap.wait()
    add_halves(net, k.grad_project, k.core_project, k.half_project)
    add_halves(net, k.grad_pool, k.core_pool, k.half_pool)
    small_moves = along_z(net, k.half_project, k.z_project, chunk_of(net))
    small_moves = small_moves + along_z(net, k.half_pool, k.z_pool)
    copy.wait()
    build_edge(far)
    pair_sums = PairSums(net, k.half_pyramid, k.z_other, k.z_pair, k.z_last)

    @pl.when(mine_first)
    def _():
        first_swap[0].wait_recv()
        add_core(near)
        pair_sums.begin()

    def trunk_rows(i, carry):
        total = 0.0
        for t in range(13):
            total = total + mm(k.shifts[t, rows_of(i), :], k.w_pyramid[t])
        k.shortcut[rows_of(i), :] = total
        return carry

    k.stream.need(w_pyramid=1, expanded=1, x=1, mask=1)
    lax.fori_loop(0, 4, trunk_rows, 0)
    mean, inverse = k.stats_3[0:1, :], k.stats_3[1:2, :]
    gain, bias = k.affine_3[0:1, :], k.affine_3[1:2, :]
    pooled = k.grad_pooled[0:1, :]

    def normed(at):
        return (k.expanded[at, :] - mean) * inverse

    def back_trunk(at):
        u = gain * normed(at) + bias + k.x[at, :].astype(F32)
        grad = k.shortcut[at, :] + wide(k.mask[at, :], 512) * pooled
        k.shortcut[at, :] = grad * slope(u)

    each_rows(1536, 32, back_trunk)
    k.stream.done(shortcut=1)

    second_swap = to_core(far)

    def far_gradients():
        weight_gradients(far)

        @pl.when(mine_first)
        def _():
            second_swap.start()
            pair_sums.go_on(k.half_pyramid)

    bias_grad, gain_grad = gradient_sums(
        net, k.shortcut, normed, k.out_1, k.in_1, meanwhile=far_gradients
    )
    keep_rows(k.norm_3, gain_grad, bias_grad)

    def back_expanded(at):
        shared = wide(k.mask[at, :], 512) / counted * gain
        grad = gain * k.shortcut[at, :] - shared * (bias_grad + normed(at) * gain_grad)
        k.grad_expanded[at, :] = (inverse * grad).astype(BF16)

    each_rows(1536, 32, back_expanded)
    k.stream.done(grad_expanded=1)
    for move_ in small_moves:
        move_.wait()
    k.sum_project[...] = finish_z(net, k.half_project, k.z_project, chunk_of(net)).astype(BF16)
    k.sum_pool[...] = finish_z(net, k.half_pool, k.z_pool)

    @pl.when(mine_second)
    def _():
        first_swap[0].wait_send()
        second_swap.wait_recv()
        add_core(far)

    @pl.when(mine_first)
    def _():
        second_swap.wait_send()
        pair_sums.finish(k.sum_pyramid)


def pair_scratch():
    return dict(
        z_other=pltpu.VMEM((2, 16, 32, 512), BF16),
        z_pair=pltpu.VMEM((2, 16, 32, 512), BF16),
        z_last=pltpu.VMEM((16, 32, 512), BF16),
    )


def run_pyramid_backward(args):
    return call_kernel(
        pyramid_backward,
        "pyramid_back",
        2,
        args,
        dict(
            shortcut=((1536, 512), F32),
            grad_expanded=((1536, 512), BF16),
            norm_3=((8, 512), F32),
            half_pyramid=((4, 16, 32, 512), BF16),
            sum_pyramid=((2, 16, 32, 256), BF16),
            sum_project=((32, 384), BF16),
            sum_pool=((64, 256), F32),
        ),
        dict(
            half_project=pltpu.VMEM((4, 32, 384), BF16),
            half_pool=pltpu.VMEM((4, 64, 256), BF16),
            **pair_scratch(),
            z_project=pltpu.VMEM((3, 32, 384), BF16),
            z_pool=pltpu.VMEM((3, 64, 256), BF16),
            grad_pyramid=pltpu.VMEM((8, 16, 32, 512), BF16),
            core_pyramid=pltpu.VMEM((4, 16, 32, 512), BF16),
            core_project=pltpu.VMEM((4, 32, 384), BF16),
            core_pool=pltpu.VMEM((4, 64, 256), BF16),
            blocks=pltpu.VMEM((4, 1536, 256), BF16),
            other=pltpu.VMEM((4, 1536, 128), BF16),
            cells=pltpu.VMEM((4, 12, 208, 128), F32),
            shifts=pltpu.VMEM((13, 1536, 256), BF16),
            **exchange_scratch(1),
        ),
        48,
        stream=dict(w_pyramid=1, expanded=1, x=1, mask=1, trunk=1, shortcut=1, grad_expanded=1),
    )


def bottleneck_backward(net, k):
    counted = pixel_count(k.boxes)
    loads = load_taps(k)
    high, source = net.z // 2, net.slot // 2
    here = net.m * 8 + net.slot
    owners, givers = [], []
    for i in range(2):
        part = 2 * net.m + i
        column = 2 * net.r + lax.rem(net.z + net.m, 2)
        owners.append((column, part // 4, lax.rem(part, 4)))
        givers.append((source, net.m // 2, lax.rem(net.m + source, 2) + 2 * i))

    def elsewhere(device):
        return device[0] * 8 + device[1] * 4 + device[2] != here

    moves = elsewhere(owners[0])
    stays = jnp.logical_not(moves)
    greet(
        [net.side, net.over, net.diagonal] + net.group + [owners[1]],
        [(owners[0], moves), (givers[0], elsewhere(givers[0])), (givers[1], elsewhere(givers[1]))],
    )

    def to_owners(views, arrived, sem):
        base = net.count
        net.count += 2

        def copy(i, g, device):
            return pltpu.make_async_remote_copy(
                src_ref=views(i),
                dst_ref=arrived.at[g],
                send_sem=net.send_sems.at[base + i],
                recv_sem=net.recv_sems.at[base + g],
                device_id=device,
                device_id_type=MESH,
            )

        first, second = copy(0, high, owners[0]), copy(1, high, owners[1])
        kept = pltpu.make_async_copy(views(0), arrived.at[high], sem)

        def begin():
            pl.when(moves)(first.start)
            pl.when(stays)(kept.start)
            second.start()

        def wait():
            pl.when(moves)(first.wait_send)
            pl.when(stays)(kept.wait)
            second.wait_send()
            for g in range(2):
                pl.when(elsewhere(givers[g]))(copy(0, g, owners[1]).wait_recv)

        begin()
        return wait

    def lanes_for(i):
        return pl.ds(i * 256, 256)

    early = net.r == net.m // 2
    is_late = net.r == 1 - net.m // 2
    pair_sums = PairSums(net, k.far_half_pyramid, k.z_other, k.z_pair, k.z_last)

    odd_z = lax.rem(net.z, 2)
    lone = early & (odd_z == 0)
    beside = early & (odd_z == 1)
    stay = pltpu.make_async_copy(k.pyramid_sum, k.relay.at[0], k.local_sems.at[9])

    def remote(src, dst, send, arrive, device):
        return pltpu.make_async_remote_copy(
            src_ref=src,
            dst_ref=dst,
            send_sem=net.send_sems.at[send],
            recv_sem=net.recv_sems.at[arrive],
            device_id=device,
            device_id_type=MESH,
        )

    base = net.count
    net.count += 6
    to_side = remote(k.pyramid_sum, k.relay.at[0], base, base, net.side)
    across = (net.m ^ (2 + odd_z), net.r, net.z)
    to_across = remote(k.pyramid_sum, k.relay.at[1], base + 1, base + 1, across)
    plane = lax.rem(net.m + net.z, 2)

    def forward(e, i):
        device = (net.m, net.r if e == 0 else 1 - net.r, 2 * plane + i)
        return remote(
            k.relay.at[e, i], k.own_pyramid.at[high], base + 2 + 2 * e + i, base + 2 + high, device
        )

    forwards = [[forward(e, i) for i in range(2)] for e in range(2)]
    keep = pltpu.make_async_copy(k.relay.at[0, odd_z], k.own_pyramid.at[high], k.local_sems.at[12])
    keeps = early & (plane == high)

    def kept_here(i):
        return keeps & (odd_z == i)

    def begin_early():
        pl.when(lone)(stay.start)
        pl.when(beside)(to_side.start)

    def relay_early():
        pl.when(lone)(stay.wait)
        pl.when(beside)(to_side.wait)
        for i in range(2):
            pl.when(early & jnp.logical_not(kept_here(i)))(forwards[0][i].start)
        pl.when(keeps)(keep.start)

    def relay_late():
        pl.when(early)(to_across.wait_recv)
        for i in range(2):
            pl.when(early)(forwards[1][i].start)

    def wait_pyramid():
        pl.when(is_late)(to_across.wait_send)
        for i in range(2):
            pl.when(early & jnp.logical_not(kept_here(i)))(forwards[0][i].wait_send)
            pl.when(early)(forwards[1][i].wait_send)
        pl.when(keeps)(keep.wait)
        for g in range(2):
            local = early & (lax.rem(net.z // 2 + net.m, 2) + 2 * g == net.z)
            arrival = remote(k.relay.at[0, 0], k.own_pyramid.at[g], base, base + 2 + g, net.core)
            pl.when(jnp.logical_not(local))(arrival.wait_recv)


    @pl.when(is_late)
    def _():
        pair_sums.begin()

    @pl.when(early)
    def _():
        k.pyramid_sum[...] = k.sum_pyramid[...]

    wait_project = to_owners(lambda i: k.sum_project, k.own_project, k.local_sems.at[10])

    def rows_of(i, size=384):
        return pl.ds(pl.multiple_of(i * size, 128), size)

    def expand_half(half):
        def expand_rows(at):
            at = pl.ds(pl.multiple_of(at.start + half * 768, 128), 384)
            total = mm_t(k.grad_expanded[at, :], k.w_expand[...])
            for b in range(4):
                k.part[b, at, :] = total[:, b * 128 : b * 128 + 128]

        each_rows(768, 384, expand_rows)

    swaps, late_moves = [], []

    def expand_gradient():
        k.stream.need(hidden_two=1)

        def body(b, carry):
            grad = tm_m(k.hidden_two[:, lane_block(b)], k.grad_expanded[...])
            k.grad_expand[pl.ds(2 * b, 2)] = grad.reshape(2, 64, 512).astype(BF16)
            return carry

        lax.fori_loop(0, 4, body, 0)
        swaps.append(core_halves(net, k.grad_expand, k.core_expand))

    sum_scatter(net, k.part, scatter_refs(k, "sum"), k.grad_2, meanwhile=expand_gradient, produce=expand_half)
    k.stream.need(dilated=1, mask=1)

    def norm_back(grad, value, stats, affine, outgoing, incoming, store, kept, meanwhile=None):
        mean, inverse = stats[0:1, :], stats[1:2, :]
        gain, bias = affine[0:1, :], affine[1:2, :]

        def normed(at):
            return (value[at, :] - mean) * inverse

        def through(at):
            grad[at, :] = grad[at, :] * slope(gain * normed(at) + bias)

        each_rows(1536, 128, through)
        bias_grad, gain_grad = gradient_sums(
            net, grad, normed, outgoing, incoming, meanwhile=meanwhile
        )
        keep_rows(kept, gain_grad, bias_grad)

        def back(at):
            shared = k.mask[at, :] / counted * gain
            result = gain * grad[at, :] - shared * (bias_grad + normed(at) * gain_grad)
            store(at, (inverse * result).astype(BF16))

        each_rows(1536, 128, back)

    def store_2(at, value):
        k.grad_pad[pl.ds(pl.multiple_of(at.start + 512, 128), 128), :] = value

    def pass_expand():
        k.stream.need(half_pyramid=1)
        begin_early()

        @pl.when(is_late)
        def _():
            pair_sums.go_on(k.half_pyramid)

        swaps.pop().wait()
        add_halves(net, k.grad_expand, k.core_expand, k.half_expand)
        late_moves.extend(along_z(net, k.half_expand, k.z_expand))

    norm_back(
        k.grad_2,
        k.dilated,
        k.stats_2,
        k.affine_2,
        k.out_2,
        k.in_2,
        store_2,
        k.norm_2,
        meanwhile=pass_expand,
    )
    halo = send_halo(net, k.grad_pad)
    zero_margins(k.cells, 8, 128)
    halo.wait()

    def spread(i, carry):
        k.cells[i, 8:136, :] = k.grad_pad[rows_of(i, 128), :].astype(F32)
        for j in range(3):
            start = 8 - 4 * (j - 1)
            k.grad_taps[rows_of(i, 128), j * 128 : j * 128 + 128] = k.cells[
                i, start : start + 128, :
            ].astype(BF16)
        return carry

    lax.fori_loop(0, 20, spread, 0)
    for load in loads:
        load.wait()

    def dilated_rows(i, carry):
        total = 0.0
        for tap in range(3):
            at = pl.ds(pl.multiple_of((i * 3 + 8 - 4 * tap) * 128, 128), 384)
            total = total + mm_t(k.grad_taps[at, :], k.w_taps[tap])
        for b in range(4):
            k.part[b, rows_of(i), :] = total[:, b * 128 : b * 128 + 128]
        return carry

    def dilated_half(half):
        lax.fori_loop(2 * half, 2 * half + 2, dilated_rows, 0)

    def dilated_gradient():
        k.stream.need(hidden=1)

        for i in range(3):

            def body(b, carry):
                band = k.hidden[pl.ds(i * 512, 1536), lane_block(b)]
                grad = tm_m(band, k.grad_taps[pl.ds(512, 1536), :])
                for j in range(3):
                    block = grad[:, j * 128 : j * 128 + 128].reshape(2, 64, 128)
                    rows = slice((i * 3 + j) * 64, (i * 3 + j) * 64 + 64)
                    k.grad_dilated[pl.ds(2 * b, 2), rows, :] = block.astype(BF16)
                return carry

            lax.fori_loop(0, 4, body, 0)
        swaps.append(core_halves(net, k.grad_dilated, k.core_dilated))

    sum_scatter(net, k.part, scatter_refs(k, "sum2"), k.grad_1, meanwhile=dilated_gradient, produce=dilated_half)
    k.stream.need(reduced=1)

    def store_1(at, value):
        k.grad_reduced[at, lane_block(net.m)] = value

    def pass_halves():
        @pl.when(is_late)
        def _():
            pair_sums.finish(k.pyramid_sum)
            to_across.start()

        relay_early()
        swaps.pop().wait()
        add_halves(net, k.grad_dilated, k.core_dilated, k.half_dilated)
        late_moves.extend(along_z(net, k.half_dilated, k.z_dilated))

    norm_back(
        k.grad_1,
        k.reduced,
        k.stats_1,
        k.affine_1,
        k.out_1,
        k.in_1,
        store_1,
        k.norm_1,
        meanwhile=pass_halves,
    )
    gather_blocks(net, lambda b, at: k.grad_reduced.at[at, lane_block(b)], 1536)

    relay_late()
    k.stream.need(x=1)

    def reduce_gradient(b, carry):
        grad = tm_m(k.grad_reduced[:, lane_block(b)], k.x[...])
        k.grad_reduce[pl.ds(2 * b, 2)] = grad.reshape(2, 64, 512).astype(BF16)
        return carry

    lax.fori_loop(0, 4, reduce_gradient, 0)
    swap = core_halves(net, k.grad_reduce, k.core_reduce)

    swap.wait()
    add_halves(net, k.grad_reduce, k.core_reduce, k.half_reduce)
    reduce_moves = along_z(net, k.half_reduce, k.z_reduce, chunk_of(net))

    k.stream.need(shortcut=1, w_reduce=1)

    def input_rows(at):
        total = k.shortcut[at, :]
        for b in range(4):
            total = total + mm_t(k.grad_reduced[at, b * 128 : b * 128 + 128], k.w_reduce[b])
        k.grad_input[at, :] = total

    each_rows(1536, 384, input_rows)
    k.stream.done(grad_input=1)
    for move_ in reduce_moves:
        move_.wait()
    k.sum_reduce[...] = finish_z(net, k.half_reduce, k.z_reduce, chunk_of(net)).astype(BF16)
    wait_reduce = to_owners(
        lambda i: k.sum_reduce.at[:, lanes_for(i)], k.own_reduce, k.local_sems.at[11]
    )
    for move_ in late_moves:
        move_.wait()
    k.sum_dilated[...] = finish_z(net, k.half_dilated, k.z_dilated)
    k.sum_expand[...] = finish_z(net, k.half_expand, k.z_expand)
    wait_pyramid()
    wait_project()
    wait_reduce()


def run_bottleneck_backward(args):
    return call_kernel(
        bottleneck_backward,
        "bottleneck_back",
        3,
        args,
        dict(
            grad_input=((1536, 512), F32),
            norm_2=((8, 128), F32),
            norm_1=((8, 128), F32),
            own_pyramid=((2, 16, 32, 256), BF16),
            own_project=((2, 32, 384), BF16),
            sum_dilated=((576, 128), F32),
            sum_expand=((64, 512), F32),
            own_reduce=((2, 64, 256), BF16),
        ),
        dict(
            grad_taps=pltpu.VMEM((2560, 384), BF16),
            grad_reduced=pltpu.VMEM((1536, 512), BF16),
            **pair_scratch(),
            relay=pltpu.VMEM((2, 2, 16, 32, 256), BF16),
            pyramid_sum=pltpu.VMEM((2, 16, 32, 256), BF16),
            sum_reduce=pltpu.VMEM((64, 512), BF16),
            grad_expand=pltpu.VMEM((8, 64, 512), BF16),
            core_expand=pltpu.VMEM((4, 64, 512), BF16),
            half_expand=pltpu.VMEM((4, 64, 512), BF16),
            z_expand=pltpu.VMEM((3, 64, 512), BF16),
            grad_reduce=pltpu.VMEM((8, 64, 512), BF16),
            core_reduce=pltpu.VMEM((4, 64, 512), BF16),
            half_reduce=pltpu.VMEM((4, 64, 512), BF16),
            z_reduce=pltpu.VMEM((3, 64, 512), BF16),
            grad_dilated=pltpu.VMEM((8, 576, 128), BF16),
            core_dilated=pltpu.VMEM((4, 576, 128), BF16),
            half_dilated=pltpu.VMEM((4, 576, 128), BF16),
            z_dilated=pltpu.VMEM((3, 576, 128), BF16),
            w_taps=pltpu.VMEM((3, 512, 384), BF16),
            part=pltpu.VMEM((4, 1536, 128), F32),
            **scatter_scratch("sum", 1536, 128),
            **scatter_scratch("sum2", 1536, 128),
            grad_2=pltpu.VMEM((1536, 128), F32),
            grad_1=pltpu.VMEM((1536, 128), F32),
            grad_pad=pltpu.VMEM((2560, 128), BF16),
            cells=pltpu.VMEM((20, 144, 128), F32),
            **exchange_scratch(2),
            **exchange_scratch(1),
            local_sems=pltpu.SemaphoreType.DMA((13,)),
        ),
        96,
        hbm=dict(w_dilated=1),
        stream=dict(half_pyramid=1, hidden_two=1, dilated=1, mask=1, hidden=1, reduced=1, x=1, shortcut=1, w_reduce=1, grad_input=1),
    )


def finish(net, k):
    counted = pixel_count(k.boxes)
    odd = lax.rem(lax.axis_index("batch"), 2)

    def rows_for(i):
        return slice(i * 32, i * 32 + 32)

    nothing = jnp.zeros((64, 256), F32)
    for tap in (9, 10, 11, 15, 16, 17, 18, 19, 20, 24, 25, 26):
        k.grad_rates[tap] = nothing
    for slot in range(16):
        for i in range(2):
            block = k.own_pyramid[i, slot].astype(F32)
            if slot == 0:
                k.grad_point[rows_for(i), :] = block
            else:
                tap = slot - 1 if slot < 10 else slot + 2 if slot < 13 else slot + 8
                k.grad_rates[tap, rows_for(i), :] = block
    k.stream.done(grad_rates=1)
    k.stream.need(from_input=1)
    leave = pltpu.make_async_copy(k.from_input, k.grad_input, k.sem.at[0])
    leave.start()
    for y in range(6):
        turned = k.packed[y * 128 : y * 128 + 128, :].astype(F32).T.astype(BF16)
        k.features[y] = turned[0:64, :]
        k.features[y + 6] = turned[64:128, :]
    k.turned[...] = jnp.concatenate([k.own_project[i].astype(F32) for i in range(2)], axis=0).T
    for slot in range(5):
        start = pl.multiple_of(slot * 64 + odd * 32, 32)
        k.grad_project[slot] = k.turned[pl.ds(start, 32), :]
    k.grad_reduce[...] = jnp.concatenate(
        [k.own_reduce[i].astype(F32) for i in range(2)], axis=0
    ).T
    k.grad_dilated[...] = k.from_dilated[...].reshape(9, 64, 128)
    k.grad_expand[...] = k.from_expand[...]
    k.grad_pool[...] = k.from_pool[...]
    k.grad_norm_1[...] = k.norm_1[0:2, :]
    k.grad_norm_2[...] = k.norm_2[0:2, :]
    k.grad_norm_3[...] = k.norm_3[0:2, :]
    for b in range(4):
        k.grad_norm_b[:, b, :] = k.norm_b[0:2, b * 64 : b * 64 + 64]
    k.grad_norm_pool[...] = k.norm_pool[0:2, 0:64]
    k.grad_norm_p[...] = k.norm_p[0:2, 0:64]
    k.grad_head_weight[...] = k.head_sums[0:22, 0:256]
    columns = k.head_sums[:, 256:384].T
    k.grad_head_bias[...] = columns[0:1, 0:22]
    loss = columns[1:2, :]
    task = lax.broadcasted_iota(jnp.int32, (1, 32), 1)

    def total(inside):
        return jnp.sum(jnp.where(inside, loss, 0.0), axis=1, keepdims=True) / counted

    terms = [total(task == 0), total(task == 19), total((task == 20) | (task == 21))]
    lane = lax.broadcasted_iota(jnp.int32, (1, 128), 1)
    losses = jnp.where(lane == 0, terms[0], jnp.where(lane == 1, terms[1], terms[2]))
    log_vars = jnp.where(
        lane == 0, k.log_vars[0], jnp.where(lane == 1, k.log_vars[1], k.log_vars[2])
    )
    weighted = jnp.exp(-log_vars) * losses
    k.total_loss[...] = jnp.sum(
        jnp.where(lane < 3, weighted + log_vars, 0.0), axis=1, keepdims=True
    )
    k.grad_log_vars[...] = (1.0 - weighted)[:, 0:3]

    leave.wait()


def run_finish(args):
    return call_kernel(
        finish,
        "finish",
        None,
        args,
        dict(
            features=((12, 64, 128), BF16),
            total_loss=((1, 1), F32),
            grad_input=((1536, 512), F32),
            grad_reduce=((256, 128), F32),
            grad_dilated=((9, 64, 128), F32),
            grad_expand=((64, 512), F32),
            grad_norm_1=((2, 128), F32),
            grad_norm_2=((2, 128), F32),
            grad_norm_3=((2, 512), F32),
            grad_point=((64, 256), F32),
            grad_rates=((27, 64, 256), F32),
            grad_pool=((64, 256), F32),
            grad_norm_b=((2, 4, 64), F32),
            grad_norm_pool=((2, 64), F32),
            grad_project=((5, 32, 64), F32),
            grad_norm_p=((2, 64), F32),
            grad_head_weight=((22, 256), F32),
            grad_head_bias=((1, 22), F32),
            grad_log_vars=((1, 3), F32),
        ),
        dict(turned=pltpu.VMEM((384, 64), F32), sem=pltpu.SemaphoreType.DMA((1,))),
        0,
        hbm=dict(grad_input=1),
        stream=dict(from_input=1, grad_rates=1),
        smem=dict(boxes=1, log_vars=1),
    )


def fast_local(
    trunk_input,
    conv_reduce,
    conv_dilated,
    conv_expand,
    reduction_norm_params,
    dilated_norm_params,
    expansion_norm_params,
    aspp_point,
    aspp_rates,
    aspp_pool,
    branch_norms,
    pooling_norm_params,
    aspp_project,
    projection_norm_params,
    head_weight,
    head_bias,
    log_vars,
    crop_boxes,
    seg_labels,
    depth_target,
    normal_target,
):
    x = trunk_input.reshape(1536, 512)
    forward = run_bottleneck(
        dict(
            x=x,
            conv_reduce=conv_reduce,
            w_dilated=conv_dilated,
            w_expand=conv_expand,
            aspp_point=aspp_point,
            aspp_rates=aspp_rates,
            project=aspp_project.transpose(1, 0, 2),
            affine_1=reduction_norm_params,
            affine_2=dilated_norm_params,
            affine_3=expansion_norm_params,
            boxes=crop_boxes,
        )
    )
    w_pyramid = forward.w_pyramid.reshape(13, 256, 512)

    middle = run_pyramid(
        dict(
            trunk=forward.trunk,
            mask=forward.mask,
            w_pyramid=w_pyramid,
            branch_norms=branch_norms,
            norm_project=projection_norm_params,
            norm_pooling=pooling_norm_params,
            aspp_pool=aspp_pool,
            w_slots=forward.w_project,
            head_weight=head_weight.T,
            head_bias=head_bias,
            log_vars=log_vars,
            labels=seg_labels.transpose(1, 0, 2),
            depth=depth_target.transpose(1, 0, 2),
            normal=normal_target.transpose(0, 2, 1, 3).reshape(12, 2, 128),
            boxes=crop_boxes,
        )
    )
    back = run_pyramid_backward(
        dict(
            grad_branches=middle.grad_branches,
            w_pyramid=w_pyramid,
            x=x,
            trunk=forward.trunk,
            expanded=forward.expanded,
            stats_3=forward.stats_3,
            affine_3=expansion_norm_params,
            mask=forward.mask,
            grad_pooled=middle.grad_pooled,
            grad_project=middle.grad_project,
            grad_pool=middle.grad_pool,
            boxes=crop_boxes,
        )
    )
    last = run_bottleneck_backward(
        dict(
            grad_expanded=back.grad_expanded,
            shortcut=back.shortcut,
            w_reduce=forward.w_reduce,
            half_pyramid=back.half_pyramid,
            sum_pyramid=back.sum_pyramid,
            sum_project=back.sum_project,
            x=x,
            hidden=forward.hidden,
            hidden_two=forward.hidden_two,
            w_expand=conv_expand,
            w_dilated=conv_dilated,
            dilated=forward.dilated,
            stats_2=forward.stats_2,
            affine_2=dilated_norm_params,
            reduced=forward.reduced,
            stats_1=forward.stats_1,
            affine_1=reduction_norm_params,
            mask=forward.mask,
            boxes=crop_boxes,
        )
    )
    done = run_finish(
        dict(
            from_input=last.grad_input,
            own_pyramid=last.own_pyramid,
            packed=middle.features,
            own_project=last.own_project,
            own_reduce=last.own_reduce,
            from_dilated=last.sum_dilated,
            from_expand=last.sum_expand,
            from_pool=back.sum_pool,
            norm_1=last.norm_1,
            norm_2=last.norm_2,
            norm_3=back.norm_3,
            norm_b=middle.norm_b,
            norm_pool=middle.norm_pool,
            norm_p=middle.norm_p,
            head_sums=middle.head_sums,
            log_vars=log_vars,
            boxes=crop_boxes,
        )
    )
    return (
        done.features.transpose(0, 2, 1).reshape(1, 12, 128, 64),
        done.total_loss.reshape(()),
        done.grad_input.reshape(1, 12, 128, 512),
        done.grad_reduce,
        done.grad_dilated.reshape(3, 3, 64, 128),
        done.grad_expand,
        done.grad_norm_1,
        done.grad_norm_2,
        done.grad_norm_3,
        done.grad_point,
        done.grad_rates.reshape(3, 3, 3, 64, 256),
        done.grad_pool,
        done.grad_norm_b,
        done.grad_norm_pool,
        done.grad_project.transpose(2, 0, 1),
        done.grad_norm_p,
        done.grad_head_weight.T,
        done.grad_head_bias.reshape(22),
        done.grad_log_vars.reshape(3),
    )


def local(
    trunk_input,
    conv_reduce,
    conv_dilated,
    conv_expand,
    reduction_norm_params,
    dilated_norm_params,
    expansion_norm_params,
    aspp_point,
    aspp_rates,
    aspp_pool,
    branch_norms,
    pooling_norm_params,
    aspp_project,
    projection_norm_params,
    head_weight,
    head_bias,
    log_vars,
    crop_boxes,
    seg_labels,
    depth_target,
    normal_target,
):
    image_inputs, tile_row_count, frame_columns, quarter = trunk_input.shape
    pixels = image_inputs * tile_row_count * frame_columns
    branch_part = aspp_point.shape[0]
    branch_total = lax.axis_size("branch")
    row_portion = 1.0 / lax.axis_size("rows")
    image_overall_count = float(crop_boxes.shape[0])
    first_image = lax.axis_index("batch") * image_inputs
    first_row = lax.axis_index("rows") * tile_row_count
    my_boxes = lax.dynamic_slice_in_dim(crop_boxes, first_image, image_inputs, 0)
    row_ids = first_row + jnp.arange(tile_row_count, dtype=jnp.int32)
    col_ids = jnp.arange(frame_columns, dtype=jnp.int32)
    inside_rows = (row_ids[None, :] >= my_boxes[:, 0:1]) & (
        row_ids[None, :] < my_boxes[:, 0:1] + my_boxes[:, 2:3]
    )
    inside_cols = (col_ids[None, :] >= my_boxes[:, 1:2]) & (
        col_ids[None, :] < my_boxes[:, 1:2] + my_boxes[:, 3:4]
    )
    valid_mask = (inside_rows[:, :, None] & inside_cols[:, None, :]).astype(jnp.float32)
    mask_column_vector = valid_mask.reshape(pixels, 1)
    mask_flat = valid_mask.reshape(pixels)
    pixel_number_count = jnp.sum((crop_boxes[:, 2] * crop_boxes[:, 3]).astype(jnp.float32))
    image_areas = (my_boxes[:, 2] * my_boxes[:, 3]).astype(jnp.float32)
    input_full = widen(trunk_input)
    reduced_output = forward_dot(input_full, conv_reduce).reshape(pixels, -1)
    normalized_first, standardized_first, inverse_deviation_first = norm_ahead_pass(
        reduced_output, mask_column_vector, pixel_number_count, reduction_norm_params
    )
    hidden_one = (
        jax.nn.silu(normalized_first)
        .astype(jnp.bfloat16)
        .reshape(image_inputs, tile_row_count, frame_columns, -1)
    )
    hidden_full = widen(pad_rows(hidden_one))
    dilated_out = 0.0
    for row_tap in range(3):
        band = hidden_full[:, 4 * row_tap : 4 * row_tap + tile_row_count]
        for col_tap in range(3):
            dilated_out = dilated_out + forward_dot(
                move(band, -(col_tap - 1) * 4, 2), conv_dilated[row_tap, col_tap]
            )
    normalized_second, standardized_second, inverse_deviation_second = norm_ahead_pass(
        dilated_out.reshape(pixels, -1), mask_column_vector, pixel_number_count, dilated_norm_params
    )
    hidden_two = (
        jax.nn.silu(normalized_second)
        .astype(jnp.bfloat16)
        .reshape(image_inputs, tile_row_count, frame_columns, -1)
    )
    hidden_two_full = widen(hidden_two)
    expanded_output = forward_dot(hidden_two_full, conv_expand).reshape(pixels, -1)
    normalized_third, standardized_third, inverse_deviation_third = norm_ahead_pass(
        expanded_output, mask_column_vector, pixel_number_count, expansion_norm_params
    )
    residual_sum = normalized_third + trunk_input.reshape(pixels, -1).astype(jnp.float32)
    trunk_out = (
        jax.nn.silu(residual_sum)
        .astype(jnp.bfloat16)
        .reshape(image_inputs, tile_row_count, frame_columns, quarter)
    )
    trunk_full = widen(trunk_out)
    branch_outs = [backward_dot(trunk_full, aspp_point)]
    for branch_id in range(3):
        dilation = RATES[branch_id]
        hops = dilation // tile_row_count
        partials = [0.0, 0.0, 0.0]
        for col_tap in range(3):
            shifted = move(trunk_full, -(col_tap - 1) * dilation, 2)
            products = backward_dot(shifted, stacked_taps(aspp_rates[branch_id], col_tap))
            for row_tap in range(3):
                partials[row_tap] = (
                    partials[row_tap]
                    + products[..., row_tap * branch_part : (row_tap + 1) * branch_part]
                )
        upper = send_down(partials[0].astype(jnp.bfloat16), hops).astype(jnp.float32)
        lower_part = send_up(partials[2].astype(jnp.bfloat16), hops).astype(jnp.float32)
        branch_outs.append(partials[1] + upper + lower_part)
    spatial_flattened = jnp.stack(branch_outs, axis=3).reshape(pixels, -1)
    branch_gain_bias = branch_norms.reshape(2, -1)
    normalized_spatial, standardized_spatial, inverse_deviation_spatial = norm_ahead_pass(
        spatial_flattened, mask_column_vector, pixel_number_count, branch_gain_bias
    )
    spatial_act = (
        jax.nn.silu(normalized_spatial)
        .astype(jnp.bfloat16)
        .reshape(image_inputs, tile_row_count, frame_columns, 4, branch_part)
    )
    pooled_local = lax.dot_general(
        valid_mask.astype(jnp.bfloat16),
        trunk_full,
        (((1, 2), (1, 2)), ((0,), (0,))),
        preferred_element_type=jnp.float32,
    )
    pooled = (over_rows(pooled_local) / image_areas[:, None]).astype(jnp.bfloat16)
    pooling_convolution = backward_dot(pooled, aspp_pool)
    normalized_poolbranch, standardized_poolbranch, inverse_deviation_poolbranch = norm_ahead_pass(
        pooling_convolution, row_portion, image_overall_count, pooling_norm_params
    )
    pool_act = jax.nn.silu(normalized_poolbranch).astype(jnp.bfloat16)
    pool_wide = jnp.broadcast_to(
        pool_act[:, None, None, None, :],
        (image_inputs, tile_row_count, frame_columns, 1, branch_part),
    )
    concat = jnp.concatenate([spatial_act, pool_wide], axis=3)
    concat_flat = widen(concat).reshape(pixels, -1)
    proj_kernel = (
        aspp_project.reshape(branch_part, 5, branch_total, branch_part)
        .transpose(0, 2, 1, 3)
        .reshape(branch_part, 5 * branch_total * branch_part)
    )
    projected_output = backward_dot(concat_flat, proj_kernel)
    normalized_projector, standardized_projector, inverse_deviation_projector = norm_ahead_pass(
        projected_output, mask_column_vector, pixel_number_count, projection_norm_params
    )
    features = (
        jax.nn.silu(normalized_projector)
        .astype(jnp.bfloat16)
        .reshape(image_inputs, tile_row_count, frame_columns, -1)
    )
    features_wide = widen(features).reshape(pixels, -1).astype(jnp.float32)
    head_wide = head_weight.astype(jnp.float32)
    logits = jnp.dot(features_wide, head_wide, precision=HIGH) + head_bias
    classes = head_bias.shape[0] - 3
    seg_logits = logits[:, :classes]
    labels_flat = seg_labels.reshape(pixels)
    classes_hot = (labels_flat[:, None] == jnp.arange(classes, dtype=jnp.int32)[None, :]).astype(
        jnp.float32
    )
    cross = jax.nn.logsumexp(seg_logits, axis=1) - jnp.sum(seg_logits * classes_hot, axis=1)
    depth_gap = logits[:, classes] - depth_target.reshape(pixels)
    smooth_abs = jnp.sqrt(depth_gap * depth_gap + 1.0)
    normal_gap = logits[:, classes + 1 :] - jnp.moveaxis(normal_target, 1, 3).reshape(pixels, 2)
    local_losses = jnp.stack(
        [
            jnp.sum(mask_flat * cross),
            jnp.sum(mask_flat * (smooth_abs - 1.0)),
            jnp.sum(mask_flat * jnp.sum(normal_gap * normal_gap, axis=1)),
        ]
    )
    task_weights = jnp.exp(-log_vars)
    grad_seg = (jax.nn.softmax(seg_logits, axis=1) - classes_hot) * (
        task_weights[0] / pixel_number_count * mask_flat
    )[:, None]
    grad_depth = depth_gap / smooth_abs * (task_weights[1] / pixel_number_count * mask_flat)
    grad_normal = 2.0 * normal_gap * (task_weights[2] / pixel_number_count * mask_flat)[:, None]
    grad_logits = jnp.concatenate([grad_seg, grad_depth[:, None], grad_normal], axis=1)
    head_local = lax.dot_general(
        features_wide, grad_logits, (((0,), (0,)), ((), ())), precision=HIGH
    )
    loss_parts, grad_head_weight, grad_head_bias = lax.psum(
        (local_losses, head_local, jnp.sum(grad_logits, axis=0)), ("rows", "batch")
    )
    task_losses = loss_parts / pixel_number_count
    total_loss = jnp.sum(task_weights * task_losses + log_vars)
    grad_log_vars = 1.0 - task_weights * task_losses
    grad_features = jnp.dot(grad_logits, head_wide.T, precision=HIGH)
    my_features_grad = lax.dynamic_slice_in_dim(
        grad_features, lax.axis_index("branch") * branch_part, branch_part, 1
    )
    gradient_before_projector = my_features_grad * silu_slope(normalized_projector)
    grad_proj_in, grad_project_norm = norm_reverse_pass(
        gradient_before_projector,
        standardized_projector,
        inverse_deviation_projector,
        1.0,
        mask_column_vector,
        pixel_number_count,
        projection_norm_params,
    )
    grad_proj_low = grad_proj_in.astype(jnp.bfloat16)
    proj_kernel_grad = lax.dot_general(
        grad_proj_low, concat_flat, (((0,), (0,)), ((), ())), preferred_element_type=jnp.float32
    )
    grad_project_local = (
        proj_kernel_grad.reshape(branch_part, branch_total, 5, branch_part)
        .transpose(0, 2, 1, 3)
        .reshape(branch_part, 5, branch_total * branch_part)
    )
    concat_grad = forward_dot(grad_proj_low, proj_kernel).reshape(
        image_inputs, tile_row_count, frame_columns, -1
    )
    concat_grad = narrow(concat_grad).reshape(pixels, 5, branch_part)
    pool_grad_img = over_rows(
        jnp.sum(concat_grad[:, 4, :].reshape(image_inputs, -1, branch_part), axis=1)
    )
    gradient_before_poolbranch = pool_grad_img * silu_slope(normalized_poolbranch)
    grad_pool_conv, grad_pool_norm = norm_reverse_pass(
        gradient_before_poolbranch,
        standardized_poolbranch,
        inverse_deviation_poolbranch,
        row_portion,
        1.0,
        image_overall_count,
        pooling_norm_params,
    )
    pool_conv_low = grad_pool_conv.astype(jnp.bfloat16)
    grad_pool_local = (
        lax.dot_general(
            pool_conv_low, pooled, (((0,), (0,)), ((), ())), preferred_element_type=jnp.float32
        )
        * row_portion
    )
    pooled_grad = forward_dot(pool_conv_low, aspp_pool)
    gradient_before_spatialbranch = concat_grad[:, :4, :].reshape(pixels, -1) * silu_slope(
        normalized_spatial
    )
    grad_spatial, branch_norm_grad = norm_reverse_pass(
        gradient_before_spatialbranch,
        standardized_spatial,
        inverse_deviation_spatial,
        1.0,
        mask_column_vector,
        pixel_number_count,
        branch_gain_bias,
    )
    grad_branch_norms = branch_norm_grad.reshape(2, 4, branch_part)
    spatial_low = grad_spatial.astype(jnp.bfloat16).reshape(
        image_inputs, tile_row_count, frame_columns, 4, branch_part
    )
    point_grad = spatial_low[:, :, :, 0]
    grad_point_local = pixel_dot(point_grad, trunk_full)
    trunk_grad = forward_dot(point_grad, aspp_point)
    trunk_grad = (
        trunk_grad + valid_mask[..., None] * (pooled_grad / image_areas[:, None])[:, None, None, :]
    )
    rate_grads = []
    for branch_id in range(3):
        dilation = RATES[branch_id]
        hops = dilation // tile_row_count
        centre = spatial_low[:, :, :, branch_id + 1]
        grad_taps = jnp.concatenate(
            [send_up(centre, hops), centre, send_down(centre, hops)], axis=3
        )
        per_col = []
        for col_tap in range(3):
            shifted = move(trunk_full, -(col_tap - 1) * dilation, 2)
            per_col.append(pixel_dot(grad_taps, shifted))
            tap_grad = forward_dot(grad_taps, stacked_taps(aspp_rates[branch_id], col_tap))
            trunk_grad = trunk_grad + move(tap_grad, (col_tap - 1) * dilation, 2)
        col_stack = jnp.stack(per_col, axis=0).reshape(3, 3, branch_part, -1)
        rate_grads.append(col_stack.transpose(1, 0, 2, 3))
    grad_rates_local = jnp.stack(rate_grads, axis=0)
    trunk_own = narrow(trunk_grad).reshape(pixels, -1)
    gradient_shortcut = trunk_own * silu_slope(residual_sum)
    grad_expanded, grad_norm_expand = norm_reverse_pass(
        gradient_shortcut,
        standardized_third,
        inverse_deviation_third,
        1.0,
        mask_column_vector,
        pixel_number_count,
        expansion_norm_params,
    )
    expanded_low = grad_expanded.astype(jnp.bfloat16).reshape(
        image_inputs, tile_row_count, frame_columns, -1
    )
    grad_expand_local = pixel_dot(hidden_two_full, expanded_low)
    hidden_two_grad = narrow(backward_dot(expanded_low, conv_expand)).reshape(pixels, -1)
    gradient_before_second = hidden_two_grad * silu_slope(normalized_second)
    gradient_dilated_input, gradient_dilated_norm = norm_reverse_pass(
        gradient_before_second,
        standardized_second,
        inverse_deviation_second,
        1.0,
        mask_column_vector,
        pixel_number_count,
        dilated_norm_params,
    )
    dilated_lowprec = gradient_dilated_input.astype(jnp.bfloat16).reshape(
        image_inputs, tile_row_count, frame_columns, -1
    )
    dilated_padded = pad_rows(dilated_lowprec)
    hidden_one_grad = 0.0
    kernel_grads = []
    for row_tap in range(3):
        band = hidden_full[:, 4 * row_tap : 4 * row_tap + tile_row_count]
        grad_band = dilated_padded[:, 8 - 4 * row_tap : 8 - 4 * row_tap + tile_row_count]
        for col_tap in range(3):
            kernel_grads.append(pixel_dot(move(band, -(col_tap - 1) * 4, 2), dilated_lowprec))
            hidden_one_grad = hidden_one_grad + backward_dot(
                move(grad_band, (col_tap - 1) * 4, 2), conv_dilated[row_tap, col_tap]
            )
    grad_dilated_local = jnp.stack(kernel_grads, axis=0).reshape(3, 3, hidden_full.shape[3], -1)
    hidden_one_own = narrow(hidden_one_grad).reshape(pixels, -1)
    gradient_before_first = hidden_one_own * silu_slope(normalized_first)
    grad_reduced, grad_norm_reduce = norm_reverse_pass(
        gradient_before_first,
        standardized_first,
        inverse_deviation_first,
        1.0,
        mask_column_vector,
        pixel_number_count,
        reduction_norm_params,
    )
    reduced_low = grad_reduced.astype(jnp.bfloat16).reshape(
        image_inputs, tile_row_count, frame_columns, -1
    )
    grad_reduce_local = pixel_dot(input_full, reduced_low)
    input_grad = narrow(backward_dot(reduced_low, conv_reduce))
    grad_input = input_grad + gradient_shortcut.reshape(
        image_inputs, tile_row_count, frame_columns, quarter
    )
    grad_reduce, grad_dilated, grad_expand, grad_point, grad_rates, grad_pool, grad_project = (
        lax.psum_scatter(grad_reduce_local, ("rows", "batch"), scatter_dimension=0, tiled=True),
        lax.psum_scatter(grad_dilated_local, ("rows", "batch"), scatter_dimension=2, tiled=True),
        lax.psum_scatter(grad_expand_local, ("rows", "batch"), scatter_dimension=0, tiled=True),
        lax.psum_scatter(grad_point_local, ("rows", "batch"), scatter_dimension=1, tiled=True),
        lax.psum_scatter(grad_rates_local, ("rows", "batch"), scatter_dimension=4, tiled=True),
        lax.psum_scatter(grad_pool_local, ("rows", "batch"), scatter_dimension=1, tiled=True),
        lax.psum_scatter(grad_project_local, ("rows", "batch"), scatter_dimension=2, tiled=True),
    )
    return (
        features,
        total_loss,
        grad_input,
        grad_reduce,
        grad_dilated,
        grad_expand,
        grad_norm_reduce,
        gradient_dilated_norm,
        grad_norm_expand,
        grad_point,
        grad_rates,
        grad_pool,
        grad_branch_norms,
        grad_pool_norm,
        grad_project,
        grad_project_norm,
        grad_head_weight,
        grad_head_bias,
        grad_log_vars,
    )


def solution(mesh):
    in_specs = (
        P("batch", "rows", None, "branch"),
        P(None, "branch"),
        P(None, None, None, "branch"),
        P(None, "branch"),
        P(None, "branch"),
        P(None, "branch"),
        P(None, "branch"),
        P("branch", None),
        P(None, None, None, "branch", None),
        P("branch", None),
        P(None, None, "branch"),
        P(None, "branch"),
        P("branch", None, None),
        P(None, "branch"),
        P(),
        P(),
        P(),
        P(),
        P("batch", "rows", None),
        P("batch", "rows", None),
        P("batch", None, "rows", None),
    )
    out_specs = (
        P("batch", "rows", None, "branch"),
        P(),
        P("batch", "rows", None, "branch"),
        P(("rows", "batch"), "branch"),
        P(None, None, ("rows", "batch"), "branch"),
        P(("rows", "batch"), "branch"),
        P(None, "branch"),
        P(None, "branch"),
        P(None, "branch"),
        P("branch", ("rows", "batch")),
        P(None, None, None, "branch", ("rows", "batch")),
        P("branch", ("rows", "batch")),
        P(None, None, "branch"),
        P(None, "branch"),
        P("branch", None, ("rows", "batch")),
        P(None, "branch"),
        P(),
        P(),
        P(),
    )
    small = (mesh.shape["branch"], mesh.shape["rows"], mesh.shape["batch"]) == (4, 2, 4)
    body = fast_local if small else local
    return jax.shard_map(body, mesh=mesh, in_specs=in_specs, out_specs=out_specs, check_vma=False)
```

```python
import types

import jax
import jax.numpy as jnp
from jax import lax
from jax.experimental import pallas as pl
from jax.experimental.pallas import tpu as pltpu
from jax.sharding import PartitionSpec as P

EPS = 1e-05
HIGH = lax.Precision.HIGHEST
RATES = (12, 24, 36)


def padded(cells, sides, width):
    for axis, dim in sides:
        count = lax.axis_size(axis)
        ends = count - 1
        head = lax.slice_in_dim(cells, 0, width, axis=dim)
        tail = lax.slice_in_dim(cells, cells.shape[dim] - width, cells.shape[dim], axis=dim)
        cells = jnp.concatenate(
            [
                lax.ppermute(tail, axis, [(i, (i + 1) % count) for i in range(ends)]),
                cells,
                lax.ppermute(head, axis, [((i + 1) % count, i) for i in range(ends)]),
            ],
            axis=dim,
        )
    return cells


def shifted_2(block, axis, distance):
    devices = range(lax.axis_size(axis))
    route = [(i - distance, i) for i in devices if i - distance in devices]
    return lax.ppermute(block, axis, route)


def move(tensor, offset, axis_id):
    length = tensor.shape[axis_id]
    if offset == 0:
        return tensor
    widths = [(0, 0)] * tensor.ndim
    if offset > 0:
        widths[axis_id] = (offset, 0)
        return lax.slice_in_dim(jnp.pad(tensor, widths), 0, length, axis=axis_id)
    widths[axis_id] = (0, -offset)
    return lax.slice_in_dim(jnp.pad(tensor, widths), -offset, length - offset, axis=axis_id)


def forward_dot(lhs_arr, rhs_arr):
    return jnp.dot(lhs_arr, rhs_arr, preferred_element_type=jnp.float32)


def backward_dot(grad_arr, kernel):
    return lax.dot_general(
        grad_arr,
        kernel,
        (((grad_arr.ndim - 1,), (1,)), ((), ())),
        preferred_element_type=jnp.float32,
    )


def pixel_dot(source, grad_arr):
    return lax.dot_general(
        source, grad_arr, (((0, 1, 2), (0, 1, 2)), ((), ())), preferred_element_type=jnp.float32
    )


def silu_slope(pre_act):
    sigmoid_v = jax.nn.sigmoid(pre_act)
    return sigmoid_v * (1.0 + pre_act * (1.0 - sigmoid_v))


def widen(tensor):
    return lax.all_gather(tensor, "branch", axis=3, tiled=True)


def narrow(tensor):
    return lax.psum_scatter(
        tensor.astype(jnp.bfloat16), "branch", scatter_dimension=3, tiled=True
    ).astype(jnp.float32)


def pad_rows(tensor):
    return padded(tensor, (("rows", 1),), 4)


def send_down(tensor, hops):
    if hops >= lax.axis_size("rows"):
        return jnp.zeros_like(tensor)
    return shifted_2(tensor, "rows", hops)


def send_up(tensor, hops):
    if hops >= lax.axis_size("rows"):
        return jnp.zeros_like(tensor)
    return shifted_2(tensor, "rows", -hops)


def over_rows(tensor):
    return lax.psum(tensor, "rows")


def norm_ahead_pass(tensor, weight, counted, affine):
    summed = lax.psum(jnp.sum(tensor * weight, axis=0), ("rows", "batch"))
    mean_val = summed / counted
    centered = tensor - mean_val
    spread = lax.psum(jnp.sum(weight * centered * centered, axis=0), ("rows", "batch"))
    variance = spread / counted
    inverse = lax.rsqrt(variance + EPS)
    normed = centered * inverse
    return (affine[0] * normed + affine[1], normed, inverse)


def norm_reverse_pass(grad_out, normed, inverse, weight_all, weight_stat, counted, affine):
    grad_bias, grad_gain = lax.psum(
        (jnp.sum(grad_out * weight_all, axis=0), jnp.sum(grad_out * normed * weight_all, axis=0)),
        ("rows", "batch"),
    )
    gain_row = affine[0]
    grad_in = inverse * (
        gain_row * grad_out - weight_stat / counted * gain_row * (grad_bias + normed * grad_gain)
    )
    return (grad_in, jnp.stack([grad_gain, grad_bias]))


def stacked_taps(kernels, col_tap):
    return jnp.concatenate([kernels[0, col_tap], kernels[1, col_tap], kernels[2, col_tap]], axis=0)


MESH = pl.DeviceIdType.MESH
F32 = jnp.float32
BF16 = jnp.bfloat16
VMEM_LIMIT = 60 * 2**20


class Net:
    def __init__(self, send_sems, recv_sems):
        self.m = lax.axis_index("branch")
        self.r = lax.axis_index("rows")
        self.z = lax.axis_index("batch")
        self.send_sems, self.recv_sems, self.count = send_sems, recv_sems, 0
        self.side = (self.m ^ 1, self.r, self.z)
        self.over = (self.m ^ 2, self.r, self.z)
        self.diagonal = (self.m ^ 3, self.r, self.z)
        self.core = (self.m, 1 - self.r, self.z)
        self.slot = self.r * 4 + self.z
        self.group = [
            (self.m, lax.rem(self.r + i, 2), lax.rem(self.z + j, 4))
            for i in range(2)
            for j in range(4)
            if i or j
        ]

    def send(self, src, dst, device):
        i = self.count
        self.count += 1
        copy = pltpu.make_async_remote_copy(
            src_ref=src,
            dst_ref=dst,
            send_sem=self.send_sems.at[i],
            recv_sem=self.recv_sems.at[i],
            device_id=device,
            device_id_type=MESH,
        )
        copy.start()
        return copy


def greet(peers, perhaps=()):
    barrier = pltpu.get_barrier_semaphore()
    for peer in peers:
        pl.semaphore_signal(barrier, inc=1, device_id=peer, device_id_type=MESH)
    awaited = len(peers)
    for peer, there in perhaps:

        @pl.when(there)
        def _(peer=peer):
            pl.semaphore_signal(barrier, inc=1, device_id=peer, device_id_type=MESH)

        awaited = awaited + there.astype(jnp.int32)
    pl.semaphore_wait(barrier, awaited)


def each_rows(total, step, body):
    def run(i, carry):
        body(pl.ds(pl.multiple_of(i * step, step), step))
        return carry

    lax.fori_loop(0, total // step, run, 0)


def lane_block(index, width=128):
    return pl.ds(pl.multiple_of(index * width, width), width)


def wide(tile, width):
    count = width // tile.shape[1]
    return tile if count == 1 else jnp.concatenate([tile] * count, axis=1)


def column_sums(fn, total, width, number):
    step = 16384 // width

    def run(i, sums):
        terms = fn(pl.ds(pl.multiple_of(i * step, step), step))
        return tuple(
            s + jnp.sum(t.reshape(step // 8, 8, width), axis=0) for s, t in zip(sums, terms)
        )

    sums = lax.fori_loop(
        0, total // step, run, tuple(jnp.zeros((8, width), F32) for _ in range(number))
    )
    return [jnp.sum(s, axis=0, keepdims=True) for s in sums]


def fold(row):
    return row + pltpu.roll(wide(row, 128), 64, 1)


def exchange(net, outgoing, incoming, meanwhile=None):
    copies = [net.send(outgoing, incoming.at[net.slot], peer) for peer in net.group]
    incoming[net.slot] = outgoing[...]
    if meanwhile is not None:
        meanwhile()
    for copy in copies:
        copy.wait()


def pack(outgoing, first, second, extra=None):
    for i in range(first.shape[1] // 128):
        outgoing[2 * i : 2 * i + 1, :] = first[:, i * 128 : i * 128 + 128]
        outgoing[2 * i + 1 : 2 * i + 2, :] = second[:, i * 128 : i * 128 + 128]
    if extra is not None:
        outgoing[4:5, :] = extra


def unpack(incoming, width):
    count = width // 128
    firsts = [incoming[:, 2 * i, :] for i in range(count)]
    seconds = [incoming[:, 2 * i + 1, :] for i in range(count)]
    return jnp.concatenate(firsts, axis=1), jnp.concatenate(seconds, axis=1)


def statistics(
    net, value_ref, mask_ref, counts, outgoing, incoming, counted, folded=False, extra=None
):
    total, width = value_ref.shape
    same = fold if folded else (lambda row: row)
    (first,) = column_sums(
        lambda at: (value_ref[at, :] * wide(mask_ref[at, :], width),), total, width, 1
    )
    first = same(first)
    own = jnp.sum(jnp.where(lax.broadcasted_iota(jnp.int32, (8, 128), 0) == net.slot, counts, 0.0), axis=0, keepdims=True)
    centre = first / jnp.maximum(wide(own, width), 1.0)

    def squares(at):
        gap = value_ref[at, :] - centre
        return (gap * gap * wide(mask_ref[at, :], width),)

    second = same(column_sums(squares, total, width, 1)[0])
    pack(outgoing, first, second, extra)
    exchange(net, outgoing, incoming)
    firsts, seconds = unpack(incoming, width)
    numbers = wide(counts, width)
    mean = jnp.sum(firsts, axis=0, keepdims=True) / counted
    drift = firsts / jnp.maximum(numbers, 1.0) - mean
    variance = jnp.sum(seconds + numbers * drift * drift, axis=0, keepdims=True) / counted
    return mean, lax.rsqrt(variance + EPS)


def gather_blocks(net, part, rows, meanwhile=None):
    pieces, size = 4, rows // 4
    own, side, over = net.m, net.m ^ 1, net.m ^ 2

    def at(i):
        return pl.ds(i * size, size)

    to_side, to_over = [], []
    for i in range(pieces):
        j = pieces - 1 - i
        to_side.append(net.send(part(own, at(i)), part(own, at(i)), net.side))
        to_over.append(net.send(part(own, at(j)), part(own, at(j)), net.over))
    passed = []
    for i in range(pieces):
        j = pieces - 1 - i
        to_side[i].wait_recv()
        if i < pieces // 2:
            passed.append(net.send(part(side, at(i)), part(side, at(i)), net.over))
        to_over[i].wait_recv()
        if i < pieces // 2:
            passed.append(net.send(part(over, at(j)), part(over, at(j)), net.side))
    if meanwhile is not None:
        meanwhile()
    for copy in to_side + to_over:
        copy.wait_send()
    for copy in passed:
        copy.wait()


def sum_scatter(net, part, bufs, out, meanwhile=None, produce=None):
    far, to_side, to_over, far_side, far_over, from_side, from_over = bufs
    rows, width = out.shape
    half, step = rows // 2, 16384 // width
    head, tail = pl.ds(0, half), pl.ds(half, half)
    across, side, over = net.m ^ 3, net.m ^ 1, net.m ^ 2

    def fill(target, index, base, count=half):
        size = min(step, count) if count % step == 0 else 64

        def body(at):
            rows_at = pl.ds(pl.multiple_of(at.start + base, size), size)
            target[rows_at, :] = part[index, rows_at, :].astype(BF16)

        each_rows(count, size, body)

    def combine(target, index, base, arrived):
        def body(at):
            rows_at = pl.ds(pl.multiple_of(at.start + base, step), step)
            target[rows_at, :] = (part[index, rows_at, :] + arrived[at, :].astype(F32)).astype(BF16)

        each_rows(half, step, body)

    quarter, first, second = half // 2, [], []
    for i in range(2):
        if produce is not None:
            produce(i)
        at = pl.ds(i * quarter, quarter)
        fill(far, across, i * quarter, quarter)
        first.append(net.send(far.at[at], far_side.at[at], net.side))
        fill(far, across, half + i * quarter, quarter)
        below = pl.ds(half + i * quarter, quarter)
        second.append(net.send(far.at[below], far_over.at[at], net.over))
    fill(to_side, side, 0)
    third = net.send(to_side.at[head], from_side.at[head], net.side)
    fill(to_over, over, half)
    fourth = net.send(to_over.at[tail], from_over.at[tail], net.over)
    for copy in second:
        copy.wait_recv()
    combine(to_side, side, half, far_over)
    fifth = net.send(to_side.at[tail], from_side.at[tail], net.side)
    for copy in first:
        copy.wait_recv()
    combine(to_over, over, 0, far_side)
    sixth = net.send(to_over.at[head], from_over.at[head], net.over)
    if meanwhile is not None:
        meanwhile()
    for copy in (third, fourth, fifth, sixth):
        copy.wait_recv()

    def body(at):
        out[at, :] = (
            part[net.m, at, :] + from_side[at, :].astype(F32) + from_over[at, :].astype(F32)
        )

    each_rows(rows, step, body)
    for copy in (*first, *second, third, fourth, fifth, sixth):
        copy.wait_send()


def gradient_sums(
    net, grad_ref, normed, outgoing, incoming, folded=False, extra=None, meanwhile=None
):
    total, width = grad_ref.shape
    same = fold if folded else (lambda row: row)
    bias, gain = column_sums(
        lambda at: (grad_ref[at, :], grad_ref[at, :] * normed(at)), total, width, 2
    )
    pack(outgoing, same(bias), same(gain), extra)
    exchange(net, outgoing, incoming, meanwhile)
    biases, gains = unpack(incoming, width)
    return jnp.sum(biases, axis=0, keepdims=True), jnp.sum(gains, axis=0, keepdims=True)


def keep_rows(ref, first, second):
    width = ref.shape[1]
    ref[0:1, :] = first
    ref[1:2, :] = second
    ref[2:8, :] = jnp.zeros((6, width), F32)


def pair(a, b):
    low = lax.broadcasted_iota(jnp.int32, (a.shape[0], 128), 1) < 64
    results = []
    for g in range(2):
        left, right = a[:, g * 128 : g * 128 + 128], b[:, g * 128 : g * 128 + 128]
        results.append(jnp.where(low, left, pltpu.roll(right, 64, 1)))
        results.append(jnp.where(low, pltpu.roll(left, 64, 1), right))
    return results


def unpair(blocks):
    low = lax.broadcasted_iota(jnp.int32, blocks[0].shape, 1) < 64
    firsts, seconds = [], []
    for g in range(2):
        left, right = blocks[2 * g], blocks[2 * g + 1]
        firsts.append(jnp.where(low, left, pltpu.roll(right, 64, 1)))
        seconds.append(jnp.where(low, pltpu.roll(left, 64, 1), right))
    return jnp.concatenate(firsts, axis=1), jnp.concatenate(seconds, axis=1)


def split_three(row):
    high = row.astype(BF16)
    rest = row - high.astype(F32)
    middle = rest.astype(BF16)
    low = (rest - middle.astype(F32)).astype(BF16)
    return high, middle, low


def zero_margins(ref, side, width):
    rows, _, lanes = ref.shape
    ref[:, 0:side, :] = jnp.zeros((rows, side, lanes), F32)
    ref[:, side + width : 2 * side + width, :] = jnp.zeros((rows, side, lanes), F32)


def scatter_buffers(rows, width):
    whole, half = pltpu.VMEM((rows, width), BF16), pltpu.VMEM((rows // 2, width), BF16)
    return [whole, whole, whole, half, half, whole, whole]


def sigmoid(u):
    return 0.5 * jnp.tanh(0.5 * u) + 0.5


def slope(u):
    s = sigmoid(u)
    return s * (1.0 + u * (1.0 - s))


def mm(a, b):
    return jnp.dot(a, b, preferred_element_type=F32)


def mm_t(a, b):
    return lax.dot_general(a, b, (((1,), (1,)), ((), ())), preferred_element_type=F32)


def tm_m(a, b):
    return lax.dot_general(a, b, (((0,), (0,)), ((), ())), preferred_element_type=F32)


class Streams:
    def __init__(self, ins, outs, sems):
        self.ins = {n: pltpu.make_async_copy(*pair, sems.at[i]) for i, (n, pair) in enumerate(ins)}
        self.outs = {
            n: pltpu.make_async_copy(*pair, sems.at[len(ins) + i])
            for i, (n, pair) in enumerate(outs)
        }
        self.left = []
        for copy in self.ins.values():
            copy.start()

    def need(self, **names):
        for name in names:
            self.ins.pop(name).wait()

    def done(self, **names):
        for name in names:
            copy = self.outs.pop(name)
            copy.start()
            self.left.append(copy)

    def finish(self):
        self.need(**dict.fromkeys(self.ins))
        self.done(**dict.fromkeys(self.outs))
        for copy in self.left:
            copy.wait()


def call_kernel(
    body, name, number, args, outs, scratch, sems, hbm={}, smem=dict(boxes=1), stream={}
):
    vmem, anywhere = pl.BlockSpec(memory_space=pltpu.VMEM), pl.BlockSpec(memory_space=pl.ANY)
    stream_in = [n for n in args if n in stream]
    stream_out = [n for n in outs if n in stream]
    buffers = {n: pltpu.VMEM(args[n].shape, args[n].dtype) for n in stream_in}
    buffers.update({n: pltpu.VMEM(*outs[n]) for n in stream_out})
    names = [f"far_{n}" if n in stream else n for n in [*args, *outs]]
    names = [*names, *scratch, *buffers, "stream_sems"]
    places = {name: anywhere for name in [*hbm, *stream]}
    places.update({name: pl.BlockSpec(memory_space=pltpu.SMEM) for name in smem})

    def kernel(*refs):
        k = types.SimpleNamespace(**dict(zip(names, refs)))
        held = vars(k)
        k.stream = Streams(
            [(n, (held[f"far_{n}"], held[n])) for n in stream_in],
            [(n, (held[n], held[f"far_{n}"])) for n in stream_out],
            k.stream_sems,
        )
        body(Net(refs[-2], refs[-1]) if sems else None, k)
        k.stream.finish()

    results = pl.pallas_call(
        kernel,
        out_shape=[jax.ShapeDtypeStruct(s, d) for s, d in outs.values()],
        in_specs=[places.get(name, vmem) for name in args],
        out_specs=[places.get(name, vmem) for name in outs],
        scratch_shapes=[
            *scratch.values(),
            *buffers.values(),
            pltpu.SemaphoreType.DMA((max(len(buffers), 1),)),
            *([pltpu.SemaphoreType.DMA((sems,))] * (2 if sems else 0)),
        ],
        name=name,
        compiler_params=pltpu.CompilerParams(
            collective_id=number, has_side_effects=bool(sems), vmem_limit_bytes=VMEM_LIMIT
        ),
    )(*args.values())
    return types.SimpleNamespace(**dict(zip(outs, results)))


def pixel_count(boxes):
    total = boxes[0, 2] * boxes[0, 3]
    for b in range(1, 4):
        total = total + boxes[b, 2] * boxes[b, 3]
    return total.astype(F32)


def tile_counts(net, boxes):
    slot = lax.broadcasted_iota(jnp.int32, (8, 128), 0)
    result = jnp.zeros((8, 128), F32)
    for s in range(8):
        top, height, width = boxes[s % 4, 0], boxes[s % 4, 2], boxes[s % 4, 3]
        first, last = (s // 4) * 12, (s // 4) * 12 + 12
        rows = jnp.minimum(top + height, last) - jnp.maximum(top, first)
        result = jnp.where(slot == s, (jnp.maximum(rows, 0) * width).astype(F32), result)
    return result


def exchange_scratch(label):
    return {
        f"out_{label}": pltpu.VMEM((8, 128), F32),
        f"in_{label}": pltpu.VMEM((8, 8, 128), F32),
    }


def scatter_scratch(label, rows, width):
    return {f"{label}_{i}": b for i, b in enumerate(scatter_buffers(rows, width))}


def scatter_refs(k, label):
    return [getattr(k, f"{label}_{i}") for i in range(7)]


def load_taps(k):
    loads = []
    for i in range(3):
        for j in range(3):
            loads.append(
                pltpu.make_async_copy(
                    k.w_dilated.at[i, j],
                    k.w_taps.at[i, :, pl.ds(j * 128, 128)],
                    k.local_sems.at[i * 3 + j],
                )
            )
            loads[-1].start()
    return loads


def send_halo(net, padded):
    lanes = padded.shape[1]
    padded[pl.ds(pl.multiple_of(net.r * 2048, 128), 512), :] = jnp.zeros((512, lanes), BF16)
    return net.send(
        padded.at[pl.ds(pl.multiple_of(1536 - net.r * 1024, 128), 512)],
        padded.at[pl.ds(pl.multiple_of(net.r * 2048, 128), 512)],
        net.core,
    )


def bottleneck_forward(net, k):
    counted, counts = pixel_count(k.boxes), tile_counts(net, k.boxes)
    loads = load_taps(k)
    own_reduce = pltpu.make_async_copy(
        k.conv_reduce.at[lane_block(net.m, 512)], k.w_reduce.at[net.m], k.local_sems.at[9]
    )
    own_reduce.start()
    greet([net.side, net.over, net.diagonal] + net.group)
    branches = [(net.m ^ 3, net.diagonal), (net.m ^ 1, net.side), (net.m ^ 2, net.over)]
    arrivals = [
        net.send(k.conv_reduce.at[lane_block(b, 512)], k.w_reduce.at[net.m], peer)
        for b, peer in branches
    ]

    top, left_edge = k.boxes[net.z, 0], k.boxes[net.z, 1]
    bottom, right_edge = top + k.boxes[net.z, 2], left_edge + k.boxes[net.z, 3]
    column = lax.broadcasted_iota(jnp.int32, (128, 128), 0)
    column_inside = jnp.where((column >= left_edge) & (column < right_edge), 1.0, 0.0)

    def mask_rows(i, carry):
        row = jnp.full((128, 128), net.r * 12 + i, jnp.int32)
        inside = jnp.where((row >= top) & (row < bottom), column_inside, 0.0)
        k.mask[pl.ds(pl.multiple_of(i * 128, 128), 128), :] = inside
        return carry

    lax.fori_loop(0, 12, mask_rows, 0)
    k.stream.done(mask=1)
    k.stream.need(x=1)

    def reduce_for(b):
        def reduce_rows(at):
            k.part[b, at, :] = mm(k.x[at, :], k.w_reduce[b])

        each_rows(1536, 384, reduce_rows)

    own_reduce.wait()
    reduce_for(net.m)
    arrivals[1].wait()
    reduce_for(net.m ^ 1)
    arrivals[2].wait()
    reduce_for(net.m ^ 2)
    arrivals[0].wait()
    k.stream.done(w_reduce=1)

    def far_half(half):
        for i in (half, half + 2):
            at = pl.ds(i * 384, 384)
            k.part[net.m ^ 3, at, :] = mm(k.x[at, :], k.w_reduce[net.m ^ 3])

    sum_scatter(net, k.part, scatter_refs(k, "sum"), k.reduced, produce=far_half)
    k.stream.done(reduced=1)

    half = pl.ds(pl.multiple_of(net.r * 32, 32), 32)
    late = []

    def weight_block(kind, b):
        lanes = lane_block(b, 512)
        if kind == "edge":
            return k.aspp_rates.at[0, 2 * net.r, :, :, lanes], k.w_pyramid.at[pl.ds(10, 3), net.m]
        if kind == "point":
            return k.aspp_point.at[half, lanes], k.w_pyramid.at[0, net.m, half]
        if kind == "project":
            return k.project.at[:, half], k.w_project.at[net.m, :, half]
        return (
            k.aspp_rates.at[kind, 1, :, half, lanes],
            k.w_pyramid.at[pl.ds(1 + 3 * kind, 3), net.m, half],
        )

    def spread_weights(*kinds):
        for kind in kinds:
            src, dst = weight_block(kind, net.m)
            late.append(pltpu.make_async_copy(src, dst, k.local_sems.at[10 + len(late) // 4]))
            late[-1].start()
            for b, peer in branches:
                src, dst = weight_block(kind, b)
                late.append(net.send(src, dst, peer))

    spread_weights("edge")
    mean, inverse = statistics(net, k.reduced, k.mask, counts, k.out_1, k.in_1, counted)
    keep_rows(k.stats_1, mean, inverse)

    def activate_1(at):
        u = k.affine_1[0:1, :] * ((k.reduced[at, :] - mean) * inverse) + k.affine_1[1:2, :]
        rows_at = pl.ds(pl.multiple_of(at.start + 512, 128), 128)
        k.hidden[rows_at, lane_block(net.m)] = (u * sigmoid(u)).astype(BF16)

    each_rows(1536, 128, activate_1)
    gather_blocks(
        net, lambda b, at: k.hidden.at[pl.ds(at.start + 512, at.size), lane_block(b)], 1536
    )
    halo = send_halo(net, k.hidden)
    spread_weights("project", "point", 0)
    zero_margins(k.left, 8, 128)
    zero_margins(k.right, 8, 128)
    for load in loads:
        load.wait()
    halo.wait()
    k.stream.done(hidden=1)

    def dilated_rows(i, carry):
        total = 0.0
        for tap in range(3):
            rows_at = pl.ds(pl.multiple_of((i * 3 + 4 * tap) * 128, 128), 384)
            total = total + mm(k.hidden[rows_at, :], k.w_taps[tap])
        k.dilated[pl.ds(pl.multiple_of(i * 384, 128), 384), :] = total[:, 128:256]
        k.left[pl.ds(i * 3, 3), 8:136, :] = total[:, 0:128].reshape(3, 128, 128)
        k.right[pl.ds(i * 3, 3), 8:136, :] = total[:, 256:384].reshape(3, 128, 128)
        return carry

    lax.fori_loop(0, 4, dilated_rows, 0)

    def add_columns(i, carry):
        at = pl.ds(pl.multiple_of(i * 128, 128), 128)
        k.dilated[at, :] = k.dilated[at, :] + k.left[i, 4:132, :] + k.right[i, 12:140, :]
        return carry

    lax.fori_loop(0, 12, add_columns, 0)
    k.stream.done(dilated=1)
    mean_2, inverse_2 = statistics(net, k.dilated, k.mask, counts, k.out_2, k.in_2, counted)
    keep_rows(k.stats_2, mean_2, inverse_2)

    def activate_2(at):
        u = k.affine_2[0:1, :] * ((k.dilated[at, :] - mean_2) * inverse_2) + k.affine_2[1:2, :]
        k.hidden_two[at, lane_block(net.m)] = (u * sigmoid(u)).astype(BF16)

    each_rows(1536, 128, activate_2)
    gather_blocks(net, lambda b, at: k.hidden_two.at[at, lane_block(b)], 1536)
    spread_weights(1, 2)
    k.stream.done(hidden_two=1)
    k.stream.need(w_expand=1)

    def expand_rows(at):
        k.expanded[at, :] = mm(k.hidden_two[at, :], k.w_expand[...])

    each_rows(1536, 384, expand_rows)
    k.stream.done(expanded=1)
    mean_3, inverse_3 = statistics(net, k.expanded, k.mask, counts, k.out_3, k.in_3, counted)
    keep_rows(k.stats_3, mean_3, inverse_3)
    def activate_3(at):
        u = k.affine_3[0:1, :] * ((k.expanded[at, :] - mean_3) * inverse_3) + k.affine_3[1:2, :]
        u = u + k.x[at, :].astype(F32)
        k.trunk[at, :] = (u * sigmoid(u)).astype(BF16)

    each_rows(1536, 32, activate_3)
    for copy in late:
        copy.wait()


def run_bottleneck(args):
    return call_kernel(
        bottleneck_forward,
        "bottleneck",
        0,
        args,
        dict(
            mask=((1536, 128), F32),
            w_reduce=((4, 512, 128), BF16),
            w_pyramid=((13, 4, 64, 512), BF16),
            w_project=((4, 5, 64, 256), BF16),
            reduced=((1536, 128), F32),
            stats_1=((8, 128), F32),
            hidden=((2560, 512), BF16),
            dilated=((1536, 128), F32),
            stats_2=((8, 128), F32),
            hidden_two=((1536, 512), BF16),
            expanded=((1536, 512), F32),
            stats_3=((8, 512), F32),
            trunk=((1536, 512), BF16),
        ),
        dict(
            w_taps=pltpu.VMEM((3, 512, 384), BF16),
            part=pltpu.VMEM((4, 1536, 128), F32),
            **scatter_scratch("sum", 1536, 128),
            left=pltpu.VMEM((12, 144, 128), F32),
            right=pltpu.VMEM((12, 144, 128), F32),
            **exchange_scratch(1),
            **exchange_scratch(2),
            **exchange_scratch(3),
            local_sems=pltpu.SemaphoreType.DMA((16,)),
        ),
        96,
        hbm=dict(conv_reduce=1, w_dilated=1, aspp_point=1, aspp_rates=1, project=1, w_pyramid=1, w_project=1),
        stream=dict(x=1, w_expand=1, mask=1, w_reduce=1, reduced=1, hidden=1, dilated=1, hidden_two=1, expanded=1),
    )


def pyramid_forward(net, k):
    counted, counts = pixel_count(k.boxes), tile_counts(net, k.boxes)
    area = (k.boxes[net.z, 2] * k.boxes[net.z, 3]).astype(F32)
    near = [
        (lax.rem(net.m + a, 4), lax.rem(net.r + b, 2), net.z)
        for a in range(4)
        for b in range(2)
        if a or b
    ]
    own_rows = pl.ds(pl.multiple_of(net.r * 32, 32), 32)
    common = (pl.ds(0, 10), slice(None), own_rows)
    every = (slice(None), slice(None), own_rows)
    weight_copies = [
        pltpu.make_async_copy(source.at[view], target.at[view], k.local_sems.at[i])
        for i, (source, target, view) in enumerate(
            (
                (k.far_pyramid, k.w_pyramid, common),
                (k.far_pyramid, k.w_pyramid, pl.ds(10, 3)),
                (k.far_slots, k.w_slots, every),
            )
        )
    ]
    for copy in weight_copies:
        copy.start()
    greet(net.group + [peer for i, peer in enumerate(near) if i])
    weight_copies.append(net.send(k.far_pyramid.at[common], k.w_pyramid.at[common], net.core))
    weight_copies.append(net.send(k.far_slots.at[every], k.w_slots.at[every], net.core))

    for b in range(4):
        k.affine_b[0:2, b * 64 : b * 64 + 64] = k.branch_norms[:, b, :]
    for i in range(2):
        k.affine_p[0:2, i * 64 : i * 64 + 64] = k.norm_project[...]
        k.affine_p[2:4, i * 64 : i * 64 + 64] = k.norm_pooling[...]
    k.head_rows[...] = jnp.zeros((32, 256), F32)
    k.head_rows[0:22, :] = k.head_weight[...].astype(F32)

    k.stream.need(mask=1)

    (own_sum,) = column_sums(
        lambda at: (k.trunk[at, :].astype(F32) * wide(k.mask[at, :], 512),), 1536, 512, 1
    )
    k.out_pool[...] = jnp.broadcast_to(own_sum, (8, 512))
    place = net.m * 2 + net.r
    pool_copies = [net.send(k.out_pool, k.in_pool.at[place], peer) for peer in near]
    k.in_pool[place] = k.out_pool[...]

    zero_margins(k.cells, 40, 128)

    def fill(i, carry):
        at = pl.ds(pl.multiple_of(i * 128, 128), 128)
        k.cells[i, 40:168, :] = k.trunk[at, :].astype(F32)
        return carry

    lax.fori_loop(0, 12, fill, 0)

    def shifted(i, offset):
        cells = k.cells[pl.ds(i * 3, 3), 40 + offset : 168 + offset, :]
        return cells.reshape(384, 512).astype(BF16)

    def rows_of(i):
        return pl.ds(pl.multiple_of(i * 384, 128), 384)

    def edge_rows(i, carry):
        total = 0.0
        for j in range(3):
            total = total + mm_t(shifted(i, 12 * (j - 1)), k.w_pyramid[10 + j].reshape(256, 512))
        k.edge_out[rows_of(i), :] = total.astype(BF16)
        return carry

    weight_copies.pop(1).wait()
    lax.fori_loop(0, 4, edge_rows, 0)
    edge = net.send(k.edge_out, k.edge_in, net.core)

    def outer_rows(i, carry):
        second, third = 0.0, 0.0
        for j in range(3):
            second = second + mm_t(shifted(i, 24 * (j - 1)), k.w_pyramid[4 + j].reshape(256, 512))
        for j in range(3):
            third = third + mm_t(shifted(i, 36 * (j - 1)), k.w_pyramid[7 + j].reshape(256, 512))
        for b, block in enumerate(pair(second, third)):
            k.part[b, rows_of(i), 128:256] = block
        return carry

    def inner_rows(i, carry):
        point = mm_t(k.trunk[rows_of(i), :], k.w_pyramid[0].reshape(256, 512))
        first = k.edge_in[rows_of(i), :].astype(F32)
        for j in range(3):
            first = first + mm_t(shifted(i, 12 * (j - 1)), k.w_pyramid[1 + j].reshape(256, 512))
        for b, block in enumerate(pair(point, first)):
            k.part[b, rows_of(i), 0:128] = block
        return carry

    def alternate(body, half):
        def run(i, carry):
            return body(half + 2 * i, carry)

        lax.fori_loop(0, 2, run, 0)

    def half_tile(half):
        alternate(outer_rows, half)
        if half == 0:
            edge.wait()
        alternate(inner_rows, half)

    for copy in weight_copies:
        copy.wait()
    k.stream.done(w_pyramid=1)

    sum_scatter(net, k.part, scatter_refs(k, "sum"), k.branches, produce=half_tile)

    low_256 = lax.broadcasted_iota(jnp.int32, (256, 128), 1) < 64
    odd = lax.rem(net.m, 2) == 1

    def slot(s):
        lanes = lane_block(net.m // 2)
        block = jnp.concatenate([k.w_slots[b, s, :, lanes] for b in range(4)], axis=0).astype(F32)
        return jnp.where(odd, pltpu.roll(block, 64, 1), block)

    for s in range(0, 4, 2):
        both = jnp.where(low_256, slot(s), pltpu.roll(slot(s + 1), 64, 1))
        k.w_project[:, s * 64 : s * 64 + 128] = both.astype(BF16)
    k.w_slot[...] = jnp.where(low_256, slot(4), 0.0).astype(BF16)
    k.w_pool[0:64, :] = k.aspp_pool[...]
    k.w_pool[64:128, :] = k.aspp_pool[...]

    for copy in pool_copies:
        copy.wait()
    for b in range(4):
        pooled = (k.in_pool[2 * b, 0:1, :] + k.in_pool[2 * b + 1, 0:1, :]) / area
        k.pooled[:, b * 512 : b * 512 + 512] = jnp.broadcast_to(pooled, (16, 512)).astype(BF16)
    pool_conv = mm_t(k.pooled[...], k.w_pool[...])[0:1, :]
    mean, inverse = statistics(
        net, k.branches, k.mask, counts, k.out_1, k.in_1, counted, extra=pool_conv
    )
    every = k.in_1[0:4, 4, :]
    pool_mean = jnp.sum(every, axis=0, keepdims=True) / 4.0
    pool_gap = every - pool_mean
    pool_inverse = lax.rsqrt(jnp.sum(pool_gap * pool_gap, axis=0, keepdims=True) / 4.0 + EPS)
    pool_normed = pool_gap * pool_inverse
    pool_gain, pool_bias = k.affine_p[2:3, :], k.affine_p[3:4, :]
    pool_u = pool_gain * pool_normed + pool_bias
    k.rows_scratch[0:4, :] = pool_u * sigmoid(pool_u)
    pool_act = jnp.broadcast_to(k.rows_scratch[pl.ds(net.z, 1), :], (16, 128)).astype(BF16)

    def normed_branch(at):
        return (k.branches[at, :] - mean) * inverse

    gain_b, bias_b = k.affine_b[0:1, :], k.affine_b[1:2, :]

    def activate_branches(at):
        u = gain_b * normed_branch(at) + bias_b
        k.spatial[at, :] = (u * sigmoid(u)).astype(BF16)

    each_rows(1536, 64, activate_branches)

    pool_row = mm_t(pool_act, k.w_slot[...])[0:1, :]

    def project_rows(i, carry):
        at = pl.ds(pl.multiple_of(i * 192, 64), 192)
        below = pl.ds(pl.multiple_of(i * 192 + 768, 64), 192)
        first = mm_t(k.spatial[at, :], k.w_project[...]) + pool_row
        second = mm_t(k.spatial[below, :], k.w_project[...]) + pool_row
        for b, block in enumerate(pair(first, second)):
            k.part_2[b, at, :] = block
        return carry

    def project_half(half):
        alternate(project_rows, half)

    low_128 = lax.broadcasted_iota(jnp.int32, (128, 128), 1) < 64

    def pair_mask(at):
        below = pl.ds(pl.multiple_of(at.start + 768, 128), 128)
        k.mask_pairs[at, :] = jnp.where(low_128, k.mask[at, :], k.mask[below, :])

    each_rows(768, 128, pair_mask)
    sum_scatter(net, k.part_2, scatter_refs(k, "sum2"), k.projected, produce=project_half)
    mean_p, inverse_p = statistics(
        net, k.projected, k.mask_pairs, counts, k.out_2, k.in_2, counted, folded=True
    )
    gain_p, bias_p = k.affine_p[0:1, :], k.affine_p[1:2, :]

    def normed_projected(at):
        return (k.projected[at, :] - mean_p) * inverse_p

    def activate_projected(at):
        u = gain_p * normed_projected(at) + bias_p
        k.gathered[net.m, at, :] = (u * sigmoid(u)).astype(BF16)

    each_rows(768, 128, activate_projected)
    gather_blocks(net, lambda b, at: k.gathered.at[b, at], 768)

    def spread(source, target):
        def body(at):
            first, second = unpair([source[b, at, :].astype(F32) for b in range(4)])
            target[at, :] = first.astype(BF16)
            target[pl.ds(pl.multiple_of(at.start + 768, 128), 128), :] = second.astype(BF16)

        each_rows(768, 128, body)

    k.features[...] = k.gathered[net.m]
    spread(k.gathered, k.wide_features)

    class_row = lax.broadcasted_iota(jnp.int32, (32, 512), 0)
    is_class, is_depth = class_row < 19, class_row == 19
    is_normal = (class_row == 20) | (class_row == 21)
    tile_row = lax.broadcasted_iota(jnp.int32, (32, 128), 0)
    bias_column = jnp.zeros((32, 128), F32)
    for c in range(22):
        bias_column = jnp.where(tile_row == c, k.head_bias[c], bias_column)
    task = [jnp.exp(jnp.full((32, 128), -k.log_vars[t], F32)) / counted for t in range(3)]
    weight_column = jnp.where(tile_row < 19, task[0], jnp.where(tile_row == 19, task[1], task[2]))
    bias_column, weight_column = wide(bias_column, 512), wide(weight_column, 512)
    k.head[...] = k.head_rows[...].astype(BF16)
    top_row, left_edge = k.boxes[net.z, 0], k.boxes[net.z, 1]
    bottom_row, right_edge = top_row + k.boxes[net.z, 2], left_edge + k.boxes[net.z, 3]
    lane = lax.broadcasted_iota(jnp.int32, (1, 512), 1)

    def four_rows(rows):
        return jnp.concatenate(rows, axis=1)
    loss_sums, bias_sums = 0.0, 0.0
    for chunk in range(3):
        at = pl.ds(chunk * 512, 512)
        logits = mm_t(k.head[...], k.wide_features[at, :]) + bias_column
        row_id, column_id = net.r * 12 + chunk * 4 + lane // 128, lane % 128
        inside = (row_id >= top_row) & (row_id < bottom_row)
        inside = inside & (column_id >= left_edge) & (column_id < right_edge)
        inside = jnp.where(inside, 1.0, 0.0)
        span = range(chunk * 4, chunk * 4 + 4)
        label = four_rows([k.labels[y] for y in span])
        target = jnp.where(is_depth, four_rows([k.depth[y] for y in span]), 0.0)
        for n in range(2):
            normal = four_rows([k.normal[y, n : n + 1, :] for y in span])
            target = jnp.where(class_row == 20 + n, normal, target)
        top = jnp.max(jnp.where(is_class, logits, -jnp.inf), axis=0, keepdims=True)
        powers = jnp.where(is_class, jnp.exp(jnp.where(is_class, logits - top, 0.0)), 0.0)
        power_sum = jnp.sum(powers, axis=0, keepdims=True)
        onehot = jnp.where(class_row == label, 1.0, 0.0)
        cross = jnp.log(power_sum) + top - jnp.sum(logits * onehot, axis=0, keepdims=True)
        gap = logits - target
        smooth = jnp.sqrt(gap * gap + 1.0)
        loss = jnp.where(class_row == 0, cross, 0.0)
        loss = jnp.where(is_depth, smooth - 1.0, loss)
        loss = jnp.where(is_normal, gap * gap, loss) * inside
        grad = jnp.where(is_class, powers / power_sum - onehot, 0.0)
        grad = jnp.where(is_depth, gap / smooth, grad)
        grad = jnp.where(is_normal, 2.0 * gap, grad) * (weight_column * inside)
        loss_sums = loss_sums + jnp.sum(loss, axis=1, keepdims=True)
        bias_sums = bias_sums + jnp.sum(grad, axis=1, keepdims=True)
        high = grad.astype(BF16)
        k.grad_logits[0:32, at] = high
        k.grad_logits[32:64, at] = (grad - high.astype(F32)).astype(BF16)
    head_terms = mm(k.grad_logits[...], k.wide_features[...])
    k.out_head[:, 0:256] = head_terms[0:32, :] + head_terms[32:64, :]
    first_lane = lax.broadcasted_iota(jnp.int32, (32, 128), 1) == 0
    k.out_head[:, 256:384] = jnp.where(first_lane, bias_sums, loss_sums)
    quarter = pl.ds(pl.multiple_of(net.m * 8, 8), 8)
    head_copies = [
        net.send(k.out_head.at[quarter], k.in_head.at[net.slot], peer) for peer in net.group
    ]
    k.in_head[net.slot] = k.out_head[quarter, :]

    own_head = k.head_rows[:, lane_block(net.m // 2)]
    own_head = jnp.where(odd, pltpu.roll(own_head, 64, 1), own_head)
    own_head = jnp.where(low_128[0:32, :], own_head, 0.0)
    head_low = jnp.concatenate([own_head, own_head], axis=0).astype(BF16)
    own_head = pltpu.roll(own_head, 64, 1)
    head_high = jnp.concatenate([own_head, own_head], axis=0).astype(BF16)
    k.grad_p[...] = tm_m(k.grad_logits[:, 0:768], head_low) + tm_m(
        k.grad_logits[:, 768:1536], head_high
    )

    def back_features(at):
        k.grad_p[at, :] = k.grad_p[at, :] * slope(gain_p * normed_projected(at) + bias_p)

    each_rows(768, 128, back_features)
    bias_grad, gain_grad = gradient_sums(
        net, k.grad_p, normed_projected, k.out_3, k.in_3, folded=True
    )
    keep_rows(k.norm_p, gain_grad, bias_grad)

    def back_projected(at):
        shared = k.mask_pairs[at, :] / counted * gain_p
        grad = gain_p * k.grad_p[at, :] - shared * (bias_grad + normed_projected(at) * gain_grad)
        k.gathered_grad[net.m, at, :] = (inverse_p * grad).astype(BF16)

    each_rows(768, 128, back_projected)
    gather_blocks(net, lambda b, at: k.gathered_grad.at[b, at], 768)
    spread(k.gathered_grad, k.grad_projected)
    (pixel_sum,) = column_sums(lambda at: (k.grad_projected[at, :].astype(F32),), 1536, 256, 1)
    row_16 = lax.broadcasted_iota(jnp.int32, (16, 256), 0)
    terms = jnp.zeros((16, 256), F32)
    for i, term in enumerate(split_three(pixel_sum)):
        terms = jnp.where(row_16 == i, term.astype(F32), terms)
    terms = terms.astype(BF16)
    tall = jnp.concatenate([terms] * 8, axis=0)
    pool_grad = jnp.sum(mm(tall, k.w_slot[...]), axis=0, keepdims=True) * 0.125

    def project_gradient():
        for b in range(2):
            lanes = slice(b * 128, b * 128 + 128)
            grad = tm_m(k.grad_projected[:, lanes], k.spatial[...])
            k.grad_project[b * 4 : b * 4 + 4, :, 0:256] = grad.reshape(4, 32, 256).astype(BF16)
        grad = tm_m(terms, pool_act)
        k.grad_project[:, :, 256:384] = grad.reshape(8, 32, 128).astype(BF16)

    def back_spatial(at):
        grad = mm(k.grad_projected[at, :], k.w_project[...])
        k.grad_b[at, :] = grad * slope(gain_b * normed_branch(at) + bias_b)

    each_rows(1536, 128, back_spatial)
    bias_grad_b, gain_grad_b = gradient_sums(
        net,
        k.grad_b,
        normed_branch,
        k.out_4,
        k.in_4,
        extra=pool_grad,
        meanwhile=project_gradient,
    )
    keep_rows(k.norm_b, gain_grad_b, bias_grad_b)

    pool_terms = k.in_4[0:4, 4, :] + k.in_4[4:8, 4, :]
    pool_terms = pool_terms * slope(pool_u)
    pool_bias_grad = jnp.sum(pool_terms, axis=0, keepdims=True)
    pool_gain_grad = jnp.sum(pool_terms * pool_normed, axis=0, keepdims=True)
    keep_rows(k.norm_pool, pool_gain_grad, pool_bias_grad)
    pool_back = pool_inverse * (
        pool_gain * pool_terms
        - pool_gain / 4.0 * (pool_bias_grad + pool_normed * pool_gain_grad)
    )
    low = lax.broadcasted_iota(jnp.int32, (4, 128), 1) < 64
    k.rows_scratch[4:8, :] = jnp.where(low, pool_back, 0.0)
    grad_conv = jnp.broadcast_to(k.rows_scratch[pl.ds(net.z + 4, 1), :], (16, 128)).astype(BF16)
    spread_back = mm(grad_conv, k.w_pool[...])[0:8, :]
    for b in range(4):
        k.out_back[b] = spread_back[:, b * 512 : b * 512 + 512]
    back_copies = [
        net.send(k.out_back.at[lax.rem(net.m + a, 4)], k.in_back.at[a], (lax.rem(net.m + a, 4), net.r, net.z))
        for a in range(1, 4)
    ]

    only_first = lax.broadcasted_iota(jnp.int32, (16, 128), 0) == 0
    one_row = jnp.where(only_first, grad_conv.astype(F32) * 0.5, 0.0).astype(BF16)
    for e in range(8):
        grad = tm_m(one_row, k.pooled[:, e * 256 : e * 256 + 256])
        k.grad_pool[e] = grad[0:64, :].astype(BF16)

    def back_branches(at):
        shared = wide(k.mask[at, :], 256) / counted * gain_b
        grad = gain_b * k.grad_b[at, :] - shared * (bias_grad_b + normed_branch(at) * gain_grad_b)
        k.grad_branches[at, :] = (inverse * grad).astype(BF16)

    for copy in back_copies:
        copy.wait()
    k.grad_pooled[...] = (k.out_back[net.m] + k.in_back[1] + k.in_back[2] + k.in_back[3]) / area
    for copy in head_copies:
        copy.wait()
    k.head_sums[quarter, :] = jnp.sum(k.in_head[...], axis=0)
    head_copies = [
        net.send(k.head_sums.at[quarter], k.head_sums.at[quarter], (lax.rem(net.m + a, 4), net.r, net.z))
        for a in range(1, 4)
    ]
    each_rows(1536, 64, back_branches)
    for copy in head_copies:
        copy.wait()


def run_pyramid(args):
    return call_kernel(
        pyramid_forward,
        "pyramid",
        1,
        args,
        dict(
            w_pyramid=((13, 4, 64, 512), BF16),
            features=((768, 128), BF16),
            norm_p=((8, 128), F32),
            grad_project=((8, 32, 384), BF16),
            grad_pool=((8, 64, 256), BF16),
            norm_b=((8, 256), F32),
            norm_pool=((8, 128), F32),
            grad_branches=((1536, 256), BF16),
            grad_pooled=((8, 512), F32),
            head_sums=((32, 384), F32),
        ),
        dict(
            w_slots=pltpu.VMEM((4, 5, 64, 256), BF16),
            local_sems=pltpu.SemaphoreType.DMA((3,)),
            affine_b=pltpu.VMEM((8, 256), F32),
            affine_p=pltpu.VMEM((8, 128), F32),
            head_rows=pltpu.VMEM((32, 256), F32),
            head=pltpu.VMEM((32, 256), BF16),
            pooled=pltpu.VMEM((16, 2048), BF16),
            spatial=pltpu.VMEM((1536, 256), BF16),
            grad_projected=pltpu.VMEM((1536, 256), BF16),
            w_project=pltpu.VMEM((256, 256), BF16),
            w_slot=pltpu.VMEM((256, 128), BF16),
            w_pool=pltpu.VMEM((128, 2048), BF16),
            mask_pairs=pltpu.VMEM((768, 128), F32),
            out_pool=pltpu.VMEM((8, 512), F32),
            in_pool=pltpu.VMEM((8, 8, 512), F32),
            cells=pltpu.VMEM((12, 208, 512), F32),
            edge_out=pltpu.VMEM((1536, 256), BF16),
            edge_in=pltpu.VMEM((1536, 256), BF16),
            part=pltpu.VMEM((4, 1536, 256), F32),
            **scatter_scratch("sum", 1536, 256),
            branches=pltpu.VMEM((1536, 256), F32),
            rows_scratch=pltpu.VMEM((8, 128), F32),
            part_2=pltpu.VMEM((4, 768, 128), F32),
            **scatter_scratch("sum2", 768, 128),
            projected=pltpu.VMEM((768, 128), F32),
            gathered=pltpu.VMEM((4, 768, 128), BF16),
            wide_features=pltpu.VMEM((1536, 256), BF16),
            grad_logits=pltpu.VMEM((64, 1536), BF16),
            out_head=pltpu.VMEM((32, 384), F32),
            in_head=pltpu.VMEM((8, 8, 384), F32),
            grad_p=pltpu.VMEM((768, 128), F32),
            gathered_grad=pltpu.VMEM((4, 768, 128), BF16),
            grad_b=pltpu.VMEM((1536, 256), F32),
            out_back=pltpu.VMEM((4, 8, 512), F32),
            in_back=pltpu.VMEM((4, 8, 512), F32),
            **exchange_scratch(1),
            **exchange_scratch(2),
            **exchange_scratch(3),
            **exchange_scratch(4),
        ),
        96,
        smem=dict(boxes=1, head_bias=1, log_vars=1),
        hbm=dict(far_pyramid=1, far_slots=1),
        stream=dict(mask=1, w_pyramid=1),
    )


def core_halves(net, whole, arrived):
    away = pl.ds(pl.multiple_of(4 - 4 * net.r, 4), 4)
    return net.send(whole.at[away], arrived, net.core)


def add_halves(net, whole, arrived, target):
    for z in range(4):
        total = whole[4 * net.r + z].astype(F32) + arrived[z].astype(F32)
        target[z] = total.astype(target.dtype)


def chunk_of(net):
    return lambda z: 2 * lax.rem(z + net.m, 2) + z // 2


def along_z(net, source, target, chunk=lambda z: z):
    copies = []
    for d in (1, 2, 3):
        there = lax.rem(net.z + d, 4)
        copies.append(
            net.send(source.at[chunk(there)], target.at[d - 1], (net.m, net.r, there))
        )
    return copies


def finish_z(net, half, arrived, chunk=lambda z: z):
    return half[chunk(net.z)].astype(F32) + sum(arrived[d].astype(F32) for d in range(3))


class PairSums:
    def __init__(self, net, half, other, pair, last):
        self.net, self.half, self.other, self.pair, self.last = net, half, other, pair, last
        kept, away = lax.rem(net.z + net.m, 2), lax.rem(net.z + net.m + 1, 2)
        self.kept = 2 * kept
        beside = net.z + 1 - 2 * lax.rem(net.z, 2)
        self.first = self.copy(half.at[pl.ds(2 * away, 2)], other, beside)
        self.high = net.z // 2
        self.second = self.copy(pair.at[1 - self.high], last, net.z + 2 - 4 * self.high)

    def copy(self, src, dst, z):
        net, i = self.net, self.net.count
        net.count += 1
        return pltpu.make_async_remote_copy(
            src_ref=src,
            dst_ref=dst,
            send_sem=net.send_sems.at[i],
            recv_sem=net.recv_sems.at[i],
            device_id=(net.m, net.r, z),
            device_id_type=MESH,
        )

    def begin(self):
        self.first.start()

    def go_on(self, half):
        self.first.wait()

        def body(i, carry):
            for h in range(2):
                total = half[self.kept + h, i].astype(F32) + self.other[h, i].astype(F32)
                self.pair[h, i] = total.astype(BF16)
            return carry

        lax.fori_loop(0, half.shape[1], body, 0)
        self.second.start()

    def finish(self, target):
        self.second.wait()

        def body(i, carry):
            total = self.pair[self.high, i].astype(F32) + self.last[i].astype(F32)
            target[0, i] = total[:, 0:256].astype(BF16)
            target[1, i] = total[:, 256:512].astype(BF16)
            return carry

        lax.fori_loop(0, target.shape[1], body, 0)


def pyramid_backward(net, k):
    counted = pixel_count(k.boxes)
    greet([net.side, net.over] + net.group)
    k.blocks[net.m] = k.grad_branches[...]
    small = [
        core_halves(net, k.grad_project, k.core_project),
        core_halves(net, k.grad_pool, k.core_pool),
    ]
    for c in range(4):
        zero_margins(k.cells.at[c], 40, 128)

    def rows_of(i, size=384):
        return pl.ds(pl.multiple_of(i * size, 128), size)

    low = lax.broadcasted_iota(jnp.int32, (128, 128), 1) < 64
    near = net.m // 2
    far = 1 - near
    mine_first = net.r == near
    mine_second = net.r == far

    def both(source, pair_of, i, lane):
        at = slice(lane * 128, lane * 128 + 128)
        left = source[2 * pair_of, rows_of(i, 128), at].astype(F32)
        right = source[2 * pair_of + 1, rows_of(i, 128), at].astype(F32)
        first = jnp.where(low, left, pltpu.roll(right, 64, 1))
        return first, jnp.where(low, pltpu.roll(left, 64, 1), right)

    def shift_rows(pair_of, i, cell, rate, base):
        for j in range(3):
            start = 40 - rate * (j - 1)
            block = k.cells[cell, i, start : start + 128, :].astype(BF16)
            k.shifts[base + j, rows_of(i, 128), lane_block(pair_of)] = block

    def build(pair_of):
        def fill(i, carry):
            point, first = both(k.blocks, pair_of, i, 0)
            k.shifts[0, rows_of(i, 128), lane_block(pair_of)] = point.astype(BF16)
            second, third = both(k.blocks, pair_of, i, 1)
            k.cells[0, i, 40:168, :] = first
            k.cells[1, i, 40:168, :] = second
            k.cells[2, i, 40:168, :] = third
            return carry

        lax.fori_loop(0, 12, fill, 0)

        def spread(i, carry):
            for cell, rate, base in ((0, 12, 1), (1, 24, 4), (2, 36, 7)):
                shift_rows(pair_of, i, cell, rate, base)
            return carry

        lax.fori_loop(0, 12, spread, 0)

    def build_edge(pair_of):
        def fill(i, carry):
            k.cells[3, i, 40:168, :] = both(k.other, pair_of, i, 0)[1]
            return carry

        lax.fori_loop(0, 12, fill, 0)

        def spread(i, carry):
            shift_rows(pair_of, i, 3, 12, 10)
            return carry

        lax.fori_loop(0, 12, spread, 0)

    def weight_gradients(pair_of):
        owners = pl.ds(4 * pair_of, 4)

        def run(start, stop, shift):
            def body(t, carry):
                grad = tm_m(k.shifts[t, :, lane_block(pair_of)], k.trunk[...])
                k.grad_pyramid[owners, t + shift] = grad.reshape(4, 32, 512).astype(BF16)
                return carry

            lax.fori_loop(start, stop, body, 0)

        run(0, 1, 0)
        run(1, 4, 3)
        run(4, 10, 6)
        run(10, 13, net.r * 6 - 9)
        for j in range(3):
            k.grad_pyramid[owners, 7 - net.r * 6 + j] = jnp.zeros((4, 32, 512), BF16)

    def beside(pair_of):
        view = (pl.ds(2 * pair_of, 2), slice(None), pl.ds(0, 128))
        return net.send(k.blocks.at[view], k.other.at[pl.ds(2 * pair_of, 2)], net.core)

    def to_core(pair_of):
        i = net.count
        net.count += 1
        return pltpu.make_async_remote_copy(
            src_ref=k.grad_pyramid.at[pl.ds(4 * pair_of, 4)],
            dst_ref=k.core_pyramid,
            send_sem=net.send_sems.at[i],
            recv_sem=net.recv_sems.at[i],
            device_id=net.core,
            device_id_type=MESH,
        )

    def add_core(pair_of):
        def body(i, carry):
            for z in range(4):
                total = k.grad_pyramid[4 * pair_of + z, i].astype(F32)
                total = total + k.core_pyramid[z, i].astype(F32)
                k.half_pyramid[z, i] = total.astype(BF16)
            return carry

        lax.fori_loop(0, 16, body, 0)

    first_swap = []

    def near_pair():
        copy = beside(near)
        build(near)
        copy.wait()
        build_edge(near)
        k.stream.need(trunk=1)
        weight_gradients(near)
        first_swap.append(to_core(near))
        pl.when(mine_second)(first_swap[0].start)

    gather_blocks(net, lambda b, at: k.blocks.at[b, at], 1536, meanwhile=near_pair)
    copy = beside(far)
    build(far)
    for swap in small:
        swap.wait()
    add_halves(net, k.grad_project, k.core_project, k.half_project)
    add_halves(net, k.grad_pool, k.core_pool, k.half_pool)
    small_moves = along_z(net, k.half_project, k.z_project, chunk_of(net))
    small_moves = small_moves + along_z(net, k.half_pool, k.z_pool)
    copy.wait()
    build_edge(far)
    pair_sums = PairSums(net, k.half_pyramid, k.z_other, k.z_pair, k.z_last)

    @pl.when(mine_first)
    def _():
        first_swap[0].wait_recv()
        add_core(near)
        pair_sums.begin()

    def trunk_rows(i, carry):
        total = 0.0
        for t in range(13):
            total = total + mm(k.shifts[t, rows_of(i), :], k.w_pyramid[t])
        k.shortcut[rows_of(i), :] = total
        return carry

    k.stream.need(w_pyramid=1, expanded=1, x=1, mask=1)
    lax.fori_loop(0, 4, trunk_rows, 0)
    mean, inverse = k.stats_3[0:1, :], k.stats_3[1:2, :]
    gain, bias = k.affine_3[0:1, :], k.affine_3[1:2, :]
    pooled = k.grad_pooled[0:1, :]

    def normed(at):
        return (k.expanded[at, :] - mean) * inverse

    def back_trunk(at):
        u = gain * normed(at) + bias + k.x[at, :].astype(F32)
        grad = k.shortcut[at, :] + wide(k.mask[at, :], 512) * pooled
        k.shortcut[at, :] = grad * slope(u)

    each_rows(1536, 32, back_trunk)
    k.stream.done(shortcut=1)

    second_swap = to_core(far)

    def far_gradients():
        weight_gradients(far)

        @pl.when(mine_first)
        def _():
            second_swap.start()
            pair_sums.go_on(k.half_pyramid)

    bias_grad, gain_grad = gradient_sums(
        net, k.shortcut, normed, k.out_1, k.in_1, meanwhile=far_gradients
    )
    keep_rows(k.norm_3, gain_grad, bias_grad)

    def back_expanded(at):
        shared = wide(k.mask[at, :], 512) / counted * gain
        grad = gain * k.shortcut[at, :] - shared * (bias_grad + normed(at) * gain_grad)
        k.grad_expanded[at, :] = (inverse * grad).astype(BF16)

    each_rows(1536, 32, back_expanded)
    k.stream.done(grad_expanded=1)
    for move_ in small_moves:
        move_.wait()
    k.sum_project[...] = finish_z(net, k.half_project, k.z_project, chunk_of(net)).astype(BF16)
    k.sum_pool[...] = finish_z(net, k.half_pool, k.z_pool)

    @pl.when(mine_second)
    def _():
        first_swap[0].wait_send()
        second_swap.wait_recv()
        add_core(far)

    @pl.when(mine_first)
    def _():
        second_swap.wait_send()
        pair_sums.finish(k.sum_pyramid)


def pair_scratch():
    return dict(
        z_other=pltpu.VMEM((2, 16, 32, 512), BF16),
        z_pair=pltpu.VMEM((2, 16, 32, 512), BF16),
        z_last=pltpu.VMEM((16, 32, 512), BF16),
    )


def run_pyramid_backward(args):
    return call_kernel(
        pyramid_backward,
        "pyramid_back",
        2,
        args,
        dict(
            shortcut=((1536, 512), F32),
            grad_expanded=((1536, 512), BF16),
            norm_3=((8, 512), F32),
            half_pyramid=((4, 16, 32, 512), BF16),
            sum_pyramid=((2, 16, 32, 256), BF16),
            sum_project=((32, 384), BF16),
            sum_pool=((64, 256), F32),
        ),
        dict(
            half_project=pltpu.VMEM((4, 32, 384), BF16),
            half_pool=pltpu.VMEM((4, 64, 256), BF16),
            **pair_scratch(),
            z_project=pltpu.VMEM((3, 32, 384), BF16),
            z_pool=pltpu.VMEM((3, 64, 256), BF16),
            grad_pyramid=pltpu.VMEM((8, 16, 32, 512), BF16),
            core_pyramid=pltpu.VMEM((4, 16, 32, 512), BF16),
            core_project=pltpu.VMEM((4, 32, 384), BF16),
            core_pool=pltpu.VMEM((4, 64, 256), BF16),
            blocks=pltpu.VMEM((4, 1536, 256), BF16),
            other=pltpu.VMEM((4, 1536, 128), BF16),
            cells=pltpu.VMEM((4, 12, 208, 128), F32),
            shifts=pltpu.VMEM((13, 1536, 256), BF16),
            **exchange_scratch(1),
        ),
        48,
        stream=dict(w_pyramid=1, expanded=1, x=1, mask=1, trunk=1, shortcut=1, grad_expanded=1),
    )


def bottleneck_backward(net, k):
    counted = pixel_count(k.boxes)
    loads = load_taps(k)
    high, source = net.z // 2, net.slot // 2
    here = net.m * 8 + net.slot
    owners, givers = [], []
    for i in range(2):
        part = 2 * net.m + i
        column = 2 * net.r + lax.rem(net.z + net.m, 2)
        owners.append((column, part // 4, lax.rem(part, 4)))
        givers.append((source, net.m // 2, lax.rem(net.m + source, 2) + 2 * i))

    def elsewhere(device):
        return device[0] * 8 + device[1] * 4 + device[2] != here

    moves = elsewhere(owners[0])
    stays = jnp.logical_not(moves)
    greet(
        [net.side, net.over, net.diagonal] + net.group + [owners[1]],
        [(owners[0], moves), (givers[0], elsewhere(givers[0])), (givers[1], elsewhere(givers[1]))],
    )

    def to_owners(views, arrived, sem):
        base = net.count
        net.count += 2

        def copy(i, g, device):
            return pltpu.make_async_remote_copy(
                src_ref=views(i),
                dst_ref=arrived.at[g],
                send_sem=net.send_sems.at[base + i],
                recv_sem=net.recv_sems.at[base + g],
                device_id=device,
                device_id_type=MESH,
            )

        first, second = copy(0, high, owners[0]), copy(1, high, owners[1])
        kept = pltpu.make_async_copy(views(0), arrived.at[high], sem)

        def begin():
            pl.when(moves)(first.start)
            pl.when(stays)(kept.start)
            second.start()

        def wait():
            pl.when(moves)(first.wait_send)
            pl.when(stays)(kept.wait)
            second.wait_send()
            for g in range(2):
                pl.when(elsewhere(givers[g]))(copy(0, g, owners[1]).wait_recv)

        begin()
        return wait

    def lanes_for(i):
        return pl.ds(i * 256, 256)

    early = net.r == net.m // 2
    is_late = net.r == 1 - net.m // 2
    pair_sums = PairSums(net, k.far_half_pyramid, k.z_other, k.z_pair, k.z_last)

    odd_z = lax.rem(net.z, 2)
    lone = early & (odd_z == 0)
    beside = early & (odd_z == 1)
    stay = pltpu.make_async_copy(k.pyramid_sum, k.relay.at[0], k.local_sems.at[9])

    def remote(src, dst, send, arrive, device):
        return pltpu.make_async_remote_copy(
            src_ref=src,
            dst_ref=dst,
            send_sem=net.send_sems.at[send],
            recv_sem=net.recv_sems.at[arrive],
            device_id=device,
            device_id_type=MESH,
        )

    base = net.count
    net.count += 6
    to_side = remote(k.pyramid_sum, k.relay.at[0], base, base, net.side)
    across = (net.m ^ (2 + odd_z), net.r, net.z)
    to_across = remote(k.pyramid_sum, k.relay.at[1], base + 1, base + 1, across)
    plane = lax.rem(net.m + net.z, 2)

    def forward(e, i):
        device = (net.m, net.r if e == 0 else 1 - net.r, 2 * plane + i)
        return remote(
            k.relay.at[e, i], k.own_pyramid.at[high], base + 2 + 2 * e + i, base + 2 + high, device
        )

    forwards = [[forward(e, i) for i in range(2)] for e in range(2)]
    keep = pltpu.make_async_copy(k.relay.at[0, odd_z], k.own_pyramid.at[high], k.local_sems.at[12])
    keeps = early & (plane == high)

    def kept_here(i):
        return keeps & (odd_z == i)

    def begin_early():
        pl.when(lone)(stay.start)
        pl.when(beside)(to_side.start)

    def relay_early():
        pl.when(lone)(stay.wait)
        pl.when(beside)(to_side.wait)
        for i in range(2):
            pl.when(early & jnp.logical_not(kept_here(i)))(forwards[0][i].start)
        pl.when(keeps)(keep.start)

    def relay_late():
        pl.when(early)(to_across.wait_recv)
        for i in range(2):
            pl.when(early)(forwards[1][i].start)

    def wait_pyramid():
        pl.when(is_late)(to_across.wait_send)
        for i in range(2):
            pl.when(early & jnp.logical_not(kept_here(i)))(forwards[0][i].wait_send)
            pl.when(early)(forwards[1][i].wait_send)
        pl.when(keeps)(keep.wait)
        for g in range(2):
            local = early & (lax.rem(net.z // 2 + net.m, 2) + 2 * g == net.z)
            arrival = remote(k.relay.at[0, 0], k.own_pyramid.at[g], base, base + 2 + g, net.core)
            pl.when(jnp.logical_not(local))(arrival.wait_recv)


    @pl.when(is_late)
    def _():
        pair_sums.begin()

    @pl.when(early)
    def _():
        k.pyramid_sum[...] = k.sum_pyramid[...]

    wait_project = to_owners(lambda i: k.sum_project, k.own_project, k.local_sems.at[10])

    def rows_of(i, size=384):
        return pl.ds(pl.multiple_of(i * size, 128), size)

    def expand_half(half):
        for i in (half, half + 2):
            at = pl.ds(i * 384, 384)
            total = mm_t(k.grad_expanded[at, :], k.w_expand[...])
            for b in range(4):
                k.part[b, at, :] = total[:, b * 128 : b * 128 + 128]

    swaps, late_moves = [], []

    def expand_gradient():
        k.stream.need(hidden_two=1)

        def body(b, carry):
            grad = tm_m(k.hidden_two[:, lane_block(b)], k.grad_expanded[...])
            k.grad_expand[pl.ds(2 * b, 2)] = grad.reshape(2, 64, 512).astype(BF16)
            return carry

        lax.fori_loop(0, 4, body, 0)
        swaps.append(core_halves(net, k.grad_expand, k.core_expand))

    sum_scatter(net, k.part, scatter_refs(k, "sum"), k.grad_2, meanwhile=expand_gradient, produce=expand_half)
    k.stream.need(dilated=1, mask=1)

    def norm_back(grad, value, stats, affine, outgoing, incoming, store, kept, meanwhile=None):
        mean, inverse = stats[0:1, :], stats[1:2, :]
        gain, bias = affine[0:1, :], affine[1:2, :]

        def normed(at):
            return (value[at, :] - mean) * inverse

        def through(at):
            grad[at, :] = grad[at, :] * slope(gain * normed(at) + bias)

        each_rows(1536, 128, through)
        bias_grad, gain_grad = gradient_sums(
            net, grad, normed, outgoing, incoming, meanwhile=meanwhile
        )
        keep_rows(kept, gain_grad, bias_grad)

        def back(at):
            shared = k.mask[at, :] / counted * gain
            result = gain * grad[at, :] - shared * (bias_grad + normed(at) * gain_grad)
            store(at, (inverse * result).astype(BF16))

        each_rows(1536, 128, back)

    def store_2(at, value):
        k.grad_pad[pl.ds(pl.multiple_of(at.start + 512, 128), 128), :] = value

    def pass_expand():
        k.stream.need(half_pyramid=1)
        begin_early()

        @pl.when(is_late)
        def _():
            pair_sums.go_on(k.half_pyramid)

        swaps.pop().wait()
        add_halves(net, k.grad_expand, k.core_expand, k.half_expand)
        late_moves.extend(along_z(net, k.half_expand, k.z_expand))

    norm_back(
        k.grad_2,
        k.dilated,
        k.stats_2,
        k.affine_2,
        k.out_2,
        k.in_2,
        store_2,
        k.norm_2,
        meanwhile=pass_expand,
    )
    halo = send_halo(net, k.grad_pad)
    zero_margins(k.cells, 8, 128)
    halo.wait()

    def spread(i, carry):
        k.cells[i, 8:136, :] = k.grad_pad[rows_of(i, 128), :].astype(F32)
        for j in range(3):
            start = 8 - 4 * (j - 1)
            k.grad_taps[rows_of(i, 128), j * 128 : j * 128 + 128] = k.cells[
                i, start : start + 128, :
            ].astype(BF16)
        return carry

    lax.fori_loop(0, 20, spread, 0)
    for load in loads:
        load.wait()

    def dilated_rows(i, carry):
        total = 0.0
        for tap in range(3):
            at = pl.ds(pl.multiple_of((i * 3 + 8 - 4 * tap) * 128, 128), 384)
            total = total + mm_t(k.grad_taps[at, :], k.w_taps[tap])
        for b in range(4):
            k.part[b, rows_of(i), :] = total[:, b * 128 : b * 128 + 128]
        return carry

    def dilated_half(half):
        def run(i, carry):
            return dilated_rows(half + 2 * i, carry)

        lax.fori_loop(0, 2, run, 0)

    def dilated_gradient():
        k.stream.need(hidden=1)

        for i in range(3):

            def body(b, carry):
                band = k.hidden[pl.ds(i * 512, 1536), lane_block(b)]
                grad = tm_m(band, k.grad_taps[pl.ds(512, 1536), :])
                for j in range(3):
                    block = grad[:, j * 128 : j * 128 + 128].reshape(2, 64, 128)
                    rows = slice((i * 3 + j) * 64, (i * 3 + j) * 64 + 64)
                    k.grad_dilated[pl.ds(2 * b, 2), rows, :] = block.astype(BF16)
                return carry

            lax.fori_loop(0, 4, body, 0)
        swaps.append(core_halves(net, k.grad_dilated, k.core_dilated))

    sum_scatter(net, k.part, scatter_refs(k, "sum2"), k.grad_1, meanwhile=dilated_gradient, produce=dilated_half)
    k.stream.need(reduced=1)

    def store_1(at, value):
        k.grad_reduced[at, lane_block(net.m)] = value

    def pass_halves():
        @pl.when(is_late)
        def _():
            pair_sums.finish(k.pyramid_sum)
            to_across.start()

        relay_early()
        swaps.pop().wait()
        add_halves(net, k.grad_dilated, k.core_dilated, k.half_dilated)
        late_moves.extend(along_z(net, k.half_dilated, k.z_dilated))

    norm_back(
        k.grad_1,
        k.reduced,
        k.stats_1,
        k.affine_1,
        k.out_1,
        k.in_1,
        store_1,
        k.norm_1,
        meanwhile=pass_halves,
    )
    gather_blocks(net, lambda b, at: k.grad_reduced.at[at, lane_block(b)], 1536)

    relay_late()
    k.stream.need(x=1)

    def reduce_gradient(b, carry):
        grad = tm_m(k.grad_reduced[:, lane_block(b)], k.x[...])
        k.grad_reduce[pl.ds(2 * b, 2)] = grad.reshape(2, 64, 512).astype(BF16)
        return carry

    lax.fori_loop(0, 4, reduce_gradient, 0)
    swap = core_halves(net, k.grad_reduce, k.core_reduce)

    swap.wait()
    add_halves(net, k.grad_reduce, k.core_reduce, k.half_reduce)
    reduce_moves = along_z(net, k.half_reduce, k.z_reduce, chunk_of(net))

    k.stream.need(shortcut=1, w_reduce=1)

    def input_rows(at):
        total = k.shortcut[at, :]
        for b in range(4):
            total = total + mm_t(k.grad_reduced[at, b * 128 : b * 128 + 128], k.w_reduce[b])
        k.grad_input[at, :] = total

    each_rows(1536, 384, input_rows)
    k.stream.done(grad_input=1)
    for move_ in reduce_moves:
        move_.wait()
    k.sum_reduce[...] = finish_z(net, k.half_reduce, k.z_reduce, chunk_of(net)).astype(BF16)
    wait_reduce = to_owners(
        lambda i: k.sum_reduce.at[:, lanes_for(i)], k.own_reduce, k.local_sems.at[11]
    )
    for move_ in late_moves:
        move_.wait()
    k.sum_dilated[...] = finish_z(net, k.half_dilated, k.z_dilated)
    k.sum_expand[...] = finish_z(net, k.half_expand, k.z_expand)
    wait_pyramid()
    wait_project()
    wait_reduce()


def run_bottleneck_backward(args):
    return call_kernel(
        bottleneck_backward,
        "bottleneck_back",
        3,
        args,
        dict(
            grad_input=((1536, 512), F32),
            norm_2=((8, 128), F32),
            norm_1=((8, 128), F32),
            own_pyramid=((2, 16, 32, 256), BF16),
            own_project=((2, 32, 384), BF16),
            sum_dilated=((576, 128), F32),
            sum_expand=((64, 512), F32),
            own_reduce=((2, 64, 256), BF16),
        ),
        dict(
            grad_taps=pltpu.VMEM((2560, 384), BF16),
            grad_reduced=pltpu.VMEM((1536, 512), BF16),
            **pair_scratch(),
            relay=pltpu.VMEM((2, 2, 16, 32, 256), BF16),
            pyramid_sum=pltpu.VMEM((2, 16, 32, 256), BF16),
            sum_reduce=pltpu.VMEM((64, 512), BF16),
            grad_expand=pltpu.VMEM((8, 64, 512), BF16),
            core_expand=pltpu.VMEM((4, 64, 512), BF16),
            half_expand=pltpu.VMEM((4, 64, 512), BF16),
            z_expand=pltpu.VMEM((3, 64, 512), BF16),
            grad_reduce=pltpu.VMEM((8, 64, 512), BF16),
            core_reduce=pltpu.VMEM((4, 64, 512), BF16),
            half_reduce=pltpu.VMEM((4, 64, 512), BF16),
            z_reduce=pltpu.VMEM((3, 64, 512), BF16),
            grad_dilated=pltpu.VMEM((8, 576, 128), BF16),
            core_dilated=pltpu.VMEM((4, 576, 128), BF16),
            half_dilated=pltpu.VMEM((4, 576, 128), BF16),
            z_dilated=pltpu.VMEM((3, 576, 128), BF16),
            w_taps=pltpu.VMEM((3, 512, 384), BF16),
            part=pltpu.VMEM((4, 1536, 128), F32),
            **scatter_scratch("sum", 1536, 128),
            **scatter_scratch("sum2", 1536, 128),
            grad_2=pltpu.VMEM((1536, 128), F32),
            grad_1=pltpu.VMEM((1536, 128), F32),
            grad_pad=pltpu.VMEM((2560, 128), BF16),
            cells=pltpu.VMEM((20, 144, 128), F32),
            **exchange_scratch(2),
            **exchange_scratch(1),
            local_sems=pltpu.SemaphoreType.DMA((13,)),
        ),
        96,
        hbm=dict(w_dilated=1),
        stream=dict(half_pyramid=1, hidden_two=1, dilated=1, mask=1, hidden=1, reduced=1, x=1, shortcut=1, w_reduce=1, grad_input=1),
    )


def finish(net, k):
    counted = pixel_count(k.boxes)
    odd = lax.rem(lax.axis_index("batch"), 2)

    def rows_for(i):
        return slice(i * 32, i * 32 + 32)

    nothing = jnp.zeros((64, 256), F32)
    for tap in (9, 10, 11, 15, 16, 17, 18, 19, 20, 24, 25, 26):
        k.grad_rates[tap] = nothing
    for slot in range(16):
        for i in range(2):
            block = k.own_pyramid[i, slot].astype(F32)
            if slot == 0:
                k.grad_point[rows_for(i), :] = block
            else:
                tap = slot - 1 if slot < 10 else slot + 2 if slot < 13 else slot + 8
                k.grad_rates[tap, rows_for(i), :] = block
    k.stream.done(grad_rates=1)
    k.stream.need(from_input=1)
    leave = pltpu.make_async_copy(k.from_input, k.grad_input, k.sem.at[0])
    leave.start()
    for y in range(6):
        turned = k.packed[y * 128 : y * 128 + 128, :].astype(F32).T.astype(BF16)
        k.features[y] = turned[0:64, :]
        k.features[y + 6] = turned[64:128, :]
    k.turned[...] = jnp.concatenate([k.own_project[i].astype(F32) for i in range(2)], axis=0).T
    for slot in range(5):
        start = pl.multiple_of(slot * 64 + odd * 32, 32)
        k.grad_project[slot] = k.turned[pl.ds(start, 32), :]
    k.grad_reduce[...] = jnp.concatenate(
        [k.own_reduce[i].astype(F32) for i in range(2)], axis=0
    ).T
    k.grad_dilated[...] = k.from_dilated[...].reshape(9, 64, 128)
    k.grad_expand[...] = k.from_expand[...]
    k.grad_pool[...] = k.from_pool[...]
    k.grad_norm_1[...] = k.norm_1[0:2, :]
    k.grad_norm_2[...] = k.norm_2[0:2, :]
    k.grad_norm_3[...] = k.norm_3[0:2, :]
    for b in range(4):
        k.grad_norm_b[:, b, :] = k.norm_b[0:2, b * 64 : b * 64 + 64]
    k.grad_norm_pool[...] = k.norm_pool[0:2, 0:64]
    k.grad_norm_p[...] = k.norm_p[0:2, 0:64]
    k.grad_head_weight[...] = k.head_sums[0:22, 0:256]
    columns = k.head_sums[:, 256:384].T
    k.grad_head_bias[...] = columns[0:1, 0:22]
    loss = columns[1:2, :]
    task = lax.broadcasted_iota(jnp.int32, (1, 32), 1)

    def total(inside):
        return jnp.sum(jnp.where(inside, loss, 0.0), axis=1, keepdims=True) / counted

    terms = [total(task == 0), total(task == 19), total((task == 20) | (task == 21))]
    lane = lax.broadcasted_iota(jnp.int32, (1, 128), 1)
    losses = jnp.where(lane == 0, terms[0], jnp.where(lane == 1, terms[1], terms[2]))
    log_vars = jnp.where(
        lane == 0, k.log_vars[0], jnp.where(lane == 1, k.log_vars[1], k.log_vars[2])
    )
    weighted = jnp.exp(-log_vars) * losses
    k.total_loss[...] = jnp.sum(
        jnp.where(lane < 3, weighted + log_vars, 0.0), axis=1, keepdims=True
    )
    k.grad_log_vars[...] = (1.0 - weighted)[:, 0:3]

    leave.wait()


def run_finish(args):
    return call_kernel(
        finish,
        "finish",
        None,
        args,
        dict(
            features=((12, 64, 128), BF16),
            total_loss=((1, 1), F32),
            grad_input=((1536, 512), F32),
            grad_reduce=((256, 128), F32),
            grad_dilated=((9, 64, 128), F32),
            grad_expand=((64, 512), F32),
            grad_norm_1=((2, 128), F32),
            grad_norm_2=((2, 128), F32),
            grad_norm_3=((2, 512), F32),
            grad_point=((64, 256), F32),
            grad_rates=((27, 64, 256), F32),
            grad_pool=((64, 256), F32),
            grad_norm_b=((2, 4, 64), F32),
            grad_norm_pool=((2, 64), F32),
            grad_project=((5, 32, 64), F32),
            grad_norm_p=((2, 64), F32),
            grad_head_weight=((22, 256), F32),
            grad_head_bias=((1, 22), F32),
            grad_log_vars=((1, 3), F32),
        ),
        dict(turned=pltpu.VMEM((384, 64), F32), sem=pltpu.SemaphoreType.DMA((1,))),
        0,
        hbm=dict(grad_input=1),
        stream=dict(from_input=1, grad_rates=1),
        smem=dict(boxes=1, log_vars=1),
    )


def fast_local(
    trunk_input,
    conv_reduce,
    conv_dilated,
    conv_expand,
    reduction_norm_params,
    dilated_norm_params,
    expansion_norm_params,
    aspp_point,
    aspp_rates,
    aspp_pool,
    branch_norms,
    pooling_norm_params,
    aspp_project,
    projection_norm_params,
    head_weight,
    head_bias,
    log_vars,
    crop_boxes,
    seg_labels,
    depth_target,
    normal_target,
):
    x = trunk_input.reshape(1536, 512)
    forward = run_bottleneck(
        dict(
            x=x,
            conv_reduce=conv_reduce,
            w_dilated=conv_dilated,
            w_expand=conv_expand,
            aspp_point=aspp_point,
            aspp_rates=aspp_rates,
            project=aspp_project.transpose(1, 0, 2),
            affine_1=reduction_norm_params,
            affine_2=dilated_norm_params,
            affine_3=expansion_norm_params,
            boxes=crop_boxes,
        )
    )
    middle = run_pyramid(
        dict(
            trunk=forward.trunk,
            mask=forward.mask,
            far_pyramid=forward.w_pyramid,
            branch_norms=branch_norms,
            norm_project=projection_norm_params,
            norm_pooling=pooling_norm_params,
            aspp_pool=aspp_pool,
            far_slots=forward.w_project,
            head_weight=head_weight.T,
            head_bias=head_bias,
            log_vars=log_vars,
            labels=seg_labels.transpose(1, 0, 2),
            depth=depth_target.transpose(1, 0, 2),
            normal=normal_target.transpose(0, 2, 1, 3).reshape(12, 2, 128),
            boxes=crop_boxes,
        )
    )
    back = run_pyramid_backward(
        dict(
            grad_branches=middle.grad_branches,
            w_pyramid=middle.w_pyramid.reshape(13, 256, 512),
            x=x,
            trunk=forward.trunk,
            expanded=forward.expanded,
            stats_3=forward.stats_3,
            affine_3=expansion_norm_params,
            mask=forward.mask,
            grad_pooled=middle.grad_pooled,
            grad_project=middle.grad_project,
            grad_pool=middle.grad_pool,
            boxes=crop_boxes,
        )
    )
    last = run_bottleneck_backward(
        dict(
            grad_expanded=back.grad_expanded,
            shortcut=back.shortcut,
            w_reduce=forward.w_reduce,
            half_pyramid=back.half_pyramid,
            sum_pyramid=back.sum_pyramid,
            sum_project=back.sum_project,
            x=x,
            hidden=forward.hidden,
            hidden_two=forward.hidden_two,
            w_expand=conv_expand,
            w_dilated=conv_dilated,
            dilated=forward.dilated,
            stats_2=forward.stats_2,
            affine_2=dilated_norm_params,
            reduced=forward.reduced,
            stats_1=forward.stats_1,
            affine_1=reduction_norm_params,
            mask=forward.mask,
            boxes=crop_boxes,
        )
    )
    done = run_finish(
        dict(
            from_input=last.grad_input,
            own_pyramid=last.own_pyramid,
            packed=middle.features,
            own_project=last.own_project,
            own_reduce=last.own_reduce,
            from_dilated=last.sum_dilated,
            from_expand=last.sum_expand,
            from_pool=back.sum_pool,
            norm_1=last.norm_1,
            norm_2=last.norm_2,
            norm_3=back.norm_3,
            norm_b=middle.norm_b,
            norm_pool=middle.norm_pool,
            norm_p=middle.norm_p,
            head_sums=middle.head_sums,
            log_vars=log_vars,
            boxes=crop_boxes,
        )
    )
    return (
        done.features.transpose(0, 2, 1).reshape(1, 12, 128, 64),
        done.total_loss.reshape(()),
        done.grad_input.reshape(1, 12, 128, 512),
        done.grad_reduce,
        done.grad_dilated.reshape(3, 3, 64, 128),
        done.grad_expand,
        done.grad_norm_1,
        done.grad_norm_2,
        done.grad_norm_3,
        done.grad_point,
        done.grad_rates.reshape(3, 3, 3, 64, 256),
        done.grad_pool,
        done.grad_norm_b,
        done.grad_norm_pool,
        done.grad_project.transpose(2, 0, 1),
        done.grad_norm_p,
        done.grad_head_weight.T,
        done.grad_head_bias.reshape(22),
        done.grad_log_vars.reshape(3),
    )


def local(
    trunk_input,
    conv_reduce,
    conv_dilated,
    conv_expand,
    reduction_norm_params,
    dilated_norm_params,
    expansion_norm_params,
    aspp_point,
    aspp_rates,
    aspp_pool,
    branch_norms,
    pooling_norm_params,
    aspp_project,
    projection_norm_params,
    head_weight,
    head_bias,
    log_vars,
    crop_boxes,
    seg_labels,
    depth_target,
    normal_target,
):
    image_inputs, tile_row_count, frame_columns, quarter = trunk_input.shape
    pixels = image_inputs * tile_row_count * frame_columns
    branch_part = aspp_point.shape[0]
    branch_total = lax.axis_size("branch")
    row_portion = 1.0 / lax.axis_size("rows")
    image_overall_count = float(crop_boxes.shape[0])
    first_image = lax.axis_index("batch") * image_inputs
    first_row = lax.axis_index("rows") * tile_row_count
    my_boxes = lax.dynamic_slice_in_dim(crop_boxes, first_image, image_inputs, 0)
    row_ids = first_row + jnp.arange(tile_row_count, dtype=jnp.int32)
    col_ids = jnp.arange(frame_columns, dtype=jnp.int32)
    inside_rows = (row_ids[None, :] >= my_boxes[:, 0:1]) & (
        row_ids[None, :] < my_boxes[:, 0:1] + my_boxes[:, 2:3]
    )
    inside_cols = (col_ids[None, :] >= my_boxes[:, 1:2]) & (
        col_ids[None, :] < my_boxes[:, 1:2] + my_boxes[:, 3:4]
    )
    valid_mask = (inside_rows[:, :, None] & inside_cols[:, None, :]).astype(jnp.float32)
    mask_column_vector = valid_mask.reshape(pixels, 1)
    mask_flat = valid_mask.reshape(pixels)
    pixel_number_count = jnp.sum((crop_boxes[:, 2] * crop_boxes[:, 3]).astype(jnp.float32))
    image_areas = (my_boxes[:, 2] * my_boxes[:, 3]).astype(jnp.float32)
    input_full = widen(trunk_input)
    reduced_output = forward_dot(input_full, conv_reduce).reshape(pixels, -1)
    normalized_first, standardized_first, inverse_deviation_first = norm_ahead_pass(
        reduced_output, mask_column_vector, pixel_number_count, reduction_norm_params
    )
    hidden_one = (
        jax.nn.silu(normalized_first)
        .astype(jnp.bfloat16)
        .reshape(image_inputs, tile_row_count, frame_columns, -1)
    )
    hidden_full = widen(pad_rows(hidden_one))
    dilated_out = 0.0
    for row_tap in range(3):
        band = hidden_full[:, 4 * row_tap : 4 * row_tap + tile_row_count]
        for col_tap in range(3):
            dilated_out = dilated_out + forward_dot(
                move(band, -(col_tap - 1) * 4, 2), conv_dilated[row_tap, col_tap]
            )
    normalized_second, standardized_second, inverse_deviation_second = norm_ahead_pass(
        dilated_out.reshape(pixels, -1), mask_column_vector, pixel_number_count, dilated_norm_params
    )
    hidden_two = (
        jax.nn.silu(normalized_second)
        .astype(jnp.bfloat16)
        .reshape(image_inputs, tile_row_count, frame_columns, -1)
    )
    hidden_two_full = widen(hidden_two)
    expanded_output = forward_dot(hidden_two_full, conv_expand).reshape(pixels, -1)
    normalized_third, standardized_third, inverse_deviation_third = norm_ahead_pass(
        expanded_output, mask_column_vector, pixel_number_count, expansion_norm_params
    )
    residual_sum = normalized_third + trunk_input.reshape(pixels, -1).astype(jnp.float32)
    trunk_out = (
        jax.nn.silu(residual_sum)
        .astype(jnp.bfloat16)
        .reshape(image_inputs, tile_row_count, frame_columns, quarter)
    )
    trunk_full = widen(trunk_out)
    branch_outs = [backward_dot(trunk_full, aspp_point)]
    for branch_id in range(3):
        dilation = RATES[branch_id]
        hops = dilation // tile_row_count
        partials = [0.0, 0.0, 0.0]
        for col_tap in range(3):
            shifted = move(trunk_full, -(col_tap - 1) * dilation, 2)
            products = backward_dot(shifted, stacked_taps(aspp_rates[branch_id], col_tap))
            for row_tap in range(3):
                partials[row_tap] = (
                    partials[row_tap]
                    + products[..., row_tap * branch_part : (row_tap + 1) * branch_part]
                )
        upper = send_down(partials[0].astype(jnp.bfloat16), hops).astype(jnp.float32)
        lower_part = send_up(partials[2].astype(jnp.bfloat16), hops).astype(jnp.float32)
        branch_outs.append(partials[1] + upper + lower_part)
    spatial_flattened = jnp.stack(branch_outs, axis=3).reshape(pixels, -1)
    branch_gain_bias = branch_norms.reshape(2, -1)
    normalized_spatial, standardized_spatial, inverse_deviation_spatial = norm_ahead_pass(
        spatial_flattened, mask_column_vector, pixel_number_count, branch_gain_bias
    )
    spatial_act = (
        jax.nn.silu(normalized_spatial)
        .astype(jnp.bfloat16)
        .reshape(image_inputs, tile_row_count, frame_columns, 4, branch_part)
    )
    pooled_local = lax.dot_general(
        valid_mask.astype(jnp.bfloat16),
        trunk_full,
        (((1, 2), (1, 2)), ((0,), (0,))),
        preferred_element_type=jnp.float32,
    )
    pooled = (over_rows(pooled_local) / image_areas[:, None]).astype(jnp.bfloat16)
    pooling_convolution = backward_dot(pooled, aspp_pool)
    normalized_poolbranch, standardized_poolbranch, inverse_deviation_poolbranch = norm_ahead_pass(
        pooling_convolution, row_portion, image_overall_count, pooling_norm_params
    )
    pool_act = jax.nn.silu(normalized_poolbranch).astype(jnp.bfloat16)
    pool_wide = jnp.broadcast_to(
        pool_act[:, None, None, None, :],
        (image_inputs, tile_row_count, frame_columns, 1, branch_part),
    )
    concat = jnp.concatenate([spatial_act, pool_wide], axis=3)
    concat_flat = widen(concat).reshape(pixels, -1)
    proj_kernel = (
        aspp_project.reshape(branch_part, 5, branch_total, branch_part)
        .transpose(0, 2, 1, 3)
        .reshape(branch_part, 5 * branch_total * branch_part)
    )
    projected_output = backward_dot(concat_flat, proj_kernel)
    normalized_projector, standardized_projector, inverse_deviation_projector = norm_ahead_pass(
        projected_output, mask_column_vector, pixel_number_count, projection_norm_params
    )
    features = (
        jax.nn.silu(normalized_projector)
        .astype(jnp.bfloat16)
        .reshape(image_inputs, tile_row_count, frame_columns, -1)
    )
    features_wide = widen(features).reshape(pixels, -1).astype(jnp.float32)
    head_wide = head_weight.astype(jnp.float32)
    logits = jnp.dot(features_wide, head_wide, precision=HIGH) + head_bias
    classes = head_bias.shape[0] - 3
    seg_logits = logits[:, :classes]
    labels_flat = seg_labels.reshape(pixels)
    classes_hot = (labels_flat[:, None] == jnp.arange(classes, dtype=jnp.int32)[None, :]).astype(
        jnp.float32
    )
    cross = jax.nn.logsumexp(seg_logits, axis=1) - jnp.sum(seg_logits * classes_hot, axis=1)
    depth_gap = logits[:, classes] - depth_target.reshape(pixels)
    smooth_abs = jnp.sqrt(depth_gap * depth_gap + 1.0)
    normal_gap = logits[:, classes + 1 :] - jnp.moveaxis(normal_target, 1, 3).reshape(pixels, 2)
    local_losses = jnp.stack(
        [
            jnp.sum(mask_flat * cross),
            jnp.sum(mask_flat * (smooth_abs - 1.0)),
            jnp.sum(mask_flat * jnp.sum(normal_gap * normal_gap, axis=1)),
        ]
    )
    task_weights = jnp.exp(-log_vars)
    grad_seg = (jax.nn.softmax(seg_logits, axis=1) - classes_hot) * (
        task_weights[0] / pixel_number_count * mask_flat
    )[:, None]
    grad_depth = depth_gap / smooth_abs * (task_weights[1] / pixel_number_count * mask_flat)
    grad_normal = 2.0 * normal_gap * (task_weights[2] / pixel_number_count * mask_flat)[:, None]
    grad_logits = jnp.concatenate([grad_seg, grad_depth[:, None], grad_normal], axis=1)
    head_local = lax.dot_general(
        features_wide, grad_logits, (((0,), (0,)), ((), ())), precision=HIGH
    )
    loss_parts, grad_head_weight, grad_head_bias = lax.psum(
        (local_losses, head_local, jnp.sum(grad_logits, axis=0)), ("rows", "batch")
    )
    task_losses = loss_parts / pixel_number_count
    total_loss = jnp.sum(task_weights * task_losses + log_vars)
    grad_log_vars = 1.0 - task_weights * task_losses
    grad_features = jnp.dot(grad_logits, head_wide.T, precision=HIGH)
    my_features_grad = lax.dynamic_slice_in_dim(
        grad_features, lax.axis_index("branch") * branch_part, branch_part, 1
    )
    gradient_before_projector = my_features_grad * silu_slope(normalized_projector)
    grad_proj_in, grad_project_norm = norm_reverse_pass(
        gradient_before_projector,
        standardized_projector,
        inverse_deviation_projector,
        1.0,
        mask_column_vector,
        pixel_number_count,
        projection_norm_params,
    )
    grad_proj_low = grad_proj_in.astype(jnp.bfloat16)
    proj_kernel_grad = lax.dot_general(
        grad_proj_low, concat_flat, (((0,), (0,)), ((), ())), preferred_element_type=jnp.float32
    )
    grad_project_local = (
        proj_kernel_grad.reshape(branch_part, branch_total, 5, branch_part)
        .transpose(0, 2, 1, 3)
        .reshape(branch_part, 5, branch_total * branch_part)
    )
    concat_grad = forward_dot(grad_proj_low, proj_kernel).reshape(
        image_inputs, tile_row_count, frame_columns, -1
    )
    concat_grad = narrow(concat_grad).reshape(pixels, 5, branch_part)
    pool_grad_img = over_rows(
        jnp.sum(concat_grad[:, 4, :].reshape(image_inputs, -1, branch_part), axis=1)
    )
    gradient_before_poolbranch = pool_grad_img * silu_slope(normalized_poolbranch)
    grad_pool_conv, grad_pool_norm = norm_reverse_pass(
        gradient_before_poolbranch,
        standardized_poolbranch,
        inverse_deviation_poolbranch,
        row_portion,
        1.0,
        image_overall_count,
        pooling_norm_params,
    )
    pool_conv_low = grad_pool_conv.astype(jnp.bfloat16)
    grad_pool_local = (
        lax.dot_general(
            pool_conv_low, pooled, (((0,), (0,)), ((), ())), preferred_element_type=jnp.float32
        )
        * row_portion
    )
    pooled_grad = forward_dot(pool_conv_low, aspp_pool)
    gradient_before_spatialbranch = concat_grad[:, :4, :].reshape(pixels, -1) * silu_slope(
        normalized_spatial
    )
    grad_spatial, branch_norm_grad = norm_reverse_pass(
        gradient_before_spatialbranch,
        standardized_spatial,
        inverse_deviation_spatial,
        1.0,
        mask_column_vector,
        pixel_number_count,
        branch_gain_bias,
    )
    grad_branch_norms = branch_norm_grad.reshape(2, 4, branch_part)
    spatial_low = grad_spatial.astype(jnp.bfloat16).reshape(
        image_inputs, tile_row_count, frame_columns, 4, branch_part
    )
    point_grad = spatial_low[:, :, :, 0]
    grad_point_local = pixel_dot(point_grad, trunk_full)
    trunk_grad = forward_dot(point_grad, aspp_point)
    trunk_grad = (
        trunk_grad + valid_mask[..., None] * (pooled_grad / image_areas[:, None])[:, None, None, :]
    )
    rate_grads = []
    for branch_id in range(3):
        dilation = RATES[branch_id]
        hops = dilation // tile_row_count
        centre = spatial_low[:, :, :, branch_id + 1]
        grad_taps = jnp.concatenate(
            [send_up(centre, hops), centre, send_down(centre, hops)], axis=3
        )
        per_col = []
        for col_tap in range(3):
            shifted = move(trunk_full, -(col_tap - 1) * dilation, 2)
            per_col.append(pixel_dot(grad_taps, shifted))
            tap_grad = forward_dot(grad_taps, stacked_taps(aspp_rates[branch_id], col_tap))
            trunk_grad = trunk_grad + move(tap_grad, (col_tap - 1) * dilation, 2)
        col_stack = jnp.stack(per_col, axis=0).reshape(3, 3, branch_part, -1)
        rate_grads.append(col_stack.transpose(1, 0, 2, 3))
    grad_rates_local = jnp.stack(rate_grads, axis=0)
    trunk_own = narrow(trunk_grad).reshape(pixels, -1)
    gradient_shortcut = trunk_own * silu_slope(residual_sum)
    grad_expanded, grad_norm_expand = norm_reverse_pass(
        gradient_shortcut,
        standardized_third,
        inverse_deviation_third,
        1.0,
        mask_column_vector,
        pixel_number_count,
        expansion_norm_params,
    )
    expanded_low = grad_expanded.astype(jnp.bfloat16).reshape(
        image_inputs, tile_row_count, frame_columns, -1
    )
    grad_expand_local = pixel_dot(hidden_two_full, expanded_low)
    hidden_two_grad = narrow(backward_dot(expanded_low, conv_expand)).reshape(pixels, -1)
    gradient_before_second = hidden_two_grad * silu_slope(normalized_second)
    gradient_dilated_input, gradient_dilated_norm = norm_reverse_pass(
        gradient_before_second,
        standardized_second,
        inverse_deviation_second,
        1.0,
        mask_column_vector,
        pixel_number_count,
        dilated_norm_params,
    )
    dilated_lowprec = gradient_dilated_input.astype(jnp.bfloat16).reshape(
        image_inputs, tile_row_count, frame_columns, -1
    )
    dilated_padded = pad_rows(dilated_lowprec)
    hidden_one_grad = 0.0
    kernel_grads = []
    for row_tap in range(3):
        band = hidden_full[:, 4 * row_tap : 4 * row_tap + tile_row_count]
        grad_band = dilated_padded[:, 8 - 4 * row_tap : 8 - 4 * row_tap + tile_row_count]
        for col_tap in range(3):
            kernel_grads.append(pixel_dot(move(band, -(col_tap - 1) * 4, 2), dilated_lowprec))
            hidden_one_grad = hidden_one_grad + backward_dot(
                move(grad_band, (col_tap - 1) * 4, 2), conv_dilated[row_tap, col_tap]
            )
    grad_dilated_local = jnp.stack(kernel_grads, axis=0).reshape(3, 3, hidden_full.shape[3], -1)
    hidden_one_own = narrow(hidden_one_grad).reshape(pixels, -1)
    gradient_before_first = hidden_one_own * silu_slope(normalized_first)
    grad_reduced, grad_norm_reduce = norm_reverse_pass(
        gradient_before_first,
        standardized_first,
        inverse_deviation_first,
        1.0,
        mask_column_vector,
        pixel_number_count,
        reduction_norm_params,
    )
    reduced_low = grad_reduced.astype(jnp.bfloat16).reshape(
        image_inputs, tile_row_count, frame_columns, -1
    )
    grad_reduce_local = pixel_dot(input_full, reduced_low)
    input_grad = narrow(backward_dot(reduced_low, conv_reduce))
    grad_input = input_grad + gradient_shortcut.reshape(
        image_inputs, tile_row_count, frame_columns, quarter
    )
    grad_reduce, grad_dilated, grad_expand, grad_point, grad_rates, grad_pool, grad_project = (
        lax.psum_scatter(grad_reduce_local, ("rows", "batch"), scatter_dimension=0, tiled=True),
        lax.psum_scatter(grad_dilated_local, ("rows", "batch"), scatter_dimension=2, tiled=True),
        lax.psum_scatter(grad_expand_local, ("rows", "batch"), scatter_dimension=0, tiled=True),
        lax.psum_scatter(grad_point_local, ("rows", "batch"), scatter_dimension=1, tiled=True),
        lax.psum_scatter(grad_rates_local, ("rows", "batch"), scatter_dimension=4, tiled=True),
        lax.psum_scatter(grad_pool_local, ("rows", "batch"), scatter_dimension=1, tiled=True),
        lax.psum_scatter(grad_project_local, ("rows", "batch"), scatter_dimension=2, tiled=True),
    )
    return (
        features,
        total_loss,
        grad_input,
        grad_reduce,
        grad_dilated,
        grad_expand,
        grad_norm_reduce,
        gradient_dilated_norm,
        grad_norm_expand,
        grad_point,
        grad_rates,
        grad_pool,
        grad_branch_norms,
        grad_pool_norm,
        grad_project,
        grad_project_norm,
        grad_head_weight,
        grad_head_bias,
        grad_log_vars,
    )


def solution(mesh):
    in_specs = (
        P("batch", "rows", None, "branch"),
        P(None, "branch"),
        P(None, None, None, "branch"),
        P(None, "branch"),
        P(None, "branch"),
        P(None, "branch"),
        P(None, "branch"),
        P("branch", None),
        P(None, None, None, "branch", None),
        P("branch", None),
        P(None, None, "branch"),
        P(None, "branch"),
        P("branch", None, None),
        P(None, "branch"),
        P(),
        P(),
        P(),
        P(),
        P("batch", "rows", None),
        P("batch", "rows", None),
        P("batch", None, "rows", None),
    )
    out_specs = (
        P("batch", "rows", None, "branch"),
        P(),
        P("batch", "rows", None, "branch"),
        P(("rows", "batch"), "branch"),
        P(None, None, ("rows", "batch"), "branch"),
        P(("rows", "batch"), "branch"),
        P(None, "branch"),
        P(None, "branch"),
        P(None, "branch"),
        P("branch", ("rows", "batch")),
        P(None, None, None, "branch", ("rows", "batch")),
        P("branch", ("rows", "batch")),
        P(None, None, "branch"),
        P(None, "branch"),
        P("branch", None, ("rows", "batch")),
        P(None, "branch"),
        P(),
        P(),
        P(),
    )
    small = (mesh.shape["branch"], mesh.shape["rows"], mesh.shape["batch"]) == (4, 2, 4)
    body = fast_local if small else local
    return jax.shard_map(body, mesh=mesh, in_specs=in_specs, out_specs=out_specs, check_vma=False)
```

```python
import types

import jax
import jax.numpy as jnp
from jax import lax
from jax.experimental import pallas as pl
from jax.experimental.pallas import tpu as pltpu
from jax.sharding import PartitionSpec as P

EPS = 1e-05
HIGH = lax.Precision.HIGHEST
RATES = (12, 24, 36)


def padded(cells, sides, width):
    for axis, dim in sides:
        count = lax.axis_size(axis)
        ends = count - 1
        head = lax.slice_in_dim(cells, 0, width, axis=dim)
        tail = lax.slice_in_dim(cells, cells.shape[dim] - width, cells.shape[dim], axis=dim)
        cells = jnp.concatenate(
            [
                lax.ppermute(tail, axis, [(i, (i + 1) % count) for i in range(ends)]),
                cells,
                lax.ppermute(head, axis, [((i + 1) % count, i) for i in range(ends)]),
            ],
            axis=dim,
        )
    return cells


def shifted_2(block, axis, distance):
    devices = range(lax.axis_size(axis))
    route = [(i - distance, i) for i in devices if i - distance in devices]
    return lax.ppermute(block, axis, route)


def move(tensor, offset, axis_id):
    length = tensor.shape[axis_id]
    if offset == 0:
        return tensor
    widths = [(0, 0)] * tensor.ndim
    if offset > 0:
        widths[axis_id] = (offset, 0)
        return lax.slice_in_dim(jnp.pad(tensor, widths), 0, length, axis=axis_id)
    widths[axis_id] = (0, -offset)
    return lax.slice_in_dim(jnp.pad(tensor, widths), -offset, length - offset, axis=axis_id)


def forward_dot(lhs_arr, rhs_arr):
    return jnp.dot(lhs_arr, rhs_arr, preferred_element_type=jnp.float32)


def backward_dot(grad_arr, kernel):
    return lax.dot_general(
        grad_arr,
        kernel,
        (((grad_arr.ndim - 1,), (1,)), ((), ())),
        preferred_element_type=jnp.float32,
    )


def pixel_dot(source, grad_arr):
    return lax.dot_general(
        source, grad_arr, (((0, 1, 2), (0, 1, 2)), ((), ())), preferred_element_type=jnp.float32
    )


def silu_slope(pre_act):
    sigmoid_v = jax.nn.sigmoid(pre_act)
    return sigmoid_v * (1.0 + pre_act * (1.0 - sigmoid_v))


def widen(tensor):
    return lax.all_gather(tensor, "branch", axis=3, tiled=True)


def narrow(tensor):
    return lax.psum_scatter(
        tensor.astype(jnp.bfloat16), "branch", scatter_dimension=3, tiled=True
    ).astype(jnp.float32)


def pad_rows(tensor):
    return padded(tensor, (("rows", 1),), 4)


def send_down(tensor, hops):
    if hops >= lax.axis_size("rows"):
        return jnp.zeros_like(tensor)
    return shifted_2(tensor, "rows", hops)


def send_up(tensor, hops):
    if hops >= lax.axis_size("rows"):
        return jnp.zeros_like(tensor)
    return shifted_2(tensor, "rows", -hops)


def over_rows(tensor):
    return lax.psum(tensor, "rows")


def norm_ahead_pass(tensor, weight, counted, affine):
    summed = lax.psum(jnp.sum(tensor * weight, axis=0), ("rows", "batch"))
    mean_val = summed / counted
    centered = tensor - mean_val
    spread = lax.psum(jnp.sum(weight * centered * centered, axis=0), ("rows", "batch"))
    variance = spread / counted
    inverse = lax.rsqrt(variance + EPS)
    normed = centered * inverse
    return (affine[0] * normed + affine[1], normed, inverse)


def norm_reverse_pass(grad_out, normed, inverse, weight_all, weight_stat, counted, affine):
    grad_bias, grad_gain = lax.psum(
        (jnp.sum(grad_out * weight_all, axis=0), jnp.sum(grad_out * normed * weight_all, axis=0)),
        ("rows", "batch"),
    )
    gain_row = affine[0]
    grad_in = inverse * (
        gain_row * grad_out - weight_stat / counted * gain_row * (grad_bias + normed * grad_gain)
    )
    return (grad_in, jnp.stack([grad_gain, grad_bias]))


def stacked_taps(kernels, col_tap):
    return jnp.concatenate([kernels[0, col_tap], kernels[1, col_tap], kernels[2, col_tap]], axis=0)


MESH = pl.DeviceIdType.MESH
F32 = jnp.float32
BF16 = jnp.bfloat16
VMEM_LIMIT = 60 * 2**20


class Net:
    def __init__(self, send_sems, recv_sems):
        self.m = lax.axis_index("branch")
        self.r = lax.axis_index("rows")
        self.z = lax.axis_index("batch")
        self.send_sems, self.recv_sems, self.count = send_sems, recv_sems, 0
        self.side = (self.m ^ 1, self.r, self.z)
        self.over = (self.m ^ 2, self.r, self.z)
        self.diagonal = (self.m ^ 3, self.r, self.z)
        self.core = (self.m, 1 - self.r, self.z)
        self.slot = self.r * 4 + self.z
        self.group = [
            (self.m, lax.rem(self.r + i, 2), lax.rem(self.z + j, 4))
            for i in range(2)
            for j in range(4)
            if i or j
        ]

    def send(self, src, dst, device):
        i = self.count
        self.count += 1
        copy = pltpu.make_async_remote_copy(
            src_ref=src,
            dst_ref=dst,
            send_sem=self.send_sems.at[i],
            recv_sem=self.recv_sems.at[i],
            device_id=device,
            device_id_type=MESH,
        )
        copy.start()
        return copy


def greet(peers, perhaps=()):
    barrier = pltpu.get_barrier_semaphore()
    for peer in peers:
        pl.semaphore_signal(barrier, inc=1, device_id=peer, device_id_type=MESH)
    awaited = len(peers)
    for peer, there in perhaps:

        @pl.when(there)
        def _(peer=peer):
            pl.semaphore_signal(barrier, inc=1, device_id=peer, device_id_type=MESH)

        awaited = awaited + there.astype(jnp.int32)
    pl.semaphore_wait(barrier, awaited)


def each_rows(total, step, body):
    def run(i, carry):
        body(pl.ds(pl.multiple_of(i * step, step), step))
        return carry

    lax.fori_loop(0, total // step, run, 0)


def lane_block(index, width=128):
    return pl.ds(pl.multiple_of(index * width, width), width)


def wide(tile, width):
    count = width // tile.shape[1]
    return tile if count == 1 else jnp.concatenate([tile] * count, axis=1)


def column_sums(fn, total, width, number):
    step = 16384 // width

    def run(i, sums):
        terms = fn(pl.ds(pl.multiple_of(i * step, step), step))
        return tuple(
            s + jnp.sum(t.reshape(step // 8, 8, width), axis=0) for s, t in zip(sums, terms)
        )

    sums = lax.fori_loop(
        0, total // step, run, tuple(jnp.zeros((8, width), F32) for _ in range(number))
    )
    return [jnp.sum(s, axis=0, keepdims=True) for s in sums]


def fold(row):
    return row + pltpu.roll(wide(row, 128), 64, 1)


def exchange(net, outgoing, incoming, meanwhile=None):
    copies = [net.send(outgoing, incoming.at[net.slot], peer) for peer in net.group]
    incoming[net.slot] = outgoing[...]
    if meanwhile is not None:
        meanwhile()
    for copy in copies:
        copy.wait()


def pack(outgoing, first, second, extra=None):
    for i in range(first.shape[1] // 128):
        outgoing[2 * i : 2 * i + 1, :] = first[:, i * 128 : i * 128 + 128]
        outgoing[2 * i + 1 : 2 * i + 2, :] = second[:, i * 128 : i * 128 + 128]
    if extra is not None:
        outgoing[4:5, :] = extra


def unpack(incoming, width):
    count = width // 128
    firsts = [incoming[:, 2 * i, :] for i in range(count)]
    seconds = [incoming[:, 2 * i + 1, :] for i in range(count)]
    return jnp.concatenate(firsts, axis=1), jnp.concatenate(seconds, axis=1)


def statistics(
    net, value_ref, mask_ref, counts, outgoing, incoming, counted, folded=False, extra=None
):
    total, width = value_ref.shape
    same = fold if folded else (lambda row: row)
    (first,) = column_sums(
        lambda at: (value_ref[at, :] * wide(mask_ref[at, :], width),), total, width, 1
    )
    first = same(first)
    own = jnp.sum(jnp.where(lax.broadcasted_iota(jnp.int32, (8, 128), 0) == net.slot, counts, 0.0), axis=0, keepdims=True)
    centre = first / jnp.maximum(wide(own, width), 1.0)

    def squares(at):
        gap = value_ref[at, :] - centre
        return (gap * gap * wide(mask_ref[at, :], width),)

    second = same(column_sums(squares, total, width, 1)[0])
    pack(outgoing, first, second, extra)
    exchange(net, outgoing, incoming)
    firsts, seconds = unpack(incoming, width)
    numbers = wide(counts, width)
    mean = jnp.sum(firsts, axis=0, keepdims=True) / counted
    drift = firsts / jnp.maximum(numbers, 1.0) - mean
    variance = jnp.sum(seconds + numbers * drift * drift, axis=0, keepdims=True) / counted
    return mean, lax.rsqrt(variance + EPS)


def gather_blocks(net, part, rows, meanwhile=None):
    pieces, size = 4, rows // 4
    own, side, over = net.m, net.m ^ 1, net.m ^ 2

    def at(i):
        return pl.ds(i * size, size)

    to_side, to_over = [], []
    for i in range(pieces):
        j = pieces - 1 - i
        to_side.append(net.send(part(own, at(i)), part(own, at(i)), net.side))
        to_over.append(net.send(part(own, at(j)), part(own, at(j)), net.over))
    passed = []
    for i in range(pieces):
        j = pieces - 1 - i
        to_side[i].wait_recv()
        if i < pieces // 2:
            passed.append(net.send(part(side, at(i)), part(side, at(i)), net.over))
        to_over[i].wait_recv()
        if i < pieces // 2:
            passed.append(net.send(part(over, at(j)), part(over, at(j)), net.side))
    if meanwhile is not None:
        meanwhile()
    for copy in to_side + to_over:
        copy.wait_send()
    for copy in passed:
        copy.wait()


def sum_scatter(net, part, bufs, out, meanwhile=None, produce=None):
    far, to_side, to_over, far_side, far_over, from_side, from_over = bufs
    rows, width = out.shape
    half, step = rows // 2, 16384 // width
    head, tail = pl.ds(0, half), pl.ds(half, half)
    across, side, over = net.m ^ 3, net.m ^ 1, net.m ^ 2

    def fill(target, index, base, count=half):
        size = min(step, count) if count % step == 0 else 64

        def body(at):
            rows_at = pl.ds(pl.multiple_of(at.start + base, size), size)
            target[rows_at, :] = part[index, rows_at, :].astype(BF16)

        each_rows(count, size, body)

    def combine(target, index, base, arrived):
        def body(at):
            rows_at = pl.ds(pl.multiple_of(at.start + base, step), step)
            target[rows_at, :] = (part[index, rows_at, :] + arrived[at, :].astype(F32)).astype(BF16)

        each_rows(half, step, body)

    quarter, first, second = half // 2, [], []
    for i in range(2):
        if produce is not None:
            produce(i)
        at = pl.ds(i * quarter, quarter)
        fill(far, across, i * quarter, quarter)
        first.append(net.send(far.at[at], far_side.at[at], net.side))
        fill(far, across, half + i * quarter, quarter)
        below = pl.ds(half + i * quarter, quarter)
        second.append(net.send(far.at[below], far_over.at[at], net.over))
    fill(to_side, side, 0)
    third = net.send(to_side.at[head], from_side.at[head], net.side)
    fill(to_over, over, half)
    fourth = net.send(to_over.at[tail], from_over.at[tail], net.over)
    for copy in second:
        copy.wait_recv()
    combine(to_side, side, half, far_over)
    fifth = net.send(to_side.at[tail], from_side.at[tail], net.side)
    for copy in first:
        copy.wait_recv()
    combine(to_over, over, 0, far_side)
    sixth = net.send(to_over.at[head], from_over.at[head], net.over)
    if meanwhile is not None:
        meanwhile()
    for copy in (third, fourth, fifth, sixth):
        copy.wait_recv()

    def body(at):
        out[at, :] = (
            part[net.m, at, :] + from_side[at, :].astype(F32) + from_over[at, :].astype(F32)
        )

    each_rows(rows, step, body)
    for copy in (*first, *second, third, fourth, fifth, sixth):
        copy.wait_send()


def gradient_sums(
    net, grad_ref, normed, outgoing, incoming, folded=False, extra=None, meanwhile=None
):
    total, width = grad_ref.shape
    same = fold if folded else (lambda row: row)
    bias, gain = column_sums(
        lambda at: (grad_ref[at, :], grad_ref[at, :] * normed(at)), total, width, 2
    )
    pack(outgoing, same(bias), same(gain), extra)
    exchange(net, outgoing, incoming, meanwhile)
    biases, gains = unpack(incoming, width)
    return jnp.sum(biases, axis=0, keepdims=True), jnp.sum(gains, axis=0, keepdims=True)


def keep_rows(ref, first, second):
    width = ref.shape[1]
    ref[0:1, :] = first
    ref[1:2, :] = second
    ref[2:8, :] = jnp.zeros((6, width), F32)


def pair(a, b):
    low = lax.broadcasted_iota(jnp.int32, (a.shape[0], 128), 1) < 64
    results = []
    for g in range(2):
        left, right = a[:, g * 128 : g * 128 + 128], b[:, g * 128 : g * 128 + 128]
        results.append(jnp.where(low, left, pltpu.roll(right, 64, 1)))
        results.append(jnp.where(low, pltpu.roll(left, 64, 1), right))
    return results


def unpair(blocks):
    low = lax.broadcasted_iota(jnp.int32, blocks[0].shape, 1) < 64
    firsts, seconds = [], []
    for g in range(2):
        left, right = blocks[2 * g], blocks[2 * g + 1]
        firsts.append(jnp.where(low, left, pltpu.roll(right, 64, 1)))
        seconds.append(jnp.where(low, pltpu.roll(left, 64, 1), right))
    return jnp.concatenate(firsts, axis=1), jnp.concatenate(seconds, axis=1)


def split_three(row):
    high = row.astype(BF16)
    rest = row - high.astype(F32)
    middle = rest.astype(BF16)
    low = (rest - middle.astype(F32)).astype(BF16)
    return high, middle, low


def zero_margins(ref, side, width):
    rows, _, lanes = ref.shape
    ref[:, 0:side, :] = jnp.zeros((rows, side, lanes), F32)
    ref[:, side + width : 2 * side + width, :] = jnp.zeros((rows, side, lanes), F32)


def scatter_buffers(rows, width):
    whole, half = pltpu.VMEM((rows, width), BF16), pltpu.VMEM((rows // 2, width), BF16)
    return [whole, whole, whole, half, half, whole, whole]


def sigmoid(u):
    return 0.5 * jnp.tanh(0.5 * u) + 0.5


def slope(u):
    s = sigmoid(u)
    return s * (1.0 + u * (1.0 - s))


def mm(a, b):
    return jnp.dot(a, b, preferred_element_type=F32)


def mm_t(a, b):
    return lax.dot_general(a, b, (((1,), (1,)), ((), ())), preferred_element_type=F32)


def tm_m(a, b):
    return lax.dot_general(a, b, (((0,), (0,)), ((), ())), preferred_element_type=F32)


class Streams:
    def __init__(self, ins, outs, sems):
        self.ins = {n: pltpu.make_async_copy(*pair, sems.at[i]) for i, (n, pair) in enumerate(ins)}
        self.outs = {
            n: pltpu.make_async_copy(*pair, sems.at[len(ins) + i])
            for i, (n, pair) in enumerate(outs)
        }
        self.left = []
        for copy in self.ins.values():
            copy.start()

    def need(self, **names):
        for name in names:
            self.ins.pop(name).wait()

    def done(self, **names):
        for name in names:
            copy = self.outs.pop(name)
            copy.start()
            self.left.append(copy)

    def finish(self):
        self.need(**dict.fromkeys(self.ins))
        self.done(**dict.fromkeys(self.outs))
        for copy in self.left:
            copy.wait()


def call_kernel(
    body, name, number, args, outs, scratch, sems, hbm={}, smem=dict(boxes=1), stream={}
):
    vmem, anywhere = pl.BlockSpec(memory_space=pltpu.VMEM), pl.BlockSpec(memory_space=pl.ANY)
    stream_in = [n for n in args if n in stream]
    stream_out = [n for n in outs if n in stream]
    buffers = {n: pltpu.VMEM(args[n].shape, args[n].dtype) for n in stream_in}
    buffers.update({n: pltpu.VMEM(*outs[n]) for n in stream_out})
    names = [f"far_{n}" if n in stream else n for n in [*args, *outs]]
    names = [*names, *scratch, *buffers, "stream_sems"]
    places = {name: anywhere for name in [*hbm, *stream]}
    places.update({name: pl.BlockSpec(memory_space=pltpu.SMEM) for name in smem})

    def kernel(*refs):
        k = types.SimpleNamespace(**dict(zip(names, refs)))
        held = vars(k)
        k.stream = Streams(
            [(n, (held[f"far_{n}"], held[n])) for n in stream_in],
            [(n, (held[n], held[f"far_{n}"])) for n in stream_out],
            k.stream_sems,
        )
        body(Net(refs[-2], refs[-1]) if sems else None, k)
        k.stream.finish()

    results = pl.pallas_call(
        kernel,
        out_shape=[jax.ShapeDtypeStruct(s, d) for s, d in outs.values()],
        in_specs=[places.get(name, vmem) for name in args],
        out_specs=[places.get(name, vmem) for name in outs],
        scratch_shapes=[
            *scratch.values(),
            *buffers.values(),
            pltpu.SemaphoreType.DMA((max(len(buffers), 1),)),
            *([pltpu.SemaphoreType.DMA((sems,))] * (2 if sems else 0)),
        ],
        name=name,
        compiler_params=pltpu.CompilerParams(
            collective_id=number, has_side_effects=bool(sems), vmem_limit_bytes=VMEM_LIMIT
        ),
    )(*args.values())
    return types.SimpleNamespace(**dict(zip(outs, results)))


def pixel_count(boxes):
    total = boxes[0, 2] * boxes[0, 3]
    for b in range(1, 4):
        total = total + boxes[b, 2] * boxes[b, 3]
    return total.astype(F32)


def tile_counts(net, boxes):
    slot = lax.broadcasted_iota(jnp.int32, (8, 128), 0)
    result = jnp.zeros((8, 128), F32)
    for s in range(8):
        top, height, width = boxes[s % 4, 0], boxes[s % 4, 2], boxes[s % 4, 3]
        first, last = (s // 4) * 12, (s // 4) * 12 + 12
        rows = jnp.minimum(top + height, last) - jnp.maximum(top, first)
        result = jnp.where(slot == s, (jnp.maximum(rows, 0) * width).astype(F32), result)
    return result


def exchange_scratch(label):
    return {
        f"out_{label}": pltpu.VMEM((8, 128), F32),
        f"in_{label}": pltpu.VMEM((8, 8, 128), F32),
    }


def scatter_scratch(label, rows, width):
    return {f"{label}_{i}": b for i, b in enumerate(scatter_buffers(rows, width))}


def scatter_refs(k, label):
    return [getattr(k, f"{label}_{i}") for i in range(7)]


def load_taps(k):
    loads = []
    for i in range(3):
        for j in range(3):
            loads.append(
                pltpu.make_async_copy(
                    k.w_dilated.at[i, j],
                    k.w_taps.at[i, :, pl.ds(j * 128, 128)],
                    k.local_sems.at[i * 3 + j],
                )
            )
            loads[-1].start()
    return loads


def send_halo(net, padded):
    lanes = padded.shape[1]
    padded[pl.ds(pl.multiple_of(net.r * 2048, 128), 512), :] = jnp.zeros((512, lanes), BF16)
    return net.send(
        padded.at[pl.ds(pl.multiple_of(1536 - net.r * 1024, 128), 512)],
        padded.at[pl.ds(pl.multiple_of(net.r * 2048, 128), 512)],
        net.core,
    )


def bottleneck_forward(net, k):
    counted, counts = pixel_count(k.boxes), tile_counts(net, k.boxes)
    loads = load_taps(k)
    own_reduce = pltpu.make_async_copy(
        k.conv_reduce.at[lane_block(net.m, 512)], k.w_reduce.at[net.m], k.local_sems.at[9]
    )
    own_reduce.start()
    greet([net.side, net.over, net.diagonal] + net.group)
    branches = [(net.m ^ 3, net.diagonal), (net.m ^ 1, net.side), (net.m ^ 2, net.over)]
    arrivals = [
        net.send(k.conv_reduce.at[lane_block(b, 512)], k.w_reduce.at[net.m], peer)
        for b, peer in branches
    ]

    top, left_edge = k.boxes[net.z, 0], k.boxes[net.z, 1]
    bottom, right_edge = top + k.boxes[net.z, 2], left_edge + k.boxes[net.z, 3]
    column = lax.broadcasted_iota(jnp.int32, (128, 128), 0)
    column_inside = jnp.where((column >= left_edge) & (column < right_edge), 1.0, 0.0)

    def mask_rows(i, carry):
        row = jnp.full((128, 128), net.r * 12 + i, jnp.int32)
        inside = jnp.where((row >= top) & (row < bottom), column_inside, 0.0)
        k.mask[pl.ds(pl.multiple_of(i * 128, 128), 128), :] = inside
        return carry

    lax.fori_loop(0, 12, mask_rows, 0)
    k.stream.done(mask=1)
    k.stream.need(x=1)

    def reduce_for(b):
        def reduce_rows(at):
            k.part[b, at, :] = mm(k.x[at, :], k.w_reduce[b])

        each_rows(1536, 384, reduce_rows)

    own_reduce.wait()
    reduce_for(net.m)
    arrivals[1].wait()
    reduce_for(net.m ^ 1)
    arrivals[2].wait()
    reduce_for(net.m ^ 2)
    arrivals[0].wait()
    k.stream.done(w_reduce=1)

    def far_half(half):
        for i in (half, half + 2):
            at = pl.ds(i * 384, 384)
            k.part[net.m ^ 3, at, :] = mm(k.x[at, :], k.w_reduce[net.m ^ 3])

    sum_scatter(net, k.part, scatter_refs(k, "sum"), k.reduced, produce=far_half)
    k.stream.done(reduced=1)

    half = pl.ds(pl.multiple_of(net.r * 32, 32), 32)
    late = []

    def weight_block(kind, b):
        lanes = lane_block(b, 512)
        if kind == "edge":
            return k.aspp_rates.at[0, 2 * net.r, :, :, lanes], k.w_pyramid.at[pl.ds(10, 3), net.m]
        if kind == "point":
            return k.aspp_point.at[half, lanes], k.w_pyramid.at[0, net.m, half]
        if kind == "project":
            return k.project.at[:, half], k.w_project.at[net.m, :, half]
        return (
            k.aspp_rates.at[kind, 1, :, half, lanes],
            k.w_pyramid.at[pl.ds(1 + 3 * kind, 3), net.m, half],
        )

    def spread_weights(*kinds):
        for kind in kinds:
            src, dst = weight_block(kind, net.m)
            late.append(pltpu.make_async_copy(src, dst, k.local_sems.at[10 + len(late) // 4]))
            late[-1].start()
            for b, peer in branches:
                src, dst = weight_block(kind, b)
                late.append(net.send(src, dst, peer))

    spread_weights("edge")
    mean, inverse = statistics(net, k.reduced, k.mask, counts, k.out_1, k.in_1, counted)
    keep_rows(k.stats_1, mean, inverse)

    def activate_1(at):
        u = k.affine_1[0:1, :] * ((k.reduced[at, :] - mean) * inverse) + k.affine_1[1:2, :]
        rows_at = pl.ds(pl.multiple_of(at.start + 512, 128), 128)
        k.hidden[rows_at, lane_block(net.m)] = (u * sigmoid(u)).astype(BF16)

    each_rows(1536, 128, activate_1)
    gather_blocks(
        net, lambda b, at: k.hidden.at[pl.ds(at.start + 512, at.size), lane_block(b)], 1536
    )
    halo = send_halo(net, k.hidden)
    spread_weights("project", "point", 0)
    zero_margins(k.left, 8, 128)
    zero_margins(k.right, 8, 128)
    for load in loads:
        load.wait()
    halo.wait()
    k.stream.done(hidden=1)

    def dilated_rows(i, carry):
        total = 0.0
        for tap in range(3):
            rows_at = pl.ds(pl.multiple_of((i * 3 + 4 * tap) * 128, 128), 384)
            total = total + mm(k.hidden[rows_at, :], k.w_taps[tap])
        k.dilated[pl.ds(pl.multiple_of(i * 384, 128), 384), :] = total[:, 128:256]
        k.left[pl.ds(i * 3, 3), 8:136, :] = total[:, 0:128].reshape(3, 128, 128)
        k.right[pl.ds(i * 3, 3), 8:136, :] = total[:, 256:384].reshape(3, 128, 128)
        return carry

    lax.fori_loop(0, 4, dilated_rows, 0)

    def add_columns(i, carry):
        at = pl.ds(pl.multiple_of(i * 128, 128), 128)
        k.dilated[at, :] = k.dilated[at, :] + k.left[i, 4:132, :] + k.right[i, 12:140, :]
        return carry

    lax.fori_loop(0, 12, add_columns, 0)
    k.stream.done(dilated=1)
    mean_2, inverse_2 = statistics(net, k.dilated, k.mask, counts, k.out_2, k.in_2, counted)
    keep_rows(k.stats_2, mean_2, inverse_2)

    def activate_2(at):
        u = k.affine_2[0:1, :] * ((k.dilated[at, :] - mean_2) * inverse_2) + k.affine_2[1:2, :]
        k.hidden_two[at, lane_block(net.m)] = (u * sigmoid(u)).astype(BF16)

    each_rows(1536, 128, activate_2)
    gather_blocks(net, lambda b, at: k.hidden_two.at[at, lane_block(b)], 1536)
    spread_weights(1, 2)
    k.stream.done(hidden_two=1)
    k.stream.need(w_expand=1)

    def expand_rows(at):
        k.expanded[at, :] = mm(k.hidden_two[at, :], k.w_expand[...])

    each_rows(1536, 384, expand_rows)
    k.stream.done(expanded=1)
    mean_3, inverse_3 = statistics(net, k.expanded, k.mask, counts, k.out_3, k.in_3, counted)
    keep_rows(k.stats_3, mean_3, inverse_3)
    def activate_3(at):
        u = k.affine_3[0:1, :] * ((k.expanded[at, :] - mean_3) * inverse_3) + k.affine_3[1:2, :]
        u = u + k.x[at, :].astype(F32)
        k.trunk[at, :] = (u * sigmoid(u)).astype(BF16)

    each_rows(1536, 32, activate_3)
    for copy in late:
        copy.wait()


def run_bottleneck(args):
    return call_kernel(
        bottleneck_forward,
        "bottleneck",
        0,
        args,
        dict(
            mask=((1536, 128), F32),
            w_reduce=((4, 512, 128), BF16),
            w_pyramid=((13, 4, 64, 512), BF16),
            w_project=((4, 5, 64, 256), BF16),
            reduced=((1536, 128), F32),
            stats_1=((8, 128), F32),
            hidden=((2560, 512), BF16),
            dilated=((1536, 128), F32),
            stats_2=((8, 128), F32),
            hidden_two=((1536, 512), BF16),
            expanded=((1536, 512), F32),
            stats_3=((8, 512), F32),
            trunk=((1536, 512), BF16),
        ),
        dict(
            w_taps=pltpu.VMEM((3, 512, 384), BF16),
            part=pltpu.VMEM((4, 1536, 128), F32),
            **scatter_scratch("sum", 1536, 128),
            left=pltpu.VMEM((12, 144, 128), F32),
            right=pltpu.VMEM((12, 144, 128), F32),
            **exchange_scratch(1),
            **exchange_scratch(2),
            **exchange_scratch(3),
            local_sems=pltpu.SemaphoreType.DMA((16,)),
        ),
        96,
        hbm=dict(conv_reduce=1, w_dilated=1, aspp_point=1, aspp_rates=1, project=1, w_pyramid=1, w_project=1),
        stream=dict(x=1, w_expand=1, mask=1, w_reduce=1, reduced=1, hidden=1, dilated=1, hidden_two=1, expanded=1),
    )


def pyramid_forward(net, k):
    counted, counts = pixel_count(k.boxes), tile_counts(net, k.boxes)
    area = (k.boxes[net.z, 2] * k.boxes[net.z, 3]).astype(F32)
    near = [
        (lax.rem(net.m + a, 4), lax.rem(net.r + b, 2), net.z)
        for a in range(4)
        for b in range(2)
        if a or b
    ]
    own_rows = pl.ds(pl.multiple_of(net.r * 32, 32), 32)
    common = (pl.ds(0, 10), slice(None), own_rows)
    every = (slice(None), slice(None), own_rows)
    weight_copies = [
        pltpu.make_async_copy(source.at[view], target.at[view], k.local_sems.at[i])
        for i, (source, target, view) in enumerate(
            (
                (k.far_pyramid, k.w_pyramid, common),
                (k.far_pyramid, k.w_pyramid, pl.ds(10, 3)),
                (k.far_slots, k.w_slots, every),
            )
        )
    ]
    for copy in weight_copies:
        copy.start()
    greet(net.group + [peer for i, peer in enumerate(near) if i])
    weight_copies.append(net.send(k.far_pyramid.at[common], k.w_pyramid.at[common], net.core))
    weight_copies.append(net.send(k.far_slots.at[every], k.w_slots.at[every], net.core))

    for b in range(4):
        k.affine_b[0:2, b * 64 : b * 64 + 64] = k.branch_norms[:, b, :]
    for i in range(2):
        k.affine_p[0:2, i * 64 : i * 64 + 64] = k.norm_project[...]
        k.affine_p[2:4, i * 64 : i * 64 + 64] = k.norm_pooling[...]
    k.head_rows[...] = jnp.zeros((32, 256), F32)
    k.head_rows[0:22, :] = k.head_weight[...].astype(F32)

    k.stream.need(mask=1)

    (own_sum,) = column_sums(
        lambda at: (k.trunk[at, :].astype(F32) * wide(k.mask[at, :], 512),), 1536, 512, 1
    )
    k.out_pool[...] = jnp.broadcast_to(own_sum, (8, 512))
    place = net.m * 2 + net.r
    pool_copies = [net.send(k.out_pool, k.in_pool.at[place], peer) for peer in near]
    k.in_pool[place] = k.out_pool[...]

    zero_margins(k.cells, 40, 128)

    def fill(i, carry):
        at = pl.ds(pl.multiple_of(i * 128, 128), 128)
        k.cells[i, 40:168, :] = k.trunk[at, :].astype(F32)
        return carry

    lax.fori_loop(0, 12, fill, 0)

    def shifted(i, offset):
        cells = k.cells[pl.ds(i * 3, 3), 40 + offset : 168 + offset, :]
        return cells.reshape(384, 512).astype(BF16)

    def rows_of(i):
        return pl.ds(pl.multiple_of(i * 384, 128), 384)

    def edge_rows(i, carry):
        total = 0.0
        for j in range(3):
            total = total + mm_t(shifted(i, 12 * (j - 1)), k.w_pyramid[10 + j].reshape(256, 512))
        k.edge_out[rows_of(i), :] = total.astype(BF16)
        return carry

    weight_copies.pop(1).wait()
    lax.fori_loop(0, 4, edge_rows, 0)
    edge = net.send(k.edge_out, k.edge_in, net.core)

    def outer_rows(i, carry):
        second, third = 0.0, 0.0
        for j in range(3):
            second = second + mm_t(shifted(i, 24 * (j - 1)), k.w_pyramid[4 + j].reshape(256, 512))
        for j in range(3):
            third = third + mm_t(shifted(i, 36 * (j - 1)), k.w_pyramid[7 + j].reshape(256, 512))
        for b, block in enumerate(pair(second, third)):
            k.part[b, rows_of(i), 128:256] = block
        return carry

    def inner_rows(i, carry):
        point = mm_t(k.trunk[rows_of(i), :], k.w_pyramid[0].reshape(256, 512))
        first = k.edge_in[rows_of(i), :].astype(F32)
        for j in range(3):
            first = first + mm_t(shifted(i, 12 * (j - 1)), k.w_pyramid[1 + j].reshape(256, 512))
        for b, block in enumerate(pair(point, first)):
            k.part[b, rows_of(i), 0:128] = block
        return carry

    def alternate(body, half):
        def run(i, carry):
            return body(half + 2 * i, carry)

        lax.fori_loop(0, 2, run, 0)

    def half_tile(half):
        alternate(outer_rows, half)
        if half == 0:
            edge.wait()
        alternate(inner_rows, half)

    for copy in weight_copies:
        copy.wait()
    k.stream.done(w_pyramid=1)

    sum_scatter(net, k.part, scatter_refs(k, "sum"), k.branches, produce=half_tile)

    low_256 = lax.broadcasted_iota(jnp.int32, (256, 128), 1) < 64
    odd = lax.rem(net.m, 2) == 1

    def slot(s):
        lanes = lane_block(net.m // 2)
        block = jnp.concatenate([k.w_slots[b, s, :, lanes] for b in range(4)], axis=0).astype(F32)
        return jnp.where(odd, pltpu.roll(block, 64, 1), block)

    for s in range(0, 4, 2):
        both = jnp.where(low_256, slot(s), pltpu.roll(slot(s + 1), 64, 1))
        k.w_project[:, s * 64 : s * 64 + 128] = both.astype(BF16)
    k.w_slot[...] = jnp.where(low_256, slot(4), 0.0).astype(BF16)
    k.w_pool[0:64, :] = k.aspp_pool[...]
    k.w_pool[64:128, :] = k.aspp_pool[...]

    for copy in pool_copies:
        copy.wait()
    for b in range(4):
        pooled = (k.in_pool[2 * b, 0:1, :] + k.in_pool[2 * b + 1, 0:1, :]) / area
        k.pooled[:, b * 512 : b * 512 + 512] = jnp.broadcast_to(pooled, (16, 512)).astype(BF16)
    pool_conv = mm_t(k.pooled[...], k.w_pool[...])[0:1, :]
    mean, inverse = statistics(
        net, k.branches, k.mask, counts, k.out_1, k.in_1, counted, extra=pool_conv
    )
    every = k.in_1[0:4, 4, :]
    pool_mean = jnp.sum(every, axis=0, keepdims=True) / 4.0
    pool_gap = every - pool_mean
    pool_inverse = lax.rsqrt(jnp.sum(pool_gap * pool_gap, axis=0, keepdims=True) / 4.0 + EPS)
    pool_normed = pool_gap * pool_inverse
    pool_gain, pool_bias = k.affine_p[2:3, :], k.affine_p[3:4, :]
    pool_u = pool_gain * pool_normed + pool_bias
    k.rows_scratch[0:4, :] = pool_u * sigmoid(pool_u)
    pool_act = jnp.broadcast_to(k.rows_scratch[pl.ds(net.z, 1), :], (16, 128)).astype(BF16)

    def normed_branch(at):
        return (k.branches[at, :] - mean) * inverse

    gain_b, bias_b = k.affine_b[0:1, :], k.affine_b[1:2, :]

    def activate_branches(at):
        u = gain_b * normed_branch(at) + bias_b
        k.spatial[at, :] = (u * sigmoid(u)).astype(BF16)

    each_rows(1536, 64, activate_branches)

    pool_row = mm_t(pool_act, k.w_slot[...])[0:1, :]

    def project_rows(i, carry):
        at = pl.ds(pl.multiple_of(i * 192, 64), 192)
        below = pl.ds(pl.multiple_of(i * 192 + 768, 64), 192)
        first = mm_t(k.spatial[at, :], k.w_project[...]) + pool_row
        second = mm_t(k.spatial[below, :], k.w_project[...]) + pool_row
        for b, block in enumerate(pair(first, second)):
            k.part_2[b, at, :] = block
        return carry

    def project_half(half):
        alternate(project_rows, half)

    low_128 = lax.broadcasted_iota(jnp.int32, (128, 128), 1) < 64

    def pair_mask(at):
        below = pl.ds(pl.multiple_of(at.start + 768, 128), 128)
        k.mask_pairs[at, :] = jnp.where(low_128, k.mask[at, :], k.mask[below, :])

    each_rows(768, 128, pair_mask)
    sum_scatter(net, k.part_2, scatter_refs(k, "sum2"), k.projected, produce=project_half)
    mean_p, inverse_p = statistics(
        net, k.projected, k.mask_pairs, counts, k.out_2, k.in_2, counted, folded=True
    )
    gain_p, bias_p = k.affine_p[0:1, :], k.affine_p[1:2, :]

    def normed_projected(at):
        return (k.projected[at, :] - mean_p) * inverse_p

    def activate_projected(at):
        u = gain_p * normed_projected(at) + bias_p
        k.gathered[net.m, at, :] = (u * sigmoid(u)).astype(BF16)

    each_rows(768, 128, activate_projected)
    gather_blocks(net, lambda b, at: k.gathered.at[b, at], 768)

    def spread(source, target):
        def body(at):
            first, second = unpair([source[b, at, :].astype(F32) for b in range(4)])
            target[at, :] = first.astype(BF16)
            target[pl.ds(pl.multiple_of(at.start + 768, 128), 128), :] = second.astype(BF16)

        each_rows(768, 128, body)

    k.features[...] = k.gathered[net.m]
    spread(k.gathered, k.wide_features)

    class_row = lax.broadcasted_iota(jnp.int32, (32, 512), 0)
    is_class, is_depth = class_row < 19, class_row == 19
    is_normal = (class_row == 20) | (class_row == 21)
    tile_row = lax.broadcasted_iota(jnp.int32, (32, 128), 0)
    bias_column = jnp.zeros((32, 128), F32)
    for c in range(22):
        bias_column = jnp.where(tile_row == c, k.head_bias[c], bias_column)
    task = [jnp.exp(jnp.full((32, 128), -k.log_vars[t], F32)) / counted for t in range(3)]
    weight_column = jnp.where(tile_row < 19, task[0], jnp.where(tile_row == 19, task[1], task[2]))
    bias_column, weight_column = wide(bias_column, 512), wide(weight_column, 512)
    k.head[...] = k.head_rows[...].astype(BF16)
    top_row, left_edge = k.boxes[net.z, 0], k.boxes[net.z, 1]
    bottom_row, right_edge = top_row + k.boxes[net.z, 2], left_edge + k.boxes[net.z, 3]
    lane = lax.broadcasted_iota(jnp.int32, (1, 512), 1)

    def four_rows(rows):
        return jnp.concatenate(rows, axis=1)
    loss_sums, bias_sums = 0.0, 0.0
    for chunk in range(3):
        at = pl.ds(chunk * 512, 512)
        logits = mm_t(k.head[...], k.wide_features[at, :]) + bias_column
        row_id, column_id = net.r * 12 + chunk * 4 + lane // 128, lane % 128
        inside = (row_id >= top_row) & (row_id < bottom_row)
        inside = inside & (column_id >= left_edge) & (column_id < right_edge)
        inside = jnp.where(inside, 1.0, 0.0)
        span = range(chunk * 4, chunk * 4 + 4)
        label = four_rows([k.labels[y] for y in span])
        target = jnp.where(is_depth, four_rows([k.depth[y] for y in span]), 0.0)
        for n in range(2):
            normal = four_rows([k.normal[y, n : n + 1, :] for y in span])
            target = jnp.where(class_row == 20 + n, normal, target)
        top = jnp.max(jnp.where(is_class, logits, -jnp.inf), axis=0, keepdims=True)
        powers = jnp.where(is_class, jnp.exp(jnp.where(is_class, logits - top, 0.0)), 0.0)
        power_sum = jnp.sum(powers, axis=0, keepdims=True)
        onehot = jnp.where(class_row == label, 1.0, 0.0)
        cross = jnp.log(power_sum) + top - jnp.sum(logits * onehot, axis=0, keepdims=True)
        gap = logits - target
        smooth = jnp.sqrt(gap * gap + 1.0)
        loss = jnp.where(class_row == 0, cross, 0.0)
        loss = jnp.where(is_depth, smooth - 1.0, loss)
        loss = jnp.where(is_normal, gap * gap, loss) * inside
        grad = jnp.where(is_class, powers / power_sum - onehot, 0.0)
        grad = jnp.where(is_depth, gap / smooth, grad)
        grad = jnp.where(is_normal, 2.0 * gap, grad) * (weight_column * inside)
        loss_sums = loss_sums + jnp.sum(loss, axis=1, keepdims=True)
        bias_sums = bias_sums + jnp.sum(grad, axis=1, keepdims=True)
        high = grad.astype(BF16)
        k.grad_logits[0:32, at] = high
        k.grad_logits[32:64, at] = (grad - high.astype(F32)).astype(BF16)
    head_terms = mm(k.grad_logits[...], k.wide_features[...])
    k.out_head[:, 0:256] = head_terms[0:32, :] + head_terms[32:64, :]
    first_lane = lax.broadcasted_iota(jnp.int32, (32, 128), 1) == 0
    k.out_head[:, 256:384] = jnp.where(first_lane, bias_sums, loss_sums)
    quarter = pl.ds(pl.multiple_of(net.m * 8, 8), 8)
    head_copies = [
        net.send(k.out_head.at[quarter], k.in_head.at[net.slot], peer) for peer in net.group
    ]
    k.in_head[net.slot] = k.out_head[quarter, :]

    own_head = k.head_rows[:, lane_block(net.m // 2)]
    own_head = jnp.where(odd, pltpu.roll(own_head, 64, 1), own_head)
    own_head = jnp.where(low_128[0:32, :], own_head, 0.0)
    head_low = jnp.concatenate([own_head, own_head], axis=0).astype(BF16)
    own_head = pltpu.roll(own_head, 64, 1)
    head_high = jnp.concatenate([own_head, own_head], axis=0).astype(BF16)
    k.grad_p[...] = tm_m(k.grad_logits[:, 0:768], head_low) + tm_m(
        k.grad_logits[:, 768:1536], head_high
    )

    def back_features(at):
        k.grad_p[at, :] = k.grad_p[at, :] * slope(gain_p * normed_projected(at) + bias_p)

    each_rows(768, 128, back_features)
    bias_grad, gain_grad = gradient_sums(
        net, k.grad_p, normed_projected, k.out_3, k.in_3, folded=True
    )
    keep_rows(k.norm_p, gain_grad, bias_grad)

    def back_projected(at):
        shared = k.mask_pairs[at, :] / counted * gain_p
        grad = gain_p * k.grad_p[at, :] - shared * (bias_grad + normed_projected(at) * gain_grad)
        k.gathered_grad[net.m, at, :] = (inverse_p * grad).astype(BF16)

    each_rows(768, 128, back_projected)
    gather_blocks(net, lambda b, at: k.gathered_grad.at[b, at], 768)
    spread(k.gathered_grad, k.grad_projected)
    (pixel_sum,) = column_sums(lambda at: (k.grad_projected[at, :].astype(F32),), 1536, 256, 1)
    row_16 = lax.broadcasted_iota(jnp.int32, (16, 256), 0)
    terms = jnp.zeros((16, 256), F32)
    for i, term in enumerate(split_three(pixel_sum)):
        terms = jnp.where(row_16 == i, term.astype(F32), terms)
    terms = terms.astype(BF16)
    tall = jnp.concatenate([terms] * 8, axis=0)
    pool_grad = jnp.sum(mm(tall, k.w_slot[...]), axis=0, keepdims=True) * 0.125

    def project_gradient():
        for b in range(2):
            lanes = slice(b * 128, b * 128 + 128)
            grad = tm_m(k.grad_projected[:, lanes], k.spatial[...])
            k.grad_project[b * 4 : b * 4 + 4, :, 0:256] = grad.reshape(4, 32, 256).astype(BF16)
        grad = tm_m(terms, pool_act)
        k.grad_project[:, :, 256:384] = grad.reshape(8, 32, 128).astype(BF16)

    def back_spatial(at):
        grad = mm(k.grad_projected[at, :], k.w_project[...])
        k.grad_b[at, :] = grad * slope(gain_b * normed_branch(at) + bias_b)

    each_rows(1536, 128, back_spatial)
    bias_grad_b, gain_grad_b = gradient_sums(
        net,
        k.grad_b,
        normed_branch,
        k.out_4,
        k.in_4,
        extra=pool_grad,
        meanwhile=project_gradient,
    )
    keep_rows(k.norm_b, gain_grad_b, bias_grad_b)

    pool_terms = k.in_4[0:4, 4, :] + k.in_4[4:8, 4, :]
    pool_terms = pool_terms * slope(pool_u)
    pool_bias_grad = jnp.sum(pool_terms, axis=0, keepdims=True)
    pool_gain_grad = jnp.sum(pool_terms * pool_normed, axis=0, keepdims=True)
    keep_rows(k.norm_pool, pool_gain_grad, pool_bias_grad)
    pool_back = pool_inverse * (
        pool_gain * pool_terms
        - pool_gain / 4.0 * (pool_bias_grad + pool_normed * pool_gain_grad)
    )
    low = lax.broadcasted_iota(jnp.int32, (4, 128), 1) < 64
    k.rows_scratch[4:8, :] = jnp.where(low, pool_back, 0.0)
    grad_conv = jnp.broadcast_to(k.rows_scratch[pl.ds(net.z + 4, 1), :], (16, 128)).astype(BF16)
    spread_back = mm(grad_conv, k.w_pool[...])[0:8, :]
    for b in range(4):
        k.out_back[b] = spread_back[:, b * 512 : b * 512 + 512]
    back_copies = [
        net.send(k.out_back.at[lax.rem(net.m + a, 4)], k.in_back.at[a], (lax.rem(net.m + a, 4), net.r, net.z))
        for a in range(1, 4)
    ]

    only_first = lax.broadcasted_iota(jnp.int32, (16, 128), 0) == 0
    one_row = jnp.where(only_first, grad_conv.astype(F32) * 0.5, 0.0).astype(BF16)
    for e in range(8):
        grad = tm_m(one_row, k.pooled[:, e * 256 : e * 256 + 256])
        k.grad_pool[e] = grad[0:64, :].astype(BF16)

    def back_branches(at):
        shared = wide(k.mask[at, :], 256) / counted * gain_b
        grad = gain_b * k.grad_b[at, :] - shared * (bias_grad_b + normed_branch(at) * gain_grad_b)
        k.grad_branches[at, :] = (inverse * grad).astype(BF16)

    for copy in back_copies:
        copy.wait()
    k.grad_pooled[...] = (k.out_back[net.m] + k.in_back[1] + k.in_back[2] + k.in_back[3]) / area
    for copy in head_copies:
        copy.wait()
    k.head_sums[quarter, :] = jnp.sum(k.in_head[...], axis=0)
    head_copies = [
        net.send(k.head_sums.at[quarter], k.head_sums.at[quarter], (lax.rem(net.m + a, 4), net.r, net.z))
        for a in range(1, 4)
    ]
    each_rows(1536, 64, back_branches)
    for copy in head_copies:
        copy.wait()


def run_pyramid(args):
    return call_kernel(
        pyramid_forward,
        "pyramid",
        1,
        args,
        dict(
            w_pyramid=((13, 4, 64, 512), BF16),
            features=((768, 128), BF16),
            norm_p=((8, 128), F32),
            grad_project=((8, 32, 384), BF16),
            grad_pool=((8, 64, 256), BF16),
            norm_b=((8, 256), F32),
            norm_pool=((8, 128), F32),
            grad_branches=((1536, 256), BF16),
            grad_pooled=((8, 512), F32),
            head_sums=((32, 384), F32),
        ),
        dict(
            w_slots=pltpu.VMEM((4, 5, 64, 256), BF16),
            local_sems=pltpu.SemaphoreType.DMA((3,)),
            affine_b=pltpu.VMEM((8, 256), F32),
            affine_p=pltpu.VMEM((8, 128), F32),
            head_rows=pltpu.VMEM((32, 256), F32),
            head=pltpu.VMEM((32, 256), BF16),
            pooled=pltpu.VMEM((16, 2048), BF16),
            spatial=pltpu.VMEM((1536, 256), BF16),
            grad_projected=pltpu.VMEM((1536, 256), BF16),
            w_project=pltpu.VMEM((256, 256), BF16),
            w_slot=pltpu.VMEM((256, 128), BF16),
            w_pool=pltpu.VMEM((128, 2048), BF16),
            mask_pairs=pltpu.VMEM((768, 128), F32),
            out_pool=pltpu.VMEM((8, 512), F32),
            in_pool=pltpu.VMEM((8, 8, 512), F32),
            cells=pltpu.VMEM((12, 208, 512), F32),
            edge_out=pltpu.VMEM((1536, 256), BF16),
            edge_in=pltpu.VMEM((1536, 256), BF16),
            part=pltpu.VMEM((4, 1536, 256), F32),
            **scatter_scratch("sum", 1536, 256),
            branches=pltpu.VMEM((1536, 256), F32),
            rows_scratch=pltpu.VMEM((8, 128), F32),
            part_2=pltpu.VMEM((4, 768, 128), F32),
            **scatter_scratch("sum2", 768, 128),
            projected=pltpu.VMEM((768, 128), F32),
            gathered=pltpu.VMEM((4, 768, 128), BF16),
            wide_features=pltpu.VMEM((1536, 256), BF16),
            grad_logits=pltpu.VMEM((64, 1536), BF16),
            out_head=pltpu.VMEM((32, 384), F32),
            in_head=pltpu.VMEM((8, 8, 384), F32),
            grad_p=pltpu.VMEM((768, 128), F32),
            gathered_grad=pltpu.VMEM((4, 768, 128), BF16),
            grad_b=pltpu.VMEM((1536, 256), F32),
            out_back=pltpu.VMEM((4, 8, 512), F32),
            in_back=pltpu.VMEM((4, 8, 512), F32),
            **exchange_scratch(1),
            **exchange_scratch(2),
            **exchange_scratch(3),
            **exchange_scratch(4),
        ),
        96,
        smem=dict(boxes=1, head_bias=1, log_vars=1),
        hbm=dict(far_pyramid=1, far_slots=1),
        stream=dict(mask=1, w_pyramid=1),
    )


def core_halves(net, whole, arrived):
    away = pl.ds(pl.multiple_of(4 - 4 * net.r, 4), 4)
    return net.send(whole.at[away], arrived, net.core)


def add_halves(net, whole, arrived, target):
    for z in range(4):
        total = whole[4 * net.r + z].astype(F32) + arrived[z].astype(F32)
        target[z] = total.astype(target.dtype)


def chunk_of(net):
    return lambda z: 2 * lax.rem(z + net.m, 2) + z // 2


def along_z(net, source, target, chunk=lambda z: z):
    copies = []
    for d in (1, 2, 3):
        there = lax.rem(net.z + d, 4)
        copies.append(
            net.send(source.at[chunk(there)], target.at[d - 1], (net.m, net.r, there))
        )
    return copies


def finish_z(net, half, arrived, chunk=lambda z: z):
    return half[chunk(net.z)].astype(F32) + sum(arrived[d].astype(F32) for d in range(3))


class PairSums:
    def __init__(self, net, half, other, pair, last):
        self.net, self.half, self.other, self.pair, self.last = net, half, other, pair, last
        kept, away = lax.rem(net.z + net.m, 2), lax.rem(net.z + net.m + 1, 2)
        self.kept = 2 * kept
        beside = net.z + 1 - 2 * lax.rem(net.z, 2)
        self.first = self.copy(half.at[pl.ds(2 * away, 2)], other, beside)
        self.high = net.z // 2
        if last is not None:
            self.second = self.copy(pair.at[1 - self.high], last, net.z + 2 - 4 * self.high)

    def copy(self, src, dst, z):
        net, i = self.net, self.net.count
        net.count += 1
        return pltpu.make_async_remote_copy(
            src_ref=src,
            dst_ref=dst,
            send_sem=net.send_sems.at[i],
            recv_sem=net.recv_sems.at[i],
            device_id=(net.m, net.r, z),
            device_id_type=MESH,
        )

    def go_on(self, half):
        self.first.wait()

        def body(i, carry):
            for h in range(2):
                total = half[self.kept + h, i].astype(F32) + self.other[h, i].astype(F32)
                self.pair[h, i] = total.astype(BF16)
            return carry

        lax.fori_loop(0, half.shape[1], body, 0)

    def finish(self, target):
        self.second.wait()

        def body(i, carry):
            total = self.pair[self.high, i].astype(F32) + self.last[i].astype(F32)
            target[0, i] = total[:, 0:256].astype(BF16)
            target[1, i] = total[:, 256:512].astype(BF16)
            return carry

        lax.fori_loop(0, target.shape[1], body, 0)


def pyramid_backward(net, k):
    counted = pixel_count(k.boxes)
    greet([net.side, net.over] + net.group)
    k.blocks[net.m] = k.grad_branches[...]
    small = [
        core_halves(net, k.grad_project, k.core_project),
        core_halves(net, k.grad_pool, k.core_pool),
    ]
    for c in range(4):
        zero_margins(k.cells.at[c], 40, 128)

    def rows_of(i, size=384):
        return pl.ds(pl.multiple_of(i * size, 128), size)

    low = lax.broadcasted_iota(jnp.int32, (128, 128), 1) < 64
    near = net.m // 2
    far = 1 - near
    mine_first = net.r == near
    mine_second = net.r == far

    def both(source, pair_of, i, lane):
        at = slice(lane * 128, lane * 128 + 128)
        left = source[2 * pair_of, rows_of(i, 128), at].astype(F32)
        right = source[2 * pair_of + 1, rows_of(i, 128), at].astype(F32)
        first = jnp.where(low, left, pltpu.roll(right, 64, 1))
        return first, jnp.where(low, pltpu.roll(left, 64, 1), right)

    def shift_rows(pair_of, i, cell, rate, base):
        for j in range(3):
            start = 40 - rate * (j - 1)
            block = k.cells[cell, i, start : start + 128, :].astype(BF16)
            k.shifts[base + j, rows_of(i, 128), lane_block(pair_of)] = block

    def build(pair_of):
        def fill(i, carry):
            point, first = both(k.blocks, pair_of, i, 0)
            k.shifts[0, rows_of(i, 128), lane_block(pair_of)] = point.astype(BF16)
            second, third = both(k.blocks, pair_of, i, 1)
            k.cells[0, i, 40:168, :] = first
            k.cells[1, i, 40:168, :] = second
            k.cells[2, i, 40:168, :] = third
            return carry

        lax.fori_loop(0, 12, fill, 0)

        def spread(i, carry):
            for cell, rate, base in ((0, 12, 1), (1, 24, 4), (2, 36, 7)):
                shift_rows(pair_of, i, cell, rate, base)
            return carry

        lax.fori_loop(0, 12, spread, 0)

    def build_edge(pair_of):
        def fill(i, carry):
            k.cells[3, i, 40:168, :] = both(k.other, pair_of, i, 0)[1]
            return carry

        lax.fori_loop(0, 12, fill, 0)

        def spread(i, carry):
            shift_rows(pair_of, i, 3, 12, 10)
            return carry

        lax.fori_loop(0, 12, spread, 0)

    def weight_gradients(pair_of, between=None):
        owners = pl.ds(4 * pair_of, 4)

        def run(start, stop, shift):
            def body(t, carry):
                grad = tm_m(k.shifts[t, :, lane_block(pair_of)], k.trunk[...])
                k.grad_pyramid[owners, t + shift] = grad.reshape(4, 32, 512).astype(BF16)
                return carry

            lax.fori_loop(start, stop, body, 0)

        run(0, 1, 0)
        run(1, 4, 3)
        run(10, 13, net.r * 6 - 9)
        for j in range(3):
            k.grad_pyramid[owners, 7 - net.r * 6 + j] = jnp.zeros((4, 32, 512), BF16)
        if between is not None:
            between()
        run(4, 10, 6)

    def beside(pair_of):
        view = (pl.ds(2 * pair_of, 2), slice(None), pl.ds(0, 128))
        return net.send(k.blocks.at[view], k.other.at[pl.ds(2 * pair_of, 2)], net.core)

    def to_core(pair_of, low, high):
        i = net.count
        net.count += 1
        taps = pl.ds(low, high - low)
        return pltpu.make_async_remote_copy(
            src_ref=k.grad_pyramid.at[pl.ds(4 * pair_of, 4), taps],
            dst_ref=k.core_pyramid.at[:, taps],
            send_sem=net.send_sems.at[i],
            recv_sem=net.recv_sems.at[i],
            device_id=net.core,
            device_id_type=MESH,
        )

    def add_core(pair_of, low, high):
        def body(i, carry):
            for z in range(4):
                total = k.grad_pyramid[4 * pair_of + z, i].astype(F32)
                total = total + k.core_pyramid[z, i].astype(F32)
                k.half_pyramid[z, i] = total.astype(BF16)
            return carry

        lax.fori_loop(low, high, body, 0)

    first_swap = []

    def near_pair():
        copy = beside(near)
        build(near)
        copy.wait()
        build_edge(near)
        k.stream.need(trunk=1)
        weight_gradients(near)
        first_swap.append(to_core(near, 0, 16))
        pl.when(mine_second)(first_swap[0].start)

    gather_blocks(net, lambda b, at: k.blocks.at[b, at], 1536, meanwhile=near_pair)
    copy = beside(far)
    build(far)
    for swap in small:
        swap.wait()
    add_halves(net, k.grad_project, k.core_project, k.half_project)
    add_halves(net, k.grad_pool, k.core_pool, k.half_pool)
    small_moves = along_z(net, k.half_project, k.z_project, chunk_of(net))
    small_moves = small_moves + along_z(net, k.half_pool, k.z_pool)
    copy.wait()
    build_edge(far)
    pair_sums = PairSums(net, k.half_pyramid, k.z_other, k.z_pair, None)

    @pl.when(mine_first)
    def _():
        first_swap[0].wait_recv()
        add_core(near, 0, 16)
        pair_sums.first.start()

    def trunk_rows(i, carry):
        total = 0.0
        for t in range(13):
            total = total + mm(k.shifts[t, rows_of(i), :], k.w_pyramid[t])
        k.shortcut[rows_of(i), :] = total
        return carry

    k.stream.need(w_pyramid=1, expanded=1, x=1, mask=1)
    lax.fori_loop(0, 4, trunk_rows, 0)
    mean, inverse = k.stats_3[0:1, :], k.stats_3[1:2, :]
    gain, bias = k.affine_3[0:1, :], k.affine_3[1:2, :]
    pooled = k.grad_pooled[0:1, :]

    def normed(at):
        return (k.expanded[at, :] - mean) * inverse

    def back_trunk(at):
        u = gain * normed(at) + bias + k.x[at, :].astype(F32)
        grad = k.shortcut[at, :] + wide(k.mask[at, :], 512) * pooled
        k.shortcut[at, :] = grad * slope(u)

    each_rows(1536, 32, back_trunk)
    k.stream.done(shortcut=1)

    second_swap = [to_core(far, 0, 10), to_core(far, 10, 16)]

    def far_gradients():
        weight_gradients(far, lambda: pl.when(mine_first)(second_swap[0].start))

        @pl.when(mine_first)
        def _():
            second_swap[1].start()
            pair_sums.go_on(k.half_pyramid)

    bias_grad, gain_grad = gradient_sums(
        net, k.shortcut, normed, k.out_1, k.in_1, meanwhile=far_gradients
    )
    keep_rows(k.norm_3, gain_grad, bias_grad)

    def back_expanded(at):
        shared = wide(k.mask[at, :], 512) / counted * gain
        grad = gain * k.shortcut[at, :] - shared * (bias_grad + normed(at) * gain_grad)
        k.grad_expanded[at, :] = (inverse * grad).astype(BF16)

    each_rows(1536, 32, back_expanded)
    k.stream.done(grad_expanded=1)
    for move_ in small_moves:
        move_.wait()
    k.sum_project[...] = finish_z(net, k.half_project, k.z_project, chunk_of(net)).astype(BF16)
    k.sum_pool[...] = finish_z(net, k.half_pool, k.z_pool)

    @pl.when(mine_second)
    def _():
        first_swap[0].wait_send()
        second_swap[0].wait_recv()
        add_core(far, 0, 10)
        second_swap[1].wait_recv()
        add_core(far, 10, 16)

    @pl.when(mine_first)
    def _():
        for swap in second_swap:
            swap.wait_send()


def run_pyramid_backward(args):
    return call_kernel(
        pyramid_backward,
        "pyramid_back",
        2,
        args,
        dict(
            shortcut=((1536, 512), F32),
            grad_expanded=((1536, 512), BF16),
            norm_3=((8, 512), F32),
            half_pyramid=((4, 16, 32, 512), BF16),
            z_pair=((2, 16, 32, 512), BF16),
            sum_project=((32, 384), BF16),
            sum_pool=((64, 256), F32),
        ),
        dict(
            half_project=pltpu.VMEM((4, 32, 384), BF16),
            half_pool=pltpu.VMEM((4, 64, 256), BF16),
            z_other=pltpu.VMEM((2, 16, 32, 512), BF16),
            z_project=pltpu.VMEM((3, 32, 384), BF16),
            z_pool=pltpu.VMEM((3, 64, 256), BF16),
            grad_pyramid=pltpu.VMEM((8, 16, 32, 512), BF16),
            core_pyramid=pltpu.VMEM((4, 16, 32, 512), BF16),
            core_project=pltpu.VMEM((4, 32, 384), BF16),
            core_pool=pltpu.VMEM((4, 64, 256), BF16),
            blocks=pltpu.VMEM((4, 1536, 256), BF16),
            other=pltpu.VMEM((4, 1536, 128), BF16),
            cells=pltpu.VMEM((4, 12, 208, 128), F32),
            shifts=pltpu.VMEM((13, 1536, 256), BF16),
            **exchange_scratch(1),
        ),
        48,
        stream=dict(w_pyramid=1, expanded=1, x=1, mask=1, trunk=1, shortcut=1, grad_expanded=1),
    )


def bottleneck_backward(net, k):
    counted = pixel_count(k.boxes)
    loads = load_taps(k)
    high, source = net.z // 2, net.slot // 2
    here = net.m * 8 + net.slot
    owners, givers = [], []
    for i in range(2):
        part = 2 * net.m + i
        column = 2 * net.r + lax.rem(net.z + net.m, 2)
        owners.append((column, part // 4, lax.rem(part, 4)))
        givers.append((source, net.m // 2, lax.rem(net.m + source, 2) + 2 * i))

    def elsewhere(device):
        return device[0] * 8 + device[1] * 4 + device[2] != here

    moves = elsewhere(owners[0])
    stays = jnp.logical_not(moves)
    greet(
        [net.side, net.over, net.diagonal] + net.group + [owners[1]],
        [(owners[0], moves), (givers[0], elsewhere(givers[0])), (givers[1], elsewhere(givers[1]))],
    )

    def to_owners(views, arrived, sem):
        base = net.count
        net.count += 2

        def copy(i, g, device):
            return pltpu.make_async_remote_copy(
                src_ref=views(i),
                dst_ref=arrived.at[g],
                send_sem=net.send_sems.at[base + i],
                recv_sem=net.recv_sems.at[base + g],
                device_id=device,
                device_id_type=MESH,
            )

        first, second = copy(0, high, owners[0]), copy(1, high, owners[1])
        kept = pltpu.make_async_copy(views(0), arrived.at[high], sem)

        def begin():
            pl.when(moves)(first.start)
            pl.when(stays)(kept.start)
            second.start()

        def wait():
            pl.when(moves)(first.wait_send)
            pl.when(stays)(kept.wait)
            second.wait_send()
            for g in range(2):
                pl.when(elsewhere(givers[g]))(copy(0, g, owners[1]).wait_recv)

        begin()
        return wait

    def lanes_for(i):
        return pl.ds(i * 256, 256)

    early = net.r == net.m // 2
    is_late = net.r == 1 - net.m // 2
    pair_sums = PairSums(net, k.far_half_pyramid, k.z_other, k.z_pair, k.z_last)

    odd_z = lax.rem(net.z, 2)
    lone = early & (odd_z == 0)
    beside = early & (odd_z == 1)
    stay = pltpu.make_async_copy(k.pyramid_sum, k.relay.at[0], k.local_sems.at[9])

    def remote(src, dst, send, arrive, device):
        return pltpu.make_async_remote_copy(
            src_ref=src,
            dst_ref=dst,
            send_sem=net.send_sems.at[send],
            recv_sem=net.recv_sems.at[arrive],
            device_id=device,
            device_id_type=MESH,
        )

    base = net.count
    net.count += 6
    to_side = remote(k.pyramid_sum, k.relay.at[0], base, base, net.side)
    across = (net.m ^ (2 + odd_z), net.r, net.z)
    to_across = remote(k.pyramid_sum, k.relay.at[1], base + 1, base + 1, across)
    plane = lax.rem(net.m + net.z, 2)

    def forward(e, i):
        device = (net.m, net.r if e == 0 else 1 - net.r, 2 * plane + i)
        return remote(
            k.relay.at[e, i], k.own_pyramid.at[high], base + 2 + 2 * e + i, base + 2 + high, device
        )

    forwards = [[forward(e, i) for i in range(2)] for e in range(2)]
    keep = pltpu.make_async_copy(k.relay.at[0, odd_z], k.own_pyramid.at[high], k.local_sems.at[12])
    keeps = early & (plane == high)

    def kept_here(i):
        return keeps & (odd_z == i)

    def begin_early():
        pl.when(lone)(stay.start)
        pl.when(beside)(to_side.start)

    def relay_early():
        pl.when(lone)(stay.wait)
        pl.when(beside)(to_side.wait)
        for i in range(2):
            pl.when(early & jnp.logical_not(kept_here(i)))(forwards[0][i].start)
        pl.when(keeps)(keep.start)

    def relay_late():
        pl.when(early)(to_across.wait_recv)
        for i in range(2):
            pl.when(early)(forwards[1][i].start)

    def wait_pyramid():
        pl.when(is_late)(to_across.wait_send)
        for i in range(2):
            pl.when(early & jnp.logical_not(kept_here(i)))(forwards[0][i].wait_send)
            pl.when(early)(forwards[1][i].wait_send)
        pl.when(keeps)(keep.wait)
        for g in range(2):
            local = early & (lax.rem(net.z // 2 + net.m, 2) + 2 * g == net.z)
            arrival = remote(k.relay.at[0, 0], k.own_pyramid.at[g], base, base + 2 + g, net.core)
            pl.when(jnp.logical_not(local))(arrival.wait_recv)


    k.stream.need(z_pair=1)
    pl.when(is_late)(pair_sums.first.start)
    pl.when(early)(pair_sums.second.start)
    wait_project = to_owners(lambda i: k.sum_project, k.own_project, k.local_sems.at[10])

    def rows_of(i, size=384):
        return pl.ds(pl.multiple_of(i * size, 128), size)

    def expand_half(half):
        for i in (half, half + 2):
            at = pl.ds(i * 384, 384)
            total = mm_t(k.grad_expanded[at, :], k.w_expand[...])
            for b in range(4):
                k.part[b, at, :] = total[:, b * 128 : b * 128 + 128]

    swaps, late_moves = [], []

    def expand_gradient():
        k.stream.need(hidden_two=1)

        def body(b, carry):
            grad = tm_m(k.hidden_two[:, lane_block(b)], k.grad_expanded[...])
            k.grad_expand[pl.ds(2 * b, 2)] = grad.reshape(2, 64, 512).astype(BF16)
            return carry

        lax.fori_loop(0, 4, body, 0)
        swaps.append(core_halves(net, k.grad_expand, k.core_expand))

    sum_scatter(net, k.part, scatter_refs(k, "sum"), k.grad_2, meanwhile=expand_gradient, produce=expand_half)
    k.stream.need(dilated=1, mask=1)

    def norm_back(grad, value, stats, affine, outgoing, incoming, store, kept, meanwhile=None):
        mean, inverse = stats[0:1, :], stats[1:2, :]
        gain, bias = affine[0:1, :], affine[1:2, :]

        def normed(at):
            return (value[at, :] - mean) * inverse

        def through(at):
            grad[at, :] = grad[at, :] * slope(gain * normed(at) + bias)

        each_rows(1536, 128, through)
        bias_grad, gain_grad = gradient_sums(
            net, grad, normed, outgoing, incoming, meanwhile=meanwhile
        )
        keep_rows(kept, gain_grad, bias_grad)

        def back(at):
            shared = k.mask[at, :] / counted * gain
            result = gain * grad[at, :] - shared * (bias_grad + normed(at) * gain_grad)
            store(at, (inverse * result).astype(BF16))

        each_rows(1536, 128, back)

    def store_2(at, value):
        k.grad_pad[pl.ds(pl.multiple_of(at.start + 512, 128), 128), :] = value

    def pass_expand():
        k.stream.need(half_pyramid=1)
        @pl.when(is_late)
        def _():
            pair_sums.go_on(k.half_pyramid)
            pair_sums.second.start()

        @pl.when(early)
        def _():
            pair_sums.finish(k.pyramid_sum)

        begin_early()
        swaps.pop().wait()
        add_halves(net, k.grad_expand, k.core_expand, k.half_expand)
        late_moves.extend(along_z(net, k.half_expand, k.z_expand))

    norm_back(
        k.grad_2,
        k.dilated,
        k.stats_2,
        k.affine_2,
        k.out_2,
        k.in_2,
        store_2,
        k.norm_2,
        meanwhile=pass_expand,
    )
    halo = send_halo(net, k.grad_pad)
    zero_margins(k.cells, 8, 128)
    halo.wait()

    def spread(i, carry):
        k.cells[i, 8:136, :] = k.grad_pad[rows_of(i, 128), :].astype(F32)
        for j in range(3):
            start = 8 - 4 * (j - 1)
            k.grad_taps[rows_of(i, 128), j * 128 : j * 128 + 128] = k.cells[
                i, start : start + 128, :
            ].astype(BF16)
        return carry

    lax.fori_loop(0, 20, spread, 0)
    for load in loads:
        load.wait()

    def dilated_rows(i, carry):
        total = 0.0
        for tap in range(3):
            at = pl.ds(pl.multiple_of((i * 3 + 8 - 4 * tap) * 128, 128), 384)
            total = total + mm_t(k.grad_taps[at, :], k.w_taps[tap])
        for b in range(4):
            k.part[b, rows_of(i), :] = total[:, b * 128 : b * 128 + 128]
        return carry

    def dilated_half(half):
        def run(i, carry):
            return dilated_rows(half + 2 * i, carry)

        lax.fori_loop(0, 2, run, 0)

    def dilated_gradient():
        k.stream.need(hidden=1)

        for i in range(3):

            def body(b, carry):
                band = k.hidden[pl.ds(i * 512, 1536), lane_block(b)]
                grad = tm_m(band, k.grad_taps[pl.ds(512, 1536), :])
                for j in range(3):
                    block = grad[:, j * 128 : j * 128 + 128].reshape(2, 64, 128)
                    rows = slice((i * 3 + j) * 64, (i * 3 + j) * 64 + 64)
                    k.grad_dilated[pl.ds(2 * b, 2), rows, :] = block.astype(BF16)
                return carry

            lax.fori_loop(0, 4, body, 0)
        swaps.append(core_halves(net, k.grad_dilated, k.core_dilated))

    sum_scatter(net, k.part, scatter_refs(k, "sum2"), k.grad_1, meanwhile=dilated_gradient, produce=dilated_half)
    k.stream.need(reduced=1)

    def store_1(at, value):
        k.grad_reduced[at, lane_block(net.m)] = value

    def pass_halves():
        @pl.when(is_late)
        def _():
            pair_sums.finish(k.pyramid_sum)
            to_across.start()

        relay_early()
        swaps.pop().wait()
        add_halves(net, k.grad_dilated, k.core_dilated, k.half_dilated)
        late_moves.extend(along_z(net, k.half_dilated, k.z_dilated))

    norm_back(
        k.grad_1,
        k.reduced,
        k.stats_1,
        k.affine_1,
        k.out_1,
        k.in_1,
        store_1,
        k.norm_1,
        meanwhile=pass_halves,
    )

    def reduce_gradients(pair_of):
        def body(i, carry):
            b = 2 * pair_of + i
            grad = tm_m(k.grad_reduced[:, lane_block(b)], k.x[...])
            k.grad_reduce[pl.ds(2 * b, 2)] = grad.reshape(2, 64, 512).astype(BF16)
            return carry

        lax.fori_loop(0, 2, body, 0)

    def near_gradients():
        relay_late()
        k.stream.need(x=1)
        reduce_gradients(net.m // 2)

    gather_blocks(
        net,
        lambda b, at: k.grad_reduced.at[at, lane_block(b)],
        1536,
        meanwhile=near_gradients,
    )

    reduce_gradients(1 - net.m // 2)
    swap = core_halves(net, k.grad_reduce, k.core_reduce)

    swap.wait()
    add_halves(net, k.grad_reduce, k.core_reduce, k.half_reduce)
    reduce_moves = along_z(net, k.half_reduce, k.z_reduce, chunk_of(net))

    k.stream.need(shortcut=1, w_reduce=1)

    def input_rows(at):
        total = k.shortcut[at, :]
        for b in range(4):
            total = total + mm_t(k.grad_reduced[at, b * 128 : b * 128 + 128], k.w_reduce[b])
        k.grad_input[at, :] = total

    each_rows(1536, 384, input_rows)
    k.stream.done(grad_input=1)
    for move_ in reduce_moves:
        move_.wait()
    k.sum_reduce[...] = finish_z(net, k.half_reduce, k.z_reduce, chunk_of(net)).astype(BF16)
    wait_reduce = to_owners(
        lambda i: k.sum_reduce.at[:, lanes_for(i)], k.own_reduce, k.local_sems.at[11]
    )
    for move_ in late_moves:
        move_.wait()
    k.sum_dilated[...] = finish_z(net, k.half_dilated, k.z_dilated)
    k.sum_expand[...] = finish_z(net, k.half_expand, k.z_expand)
    wait_pyramid()
    wait_project()
    wait_reduce()


def run_bottleneck_backward(args):
    return call_kernel(
        bottleneck_backward,
        "bottleneck_back",
        3,
        args,
        dict(
            grad_input=((1536, 512), F32),
            norm_2=((8, 128), F32),
            norm_1=((8, 128), F32),
            own_pyramid=((2, 16, 32, 256), BF16),
            own_project=((2, 32, 384), BF16),
            sum_dilated=((576, 128), F32),
            sum_expand=((64, 512), F32),
            own_reduce=((2, 64, 256), BF16),
        ),
        dict(
            grad_taps=pltpu.VMEM((2560, 384), BF16),
            grad_reduced=pltpu.VMEM((1536, 512), BF16),
            z_other=pltpu.VMEM((2, 16, 32, 512), BF16),
            z_last=pltpu.VMEM((16, 32, 512), BF16),
            relay=pltpu.VMEM((2, 2, 16, 32, 256), BF16),
            pyramid_sum=pltpu.VMEM((2, 16, 32, 256), BF16),
            sum_reduce=pltpu.VMEM((64, 512), BF16),
            grad_expand=pltpu.VMEM((8, 64, 512), BF16),
            core_expand=pltpu.VMEM((4, 64, 512), BF16),
            half_expand=pltpu.VMEM((4, 64, 512), BF16),
            z_expand=pltpu.VMEM((3, 64, 512), BF16),
            grad_reduce=pltpu.VMEM((8, 64, 512), BF16),
            core_reduce=pltpu.VMEM((4, 64, 512), BF16),
            half_reduce=pltpu.VMEM((4, 64, 512), BF16),
            z_reduce=pltpu.VMEM((3, 64, 512), BF16),
            grad_dilated=pltpu.VMEM((8, 576, 128), BF16),
            core_dilated=pltpu.VMEM((4, 576, 128), BF16),
            half_dilated=pltpu.VMEM((4, 576, 128), BF16),
            z_dilated=pltpu.VMEM((3, 576, 128), BF16),
            w_taps=pltpu.VMEM((3, 512, 384), BF16),
            part=pltpu.VMEM((4, 1536, 128), F32),
            **scatter_scratch("sum", 1536, 128),
            **scatter_scratch("sum2", 1536, 128),
            grad_2=pltpu.VMEM((1536, 128), F32),
            grad_1=pltpu.VMEM((1536, 128), F32),
            grad_pad=pltpu.VMEM((2560, 128), BF16),
            cells=pltpu.VMEM((20, 144, 128), F32),
            **exchange_scratch(2),
            **exchange_scratch(1),
            local_sems=pltpu.SemaphoreType.DMA((13,)),
        ),
        96,
        hbm=dict(w_dilated=1),
        stream=dict(z_pair=1, half_pyramid=1, hidden_two=1, dilated=1, mask=1, hidden=1, reduced=1, x=1, shortcut=1, w_reduce=1, grad_input=1),
    )


def finish(net, k):
    counted = pixel_count(k.boxes)
    odd = lax.rem(lax.axis_index("batch"), 2)

    def rows_for(i):
        return slice(i * 32, i * 32 + 32)

    nothing = jnp.zeros((64, 256), F32)
    for tap in (9, 10, 11, 15, 16, 17, 18, 19, 20, 24, 25, 26):
        k.grad_rates[tap] = nothing
    for slot in range(16):
        for i in range(2):
            block = k.own_pyramid[i, slot].astype(F32)
            if slot == 0:
                k.grad_point[rows_for(i), :] = block
            else:
                tap = slot - 1 if slot < 10 else slot + 2 if slot < 13 else slot + 8
                k.grad_rates[tap, rows_for(i), :] = block
    k.stream.done(grad_rates=1)
    k.stream.need(from_input=1)
    leave = pltpu.make_async_copy(k.from_input, k.grad_input, k.sem.at[0])
    leave.start()
    for y in range(6):
        turned = k.packed[y * 128 : y * 128 + 128, :].astype(F32).T.astype(BF16)
        k.features[y] = turned[0:64, :]
        k.features[y + 6] = turned[64:128, :]
    k.turned[...] = jnp.concatenate([k.own_project[i].astype(F32) for i in range(2)], axis=0).T
    for slot in range(5):
        start = pl.multiple_of(slot * 64 + odd * 32, 32)
        k.grad_project[slot] = k.turned[pl.ds(start, 32), :]
    k.grad_reduce[...] = jnp.concatenate(
        [k.own_reduce[i].astype(F32) for i in range(2)], axis=0
    ).T
    k.grad_dilated[...] = k.from_dilated[...].reshape(9, 64, 128)
    k.grad_expand[...] = k.from_expand[...]
    k.grad_pool[...] = k.from_pool[...]
    k.grad_norm_1[...] = k.norm_1[0:2, :]
    k.grad_norm_2[...] = k.norm_2[0:2, :]
    k.grad_norm_3[...] = k.norm_3[0:2, :]
    for b in range(4):
        k.grad_norm_b[:, b, :] = k.norm_b[0:2, b * 64 : b * 64 + 64]
    k.grad_norm_pool[...] = k.norm_pool[0:2, 0:64]
    k.grad_norm_p[...] = k.norm_p[0:2, 0:64]
    k.grad_head_weight[...] = k.head_sums[0:22, 0:256]
    columns = k.head_sums[:, 256:384].T
    k.grad_head_bias[...] = columns[0:1, 0:22]
    loss = columns[1:2, :]
    task = lax.broadcasted_iota(jnp.int32, (1, 32), 1)

    def total(inside):
        return jnp.sum(jnp.where(inside, loss, 0.0), axis=1, keepdims=True) / counted

    terms = [total(task == 0), total(task == 19), total((task == 20) | (task == 21))]
    lane = lax.broadcasted_iota(jnp.int32, (1, 128), 1)
    losses = jnp.where(lane == 0, terms[0], jnp.where(lane == 1, terms[1], terms[2]))
    log_vars = jnp.where(
        lane == 0, k.log_vars[0], jnp.where(lane == 1, k.log_vars[1], k.log_vars[2])
    )
    weighted = jnp.exp(-log_vars) * losses
    k.total_loss[...] = jnp.sum(
        jnp.where(lane < 3, weighted + log_vars, 0.0), axis=1, keepdims=True
    )
    k.grad_log_vars[...] = (1.0 - weighted)[:, 0:3]

    leave.wait()


def run_finish(args):
    return call_kernel(
        finish,
        "finish",
        None,
        args,
        dict(
            features=((12, 64, 128), BF16),
            total_loss=((1, 1), F32),
            grad_input=((1536, 512), F32),
            grad_reduce=((256, 128), F32),
            grad_dilated=((9, 64, 128), F32),
            grad_expand=((64, 512), F32),
            grad_norm_1=((2, 128), F32),
            grad_norm_2=((2, 128), F32),
            grad_norm_3=((2, 512), F32),
            grad_point=((64, 256), F32),
            grad_rates=((27, 64, 256), F32),
            grad_pool=((64, 256), F32),
            grad_norm_b=((2, 4, 64), F32),
            grad_norm_pool=((2, 64), F32),
            grad_project=((5, 32, 64), F32),
            grad_norm_p=((2, 64), F32),
            grad_head_weight=((22, 256), F32),
            grad_head_bias=((1, 22), F32),
            grad_log_vars=((1, 3), F32),
        ),
        dict(turned=pltpu.VMEM((384, 64), F32), sem=pltpu.SemaphoreType.DMA((1,))),
        0,
        hbm=dict(grad_input=1),
        stream=dict(from_input=1, grad_rates=1),
        smem=dict(boxes=1, log_vars=1),
    )


def fast_local(
    trunk_input,
    conv_reduce,
    conv_dilated,
    conv_expand,
    reduction_norm_params,
    dilated_norm_params,
    expansion_norm_params,
    aspp_point,
    aspp_rates,
    aspp_pool,
    branch_norms,
    pooling_norm_params,
    aspp_project,
    projection_norm_params,
    head_weight,
    head_bias,
    log_vars,
    crop_boxes,
    seg_labels,
    depth_target,
    normal_target,
):
    x = trunk_input.reshape(1536, 512)
    forward = run_bottleneck(
        dict(
            x=x,
            conv_reduce=conv_reduce,
            w_dilated=conv_dilated,
            w_expand=conv_expand,
            aspp_point=aspp_point,
            aspp_rates=aspp_rates,
            project=aspp_project.transpose(1, 0, 2),
            affine_1=reduction_norm_params,
            affine_2=dilated_norm_params,
            affine_3=expansion_norm_params,
            boxes=crop_boxes,
        )
    )
    middle = run_pyramid(
        dict(
            trunk=forward.trunk,
            mask=forward.mask,
            far_pyramid=forward.w_pyramid,
            branch_norms=branch_norms,
            norm_project=projection_norm_params,
            norm_pooling=pooling_norm_params,
            aspp_pool=aspp_pool,
            far_slots=forward.w_project,
            head_weight=head_weight.T,
            head_bias=head_bias,
            log_vars=log_vars,
            labels=seg_labels.transpose(1, 0, 2),
            depth=depth_target.transpose(1, 0, 2),
            normal=normal_target.transpose(0, 2, 1, 3).reshape(12, 2, 128),
            boxes=crop_boxes,
        )
    )
    back = run_pyramid_backward(
        dict(
            grad_branches=middle.grad_branches,
            w_pyramid=middle.w_pyramid.reshape(13, 256, 512),
            x=x,
            trunk=forward.trunk,
            expanded=forward.expanded,
            stats_3=forward.stats_3,
            affine_3=expansion_norm_params,
            mask=forward.mask,
            grad_pooled=middle.grad_pooled,
            grad_project=middle.grad_project,
            grad_pool=middle.grad_pool,
            boxes=crop_boxes,
        )
    )
    last = run_bottleneck_backward(
        dict(
            grad_expanded=back.grad_expanded,
            shortcut=back.shortcut,
            w_reduce=forward.w_reduce,
            half_pyramid=back.half_pyramid,
            z_pair=back.z_pair,
            sum_project=back.sum_project,
            x=x,
            hidden=forward.hidden,
            hidden_two=forward.hidden_two,
            w_expand=conv_expand,
            w_dilated=conv_dilated,
            dilated=forward.dilated,
            stats_2=forward.stats_2,
            affine_2=dilated_norm_params,
            reduced=forward.reduced,
            stats_1=forward.stats_1,
            affine_1=reduction_norm_params,
            mask=forward.mask,
            boxes=crop_boxes,
        )
    )
    done = run_finish(
        dict(
            from_input=last.grad_input,
            own_pyramid=last.own_pyramid,
            packed=middle.features,
            own_project=last.own_project,
            own_reduce=last.own_reduce,
            from_dilated=last.sum_dilated,
            from_expand=last.sum_expand,
            from_pool=back.sum_pool,
            norm_1=last.norm_1,
            norm_2=last.norm_2,
            norm_3=back.norm_3,
            norm_b=middle.norm_b,
            norm_pool=middle.norm_pool,
            norm_p=middle.norm_p,
            head_sums=middle.head_sums,
            log_vars=log_vars,
            boxes=crop_boxes,
        )
    )
    return (
        done.features.transpose(0, 2, 1).reshape(1, 12, 128, 64),
        done.total_loss.reshape(()),
        done.grad_input.reshape(1, 12, 128, 512),
        done.grad_reduce,
        done.grad_dilated.reshape(3, 3, 64, 128),
        done.grad_expand,
        done.grad_norm_1,
        done.grad_norm_2,
        done.grad_norm_3,
        done.grad_point,
        done.grad_rates.reshape(3, 3, 3, 64, 256),
        done.grad_pool,
        done.grad_norm_b,
        done.grad_norm_pool,
        done.grad_project.transpose(2, 0, 1),
        done.grad_norm_p,
        done.grad_head_weight.T,
        done.grad_head_bias.reshape(22),
        done.grad_log_vars.reshape(3),
    )


def local(
    trunk_input,
    conv_reduce,
    conv_dilated,
    conv_expand,
    reduction_norm_params,
    dilated_norm_params,
    expansion_norm_params,
    aspp_point,
    aspp_rates,
    aspp_pool,
    branch_norms,
    pooling_norm_params,
    aspp_project,
    projection_norm_params,
    head_weight,
    head_bias,
    log_vars,
    crop_boxes,
    seg_labels,
    depth_target,
    normal_target,
):
    image_inputs, tile_row_count, frame_columns, quarter = trunk_input.shape
    pixels = image_inputs * tile_row_count * frame_columns
    branch_part = aspp_point.shape[0]
    branch_total = lax.axis_size("branch")
    row_portion = 1.0 / lax.axis_size("rows")
    image_overall_count = float(crop_boxes.shape[0])
    first_image = lax.axis_index("batch") * image_inputs
    first_row = lax.axis_index("rows") * tile_row_count
    my_boxes = lax.dynamic_slice_in_dim(crop_boxes, first_image, image_inputs, 0)
    row_ids = first_row + jnp.arange(tile_row_count, dtype=jnp.int32)
    col_ids = jnp.arange(frame_columns, dtype=jnp.int32)
    inside_rows = (row_ids[None, :] >= my_boxes[:, 0:1]) & (
        row_ids[None, :] < my_boxes[:, 0:1] + my_boxes[:, 2:3]
    )
    inside_cols = (col_ids[None, :] >= my_boxes[:, 1:2]) & (
        col_ids[None, :] < my_boxes[:, 1:2] + my_boxes[:, 3:4]
    )
    valid_mask = (inside_rows[:, :, None] & inside_cols[:, None, :]).astype(jnp.float32)
    mask_column_vector = valid_mask.reshape(pixels, 1)
    mask_flat = valid_mask.reshape(pixels)
    pixel_number_count = jnp.sum((crop_boxes[:, 2] * crop_boxes[:, 3]).astype(jnp.float32))
    image_areas = (my_boxes[:, 2] * my_boxes[:, 3]).astype(jnp.float32)
    input_full = widen(trunk_input)
    reduced_output = forward_dot(input_full, conv_reduce).reshape(pixels, -1)
    normalized_first, standardized_first, inverse_deviation_first = norm_ahead_pass(
        reduced_output, mask_column_vector, pixel_number_count, reduction_norm_params
    )
    hidden_one = (
        jax.nn.silu(normalized_first)
        .astype(jnp.bfloat16)
        .reshape(image_inputs, tile_row_count, frame_columns, -1)
    )
    hidden_full = widen(pad_rows(hidden_one))
    dilated_out = 0.0
    for row_tap in range(3):
        band = hidden_full[:, 4 * row_tap : 4 * row_tap + tile_row_count]
        for col_tap in range(3):
            dilated_out = dilated_out + forward_dot(
                move(band, -(col_tap - 1) * 4, 2), conv_dilated[row_tap, col_tap]
            )
    normalized_second, standardized_second, inverse_deviation_second = norm_ahead_pass(
        dilated_out.reshape(pixels, -1), mask_column_vector, pixel_number_count, dilated_norm_params
    )
    hidden_two = (
        jax.nn.silu(normalized_second)
        .astype(jnp.bfloat16)
        .reshape(image_inputs, tile_row_count, frame_columns, -1)
    )
    hidden_two_full = widen(hidden_two)
    expanded_output = forward_dot(hidden_two_full, conv_expand).reshape(pixels, -1)
    normalized_third, standardized_third, inverse_deviation_third = norm_ahead_pass(
        expanded_output, mask_column_vector, pixel_number_count, expansion_norm_params
    )
    residual_sum = normalized_third + trunk_input.reshape(pixels, -1).astype(jnp.float32)
    trunk_out = (
        jax.nn.silu(residual_sum)
        .astype(jnp.bfloat16)
        .reshape(image_inputs, tile_row_count, frame_columns, quarter)
    )
    trunk_full = widen(trunk_out)
    branch_outs = [backward_dot(trunk_full, aspp_point)]
    for branch_id in range(3):
        dilation = RATES[branch_id]
        hops = dilation // tile_row_count
        partials = [0.0, 0.0, 0.0]
        for col_tap in range(3):
            shifted = move(trunk_full, -(col_tap - 1) * dilation, 2)
            products = backward_dot(shifted, stacked_taps(aspp_rates[branch_id], col_tap))
            for row_tap in range(3):
                partials[row_tap] = (
                    partials[row_tap]
                    + products[..., row_tap * branch_part : (row_tap + 1) * branch_part]
                )
        upper = send_down(partials[0].astype(jnp.bfloat16), hops).astype(jnp.float32)
        lower_part = send_up(partials[2].astype(jnp.bfloat16), hops).astype(jnp.float32)
        branch_outs.append(partials[1] + upper + lower_part)
    spatial_flattened = jnp.stack(branch_outs, axis=3).reshape(pixels, -1)
    branch_gain_bias = branch_norms.reshape(2, -1)
    normalized_spatial, standardized_spatial, inverse_deviation_spatial = norm_ahead_pass(
        spatial_flattened, mask_column_vector, pixel_number_count, branch_gain_bias
    )
    spatial_act = (
        jax.nn.silu(normalized_spatial)
        .astype(jnp.bfloat16)
        .reshape(image_inputs, tile_row_count, frame_columns, 4, branch_part)
    )
    pooled_local = lax.dot_general(
        valid_mask.astype(jnp.bfloat16),
        trunk_full,
        (((1, 2), (1, 2)), ((0,), (0,))),
        preferred_element_type=jnp.float32,
    )
    pooled = (over_rows(pooled_local) / image_areas[:, None]).astype(jnp.bfloat16)
    pooling_convolution = backward_dot(pooled, aspp_pool)
    normalized_poolbranch, standardized_poolbranch, inverse_deviation_poolbranch = norm_ahead_pass(
        pooling_convolution, row_portion, image_overall_count, pooling_norm_params
    )
    pool_act = jax.nn.silu(normalized_poolbranch).astype(jnp.bfloat16)
    pool_wide = jnp.broadcast_to(
        pool_act[:, None, None, None, :],
        (image_inputs, tile_row_count, frame_columns, 1, branch_part),
    )
    concat = jnp.concatenate([spatial_act, pool_wide], axis=3)
    concat_flat = widen(concat).reshape(pixels, -1)
    proj_kernel = (
        aspp_project.reshape(branch_part, 5, branch_total, branch_part)
        .transpose(0, 2, 1, 3)
        .reshape(branch_part, 5 * branch_total * branch_part)
    )
    projected_output = backward_dot(concat_flat, proj_kernel)
    normalized_projector, standardized_projector, inverse_deviation_projector = norm_ahead_pass(
        projected_output, mask_column_vector, pixel_number_count, projection_norm_params
    )
    features = (
        jax.nn.silu(normalized_projector)
        .astype(jnp.bfloat16)
        .reshape(image_inputs, tile_row_count, frame_columns, -1)
    )
    features_wide = widen(features).reshape(pixels, -1).astype(jnp.float32)
    head_wide = head_weight.astype(jnp.float32)
    logits = jnp.dot(features_wide, head_wide, precision=HIGH) + head_bias
    classes = head_bias.shape[0] - 3
    seg_logits = logits[:, :classes]
    labels_flat = seg_labels.reshape(pixels)
    classes_hot = (labels_flat[:, None] == jnp.arange(classes, dtype=jnp.int32)[None, :]).astype(
        jnp.float32
    )
    cross = jax.nn.logsumexp(seg_logits, axis=1) - jnp.sum(seg_logits * classes_hot, axis=1)
    depth_gap = logits[:, classes] - depth_target.reshape(pixels)
    smooth_abs = jnp.sqrt(depth_gap * depth_gap + 1.0)
    normal_gap = logits[:, classes + 1 :] - jnp.moveaxis(normal_target, 1, 3).reshape(pixels, 2)
    local_losses = jnp.stack(
        [
            jnp.sum(mask_flat * cross),
            jnp.sum(mask_flat * (smooth_abs - 1.0)),
            jnp.sum(mask_flat * jnp.sum(normal_gap * normal_gap, axis=1)),
        ]
    )
    task_weights = jnp.exp(-log_vars)
    grad_seg = (jax.nn.softmax(seg_logits, axis=1) - classes_hot) * (
        task_weights[0] / pixel_number_count * mask_flat
    )[:, None]
    grad_depth = depth_gap / smooth_abs * (task_weights[1] / pixel_number_count * mask_flat)
    grad_normal = 2.0 * normal_gap * (task_weights[2] / pixel_number_count * mask_flat)[:, None]
    grad_logits = jnp.concatenate([grad_seg, grad_depth[:, None], grad_normal], axis=1)
    head_local = lax.dot_general(
        features_wide, grad_logits, (((0,), (0,)), ((), ())), precision=HIGH
    )
    loss_parts, grad_head_weight, grad_head_bias = lax.psum(
        (local_losses, head_local, jnp.sum(grad_logits, axis=0)), ("rows", "batch")
    )
    task_losses = loss_parts / pixel_number_count
    total_loss = jnp.sum(task_weights * task_losses + log_vars)
    grad_log_vars = 1.0 - task_weights * task_losses
    grad_features = jnp.dot(grad_logits, head_wide.T, precision=HIGH)
    my_features_grad = lax.dynamic_slice_in_dim(
        grad_features, lax.axis_index("branch") * branch_part, branch_part, 1
    )
    gradient_before_projector = my_features_grad * silu_slope(normalized_projector)
    grad_proj_in, grad_project_norm = norm_reverse_pass(
        gradient_before_projector,
        standardized_projector,
        inverse_deviation_projector,
        1.0,
        mask_column_vector,
        pixel_number_count,
        projection_norm_params,
    )
    grad_proj_low = grad_proj_in.astype(jnp.bfloat16)
    proj_kernel_grad = lax.dot_general(
        grad_proj_low, concat_flat, (((0,), (0,)), ((), ())), preferred_element_type=jnp.float32
    )
    grad_project_local = (
        proj_kernel_grad.reshape(branch_part, branch_total, 5, branch_part)
        .transpose(0, 2, 1, 3)
        .reshape(branch_part, 5, branch_total * branch_part)
    )
    concat_grad = forward_dot(grad_proj_low, proj_kernel).reshape(
        image_inputs, tile_row_count, frame_columns, -1
    )
    concat_grad = narrow(concat_grad).reshape(pixels, 5, branch_part)
    pool_grad_img = over_rows(
        jnp.sum(concat_grad[:, 4, :].reshape(image_inputs, -1, branch_part), axis=1)
    )
    gradient_before_poolbranch = pool_grad_img * silu_slope(normalized_poolbranch)
    grad_pool_conv, grad_pool_norm = norm_reverse_pass(
        gradient_before_poolbranch,
        standardized_poolbranch,
        inverse_deviation_poolbranch,
        row_portion,
        1.0,
        image_overall_count,
        pooling_norm_params,
    )
    pool_conv_low = grad_pool_conv.astype(jnp.bfloat16)
    grad_pool_local = (
        lax.dot_general(
            pool_conv_low, pooled, (((0,), (0,)), ((), ())), preferred_element_type=jnp.float32
        )
        * row_portion
    )
    pooled_grad = forward_dot(pool_conv_low, aspp_pool)
    gradient_before_spatialbranch = concat_grad[:, :4, :].reshape(pixels, -1) * silu_slope(
        normalized_spatial
    )
    grad_spatial, branch_norm_grad = norm_reverse_pass(
        gradient_before_spatialbranch,
        standardized_spatial,
        inverse_deviation_spatial,
        1.0,
        mask_column_vector,
        pixel_number_count,
        branch_gain_bias,
    )
    grad_branch_norms = branch_norm_grad.reshape(2, 4, branch_part)
    spatial_low = grad_spatial.astype(jnp.bfloat16).reshape(
        image_inputs, tile_row_count, frame_columns, 4, branch_part
    )
    point_grad = spatial_low[:, :, :, 0]
    grad_point_local = pixel_dot(point_grad, trunk_full)
    trunk_grad = forward_dot(point_grad, aspp_point)
    trunk_grad = (
        trunk_grad + valid_mask[..., None] * (pooled_grad / image_areas[:, None])[:, None, None, :]
    )
    rate_grads = []
    for branch_id in range(3):
        dilation = RATES[branch_id]
        hops = dilation // tile_row_count
        centre = spatial_low[:, :, :, branch_id + 1]
        grad_taps = jnp.concatenate(
            [send_up(centre, hops), centre, send_down(centre, hops)], axis=3
        )
        per_col = []
        for col_tap in range(3):
            shifted = move(trunk_full, -(col_tap - 1) * dilation, 2)
            per_col.append(pixel_dot(grad_taps, shifted))
            tap_grad = forward_dot(grad_taps, stacked_taps(aspp_rates[branch_id], col_tap))
            trunk_grad = trunk_grad + move(tap_grad, (col_tap - 1) * dilation, 2)
        col_stack = jnp.stack(per_col, axis=0).reshape(3, 3, branch_part, -1)
        rate_grads.append(col_stack.transpose(1, 0, 2, 3))
    grad_rates_local = jnp.stack(rate_grads, axis=0)
    trunk_own = narrow(trunk_grad).reshape(pixels, -1)
    gradient_shortcut = trunk_own * silu_slope(residual_sum)
    grad_expanded, grad_norm_expand = norm_reverse_pass(
        gradient_shortcut,
        standardized_third,
        inverse_deviation_third,
        1.0,
        mask_column_vector,
        pixel_number_count,
        expansion_norm_params,
    )
    expanded_low = grad_expanded.astype(jnp.bfloat16).reshape(
        image_inputs, tile_row_count, frame_columns, -1
    )
    grad_expand_local = pixel_dot(hidden_two_full, expanded_low)
    hidden_two_grad = narrow(backward_dot(expanded_low, conv_expand)).reshape(pixels, -1)
    gradient_before_second = hidden_two_grad * silu_slope(normalized_second)
    gradient_dilated_input, gradient_dilated_norm = norm_reverse_pass(
        gradient_before_second,
        standardized_second,
        inverse_deviation_second,
        1.0,
        mask_column_vector,
        pixel_number_count,
        dilated_norm_params,
    )
    dilated_lowprec = gradient_dilated_input.astype(jnp.bfloat16).reshape(
        image_inputs, tile_row_count, frame_columns, -1
    )
    dilated_padded = pad_rows(dilated_lowprec)
    hidden_one_grad = 0.0
    kernel_grads = []
    for row_tap in range(3):
        band = hidden_full[:, 4 * row_tap : 4 * row_tap + tile_row_count]
        grad_band = dilated_padded[:, 8 - 4 * row_tap : 8 - 4 * row_tap + tile_row_count]
        for col_tap in range(3):
            kernel_grads.append(pixel_dot(move(band, -(col_tap - 1) * 4, 2), dilated_lowprec))
            hidden_one_grad = hidden_one_grad + backward_dot(
                move(grad_band, (col_tap - 1) * 4, 2), conv_dilated[row_tap, col_tap]
            )
    grad_dilated_local = jnp.stack(kernel_grads, axis=0).reshape(3, 3, hidden_full.shape[3], -1)
    hidden_one_own = narrow(hidden_one_grad).reshape(pixels, -1)
    gradient_before_first = hidden_one_own * silu_slope(normalized_first)
    grad_reduced, grad_norm_reduce = norm_reverse_pass(
        gradient_before_first,
        standardized_first,
        inverse_deviation_first,
        1.0,
        mask_column_vector,
        pixel_number_count,
        reduction_norm_params,
    )
    reduced_low = grad_reduced.astype(jnp.bfloat16).reshape(
        image_inputs, tile_row_count, frame_columns, -1
    )
    grad_reduce_local = pixel_dot(input_full, reduced_low)
    input_grad = narrow(backward_dot(reduced_low, conv_reduce))
    grad_input = input_grad + gradient_shortcut.reshape(
        image_inputs, tile_row_count, frame_columns, quarter
    )
    grad_reduce, grad_dilated, grad_expand, grad_point, grad_rates, grad_pool, grad_project = (
        lax.psum_scatter(grad_reduce_local, ("rows", "batch"), scatter_dimension=0, tiled=True),
        lax.psum_scatter(grad_dilated_local, ("rows", "batch"), scatter_dimension=2, tiled=True),
        lax.psum_scatter(grad_expand_local, ("rows", "batch"), scatter_dimension=0, tiled=True),
        lax.psum_scatter(grad_point_local, ("rows", "batch"), scatter_dimension=1, tiled=True),
        lax.psum_scatter(grad_rates_local, ("rows", "batch"), scatter_dimension=4, tiled=True),
        lax.psum_scatter(grad_pool_local, ("rows", "batch"), scatter_dimension=1, tiled=True),
        lax.psum_scatter(grad_project_local, ("rows", "batch"), scatter_dimension=2, tiled=True),
    )
    return (
        features,
        total_loss,
        grad_input,
        grad_reduce,
        grad_dilated,
        grad_expand,
        grad_norm_reduce,
        gradient_dilated_norm,
        grad_norm_expand,
        grad_point,
        grad_rates,
        grad_pool,
        grad_branch_norms,
        grad_pool_norm,
        grad_project,
        grad_project_norm,
        grad_head_weight,
        grad_head_bias,
        grad_log_vars,
    )


def solution(mesh):
    in_specs = (
        P("batch", "rows", None, "branch"),
        P(None, "branch"),
        P(None, None, None, "branch"),
        P(None, "branch"),
        P(None, "branch"),
        P(None, "branch"),
        P(None, "branch"),
        P("branch", None),
        P(None, None, None, "branch", None),
        P("branch", None),
        P(None, None, "branch"),
        P(None, "branch"),
        P("branch", None, None),
        P(None, "branch"),
        P(),
        P(),
        P(),
        P(),
        P("batch", "rows", None),
        P("batch", "rows", None),
        P("batch", None, "rows", None),
    )
    out_specs = (
        P("batch", "rows", None, "branch"),
        P(),
        P("batch", "rows", None, "branch"),
        P(("rows", "batch"), "branch"),
        P(None, None, ("rows", "batch"), "branch"),
        P(("rows", "batch"), "branch"),
        P(None, "branch"),
        P(None, "branch"),
        P(None, "branch"),
        P("branch", ("rows", "batch")),
        P(None, None, None, "branch", ("rows", "batch")),
        P("branch", ("rows", "batch")),
        P(None, None, "branch"),
        P(None, "branch"),
        P("branch", None, ("rows", "batch")),
        P(None, "branch"),
        P(),
        P(),
        P(),
    )
    small = (mesh.shape["branch"], mesh.shape["rows"], mesh.shape["batch"]) == (4, 2, 4)
    body = fast_local if small else local
    return jax.shard_map(body, mesh=mesh, in_specs=in_specs, out_specs=out_specs, check_vma=False)
```

```python
import types

import jax
import jax.numpy as jnp
from jax import lax
from jax.experimental import pallas as pl
from jax.experimental.pallas import tpu as pltpu
from jax.sharding import PartitionSpec as P

EPS = 1e-05
HIGH = lax.Precision.HIGHEST
RATES = (12, 24, 36)


def padded(cells, sides, width):
    for axis, dim in sides:
        count = lax.axis_size(axis)
        ends = count - 1
        head = lax.slice_in_dim(cells, 0, width, axis=dim)
        tail = lax.slice_in_dim(cells, cells.shape[dim] - width, cells.shape[dim], axis=dim)
        cells = jnp.concatenate(
            [
                lax.ppermute(tail, axis, [(i, (i + 1) % count) for i in range(ends)]),
                cells,
                lax.ppermute(head, axis, [((i + 1) % count, i) for i in range(ends)]),
            ],
            axis=dim,
        )
    return cells


def shifted_2(block, axis, distance):
    devices = range(lax.axis_size(axis))
    route = [(i - distance, i) for i in devices if i - distance in devices]
    return lax.ppermute(block, axis, route)


def move(tensor, offset, axis_id):
    length = tensor.shape[axis_id]
    if offset == 0:
        return tensor
    widths = [(0, 0)] * tensor.ndim
    if offset > 0:
        widths[axis_id] = (offset, 0)
        return lax.slice_in_dim(jnp.pad(tensor, widths), 0, length, axis=axis_id)
    widths[axis_id] = (0, -offset)
    return lax.slice_in_dim(jnp.pad(tensor, widths), -offset, length - offset, axis=axis_id)


def forward_dot(lhs_arr, rhs_arr):
    return jnp.dot(lhs_arr, rhs_arr, preferred_element_type=jnp.float32)


def backward_dot(grad_arr, kernel):
    return lax.dot_general(
        grad_arr,
        kernel,
        (((grad_arr.ndim - 1,), (1,)), ((), ())),
        preferred_element_type=jnp.float32,
    )


def pixel_dot(source, grad_arr):
    return lax.dot_general(
        source, grad_arr, (((0, 1, 2), (0, 1, 2)), ((), ())), preferred_element_type=jnp.float32
    )


def silu_slope(pre_act):
    sigmoid_v = jax.nn.sigmoid(pre_act)
    return sigmoid_v * (1.0 + pre_act * (1.0 - sigmoid_v))


def widen(tensor):
    return lax.all_gather(tensor, "branch", axis=3, tiled=True)


def narrow(tensor):
    return lax.psum_scatter(
        tensor.astype(jnp.bfloat16), "branch", scatter_dimension=3, tiled=True
    ).astype(jnp.float32)


def pad_rows(tensor):
    return padded(tensor, (("rows", 1),), 4)


def send_down(tensor, hops):
    if hops >= lax.axis_size("rows"):
        return jnp.zeros_like(tensor)
    return shifted_2(tensor, "rows", hops)


def send_up(tensor, hops):
    if hops >= lax.axis_size("rows"):
        return jnp.zeros_like(tensor)
    return shifted_2(tensor, "rows", -hops)


def over_rows(tensor):
    return lax.psum(tensor, "rows")


def norm_ahead_pass(tensor, weight, counted, affine):
    summed = lax.psum(jnp.sum(tensor * weight, axis=0), ("rows", "batch"))
    mean_val = summed / counted
    centered = tensor - mean_val
    spread = lax.psum(jnp.sum(weight * centered * centered, axis=0), ("rows", "batch"))
    variance = spread / counted
    inverse = lax.rsqrt(variance + EPS)
    normed = centered * inverse
    return (affine[0] * normed + affine[1], normed, inverse)


def norm_reverse_pass(grad_out, normed, inverse, weight_all, weight_stat, counted, affine):
    grad_bias, grad_gain = lax.psum(
        (jnp.sum(grad_out * weight_all, axis=0), jnp.sum(grad_out * normed * weight_all, axis=0)),
        ("rows", "batch"),
    )
    gain_row = affine[0]
    grad_in = inverse * (
        gain_row * grad_out - weight_stat / counted * gain_row * (grad_bias + normed * grad_gain)
    )
    return (grad_in, jnp.stack([grad_gain, grad_bias]))


def stacked_taps(kernels, col_tap):
    return jnp.concatenate([kernels[0, col_tap], kernels[1, col_tap], kernels[2, col_tap]], axis=0)


MESH = pl.DeviceIdType.MESH
F32 = jnp.float32
BF16 = jnp.bfloat16
VMEM_LIMIT = 60 * 2**20


class Net:
    def __init__(self, send_sems, recv_sems):
        self.m = lax.axis_index("branch")
        self.r = lax.axis_index("rows")
        self.z = lax.axis_index("batch")
        self.send_sems, self.recv_sems, self.count = send_sems, recv_sems, 0
        self.side = (self.m ^ 1, self.r, self.z)
        self.over = (self.m ^ 2, self.r, self.z)
        self.diagonal = (self.m ^ 3, self.r, self.z)
        self.core = (self.m, 1 - self.r, self.z)
        self.slot = self.r * 4 + self.z
        self.group = [
            (self.m, lax.rem(self.r + i, 2), lax.rem(self.z + j, 4))
            for i in range(2)
            for j in range(4)
            if i or j
        ]

    def send(self, src, dst, device):
        i = self.count
        self.count += 1
        copy = pltpu.make_async_remote_copy(
            src_ref=src,
            dst_ref=dst,
            send_sem=self.send_sems.at[i],
            recv_sem=self.recv_sems.at[i],
            device_id=device,
            device_id_type=MESH,
        )
        copy.start()
        return copy


def greet(peers, perhaps=()):
    barrier = pltpu.get_barrier_semaphore()
    for peer in peers:
        pl.semaphore_signal(barrier, inc=1, device_id=peer, device_id_type=MESH)
    awaited = len(peers)
    for peer, there in perhaps:

        @pl.when(there)
        def _(peer=peer):
            pl.semaphore_signal(barrier, inc=1, device_id=peer, device_id_type=MESH)

        awaited = awaited + there.astype(jnp.int32)
    pl.semaphore_wait(barrier, awaited)


def each_rows(total, step, body):
    def run(i, carry):
        body(pl.ds(pl.multiple_of(i * step, step), step))
        return carry

    lax.fori_loop(0, total // step, run, 0, unroll=2)


def lane_block(index, width=128):
    return pl.ds(pl.multiple_of(index * width, width), width)


def wide(tile, width):
    count = width // tile.shape[1]
    return tile if count == 1 else jnp.concatenate([tile] * count, axis=1)


def column_sums(fn, total, width, number):
    step = 32768 // width

    def run(i, sums):
        terms = fn(pl.ds(pl.multiple_of(i * step, step), step))
        return tuple(
            s + jnp.sum(t.reshape(step // 8, 8, width), axis=0) for s, t in zip(sums, terms)
        )

    sums = lax.fori_loop(
        0, total // step, run, tuple(jnp.zeros((8, width), F32) for _ in range(number))
    )
    return [jnp.sum(s, axis=0, keepdims=True) for s in sums]


def fold(row):
    return row + pltpu.roll(wide(row, 128), 64, 1)


def exchange(net, outgoing, incoming, meanwhile=None):
    copies = [net.send(outgoing, incoming.at[net.slot], peer) for peer in net.group]
    incoming[net.slot] = outgoing[...]
    if meanwhile is not None:
        meanwhile()
    for copy in copies:
        copy.wait()


def pack(outgoing, first, second, extra=None):
    for i in range(first.shape[1] // 128):
        outgoing[2 * i : 2 * i + 1, :] = first[:, i * 128 : i * 128 + 128]
        outgoing[2 * i + 1 : 2 * i + 2, :] = second[:, i * 128 : i * 128 + 128]
    if extra is not None:
        outgoing[4:5, :] = extra


def unpack(incoming, width):
    count = width // 128
    firsts = [incoming[:, 2 * i, :] for i in range(count)]
    seconds = [incoming[:, 2 * i + 1, :] for i in range(count)]
    return jnp.concatenate(firsts, axis=1), jnp.concatenate(seconds, axis=1)


def statistics(
    net,
    value_ref,
    mask_ref,
    counts,
    outgoing,
    incoming,
    counted,
    folded=False,
    extra=None,
    meanwhile=None,
):
    total, width = value_ref.shape
    same = fold if folded else (lambda row: row)
    (first,) = column_sums(
        lambda at: (value_ref[at, :] * wide(mask_ref[at, :], width),), total, width, 1
    )
    first = same(first)
    own = jnp.sum(jnp.where(lax.broadcasted_iota(jnp.int32, (8, 128), 0) == net.slot, counts, 0.0), axis=0, keepdims=True)
    centre = first / jnp.maximum(wide(own, width), 1.0)

    def squares(at):
        gap = value_ref[at, :] - centre
        return (gap * gap * wide(mask_ref[at, :], width),)

    second = same(column_sums(squares, total, width, 1)[0])
    pack(outgoing, first, second, extra)
    exchange(net, outgoing, incoming, meanwhile)
    firsts, seconds = unpack(incoming, width)
    numbers = wide(counts, width)
    mean = jnp.sum(firsts, axis=0, keepdims=True) / counted
    drift = firsts / jnp.maximum(numbers, 1.0) - mean
    variance = jnp.sum(seconds + numbers * drift * drift, axis=0, keepdims=True) / counted
    return mean, lax.rsqrt(variance + EPS)


def gather_blocks(net, part, rows, meanwhile=None):
    pieces, size = 4, rows // 4
    own, side, over = net.m, net.m ^ 1, net.m ^ 2

    def at(i):
        return pl.ds(i * size, size)

    to_side, to_over = [], []
    for i in range(pieces):
        j = pieces - 1 - i
        to_side.append(net.send(part(own, at(i)), part(own, at(i)), net.side))
        to_over.append(net.send(part(own, at(j)), part(own, at(j)), net.over))
    passed = []
    for i in range(pieces):
        j = pieces - 1 - i
        to_side[i].wait_recv()
        if i < pieces // 2:
            passed.append(net.send(part(side, at(i)), part(side, at(i)), net.over))
        to_over[i].wait_recv()
        if i < pieces // 2:
            passed.append(net.send(part(over, at(j)), part(over, at(j)), net.side))
    if meanwhile is not None:
        meanwhile()
    for copy in to_side + to_over:
        copy.wait_send()
    for copy in passed:
        copy.wait()


def sum_scatter(net, part, bufs, out, meanwhile=None, produce=None):
    far, to_side, to_over, far_side, far_over, from_side, from_over = bufs
    rows, width = out.shape
    half, step = rows // 2, 16384 // width
    head, tail = pl.ds(0, half), pl.ds(half, half)
    across, side, over = net.m ^ 3, net.m ^ 1, net.m ^ 2

    def fill(target, index, base, count=half):
        size = min(step, count) if count % step == 0 else 64

        def body(at):
            rows_at = pl.ds(pl.multiple_of(at.start + base, size), size)
            target[rows_at, :] = part[index, rows_at, :].astype(BF16)

        each_rows(count, size, body)

    def combine(target, index, base, arrived):
        def body(at):
            rows_at = pl.ds(pl.multiple_of(at.start + base, step), step)
            target[rows_at, :] = (part[index, rows_at, :] + arrived[at, :].astype(F32)).astype(BF16)

        each_rows(half, step, body)

    quarter, first, second = half // 2, [], []
    for i in range(2):
        if produce is not None:
            produce(i)
        at = pl.ds(i * quarter, quarter)
        fill(far, across, i * quarter, quarter)
        first.append(net.send(far.at[at], far_side.at[at], net.side))
        fill(far, across, half + i * quarter, quarter)
        below = pl.ds(half + i * quarter, quarter)
        second.append(net.send(far.at[below], far_over.at[at], net.over))
    fill(to_side, side, 0)
    third = net.send(to_side.at[head], from_side.at[head], net.side)
    fill(to_over, over, half)
    fourth = net.send(to_over.at[tail], from_over.at[tail], net.over)
    for copy in second:
        copy.wait_recv()
    combine(to_side, side, half, far_over)
    fifth = net.send(to_side.at[tail], from_side.at[tail], net.side)
    for copy in first:
        copy.wait_recv()
    combine(to_over, over, 0, far_side)
    sixth = net.send(to_over.at[head], from_over.at[head], net.over)
    if meanwhile is not None:
        meanwhile()
    for copy in (third, fourth, fifth, sixth):
        copy.wait_recv()

    def body(at):
        out[at, :] = (
            part[net.m, at, :] + from_side[at, :].astype(F32) + from_over[at, :].astype(F32)
        )

    each_rows(rows, step, body)
    for copy in (*first, *second, third, fourth, fifth, sixth):
        copy.wait_send()


def gradient_sums(
    net, grad_ref, normed, outgoing, incoming, folded=False, extra=None, meanwhile=None
):
    total, width = grad_ref.shape
    same = fold if folded else (lambda row: row)
    bias, gain = column_sums(
        lambda at: (grad_ref[at, :], grad_ref[at, :] * normed(at)), total, width, 2
    )
    pack(outgoing, same(bias), same(gain), extra)
    exchange(net, outgoing, incoming, meanwhile)
    biases, gains = unpack(incoming, width)
    return jnp.sum(biases, axis=0, keepdims=True), jnp.sum(gains, axis=0, keepdims=True)


def keep_rows(ref, first, second):
    width = ref.shape[1]
    ref[0:1, :] = first
    ref[1:2, :] = second
    ref[2:8, :] = jnp.zeros((6, width), F32)


def pair(a, b):
    low = lax.broadcasted_iota(jnp.int32, (a.shape[0], 128), 1) < 64
    results = []
    for g in range(2):
        left, right = a[:, g * 128 : g * 128 + 128], b[:, g * 128 : g * 128 + 128]
        results.append(jnp.where(low, left, pltpu.roll(right, 64, 1)))
        results.append(jnp.where(low, pltpu.roll(left, 64, 1), right))
    return results


def unpair(blocks):
    low = lax.broadcasted_iota(jnp.int32, blocks[0].shape, 1) < 64
    firsts, seconds = [], []
    for g in range(2):
        left, right = blocks[2 * g], blocks[2 * g + 1]
        firsts.append(jnp.where(low, left, pltpu.roll(right, 64, 1)))
        seconds.append(jnp.where(low, pltpu.roll(left, 64, 1), right))
    return jnp.concatenate(firsts, axis=1), jnp.concatenate(seconds, axis=1)


def split_three(row):
    high = row.astype(BF16)
    rest = row - high.astype(F32)
    middle = rest.astype(BF16)
    low = (rest - middle.astype(F32)).astype(BF16)
    return high, middle, low


def zero_margins(ref, side, width):
    rows, _, lanes = ref.shape
    ref[:, 0:side, :] = jnp.zeros((rows, side, lanes), F32)
    ref[:, side + width : 2 * side + width, :] = jnp.zeros((rows, side, lanes), F32)


def scatter_buffers(rows, width):
    whole, half = pltpu.VMEM((rows, width), BF16), pltpu.VMEM((rows // 2, width), BF16)
    return [whole, whole, whole, half, half, whole, whole]


def sigmoid(u):
    return 0.5 * jnp.tanh(0.5 * u) + 0.5


def slope(u):
    s = sigmoid(u)
    return s * (1.0 + u * (1.0 - s))


def mm(a, b):
    return jnp.dot(a, b, preferred_element_type=F32)


def mm_t(a, b):
    return lax.dot_general(a, b, (((1,), (1,)), ((), ())), preferred_element_type=F32)


def tm_m(a, b):
    return lax.dot_general(a, b, (((0,), (0,)), ((), ())), preferred_element_type=F32)


class Streams:
    def __init__(self, ins, outs, sems):
        self.ins = {n: pltpu.make_async_copy(*pair, sems.at[i]) for i, (n, pair) in enumerate(ins)}
        self.outs = {
            n: pltpu.make_async_copy(*pair, sems.at[len(ins) + i])
            for i, (n, pair) in enumerate(outs)
        }
        self.left = []
        for copy in self.ins.values():
            copy.start()

    def need(self, **names):
        for name in names:
            self.ins.pop(name).wait()

    def done(self, **names):
        for name in names:
            copy = self.outs.pop(name)
            copy.start()
            self.left.append(copy)

    def finish(self):
        self.need(**dict.fromkeys(self.ins))
        self.done(**dict.fromkeys(self.outs))
        for copy in self.left:
            copy.wait()


def call_kernel(
    body, name, number, args, outs, scratch, sems, hbm={}, smem=dict(boxes=1), stream={}
):
    vmem, anywhere = pl.BlockSpec(memory_space=pltpu.VMEM), pl.BlockSpec(memory_space=pl.ANY)
    stream_in = [n for n in args if n in stream]
    stream_out = [n for n in outs if n in stream]
    buffers = {n: pltpu.VMEM(args[n].shape, args[n].dtype) for n in stream_in}
    buffers.update({n: pltpu.VMEM(*outs[n]) for n in stream_out})
    names = [f"far_{n}" if n in stream else n for n in [*args, *outs]]
    names = [*names, *scratch, *buffers, "stream_sems"]
    places = {name: anywhere for name in [*hbm, *stream]}
    places.update({name: pl.BlockSpec(memory_space=pltpu.SMEM) for name in smem})

    def kernel(*refs):
        k = types.SimpleNamespace(**dict(zip(names, refs)))
        held = vars(k)
        k.stream = Streams(
            [(n, (held[f"far_{n}"], held[n])) for n in stream_in],
            [(n, (held[n], held[f"far_{n}"])) for n in stream_out],
            k.stream_sems,
        )
        body(Net(refs[-2], refs[-1]) if sems else None, k)
        k.stream.finish()

    results = pl.pallas_call(
        kernel,
        out_shape=[jax.ShapeDtypeStruct(s, d) for s, d in outs.values()],
        in_specs=[places.get(name, vmem) for name in args],
        out_specs=[places.get(name, vmem) for name in outs],
        scratch_shapes=[
            *scratch.values(),
            *buffers.values(),
            pltpu.SemaphoreType.DMA((max(len(buffers), 1),)),
            *([pltpu.SemaphoreType.DMA((sems,))] * (2 if sems else 0)),
        ],
        name=name,
        compiler_params=pltpu.CompilerParams(
            collective_id=number, has_side_effects=bool(sems), vmem_limit_bytes=VMEM_LIMIT
        ),
    )(*args.values())
    return types.SimpleNamespace(**dict(zip(outs, results)))


def pixel_count(boxes):
    total = boxes[0, 2] * boxes[0, 3]
    for b in range(1, 4):
        total = total + boxes[b, 2] * boxes[b, 3]
    return total.astype(F32)


def tile_counts(net, boxes):
    slot = lax.broadcasted_iota(jnp.int32, (8, 128), 0)
    result = jnp.zeros((8, 128), F32)
    for s in range(8):
        top, height, width = boxes[s % 4, 0], boxes[s % 4, 2], boxes[s % 4, 3]
        first, last = (s // 4) * 12, (s // 4) * 12 + 12
        rows = jnp.minimum(top + height, last) - jnp.maximum(top, first)
        result = jnp.where(slot == s, (jnp.maximum(rows, 0) * width).astype(F32), result)
    return result


def exchange_scratch(label):
    return {
        f"out_{label}": pltpu.VMEM((8, 128), F32),
        f"in_{label}": pltpu.VMEM((8, 8, 128), F32),
    }


def scatter_scratch(label, rows, width):
    return {f"{label}_{i}": b for i, b in enumerate(scatter_buffers(rows, width))}


def scatter_refs(k, label):
    return [getattr(k, f"{label}_{i}") for i in range(7)]


def load_taps(k):
    loads = []
    for i in range(3):
        for j in range(3):
            loads.append(
                pltpu.make_async_copy(
                    k.w_dilated.at[i, j],
                    k.w_taps.at[i, :, pl.ds(j * 128, 128)],
                    k.local_sems.at[i * 3 + j],
                )
            )
            loads[-1].start()
    return loads


def send_halo(net, padded):
    lanes = padded.shape[1]
    padded[pl.ds(pl.multiple_of(net.r * 2048, 128), 512), :] = jnp.zeros((512, lanes), BF16)
    return net.send(
        padded.at[pl.ds(pl.multiple_of(1536 - net.r * 1024, 128), 512)],
        padded.at[pl.ds(pl.multiple_of(net.r * 2048, 128), 512)],
        net.core,
    )


def bottleneck_forward(net, k):
    counted, counts = pixel_count(k.boxes), tile_counts(net, k.boxes)
    loads = load_taps(k)
    own_reduce = pltpu.make_async_copy(
        k.conv_reduce.at[lane_block(net.m, 512)], k.w_reduce.at[net.m], k.local_sems.at[9]
    )
    own_reduce.start()
    greet([net.side, net.over, net.diagonal] + net.group)
    branches = [(net.m ^ 3, net.diagonal), (net.m ^ 1, net.side), (net.m ^ 2, net.over)]
    arrivals = [
        net.send(k.conv_reduce.at[lane_block(b, 512)], k.w_reduce.at[net.m], peer)
        for b, peer in branches
    ]

    top, left_edge = k.boxes[net.z, 0], k.boxes[net.z, 1]
    bottom, right_edge = top + k.boxes[net.z, 2], left_edge + k.boxes[net.z, 3]
    column = lax.broadcasted_iota(jnp.int32, (128, 128), 0)
    column_inside = jnp.where((column >= left_edge) & (column < right_edge), 1.0, 0.0)

    def mask_rows(i, carry):
        row = jnp.full((128, 128), net.r * 12 + i, jnp.int32)
        inside = jnp.where((row >= top) & (row < bottom), column_inside, 0.0)
        k.mask[pl.ds(pl.multiple_of(i * 128, 128), 128), :] = inside
        return carry

    lax.fori_loop(0, 12, mask_rows, 0, unroll=2)
    k.stream.done(mask=1)
    k.stream.need(x=1)

    def reduce_for(b):
        def reduce_rows(at):
            k.part[b, at, :] = mm(k.x[at, :], k.w_reduce[b])

        each_rows(1536, 384, reduce_rows)

    own_reduce.wait()
    reduce_for(net.m)
    arrivals[1].wait()
    reduce_for(net.m ^ 1)
    arrivals[2].wait()
    reduce_for(net.m ^ 2)
    arrivals[0].wait()
    k.stream.done(w_reduce=1)

    def far_half(half):
        for i in (half, half + 2):
            at = pl.ds(i * 384, 384)
            k.part[net.m ^ 3, at, :] = mm(k.x[at, :], k.w_reduce[net.m ^ 3])

    sum_scatter(net, k.part, scatter_refs(k, "sum"), k.reduced, produce=far_half)
    k.stream.done(reduced=1)

    half = pl.ds(pl.multiple_of(net.r * 32, 32), 32)
    late = []

    def weight_block(kind, b):
        lanes = lane_block(b, 512)
        if kind == "edge":
            return k.aspp_rates.at[0, 2 * net.r, :, :, lanes], k.w_pyramid.at[pl.ds(10, 3), net.m]
        if kind == "point":
            return k.aspp_point.at[half, lanes], k.w_pyramid.at[0, net.m, half]
        if kind == "project":
            return k.project.at[:, half], k.w_project.at[net.m, :, half]
        return (
            k.aspp_rates.at[kind, 1, :, half, lanes],
            k.w_pyramid.at[pl.ds(1 + 3 * kind, 3), net.m, half],
        )

    def spread_weights(*kinds):
        for kind in kinds:
            src, dst = weight_block(kind, net.m)
            late.append(pltpu.make_async_copy(src, dst, k.local_sems.at[10 + len(late) // 4]))
            late[-1].start()
            for b, peer in branches:
                src, dst = weight_block(kind, b)
                late.append(net.send(src, dst, peer))

    spread_weights("edge")
    mean, inverse = statistics(net, k.reduced, k.mask, counts, k.out_1, k.in_1, counted)
    keep_rows(k.stats_1, mean, inverse)

    def activate_1(at):
        u = k.affine_1[0:1, :] * ((k.reduced[at, :] - mean) * inverse) + k.affine_1[1:2, :]
        rows_at = pl.ds(pl.multiple_of(at.start + 512, 128), 128)
        k.hidden[rows_at, lane_block(net.m)] = (u * sigmoid(u)).astype(BF16)

    each_rows(1536, 128, activate_1)
    gather_blocks(
        net, lambda b, at: k.hidden.at[pl.ds(at.start + 512, at.size), lane_block(b)], 1536
    )
    halo = send_halo(net, k.hidden)
    spread_weights("project", "point", 0)
    zero_margins(k.left, 8, 128)
    zero_margins(k.right, 8, 128)
    for load in loads:
        load.wait()
    halo.wait()
    k.stream.done(hidden=1)

    def dilated_rows(i, carry):
        total = 0.0
        for tap in range(3):
            rows_at = pl.ds(pl.multiple_of((i * 3 + 4 * tap) * 128, 128), 384)
            total = total + mm(k.hidden[rows_at, :], k.w_taps[tap])
        k.dilated[pl.ds(pl.multiple_of(i * 384, 128), 384), :] = total[:, 128:256]
        k.left[pl.ds(i * 3, 3), 8:136, :] = total[:, 0:128].reshape(3, 128, 128)
        k.right[pl.ds(i * 3, 3), 8:136, :] = total[:, 256:384].reshape(3, 128, 128)
        return carry

    lax.fori_loop(0, 4, dilated_rows, 0)

    def add_columns(i, carry):
        at = pl.ds(pl.multiple_of(i * 128, 128), 128)
        k.dilated[at, :] = k.dilated[at, :] + k.left[i, 4:132, :] + k.right[i, 12:140, :]
        return carry

    lax.fori_loop(0, 12, add_columns, 0, unroll=2)
    k.stream.done(dilated=1)
    mean_2, inverse_2 = statistics(net, k.dilated, k.mask, counts, k.out_2, k.in_2, counted)
    keep_rows(k.stats_2, mean_2, inverse_2)

    def activate_2(at):
        u = k.affine_2[0:1, :] * ((k.dilated[at, :] - mean_2) * inverse_2) + k.affine_2[1:2, :]
        k.hidden_two[at, lane_block(net.m)] = (u * sigmoid(u)).astype(BF16)

    each_rows(1536, 128, activate_2)
    gather_blocks(net, lambda b, at: k.hidden_two.at[at, lane_block(b)], 1536)
    spread_weights(1, 2)
    k.stream.done(hidden_two=1)
    k.stream.need(w_expand=1)

    def expand_rows(at):
        k.expanded[at, :] = mm(k.hidden_two[at, :], k.w_expand[...])

    each_rows(1536, 384, expand_rows)
    k.stream.done(expanded=1)
    mean_3, inverse_3 = statistics(net, k.expanded, k.mask, counts, k.out_3, k.in_3, counted)
    keep_rows(k.stats_3, mean_3, inverse_3)
    def activate_3(at):
        u = k.affine_3[0:1, :] * ((k.expanded[at, :] - mean_3) * inverse_3) + k.affine_3[1:2, :]
        u = u + k.x[at, :].astype(F32)
        k.trunk[at, :] = (u * sigmoid(u)).astype(BF16)

    each_rows(1536, 64, activate_3)
    for copy in late:
        copy.wait()


def run_bottleneck(args):
    return call_kernel(
        bottleneck_forward,
        "bottleneck",
        0,
        args,
        dict(
            mask=((1536, 128), F32),
            w_reduce=((4, 512, 128), BF16),
            w_pyramid=((13, 4, 64, 512), BF16),
            w_project=((4, 5, 64, 256), BF16),
            reduced=((1536, 128), F32),
            stats_1=((8, 128), F32),
            hidden=((2560, 512), BF16),
            dilated=((1536, 128), F32),
            stats_2=((8, 128), F32),
            hidden_two=((1536, 512), BF16),
            expanded=((1536, 512), F32),
            stats_3=((8, 512), F32),
            trunk=((1536, 512), BF16),
        ),
        dict(
            w_taps=pltpu.VMEM((3, 512, 384), BF16),
            part=pltpu.VMEM((4, 1536, 128), F32),
            **scatter_scratch("sum", 1536, 128),
            left=pltpu.VMEM((12, 144, 128), F32),
            right=pltpu.VMEM((12, 144, 128), F32),
            **exchange_scratch(1),
            **exchange_scratch(2),
            **exchange_scratch(3),
            local_sems=pltpu.SemaphoreType.DMA((16,)),
        ),
        96,
        hbm=dict(conv_reduce=1, w_dilated=1, aspp_point=1, aspp_rates=1, project=1, w_pyramid=1, w_project=1),
        stream=dict(x=1, w_expand=1, mask=1, w_reduce=1, reduced=1, hidden=1, dilated=1, hidden_two=1, expanded=1),
    )


def pyramid_forward(net, k):
    counted, counts = pixel_count(k.boxes), tile_counts(net, k.boxes)
    area = (k.boxes[net.z, 2] * k.boxes[net.z, 3]).astype(F32)
    near = [
        (lax.rem(net.m + a, 4), lax.rem(net.r + b, 2), net.z)
        for a in range(4)
        for b in range(2)
        if a or b
    ]
    own_rows = pl.ds(pl.multiple_of(net.r * 32, 32), 32)
    common = (pl.ds(0, 10), slice(None), own_rows)
    every = (slice(None), slice(None), own_rows)
    weight_copies = [
        pltpu.make_async_copy(source.at[view], target.at[view], k.local_sems.at[i])
        for i, (source, target, view) in enumerate(
            (
                (k.far_pyramid, k.w_pyramid, common),
                (k.far_pyramid, k.w_pyramid, pl.ds(10, 3)),
                (k.far_slots, k.w_slots, every),
            )
        )
    ]
    for copy in weight_copies:
        copy.start()
    greet(net.group + [peer for i, peer in enumerate(near) if i])
    weight_copies.append(net.send(k.far_pyramid.at[common], k.w_pyramid.at[common], net.core))
    weight_copies.append(net.send(k.far_slots.at[every], k.w_slots.at[every], net.core))

    for b in range(4):
        k.affine_b[0:2, b * 64 : b * 64 + 64] = k.branch_norms[:, b, :]
    for i in range(2):
        k.affine_p[0:2, i * 64 : i * 64 + 64] = k.norm_project[...]
        k.affine_p[2:4, i * 64 : i * 64 + 64] = k.norm_pooling[...]
    k.head_rows[...] = jnp.zeros((32, 256), F32)
    k.head_rows[0:22, :] = k.head_weight[...].astype(F32)

    k.stream.need(mask=1)

    (own_sum,) = column_sums(
        lambda at: (k.trunk[at, :].astype(F32) * wide(k.mask[at, :], 512),), 1536, 512, 1
    )
    k.out_pool[...] = jnp.broadcast_to(own_sum, (8, 512))
    place = net.m * 2 + net.r
    pool_copies = [net.send(k.out_pool, k.in_pool.at[place], peer) for peer in near]
    k.in_pool[place] = k.out_pool[...]

    zero_margins(k.cells, 40, 128)

    def fill(i, carry):
        at = pl.ds(pl.multiple_of(i * 128, 128), 128)
        k.cells[i, 40:168, :] = k.trunk[at, :].astype(F32)
        return carry

    lax.fori_loop(0, 12, fill, 0, unroll=2)

    def shifted(i, offset):
        cells = k.cells[pl.ds(i * 3, 3), 40 + offset : 168 + offset, :]
        return cells.reshape(384, 512).astype(BF16)

    def rows_of(i):
        return pl.ds(pl.multiple_of(i * 384, 128), 384)

    def edge_rows(i, carry):
        total = 0.0
        for j in range(3):
            total = total + mm_t(shifted(i, 12 * (j - 1)), k.w_pyramid[10 + j].reshape(256, 512))
        k.edge_out[rows_of(i), :] = total.astype(BF16)
        return carry

    weight_copies.pop(1).wait()
    lax.fori_loop(0, 4, edge_rows, 0)
    edge = net.send(k.edge_out, k.edge_in, net.core)

    def outer_rows(i, carry):
        second, third = 0.0, 0.0
        for j in range(3):
            second = second + mm_t(shifted(i, 24 * (j - 1)), k.w_pyramid[4 + j].reshape(256, 512))
        for j in range(3):
            third = third + mm_t(shifted(i, 36 * (j - 1)), k.w_pyramid[7 + j].reshape(256, 512))
        for b, block in enumerate(pair(second, third)):
            k.part[b, rows_of(i), 128:256] = block
        return carry

    def inner_rows(i, carry):
        point = mm_t(k.trunk[rows_of(i), :], k.w_pyramid[0].reshape(256, 512))
        first = k.edge_in[rows_of(i), :].astype(F32)
        for j in range(3):
            first = first + mm_t(shifted(i, 12 * (j - 1)), k.w_pyramid[1 + j].reshape(256, 512))
        for b, block in enumerate(pair(point, first)):
            k.part[b, rows_of(i), 0:128] = block
        return carry

    def alternate(body, half):
        def run(i, carry):
            return body(half + 2 * i, carry)

        lax.fori_loop(0, 2, run, 0)

    def half_tile(half):
        alternate(outer_rows, half)
        if half == 0:
            edge.wait()
        alternate(inner_rows, half)

    for copy in weight_copies:
        copy.wait()
    k.stream.done(w_pyramid=1)

    sum_scatter(net, k.part, scatter_refs(k, "sum"), k.branches, produce=half_tile)

    low_256 = lax.broadcasted_iota(jnp.int32, (256, 128), 1) < 64
    odd = lax.rem(net.m, 2) == 1

    def slot(s):
        lanes = lane_block(net.m // 2)
        block = jnp.concatenate([k.w_slots[b, s, :, lanes] for b in range(4)], axis=0).astype(F32)
        return jnp.where(odd, pltpu.roll(block, 64, 1), block)

    for s in range(0, 4, 2):
        both = jnp.where(low_256, slot(s), pltpu.roll(slot(s + 1), 64, 1))
        k.w_project[:, s * 64 : s * 64 + 128] = both.astype(BF16)
    k.w_slot[...] = jnp.where(low_256, slot(4), 0.0).astype(BF16)
    k.w_pool[0:64, :] = k.aspp_pool[...]
    k.w_pool[64:128, :] = k.aspp_pool[...]

    for copy in pool_copies:
        copy.wait()
    for b in range(4):
        pooled = (k.in_pool[2 * b, 0:1, :] + k.in_pool[2 * b + 1, 0:1, :]) / area
        k.pooled[:, b * 512 : b * 512 + 512] = jnp.broadcast_to(pooled, (16, 512)).astype(BF16)
    pool_conv = mm_t(k.pooled[...], k.w_pool[...])[0:1, :]
    mean, inverse = statistics(
        net, k.branches, k.mask, counts, k.out_1, k.in_1, counted, extra=pool_conv
    )
    every = k.in_1[0:4, 4, :]
    pool_mean = jnp.sum(every, axis=0, keepdims=True) / 4.0
    pool_gap = every - pool_mean
    pool_inverse = lax.rsqrt(jnp.sum(pool_gap * pool_gap, axis=0, keepdims=True) / 4.0 + EPS)
    pool_normed = pool_gap * pool_inverse
    pool_gain, pool_bias = k.affine_p[2:3, :], k.affine_p[3:4, :]
    pool_u = pool_gain * pool_normed + pool_bias
    k.rows_scratch[0:4, :] = pool_u * sigmoid(pool_u)
    pool_act = jnp.broadcast_to(k.rows_scratch[pl.ds(net.z, 1), :], (16, 128)).astype(BF16)

    def normed_branch(at):
        return (k.branches[at, :] - mean) * inverse

    gain_b, bias_b = k.affine_b[0:1, :], k.affine_b[1:2, :]

    def activate_branches(at):
        u = gain_b * normed_branch(at) + bias_b
        k.spatial[at, :] = (u * sigmoid(u)).astype(BF16)

    each_rows(1536, 128, activate_branches)

    pool_row = mm_t(pool_act, k.w_slot[...])[0:1, :]

    def project_rows(i, carry):
        at = pl.ds(pl.multiple_of(i * 192, 64), 192)
        below = pl.ds(pl.multiple_of(i * 192 + 768, 64), 192)
        first = mm_t(k.spatial[at, :], k.w_project[...]) + pool_row
        second = mm_t(k.spatial[below, :], k.w_project[...]) + pool_row
        for b, block in enumerate(pair(first, second)):
            k.part_2[b, at, :] = block
        return carry

    def project_half(half):
        alternate(project_rows, half)

    low_128 = lax.broadcasted_iota(jnp.int32, (128, 128), 1) < 64

    def pair_mask(at):
        below = pl.ds(pl.multiple_of(at.start + 768, 128), 128)
        k.mask_pairs[at, :] = jnp.where(low_128, k.mask[at, :], k.mask[below, :])

    each_rows(768, 128, pair_mask)
    sum_scatter(net, k.part_2, scatter_refs(k, "sum2"), k.projected, produce=project_half)
    mean_p, inverse_p = statistics(
        net, k.projected, k.mask_pairs, counts, k.out_2, k.in_2, counted, folded=True
    )
    gain_p, bias_p = k.affine_p[0:1, :], k.affine_p[1:2, :]

    def normed_projected(at):
        return (k.projected[at, :] - mean_p) * inverse_p

    def activate_projected(at):
        u = gain_p * normed_projected(at) + bias_p
        k.gathered[net.m, at, :] = (u * sigmoid(u)).astype(BF16)

    each_rows(768, 128, activate_projected)
    gather_blocks(net, lambda b, at: k.gathered.at[b, at], 768)

    def spread(source, target):
        def body(at):
            first, second = unpair([source[b, at, :].astype(F32) for b in range(4)])
            target[at, :] = first.astype(BF16)
            target[pl.ds(pl.multiple_of(at.start + 768, 128), 128), :] = second.astype(BF16)

        each_rows(768, 128, body)

    k.features[...] = k.gathered[net.m]
    spread(k.gathered, k.wide_features)

    class_row = lax.broadcasted_iota(jnp.int32, (32, 512), 0)
    is_class, is_depth = class_row < 19, class_row == 19
    is_normal = (class_row == 20) | (class_row == 21)
    tile_row = lax.broadcasted_iota(jnp.int32, (32, 128), 0)
    bias_column = jnp.zeros((32, 128), F32)
    for c in range(22):
        bias_column = jnp.where(tile_row == c, k.head_bias[c], bias_column)
    task = [jnp.exp(jnp.full((32, 128), -k.log_vars[t], F32)) / counted for t in range(3)]
    weight_column = jnp.where(tile_row < 19, task[0], jnp.where(tile_row == 19, task[1], task[2]))
    bias_column, weight_column = wide(bias_column, 512), wide(weight_column, 512)
    k.head[...] = k.head_rows[...].astype(BF16)
    top_row, left_edge = k.boxes[net.z, 0], k.boxes[net.z, 1]
    bottom_row, right_edge = top_row + k.boxes[net.z, 2], left_edge + k.boxes[net.z, 3]
    lane = lax.broadcasted_iota(jnp.int32, (1, 512), 1)

    def four_rows(rows):
        return jnp.concatenate(rows, axis=1)
    loss_sums, bias_sums = 0.0, 0.0
    for chunk in range(3):
        at = pl.ds(chunk * 512, 512)
        logits = mm_t(k.head[...], k.wide_features[at, :]) + bias_column
        row_id, column_id = net.r * 12 + chunk * 4 + lane // 128, lane % 128
        inside = (row_id >= top_row) & (row_id < bottom_row)
        inside = inside & (column_id >= left_edge) & (column_id < right_edge)
        inside = jnp.where(inside, 1.0, 0.0)
        span = range(chunk * 4, chunk * 4 + 4)
        label = four_rows([k.labels[y] for y in span])
        target = jnp.where(is_depth, four_rows([k.depth[y] for y in span]), 0.0)
        for n in range(2):
            normal = four_rows([k.normal[y, n : n + 1, :] for y in span])
            target = jnp.where(class_row == 20 + n, normal, target)
        top = jnp.max(jnp.where(is_class, logits, -jnp.inf), axis=0, keepdims=True)
        powers = jnp.where(is_class, jnp.exp(jnp.where(is_class, logits - top, 0.0)), 0.0)
        power_sum = jnp.sum(powers, axis=0, keepdims=True)
        onehot = jnp.where(class_row == label, 1.0, 0.0)
        cross = jnp.log(power_sum) + top - jnp.sum(logits * onehot, axis=0, keepdims=True)
        gap = logits - target
        smooth = jnp.sqrt(gap * gap + 1.0)
        loss = jnp.where(class_row == 0, cross, 0.0)
        loss = jnp.where(is_depth, smooth - 1.0, loss)
        loss = jnp.where(is_normal, gap * gap, loss) * inside
        grad = jnp.where(is_class, powers / power_sum - onehot, 0.0)
        grad = jnp.where(is_depth, gap / smooth, grad)
        grad = jnp.where(is_normal, 2.0 * gap, grad) * (weight_column * inside)
        loss_sums = loss_sums + jnp.sum(loss, axis=1, keepdims=True)
        bias_sums = bias_sums + jnp.sum(grad, axis=1, keepdims=True)
        high = grad.astype(BF16)
        k.grad_logits[0:32, at] = high
        k.grad_logits[32:64, at] = (grad - high.astype(F32)).astype(BF16)
    head_terms = mm(k.grad_logits[...], k.wide_features[...])
    k.out_head[:, 0:256] = head_terms[0:32, :] + head_terms[32:64, :]
    first_lane = lax.broadcasted_iota(jnp.int32, (32, 128), 1) == 0
    k.out_head[:, 256:384] = jnp.where(first_lane, bias_sums, loss_sums)
    quarter = pl.ds(pl.multiple_of(net.m * 8, 8), 8)
    head_copies = []

    def share_head():
        for peer in net.group:
            head_copies.append(net.send(k.out_head.at[quarter], k.in_head.at[net.slot], peer))
        k.in_head[net.slot] = k.out_head[quarter, :]

    own_head = k.head_rows[:, lane_block(net.m // 2)]
    own_head = jnp.where(odd, pltpu.roll(own_head, 64, 1), own_head)
    own_head = jnp.where(low_128[0:32, :], own_head, 0.0)
    head_low = jnp.concatenate([own_head, own_head], axis=0).astype(BF16)
    own_head = pltpu.roll(own_head, 64, 1)
    head_high = jnp.concatenate([own_head, own_head], axis=0).astype(BF16)
    k.grad_p[...] = tm_m(k.grad_logits[:, 0:768], head_low) + tm_m(
        k.grad_logits[:, 768:1536], head_high
    )

    def back_features(at):
        k.grad_p[at, :] = k.grad_p[at, :] * slope(gain_p * normed_projected(at) + bias_p)

    each_rows(768, 128, back_features)
    bias_grad, gain_grad = gradient_sums(
        net, k.grad_p, normed_projected, k.out_3, k.in_3, folded=True, meanwhile=share_head
    )
    keep_rows(k.norm_p, gain_grad, bias_grad)

    def back_projected(at):
        shared = k.mask_pairs[at, :] / counted * gain_p
        grad = gain_p * k.grad_p[at, :] - shared * (bias_grad + normed_projected(at) * gain_grad)
        k.gathered_grad[net.m, at, :] = (inverse_p * grad).astype(BF16)

    each_rows(768, 128, back_projected)
    gather_blocks(net, lambda b, at: k.gathered_grad.at[b, at], 768)
    spread(k.gathered_grad, k.grad_projected)
    (pixel_sum,) = column_sums(lambda at: (k.grad_projected[at, :].astype(F32),), 1536, 256, 1)
    row_16 = lax.broadcasted_iota(jnp.int32, (16, 256), 0)
    terms = jnp.zeros((16, 256), F32)
    for i, term in enumerate(split_three(pixel_sum)):
        terms = jnp.where(row_16 == i, term.astype(F32), terms)
    terms = terms.astype(BF16)
    tall = jnp.concatenate([terms] * 8, axis=0)
    pool_grad = jnp.sum(mm(tall, k.w_slot[...]), axis=0, keepdims=True) * 0.125

    def project_gradient():
        for b in range(2):
            lanes = slice(b * 128, b * 128 + 128)
            grad = tm_m(k.grad_projected[:, lanes], k.spatial[...])
            k.grad_project[b * 4 : b * 4 + 4, :, 0:256] = grad.reshape(4, 32, 256).astype(BF16)
        grad = tm_m(terms, pool_act)
        k.grad_project[:, :, 256:384] = grad.reshape(8, 32, 128).astype(BF16)

    def back_spatial(at):
        grad = mm(k.grad_projected[at, :], k.w_project[...])
        k.grad_b[at, :] = grad * slope(gain_b * normed_branch(at) + bias_b)

    each_rows(1536, 128, back_spatial)
    bias_grad_b, gain_grad_b = gradient_sums(
        net,
        k.grad_b,
        normed_branch,
        k.out_4,
        k.in_4,
        extra=pool_grad,
        meanwhile=project_gradient,
    )
    keep_rows(k.norm_b, gain_grad_b, bias_grad_b)

    pool_terms = k.in_4[0:4, 4, :] + k.in_4[4:8, 4, :]
    pool_terms = pool_terms * slope(pool_u)
    pool_bias_grad = jnp.sum(pool_terms, axis=0, keepdims=True)
    pool_gain_grad = jnp.sum(pool_terms * pool_normed, axis=0, keepdims=True)
    keep_rows(k.norm_pool, pool_gain_grad, pool_bias_grad)
    pool_back = pool_inverse * (
        pool_gain * pool_terms
        - pool_gain / 4.0 * (pool_bias_grad + pool_normed * pool_gain_grad)
    )
    low = lax.broadcasted_iota(jnp.int32, (4, 128), 1) < 64
    k.rows_scratch[4:8, :] = jnp.where(low, pool_back, 0.0)
    grad_conv = jnp.broadcast_to(k.rows_scratch[pl.ds(net.z + 4, 1), :], (16, 128)).astype(BF16)
    spread_back = mm(grad_conv, k.w_pool[...])[0:8, :]
    for b in range(4):
        k.out_back[b] = spread_back[:, b * 512 : b * 512 + 512]
    back_copies = [
        net.send(k.out_back.at[lax.rem(net.m + a, 4)], k.in_back.at[a], (lax.rem(net.m + a, 4), net.r, net.z))
        for a in range(1, 4)
    ]

    only_first = lax.broadcasted_iota(jnp.int32, (16, 128), 0) == 0
    one_row = jnp.where(only_first, grad_conv.astype(F32) * 0.5, 0.0).astype(BF16)
    for e in range(8):
        grad = tm_m(one_row, k.pooled[:, e * 256 : e * 256 + 256])
        k.grad_pool[e] = grad[0:64, :].astype(BF16)

    def back_branches(at):
        shared = wide(k.mask[at, :], 256) / counted * gain_b
        grad = gain_b * k.grad_b[at, :] - shared * (bias_grad_b + normed_branch(at) * gain_grad_b)
        k.grad_branches[at, :] = (inverse * grad).astype(BF16)

    for copy in back_copies:
        copy.wait()
    k.grad_pooled[...] = (k.out_back[net.m] + k.in_back[1] + k.in_back[2] + k.in_back[3]) / area
    for copy in head_copies:
        copy.wait()
    k.head_sums[quarter, :] = jnp.sum(k.in_head[...], axis=0)
    head_copies = [
        net.send(k.head_sums.at[quarter], k.head_sums.at[quarter], (lax.rem(net.m + a, 4), net.r, net.z))
        for a in range(1, 4)
    ]
    each_rows(1536, 128, back_branches)
    for copy in head_copies:
        copy.wait()


def run_pyramid(args):
    return call_kernel(
        pyramid_forward,
        "pyramid",
        1,
        args,
        dict(
            w_pyramid=((13, 4, 64, 512), BF16),
            features=((768, 128), BF16),
            norm_p=((8, 128), F32),
            grad_project=((8, 32, 384), BF16),
            grad_pool=((8, 64, 256), BF16),
            norm_b=((8, 256), F32),
            norm_pool=((8, 128), F32),
            grad_branches=((1536, 256), BF16),
            grad_pooled=((8, 512), F32),
            head_sums=((32, 384), F32),
        ),
        dict(
            w_slots=pltpu.VMEM((4, 5, 64, 256), BF16),
            local_sems=pltpu.SemaphoreType.DMA((3,)),
            affine_b=pltpu.VMEM((8, 256), F32),
            affine_p=pltpu.VMEM((8, 128), F32),
            head_rows=pltpu.VMEM((32, 256), F32),
            head=pltpu.VMEM((32, 256), BF16),
            pooled=pltpu.VMEM((16, 2048), BF16),
            spatial=pltpu.VMEM((1536, 256), BF16),
            grad_projected=pltpu.VMEM((1536, 256), BF16),
            w_project=pltpu.VMEM((256, 256), BF16),
            w_slot=pltpu.VMEM((256, 128), BF16),
            w_pool=pltpu.VMEM((128, 2048), BF16),
            mask_pairs=pltpu.VMEM((768, 128), F32),
            out_pool=pltpu.VMEM((8, 512), F32),
            in_pool=pltpu.VMEM((8, 8, 512), F32),
            cells=pltpu.VMEM((12, 208, 512), F32),
            edge_out=pltpu.VMEM((1536, 256), BF16),
            edge_in=pltpu.VMEM((1536, 256), BF16),
            part=pltpu.VMEM((4, 1536, 256), F32),
            **scatter_scratch("sum", 1536, 256),
            branches=pltpu.VMEM((1536, 256), F32),
            rows_scratch=pltpu.VMEM((8, 128), F32),
            part_2=pltpu.VMEM((4, 768, 128), F32),
            **scatter_scratch("sum2", 768, 128),
            projected=pltpu.VMEM((768, 128), F32),
            gathered=pltpu.VMEM((4, 768, 128), BF16),
            wide_features=pltpu.VMEM((1536, 256), BF16),
            grad_logits=pltpu.VMEM((64, 1536), BF16),
            out_head=pltpu.VMEM((32, 384), F32),
            in_head=pltpu.VMEM((8, 8, 384), F32),
            grad_p=pltpu.VMEM((768, 128), F32),
            gathered_grad=pltpu.VMEM((4, 768, 128), BF16),
            grad_b=pltpu.VMEM((1536, 256), F32),
            out_back=pltpu.VMEM((4, 8, 512), F32),
            in_back=pltpu.VMEM((4, 8, 512), F32),
            **exchange_scratch(1),
            **exchange_scratch(2),
            **exchange_scratch(3),
            **exchange_scratch(4),
        ),
        96,
        smem=dict(boxes=1, head_bias=1, log_vars=1),
        hbm=dict(far_pyramid=1, far_slots=1),
        stream=dict(mask=1, w_pyramid=1),
    )


def core_halves(net, whole, arrived):
    away = pl.ds(pl.multiple_of(4 - 4 * net.r, 4), 4)
    return net.send(whole.at[away], arrived, net.core)


def add_halves(net, whole, arrived, target):
    for z in range(4):
        total = whole[4 * net.r + z].astype(F32) + arrived[z].astype(F32)
        target[z] = total.astype(target.dtype)


def chunk_of(net):
    return lambda z: 2 * lax.rem(z + net.m, 2) + z // 2


def along_z(net, source, target, chunk=lambda z: z):
    copies = []
    for d in (1, 2, 3):
        there = lax.rem(net.z + d, 4)
        copies.append(
            net.send(source.at[chunk(there)], target.at[d - 1], (net.m, net.r, there))
        )
    return copies


def finish_z(net, half, arrived, chunk=lambda z: z):
    return half[chunk(net.z)].astype(F32) + sum(arrived[d].astype(F32) for d in range(3))


class PairSums:
    def __init__(self, net, half, other, pair, last):
        self.net, self.half, self.other, self.pair, self.last = net, half, other, pair, last
        kept, away = lax.rem(net.z + net.m, 2), lax.rem(net.z + net.m + 1, 2)
        self.kept = 2 * kept
        beside = net.z + 1 - 2 * lax.rem(net.z, 2)
        self.first = self.copy(half.at[pl.ds(2 * away, 2)], other, beside)
        self.high = net.z // 2
        if last is not None:
            self.second = self.copy(pair.at[1 - self.high], last, net.z + 2 - 4 * self.high)

    def copy(self, src, dst, z):
        net, i = self.net, self.net.count
        net.count += 1
        return pltpu.make_async_remote_copy(
            src_ref=src,
            dst_ref=dst,
            send_sem=net.send_sems.at[i],
            recv_sem=net.recv_sems.at[i],
            device_id=(net.m, net.r, z),
            device_id_type=MESH,
        )

    def go_on(self, half):
        self.first.wait()

        def body(i, carry):
            for h in range(2):
                total = half[self.kept + h, i].astype(F32) + self.other[h, i].astype(F32)
                self.pair[h, i] = total.astype(BF16)
            return carry

        lax.fori_loop(0, half.shape[1], body, 0)

    def finish(self, target):
        self.second.wait()

        def body(i, carry):
            total = self.pair[self.high, i].astype(F32) + self.last[i].astype(F32)
            target[0, i] = total[:, 0:256].astype(BF16)
            target[1, i] = total[:, 256:512].astype(BF16)
            return carry

        lax.fori_loop(0, target.shape[1], body, 0)


def pyramid_backward(net, k):
    counted = pixel_count(k.boxes)
    greet([net.side, net.over] + net.group)
    k.blocks[net.m] = k.grad_branches[...]
    small = [
        core_halves(net, k.grad_project, k.core_project),
        core_halves(net, k.grad_pool, k.core_pool),
    ]
    for c in range(4):
        zero_margins(k.cells.at[c], 40, 128)

    def rows_of(i, size=384):
        return pl.ds(pl.multiple_of(i * size, 128), size)

    low = lax.broadcasted_iota(jnp.int32, (128, 128), 1) < 64
    near = net.m // 2
    far = 1 - near
    mine_first = net.r == near
    mine_second = net.r == far

    def both(source, pair_of, i, lane):
        at = slice(lane * 128, lane * 128 + 128)
        left = source[2 * pair_of, rows_of(i, 128), at].astype(F32)
        right = source[2 * pair_of + 1, rows_of(i, 128), at].astype(F32)
        first = jnp.where(low, left, pltpu.roll(right, 64, 1))
        return first, jnp.where(low, pltpu.roll(left, 64, 1), right)

    def shift_rows(pair_of, i, cell, rate, base):
        for j in range(3):
            start = 40 - rate * (j - 1)
            block = k.cells[cell, i, start : start + 128, :].astype(BF16)
            k.shifts[base + j, rows_of(i, 128), lane_block(pair_of)] = block

    def build(pair_of):
        def fill(i, carry):
            point, first = both(k.blocks, pair_of, i, 0)
            k.shifts[0, rows_of(i, 128), lane_block(pair_of)] = point.astype(BF16)
            second, third = both(k.blocks, pair_of, i, 1)
            k.cells[0, i, 40:168, :] = first
            k.cells[1, i, 40:168, :] = second
            k.cells[2, i, 40:168, :] = third
            return carry

        lax.fori_loop(0, 12, fill, 0, unroll=2)

        def spread(i, carry):
            for cell, rate, base in ((0, 12, 1), (1, 24, 4), (2, 36, 7)):
                shift_rows(pair_of, i, cell, rate, base)
            return carry

        lax.fori_loop(0, 12, spread, 0, unroll=2)

    def build_edge(pair_of):
        def fill(i, carry):
            k.cells[3, i, 40:168, :] = both(k.other, pair_of, i, 0)[1]
            return carry

        lax.fori_loop(0, 12, fill, 0, unroll=2)

        def spread(i, carry):
            shift_rows(pair_of, i, 3, 12, 10)
            return carry

        lax.fori_loop(0, 12, spread, 0, unroll=2)

    def weight_gradients(pair_of, between=None):
        owners = pl.ds(4 * pair_of, 4)

        def run(start, stop, shift):
            def body(t, carry):
                grad = tm_m(k.shifts[t, :, lane_block(pair_of)], k.trunk[...])
                k.grad_pyramid[owners, t + shift] = grad.reshape(4, 32, 512).astype(BF16)
                return carry

            lax.fori_loop(start, stop, body, 0)

        run(0, 1, 0)
        run(1, 4, 3)
        run(10, 13, net.r * 6 - 9)
        for j in range(3):
            k.grad_pyramid[owners, 7 - net.r * 6 + j] = jnp.zeros((4, 32, 512), BF16)
        if between is not None:
            between()
        run(4, 10, 6)

    def beside(pair_of):
        view = (pl.ds(2 * pair_of, 2), slice(None), pl.ds(0, 128))
        return net.send(k.blocks.at[view], k.other.at[pl.ds(2 * pair_of, 2)], net.core)

    def to_core(pair_of, low, high):
        i = net.count
        net.count += 1
        taps = pl.ds(low, high - low)
        return pltpu.make_async_remote_copy(
            src_ref=k.grad_pyramid.at[pl.ds(4 * pair_of, 4), taps],
            dst_ref=k.core_pyramid.at[:, taps],
            send_sem=net.send_sems.at[i],
            recv_sem=net.recv_sems.at[i],
            device_id=net.core,
            device_id_type=MESH,
        )

    def add_core(pair_of, low, high):
        def body(i, carry):
            for z in range(4):
                total = k.grad_pyramid[4 * pair_of + z, i].astype(F32)
                total = total + k.core_pyramid[z, i].astype(F32)
                k.half_pyramid[z, i] = total.astype(BF16)
            return carry

        lax.fori_loop(low, high, body, 0)

    first_swap = []

    def near_pair():
        copy = beside(near)
        build(near)
        copy.wait()
        build_edge(near)
        k.stream.need(trunk=1)
        weight_gradients(near)
        first_swap.append(to_core(near, 0, 16))
        pl.when(mine_second)(first_swap[0].start)

    gather_blocks(net, lambda b, at: k.blocks.at[b, at], 1536, meanwhile=near_pair)
    copy = beside(far)
    build(far)
    for swap in small:
        swap.wait()
    add_halves(net, k.grad_project, k.core_project, k.half_project)
    add_halves(net, k.grad_pool, k.core_pool, k.half_pool)
    small_moves = along_z(net, k.half_project, k.z_project, chunk_of(net))
    small_moves = small_moves + along_z(net, k.half_pool, k.z_pool)
    copy.wait()
    build_edge(far)
    pair_sums = PairSums(net, k.half_pyramid, k.z_other, k.z_pair, None)

    @pl.when(mine_first)
    def _():
        first_swap[0].wait_recv()
        add_core(near, 0, 16)
        pair_sums.first.start()

    def trunk_rows(i, carry):
        total = 0.0
        for t in range(13):
            total = total + mm(k.shifts[t, rows_of(i), :], k.w_pyramid[t])
        k.shortcut[rows_of(i), :] = total
        return carry

    k.stream.need(w_pyramid=1, expanded=1, x=1, mask=1)
    lax.fori_loop(0, 4, trunk_rows, 0)
    mean, inverse = k.stats_3[0:1, :], k.stats_3[1:2, :]
    gain, bias = k.affine_3[0:1, :], k.affine_3[1:2, :]
    pooled = k.grad_pooled[0:1, :]

    def normed(at):
        return (k.expanded[at, :] - mean) * inverse

    def back_trunk(at):
        u = gain * normed(at) + bias + k.x[at, :].astype(F32)
        grad = k.shortcut[at, :] + wide(k.mask[at, :], 512) * pooled
        k.shortcut[at, :] = grad * slope(u)

    each_rows(1536, 64, back_trunk)
    k.stream.done(shortcut=1)

    second_swap = [to_core(far, 0, 10), to_core(far, 10, 16)]

    def far_gradients():
        weight_gradients(far, lambda: pl.when(mine_first)(second_swap[0].start))

        @pl.when(mine_first)
        def _():
            second_swap[1].start()
            pair_sums.go_on(k.half_pyramid)

    bias_grad, gain_grad = gradient_sums(
        net, k.shortcut, normed, k.out_1, k.in_1, meanwhile=far_gradients
    )
    keep_rows(k.norm_3, gain_grad, bias_grad)

    def back_expanded(at):
        shared = wide(k.mask[at, :], 512) / counted * gain
        grad = gain * k.shortcut[at, :] - shared * (bias_grad + normed(at) * gain_grad)
        k.grad_expanded[at, :] = (inverse * grad).astype(BF16)

    each_rows(1536, 64, back_expanded)
    k.stream.done(grad_expanded=1)
    for move_ in small_moves:
        move_.wait()
    k.sum_project[...] = finish_z(net, k.half_project, k.z_project, chunk_of(net)).astype(BF16)
    k.sum_pool[...] = finish_z(net, k.half_pool, k.z_pool)

    @pl.when(mine_second)
    def _():
        first_swap[0].wait_send()
        second_swap[0].wait_recv()
        add_core(far, 0, 10)
        second_swap[1].wait_recv()
        add_core(far, 10, 16)

    @pl.when(mine_first)
    def _():
        for swap in second_swap:
            swap.wait_send()


def run_pyramid_backward(args):
    return call_kernel(
        pyramid_backward,
        "pyramid_back",
        2,
        args,
        dict(
            shortcut=((1536, 512), F32),
            grad_expanded=((1536, 512), BF16),
            norm_3=((8, 512), F32),
            half_pyramid=((4, 16, 32, 512), BF16),
            z_pair=((2, 16, 32, 512), BF16),
            sum_project=((32, 384), BF16),
            sum_pool=((64, 256), F32),
        ),
        dict(
            half_project=pltpu.VMEM((4, 32, 384), BF16),
            half_pool=pltpu.VMEM((4, 64, 256), BF16),
            z_other=pltpu.VMEM((2, 16, 32, 512), BF16),
            z_project=pltpu.VMEM((3, 32, 384), BF16),
            z_pool=pltpu.VMEM((3, 64, 256), BF16),
            grad_pyramid=pltpu.VMEM((8, 16, 32, 512), BF16),
            core_pyramid=pltpu.VMEM((4, 16, 32, 512), BF16),
            core_project=pltpu.VMEM((4, 32, 384), BF16),
            core_pool=pltpu.VMEM((4, 64, 256), BF16),
            blocks=pltpu.VMEM((4, 1536, 256), BF16),
            other=pltpu.VMEM((4, 1536, 128), BF16),
            cells=pltpu.VMEM((4, 12, 208, 128), F32),
            shifts=pltpu.VMEM((13, 1536, 256), BF16),
            **exchange_scratch(1),
        ),
        48,
        stream=dict(w_pyramid=1, expanded=1, x=1, mask=1, trunk=1, shortcut=1, grad_expanded=1),
    )


def bottleneck_backward(net, k):
    counted = pixel_count(k.boxes)
    loads = load_taps(k)
    high, source = net.z // 2, net.slot // 2
    here = net.m * 8 + net.slot
    owners, givers = [], []
    for i in range(2):
        part = 2 * net.m + i
        column = 2 * net.r + lax.rem(net.z + net.m, 2)
        owners.append((column, part // 4, lax.rem(part, 4)))
        givers.append((source, net.m // 2, lax.rem(net.m + source, 2) + 2 * i))

    def elsewhere(device):
        return device[0] * 8 + device[1] * 4 + device[2] != here

    moves = elsewhere(owners[0])
    stays = jnp.logical_not(moves)
    greet(
        [net.side, net.over, net.diagonal] + net.group + [owners[1]],
        [(owners[0], moves), (givers[0], elsewhere(givers[0])), (givers[1], elsewhere(givers[1]))],
    )

    def to_owners(views, arrived, sem):
        base = net.count
        net.count += 2

        def copy(i, g, device):
            return pltpu.make_async_remote_copy(
                src_ref=views(i),
                dst_ref=arrived.at[g],
                send_sem=net.send_sems.at[base + i],
                recv_sem=net.recv_sems.at[base + g],
                device_id=device,
                device_id_type=MESH,
            )

        first, second = copy(0, high, owners[0]), copy(1, high, owners[1])
        kept = pltpu.make_async_copy(views(0), arrived.at[high], sem)

        def begin():
            pl.when(moves)(first.start)
            pl.when(stays)(kept.start)
            second.start()

        def wait():
            pl.when(moves)(first.wait_send)
            pl.when(stays)(kept.wait)
            second.wait_send()
            for g in range(2):
                pl.when(elsewhere(givers[g]))(copy(0, g, owners[1]).wait_recv)

        begin()
        return wait

    def lanes_for(i):
        return pl.ds(i * 256, 256)

    early = net.r == net.m // 2
    is_late = net.r == 1 - net.m // 2
    pair_sums = PairSums(net, k.far_half_pyramid, k.z_other, k.z_pair, k.z_last)

    odd_z = lax.rem(net.z, 2)
    lone = early & (odd_z == 0)
    beside = early & (odd_z == 1)
    stay = pltpu.make_async_copy(k.pyramid_sum, k.relay.at[0], k.local_sems.at[9])

    def remote(src, dst, send, arrive, device):
        return pltpu.make_async_remote_copy(
            src_ref=src,
            dst_ref=dst,
            send_sem=net.send_sems.at[send],
            recv_sem=net.recv_sems.at[arrive],
            device_id=device,
            device_id_type=MESH,
        )

    base = net.count
    net.count += 6
    to_side = remote(k.pyramid_sum, k.relay.at[0], base, base, net.side)
    across = (net.m ^ (2 + odd_z), net.r, net.z)
    to_across = remote(k.pyramid_sum, k.relay.at[1], base + 1, base + 1, across)
    plane = lax.rem(net.m + net.z, 2)

    def forward(e, i):
        device = (net.m, net.r if e == 0 else 1 - net.r, 2 * plane + i)
        return remote(
            k.relay.at[e, i], k.own_pyramid.at[high], base + 2 + 2 * e + i, base + 2 + high, device
        )

    forwards = [[forward(e, i) for i in range(2)] for e in range(2)]
    keep = pltpu.make_async_copy(k.relay.at[0, odd_z], k.own_pyramid.at[high], k.local_sems.at[12])
    keeps = early & (plane == high)

    def kept_here(i):
        return keeps & (odd_z == i)

    def begin_early():
        pl.when(lone)(stay.start)
        pl.when(beside)(to_side.start)

    def relay_early():
        pl.when(lone)(stay.wait)
        pl.when(beside)(to_side.wait)
        for i in range(2):
            pl.when(early & jnp.logical_not(kept_here(i)))(forwards[0][i].start)
        pl.when(keeps)(keep.start)

    def relay_late():
        pl.when(early)(to_across.wait_recv)
        for i in range(2):
            pl.when(early)(forwards[1][i].start)

    def wait_pyramid():
        pl.when(is_late)(to_across.wait_send)
        for i in range(2):
            pl.when(early & jnp.logical_not(kept_here(i)))(forwards[0][i].wait_send)
            pl.when(early)(forwards[1][i].wait_send)
        pl.when(keeps)(keep.wait)
        for g in range(2):
            local = early & (lax.rem(net.z // 2 + net.m, 2) + 2 * g == net.z)
            arrival = remote(k.relay.at[0, 0], k.own_pyramid.at[g], base, base + 2 + g, net.core)
            pl.when(jnp.logical_not(local))(arrival.wait_recv)


    k.stream.need(z_pair=1)
    pl.when(is_late)(pair_sums.first.start)
    pl.when(early)(pair_sums.second.start)
    wait_project = to_owners(lambda i: k.sum_project, k.own_project, k.local_sems.at[10])

    def rows_of(i, size=384):
        return pl.ds(pl.multiple_of(i * size, 128), size)

    def expand_half(half):
        for i in (half, half + 2):
            at = pl.ds(i * 384, 384)
            total = mm_t(k.grad_expanded[at, :], k.w_expand[...])
            for b in range(4):
                k.part[b, at, :] = total[:, b * 128 : b * 128 + 128]

    swaps, late_moves = [], []

    def expand_gradient():
        k.stream.need(hidden_two=1)

        def body(b, carry):
            grad = tm_m(k.hidden_two[:, lane_block(b)], k.grad_expanded[...])
            k.grad_expand[pl.ds(2 * b, 2)] = grad.reshape(2, 64, 512).astype(BF16)
            return carry

        lax.fori_loop(0, 4, body, 0)
        swaps.append(core_halves(net, k.grad_expand, k.core_expand))

    sum_scatter(net, k.part, scatter_refs(k, "sum"), k.grad_2, meanwhile=expand_gradient, produce=expand_half)
    k.stream.need(dilated=1, mask=1)

    def norm_back(grad, value, stats, affine, outgoing, incoming, store, kept, meanwhile=None):
        mean, inverse = stats[0:1, :], stats[1:2, :]
        gain, bias = affine[0:1, :], affine[1:2, :]

        def normed(at):
            return (value[at, :] - mean) * inverse

        def through(at):
            grad[at, :] = grad[at, :] * slope(gain * normed(at) + bias)

        each_rows(1536, 128, through)
        bias_grad, gain_grad = gradient_sums(
            net, grad, normed, outgoing, incoming, meanwhile=meanwhile
        )
        keep_rows(kept, gain_grad, bias_grad)

        def back(at):
            shared = k.mask[at, :] / counted * gain
            result = gain * grad[at, :] - shared * (bias_grad + normed(at) * gain_grad)
            store(at, (inverse * result).astype(BF16))

        each_rows(1536, 128, back)

    def store_2(at, value):
        k.grad_pad[pl.ds(pl.multiple_of(at.start + 512, 128), 128), :] = value

    def pass_expand():
        k.stream.need(half_pyramid=1)
        @pl.when(is_late)
        def _():
            pair_sums.go_on(k.half_pyramid)
            pair_sums.second.start()

        @pl.when(early)
        def _():
            pair_sums.finish(k.pyramid_sum)

        begin_early()
        swaps.pop().wait()
        add_halves(net, k.grad_expand, k.core_expand, k.half_expand)
        late_moves.extend(along_z(net, k.half_expand, k.z_expand))

    norm_back(
        k.grad_2,
        k.dilated,
        k.stats_2,
        k.affine_2,
        k.out_2,
        k.in_2,
        store_2,
        k.norm_2,
        meanwhile=pass_expand,
    )
    halo = send_halo(net, k.grad_pad)
    zero_margins(k.cells, 8, 128)
    halo.wait()

    def spread(i, carry):
        k.cells[i, 8:136, :] = k.grad_pad[rows_of(i, 128), :].astype(F32)
        for j in range(3):
            start = 8 - 4 * (j - 1)
            k.grad_taps[rows_of(i, 128), j * 128 : j * 128 + 128] = k.cells[
                i, start : start + 128, :
            ].astype(BF16)
        return carry

    lax.fori_loop(0, 20, spread, 0)
    for load in loads:
        load.wait()

    def dilated_rows(i, carry):
        total = 0.0
        for tap in range(3):
            at = pl.ds(pl.multiple_of((i * 3 + 8 - 4 * tap) * 128, 128), 384)
            total = total + mm_t(k.grad_taps[at, :], k.w_taps[tap])
        for b in range(4):
            k.part[b, rows_of(i), :] = total[:, b * 128 : b * 128 + 128]
        return carry

    def dilated_half(half):
        def run(i, carry):
            return dilated_rows(half + 2 * i, carry)

        lax.fori_loop(0, 2, run, 0)

    def dilated_gradient():
        k.stream.need(hidden=1)

        for i in range(3):

            def body(b, carry):
                band = k.hidden[pl.ds(i * 512, 1536), lane_block(b)]
                grad = tm_m(band, k.grad_taps[pl.ds(512, 1536), :])
                for j in range(3):
                    block = grad[:, j * 128 : j * 128 + 128].reshape(2, 64, 128)
                    rows = slice((i * 3 + j) * 64, (i * 3 + j) * 64 + 64)
                    k.grad_dilated[pl.ds(2 * b, 2), rows, :] = block.astype(BF16)
                return carry

            lax.fori_loop(0, 4, body, 0)
        swaps.append(core_halves(net, k.grad_dilated, k.core_dilated))

    sum_scatter(net, k.part, scatter_refs(k, "sum2"), k.grad_1, meanwhile=dilated_gradient, produce=dilated_half)
    k.stream.need(reduced=1)

    def store_1(at, value):
        k.grad_reduced[at, lane_block(net.m)] = value

    def pass_halves():
        @pl.when(is_late)
        def _():
            pair_sums.finish(k.pyramid_sum)
            to_across.start()

        relay_early()
        swaps.pop().wait()
        add_halves(net, k.grad_dilated, k.core_dilated, k.half_dilated)
        late_moves.extend(along_z(net, k.half_dilated, k.z_dilated))

    norm_back(
        k.grad_1,
        k.reduced,
        k.stats_1,
        k.affine_1,
        k.out_1,
        k.in_1,
        store_1,
        k.norm_1,
        meanwhile=pass_halves,
    )

    def reduce_gradients(pair_of):
        def body(i, carry):
            b = 2 * pair_of + i
            grad = tm_m(k.grad_reduced[:, lane_block(b)], k.x[...])
            k.grad_reduce[pl.ds(2 * b, 2)] = grad.reshape(2, 64, 512).astype(BF16)
            return carry

        lax.fori_loop(0, 2, body, 0)

    def near_gradients():
        relay_late()
        k.stream.need(x=1)
        reduce_gradients(net.m // 2)

    gather_blocks(
        net,
        lambda b, at: k.grad_reduced.at[at, lane_block(b)],
        1536,
        meanwhile=near_gradients,
    )

    reduce_gradients(1 - net.m // 2)
    swap = core_halves(net, k.grad_reduce, k.core_reduce)

    swap.wait()
    add_halves(net, k.grad_reduce, k.core_reduce, k.half_reduce)
    reduce_moves = along_z(net, k.half_reduce, k.z_reduce, chunk_of(net))

    k.stream.need(shortcut=1, w_reduce=1)

    def input_rows(at):
        total = k.shortcut[at, :]
        for b in range(4):
            total = total + mm_t(k.grad_reduced[at, b * 128 : b * 128 + 128], k.w_reduce[b])
        k.grad_input[at, :] = total

    each_rows(1536, 384, input_rows)
    k.stream.done(grad_input=1)
    for move_ in reduce_moves:
        move_.wait()
    k.sum_reduce[...] = finish_z(net, k.half_reduce, k.z_reduce, chunk_of(net)).astype(BF16)
    wait_reduce = to_owners(
        lambda i: k.sum_reduce.at[:, lanes_for(i)], k.own_reduce, k.local_sems.at[11]
    )
    for move_ in late_moves:
        move_.wait()
    k.sum_dilated[...] = finish_z(net, k.half_dilated, k.z_dilated)
    k.sum_expand[...] = finish_z(net, k.half_expand, k.z_expand)
    wait_pyramid()
    wait_project()
    wait_reduce()


def run_bottleneck_backward(args):
    return call_kernel(
        bottleneck_backward,
        "bottleneck_back",
        3,
        args,
        dict(
            grad_input=((1536, 512), F32),
            norm_2=((8, 128), F32),
            norm_1=((8, 128), F32),
            own_pyramid=((2, 16, 32, 256), BF16),
            own_project=((2, 32, 384), BF16),
            sum_dilated=((576, 128), F32),
            sum_expand=((64, 512), F32),
            own_reduce=((2, 64, 256), BF16),
        ),
        dict(
            grad_taps=pltpu.VMEM((2560, 384), BF16),
            grad_reduced=pltpu.VMEM((1536, 512), BF16),
            z_other=pltpu.VMEM((2, 16, 32, 512), BF16),
            z_last=pltpu.VMEM((16, 32, 512), BF16),
            relay=pltpu.VMEM((2, 2, 16, 32, 256), BF16),
            pyramid_sum=pltpu.VMEM((2, 16, 32, 256), BF16),
            sum_reduce=pltpu.VMEM((64, 512), BF16),
            grad_expand=pltpu.VMEM((8, 64, 512), BF16),
            core_expand=pltpu.VMEM((4, 64, 512), BF16),
            half_expand=pltpu.VMEM((4, 64, 512), BF16),
            z_expand=pltpu.VMEM((3, 64, 512), BF16),
            grad_reduce=pltpu.VMEM((8, 64, 512), BF16),
            core_reduce=pltpu.VMEM((4, 64, 512), BF16),
            half_reduce=pltpu.VMEM((4, 64, 512), BF16),
            z_reduce=pltpu.VMEM((3, 64, 512), BF16),
            grad_dilated=pltpu.VMEM((8, 576, 128), BF16),
            core_dilated=pltpu.VMEM((4, 576, 128), BF16),
            half_dilated=pltpu.VMEM((4, 576, 128), BF16),
            z_dilated=pltpu.VMEM((3, 576, 128), BF16),
            w_taps=pltpu.VMEM((3, 512, 384), BF16),
            part=pltpu.VMEM((4, 1536, 128), F32),
            **scatter_scratch("sum", 1536, 128),
            **scatter_scratch("sum2", 1536, 128),
            grad_2=pltpu.VMEM((1536, 128), F32),
            grad_1=pltpu.VMEM((1536, 128), F32),
            grad_pad=pltpu.VMEM((2560, 128), BF16),
            cells=pltpu.VMEM((20, 144, 128), F32),
            **exchange_scratch(2),
            **exchange_scratch(1),
            local_sems=pltpu.SemaphoreType.DMA((13,)),
        ),
        96,
        hbm=dict(w_dilated=1),
        stream=dict(z_pair=1, half_pyramid=1, hidden_two=1, dilated=1, mask=1, hidden=1, reduced=1, x=1, shortcut=1, w_reduce=1, grad_input=1),
    )


def finish(net, k):
    counted = pixel_count(k.boxes)
    odd = lax.rem(lax.axis_index("batch"), 2)

    def rows_for(i):
        return slice(i * 32, i * 32 + 32)

    nothing = jnp.zeros((64, 256), F32)
    for tap in (9, 10, 11, 15, 16, 17, 18, 19, 20, 24, 25, 26):
        k.grad_rates[tap] = nothing
    for slot in range(16):
        for i in range(2):
            block = k.own_pyramid[i, slot].astype(F32)
            if slot == 0:
                k.grad_point[rows_for(i), :] = block
            else:
                tap = slot - 1 if slot < 10 else slot + 2 if slot < 13 else slot + 8
                k.grad_rates[tap, rows_for(i), :] = block
    k.stream.done(grad_rates=1)
    k.stream.need(from_input=1)
    leave = pltpu.make_async_copy(k.from_input, k.grad_input, k.sem.at[0])
    leave.start()
    for y in range(6):
        turned = k.packed[y * 128 : y * 128 + 128, :].astype(F32).T.astype(BF16)
        k.features[y] = turned[0:64, :]
        k.features[y + 6] = turned[64:128, :]
    k.turned[...] = jnp.concatenate([k.own_project[i].astype(F32) for i in range(2)], axis=0).T
    for slot in range(5):
        start = pl.multiple_of(slot * 64 + odd * 32, 32)
        k.grad_project[slot] = k.turned[pl.ds(start, 32), :]
    k.grad_reduce[...] = jnp.concatenate(
        [k.own_reduce[i].astype(F32) for i in range(2)], axis=0
    ).T
    k.grad_dilated[...] = k.from_dilated[...].reshape(9, 64, 128)
    k.grad_expand[...] = k.from_expand[...]
    k.grad_pool[...] = k.from_pool[...]
    k.grad_norm_1[...] = k.norm_1[0:2, :]
    k.grad_norm_2[...] = k.norm_2[0:2, :]
    k.grad_norm_3[...] = k.norm_3[0:2, :]
    for b in range(4):
        k.grad_norm_b[:, b, :] = k.norm_b[0:2, b * 64 : b * 64 + 64]
    k.grad_norm_pool[...] = k.norm_pool[0:2, 0:64]
    k.grad_norm_p[...] = k.norm_p[0:2, 0:64]
    k.grad_head_weight[...] = k.head_sums[0:22, 0:256]
    columns = k.head_sums[:, 256:384].T
    k.grad_head_bias[...] = columns[0:1, 0:22]
    loss = columns[1:2, :]
    task = lax.broadcasted_iota(jnp.int32, (1, 32), 1)

    def total(inside):
        return jnp.sum(jnp.where(inside, loss, 0.0), axis=1, keepdims=True) / counted

    terms = [total(task == 0), total(task == 19), total((task == 20) | (task == 21))]
    lane = lax.broadcasted_iota(jnp.int32, (1, 128), 1)
    losses = jnp.where(lane == 0, terms[0], jnp.where(lane == 1, terms[1], terms[2]))
    log_vars = jnp.where(
        lane == 0, k.log_vars[0], jnp.where(lane == 1, k.log_vars[1], k.log_vars[2])
    )
    weighted = jnp.exp(-log_vars) * losses
    k.total_loss[...] = jnp.sum(
        jnp.where(lane < 3, weighted + log_vars, 0.0), axis=1, keepdims=True
    )
    k.grad_log_vars[...] = (1.0 - weighted)[:, 0:3]

    leave.wait()


def run_finish(args):
    return call_kernel(
        finish,
        "finish",
        None,
        args,
        dict(
            features=((12, 64, 128), BF16),
            total_loss=((1, 1), F32),
            grad_input=((1536, 512), F32),
            grad_reduce=((256, 128), F32),
            grad_dilated=((9, 64, 128), F32),
            grad_expand=((64, 512), F32),
            grad_norm_1=((2, 128), F32),
            grad_norm_2=((2, 128), F32),
            grad_norm_3=((2, 512), F32),
            grad_point=((64, 256), F32),
            grad_rates=((27, 64, 256), F32),
            grad_pool=((64, 256), F32),
            grad_norm_b=((2, 4, 64), F32),
            grad_norm_pool=((2, 64), F32),
            grad_project=((5, 32, 64), F32),
            grad_norm_p=((2, 64), F32),
            grad_head_weight=((22, 256), F32),
            grad_head_bias=((1, 22), F32),
            grad_log_vars=((1, 3), F32),
        ),
        dict(turned=pltpu.VMEM((384, 64), F32), sem=pltpu.SemaphoreType.DMA((1,))),
        0,
        hbm=dict(grad_input=1),
        stream=dict(from_input=1, grad_rates=1),
        smem=dict(boxes=1, log_vars=1),
    )


def fast_local(
    trunk_input,
    conv_reduce,
    conv_dilated,
    conv_expand,
    reduction_norm_params,
    dilated_norm_params,
    expansion_norm_params,
    aspp_point,
    aspp_rates,
    aspp_pool,
    branch_norms,
    pooling_norm_params,
    aspp_project,
    projection_norm_params,
    head_weight,
    head_bias,
    log_vars,
    crop_boxes,
    seg_labels,
    depth_target,
    normal_target,
):
    x = trunk_input.reshape(1536, 512)
    forward = run_bottleneck(
        dict(
            x=x,
            conv_reduce=conv_reduce,
            w_dilated=conv_dilated,
            w_expand=conv_expand,
            aspp_point=aspp_point,
            aspp_rates=aspp_rates,
            project=aspp_project.transpose(1, 0, 2),
            affine_1=reduction_norm_params,
            affine_2=dilated_norm_params,
            affine_3=expansion_norm_params,
            boxes=crop_boxes,
        )
    )
    middle = run_pyramid(
        dict(
            trunk=forward.trunk,
            mask=forward.mask,
            far_pyramid=forward.w_pyramid,
            branch_norms=branch_norms,
            norm_project=projection_norm_params,
            norm_pooling=pooling_norm_params,
            aspp_pool=aspp_pool,
            far_slots=forward.w_project,
            head_weight=head_weight.T,
            head_bias=head_bias,
            log_vars=log_vars,
            labels=seg_labels.transpose(1, 0, 2),
            depth=depth_target.transpose(1, 0, 2),
            normal=normal_target.transpose(0, 2, 1, 3).reshape(12, 2, 128),
            boxes=crop_boxes,
        )
    )
    back = run_pyramid_backward(
        dict(
            grad_branches=middle.grad_branches,
            w_pyramid=middle.w_pyramid.reshape(13, 256, 512),
            x=x,
            trunk=forward.trunk,
            expanded=forward.expanded,
            stats_3=forward.stats_3,
            affine_3=expansion_norm_params,
            mask=forward.mask,
            grad_pooled=middle.grad_pooled,
            grad_project=middle.grad_project,
            grad_pool=middle.grad_pool,
            boxes=crop_boxes,
        )
    )
    last = run_bottleneck_backward(
        dict(
            grad_expanded=back.grad_expanded,
            shortcut=back.shortcut,
            w_reduce=forward.w_reduce,
            half_pyramid=back.half_pyramid,
            z_pair=back.z_pair,
            sum_project=back.sum_project,
            x=x,
            hidden=forward.hidden,
            hidden_two=forward.hidden_two,
            w_expand=conv_expand,
            w_dilated=conv_dilated,
            dilated=forward.dilated,
            stats_2=forward.stats_2,
            affine_2=dilated_norm_params,
            reduced=forward.reduced,
            stats_1=forward.stats_1,
            affine_1=reduction_norm_params,
            mask=forward.mask,
            boxes=crop_boxes,
        )
    )
    done = run_finish(
        dict(
            from_input=last.grad_input,
            own_pyramid=last.own_pyramid,
            packed=middle.features,
            own_project=last.own_project,
            own_reduce=last.own_reduce,
            from_dilated=last.sum_dilated,
            from_expand=last.sum_expand,
            from_pool=back.sum_pool,
            norm_1=last.norm_1,
            norm_2=last.norm_2,
            norm_3=back.norm_3,
            norm_b=middle.norm_b,
            norm_pool=middle.norm_pool,
            norm_p=middle.norm_p,
            head_sums=middle.head_sums,
            log_vars=log_vars,
            boxes=crop_boxes,
        )
    )
    return (
        done.features.transpose(0, 2, 1).reshape(1, 12, 128, 64),
        done.total_loss.reshape(()),
        done.grad_input.reshape(1, 12, 128, 512),
        done.grad_reduce,
        done.grad_dilated.reshape(3, 3, 64, 128),
        done.grad_expand,
        done.grad_norm_1,
        done.grad_norm_2,
        done.grad_norm_3,
        done.grad_point,
        done.grad_rates.reshape(3, 3, 3, 64, 256),
        done.grad_pool,
        done.grad_norm_b,
        done.grad_norm_pool,
        done.grad_project.transpose(2, 0, 1),
        done.grad_norm_p,
        done.grad_head_weight.T,
        done.grad_head_bias.reshape(22),
        done.grad_log_vars.reshape(3),
    )


def local(
    trunk_input,
    conv_reduce,
    conv_dilated,
    conv_expand,
    reduction_norm_params,
    dilated_norm_params,
    expansion_norm_params,
    aspp_point,
    aspp_rates,
    aspp_pool,
    branch_norms,
    pooling_norm_params,
    aspp_project,
    projection_norm_params,
    head_weight,
    head_bias,
    log_vars,
    crop_boxes,
    seg_labels,
    depth_target,
    normal_target,
):
    image_inputs, tile_row_count, frame_columns, quarter = trunk_input.shape
    pixels = image_inputs * tile_row_count * frame_columns
    branch_part = aspp_point.shape[0]
    branch_total = lax.axis_size("branch")
    row_portion = 1.0 / lax.axis_size("rows")
    image_overall_count = float(crop_boxes.shape[0])
    first_image = lax.axis_index("batch") * image_inputs
    first_row = lax.axis_index("rows") * tile_row_count
    my_boxes = lax.dynamic_slice_in_dim(crop_boxes, first_image, image_inputs, 0)
    row_ids = first_row + jnp.arange(tile_row_count, dtype=jnp.int32)
    col_ids = jnp.arange(frame_columns, dtype=jnp.int32)
    inside_rows = (row_ids[None, :] >= my_boxes[:, 0:1]) & (
        row_ids[None, :] < my_boxes[:, 0:1] + my_boxes[:, 2:3]
    )
    inside_cols = (col_ids[None, :] >= my_boxes[:, 1:2]) & (
        col_ids[None, :] < my_boxes[:, 1:2] + my_boxes[:, 3:4]
    )
    valid_mask = (inside_rows[:, :, None] & inside_cols[:, None, :]).astype(jnp.float32)
    mask_column_vector = valid_mask.reshape(pixels, 1)
    mask_flat = valid_mask.reshape(pixels)
    pixel_number_count = jnp.sum((crop_boxes[:, 2] * crop_boxes[:, 3]).astype(jnp.float32))
    image_areas = (my_boxes[:, 2] * my_boxes[:, 3]).astype(jnp.float32)
    input_full = widen(trunk_input)
    reduced_output = forward_dot(input_full, conv_reduce).reshape(pixels, -1)
    normalized_first, standardized_first, inverse_deviation_first = norm_ahead_pass(
        reduced_output, mask_column_vector, pixel_number_count, reduction_norm_params
    )
    hidden_one = (
        jax.nn.silu(normalized_first)
        .astype(jnp.bfloat16)
        .reshape(image_inputs, tile_row_count, frame_columns, -1)
    )
    hidden_full = widen(pad_rows(hidden_one))
    dilated_out = 0.0
    for row_tap in range(3):
        band = hidden_full[:, 4 * row_tap : 4 * row_tap + tile_row_count]
        for col_tap in range(3):
            dilated_out = dilated_out + forward_dot(
                move(band, -(col_tap - 1) * 4, 2), conv_dilated[row_tap, col_tap]
            )
    normalized_second, standardized_second, inverse_deviation_second = norm_ahead_pass(
        dilated_out.reshape(pixels, -1), mask_column_vector, pixel_number_count, dilated_norm_params
    )
    hidden_two = (
        jax.nn.silu(normalized_second)
        .astype(jnp.bfloat16)
        .reshape(image_inputs, tile_row_count, frame_columns, -1)
    )
    hidden_two_full = widen(hidden_two)
    expanded_output = forward_dot(hidden_two_full, conv_expand).reshape(pixels, -1)
    normalized_third, standardized_third, inverse_deviation_third = norm_ahead_pass(
        expanded_output, mask_column_vector, pixel_number_count, expansion_norm_params
    )
    residual_sum = normalized_third + trunk_input.reshape(pixels, -1).astype(jnp.float32)
    trunk_out = (
        jax.nn.silu(residual_sum)
        .astype(jnp.bfloat16)
        .reshape(image_inputs, tile_row_count, frame_columns, quarter)
    )
    trunk_full = widen(trunk_out)
    branch_outs = [backward_dot(trunk_full, aspp_point)]
    for branch_id in range(3):
        dilation = RATES[branch_id]
        hops = dilation // tile_row_count
        partials = [0.0, 0.0, 0.0]
        for col_tap in range(3):
            shifted = move(trunk_full, -(col_tap - 1) * dilation, 2)
            products = backward_dot(shifted, stacked_taps(aspp_rates[branch_id], col_tap))
            for row_tap in range(3):
                partials[row_tap] = (
                    partials[row_tap]
                    + products[..., row_tap * branch_part : (row_tap + 1) * branch_part]
                )
        upper = send_down(partials[0].astype(jnp.bfloat16), hops).astype(jnp.float32)
        lower_part = send_up(partials[2].astype(jnp.bfloat16), hops).astype(jnp.float32)
        branch_outs.append(partials[1] + upper + lower_part)
    spatial_flattened = jnp.stack(branch_outs, axis=3).reshape(pixels, -1)
    branch_gain_bias = branch_norms.reshape(2, -1)
    normalized_spatial, standardized_spatial, inverse_deviation_spatial = norm_ahead_pass(
        spatial_flattened, mask_column_vector, pixel_number_count, branch_gain_bias
    )
    spatial_act = (
        jax.nn.silu(normalized_spatial)
        .astype(jnp.bfloat16)
        .reshape(image_inputs, tile_row_count, frame_columns, 4, branch_part)
    )
    pooled_local = lax.dot_general(
        valid_mask.astype(jnp.bfloat16),
        trunk_full,
        (((1, 2), (1, 2)), ((0,), (0,))),
        preferred_element_type=jnp.float32,
    )
    pooled = (over_rows(pooled_local) / image_areas[:, None]).astype(jnp.bfloat16)
    pooling_convolution = backward_dot(pooled, aspp_pool)
    normalized_poolbranch, standardized_poolbranch, inverse_deviation_poolbranch = norm_ahead_pass(
        pooling_convolution, row_portion, image_overall_count, pooling_norm_params
    )
    pool_act = jax.nn.silu(normalized_poolbranch).astype(jnp.bfloat16)
    pool_wide = jnp.broadcast_to(
        pool_act[:, None, None, None, :],
        (image_inputs, tile_row_count, frame_columns, 1, branch_part),
    )
    concat = jnp.concatenate([spatial_act, pool_wide], axis=3)
    concat_flat = widen(concat).reshape(pixels, -1)
    proj_kernel = (
        aspp_project.reshape(branch_part, 5, branch_total, branch_part)
        .transpose(0, 2, 1, 3)
        .reshape(branch_part, 5 * branch_total * branch_part)
    )
    projected_output = backward_dot(concat_flat, proj_kernel)
    normalized_projector, standardized_projector, inverse_deviation_projector = norm_ahead_pass(
        projected_output, mask_column_vector, pixel_number_count, projection_norm_params
    )
    features = (
        jax.nn.silu(normalized_projector)
        .astype(jnp.bfloat16)
        .reshape(image_inputs, tile_row_count, frame_columns, -1)
    )
    features_wide = widen(features).reshape(pixels, -1).astype(jnp.float32)
    head_wide = head_weight.astype(jnp.float32)
    logits = jnp.dot(features_wide, head_wide, precision=HIGH) + head_bias
    classes = head_bias.shape[0] - 3
    seg_logits = logits[:, :classes]
    labels_flat = seg_labels.reshape(pixels)
    classes_hot = (labels_flat[:, None] == jnp.arange(classes, dtype=jnp.int32)[None, :]).astype(
        jnp.float32
    )
    cross = jax.nn.logsumexp(seg_logits, axis=1) - jnp.sum(seg_logits * classes_hot, axis=1)
    depth_gap = logits[:, classes] - depth_target.reshape(pixels)
    smooth_abs = jnp.sqrt(depth_gap * depth_gap + 1.0)
    normal_gap = logits[:, classes + 1 :] - jnp.moveaxis(normal_target, 1, 3).reshape(pixels, 2)
    local_losses = jnp.stack(
        [
            jnp.sum(mask_flat * cross),
            jnp.sum(mask_flat * (smooth_abs - 1.0)),
            jnp.sum(mask_flat * jnp.sum(normal_gap * normal_gap, axis=1)),
        ]
    )
    task_weights = jnp.exp(-log_vars)
    grad_seg = (jax.nn.softmax(seg_logits, axis=1) - classes_hot) * (
        task_weights[0] / pixel_number_count * mask_flat
    )[:, None]
    grad_depth = depth_gap / smooth_abs * (task_weights[1] / pixel_number_count * mask_flat)
    grad_normal = 2.0 * normal_gap * (task_weights[2] / pixel_number_count * mask_flat)[:, None]
    grad_logits = jnp.concatenate([grad_seg, grad_depth[:, None], grad_normal], axis=1)
    head_local = lax.dot_general(
        features_wide, grad_logits, (((0,), (0,)), ((), ())), precision=HIGH
    )
    loss_parts, grad_head_weight, grad_head_bias = lax.psum(
        (local_losses, head_local, jnp.sum(grad_logits, axis=0)), ("rows", "batch")
    )
    task_losses = loss_parts / pixel_number_count
    total_loss = jnp.sum(task_weights * task_losses + log_vars)
    grad_log_vars = 1.0 - task_weights * task_losses
    grad_features = jnp.dot(grad_logits, head_wide.T, precision=HIGH)
    my_features_grad = lax.dynamic_slice_in_dim(
        grad_features, lax.axis_index("branch") * branch_part, branch_part, 1
    )
    gradient_before_projector = my_features_grad * silu_slope(normalized_projector)
    grad_proj_in, grad_project_norm = norm_reverse_pass(
        gradient_before_projector,
        standardized_projector,
        inverse_deviation_projector,
        1.0,
        mask_column_vector,
        pixel_number_count,
        projection_norm_params,
    )
    grad_proj_low = grad_proj_in.astype(jnp.bfloat16)
    proj_kernel_grad = lax.dot_general(
        grad_proj_low, concat_flat, (((0,), (0,)), ((), ())), preferred_element_type=jnp.float32
    )
    grad_project_local = (
        proj_kernel_grad.reshape(branch_part, branch_total, 5, branch_part)
        .transpose(0, 2, 1, 3)
        .reshape(branch_part, 5, branch_total * branch_part)
    )
    concat_grad = forward_dot(grad_proj_low, proj_kernel).reshape(
        image_inputs, tile_row_count, frame_columns, -1
    )
    concat_grad = narrow(concat_grad).reshape(pixels, 5, branch_part)
    pool_grad_img = over_rows(
        jnp.sum(concat_grad[:, 4, :].reshape(image_inputs, -1, branch_part), axis=1)
    )
    gradient_before_poolbranch = pool_grad_img * silu_slope(normalized_poolbranch)
    grad_pool_conv, grad_pool_norm = norm_reverse_pass(
        gradient_before_poolbranch,
        standardized_poolbranch,
        inverse_deviation_poolbranch,
        row_portion,
        1.0,
        image_overall_count,
        pooling_norm_params,
    )
    pool_conv_low = grad_pool_conv.astype(jnp.bfloat16)
    grad_pool_local = (
        lax.dot_general(
            pool_conv_low, pooled, (((0,), (0,)), ((), ())), preferred_element_type=jnp.float32
        )
        * row_portion
    )
    pooled_grad = forward_dot(pool_conv_low, aspp_pool)
    gradient_before_spatialbranch = concat_grad[:, :4, :].reshape(pixels, -1) * silu_slope(
        normalized_spatial
    )
    grad_spatial, branch_norm_grad = norm_reverse_pass(
        gradient_before_spatialbranch,
        standardized_spatial,
        inverse_deviation_spatial,
        1.0,
        mask_column_vector,
        pixel_number_count,
        branch_gain_bias,
    )
    grad_branch_norms = branch_norm_grad.reshape(2, 4, branch_part)
    spatial_low = grad_spatial.astype(jnp.bfloat16).reshape(
        image_inputs, tile_row_count, frame_columns, 4, branch_part
    )
    point_grad = spatial_low[:, :, :, 0]
    grad_point_local = pixel_dot(point_grad, trunk_full)
    trunk_grad = forward_dot(point_grad, aspp_point)
    trunk_grad = (
        trunk_grad + valid_mask[..., None] * (pooled_grad / image_areas[:, None])[:, None, None, :]
    )
    rate_grads = []
    for branch_id in range(3):
        dilation = RATES[branch_id]
        hops = dilation // tile_row_count
        centre = spatial_low[:, :, :, branch_id + 1]
        grad_taps = jnp.concatenate(
            [send_up(centre, hops), centre, send_down(centre, hops)], axis=3
        )
        per_col = []
        for col_tap in range(3):
            shifted = move(trunk_full, -(col_tap - 1) * dilation, 2)
            per_col.append(pixel_dot(grad_taps, shifted))
            tap_grad = forward_dot(grad_taps, stacked_taps(aspp_rates[branch_id], col_tap))
            trunk_grad = trunk_grad + move(tap_grad, (col_tap - 1) * dilation, 2)
        col_stack = jnp.stack(per_col, axis=0).reshape(3, 3, branch_part, -1)
        rate_grads.append(col_stack.transpose(1, 0, 2, 3))
    grad_rates_local = jnp.stack(rate_grads, axis=0)
    trunk_own = narrow(trunk_grad).reshape(pixels, -1)
    gradient_shortcut = trunk_own * silu_slope(residual_sum)
    grad_expanded, grad_norm_expand = norm_reverse_pass(
        gradient_shortcut,
        standardized_third,
        inverse_deviation_third,
        1.0,
        mask_column_vector,
        pixel_number_count,
        expansion_norm_params,
    )
    expanded_low = grad_expanded.astype(jnp.bfloat16).reshape(
        image_inputs, tile_row_count, frame_columns, -1
    )
    grad_expand_local = pixel_dot(hidden_two_full, expanded_low)
    hidden_two_grad = narrow(backward_dot(expanded_low, conv_expand)).reshape(pixels, -1)
    gradient_before_second = hidden_two_grad * silu_slope(normalized_second)
    gradient_dilated_input, gradient_dilated_norm = norm_reverse_pass(
        gradient_before_second,
        standardized_second,
        inverse_deviation_second,
        1.0,
        mask_column_vector,
        pixel_number_count,
        dilated_norm_params,
    )
    dilated_lowprec = gradient_dilated_input.astype(jnp.bfloat16).reshape(
        image_inputs, tile_row_count, frame_columns, -1
    )
    dilated_padded = pad_rows(dilated_lowprec)
    hidden_one_grad = 0.0
    kernel_grads = []
    for row_tap in range(3):
        band = hidden_full[:, 4 * row_tap : 4 * row_tap + tile_row_count]
        grad_band = dilated_padded[:, 8 - 4 * row_tap : 8 - 4 * row_tap + tile_row_count]
        for col_tap in range(3):
            kernel_grads.append(pixel_dot(move(band, -(col_tap - 1) * 4, 2), dilated_lowprec))
            hidden_one_grad = hidden_one_grad + backward_dot(
                move(grad_band, (col_tap - 1) * 4, 2), conv_dilated[row_tap, col_tap]
            )
    grad_dilated_local = jnp.stack(kernel_grads, axis=0).reshape(3, 3, hidden_full.shape[3], -1)
    hidden_one_own = narrow(hidden_one_grad).reshape(pixels, -1)
    gradient_before_first = hidden_one_own * silu_slope(normalized_first)
    grad_reduced, grad_norm_reduce = norm_reverse_pass(
        gradient_before_first,
        standardized_first,
        inverse_deviation_first,
        1.0,
        mask_column_vector,
        pixel_number_count,
        reduction_norm_params,
    )
    reduced_low = grad_reduced.astype(jnp.bfloat16).reshape(
        image_inputs, tile_row_count, frame_columns, -1
    )
    grad_reduce_local = pixel_dot(input_full, reduced_low)
    input_grad = narrow(backward_dot(reduced_low, conv_reduce))
    grad_input = input_grad + gradient_shortcut.reshape(
        image_inputs, tile_row_count, frame_columns, quarter
    )
    grad_reduce, grad_dilated, grad_expand, grad_point, grad_rates, grad_pool, grad_project = (
        lax.psum_scatter(grad_reduce_local, ("rows", "batch"), scatter_dimension=0, tiled=True),
        lax.psum_scatter(grad_dilated_local, ("rows", "batch"), scatter_dimension=2, tiled=True),
        lax.psum_scatter(grad_expand_local, ("rows", "batch"), scatter_dimension=0, tiled=True),
        lax.psum_scatter(grad_point_local, ("rows", "batch"), scatter_dimension=1, tiled=True),
        lax.psum_scatter(grad_rates_local, ("rows", "batch"), scatter_dimension=4, tiled=True),
        lax.psum_scatter(grad_pool_local, ("rows", "batch"), scatter_dimension=1, tiled=True),
        lax.psum_scatter(grad_project_local, ("rows", "batch"), scatter_dimension=2, tiled=True),
    )
    return (
        features,
        total_loss,
        grad_input,
        grad_reduce,
        grad_dilated,
        grad_expand,
        grad_norm_reduce,
        gradient_dilated_norm,
        grad_norm_expand,
        grad_point,
        grad_rates,
        grad_pool,
        grad_branch_norms,
        grad_pool_norm,
        grad_project,
        grad_project_norm,
        grad_head_weight,
        grad_head_bias,
        grad_log_vars,
    )


def solution(mesh):
    in_specs = (
        P("batch", "rows", None, "branch"),
        P(None, "branch"),
        P(None, None, None, "branch"),
        P(None, "branch"),
        P(None, "branch"),
        P(None, "branch"),
        P(None, "branch"),
        P("branch", None),
        P(None, None, None, "branch", None),
        P("branch", None),
        P(None, None, "branch"),
        P(None, "branch"),
        P("branch", None, None),
        P(None, "branch"),
        P(),
        P(),
        P(),
        P(),
        P("batch", "rows", None),
        P("batch", "rows", None),
        P("batch", None, "rows", None),
    )
    out_specs = (
        P("batch", "rows", None, "branch"),
        P(),
        P("batch", "rows", None, "branch"),
        P(("rows", "batch"), "branch"),
        P(None, None, ("rows", "batch"), "branch"),
        P(("rows", "batch"), "branch"),
        P(None, "branch"),
        P(None, "branch"),
        P(None, "branch"),
        P("branch", ("rows", "batch")),
        P(None, None, None, "branch", ("rows", "batch")),
        P("branch", ("rows", "batch")),
        P(None, None, "branch"),
        P(None, "branch"),
        P("branch", None, ("rows", "batch")),
        P(None, "branch"),
        P(),
        P(),
        P(),
    )
    small = (mesh.shape["branch"], mesh.shape["rows"], mesh.shape["batch"]) == (4, 2, 4)
    body = fast_local if small else local
    return jax.shard_map(body, mesh=mesh, in_specs=in_specs, out_specs=out_specs, check_vma=False)
```

```python
import types

import jax
import jax.numpy as jnp
from jax import lax
from jax.experimental import pallas as pl
from jax.experimental.pallas import tpu as pltpu
from jax.sharding import PartitionSpec as P

EPS = 1e-05
HIGH = lax.Precision.HIGHEST
RATES = (12, 24, 36)


def padded(cells, sides, width):
    for axis, dim in sides:
        count = lax.axis_size(axis)
        ends = count - 1
        head = lax.slice_in_dim(cells, 0, width, axis=dim)
        tail = lax.slice_in_dim(cells, cells.shape[dim] - width, cells.shape[dim], axis=dim)
        cells = jnp.concatenate(
            [
                lax.ppermute(tail, axis, [(i, (i + 1) % count) for i in range(ends)]),
                cells,
                lax.ppermute(head, axis, [((i + 1) % count, i) for i in range(ends)]),
            ],
            axis=dim,
        )
    return cells


def shifted_2(block, axis, distance):
    devices = range(lax.axis_size(axis))
    route = [(i - distance, i) for i in devices if i - distance in devices]
    return lax.ppermute(block, axis, route)


def move(tensor, offset, axis_id):
    length = tensor.shape[axis_id]
    if offset == 0:
        return tensor
    widths = [(0, 0)] * tensor.ndim
    if offset > 0:
        widths[axis_id] = (offset, 0)
        return lax.slice_in_dim(jnp.pad(tensor, widths), 0, length, axis=axis_id)
    widths[axis_id] = (0, -offset)
    return lax.slice_in_dim(jnp.pad(tensor, widths), -offset, length - offset, axis=axis_id)


def forward_dot(lhs_arr, rhs_arr):
    return jnp.dot(lhs_arr, rhs_arr, preferred_element_type=jnp.float32)


def backward_dot(grad_arr, kernel):
    return lax.dot_general(
        grad_arr,
        kernel,
        (((grad_arr.ndim - 1,), (1,)), ((), ())),
        preferred_element_type=jnp.float32,
    )


def pixel_dot(source, grad_arr):
    return lax.dot_general(
        source, grad_arr, (((0, 1, 2), (0, 1, 2)), ((), ())), preferred_element_type=jnp.float32
    )


def silu_slope(pre_act):
    sigmoid_v = jax.nn.sigmoid(pre_act)
    return sigmoid_v * (1.0 + pre_act * (1.0 - sigmoid_v))


def widen(tensor):
    return lax.all_gather(tensor, "branch", axis=3, tiled=True)


def narrow(tensor):
    return lax.psum_scatter(
        tensor.astype(jnp.bfloat16), "branch", scatter_dimension=3, tiled=True
    ).astype(jnp.float32)


def pad_rows(tensor):
    return padded(tensor, (("rows", 1),), 4)


def send_down(tensor, hops):
    if hops >= lax.axis_size("rows"):
        return jnp.zeros_like(tensor)
    return shifted_2(tensor, "rows", hops)


def send_up(tensor, hops):
    if hops >= lax.axis_size("rows"):
        return jnp.zeros_like(tensor)
    return shifted_2(tensor, "rows", -hops)


def over_rows(tensor):
    return lax.psum(tensor, "rows")


def norm_ahead_pass(tensor, weight, counted, affine):
    summed = lax.psum(jnp.sum(tensor * weight, axis=0), ("rows", "batch"))
    mean_val = summed / counted
    centered = tensor - mean_val
    spread = lax.psum(jnp.sum(weight * centered * centered, axis=0), ("rows", "batch"))
    variance = spread / counted
    inverse = lax.rsqrt(variance + EPS)
    normed = centered * inverse
    return (affine[0] * normed + affine[1], normed, inverse)


def norm_reverse_pass(grad_out, normed, inverse, weight_all, weight_stat, counted, affine):
    grad_bias, grad_gain = lax.psum(
        (jnp.sum(grad_out * weight_all, axis=0), jnp.sum(grad_out * normed * weight_all, axis=0)),
        ("rows", "batch"),
    )
    gain_row = affine[0]
    grad_in = inverse * (
        gain_row * grad_out - weight_stat / counted * gain_row * (grad_bias + normed * grad_gain)
    )
    return (grad_in, jnp.stack([grad_gain, grad_bias]))


def stacked_taps(kernels, col_tap):
    return jnp.concatenate([kernels[0, col_tap], kernels[1, col_tap], kernels[2, col_tap]], axis=0)


MESH = pl.DeviceIdType.MESH
F32 = jnp.float32
BF16 = jnp.bfloat16
VMEM_LIMIT = 60 * 2**20


class Net:
    def __init__(self, send_sems, recv_sems):
        self.m = lax.axis_index("branch")
        self.r = lax.axis_index("rows")
        self.z = lax.axis_index("batch")
        self.send_sems, self.recv_sems, self.count = send_sems, recv_sems, 0
        self.side = (self.m ^ 1, self.r, self.z)
        self.over = (self.m ^ 2, self.r, self.z)
        self.diagonal = (self.m ^ 3, self.r, self.z)
        self.core = (self.m, 1 - self.r, self.z)
        self.slot = self.r * 4 + self.z
        self.group = [
            (self.m, lax.rem(self.r + i, 2), lax.rem(self.z + j, 4))
            for i in range(2)
            for j in range(4)
            if i or j
        ]

    def send(self, src, dst, device):
        i = self.count
        self.count += 1
        copy = pltpu.make_async_remote_copy(
            src_ref=src,
            dst_ref=dst,
            send_sem=self.send_sems.at[i],
            recv_sem=self.recv_sems.at[i],
            device_id=device,
            device_id_type=MESH,
        )
        copy.start()
        return copy


def greet(peers, perhaps=()):
    barrier = pltpu.get_barrier_semaphore()
    for peer in peers:
        pl.semaphore_signal(barrier, inc=1, device_id=peer, device_id_type=MESH)
    awaited = len(peers)
    for peer, there in perhaps:

        @pl.when(there)
        def _(peer=peer):
            pl.semaphore_signal(barrier, inc=1, device_id=peer, device_id_type=MESH)

        awaited = awaited + there.astype(jnp.int32)
    pl.semaphore_wait(barrier, awaited)


def each_rows(total, step, body):
    def run(i, carry):
        body(pl.ds(pl.multiple_of(i * step, step), step))
        return carry

    lax.fori_loop(0, total // step, run, 0, unroll=2)


def lane_block(index, width=128):
    return pl.ds(pl.multiple_of(index * width, width), width)


def wide(tile, width):
    count = width // tile.shape[1]
    return tile if count == 1 else jnp.concatenate([tile] * count, axis=1)


def column_sums(fn, total, width, number):
    step = 32768 // width

    def run(i, sums):
        terms = fn(pl.ds(pl.multiple_of(i * step, step), step))
        return tuple(
            s + jnp.sum(t.reshape(step // 8, 8, width), axis=0) for s, t in zip(sums, terms)
        )

    sums = lax.fori_loop(
        0, total // step, run, tuple(jnp.zeros((8, width), F32) for _ in range(number)),
        unroll=2,
    )
    return [jnp.sum(s, axis=0, keepdims=True) for s in sums]


def fold(row):
    return row + pltpu.roll(wide(row, 128), 64, 1)


def exchange(net, outgoing, incoming, meanwhile=None):
    copies = [net.send(outgoing, incoming.at[net.slot], peer) for peer in net.group]
    incoming[net.slot] = outgoing[...]
    if meanwhile is not None:
        meanwhile()
    for copy in copies:
        copy.wait()


def pack(outgoing, first, second, extra=None):
    for i in range(first.shape[1] // 128):
        outgoing[2 * i : 2 * i + 1, :] = first[:, i * 128 : i * 128 + 128]
        outgoing[2 * i + 1 : 2 * i + 2, :] = second[:, i * 128 : i * 128 + 128]
    if extra is not None:
        outgoing[4:5, :] = extra


def unpack(incoming, width):
    count = width // 128
    firsts = [incoming[:, 2 * i, :] for i in range(count)]
    seconds = [incoming[:, 2 * i + 1, :] for i in range(count)]
    return jnp.concatenate(firsts, axis=1), jnp.concatenate(seconds, axis=1)


def statistics(
    net,
    value_ref,
    mask_ref,
    counts,
    outgoing,
    incoming,
    counted,
    folded=False,
    extra=None,
    meanwhile=None,
):
    total, width = value_ref.shape
    same = fold if folded else (lambda row: row)
    (first,) = column_sums(
        lambda at: (value_ref[at, :] * wide(mask_ref[at, :], width),), total, width, 1
    )
    first = same(first)
    own = jnp.sum(jnp.where(lax.broadcasted_iota(jnp.int32, (8, 128), 0) == net.slot, counts, 0.0), axis=0, keepdims=True)
    centre = first / jnp.maximum(wide(own, width), 1.0)

    def squares(at):
        gap = value_ref[at, :] - centre
        return (gap * gap * wide(mask_ref[at, :], width),)

    second = same(column_sums(squares, total, width, 1)[0])
    pack(outgoing, first, second, extra)
    exchange(net, outgoing, incoming, meanwhile)
    firsts, seconds = unpack(incoming, width)
    numbers = wide(counts, width)
    mean = jnp.sum(firsts, axis=0, keepdims=True) / counted
    drift = firsts / jnp.maximum(numbers, 1.0) - mean
    variance = jnp.sum(seconds + numbers * drift * drift, axis=0, keepdims=True) / counted
    return mean, lax.rsqrt(variance + EPS)


def gather_blocks(net, part, rows, meanwhile=None):
    pieces, size = 4, rows // 4
    own, side, over = net.m, net.m ^ 1, net.m ^ 2

    def at(i):
        return pl.ds(i * size, size)

    to_side, to_over = [], []
    for i in range(pieces):
        j = pieces - 1 - i
        to_side.append(net.send(part(own, at(i)), part(own, at(i)), net.side))
        to_over.append(net.send(part(own, at(j)), part(own, at(j)), net.over))
    passed = []
    for i in range(pieces):
        j = pieces - 1 - i
        to_side[i].wait_recv()
        if i < pieces // 2:
            passed.append(net.send(part(side, at(i)), part(side, at(i)), net.over))
        to_over[i].wait_recv()
        if i < pieces // 2:
            passed.append(net.send(part(over, at(j)), part(over, at(j)), net.side))
    if meanwhile is not None:
        meanwhile()
    for copy in to_side + to_over:
        copy.wait_send()
    for copy in passed:
        copy.wait()


def sum_scatter(net, part, bufs, out, meanwhile=None, produce=None):
    far, to_side, to_over, far_side, far_over, from_side, from_over = bufs
    rows, width = out.shape
    half, step = rows // 2, 16384 // width
    head, tail = pl.ds(0, half), pl.ds(half, half)
    across, side, over = net.m ^ 3, net.m ^ 1, net.m ^ 2

    def fill(target, index, base, count=half):
        size = min(step, count) if count % step == 0 else 64

        def body(at):
            rows_at = pl.ds(pl.multiple_of(at.start + base, size), size)
            target[rows_at, :] = part[index, rows_at, :].astype(BF16)

        each_rows(count, size, body)

    def combine(target, index, base, arrived):
        def body(at):
            rows_at = pl.ds(pl.multiple_of(at.start + base, step), step)
            target[rows_at, :] = (part[index, rows_at, :] + arrived[at, :].astype(F32)).astype(BF16)

        each_rows(half, step, body)

    quarter, first, second = half // 2, [], []
    for i in range(2):
        if produce is not None:
            produce(i)
        at = pl.ds(i * quarter, quarter)
        fill(far, across, i * quarter, quarter)
        first.append(net.send(far.at[at], far_side.at[at], net.side))
        fill(far, across, half + i * quarter, quarter)
        below = pl.ds(half + i * quarter, quarter)
        second.append(net.send(far.at[below], far_over.at[at], net.over))
    fill(to_side, side, 0)
    third = net.send(to_side.at[head], from_side.at[head], net.side)
    fill(to_over, over, half)
    fourth = net.send(to_over.at[tail], from_over.at[tail], net.over)
    for copy in second:
        copy.wait_recv()
    combine(to_side, side, half, far_over)
    fifth = net.send(to_side.at[tail], from_side.at[tail], net.side)
    for copy in first:
        copy.wait_recv()
    combine(to_over, over, 0, far_side)
    sixth = net.send(to_over.at[head], from_over.at[head], net.over)
    if meanwhile is not None:
        meanwhile()
    for copy in (third, fourth, fifth, sixth):
        copy.wait_recv()

    def body(at):
        out[at, :] = (
            part[net.m, at, :] + from_side[at, :].astype(F32) + from_over[at, :].astype(F32)
        )

    each_rows(rows, step, body)
    for copy in (*first, *second, third, fourth, fifth, sixth):
        copy.wait_send()


def gradient_sums(
    net, grad_ref, normed, outgoing, incoming, folded=False, extra=None, meanwhile=None
):
    total, width = grad_ref.shape
    same = fold if folded else (lambda row: row)
    bias, gain = column_sums(
        lambda at: (grad_ref[at, :], grad_ref[at, :] * normed(at)), total, width, 2
    )
    pack(outgoing, same(bias), same(gain), extra)
    exchange(net, outgoing, incoming, meanwhile)
    biases, gains = unpack(incoming, width)
    return jnp.sum(biases, axis=0, keepdims=True), jnp.sum(gains, axis=0, keepdims=True)


def keep_rows(ref, first, second):
    width = ref.shape[1]
    ref[0:1, :] = first
    ref[1:2, :] = second
    ref[2:8, :] = jnp.zeros((6, width), F32)


def pair(a, b):
    low = lax.broadcasted_iota(jnp.int32, (a.shape[0], 128), 1) < 64
    results = []
    for g in range(2):
        left, right = a[:, g * 128 : g * 128 + 128], b[:, g * 128 : g * 128 + 128]
        results.append(jnp.where(low, left, pltpu.roll(right, 64, 1)))
        results.append(jnp.where(low, pltpu.roll(left, 64, 1), right))
    return results


def unpair(blocks):
    low = lax.broadcasted_iota(jnp.int32, blocks[0].shape, 1) < 64
    firsts, seconds = [], []
    for g in range(2):
        left, right = blocks[2 * g], blocks[2 * g + 1]
        firsts.append(jnp.where(low, left, pltpu.roll(right, 64, 1)))
        seconds.append(jnp.where(low, pltpu.roll(left, 64, 1), right))
    return jnp.concatenate(firsts, axis=1), jnp.concatenate(seconds, axis=1)


def split_three(row):
    high = row.astype(BF16)
    rest = row - high.astype(F32)
    middle = rest.astype(BF16)
    low = (rest - middle.astype(F32)).astype(BF16)
    return high, middle, low


def zero_margins(ref, side, width):
    rows, _, lanes = ref.shape
    ref[:, 0:side, :] = jnp.zeros((rows, side, lanes), F32)
    ref[:, side + width : 2 * side + width, :] = jnp.zeros((rows, side, lanes), F32)


def scatter_buffers(rows, width):
    whole, half = pltpu.VMEM((rows, width), BF16), pltpu.VMEM((rows // 2, width), BF16)
    return [whole, whole, whole, half, half, whole, whole]


def sigmoid(u):
    return 0.5 * jnp.tanh(0.5 * u) + 0.5


def slope(u):
    s = sigmoid(u)
    return s * (1.0 + u * (1.0 - s))


def mm(a, b):
    return jnp.dot(a, b, preferred_element_type=F32)


def mm_t(a, b):
    return lax.dot_general(a, b, (((1,), (1,)), ((), ())), preferred_element_type=F32)


def tm_m(a, b):
    return lax.dot_general(a, b, (((0,), (0,)), ((), ())), preferred_element_type=F32)


class Streams:
    def __init__(self, ins, outs, sems):
        self.ins = {n: pltpu.make_async_copy(*pair, sems.at[i]) for i, (n, pair) in enumerate(ins)}
        self.outs = {
            n: pltpu.make_async_copy(*pair, sems.at[len(ins) + i])
            for i, (n, pair) in enumerate(outs)
        }
        self.left = []
        for copy in self.ins.values():
            copy.start()

    def need(self, **names):
        for name in names:
            self.ins.pop(name).wait()

    def done(self, **names):
        for name in names:
            copy = self.outs.pop(name)
            copy.start()
            self.left.append(copy)

    def finish(self):
        self.need(**dict.fromkeys(self.ins))
        self.done(**dict.fromkeys(self.outs))
        for copy in self.left:
            copy.wait()


def call_kernel(
    body, name, number, args, outs, scratch, sems, hbm={}, smem=dict(boxes=1), stream={}
):
    vmem, anywhere = pl.BlockSpec(memory_space=pltpu.VMEM), pl.BlockSpec(memory_space=pl.ANY)
    stream_in = [n for n in args if n in stream]
    stream_out = [n for n in outs if n in stream]
    buffers = {n: pltpu.VMEM(args[n].shape, args[n].dtype) for n in stream_in}
    buffers.update({n: pltpu.VMEM(*outs[n]) for n in stream_out})
    names = [f"far_{n}" if n in stream else n for n in [*args, *outs]]
    names = [*names, *scratch, *buffers, "stream_sems"]
    places = {name: anywhere for name in [*hbm, *stream]}
    places.update({name: pl.BlockSpec(memory_space=pltpu.SMEM) for name in smem})

    def kernel(*refs):
        k = types.SimpleNamespace(**dict(zip(names, refs)))
        held = vars(k)
        k.stream = Streams(
            [(n, (held[f"far_{n}"], held[n])) for n in stream_in],
            [(n, (held[n], held[f"far_{n}"])) for n in stream_out],
            k.stream_sems,
        )
        body(Net(refs[-2], refs[-1]) if sems else None, k)
        k.stream.finish()

    results = pl.pallas_call(
        kernel,
        out_shape=[jax.ShapeDtypeStruct(s, d) for s, d in outs.values()],
        in_specs=[places.get(name, vmem) for name in args],
        out_specs=[places.get(name, vmem) for name in outs],
        scratch_shapes=[
            *scratch.values(),
            *buffers.values(),
            pltpu.SemaphoreType.DMA((max(len(buffers), 1),)),
            *([pltpu.SemaphoreType.DMA((sems,))] * (2 if sems else 0)),
        ],
        name=name,
        compiler_params=pltpu.CompilerParams(
            collective_id=number, has_side_effects=bool(sems), vmem_limit_bytes=VMEM_LIMIT
        ),
    )(*args.values())
    return types.SimpleNamespace(**dict(zip(outs, results)))


def pixel_count(boxes):
    total = boxes[0, 2] * boxes[0, 3]
    for b in range(1, 4):
        total = total + boxes[b, 2] * boxes[b, 3]
    return total.astype(F32)


def tile_counts(net, boxes):
    slot = lax.broadcasted_iota(jnp.int32, (8, 128), 0)
    result = jnp.zeros((8, 128), F32)
    for s in range(8):
        top, height, width = boxes[s % 4, 0], boxes[s % 4, 2], boxes[s % 4, 3]
        first, last = (s // 4) * 12, (s // 4) * 12 + 12
        rows = jnp.minimum(top + height, last) - jnp.maximum(top, first)
        result = jnp.where(slot == s, (jnp.maximum(rows, 0) * width).astype(F32), result)
    return result


def exchange_scratch(label):
    return {
        f"out_{label}": pltpu.VMEM((8, 128), F32),
        f"in_{label}": pltpu.VMEM((8, 8, 128), F32),
    }


def scatter_scratch(label, rows, width):
    return {f"{label}_{i}": b for i, b in enumerate(scatter_buffers(rows, width))}


def scatter_refs(k, label):
    return [getattr(k, f"{label}_{i}") for i in range(7)]


def load_taps(k):
    loads = []
    for i in range(3):
        for j in range(3):
            loads.append(
                pltpu.make_async_copy(
                    k.w_dilated.at[i, j],
                    k.w_taps.at[i, :, pl.ds(j * 128, 128)],
                    k.local_sems.at[i * 3 + j],
                )
            )
            loads[-1].start()
    return loads


def send_halo(net, padded):
    lanes = padded.shape[1]
    padded[pl.ds(pl.multiple_of(net.r * 2048, 128), 512), :] = jnp.zeros((512, lanes), BF16)
    return net.send(
        padded.at[pl.ds(pl.multiple_of(1536 - net.r * 1024, 128), 512)],
        padded.at[pl.ds(pl.multiple_of(net.r * 2048, 128), 512)],
        net.core,
    )


def bottleneck_forward(net, k):
    counted, counts = pixel_count(k.boxes), tile_counts(net, k.boxes)
    loads = load_taps(k)
    own_reduce = pltpu.make_async_copy(
        k.conv_reduce.at[lane_block(net.m, 512)], k.w_reduce.at[net.m], k.local_sems.at[9]
    )
    own_reduce.start()
    greet([net.side, net.over, net.diagonal] + net.group)
    branches = [(net.m ^ 3, net.diagonal), (net.m ^ 1, net.side), (net.m ^ 2, net.over)]
    arrivals = [
        net.send(k.conv_reduce.at[lane_block(b, 512)], k.w_reduce.at[net.m], peer)
        for b, peer in branches
    ]

    top, left_edge = k.boxes[net.z, 0], k.boxes[net.z, 1]
    bottom, right_edge = top + k.boxes[net.z, 2], left_edge + k.boxes[net.z, 3]
    column = lax.broadcasted_iota(jnp.int32, (128, 128), 0)
    column_inside = jnp.where((column >= left_edge) & (column < right_edge), 1.0, 0.0)

    def mask_rows(i, carry):
        row = jnp.full((128, 128), net.r * 12 + i, jnp.int32)
        inside = jnp.where((row >= top) & (row < bottom), column_inside, 0.0)
        k.mask[pl.ds(pl.multiple_of(i * 128, 128), 128), :] = inside
        return carry

    lax.fori_loop(0, 12, mask_rows, 0, unroll=2)
    k.stream.done(mask=1)
    k.stream.need(x=1)

    def reduce_for(b):
        def reduce_rows(at):
            k.part[b, at, :] = mm(k.x[at, :], k.w_reduce[b])

        each_rows(1536, 384, reduce_rows)

    own_reduce.wait()
    reduce_for(net.m)
    arrivals[1].wait()
    reduce_for(net.m ^ 1)
    arrivals[2].wait()
    reduce_for(net.m ^ 2)
    arrivals[0].wait()
    k.stream.done(w_reduce=1)

    def far_half(half):
        for i in (half, half + 2):
            at = pl.ds(i * 384, 384)
            k.part[net.m ^ 3, at, :] = mm(k.x[at, :], k.w_reduce[net.m ^ 3])

    sum_scatter(net, k.part, scatter_refs(k, "sum"), k.reduced, produce=far_half)
    k.stream.done(reduced=1)

    half = pl.ds(pl.multiple_of(net.r * 32, 32), 32)
    late = []

    def weight_block(kind, b):
        lanes = lane_block(b, 512)
        if kind == "edge":
            return k.aspp_rates.at[0, 2 * net.r, :, :, lanes], k.w_pyramid.at[pl.ds(10, 3), net.m]
        if kind == "point":
            return k.aspp_point.at[half, lanes], k.w_pyramid.at[0, net.m, half]
        if kind == "project":
            return k.project.at[:, half], k.w_project.at[net.m, :, half]
        return (
            k.aspp_rates.at[kind, 1, :, half, lanes],
            k.w_pyramid.at[pl.ds(1 + 3 * kind, 3), net.m, half],
        )

    def spread_weights(*kinds):
        for kind in kinds:
            src, dst = weight_block(kind, net.m)
            late.append(pltpu.make_async_copy(src, dst, k.local_sems.at[10 + len(late) // 4]))
            late[-1].start()
            for b, peer in branches:
                src, dst = weight_block(kind, b)
                late.append(net.send(src, dst, peer))

    spread_weights("edge")
    mean, inverse = statistics(net, k.reduced, k.mask, counts, k.out_1, k.in_1, counted)
    keep_rows(k.stats_1, mean, inverse)

    def activate_1(at):
        u = k.affine_1[0:1, :] * ((k.reduced[at, :] - mean) * inverse) + k.affine_1[1:2, :]
        rows_at = pl.ds(pl.multiple_of(at.start + 512, 128), 128)
        k.hidden[rows_at, lane_block(net.m)] = (u * sigmoid(u)).astype(BF16)

    each_rows(1536, 128, activate_1)
    gather_blocks(
        net, lambda b, at: k.hidden.at[pl.ds(at.start + 512, at.size), lane_block(b)], 1536
    )
    halo = send_halo(net, k.hidden)
    spread_weights("project", "point", 0)
    zero_margins(k.left, 8, 128)
    zero_margins(k.right, 8, 128)
    for load in loads:
        load.wait()
    halo.wait()
    k.stream.done(hidden=1)

    def dilated_rows(i, carry):
        total = 0.0
        for tap in range(3):
            rows_at = pl.ds(pl.multiple_of((i * 3 + 4 * tap) * 128, 128), 384)
            total = total + mm(k.hidden[rows_at, :], k.w_taps[tap])
        k.dilated[pl.ds(pl.multiple_of(i * 384, 128), 384), :] = total[:, 128:256]
        k.left[pl.ds(i * 3, 3), 8:136, :] = total[:, 0:128].reshape(3, 128, 128)
        k.right[pl.ds(i * 3, 3), 8:136, :] = total[:, 256:384].reshape(3, 128, 128)
        return carry

    lax.fori_loop(0, 4, dilated_rows, 0)

    def add_columns(i, carry):
        at = pl.ds(pl.multiple_of(i * 128, 128), 128)
        k.dilated[at, :] = k.dilated[at, :] + k.left[i, 4:132, :] + k.right[i, 12:140, :]
        return carry

    lax.fori_loop(0, 12, add_columns, 0, unroll=2)
    k.stream.done(dilated=1)
    mean_2, inverse_2 = statistics(net, k.dilated, k.mask, counts, k.out_2, k.in_2, counted)
    keep_rows(k.stats_2, mean_2, inverse_2)

    def activate_2(at):
        u = k.affine_2[0:1, :] * ((k.dilated[at, :] - mean_2) * inverse_2) + k.affine_2[1:2, :]
        k.hidden_two[at, lane_block(net.m)] = (u * sigmoid(u)).astype(BF16)

    each_rows(1536, 128, activate_2)
    gather_blocks(net, lambda b, at: k.hidden_two.at[at, lane_block(b)], 1536)
    spread_weights(1, 2)
    k.stream.done(hidden_two=1)
    k.stream.need(w_expand=1)

    def expand_rows(at):
        k.expanded[at, :] = mm(k.hidden_two[at, :], k.w_expand[...])

    each_rows(1536, 384, expand_rows)
    k.stream.done(expanded=1)
    mean_3, inverse_3 = statistics(net, k.expanded, k.mask, counts, k.out_3, k.in_3, counted)
    keep_rows(k.stats_3, mean_3, inverse_3)
    def activate_3(at):
        u = k.affine_3[0:1, :] * ((k.expanded[at, :] - mean_3) * inverse_3) + k.affine_3[1:2, :]
        u = u + k.x[at, :].astype(F32)
        k.trunk[at, :] = (u * sigmoid(u)).astype(BF16)

    each_rows(1536, 64, activate_3)
    for copy in late:
        copy.wait()


def run_bottleneck(args):
    return call_kernel(
        bottleneck_forward,
        "bottleneck",
        0,
        args,
        dict(
            mask=((1536, 128), F32),
            w_reduce=((4, 512, 128), BF16),
            w_pyramid=((13, 4, 64, 512), BF16),
            w_project=((4, 5, 64, 256), BF16),
            reduced=((1536, 128), F32),
            stats_1=((8, 128), F32),
            hidden=((2560, 512), BF16),
            dilated=((1536, 128), F32),
            stats_2=((8, 128), F32),
            hidden_two=((1536, 512), BF16),
            expanded=((1536, 512), F32),
            stats_3=((8, 512), F32),
            trunk=((1536, 512), BF16),
        ),
        dict(
            w_taps=pltpu.VMEM((3, 512, 384), BF16),
            part=pltpu.VMEM((4, 1536, 128), F32),
            **scatter_scratch("sum", 1536, 128),
            left=pltpu.VMEM((12, 144, 128), F32),
            right=pltpu.VMEM((12, 144, 128), F32),
            **exchange_scratch(1),
            **exchange_scratch(2),
            **exchange_scratch(3),
            local_sems=pltpu.SemaphoreType.DMA((16,)),
        ),
        96,
        hbm=dict(conv_reduce=1, w_dilated=1, aspp_point=1, aspp_rates=1, project=1, w_pyramid=1, w_project=1),
        stream=dict(x=1, w_expand=1, mask=1, w_reduce=1, reduced=1, hidden=1, dilated=1, hidden_two=1, expanded=1),
    )


def pyramid_forward(net, k):
    counted, counts = pixel_count(k.boxes), tile_counts(net, k.boxes)
    area = (k.boxes[net.z, 2] * k.boxes[net.z, 3]).astype(F32)
    near = [
        (lax.rem(net.m + a, 4), lax.rem(net.r + b, 2), net.z)
        for a in range(4)
        for b in range(2)
        if a or b
    ]
    own_rows = pl.ds(pl.multiple_of(net.r * 32, 32), 32)
    common = (pl.ds(0, 10), slice(None), own_rows)
    every = (slice(None), slice(None), own_rows)
    weight_copies = [
        pltpu.make_async_copy(source.at[view], target.at[view], k.local_sems.at[i])
        for i, (source, target, view) in enumerate(
            (
                (k.far_pyramid, k.w_pyramid, common),
                (k.far_pyramid, k.w_pyramid, pl.ds(10, 3)),
                (k.far_slots, k.w_slots, every),
            )
        )
    ]
    for copy in weight_copies:
        copy.start()
    greet(net.group + [peer for i, peer in enumerate(near) if i])
    weight_copies.append(net.send(k.far_pyramid.at[common], k.w_pyramid.at[common], net.core))
    weight_copies.append(net.send(k.far_slots.at[every], k.w_slots.at[every], net.core))

    for b in range(4):
        k.affine_b[0:2, b * 64 : b * 64 + 64] = k.branch_norms[:, b, :]
    for i in range(2):
        k.affine_p[0:2, i * 64 : i * 64 + 64] = k.norm_project[...]
        k.affine_p[2:4, i * 64 : i * 64 + 64] = k.norm_pooling[...]
    k.head_rows[...] = jnp.zeros((32, 256), F32)
    k.head_rows[0:22, :] = k.head_weight[...].astype(F32)

    k.stream.need(mask=1)

    (own_sum,) = column_sums(
        lambda at: (k.trunk[at, :].astype(F32) * wide(k.mask[at, :], 512),), 1536, 512, 1
    )
    k.out_pool[...] = jnp.broadcast_to(own_sum, (8, 512))
    place = net.m * 2 + net.r
    pool_copies = [net.send(k.out_pool, k.in_pool.at[place], peer) for peer in near]
    k.in_pool[place] = k.out_pool[...]

    zero_margins(k.cells, 40, 128)

    def fill(i, carry):
        at = pl.ds(pl.multiple_of(i * 128, 128), 128)
        k.cells[i, 40:168, :] = k.trunk[at, :].astype(F32)
        return carry

    lax.fori_loop(0, 12, fill, 0, unroll=2)

    def shifted(i, offset):
        cells = k.cells[pl.ds(i * 3, 3), 40 + offset : 168 + offset, :]
        return cells.reshape(384, 512).astype(BF16)

    def rows_of(i):
        return pl.ds(pl.multiple_of(i * 384, 128), 384)

    def edge_rows(i, carry):
        total = 0.0
        for j in range(3):
            total = total + mm_t(shifted(i, 12 * (j - 1)), k.w_pyramid[10 + j].reshape(256, 512))
        k.edge_out[rows_of(i), :] = total.astype(BF16)
        return carry

    weight_copies.pop(1).wait()
    lax.fori_loop(0, 4, edge_rows, 0)
    edge = net.send(k.edge_out, k.edge_in, net.core)

    def outer_rows(i, carry):
        second, third = 0.0, 0.0
        for j in range(3):
            second = second + mm_t(shifted(i, 24 * (j - 1)), k.w_pyramid[4 + j].reshape(256, 512))
        for j in range(3):
            third = third + mm_t(shifted(i, 36 * (j - 1)), k.w_pyramid[7 + j].reshape(256, 512))
        for b, block in enumerate(pair(second, third)):
            k.part[b, rows_of(i), 128:256] = block
        return carry

    def inner_rows(i, carry):
        point = mm_t(k.trunk[rows_of(i), :], k.w_pyramid[0].reshape(256, 512))
        first = k.edge_in[rows_of(i), :].astype(F32)
        for j in range(3):
            first = first + mm_t(shifted(i, 12 * (j - 1)), k.w_pyramid[1 + j].reshape(256, 512))
        for b, block in enumerate(pair(point, first)):
            k.part[b, rows_of(i), 0:128] = block
        return carry

    def alternate(body, half):
        def run(i, carry):
            return body(half + 2 * i, carry)

        lax.fori_loop(0, 2, run, 0)

    def half_tile(half):
        alternate(outer_rows, half)
        if half == 0:
            edge.wait()
        alternate(inner_rows, half)

    for copy in weight_copies:
        copy.wait()
    k.stream.done(w_pyramid=1)

    sum_scatter(net, k.part, scatter_refs(k, "sum"), k.branches, produce=half_tile)

    low_256 = lax.broadcasted_iota(jnp.int32, (256, 128), 1) < 64
    odd = lax.rem(net.m, 2) == 1

    def slot(s):
        lanes = lane_block(net.m // 2)
        block = jnp.concatenate([k.w_slots[b, s, :, lanes] for b in range(4)], axis=0).astype(F32)
        return jnp.where(odd, pltpu.roll(block, 64, 1), block)

    for s in range(0, 4, 2):
        both = jnp.where(low_256, slot(s), pltpu.roll(slot(s + 1), 64, 1))
        k.w_project[:, s * 64 : s * 64 + 128] = both.astype(BF16)
    k.w_slot[...] = jnp.where(low_256, slot(4), 0.0).astype(BF16)
    k.w_pool[0:64, :] = k.aspp_pool[...]
    k.w_pool[64:128, :] = k.aspp_pool[...]

    for copy in pool_copies:
        copy.wait()
    for b in range(4):
        pooled = (k.in_pool[2 * b, 0:1, :] + k.in_pool[2 * b + 1, 0:1, :]) / area
        k.pooled[:, b * 512 : b * 512 + 512] = jnp.broadcast_to(pooled, (16, 512)).astype(BF16)
    pool_conv = mm_t(k.pooled[...], k.w_pool[...])[0:1, :]
    mean, inverse = statistics(
        net, k.branches, k.mask, counts, k.out_1, k.in_1, counted, extra=pool_conv
    )
    every = k.in_1[0:4, 4, :]
    pool_mean = jnp.sum(every, axis=0, keepdims=True) / 4.0
    pool_gap = every - pool_mean
    pool_inverse = lax.rsqrt(jnp.sum(pool_gap * pool_gap, axis=0, keepdims=True) / 4.0 + EPS)
    pool_normed = pool_gap * pool_inverse
    pool_gain, pool_bias = k.affine_p[2:3, :], k.affine_p[3:4, :]
    pool_u = pool_gain * pool_normed + pool_bias
    k.rows_scratch[0:4, :] = pool_u * sigmoid(pool_u)
    pool_act = jnp.broadcast_to(k.rows_scratch[pl.ds(net.z, 1), :], (16, 128)).astype(BF16)

    def normed_branch(at):
        return (k.branches[at, :] - mean) * inverse

    gain_b, bias_b = k.affine_b[0:1, :], k.affine_b[1:2, :]

    def activate_branches(at):
        u = gain_b * normed_branch(at) + bias_b
        k.spatial[at, :] = (u * sigmoid(u)).astype(BF16)

    each_rows(1536, 128, activate_branches)

    pool_row = mm_t(pool_act, k.w_slot[...])[0:1, :]

    def project_rows(i, carry):
        at = pl.ds(pl.multiple_of(i * 192, 64), 192)
        below = pl.ds(pl.multiple_of(i * 192 + 768, 64), 192)
        first = mm_t(k.spatial[at, :], k.w_project[...]) + pool_row
        second = mm_t(k.spatial[below, :], k.w_project[...]) + pool_row
        for b, block in enumerate(pair(first, second)):
            k.part_2[b, at, :] = block
        return carry

    def project_half(half):
        alternate(project_rows, half)

    low_128 = lax.broadcasted_iota(jnp.int32, (128, 128), 1) < 64

    def pair_mask(at):
        below = pl.ds(pl.multiple_of(at.start + 768, 128), 128)
        k.mask_pairs[at, :] = jnp.where(low_128, k.mask[at, :], k.mask[below, :])

    each_rows(768, 128, pair_mask)
    sum_scatter(net, k.part_2, scatter_refs(k, "sum2"), k.projected, produce=project_half)
    mean_p, inverse_p = statistics(
        net, k.projected, k.mask_pairs, counts, k.out_2, k.in_2, counted, folded=True
    )
    gain_p, bias_p = k.affine_p[0:1, :], k.affine_p[1:2, :]

    def normed_projected(at):
        return (k.projected[at, :] - mean_p) * inverse_p

    def activate_projected(at):
        u = gain_p * normed_projected(at) + bias_p
        k.gathered[net.m, at, :] = (u * sigmoid(u)).astype(BF16)

    each_rows(768, 128, activate_projected)
    gather_blocks(net, lambda b, at: k.gathered.at[b, at], 768)

    def spread(source, target):
        def body(at):
            first, second = unpair([source[b, at, :].astype(F32) for b in range(4)])
            target[at, :] = first.astype(BF16)
            target[pl.ds(pl.multiple_of(at.start + 768, 128), 128), :] = second.astype(BF16)

        each_rows(768, 128, body)

    k.features[...] = k.gathered[net.m]
    spread(k.gathered, k.wide_features)

    class_row = lax.broadcasted_iota(jnp.int32, (32, 512), 0)
    is_class, is_depth = class_row < 19, class_row == 19
    is_normal = (class_row == 20) | (class_row == 21)
    tile_row = lax.broadcasted_iota(jnp.int32, (32, 128), 0)
    bias_column = jnp.zeros((32, 128), F32)
    for c in range(22):
        bias_column = jnp.where(tile_row == c, k.head_bias[c], bias_column)
    task = [jnp.exp(jnp.full((32, 128), -k.log_vars[t], F32)) / counted for t in range(3)]
    weight_column = jnp.where(tile_row < 19, task[0], jnp.where(tile_row == 19, task[1], task[2]))
    bias_column, weight_column = wide(bias_column, 512), wide(weight_column, 512)
    k.head[...] = k.head_rows[...].astype(BF16)
    top_row, left_edge = k.boxes[net.z, 0], k.boxes[net.z, 1]
    bottom_row, right_edge = top_row + k.boxes[net.z, 2], left_edge + k.boxes[net.z, 3]
    lane = lax.broadcasted_iota(jnp.int32, (1, 512), 1)

    def four_rows(rows):
        return jnp.concatenate(rows, axis=1)
    loss_sums, bias_sums = 0.0, 0.0
    for chunk in range(3):
        at = pl.ds(chunk * 512, 512)
        logits = mm_t(k.head[...], k.wide_features[at, :]) + bias_column
        row_id, column_id = net.r * 12 + chunk * 4 + lane // 128, lane % 128
        inside = (row_id >= top_row) & (row_id < bottom_row)
        inside = inside & (column_id >= left_edge) & (column_id < right_edge)
        inside = jnp.where(inside, 1.0, 0.0)
        span = range(chunk * 4, chunk * 4 + 4)
        label = four_rows([k.labels[y] for y in span])
        target = jnp.where(is_depth, four_rows([k.depth[y] for y in span]), 0.0)
        for n in range(2):
            normal = four_rows([k.normal[y, n : n + 1, :] for y in span])
            target = jnp.where(class_row == 20 + n, normal, target)
        top = jnp.max(jnp.where(is_class, logits, -jnp.inf), axis=0, keepdims=True)
        powers = jnp.where(is_class, jnp.exp(jnp.where(is_class, logits - top, 0.0)), 0.0)
        power_sum = jnp.sum(powers, axis=0, keepdims=True)
        onehot = jnp.where(class_row == label, 1.0, 0.0)
        cross = jnp.log(power_sum) + top - jnp.sum(logits * onehot, axis=0, keepdims=True)
        gap = logits - target
        smooth = jnp.sqrt(gap * gap + 1.0)
        loss = jnp.where(class_row == 0, cross, 0.0)
        loss = jnp.where(is_depth, smooth - 1.0, loss)
        loss = jnp.where(is_normal, gap * gap, loss) * inside
        grad = jnp.where(is_class, powers / power_sum - onehot, 0.0)
        grad = jnp.where(is_depth, gap / smooth, grad)
        grad = jnp.where(is_normal, 2.0 * gap, grad) * (weight_column * inside)
        loss_sums = loss_sums + jnp.sum(loss, axis=1, keepdims=True)
        bias_sums = bias_sums + jnp.sum(grad, axis=1, keepdims=True)
        high = grad.astype(BF16)
        k.grad_logits[0:32, at] = high
        k.grad_logits[32:64, at] = (grad - high.astype(F32)).astype(BF16)
    head_terms = mm(k.grad_logits[...], k.wide_features[...])
    k.out_head[:, 0:256] = head_terms[0:32, :] + head_terms[32:64, :]
    first_lane = lax.broadcasted_iota(jnp.int32, (32, 128), 1) == 0
    k.out_head[:, 256:384] = jnp.where(first_lane, bias_sums, loss_sums)
    quarter = pl.ds(pl.multiple_of(net.m * 8, 8), 8)
    head_copies = []

    def share_head():
        for peer in net.group:
            head_copies.append(net.send(k.out_head.at[quarter], k.in_head.at[net.slot], peer))
        k.in_head[net.slot] = k.out_head[quarter, :]

    own_head = k.head_rows[:, lane_block(net.m // 2)]
    own_head = jnp.where(odd, pltpu.roll(own_head, 64, 1), own_head)
    own_head = jnp.where(low_128[0:32, :], own_head, 0.0)
    head_low = jnp.concatenate([own_head, own_head], axis=0).astype(BF16)
    own_head = pltpu.roll(own_head, 64, 1)
    head_high = jnp.concatenate([own_head, own_head], axis=0).astype(BF16)
    k.grad_p[...] = tm_m(k.grad_logits[:, 0:768], head_low) + tm_m(
        k.grad_logits[:, 768:1536], head_high
    )

    def back_features(at):
        k.grad_p[at, :] = k.grad_p[at, :] * slope(gain_p * normed_projected(at) + bias_p)

    each_rows(768, 128, back_features)
    bias_grad, gain_grad = gradient_sums(
        net, k.grad_p, normed_projected, k.out_3, k.in_3, folded=True, meanwhile=share_head
    )
    keep_rows(k.norm_p, gain_grad, bias_grad)

    def back_projected(at):
        shared = k.mask_pairs[at, :] / counted * gain_p
        grad = gain_p * k.grad_p[at, :] - shared * (bias_grad + normed_projected(at) * gain_grad)
        k.gathered_grad[net.m, at, :] = (inverse_p * grad).astype(BF16)

    each_rows(768, 128, back_projected)
    gather_blocks(net, lambda b, at: k.gathered_grad.at[b, at], 768)
    spread(k.gathered_grad, k.grad_projected)
    (pixel_sum,) = column_sums(lambda at: (k.grad_projected[at, :].astype(F32),), 1536, 256, 1)
    row_16 = lax.broadcasted_iota(jnp.int32, (16, 256), 0)
    terms = jnp.zeros((16, 256), F32)
    for i, term in enumerate(split_three(pixel_sum)):
        terms = jnp.where(row_16 == i, term.astype(F32), terms)
    terms = terms.astype(BF16)
    tall = jnp.concatenate([terms] * 8, axis=0)
    pool_grad = jnp.sum(mm(tall, k.w_slot[...]), axis=0, keepdims=True) * 0.125

    def project_gradient():
        for b in range(2):
            lanes = slice(b * 128, b * 128 + 128)
            grad = tm_m(k.grad_projected[:, lanes], k.spatial[...])
            k.grad_project[b * 4 : b * 4 + 4, :, 0:256] = grad.reshape(4, 32, 256).astype(BF16)
        grad = tm_m(terms, pool_act)
        k.grad_project[:, :, 256:384] = grad.reshape(8, 32, 128).astype(BF16)

    def back_spatial(at):
        grad = mm(k.grad_projected[at, :], k.w_project[...])
        k.grad_b[at, :] = grad * slope(gain_b * normed_branch(at) + bias_b)

    each_rows(1536, 128, back_spatial)
    bias_grad_b, gain_grad_b = gradient_sums(
        net,
        k.grad_b,
        normed_branch,
        k.out_4,
        k.in_4,
        extra=pool_grad,
        meanwhile=project_gradient,
    )
    keep_rows(k.norm_b, gain_grad_b, bias_grad_b)

    pool_terms = k.in_4[0:4, 4, :] + k.in_4[4:8, 4, :]
    pool_terms = pool_terms * slope(pool_u)
    pool_bias_grad = jnp.sum(pool_terms, axis=0, keepdims=True)
    pool_gain_grad = jnp.sum(pool_terms * pool_normed, axis=0, keepdims=True)
    keep_rows(k.norm_pool, pool_gain_grad, pool_bias_grad)
    pool_back = pool_inverse * (
        pool_gain * pool_terms
        - pool_gain / 4.0 * (pool_bias_grad + pool_normed * pool_gain_grad)
    )
    low = lax.broadcasted_iota(jnp.int32, (4, 128), 1) < 64
    k.rows_scratch[4:8, :] = jnp.where(low, pool_back, 0.0)
    grad_conv = jnp.broadcast_to(k.rows_scratch[pl.ds(net.z + 4, 1), :], (16, 128)).astype(BF16)
    spread_back = mm(grad_conv, k.w_pool[...])[0:8, :]
    for b in range(4):
        k.out_back[b] = spread_back[:, b * 512 : b * 512 + 512]
    back_copies = [
        net.send(k.out_back.at[lax.rem(net.m + a, 4)], k.in_back.at[a], (lax.rem(net.m + a, 4), net.r, net.z))
        for a in range(1, 4)
    ]

    only_first = lax.broadcasted_iota(jnp.int32, (16, 128), 0) == 0
    one_row = jnp.where(only_first, grad_conv.astype(F32) * 0.5, 0.0).astype(BF16)
    for e in range(8):
        grad = tm_m(one_row, k.pooled[:, e * 256 : e * 256 + 256])
        k.grad_pool[e] = grad[0:64, :].astype(BF16)

    def back_branches(at):
        shared = wide(k.mask[at, :], 256) / counted * gain_b
        grad = gain_b * k.grad_b[at, :] - shared * (bias_grad_b + normed_branch(at) * gain_grad_b)
        k.grad_branches[at, :] = (inverse * grad).astype(BF16)

    for copy in back_copies:
        copy.wait()
    k.grad_pooled[...] = (k.out_back[net.m] + k.in_back[1] + k.in_back[2] + k.in_back[3]) / area
    for copy in head_copies:
        copy.wait()
    k.head_sums[quarter, :] = jnp.sum(k.in_head[...], axis=0)
    head_copies = [
        net.send(k.head_sums.at[quarter], k.head_sums.at[quarter], (lax.rem(net.m + a, 4), net.r, net.z))
        for a in range(1, 4)
    ]
    each_rows(1536, 128, back_branches)
    for copy in head_copies:
        copy.wait()


def run_pyramid(args):
    return call_kernel(
        pyramid_forward,
        "pyramid",
        1,
        args,
        dict(
            w_pyramid=((13, 4, 64, 512), BF16),
            features=((768, 128), BF16),
            norm_p=((8, 128), F32),
            grad_project=((8, 32, 384), BF16),
            grad_pool=((8, 64, 256), BF16),
            norm_b=((8, 256), F32),
            norm_pool=((8, 128), F32),
            grad_branches=((1536, 256), BF16),
            grad_pooled=((8, 512), F32),
            head_sums=((32, 384), F32),
        ),
        dict(
            w_slots=pltpu.VMEM((4, 5, 64, 256), BF16),
            local_sems=pltpu.SemaphoreType.DMA((3,)),
            affine_b=pltpu.VMEM((8, 256), F32),
            affine_p=pltpu.VMEM((8, 128), F32),
            head_rows=pltpu.VMEM((32, 256), F32),
            head=pltpu.VMEM((32, 256), BF16),
            pooled=pltpu.VMEM((16, 2048), BF16),
            spatial=pltpu.VMEM((1536, 256), BF16),
            grad_projected=pltpu.VMEM((1536, 256), BF16),
            w_project=pltpu.VMEM((256, 256), BF16),
            w_slot=pltpu.VMEM((256, 128), BF16),
            w_pool=pltpu.VMEM((128, 2048), BF16),
            mask_pairs=pltpu.VMEM((768, 128), F32),
            out_pool=pltpu.VMEM((8, 512), F32),
            in_pool=pltpu.VMEM((8, 8, 512), F32),
            cells=pltpu.VMEM((12, 208, 512), F32),
            edge_out=pltpu.VMEM((1536, 256), BF16),
            edge_in=pltpu.VMEM((1536, 256), BF16),
            part=pltpu.VMEM((4, 1536, 256), F32),
            **scatter_scratch("sum", 1536, 256),
            branches=pltpu.VMEM((1536, 256), F32),
            rows_scratch=pltpu.VMEM((8, 128), F32),
            part_2=pltpu.VMEM((4, 768, 128), F32),
            **scatter_scratch("sum2", 768, 128),
            projected=pltpu.VMEM((768, 128), F32),
            gathered=pltpu.VMEM((4, 768, 128), BF16),
            wide_features=pltpu.VMEM((1536, 256), BF16),
            grad_logits=pltpu.VMEM((64, 1536), BF16),
            out_head=pltpu.VMEM((32, 384), F32),
            in_head=pltpu.VMEM((8, 8, 384), F32),
            grad_p=pltpu.VMEM((768, 128), F32),
            gathered_grad=pltpu.VMEM((4, 768, 128), BF16),
            grad_b=pltpu.VMEM((1536, 256), F32),
            out_back=pltpu.VMEM((4, 8, 512), F32),
            in_back=pltpu.VMEM((4, 8, 512), F32),
            **exchange_scratch(1),
            **exchange_scratch(2),
            **exchange_scratch(3),
            **exchange_scratch(4),
        ),
        96,
        smem=dict(boxes=1, head_bias=1, log_vars=1),
        hbm=dict(far_pyramid=1, far_slots=1),
        stream=dict(mask=1, w_pyramid=1),
    )


def core_halves(net, whole, arrived):
    away = pl.ds(pl.multiple_of(4 - 4 * net.r, 4), 4)
    return net.send(whole.at[away], arrived, net.core)


def add_halves(net, whole, arrived, target):
    for z in range(4):
        total = whole[4 * net.r + z].astype(F32) + arrived[z].astype(F32)
        target[z] = total.astype(target.dtype)


def chunk_of(net):
    return lambda z: 2 * lax.rem(z + net.m, 2) + z // 2


def along_z(net, source, target, chunk=lambda z: z):
    copies = []
    for d in (1, 2, 3):
        there = lax.rem(net.z + d, 4)
        copies.append(
            net.send(source.at[chunk(there)], target.at[d - 1], (net.m, net.r, there))
        )
    return copies


def finish_z(net, half, arrived, chunk=lambda z: z):
    return half[chunk(net.z)].astype(F32) + sum(arrived[d].astype(F32) for d in range(3))


class PairSums:
    def __init__(self, net, half, other, pair, last):
        self.net, self.half, self.other, self.pair, self.last = net, half, other, pair, last
        kept, away = lax.rem(net.z + net.m, 2), lax.rem(net.z + net.m + 1, 2)
        self.kept = 2 * kept
        beside = net.z + 1 - 2 * lax.rem(net.z, 2)
        self.first = self.copy(half.at[pl.ds(2 * away, 2)], other, beside)
        self.high = net.z // 2
        if last is not None:
            self.second = self.copy(pair.at[1 - self.high], last, net.z + 2 - 4 * self.high)

    def copy(self, src, dst, z):
        net, i = self.net, self.net.count
        net.count += 1
        return pltpu.make_async_remote_copy(
            src_ref=src,
            dst_ref=dst,
            send_sem=net.send_sems.at[i],
            recv_sem=net.recv_sems.at[i],
            device_id=(net.m, net.r, z),
            device_id_type=MESH,
        )

    def go_on(self, half):
        self.first.wait()

        def body(i, carry):
            for h in range(2):
                total = half[self.kept + h, i].astype(F32) + self.other[h, i].astype(F32)
                self.pair[h, i] = total.astype(BF16)
            return carry

        lax.fori_loop(0, half.shape[1], body, 0, unroll=2)

    def finish(self, target):
        self.second.wait()

        def body(i, carry):
            total = self.pair[self.high, i].astype(F32) + self.last[i].astype(F32)
            target[0, i] = total[:, 0:256].astype(BF16)
            target[1, i] = total[:, 256:512].astype(BF16)
            return carry

        lax.fori_loop(0, target.shape[1], body, 0, unroll=2)


def pyramid_backward(net, k):
    counted = pixel_count(k.boxes)
    greet([net.side, net.over] + net.group)
    k.blocks[net.m] = k.grad_branches[...]
    small = [
        core_halves(net, k.grad_project, k.core_project),
        core_halves(net, k.grad_pool, k.core_pool),
    ]
    for c in range(4):
        zero_margins(k.cells.at[c], 40, 128)

    def rows_of(i, size=384):
        return pl.ds(pl.multiple_of(i * size, 128), size)

    low = lax.broadcasted_iota(jnp.int32, (128, 128), 1) < 64
    near = net.m // 2
    far = 1 - near
    mine_first = net.r == near
    mine_second = net.r == far

    def both(source, pair_of, i, lane):
        at = slice(lane * 128, lane * 128 + 128)
        left = source[2 * pair_of, rows_of(i, 128), at].astype(F32)
        right = source[2 * pair_of + 1, rows_of(i, 128), at].astype(F32)
        first = jnp.where(low, left, pltpu.roll(right, 64, 1))
        return first, jnp.where(low, pltpu.roll(left, 64, 1), right)

    def shift_rows(pair_of, i, cell, rate, base):
        for j in range(3):
            start = 40 - rate * (j - 1)
            block = k.cells[cell, i, start : start + 128, :].astype(BF16)
            k.shifts[base + j, rows_of(i, 128), lane_block(pair_of)] = block

    def build(pair_of):
        def fill(i, carry):
            point, first = both(k.blocks, pair_of, i, 0)
            k.shifts[0, rows_of(i, 128), lane_block(pair_of)] = point.astype(BF16)
            second, third = both(k.blocks, pair_of, i, 1)
            k.cells[0, i, 40:168, :] = first
            k.cells[1, i, 40:168, :] = second
            k.cells[2, i, 40:168, :] = third
            return carry

        lax.fori_loop(0, 12, fill, 0, unroll=2)

        def spread(i, carry):
            for cell, rate, base in ((0, 12, 1), (1, 24, 4), (2, 36, 7)):
                shift_rows(pair_of, i, cell, rate, base)
            return carry

        lax.fori_loop(0, 12, spread, 0, unroll=2)

    def build_edge(pair_of):
        def fill(i, carry):
            k.cells[3, i, 40:168, :] = both(k.other, pair_of, i, 0)[1]
            return carry

        lax.fori_loop(0, 12, fill, 0, unroll=2)

        def spread(i, carry):
            shift_rows(pair_of, i, 3, 12, 10)
            return carry

        lax.fori_loop(0, 12, spread, 0, unroll=2)

    def weight_gradients(pair_of, between=None):
        owners = pl.ds(4 * pair_of, 4)

        def run(start, stop, shift):
            def body(t, carry):
                grad = tm_m(k.shifts[t, :, lane_block(pair_of)], k.trunk[...])
                k.grad_pyramid[owners, t + shift] = grad.reshape(4, 32, 512).astype(BF16)
                return carry

            lax.fori_loop(start, stop, body, 0)

        run(0, 1, 0)
        run(1, 4, 3)
        run(10, 13, net.r * 6 - 9)
        for j in range(3):
            k.grad_pyramid[owners, 7 - net.r * 6 + j] = jnp.zeros((4, 32, 512), BF16)
        if between is not None:
            between()
        run(4, 10, 6)

    def beside(pair_of):
        view = (pl.ds(2 * pair_of, 2), slice(None), pl.ds(0, 128))
        return net.send(k.blocks.at[view], k.other.at[pl.ds(2 * pair_of, 2)], net.core)

    def to_core(pair_of, low, high):
        i = net.count
        net.count += 1
        taps = pl.ds(low, high - low)
        return pltpu.make_async_remote_copy(
            src_ref=k.grad_pyramid.at[pl.ds(4 * pair_of, 4), taps],
            dst_ref=k.core_pyramid.at[:, taps],
            send_sem=net.send_sems.at[i],
            recv_sem=net.recv_sems.at[i],
            device_id=net.core,
            device_id_type=MESH,
        )

    def add_core(pair_of, low, high):
        def body(i, carry):
            for z in range(4):
                total = k.grad_pyramid[4 * pair_of + z, i].astype(F32)
                total = total + k.core_pyramid[z, i].astype(F32)
                k.half_pyramid[z, i] = total.astype(BF16)
            return carry

        lax.fori_loop(low, high, body, 0, unroll=2)

    first_swap = []

    def near_pair():
        copy = beside(near)
        build(near)
        copy.wait()
        build_edge(near)
        k.stream.need(trunk=1)
        weight_gradients(near)
        first_swap.append(to_core(near, 0, 16))
        pl.when(mine_second)(first_swap[0].start)

    gather_blocks(net, lambda b, at: k.blocks.at[b, at], 1536, meanwhile=near_pair)
    copy = beside(far)
    build(far)
    for swap in small:
        swap.wait()
    add_halves(net, k.grad_project, k.core_project, k.half_project)
    add_halves(net, k.grad_pool, k.core_pool, k.half_pool)
    small_moves = along_z(net, k.half_project, k.z_project, chunk_of(net))
    small_moves = small_moves + along_z(net, k.half_pool, k.z_pool)
    copy.wait()
    build_edge(far)
    pair_sums = PairSums(net, k.half_pyramid, k.z_other, k.z_pair, None)

    @pl.when(mine_first)
    def _():
        first_swap[0].wait_recv()
        add_core(near, 0, 16)
        pair_sums.first.start()

    def trunk_rows(i, carry):
        total = 0.0
        for t in range(13):
            total = total + mm(k.shifts[t, rows_of(i), :], k.w_pyramid[t])
        k.shortcut[rows_of(i), :] = total
        return carry

    k.stream.need(w_pyramid=1, expanded=1, x=1, mask=1)
    lax.fori_loop(0, 4, trunk_rows, 0)
    mean, inverse = k.stats_3[0:1, :], k.stats_3[1:2, :]
    gain, bias = k.affine_3[0:1, :], k.affine_3[1:2, :]
    pooled = k.grad_pooled[0:1, :]

    def normed(at):
        return (k.expanded[at, :] - mean) * inverse

    def back_trunk(at):
        u = gain * normed(at) + bias + k.x[at, :].astype(F32)
        grad = k.shortcut[at, :] + wide(k.mask[at, :], 512) * pooled
        k.shortcut[at, :] = grad * slope(u)

    each_rows(1536, 64, back_trunk)
    k.stream.done(shortcut=1)

    second_swap = [to_core(far, 0, 10), to_core(far, 10, 16)]

    def far_gradients():
        weight_gradients(far, lambda: pl.when(mine_first)(second_swap[0].start))

        @pl.when(mine_first)
        def _():
            second_swap[1].start()
            pair_sums.go_on(k.half_pyramid)

    bias_grad, gain_grad = gradient_sums(
        net, k.shortcut, normed, k.out_1, k.in_1, meanwhile=far_gradients
    )
    keep_rows(k.norm_3, gain_grad, bias_grad)

    def back_expanded(at):
        shared = wide(k.mask[at, :], 512) / counted * gain
        grad = gain * k.shortcut[at, :] - shared * (bias_grad + normed(at) * gain_grad)
        k.grad_expanded[at, :] = (inverse * grad).astype(BF16)

    each_rows(1536, 64, back_expanded)
    k.stream.done(grad_expanded=1)
    for move_ in small_moves:
        move_.wait()
    k.sum_project[...] = finish_z(net, k.half_project, k.z_project, chunk_of(net)).astype(BF16)
    k.sum_pool[...] = finish_z(net, k.half_pool, k.z_pool)

    @pl.when(mine_second)
    def _():
        first_swap[0].wait_send()
        second_swap[0].wait_recv()
        add_core(far, 0, 10)
        second_swap[1].wait_recv()
        add_core(far, 10, 16)

    @pl.when(mine_first)
    def _():
        for swap in second_swap:
            swap.wait_send()


def run_pyramid_backward(args):
    return call_kernel(
        pyramid_backward,
        "pyramid_back",
        2,
        args,
        dict(
            shortcut=((1536, 512), F32),
            grad_expanded=((1536, 512), BF16),
            norm_3=((8, 512), F32),
            half_pyramid=((4, 16, 32, 512), BF16),
            z_pair=((2, 16, 32, 512), BF16),
            sum_project=((32, 384), BF16),
            sum_pool=((64, 256), F32),
        ),
        dict(
            half_project=pltpu.VMEM((4, 32, 384), BF16),
            half_pool=pltpu.VMEM((4, 64, 256), BF16),
            z_other=pltpu.VMEM((2, 16, 32, 512), BF16),
            z_project=pltpu.VMEM((3, 32, 384), BF16),
            z_pool=pltpu.VMEM((3, 64, 256), BF16),
            grad_pyramid=pltpu.VMEM((8, 16, 32, 512), BF16),
            core_pyramid=pltpu.VMEM((4, 16, 32, 512), BF16),
            core_project=pltpu.VMEM((4, 32, 384), BF16),
            core_pool=pltpu.VMEM((4, 64, 256), BF16),
            blocks=pltpu.VMEM((4, 1536, 256), BF16),
            other=pltpu.VMEM((4, 1536, 128), BF16),
            cells=pltpu.VMEM((4, 12, 208, 128), F32),
            shifts=pltpu.VMEM((13, 1536, 256), BF16),
            **exchange_scratch(1),
        ),
        48,
        stream=dict(w_pyramid=1, expanded=1, x=1, mask=1, trunk=1, shortcut=1, grad_expanded=1),
    )


def bottleneck_backward(net, k):
    counted = pixel_count(k.boxes)
    loads = load_taps(k)
    high, source = net.z // 2, net.slot // 2
    here = net.m * 8 + net.slot
    owners, givers = [], []
    for i in range(2):
        part = 2 * net.m + i
        column = 2 * net.r + lax.rem(net.z + net.m, 2)
        owners.append((column, part // 4, lax.rem(part, 4)))
        givers.append((source, net.m // 2, lax.rem(net.m + source, 2) + 2 * i))

    def elsewhere(device):
        return device[0] * 8 + device[1] * 4 + device[2] != here

    moves = elsewhere(owners[0])
    stays = jnp.logical_not(moves)
    greet(
        [net.side, net.over, net.diagonal] + net.group + [owners[1]],
        [(owners[0], moves), (givers[0], elsewhere(givers[0])), (givers[1], elsewhere(givers[1]))],
    )

    def to_owners(views, arrived, sem):
        base = net.count
        net.count += 2

        def copy(i, g, device):
            return pltpu.make_async_remote_copy(
                src_ref=views(i),
                dst_ref=arrived.at[g],
                send_sem=net.send_sems.at[base + i],
                recv_sem=net.recv_sems.at[base + g],
                device_id=device,
                device_id_type=MESH,
            )

        first, second = copy(0, high, owners[0]), copy(1, high, owners[1])
        kept = pltpu.make_async_copy(views(0), arrived.at[high], sem)

        def begin():
            pl.when(moves)(first.start)
            pl.when(stays)(kept.start)
            second.start()

        def wait():
            pl.when(moves)(first.wait_send)
            pl.when(stays)(kept.wait)
            second.wait_send()
            for g in range(2):
                pl.when(elsewhere(givers[g]))(copy(0, g, owners[1]).wait_recv)

        begin()
        return wait

    def lanes_for(i):
        return pl.ds(i * 256, 256)

    early = net.r == net.m // 2
    is_late = net.r == 1 - net.m // 2
    pair_sums = PairSums(net, k.far_half_pyramid, k.z_other, k.z_pair, k.z_last)

    odd_z = lax.rem(net.z, 2)
    lone = early & (odd_z == 0)
    beside = early & (odd_z == 1)
    stay = pltpu.make_async_copy(k.pyramid_sum, k.relay.at[0], k.local_sems.at[9])

    def remote(src, dst, send, arrive, device):
        return pltpu.make_async_remote_copy(
            src_ref=src,
            dst_ref=dst,
            send_sem=net.send_sems.at[send],
            recv_sem=net.recv_sems.at[arrive],
            device_id=device,
            device_id_type=MESH,
        )

    base = net.count
    net.count += 6
    to_side = remote(k.pyramid_sum, k.relay.at[0], base, base, net.side)
    across = (net.m ^ (2 + odd_z), net.r, net.z)
    to_across = remote(k.pyramid_sum, k.relay.at[1], base + 1, base + 1, across)
    plane = lax.rem(net.m + net.z, 2)

    def forward(e, i):
        device = (net.m, net.r if e == 0 else 1 - net.r, 2 * plane + i)
        return remote(
            k.relay.at[e, i], k.own_pyramid.at[high], base + 2 + 2 * e + i, base + 2 + high, device
        )

    forwards = [[forward(e, i) for i in range(2)] for e in range(2)]
    keep = pltpu.make_async_copy(k.relay.at[0, odd_z], k.own_pyramid.at[high], k.local_sems.at[12])
    keeps = early & (plane == high)

    def kept_here(i):
        return keeps & (odd_z == i)

    def begin_early():
        pl.when(lone)(stay.start)
        pl.when(beside)(to_side.start)

    def relay_early():
        pl.when(lone)(stay.wait)
        pl.when(beside)(to_side.wait)
        for i in range(2):
            pl.when(early & jnp.logical_not(kept_here(i)))(forwards[0][i].start)
        pl.when(keeps)(keep.start)

    def relay_late():
        pl.when(early)(to_across.wait_recv)
        for i in range(2):
            pl.when(early)(forwards[1][i].start)

    def wait_pyramid():
        pl.when(is_late)(to_across.wait_send)
        for i in range(2):
            pl.when(early & jnp.logical_not(kept_here(i)))(forwards[0][i].wait_send)
            pl.when(early)(forwards[1][i].wait_send)
        pl.when(keeps)(keep.wait)
        for g in range(2):
            local = early & (lax.rem(net.z // 2 + net.m, 2) + 2 * g == net.z)
            arrival = remote(k.relay.at[0, 0], k.own_pyramid.at[g], base, base + 2 + g, net.core)
            pl.when(jnp.logical_not(local))(arrival.wait_recv)


    k.stream.need(z_pair=1)
    pl.when(is_late)(pair_sums.first.start)
    pl.when(early)(pair_sums.second.start)
    wait_project = to_owners(lambda i: k.sum_project, k.own_project, k.local_sems.at[10])

    def rows_of(i, size=384):
        return pl.ds(pl.multiple_of(i * size, 128), size)

    def expand_half(half):
        for i in (half, half + 2):
            at = pl.ds(i * 384, 384)
            total = mm_t(k.grad_expanded[at, :], k.w_expand[...])
            for b in range(4):
                k.part[b, at, :] = total[:, b * 128 : b * 128 + 128]

    swaps, late_moves = [], []

    def expand_gradient():
        k.stream.need(hidden_two=1)

        def body(b, carry):
            grad = tm_m(k.hidden_two[:, lane_block(b)], k.grad_expanded[...])
            k.grad_expand[pl.ds(2 * b, 2)] = grad.reshape(2, 64, 512).astype(BF16)
            return carry

        lax.fori_loop(0, 4, body, 0)
        swaps.append(core_halves(net, k.grad_expand, k.core_expand))

    sum_scatter(net, k.part, scatter_refs(k, "sum"), k.grad_2, meanwhile=expand_gradient, produce=expand_half)
    k.stream.need(dilated=1, mask=1)

    def norm_back(grad, value, stats, affine, outgoing, incoming, store, kept, meanwhile=None):
        mean, inverse = stats[0:1, :], stats[1:2, :]
        gain, bias = affine[0:1, :], affine[1:2, :]

        def normed(at):
            return (value[at, :] - mean) * inverse

        def through(at):
            grad[at, :] = grad[at, :] * slope(gain * normed(at) + bias)

        each_rows(1536, 128, through)
        bias_grad, gain_grad = gradient_sums(
            net, grad, normed, outgoing, incoming, meanwhile=meanwhile
        )
        keep_rows(kept, gain_grad, bias_grad)

        def back(at):
            shared = k.mask[at, :] / counted * gain
            result = gain * grad[at, :] - shared * (bias_grad + normed(at) * gain_grad)
            store(at, (inverse * result).astype(BF16))

        each_rows(1536, 128, back)

    def store_2(at, value):
        k.grad_pad[pl.ds(pl.multiple_of(at.start + 512, 128), 128), :] = value

    def pass_expand():
        k.stream.need(half_pyramid=1)
        @pl.when(is_late)
        def _():
            pair_sums.go_on(k.half_pyramid)
            pair_sums.second.start()

        @pl.when(early)
        def _():
            pair_sums.finish(k.pyramid_sum)

        begin_early()
        swaps.pop().wait()
        add_halves(net, k.grad_expand, k.core_expand, k.half_expand)
        late_moves.extend(along_z(net, k.half_expand, k.z_expand))

    norm_back(
        k.grad_2,
        k.dilated,
        k.stats_2,
        k.affine_2,
        k.out_2,
        k.in_2,
        store_2,
        k.norm_2,
        meanwhile=pass_expand,
    )
    halo = send_halo(net, k.grad_pad)
    zero_margins(k.cells, 8, 128)
    halo.wait()

    def spread(i, carry):
        k.cells[i, 8:136, :] = k.grad_pad[rows_of(i, 128), :].astype(F32)
        for j in range(3):
            start = 8 - 4 * (j - 1)
            k.grad_taps[rows_of(i, 128), j * 128 : j * 128 + 128] = k.cells[
                i, start : start + 128, :
            ].astype(BF16)
        return carry

    lax.fori_loop(0, 20, spread, 0, unroll=2)
    for load in loads:
        load.wait()

    def dilated_rows(i, carry):
        total = 0.0
        for tap in range(3):
            at = pl.ds(pl.multiple_of((i * 3 + 8 - 4 * tap) * 128, 128), 384)
            total = total + mm_t(k.grad_taps[at, :], k.w_taps[tap])
        for b in range(4):
            k.part[b, rows_of(i), :] = total[:, b * 128 : b * 128 + 128]
        return carry

    def dilated_half(half):
        def run(i, carry):
            return dilated_rows(half + 2 * i, carry)

        lax.fori_loop(0, 2, run, 0)

    def dilated_gradient():
        k.stream.need(hidden=1)

        for i in range(3):

            def body(b, carry):
                band = k.hidden[pl.ds(i * 512, 1536), lane_block(b)]
                grad = tm_m(band, k.grad_taps[pl.ds(512, 1536), :])
                for j in range(3):
                    block = grad[:, j * 128 : j * 128 + 128].reshape(2, 64, 128)
                    rows = slice((i * 3 + j) * 64, (i * 3 + j) * 64 + 64)
                    k.grad_dilated[pl.ds(2 * b, 2), rows, :] = block.astype(BF16)
                return carry

            lax.fori_loop(0, 4, body, 0)
        swaps.append(core_halves(net, k.grad_dilated, k.core_dilated))

    sum_scatter(net, k.part, scatter_refs(k, "sum2"), k.grad_1, meanwhile=dilated_gradient, produce=dilated_half)
    k.stream.need(reduced=1)

    def store_1(at, value):
        k.grad_reduced[at, lane_block(net.m)] = value

    def pass_halves():
        @pl.when(is_late)
        def _():
            pair_sums.finish(k.pyramid_sum)
            to_across.start()

        relay_early()
        swaps.pop().wait()
        add_halves(net, k.grad_dilated, k.core_dilated, k.half_dilated)
        late_moves.extend(along_z(net, k.half_dilated, k.z_dilated))

    norm_back(
        k.grad_1,
        k.reduced,
        k.stats_1,
        k.affine_1,
        k.out_1,
        k.in_1,
        store_1,
        k.norm_1,
        meanwhile=pass_halves,
    )

    def reduce_gradients(pair_of):
        def body(i, carry):
            b = 2 * pair_of + i
            grad = tm_m(k.grad_reduced[:, lane_block(b)], k.x[...])
            k.grad_reduce[pl.ds(2 * b, 2)] = grad.reshape(2, 64, 512).astype(BF16)
            return carry

        lax.fori_loop(0, 2, body, 0)

    def near_gradients():
        relay_late()
        k.stream.need(x=1)
        reduce_gradients(net.m // 2)

    gather_blocks(
        net,
        lambda b, at: k.grad_reduced.at[at, lane_block(b)],
        1536,
        meanwhile=near_gradients,
    )

    reduce_gradients(1 - net.m // 2)
    swap = core_halves(net, k.grad_reduce, k.core_reduce)

    swap.wait()
    add_halves(net, k.grad_reduce, k.core_reduce, k.half_reduce)
    reduce_moves = along_z(net, k.half_reduce, k.z_reduce, chunk_of(net))

    k.stream.need(shortcut=1, w_reduce=1)

    def input_rows(at):
        total = k.shortcut[at, :]
        for b in range(4):
            total = total + mm_t(k.grad_reduced[at, b * 128 : b * 128 + 128], k.w_reduce[b])
        k.grad_input[at, :] = total

    each_rows(1536, 384, input_rows)
    k.stream.done(grad_input=1)
    for move_ in reduce_moves:
        move_.wait()
    k.sum_reduce[...] = finish_z(net, k.half_reduce, k.z_reduce, chunk_of(net)).astype(BF16)
    wait_reduce = to_owners(
        lambda i: k.sum_reduce.at[:, lanes_for(i)], k.own_reduce, k.local_sems.at[11]
    )
    for move_ in late_moves:
        move_.wait()
    k.sum_dilated[...] = finish_z(net, k.half_dilated, k.z_dilated)
    k.sum_expand[...] = finish_z(net, k.half_expand, k.z_expand)
    wait_pyramid()
    wait_project()
    wait_reduce()


def run_bottleneck_backward(args):
    return call_kernel(
        bottleneck_backward,
        "bottleneck_back",
        3,
        args,
        dict(
            grad_input=((1536, 512), F32),
            norm_2=((8, 128), F32),
            norm_1=((8, 128), F32),
            own_pyramid=((2, 16, 32, 256), BF16),
            own_project=((2, 32, 384), BF16),
            sum_dilated=((576, 128), F32),
            sum_expand=((64, 512), F32),
            own_reduce=((2, 64, 256), BF16),
        ),
        dict(
            grad_taps=pltpu.VMEM((2560, 384), BF16),
            grad_reduced=pltpu.VMEM((1536, 512), BF16),
            z_other=pltpu.VMEM((2, 16, 32, 512), BF16),
            z_last=pltpu.VMEM((16, 32, 512), BF16),
            relay=pltpu.VMEM((2, 2, 16, 32, 256), BF16),
            pyramid_sum=pltpu.VMEM((2, 16, 32, 256), BF16),
            sum_reduce=pltpu.VMEM((64, 512), BF16),
            grad_expand=pltpu.VMEM((8, 64, 512), BF16),
            core_expand=pltpu.VMEM((4, 64, 512), BF16),
            half_expand=pltpu.VMEM((4, 64, 512), BF16),
            z_expand=pltpu.VMEM((3, 64, 512), BF16),
            grad_reduce=pltpu.VMEM((8, 64, 512), BF16),
            core_reduce=pltpu.VMEM((4, 64, 512), BF16),
            half_reduce=pltpu.VMEM((4, 64, 512), BF16),
            z_reduce=pltpu.VMEM((3, 64, 512), BF16),
            grad_dilated=pltpu.VMEM((8, 576, 128), BF16),
            core_dilated=pltpu.VMEM((4, 576, 128), BF16),
            half_dilated=pltpu.VMEM((4, 576, 128), BF16),
            z_dilated=pltpu.VMEM((3, 576, 128), BF16),
            w_taps=pltpu.VMEM((3, 512, 384), BF16),
            part=pltpu.VMEM((4, 1536, 128), F32),
            **scatter_scratch("sum", 1536, 128),
            **scatter_scratch("sum2", 1536, 128),
            grad_2=pltpu.VMEM((1536, 128), F32),
            grad_1=pltpu.VMEM((1536, 128), F32),
            grad_pad=pltpu.VMEM((2560, 128), BF16),
            cells=pltpu.VMEM((20, 144, 128), F32),
            **exchange_scratch(2),
            **exchange_scratch(1),
            local_sems=pltpu.SemaphoreType.DMA((13,)),
        ),
        96,
        hbm=dict(w_dilated=1),
        stream=dict(z_pair=1, half_pyramid=1, hidden_two=1, dilated=1, mask=1, hidden=1, reduced=1, x=1, shortcut=1, w_reduce=1, grad_input=1),
    )


def finish(net, k):
    counted = pixel_count(k.boxes)
    odd = lax.rem(lax.axis_index("batch"), 2)

    def rows_for(i):
        return slice(i * 32, i * 32 + 32)

    nothing = jnp.zeros((64, 256), F32)
    for tap in (9, 10, 11, 15, 16, 17, 18, 19, 20, 24, 25, 26):
        k.grad_rates[tap] = nothing
    for slot in range(16):
        for i in range(2):
            block = k.own_pyramid[i, slot].astype(F32)
            if slot == 0:
                k.grad_point[rows_for(i), :] = block
            else:
                tap = slot - 1 if slot < 10 else slot + 2 if slot < 13 else slot + 8
                k.grad_rates[tap, rows_for(i), :] = block
    k.stream.done(grad_rates=1)
    k.stream.need(from_input=1)
    leave = pltpu.make_async_copy(k.from_input, k.grad_input, k.sem.at[0])
    leave.start()
    for y in range(6):
        turned = k.packed[y * 128 : y * 128 + 128, :].astype(F32).T.astype(BF16)
        k.features[y] = turned[0:64, :]
        k.features[y + 6] = turned[64:128, :]
    k.turned[...] = jnp.concatenate([k.own_project[i].astype(F32) for i in range(2)], axis=0).T
    for slot in range(5):
        start = pl.multiple_of(slot * 64 + odd * 32, 32)
        k.grad_project[slot] = k.turned[pl.ds(start, 32), :]
    k.grad_reduce[...] = jnp.concatenate(
        [k.own_reduce[i].astype(F32) for i in range(2)], axis=0
    ).T
    k.grad_dilated[...] = k.from_dilated[...].reshape(9, 64, 128)
    k.grad_expand[...] = k.from_expand[...]
    k.grad_pool[...] = k.from_pool[...]
    k.grad_norm_1[...] = k.norm_1[0:2, :]
    k.grad_norm_2[...] = k.norm_2[0:2, :]
    k.grad_norm_3[...] = k.norm_3[0:2, :]
    for b in range(4):
        k.grad_norm_b[:, b, :] = k.norm_b[0:2, b * 64 : b * 64 + 64]
    k.grad_norm_pool[...] = k.norm_pool[0:2, 0:64]
    k.grad_norm_p[...] = k.norm_p[0:2, 0:64]
    k.grad_head_weight[...] = k.head_sums[0:22, 0:256]
    columns = k.head_sums[:, 256:384].T
    k.grad_head_bias[...] = columns[0:1, 0:22]
    loss = columns[1:2, :]
    task = lax.broadcasted_iota(jnp.int32, (1, 32), 1)

    def total(inside):
        return jnp.sum(jnp.where(inside, loss, 0.0), axis=1, keepdims=True) / counted

    terms = [total(task == 0), total(task == 19), total((task == 20) | (task == 21))]
    lane = lax.broadcasted_iota(jnp.int32, (1, 128), 1)
    losses = jnp.where(lane == 0, terms[0], jnp.where(lane == 1, terms[1], terms[2]))
    log_vars = jnp.where(
        lane == 0, k.log_vars[0], jnp.where(lane == 1, k.log_vars[1], k.log_vars[2])
    )
    weighted = jnp.exp(-log_vars) * losses
    k.total_loss[...] = jnp.sum(
        jnp.where(lane < 3, weighted + log_vars, 0.0), axis=1, keepdims=True
    )
    k.grad_log_vars[...] = (1.0 - weighted)[:, 0:3]

    leave.wait()


def run_finish(args):
    return call_kernel(
        finish,
        "finish",
        None,
        args,
        dict(
            features=((12, 64, 128), BF16),
            total_loss=((1, 1), F32),
            grad_input=((1536, 512), F32),
            grad_reduce=((256, 128), F32),
            grad_dilated=((9, 64, 128), F32),
            grad_expand=((64, 512), F32),
            grad_norm_1=((2, 128), F32),
            grad_norm_2=((2, 128), F32),
            grad_norm_3=((2, 512), F32),
            grad_point=((64, 256), F32),
            grad_rates=((27, 64, 256), F32),
            grad_pool=((64, 256), F32),
            grad_norm_b=((2, 4, 64), F32),
            grad_norm_pool=((2, 64), F32),
            grad_project=((5, 32, 64), F32),
            grad_norm_p=((2, 64), F32),
            grad_head_weight=((22, 256), F32),
            grad_head_bias=((1, 22), F32),
            grad_log_vars=((1, 3), F32),
        ),
        dict(turned=pltpu.VMEM((384, 64), F32), sem=pltpu.SemaphoreType.DMA((1,))),
        0,
        hbm=dict(grad_input=1),
        stream=dict(from_input=1, grad_rates=1),
        smem=dict(boxes=1, log_vars=1),
    )


def fast_local(
    trunk_input,
    conv_reduce,
    conv_dilated,
    conv_expand,
    reduction_norm_params,
    dilated_norm_params,
    expansion_norm_params,
    aspp_point,
    aspp_rates,
    aspp_pool,
    branch_norms,
    pooling_norm_params,
    aspp_project,
    projection_norm_params,
    head_weight,
    head_bias,
    log_vars,
    crop_boxes,
    seg_labels,
    depth_target,
    normal_target,
):
    x = trunk_input.reshape(1536, 512)
    forward = run_bottleneck(
        dict(
            x=x,
            conv_reduce=conv_reduce,
            w_dilated=conv_dilated,
            w_expand=conv_expand,
            aspp_point=aspp_point,
            aspp_rates=aspp_rates,
            project=aspp_project.transpose(1, 0, 2),
            affine_1=reduction_norm_params,
            affine_2=dilated_norm_params,
            affine_3=expansion_norm_params,
            boxes=crop_boxes,
        )
    )
    middle = run_pyramid(
        dict(
            trunk=forward.trunk,
            mask=forward.mask,
            far_pyramid=forward.w_pyramid,
            branch_norms=branch_norms,
            norm_project=projection_norm_params,
            norm_pooling=pooling_norm_params,
            aspp_pool=aspp_pool,
            far_slots=forward.w_project,
            head_weight=head_weight.T,
            head_bias=head_bias,
            log_vars=log_vars,
            labels=seg_labels.transpose(1, 0, 2),
            depth=depth_target.transpose(1, 0, 2),
            normal=normal_target.transpose(0, 2, 1, 3).reshape(12, 2, 128),
            boxes=crop_boxes,
        )
    )
    back = run_pyramid_backward(
        dict(
            grad_branches=middle.grad_branches,
            w_pyramid=middle.w_pyramid.reshape(13, 256, 512),
            x=x,
            trunk=forward.trunk,
            expanded=forward.expanded,
            stats_3=forward.stats_3,
            affine_3=expansion_norm_params,
            mask=forward.mask,
            grad_pooled=middle.grad_pooled,
            grad_project=middle.grad_project,
            grad_pool=middle.grad_pool,
            boxes=crop_boxes,
        )
    )
    last = run_bottleneck_backward(
        dict(
            grad_expanded=back.grad_expanded,
            shortcut=back.shortcut,
            w_reduce=forward.w_reduce,
            half_pyramid=back.half_pyramid,
            z_pair=back.z_pair,
            sum_project=back.sum_project,
            x=x,
            hidden=forward.hidden,
            hidden_two=forward.hidden_two,
            w_expand=conv_expand,
            w_dilated=conv_dilated,
            dilated=forward.dilated,
            stats_2=forward.stats_2,
            affine_2=dilated_norm_params,
            reduced=forward.reduced,
            stats_1=forward.stats_1,
            affine_1=reduction_norm_params,
            mask=forward.mask,
            boxes=crop_boxes,
        )
    )
    done = run_finish(
        dict(
            from_input=last.grad_input,
            own_pyramid=last.own_pyramid,
            packed=middle.features,
            own_project=last.own_project,
            own_reduce=last.own_reduce,
            from_dilated=last.sum_dilated,
            from_expand=last.sum_expand,
            from_pool=back.sum_pool,
            norm_1=last.norm_1,
            norm_2=last.norm_2,
            norm_3=back.norm_3,
            norm_b=middle.norm_b,
            norm_pool=middle.norm_pool,
            norm_p=middle.norm_p,
            head_sums=middle.head_sums,
            log_vars=log_vars,
            boxes=crop_boxes,
        )
    )
    return (
        done.features.transpose(0, 2, 1).reshape(1, 12, 128, 64),
        done.total_loss.reshape(()),
        done.grad_input.reshape(1, 12, 128, 512),
        done.grad_reduce,
        done.grad_dilated.reshape(3, 3, 64, 128),
        done.grad_expand,
        done.grad_norm_1,
        done.grad_norm_2,
        done.grad_norm_3,
        done.grad_point,
        done.grad_rates.reshape(3, 3, 3, 64, 256),
        done.grad_pool,
        done.grad_norm_b,
        done.grad_norm_pool,
        done.grad_project.transpose(2, 0, 1),
        done.grad_norm_p,
        done.grad_head_weight.T,
        done.grad_head_bias.reshape(22),
        done.grad_log_vars.reshape(3),
    )


def local(
    trunk_input,
    conv_reduce,
    conv_dilated,
    conv_expand,
    reduction_norm_params,
    dilated_norm_params,
    expansion_norm_params,
    aspp_point,
    aspp_rates,
    aspp_pool,
    branch_norms,
    pooling_norm_params,
    aspp_project,
    projection_norm_params,
    head_weight,
    head_bias,
    log_vars,
    crop_boxes,
    seg_labels,
    depth_target,
    normal_target,
):
    image_inputs, tile_row_count, frame_columns, quarter = trunk_input.shape
    pixels = image_inputs * tile_row_count * frame_columns
    branch_part = aspp_point.shape[0]
    branch_total = lax.axis_size("branch")
    row_portion = 1.0 / lax.axis_size("rows")
    image_overall_count = float(crop_boxes.shape[0])
    first_image = lax.axis_index("batch") * image_inputs
    first_row = lax.axis_index("rows") * tile_row_count
    my_boxes = lax.dynamic_slice_in_dim(crop_boxes, first_image, image_inputs, 0)
    row_ids = first_row + jnp.arange(tile_row_count, dtype=jnp.int32)
    col_ids = jnp.arange(frame_columns, dtype=jnp.int32)
    inside_rows = (row_ids[None, :] >= my_boxes[:, 0:1]) & (
        row_ids[None, :] < my_boxes[:, 0:1] + my_boxes[:, 2:3]
    )
    inside_cols = (col_ids[None, :] >= my_boxes[:, 1:2]) & (
        col_ids[None, :] < my_boxes[:, 1:2] + my_boxes[:, 3:4]
    )
    valid_mask = (inside_rows[:, :, None] & inside_cols[:, None, :]).astype(jnp.float32)
    mask_column_vector = valid_mask.reshape(pixels, 1)
    mask_flat = valid_mask.reshape(pixels)
    pixel_number_count = jnp.sum((crop_boxes[:, 2] * crop_boxes[:, 3]).astype(jnp.float32))
    image_areas = (my_boxes[:, 2] * my_boxes[:, 3]).astype(jnp.float32)
    input_full = widen(trunk_input)
    reduced_output = forward_dot(input_full, conv_reduce).reshape(pixels, -1)
    normalized_first, standardized_first, inverse_deviation_first = norm_ahead_pass(
        reduced_output, mask_column_vector, pixel_number_count, reduction_norm_params
    )
    hidden_one = (
        jax.nn.silu(normalized_first)
        .astype(jnp.bfloat16)
        .reshape(image_inputs, tile_row_count, frame_columns, -1)
    )
    hidden_full = widen(pad_rows(hidden_one))
    dilated_out = 0.0
    for row_tap in range(3):
        band = hidden_full[:, 4 * row_tap : 4 * row_tap + tile_row_count]
        for col_tap in range(3):
            dilated_out = dilated_out + forward_dot(
                move(band, -(col_tap - 1) * 4, 2), conv_dilated[row_tap, col_tap]
            )
    normalized_second, standardized_second, inverse_deviation_second = norm_ahead_pass(
        dilated_out.reshape(pixels, -1), mask_column_vector, pixel_number_count, dilated_norm_params
    )
    hidden_two = (
        jax.nn.silu(normalized_second)
        .astype(jnp.bfloat16)
        .reshape(image_inputs, tile_row_count, frame_columns, -1)
    )
    hidden_two_full = widen(hidden_two)
    expanded_output = forward_dot(hidden_two_full, conv_expand).reshape(pixels, -1)
    normalized_third, standardized_third, inverse_deviation_third = norm_ahead_pass(
        expanded_output, mask_column_vector, pixel_number_count, expansion_norm_params
    )
    residual_sum = normalized_third + trunk_input.reshape(pixels, -1).astype(jnp.float32)
    trunk_out = (
        jax.nn.silu(residual_sum)
        .astype(jnp.bfloat16)
        .reshape(image_inputs, tile_row_count, frame_columns, quarter)
    )
    trunk_full = widen(trunk_out)
    branch_outs = [backward_dot(trunk_full, aspp_point)]
    for branch_id in range(3):
        dilation = RATES[branch_id]
        hops = dilation // tile_row_count
        partials = [0.0, 0.0, 0.0]
        for col_tap in range(3):
            shifted = move(trunk_full, -(col_tap - 1) * dilation, 2)
            products = backward_dot(shifted, stacked_taps(aspp_rates[branch_id], col_tap))
            for row_tap in range(3):
                partials[row_tap] = (
                    partials[row_tap]
                    + products[..., row_tap * branch_part : (row_tap + 1) * branch_part]
                )
        upper = send_down(partials[0].astype(jnp.bfloat16), hops).astype(jnp.float32)
        lower_part = send_up(partials[2].astype(jnp.bfloat16), hops).astype(jnp.float32)
        branch_outs.append(partials[1] + upper + lower_part)
    spatial_flattened = jnp.stack(branch_outs, axis=3).reshape(pixels, -1)
    branch_gain_bias = branch_norms.reshape(2, -1)
    normalized_spatial, standardized_spatial, inverse_deviation_spatial = norm_ahead_pass(
        spatial_flattened, mask_column_vector, pixel_number_count, branch_gain_bias
    )
    spatial_act = (
        jax.nn.silu(normalized_spatial)
        .astype(jnp.bfloat16)
        .reshape(image_inputs, tile_row_count, frame_columns, 4, branch_part)
    )
    pooled_local = lax.dot_general(
        valid_mask.astype(jnp.bfloat16),
        trunk_full,
        (((1, 2), (1, 2)), ((0,), (0,))),
        preferred_element_type=jnp.float32,
    )
    pooled = (over_rows(pooled_local) / image_areas[:, None]).astype(jnp.bfloat16)
    pooling_convolution = backward_dot(pooled, aspp_pool)
    normalized_poolbranch, standardized_poolbranch, inverse_deviation_poolbranch = norm_ahead_pass(
        pooling_convolution, row_portion, image_overall_count, pooling_norm_params
    )
    pool_act = jax.nn.silu(normalized_poolbranch).astype(jnp.bfloat16)
    pool_wide = jnp.broadcast_to(
        pool_act[:, None, None, None, :],
        (image_inputs, tile_row_count, frame_columns, 1, branch_part),
    )
    concat = jnp.concatenate([spatial_act, pool_wide], axis=3)
    concat_flat = widen(concat).reshape(pixels, -1)
    proj_kernel = (
        aspp_project.reshape(branch_part, 5, branch_total, branch_part)
        .transpose(0, 2, 1, 3)
        .reshape(branch_part, 5 * branch_total * branch_part)
    )
    projected_output = backward_dot(concat_flat, proj_kernel)
    normalized_projector, standardized_projector, inverse_deviation_projector = norm_ahead_pass(
        projected_output, mask_column_vector, pixel_number_count, projection_norm_params
    )
    features = (
        jax.nn.silu(normalized_projector)
        .astype(jnp.bfloat16)
        .reshape(image_inputs, tile_row_count, frame_columns, -1)
    )
    features_wide = widen(features).reshape(pixels, -1).astype(jnp.float32)
    head_wide = head_weight.astype(jnp.float32)
    logits = jnp.dot(features_wide, head_wide, precision=HIGH) + head_bias
    classes = head_bias.shape[0] - 3
    seg_logits = logits[:, :classes]
    labels_flat = seg_labels.reshape(pixels)
    classes_hot = (labels_flat[:, None] == jnp.arange(classes, dtype=jnp.int32)[None, :]).astype(
        jnp.float32
    )
    cross = jax.nn.logsumexp(seg_logits, axis=1) - jnp.sum(seg_logits * classes_hot, axis=1)
    depth_gap = logits[:, classes] - depth_target.reshape(pixels)
    smooth_abs = jnp.sqrt(depth_gap * depth_gap + 1.0)
    normal_gap = logits[:, classes + 1 :] - jnp.moveaxis(normal_target, 1, 3).reshape(pixels, 2)
    local_losses = jnp.stack(
        [
            jnp.sum(mask_flat * cross),
            jnp.sum(mask_flat * (smooth_abs - 1.0)),
            jnp.sum(mask_flat * jnp.sum(normal_gap * normal_gap, axis=1)),
        ]
    )
    task_weights = jnp.exp(-log_vars)
    grad_seg = (jax.nn.softmax(seg_logits, axis=1) - classes_hot) * (
        task_weights[0] / pixel_number_count * mask_flat
    )[:, None]
    grad_depth = depth_gap / smooth_abs * (task_weights[1] / pixel_number_count * mask_flat)
    grad_normal = 2.0 * normal_gap * (task_weights[2] / pixel_number_count * mask_flat)[:, None]
    grad_logits = jnp.concatenate([grad_seg, grad_depth[:, None], grad_normal], axis=1)
    head_local = lax.dot_general(
        features_wide, grad_logits, (((0,), (0,)), ((), ())), precision=HIGH
    )
    loss_parts, grad_head_weight, grad_head_bias = lax.psum(
        (local_losses, head_local, jnp.sum(grad_logits, axis=0)), ("rows", "batch")
    )
    task_losses = loss_parts / pixel_number_count
    total_loss = jnp.sum(task_weights * task_losses + log_vars)
    grad_log_vars = 1.0 - task_weights * task_losses
    grad_features = jnp.dot(grad_logits, head_wide.T, precision=HIGH)
    my_features_grad = lax.dynamic_slice_in_dim(
        grad_features, lax.axis_index("branch") * branch_part, branch_part, 1
    )
    gradient_before_projector = my_features_grad * silu_slope(normalized_projector)
    grad_proj_in, grad_project_norm = norm_reverse_pass(
        gradient_before_projector,
        standardized_projector,
        inverse_deviation_projector,
        1.0,
        mask_column_vector,
        pixel_number_count,
        projection_norm_params,
    )
    grad_proj_low = grad_proj_in.astype(jnp.bfloat16)
    proj_kernel_grad = lax.dot_general(
        grad_proj_low, concat_flat, (((0,), (0,)), ((), ())), preferred_element_type=jnp.float32
    )
    grad_project_local = (
        proj_kernel_grad.reshape(branch_part, branch_total, 5, branch_part)
        .transpose(0, 2, 1, 3)
        .reshape(branch_part, 5, branch_total * branch_part)
    )
    concat_grad = forward_dot(grad_proj_low, proj_kernel).reshape(
        image_inputs, tile_row_count, frame_columns, -1
    )
    concat_grad = narrow(concat_grad).reshape(pixels, 5, branch_part)
    pool_grad_img = over_rows(
        jnp.sum(concat_grad[:, 4, :].reshape(image_inputs, -1, branch_part), axis=1)
    )
    gradient_before_poolbranch = pool_grad_img * silu_slope(normalized_poolbranch)
    grad_pool_conv, grad_pool_norm = norm_reverse_pass(
        gradient_before_poolbranch,
        standardized_poolbranch,
        inverse_deviation_poolbranch,
        row_portion,
        1.0,
        image_overall_count,
        pooling_norm_params,
    )
    pool_conv_low = grad_pool_conv.astype(jnp.bfloat16)
    grad_pool_local = (
        lax.dot_general(
            pool_conv_low, pooled, (((0,), (0,)), ((), ())), preferred_element_type=jnp.float32
        )
        * row_portion
    )
    pooled_grad = forward_dot(pool_conv_low, aspp_pool)
    gradient_before_spatialbranch = concat_grad[:, :4, :].reshape(pixels, -1) * silu_slope(
        normalized_spatial
    )
    grad_spatial, branch_norm_grad = norm_reverse_pass(
        gradient_before_spatialbranch,
        standardized_spatial,
        inverse_deviation_spatial,
        1.0,
        mask_column_vector,
        pixel_number_count,
        branch_gain_bias,
    )
    grad_branch_norms = branch_norm_grad.reshape(2, 4, branch_part)
    spatial_low = grad_spatial.astype(jnp.bfloat16).reshape(
        image_inputs, tile_row_count, frame_columns, 4, branch_part
    )
    point_grad = spatial_low[:, :, :, 0]
    grad_point_local = pixel_dot(point_grad, trunk_full)
    trunk_grad = forward_dot(point_grad, aspp_point)
    trunk_grad = (
        trunk_grad + valid_mask[..., None] * (pooled_grad / image_areas[:, None])[:, None, None, :]
    )
    rate_grads = []
    for branch_id in range(3):
        dilation = RATES[branch_id]
        hops = dilation // tile_row_count
        centre = spatial_low[:, :, :, branch_id + 1]
        grad_taps = jnp.concatenate(
            [send_up(centre, hops), centre, send_down(centre, hops)], axis=3
        )
        per_col = []
        for col_tap in range(3):
            shifted = move(trunk_full, -(col_tap - 1) * dilation, 2)
            per_col.append(pixel_dot(grad_taps, shifted))
            tap_grad = forward_dot(grad_taps, stacked_taps(aspp_rates[branch_id], col_tap))
            trunk_grad = trunk_grad + move(tap_grad, (col_tap - 1) * dilation, 2)
        col_stack = jnp.stack(per_col, axis=0).reshape(3, 3, branch_part, -1)
        rate_grads.append(col_stack.transpose(1, 0, 2, 3))
    grad_rates_local = jnp.stack(rate_grads, axis=0)
    trunk_own = narrow(trunk_grad).reshape(pixels, -1)
    gradient_shortcut = trunk_own * silu_slope(residual_sum)
    grad_expanded, grad_norm_expand = norm_reverse_pass(
        gradient_shortcut,
        standardized_third,
        inverse_deviation_third,
        1.0,
        mask_column_vector,
        pixel_number_count,
        expansion_norm_params,
    )
    expanded_low = grad_expanded.astype(jnp.bfloat16).reshape(
        image_inputs, tile_row_count, frame_columns, -1
    )
    grad_expand_local = pixel_dot(hidden_two_full, expanded_low)
    hidden_two_grad = narrow(backward_dot(expanded_low, conv_expand)).reshape(pixels, -1)
    gradient_before_second = hidden_two_grad * silu_slope(normalized_second)
    gradient_dilated_input, gradient_dilated_norm = norm_reverse_pass(
        gradient_before_second,
        standardized_second,
        inverse_deviation_second,
        1.0,
        mask_column_vector,
        pixel_number_count,
        dilated_norm_params,
    )
    dilated_lowprec = gradient_dilated_input.astype(jnp.bfloat16).reshape(
        image_inputs, tile_row_count, frame_columns, -1
    )
    dilated_padded = pad_rows(dilated_lowprec)
    hidden_one_grad = 0.0
    kernel_grads = []
    for row_tap in range(3):
        band = hidden_full[:, 4 * row_tap : 4 * row_tap + tile_row_count]
        grad_band = dilated_padded[:, 8 - 4 * row_tap : 8 - 4 * row_tap + tile_row_count]
        for col_tap in range(3):
            kernel_grads.append(pixel_dot(move(band, -(col_tap - 1) * 4, 2), dilated_lowprec))
            hidden_one_grad = hidden_one_grad + backward_dot(
                move(grad_band, (col_tap - 1) * 4, 2), conv_dilated[row_tap, col_tap]
            )
    grad_dilated_local = jnp.stack(kernel_grads, axis=0).reshape(3, 3, hidden_full.shape[3], -1)
    hidden_one_own = narrow(hidden_one_grad).reshape(pixels, -1)
    gradient_before_first = hidden_one_own * silu_slope(normalized_first)
    grad_reduced, grad_norm_reduce = norm_reverse_pass(
        gradient_before_first,
        standardized_first,
        inverse_deviation_first,
        1.0,
        mask_column_vector,
        pixel_number_count,
        reduction_norm_params,
    )
    reduced_low = grad_reduced.astype(jnp.bfloat16).reshape(
        image_inputs, tile_row_count, frame_columns, -1
    )
    grad_reduce_local = pixel_dot(input_full, reduced_low)
    input_grad = narrow(backward_dot(reduced_low, conv_reduce))
    grad_input = input_grad + gradient_shortcut.reshape(
        image_inputs, tile_row_count, frame_columns, quarter
    )
    grad_reduce, grad_dilated, grad_expand, grad_point, grad_rates, grad_pool, grad_project = (
        lax.psum_scatter(grad_reduce_local, ("rows", "batch"), scatter_dimension=0, tiled=True),
        lax.psum_scatter(grad_dilated_local, ("rows", "batch"), scatter_dimension=2, tiled=True),
        lax.psum_scatter(grad_expand_local, ("rows", "batch"), scatter_dimension=0, tiled=True),
        lax.psum_scatter(grad_point_local, ("rows", "batch"), scatter_dimension=1, tiled=True),
        lax.psum_scatter(grad_rates_local, ("rows", "batch"), scatter_dimension=4, tiled=True),
        lax.psum_scatter(grad_pool_local, ("rows", "batch"), scatter_dimension=1, tiled=True),
        lax.psum_scatter(grad_project_local, ("rows", "batch"), scatter_dimension=2, tiled=True),
    )
    return (
        features,
        total_loss,
        grad_input,
        grad_reduce,
        grad_dilated,
        grad_expand,
        grad_norm_reduce,
        gradient_dilated_norm,
        grad_norm_expand,
        grad_point,
        grad_rates,
        grad_pool,
        grad_branch_norms,
        grad_pool_norm,
        grad_project,
        grad_project_norm,
        grad_head_weight,
        grad_head_bias,
        grad_log_vars,
    )


def solution(mesh):
    in_specs = (
        P("batch", "rows", None, "branch"),
        P(None, "branch"),
        P(None, None, None, "branch"),
        P(None, "branch"),
        P(None, "branch"),
        P(None, "branch"),
        P(None, "branch"),
        P("branch", None),
        P(None, None, None, "branch", None),
        P("branch", None),
        P(None, None, "branch"),
        P(None, "branch"),
        P("branch", None, None),
        P(None, "branch"),
        P(),
        P(),
        P(),
        P(),
        P("batch", "rows", None),
        P("batch", "rows", None),
        P("batch", None, "rows", None),
    )
    out_specs = (
        P("batch", "rows", None, "branch"),
        P(),
        P("batch", "rows", None, "branch"),
        P(("rows", "batch"), "branch"),
        P(None, None, ("rows", "batch"), "branch"),
        P(("rows", "batch"), "branch"),
        P(None, "branch"),
        P(None, "branch"),
        P(None, "branch"),
        P("branch", ("rows", "batch")),
        P(None, None, None, "branch", ("rows", "batch")),
        P("branch", ("rows", "batch")),
        P(None, None, "branch"),
        P(None, "branch"),
        P("branch", None, ("rows", "batch")),
        P(None, "branch"),
        P(),
        P(),
        P(),
    )
    small = (mesh.shape["branch"], mesh.shape["rows"], mesh.shape["batch"]) == (4, 2, 4)
    body = fast_local if small else local
    return jax.shard_map(body, mesh=mesh, in_specs=in_specs, out_specs=out_specs, check_vma=False)
```
